32 devices in a mesh: ctx: 8 (over z, y), fsdp: 4 (over x, core).
Axes of the slice: x: 2, y: 2, z: 4, core: 2. Of those that a mesh axis runs over, the one named last changes fastest.
Arguments:
- tokens: bfloat16 [4, 2, 512, 2048], P('fsdp', None, 'ctx'), may hold values from -6 to 6
- segments: int32 [4, 2, 512], P('fsdp'), may hold values from 0 to 9, as said below
- routes: int32 [4, 2, 512, 4], P('fsdp', None, 'ctx'), may hold values from 0 to 7, all different within a row
- cotangent: bfloat16 [4, 2, 512, 2048], P('fsdp', None, 'ctx'), may hold values from -6 to 6
- w_qkv: bfloat16 [2048, 6144], P(('ctx', 'fsdp')), may hold values from -0.125 to 0.125
- b_qkv: bfloat16 [6144], P(('ctx', 'fsdp')), may hold values from -1.1953125 to 1.1953125
- w_out: bfloat16 [2048, 2048], P(('ctx', 'fsdp')), may hold values from -0.375 to 0.375
- gain_attn: bfloat16 [2048], P(('ctx', 'fsdp')), may hold values from 0.5 to 1.5
- gain_ffn: bfloat16 [2048], P(('ctx', 'fsdp')), may hold values from 0.5 to 1.5
- w_router: bfloat16 [2048, 8], P(('ctx', 'fsdp')), may hold values from -0.0625 to 0.0625
- w_shared_gate: bfloat16 [2048], P(('ctx', 'fsdp')), may hold values from -0.125 to 0.125
- w_shared_in: bfloat16 [2048, 11264], P(('ctx', 'fsdp')), may hold values from -0.125 to 0.125
- w_shared_out: bfloat16 [5632, 2048], P(('ctx', 'fsdp')), may hold values from -0.15625 to 0.15625
- w_expert_in: bfloat16 [8, 2048, 2816], P('ctx', 'fsdp'), may hold values from -0.125 to 0.125
- w_expert_out: bfloat16 [8, 1408, 2048], P('ctx', 'fsdp'), may hold values from -0.875 to 0.875
Outputs:
- output: bfloat16 [4, 2, 512, 2048], P('fsdp', None, 'ctx')
- grad_tokens: float32 [4, 2, 512, 2048], P('fsdp', None, 'ctx')
- grad_w_qkv: float32 [2048, 6144], P(('ctx', 'fsdp'))
- grad_b_qkv: float32 [6144], P(('ctx', 'fsdp'))
- grad_w_out: float32 [2048, 2048], P(('ctx', 'fsdp'))
- grad_gain_attn: float32 [2048], P(('ctx', 'fsdp'))
- grad_gain_ffn: float32 [2048], P(('ctx', 'fsdp'))
- grad_w_router: float32 [2048, 8], P(('ctx', 'fsdp'))
- grad_w_shared_gate: float32 [2048], P(('ctx', 'fsdp'))
- grad_w_shared_in: float32 [2048, 11264], P(('ctx', 'fsdp'))
- grad_w_shared_out: float32 [5632, 2048], P(('ctx', 'fsdp'))
- grad_w_expert_in: float32 [8, 2048, 2816], P('ctx', 'fsdp')
- grad_w_expert_out: float32 [8, 1408, 2048], P('ctx', 'fsdp')
The draws below stay inside these ranges and needn't reach their ends.
Inputs may be any that keep to these rules, and one draw needn't show every extreme that they name: `segments`: along each sequence in order of position, segment numbers never fall; each sequence's last position has the number 1024 // 200 + 4. `routes`: each token names 4 different experts.
All inputs are finite; a program needn't handle non-finite values.
Results may differ from the reference program's by a relative error of at most 0.018.
Values may be sent and summed in bfloat16 or wider, within the bound.
No kernel may reach another device: no remote copies, remote signals or barrier semaphores. Data moves between devices by JAX's collectives and lax.ppermute only.
A program may use at most 448 MiB of HBM per device.

```python
import jax
import jax.numpy as jnp
from jax import lax

D = 2048
HEADS = 16
HD = 128
FS = 5632
FE = 1408
TOPK = 4
TOK_DEV = 128
MIN_DOC = 200
DOC_MOST = 2000
EXPERTS = 8
SEQS = 4
BLK = 64
HALF = 512
LEN = 1024
CAP = 64
N_CTX = 8


def draw_segments(key, part):
    key = jax.random.fold_in(key, 11)
    first_start = jax.random.randint(jax.random.fold_in(key, 1), (SEQS, 1), 1, max(BLK // 2, 2))
    long_end = HALF + BLK + jax.random.randint(jax.random.fold_in(key, 2), (SEQS, 1), 0, max(BLK // 2, 1))
    doc_count = LEN // MIN_DOC + 2
    doc_lengths = jax.random.randint(jax.random.fold_in(key, 3), (SEQS, doc_count), MIN_DOC, DOC_MOST + 1)
    bounds = jnp.concatenate([first_start, long_end, long_end + jnp.cumsum(doc_lengths, axis=1)], axis=1)
    half_index = jnp.arange(HALF, dtype=jnp.int32)
    places = jnp.stack([half_index, LEN - BLK * (half_index // BLK + 1) + half_index % BLK])
    passed = places[None, :, :, None] >= bounds[:, None, None, :]
    counted = jnp.sum(passed.astype(jnp.int32), axis=-1).astype(jnp.int32)
    last_count = jnp.max(counted, axis=(1, 2), keepdims=True)
    return (counted + (doc_count + 2) - last_count).astype(jnp.int32)


def steps_of(rng, dims, shards, low, top_value):
    gain = 1.0
    for position, blocks in shards:
        steps = jax.random.uniform(jax.random.fold_in(jax.random.fold_in(rng, 6), position), (blocks,), jnp.float32, low / len(shards), top_value / len(shards))
        gain = gain * jnp.repeat(jnp.exp(steps), dims[position] // blocks).reshape((-1,) + (1,) * (len(dims) - 1 - position))
    return gain


def choose_distinct(key, rows, count, top, lift):
    sequence = jax.random.permutation(jax.random.fold_in(key, 1), count)
    pull = sequence
    for power in range(3):
        pull = pull * pull // count
    pull = pull * lift // count
    tickets = jax.random.randint(jax.random.fold_in(key, 2), (rows, count), 0, 4096) + pull
    holders = jax.random.permutation(jax.random.fold_in(key, 3), rows)[jnp.arange(count) % rows]
    tickets = jnp.where(jnp.arange(rows)[:, None] == holders[None, :], 1 << 14, tickets)
    merit = tickets * count + jnp.arange(count)
    return lax.top_k(merit.astype(jnp.int32), top)[1].astype(jnp.int32)


def scatter_about(own_key, extent, spread, reach, shards=(), kind=jnp.bfloat16):
    entries = spread * jax.random.normal(own_key, extent, jnp.float32)
    if shards:
        entries = entries * steps_of(own_key, extent, shards, -0.22, 0.18)
    return jnp.clip(entries, -reach, reach).astype(kind)


def setup_inputs(seed: int = 0) -> dict:
    splits = jax.random.split(jax.random.key(seed), 16)
    tokens = scatter_about(splits[0], (SEQS, 2, HALF, D), 1.0, 6.0, ((0, 4), (2, 8)))
    segments = draw_segments(jax.random.fold_in(splits[15], 71), 0)
    routes = choose_distinct(splits[2], SEQS * 2 * HALF, EXPERTS, TOPK, 8192).reshape((SEQS, 2, HALF, TOPK))
    cotangent = scatter_about(splits[3], (SEQS, 2, HALF, D), 1.0, 6.0, ((0, 4), (2, 8)))
    w_qkv = scatter_about(splits[4], (D, 3 * D), D ** -0.5, 0.125, ((0, 32),))
    b_qkv = scatter_about(splits[5], (3 * D,), 0.2, 1.1953125, ((0, 32),))
    w_out = scatter_about(splits[6], (D, D), (D // 8) ** -0.5, 0.375, ((0, 32),))
    gain_attn = jnp.clip(1.0 + 0.1 * jax.random.normal(splits[7], (D,), jnp.float32), 0.5, 1.5).astype(jnp.bfloat16)
    gain_ffn = jnp.clip(1.0 + 0.1 * jax.random.normal(splits[8], (D,), jnp.float32), 0.5, 1.5).astype(jnp.bfloat16)
    w_router = scatter_about(splits[9], (D, EXPERTS), (4 * D) ** -0.5, 0.0625, ((0, 32),))
    w_shared_gate = scatter_about(splits[10], (D,), D ** -0.5, 0.125, ((0, 32),))
    w_shared_in = scatter_about(splits[11], (D, 2 * FS), D ** -0.5, 0.125, ((0, 32),))
    w_shared_out = scatter_about(splits[12], (FS, D), (FS // 4) ** -0.5, 0.15625, ((0, 32),))
    w_expert_in = scatter_about(splits[13], (EXPERTS, D, 2 * FE), D ** -0.5, 0.125, ((0, 8), (1, 4)))
    w_expert_out = scatter_about(splits[14], (EXPERTS, FE, D), (FE // 32) ** -0.5, 0.875, ((0, 8), (1, 4)))
    return {"tokens": tokens, "segments": segments, "routes": routes, "cotangent": cotangent, "w_qkv": w_qkv, "b_qkv": b_qkv, "w_out": w_out, "gain_attn": gain_attn, "gain_ffn": gain_ffn, "w_router": w_router, "w_shared_gate": w_shared_gate, "w_shared_in": w_shared_in, "w_shared_out": w_shared_out, "w_expert_in": w_expert_in, "w_expert_out": w_expert_out}


RMS_EPS = 1e-06
ROPE_THETA = 1000000.0
MASK_FILL = -1e+30
HIGHEST = lax.Precision.HIGHEST

@jax.custom_vjp
def low(v):
    return lax.optimization_barrier(v.astype(jnp.bfloat16)).astype(jnp.float32)

@jax.custom_vjp
def low_back(v):
    return v

def low_keep(v):
    return (low(v), None)

def low_pass(kept, grad):
    return (grad,)

def back_keep(v):
    return (v, None)

def back_low(kept, grad):
    return (low(grad),)
low.defvjp(low_keep, low_pass)
low_back.defvjp(back_keep, back_low)

def dealt_positions(half_len, block_len, seq_len):
    half_index = jnp.arange(half_len, dtype=jnp.int32)
    second = seq_len - block_len * (half_index // block_len + 1) + half_index % block_len
    return jnp.concatenate([half_index, second]).astype(jnp.int32)

def rope_tables(positions, head_dim):
    half_dim = head_dim // 2
    inv_freq = ROPE_THETA ** (-(jnp.arange(half_dim, dtype=jnp.float32) * 2.0 / head_dim))
    angles = positions.astype(jnp.float32)[:, None] * inv_freq[None, :]
    cos_tab = jnp.concatenate([jnp.cos(angles), jnp.cos(angles)], axis=-1)
    sine_tab = jnp.concatenate([jnp.sin(angles), jnp.sin(angles)], axis=-1)
    return (cos_tab, sine_tab)

def rotate(values, cos_tab, sine_tab):
    half_dim = values.shape[-1] // 2
    turned = jnp.concatenate([-values[..., half_dim:], values[..., :half_dim]], axis=-1)
    return values * cos_tab[:, None, :] + turned * sine_tab[:, None, :]

def rms_norm(values, gain_vec):
    return values * lax.rsqrt(lax.optimization_barrier(jnp.mean(values * values, axis=-1, keepdims=True)) + RMS_EPS) * gain_vec

def swiglu(pre_act, split_at):
    return jax.nn.silu(pre_act[..., :split_at]) * pre_act[..., split_at:]

def attend_block(queries, query_pos, query_seg, keys, values, key_pos, key_seg):
    scores = low_back(jnp.einsum('qhd,khd->hqk', queries, keys, precision=HIGHEST) * HD ** (-0.5))
    allowed = (key_pos[None, :] <= query_pos[:, None]) & (key_seg[None, :] == query_seg[:, None])
    scores = jnp.where(allowed[None], scores, MASK_FILL)
    log_total = jax.nn.logsumexp(scores, axis=-1, keepdims=True)
    weights = low(jnp.exp(scores - log_total))
    return jnp.einsum('hqk,khd->qhd', weights, values, precision=HIGHEST)

def attend_sequence(queries, keys, values, seg_row, positions):
    query_rows = min(512, LEN)
    block_count = LEN // query_rows
    checked = jax.checkpoint(attend_block)

    def per_block(item):
        return checked(item[0], item[1], item[2], keys, values, positions, seg_row)
    attended = lax.map(per_block, (queries.reshape(block_count, query_rows, HEADS, HD), positions.reshape(block_count, query_rows), seg_row.reshape(block_count, query_rows)))
    return attended.reshape(LEN, HEADS, HD)

def to_blocks(values):
    tail = values.shape[1:]
    order = (0, 2, 1, 3) + tuple(range(4, 4 + len(tail)))
    return values.reshape((SEQS, 2, N_CTX, BLK) + tail).transpose(order).reshape((SEQS * N_CTX, 2 * BLK) + tail)

def from_blocks(values):
    tail = values.shape[2:]
    order = (0, 2, 1, 3) + tuple(range(4, 4 + len(tail)))
    return values.reshape((SEQS, N_CTX, 2, BLK) + tail).transpose(order).reshape((SEQS * 2 * HALF,) + tail)

def apply_expert(item):
    rows, weight_in, weight_out = item
    pre_act = low_back(jnp.dot(rows, weight_in, precision=HIGHEST))
    hidden = low(swiglu(pre_act, FE))
    return low_back(low(jnp.dot(hidden, weight_out, precision=HIGHEST)))

def layer(token_in, w_qkv, b_qkv, w_out, gain_attn, gain_ffn, w_router, w_shared_gate, w_shared_in, w_shared_out, w_expert_in, w_expert_out, segments, routes):
    token_rows = token_in.reshape(-1, D)
    normed = low(rms_norm(token_rows, gain_attn))
    projected = low_back(jnp.dot(normed, w_qkv, precision=HIGHEST) + b_qkv)
    positions = dealt_positions(HALF, BLK, LEN)
    cos_tab, sine_tab = rope_tables(positions, HD)
    shaped = projected.reshape(SEQS, LEN, 3, HEADS, HD)
    queries = low(rotate(shaped[:, :, 0], cos_tab, sine_tab))
    keys = low(rotate(shaped[:, :, 1], cos_tab, sine_tab))
    values = low(shaped[:, :, 2])
    seg_rows = segments.reshape(SEQS, LEN)

    def per_sequence(item):
        return attend_sequence(item[0], item[1], item[2], item[3], positions)
    attended = lax.map(per_sequence, (queries, keys, values, seg_rows))
    attn_rows = low_back(low(attended.reshape(-1, D)))
    residual = token_rows + low_back(jnp.dot(attn_rows, w_out, precision=HIGHEST))
    normed_two = low(rms_norm(residual, gain_ffn))
    logits = low_back(jnp.dot(normed_two, w_router, precision=HIGHEST))
    router_probs = jax.nn.softmax(logits, axis=-1)
    route_rows = routes.reshape(-1, TOPK)
    gate_vals = jnp.take_along_axis(router_probs, route_rows, axis=1)
    shared_scale = jax.nn.sigmoid(low_back(jnp.dot(normed_two, w_shared_gate, precision=HIGHEST)))
    shared_pre = low_back(jnp.dot(normed_two, w_shared_in, precision=HIGHEST))
    shared_hid = low(swiglu(shared_pre, FS))
    shared_res = low_back(jnp.dot(shared_hid, w_shared_out, precision=HIGHEST))
    block_count = SEQS * N_CTX
    slot_count = EXPERTS * CAP
    block_routes = to_blocks(route_rows).reshape(block_count, TOK_DEV * TOPK)
    expert_marks = (block_routes[..., None] == jnp.arange(EXPERTS, dtype=jnp.int32)).astype(jnp.int32)
    pair_ranks = lax.optimization_barrier(jnp.sum((jnp.cumsum(expert_marks, axis=1) - expert_marks) * expert_marks, axis=-1))
    pair_target = jnp.where(pair_ranks < CAP, block_routes * CAP + pair_ranks, -1)
    pair_map = (pair_target[..., None] == jnp.arange(slot_count, dtype=jnp.int32)).astype(jnp.float32)
    token_map = lax.optimization_barrier(jnp.sum(pair_map.reshape(block_count, TOK_DEV, TOPK, slot_count), axis=2))
    buffer = low_back(jnp.einsum('btc,btd->bcd', token_map, to_blocks(normed_two), precision=HIGHEST))
    expert_rows = buffer.reshape(block_count, EXPERTS, CAP, D).transpose(1, 0, 2, 3).reshape(EXPERTS, block_count * CAP, D)
    expert_res = lax.map(apply_expert, (expert_rows, w_expert_in, w_expert_out))
    returned = expert_res.reshape(EXPERTS, block_count, CAP, D).transpose(1, 0, 2, 3).reshape(block_count, slot_count, D)
    pair_vals = jnp.einsum('bpc,bcd->bpd', pair_map, returned, precision=HIGHEST).reshape(block_count, TOK_DEV, TOPK, D)
    routed = from_blocks(lax.optimization_barrier(jnp.sum(to_blocks(gate_vals)[..., None] * pair_vals, axis=2)))
    result = residual + shared_scale[:, None] * shared_res + routed
    return result.reshape(SEQS, 2, HALF, D)

def reference(tokens, segments, routes, cotangent, w_qkv, b_qkv, w_out, gain_attn, gain_ffn, w_router, w_shared_gate, w_shared_in, w_shared_out, w_expert_in, w_expert_out):
    floats = [piece.astype(jnp.float32) for piece in (tokens, w_qkv, b_qkv, w_out, gain_attn, gain_ffn, w_router, w_shared_gate, w_shared_in, w_shared_out, w_expert_in, w_expert_out)]

    def forward(*pieces):
        return layer(*pieces, segments, routes)
    result, pullback = jax.vjp(forward, *floats)
    gradients = pullback(cotangent.astype(jnp.float32))
    return (result.astype(jnp.bfloat16), gradients[0], gradients[1], gradients[2], gradients[3], gradients[4], gradients[5], gradients[6], gradients[7], gradients[8], gradients[9], gradients[10], gradients[11])
```

```python
import jax
import jax.numpy as jnp
from jax import lax
from jax.sharding import PartitionSpec as P

HD = 128
HEADS = 16
FS = 5632
FE = 1408


RMS_EPS = 1e-06
ROPE_THETA = 1000000.0
MASK_FILL = -1e30
HIGHEST = lax.Precision.HIGHEST


def rope_tables(positions, head_dim):
    half_dim = head_dim // 2
    inv_freq = ROPE_THETA ** (-(jnp.arange(half_dim, dtype=jnp.float32) * 2.0 / head_dim))
    angles = positions.astype(jnp.float32)[:, None] * inv_freq[None, :]
    cos_tab = jnp.concatenate([jnp.cos(angles), jnp.cos(angles)], axis=-1)
    sine_tab = jnp.concatenate([jnp.sin(angles), jnp.sin(angles)], axis=-1)
    return (cos_tab, sine_tab)


def rotate(values, cos_tab, sine_tab):
    half_dim = values.shape[-1] // 2
    turned = jnp.concatenate([-values[..., half_dim:], values[..., :half_dim]], axis=-1)
    return values * cos_tab[:, None, :] + turned * sine_tab[:, None, :]


def rotate_back(upstream, cos_tab, sine_tab):
    half_dim = upstream.shape[-1] // 2
    scaled = upstream * sine_tab[:, None, :]
    return upstream * cos_tab[:, None, :] + jnp.concatenate(
        [scaled[..., half_dim:], -scaled[..., :half_dim]], axis=-1
    )


def rms_norm(values, gain_vec):
    inv_rms = lax.rsqrt(jnp.mean(values * values, axis=-1, keepdims=True) + RMS_EPS)
    return (values * inv_rms * gain_vec, inv_rms)


def rms_back(values, inv_rms, gain_vec, upstream):
    weighted = upstream * gain_vec
    inner_mean = jnp.mean(weighted * values, axis=-1, keepdims=True)
    return (
        inv_rms * weighted - values * inv_rms * inv_rms * inv_rms * inner_mean,
        jnp.sum(upstream * values * inv_rms, axis=0),
    )


def swiglu(pre_act, split_at):
    return jax.nn.silu(pre_act[..., :split_at]) * pre_act[..., split_at:]


def swiglu_back(pre_act, split_at, upstream):
    gate_part = pre_act[..., :split_at]
    up_part = pre_act[..., split_at:]
    sigmoid_g = jax.nn.sigmoid(gate_part)
    d_gate = upstream * up_part * sigmoid_g * (1.0 + gate_part * (1.0 - sigmoid_g))
    d_up = upstream * gate_part * sigmoid_g
    return jnp.concatenate([d_gate, d_up], axis=-1)


def ring_order(size):
    return list(range(0, size, 2)) + list(range(size - 1, 0, -2))


def ring_steps(size):
    order = ring_order(size)
    ahead = [(order[i], order[(i + 1) % size]) for i in range(size)]
    back = [(dst, src) for src, dst in ahead]
    return (ahead, back)


def ring_peers(size, ctx_index):
    order = ring_order(size)
    place = {dev: i for i, dev in enumerate(order)}
    table = jnp.array(
        [[order[(place[dev] + k) % size] for k in range(size)] for dev in range(size)], jnp.int32
    )
    row = lax.dynamic_index_in_dim(table, ctx_index, 0, keepdims=False)
    return [row[k] for k in range(size)]


def ring_gather(block, size, ctx_index):
    rows = block.shape[0] // 2
    ahead, back = ring_steps(size)
    peers = ring_peers(size, ctx_index)
    half = size // 2
    halves = (block[:rows], block[rows:])
    out = jnp.zeros((size, 2, rows) + block.shape[1:], block.dtype)
    zero = jnp.zeros((), jnp.int32)

    def put(out, piece, peer, part):
        start = (peer, jnp.full((), part, jnp.int32)) + (zero,) * block.ndim
        return lax.dynamic_update_slice(out, piece[None, None], start)

    for part in range(2):
        out = put(out, halves[part], ctx_index, part)
    fore, rear = list(halves), list(halves)
    for k in range(1, half + 1):
        for part in (0, 1):
            if k < half or part == 0:
                fore[part] = lax.ppermute(fore[part], "ctx", ahead)
                out = put(out, fore[part], peers[(size - k) % size], part)
            if k < half or part == 1:
                rear[part] = lax.ppermute(rear[part], "ctx", back)
                out = put(out, rear[part], peers[k], part)
    return out.reshape((size,) + block.shape)


def ring_scatter(parts, size, ctx_index):
    rows = parts.shape[1] // 2
    ahead, back = ring_steps(size)
    peers = ring_peers(size, ctx_index)
    half = size // 2

    def own(k, part):
        block = lax.dynamic_index_in_dim(parts, peers[k % size], 0, keepdims=False)
        return block[part * rows : (part + 1) * rows]

    sums = []
    for part in (0, 1):
        total = own(0, part).astype(jnp.float32)
        for perm, sign, first in (
            (ahead, 1, half if part == 0 else half - 1),
            (back, -1, half if part == 1 else half - 1),
        ):
            moving = own(sign * first, part)
            for k in range(first, 0, -1):
                moving = lax.ppermute(moving, "ctx", perm)
                if k > 1:
                    moving = (
                        moving.astype(jnp.float32)
                        + own(sign * (k - 1), part).astype(jnp.float32)
                    ).astype(jnp.bfloat16)
            total = total + moving.astype(jnp.float32)
        sums.append(total)
    return jnp.concatenate(sums, axis=0)


def split_columns(weight, groups, size):
    rows = weight.shape[0]
    width = weight.shape[1] // (groups * size)
    pieces = weight.reshape(rows, groups, size, width).transpose(2, 0, 1, 3)
    pieces = pieces.reshape(size, rows, groups * width)
    pieces = lax.all_to_all(pieces, "ctx", split_axis=0, concat_axis=0, tiled=True)
    whole = lax.all_gather(pieces, "fsdp", axis=0, tiled=False)
    return whole.transpose(1, 0, 2, 3).reshape(-1, groups * width)


def merge_columns(grad, groups, size, fsdp_size):
    width = grad.shape[1] // groups
    rows = grad.shape[0] // (size * fsdp_size)
    pieces = grad.reshape(size, fsdp_size, rows, groups * width).transpose(1, 0, 2, 3)
    pieces = pieces.astype(jnp.bfloat16).reshape(grad.shape)
    pieces = lax.psum_scatter(pieces, "fsdp", scatter_dimension=0, tiled=True)
    pieces = pieces.reshape(size, rows, groups * width)
    pieces = lax.all_to_all(pieces, "ctx", split_axis=0, concat_axis=0, tiled=True)
    pieces = pieces.reshape(size, rows, groups, width).transpose(1, 2, 0, 3)
    return pieces.reshape(rows, groups * size * width).astype(jnp.float32)


def local_split(
    ctx_size,
    fsdp_size,
    tokens,
    segments,
    routes,
    cotangent,
    w_qkv,
    b_qkv,
    w_out,
    gain_attn,
    gain_ffn,
    w_router,
    w_shared_gate,
    w_shared_in,
    w_shared_out,
    w_expert_in,
    w_expert_out,
):
    bf16, f32, i32 = jnp.bfloat16, jnp.float32, jnp.int32
    axes = ("ctx", "fsdp")
    device_count = ctx_size * fsdp_size
    block_len = tokens.shape[2]
    width = tokens.shape[3]
    token_count = 2 * block_len
    top_count = routes.shape[3]
    seq_len = token_count * ctx_size
    ctx_index = lax.axis_index("ctx")
    expert_count = w_router.shape[1]
    capacity = token_count * top_count // expert_count
    own_heads = HEADS // ctx_size
    own_width = own_heads * HD
    fs_own = FS // ctx_size
    score_scale = HD ** (-0.5)

    def dot(a, b):
        return jnp.dot(a, b, preferred_element_type=f32)

    def dot_t(a, b):
        return lax.dot_general(a, b, (((1,), (1,)), ((), ())), preferred_element_type=f32)

    def t_dot(a, b):
        return lax.dot_general(a, b, (((0,), (0,)), ((), ())), preferred_element_type=f32)

    def own_rows(values):
        return lax.dynamic_index_in_dim(
            values.reshape((ctx_size, token_count) + values.shape[1:]), ctx_index, 0, keepdims=False
        )

    small = jnp.concatenate(
        [gain_attn, gain_ffn, w_shared_gate, w_router.reshape(-1), b_qkv], axis=0
    )
    small = lax.all_gather(small, axes, axis=0, tiled=False)
    shard = width // device_count
    attn_gain = small[:, :shard].reshape(width).astype(f32)
    ffn_gain = small[:, shard : 2 * shard].reshape(width).astype(f32)
    gate_vector = small[:, 2 * shard : 3 * shard].reshape(width)
    router_end = 3 * shard + shard * expert_count
    router_weight = small[:, 3 * shard : router_end].reshape(width, expert_count)
    bias = small[:, router_end:].reshape(3, ctx_size, own_width).astype(f32)
    bias = lax.dynamic_index_in_dim(bias, ctx_index, 1, keepdims=False).reshape(3 * own_width)

    token_rows = ring_gather(tokens.reshape(token_count, width), ctx_size, ctx_index)
    token_rows = token_rows.reshape(seq_len, width)
    qkv_weight = split_columns(w_qkv, 3, ctx_size)
    out_weight = lax.all_gather(w_out, axes, axis=0, tiled=True)
    shared_in = split_columns(w_shared_in, 2, ctx_size)
    shared_out = lax.all_gather(w_shared_out, "fsdp", axis=0, tiled=True)
    expert_in = lax.all_gather(w_expert_in[0], "fsdp", axis=0, tiled=True)
    expert_out = lax.all_gather(w_expert_out[0], "fsdp", axis=0, tiled=True)
    route_rows = lax.all_gather(
        routes.reshape(token_count, top_count), "ctx", axis=0, tiled=False
    )
    grad_rows = ring_gather(cotangent.reshape(token_count, width), ctx_size, ctx_index)
    grad_rows = grad_rows.reshape(seq_len, width)

    block_ids = jnp.arange(ctx_size, dtype=i32)[:, None]
    local_index = jnp.arange(block_len, dtype=i32)[None, :]
    positions = jnp.stack(
        [
            block_ids * block_len + local_index,
            seq_len - (block_ids + 1) * block_len + local_index,
        ],
        axis=1,
    ).reshape(seq_len)
    seg_rows = (
        segments.reshape(2, ctx_size, block_len).transpose(1, 0, 2).reshape(seq_len)
    )
    cos_tab, sine_tab = rope_tables(positions, HD)

    inputs = token_rows.astype(f32)
    normed, inv_one_all = rms_norm(inputs, attn_gain)
    normed_low = normed.astype(bf16)
    projected = dot(normed_low, qkv_weight) + bias
    head_shape = (seq_len, own_heads, HD)
    queries = rotate(projected[:, :own_width].reshape(head_shape), cos_tab, sine_tab).astype(bf16)
    keys = rotate(
        projected[:, own_width : 2 * own_width].reshape(head_shape), cos_tab, sine_tab
    ).astype(bf16)
    values = projected[:, 2 * own_width :].reshape(head_shape).astype(bf16)
    allowed = (positions[None, :] <= positions[:, None]) & (seg_rows[None, :] == seg_rows[:, None])
    scores = jnp.einsum("qhd,khd->hqk", queries, keys, preferred_element_type=f32) * score_scale
    scores = jnp.where(allowed[None], scores, MASK_FILL)
    top_score = jnp.max(scores, axis=-1, keepdims=True)
    log_total = top_score + jnp.log(jnp.sum(jnp.exp(scores - top_score), axis=-1, keepdims=True))
    weights = jnp.exp(scores - log_total)
    weights_low = weights.astype(bf16)
    attended = jnp.einsum("hqk,khd->qhd", weights_low, values, preferred_element_type=f32)
    attn_own = attended.astype(bf16).reshape(seq_len, own_width)
    attn_all = ring_gather(attn_own, ctx_size, ctx_index)
    attn_rows = attn_all.transpose(1, 0, 2).reshape(seq_len, width)
    residual = inputs + dot(attn_rows, out_weight)

    normed_two, inv_two_all = rms_norm(residual, ffn_gain)
    low_two = normed_two.astype(bf16)
    mixed_weight = jnp.concatenate([router_weight, gate_vector[:, None]], axis=1)
    logits = dot(low_two, mixed_weight)
    probs_all = jax.nn.softmax(logits[:, :expert_count], axis=-1)
    scale_all = jax.nn.sigmoid(logits[:, expert_count])
    gate_all = lax.dynamic_index_in_dim(probs_all, ctx_index, 1, keepdims=False)
    shared_pre = dot(low_two, shared_in)
    shared_hid = swiglu(shared_pre, fs_own).astype(bf16)
    shared_res = dot(shared_hid, shared_out)

    named = jnp.any(route_rows == ctx_index, axis=-1)
    before = jnp.arange(token_count)[:, None] < jnp.arange(token_count)[None, :]
    rank = dot(named.astype(bf16), before.astype(bf16)).astype(i32)
    slot_of = jnp.where(named & (rank < capacity), rank, -1)
    slot_mask = slot_of[:, None, :] == jnp.arange(capacity, dtype=i32)[None, :, None]
    slot_map = slot_mask.astype(bf16)
    blocks_two = low_two.reshape(ctx_size, token_count, width)
    blocks_grad = grad_rows.reshape(ctx_size, token_count, width)
    gate_blocks = gate_all.reshape(ctx_size, token_count)

    def to_slots(blocks):
        picked = jnp.einsum("bmt,btd->bmd", slot_map, blocks, preferred_element_type=f32)
        return picked.reshape(ctx_size * capacity, width)

    def to_tokens(slots):
        spread = jnp.einsum(
            "bmt,bmd->btd",
            slot_map,
            slots.reshape(ctx_size, capacity, width),
            preferred_element_type=f32,
        )
        return spread.reshape(seq_len, width)

    buffer = to_slots(blocks_two).astype(bf16)
    expert_pre = dot(buffer, expert_in)
    expert_hid = swiglu(expert_pre, FE).astype(bf16)
    expert_res = dot(expert_hid, expert_out).astype(bf16)
    routed = gate_all[:, None] * to_tokens(expert_res)
    out_parts = (scale_all[:, None] * shared_res + routed).astype(bf16)
    out_sum = ring_scatter(
        out_parts.reshape(ctx_size, token_count, width), ctx_size, ctx_index
    )
    own_residual = own_rows(residual)
    output = (own_residual + out_sum).astype(bf16).reshape(tokens.shape)

    grad_slots = to_slots(blocks_grad)
    gate_slots = jnp.sum(jnp.where(slot_mask, gate_blocks[:, None, :], 0.0), axis=-1).reshape(-1, 1)
    grad_res = (gate_slots * grad_slots).astype(bf16)
    slot_dots = jnp.sum(grad_slots * expert_res.astype(f32), axis=-1).reshape(ctx_size, capacity, 1)
    grad_gates = jnp.sum(jnp.where(slot_mask, slot_dots, 0.0), axis=1)
    grad_expert_out = t_dot(expert_hid, grad_res)
    grad_hid = dot_t(grad_res, expert_out)
    grad_pre = swiglu_back(expert_pre, FE, grad_hid).astype(bf16)
    grad_expert_in = t_dot(buffer, grad_pre)
    grad_buffer = dot_t(grad_pre, expert_in).astype(bf16)

    grad_f32 = grad_rows.astype(f32)
    grad_shared_res = (scale_all[:, None] * grad_f32).astype(bf16)
    gate_dots = jnp.sum(grad_f32 * shared_res, axis=-1).reshape(ctx_size, token_count)
    grad_shared_out = t_dot(shared_hid, grad_shared_res)
    grad_shared_hid = dot_t(grad_shared_res, shared_out)
    grad_shared_pre = swiglu_back(shared_pre, fs_own, grad_shared_hid).astype(bf16)
    grad_shared_in = t_dot(low_two, grad_shared_pre)
    two_parts = (dot_t(grad_shared_pre, shared_in) + to_tokens(grad_buffer)).astype(bf16)
    grad_two = ring_scatter(
        two_parts.reshape(ctx_size, token_count, width), ctx_size, ctx_index
    )

    dots = jnp.stack([grad_gates, gate_dots], axis=1)
    dots = lax.all_to_all(dots, "ctx", split_axis=0, concat_axis=0, tiled=True)
    own_probs = own_rows(probs_all)
    own_scale = own_rows(scale_all)
    own_low = own_rows(low_two)
    own_chosen = routes.reshape(token_count, top_count)
    chosen_mask = jnp.any(
        own_chosen[..., None] == jnp.arange(expert_count, dtype=i32), axis=1
    )
    grad_probs = jnp.where(chosen_mask, dots[:, 0].T, 0.0)
    grad_logits = (
        own_probs * (grad_probs - jnp.sum(own_probs * grad_probs, axis=-1, keepdims=True))
    ).astype(bf16)
    grad_gate_pre = (jnp.sum(dots[:, 1], axis=0) * own_scale * (1.0 - own_scale)).astype(bf16)
    grad_router = t_dot(own_low, grad_logits)
    grad_gate_vector = t_dot(own_low, grad_gate_pre[:, None])
    grad_two = grad_two + dot_t(grad_logits, router_weight)
    grad_two = grad_two + grad_gate_pre.astype(f32)[:, None] * gate_vector.astype(f32)[None, :]
    grad_resid_norm, grad_gain_two = rms_back(
        own_residual, own_rows(inv_two_all), ffn_gain, grad_two
    )
    grad_resid = cotangent.reshape(token_count, width).astype(f32) + grad_resid_norm

    grad_mixed = grad_resid.astype(bf16)
    grad_attn_rows = dot_t(grad_mixed, out_weight).astype(bf16)
    grad_attn = lax.all_to_all(
        grad_attn_rows.reshape(token_count, ctx_size, own_width).transpose(1, 0, 2),
        "ctx",
        split_axis=0,
        concat_axis=0,
        tiled=True,
    ).reshape(head_shape)
    mixed_all = ring_gather(grad_mixed, ctx_size, ctx_index).reshape(seq_len, width)
    grad_out_weight = t_dot(attn_own, mixed_all)
    grad_weights = jnp.einsum("qhd,khd->hqk", grad_attn, values, preferred_element_type=f32)
    delta = jnp.sum(weights * grad_weights, axis=-1, keepdims=True)
    grad_scores = jnp.where(allowed[None], weights * (grad_weights - delta), 0.0).astype(bf16)
    grad_q = jnp.einsum("hqk,khd->qhd", grad_scores, keys, preferred_element_type=f32) * score_scale
    grad_k = (
        jnp.einsum("hqk,qhd->khd", grad_scores, queries, preferred_element_type=f32) * score_scale
    )
    grad_v = jnp.einsum("hqk,qhd->khd", weights_low, grad_attn, preferred_element_type=f32)
    grad_projected = jnp.concatenate(
        [
            rotate_back(grad_q, cos_tab, sine_tab).reshape(seq_len, own_width),
            rotate_back(grad_k, cos_tab, sine_tab).reshape(seq_len, own_width),
            grad_v.reshape(seq_len, own_width),
        ],
        axis=-1,
    ).astype(bf16)
    one_parts = dot_t(grad_projected, qkv_weight).astype(bf16)
    grad_normed = ring_scatter(
        one_parts.reshape(ctx_size, token_count, width), ctx_size, ctx_index
    )
    grad_inputs_norm, grad_gain_one = rms_back(
        tokens.reshape(token_count, width).astype(f32),
        own_rows(inv_one_all),
        attn_gain,
        grad_normed,
    )
    grad_tokens = (grad_resid + grad_inputs_norm).reshape(tokens.shape)
    grad_qkv_weight = t_dot(normed_low, grad_projected)
    grad_bias = jnp.sum(grad_projected.astype(f32), axis=0).reshape(3, 1, own_width)
    grad_bias = jnp.where(
        jnp.arange(ctx_size, dtype=i32)[None, :, None] == ctx_index, grad_bias, 0.0
    )

    def sum_rows(grad):
        return lax.psum_scatter(
            grad.astype(bf16), "fsdp", scatter_dimension=0, tiled=True
        ).astype(f32)

    small_grads = jnp.concatenate(
        [
            piece.reshape(device_count, -1)
            for piece in (grad_gain_one, grad_gain_two, grad_gate_vector, grad_router, grad_bias)
        ],
        axis=1,
    )
    small_grads = lax.psum_scatter(small_grads, axes, scatter_dimension=0, tiled=False)
    return (
        output,
        grad_tokens,
        merge_columns(grad_qkv_weight, 3, ctx_size, fsdp_size),
        small_grads[router_end:],
        sum_rows(grad_out_weight),
        small_grads[:shard],
        small_grads[shard : 2 * shard],
        small_grads[3 * shard : router_end].reshape(shard, expert_count),
        small_grads[2 * shard : 3 * shard],
        merge_columns(grad_shared_in, 2, ctx_size, fsdp_size),
        sum_rows(grad_shared_out),
        sum_rows(grad_expert_in)[None],
        sum_rows(grad_expert_out)[None],
    )


def local_wide(
    tokens,
    segments,
    routes,
    cotangent,
    w_qkv,
    b_qkv,
    w_out,
    gain_attn,
    gain_ffn,
    w_router,
    w_shared_gate,
    w_shared_in,
    w_shared_out,
    w_expert_in,
    w_expert_out,
):
    block_len = tokens.shape[2]
    model_width = tokens.shape[3]
    token_count = 2 * block_len
    top_count = routes.shape[3]
    half_len = segments.shape[2]
    seq_len = 2 * half_len
    ctx_index = lax.axis_index("ctx")
    head_count = model_width // HD
    expert_count = w_router.shape[1]
    capacity = token_count * top_count // expert_count
    slot_count = expert_count * capacity
    key_rows = min(512, seq_len)
    key_blocks = seq_len // key_rows
    score_scale = HD ** (-0.5)
    head_shape = (token_count, head_count, HD)
    attn_set = (
        lax.all_gather(w_qkv, ("ctx", "fsdp"), axis=0, tiled=True),
        lax.all_gather(b_qkv, ("ctx", "fsdp"), axis=0, tiled=True),
        lax.all_gather(w_out, ("ctx", "fsdp"), axis=0, tiled=True),
        lax.all_gather(gain_attn, ("ctx", "fsdp"), axis=0, tiled=True),
    )
    qkv_weight, qkv_bias, out_weight, attn_gain = attn_set
    inputs = tokens.reshape(token_count, model_width).astype(jnp.float32)
    normed, inv_one = rms_norm(inputs, attn_gain.astype(jnp.float32))
    normed_low = normed.astype(jnp.bfloat16)
    projected = jnp.dot(
        normed_low, qkv_weight, preferred_element_type=jnp.float32
    ) + qkv_bias.astype(jnp.float32)
    local_index = jnp.arange(block_len, dtype=jnp.int32)
    query_pos = jnp.concatenate(
        [ctx_index * block_len + local_index, seq_len - (ctx_index + 1) * block_len + local_index]
    )
    half_index = jnp.arange(half_len, dtype=jnp.int32)
    key_pos = jnp.concatenate(
        [half_index, seq_len - block_len * (half_index // block_len + 1) + half_index % block_len]
    ).reshape(key_blocks, key_rows)
    key_seg = segments.reshape(key_blocks, key_rows)
    query_seg = lax.dynamic_slice_in_dim(segments[0], ctx_index * block_len, block_len, 1).reshape(
        token_count
    )
    cos_tab, sine_tab = rope_tables(query_pos, HD)
    queries = rotate(projected[:, :model_width].reshape(head_shape), cos_tab, sine_tab).astype(
        jnp.bfloat16
    )
    keys_own = rotate(
        projected[:, model_width : 2 * model_width].reshape(head_shape), cos_tab, sine_tab
    ).astype(jnp.bfloat16)
    values_own = projected[:, 2 * model_width :].astype(jnp.bfloat16)
    keys_all, values_all = (
        lax.all_gather(keys_own.reshape(2, block_len, model_width), "ctx", axis=1, tiled=True),
        lax.all_gather(values_own.reshape(2, block_len, model_width), "ctx", axis=1, tiled=True),
    )
    keys_all = keys_all.reshape(key_blocks, key_rows, head_count, HD)
    values_all = values_all.reshape(key_blocks, key_rows, head_count, HD)

    def score_block(key_blk, pos_blk, seg_blk):
        raw_scores = (
            jnp.einsum("qhd,khd->hqk", queries, key_blk, preferred_element_type=jnp.float32)
            * score_scale
        )
        allowed = (pos_blk[None, :] <= query_pos[:, None]) & (
            seg_blk[None, :] == query_seg[:, None]
        )
        return (jnp.where(allowed[None], raw_scores, MASK_FILL), allowed)

    def total_step(running, key_part):
        run_max, run_sum = running
        scores = score_block(key_part[0], key_part[1], key_part[2])[0]
        new_max = jnp.maximum(run_max, jnp.max(scores, axis=-1))
        run_sum = run_sum * jnp.exp(run_max - new_max) + jnp.sum(
            jnp.exp(scores - new_max[..., None]), axis=-1
        )
        return ((new_max, run_sum), None)

    start_max = jnp.full((head_count, token_count), MASK_FILL, jnp.float32)
    start_sum = jnp.zeros((head_count, token_count), jnp.float32)
    (run_max, run_sum), unused = lax.scan(
        total_step, (start_max, start_sum), (keys_all, key_pos, key_seg)
    )
    log_total = run_max + jnp.log(run_sum)

    def attend_step(summed, key_part):
        key_blk, value_blk, pos_blk, seg_blk = key_part
        scores = score_block(key_blk, pos_blk, seg_blk)[0]
        weights = jnp.exp(scores - log_total[..., None]).astype(jnp.bfloat16)
        return (
            summed
            + jnp.einsum("hqk,khd->qhd", weights, value_blk, preferred_element_type=jnp.float32),
            None,
        )

    key_stack = (keys_all, values_all, key_pos, key_seg)
    attended, unused = lax.scan(attend_step, jnp.zeros(head_shape, jnp.float32), key_stack)
    attn_low = attended.reshape(token_count, model_width).astype(jnp.bfloat16)
    residual = inputs + jnp.dot(attn_low, out_weight, preferred_element_type=jnp.float32)
    ffn_set = (
        lax.all_gather(gain_ffn, ("ctx", "fsdp"), axis=0, tiled=True),
        lax.all_gather(w_router, ("ctx", "fsdp"), axis=0, tiled=True),
        lax.all_gather(w_shared_gate, ("ctx", "fsdp"), axis=0, tiled=True),
        lax.all_gather(w_shared_in, ("ctx", "fsdp"), axis=0, tiled=True),
        lax.all_gather(w_shared_out, ("ctx", "fsdp"), axis=0, tiled=True),
    )
    ffn_gain, router_weight, gate_vector, shared_in, shared_out = ffn_set
    normed_two, inv_two = rms_norm(residual, ffn_gain.astype(jnp.float32))
    low_two = normed_two.astype(jnp.bfloat16)
    logits = jnp.dot(low_two, router_weight, preferred_element_type=jnp.float32)
    router_probs = jax.nn.softmax(logits, axis=-1)
    chosen = routes.reshape(token_count, top_count)
    chosen_mask = chosen[..., None] == jnp.arange(expert_count, dtype=jnp.int32)
    gate_vals = jnp.sum(jnp.where(chosen_mask, router_probs[:, None, :], 0.0), axis=-1)
    shared_scale = jax.nn.sigmoid(jnp.dot(low_two, gate_vector, preferred_element_type=jnp.float32))
    shared_pre = jnp.dot(low_two, shared_in, preferred_element_type=jnp.float32)
    shared_hid = swiglu(shared_pre, FS).astype(jnp.bfloat16)
    shared_res = jnp.dot(shared_hid, shared_out, preferred_element_type=jnp.float32)
    pair_routes = chosen.reshape(token_count * top_count)
    expert_marks = (
        pair_routes[:, None] == jnp.arange(expert_count, dtype=jnp.int32)[None, :]
    ).astype(jnp.int32)
    pair_ranks = jnp.sum((jnp.cumsum(expert_marks, axis=0) - expert_marks) * expert_marks, axis=1)
    pair_target = jnp.where(pair_ranks < capacity, pair_routes * capacity + pair_ranks, -1)
    pair_map = pair_target[:, None] == jnp.arange(slot_count, dtype=jnp.int32)[None, :]
    pair_low = pair_map.astype(jnp.bfloat16)
    token_map = jnp.sum(
        pair_map.reshape(token_count, top_count, slot_count).astype(jnp.int32), axis=1
    ).astype(jnp.bfloat16)
    outgoing = jnp.einsum(
        "tc,td->cd", token_map, low_two, preferred_element_type=jnp.float32
    ).astype(jnp.bfloat16)
    incoming = lax.all_to_all(
        outgoing.reshape(expert_count, capacity, model_width),
        "ctx",
        split_axis=0,
        concat_axis=1,
        tiled=True,
    )
    expert_in, expert_out = (
        lax.all_gather(w_expert_in, "fsdp", axis=1, tiled=True),
        lax.all_gather(w_expert_out, "fsdp", axis=1, tiled=True),
    )
    expert_pre = jnp.einsum("erd,edf->erf", incoming, expert_in, preferred_element_type=jnp.float32)
    expert_hid = swiglu(expert_pre, FE).astype(jnp.bfloat16)
    expert_res = jnp.einsum(
        "erf,efd->erd", expert_hid, expert_out, preferred_element_type=jnp.float32
    ).astype(jnp.bfloat16)
    returned = lax.all_to_all(expert_res, "ctx", split_axis=1, concat_axis=0, tiled=True).reshape(
        slot_count, model_width
    )
    pair_vals = jnp.dot(pair_low, returned, preferred_element_type=jnp.float32).reshape(
        token_count, top_count, model_width
    )
    routed = jnp.sum(gate_vals[..., None] * pair_vals, axis=1)
    output = (
        (residual + shared_scale[:, None] * shared_res + routed)
        .astype(jnp.bfloat16)
        .reshape(tokens.shape)
    )
    grad_out = cotangent.reshape(token_count, model_width).astype(jnp.float32)
    pair_grads = gate_vals[..., None] * grad_out[:, None, :]
    grad_gates = jnp.sum(grad_out[:, None, :] * pair_vals, axis=-1)
    grad_returned = jnp.einsum(
        "pc,pd->cd",
        pair_map.astype(jnp.float32),
        pair_grads.reshape(token_count * top_count, model_width),
        precision=HIGHEST,
    ).astype(jnp.bfloat16)
    grad_res = lax.all_to_all(
        grad_returned.reshape(expert_count, capacity, model_width),
        "ctx",
        split_axis=0,
        concat_axis=1,
        tiled=True,
    )
    grad_expert_out = jnp.einsum(
        "erf,erd->efd", expert_hid, grad_res, preferred_element_type=jnp.float32
    )
    grad_hid = jnp.einsum("erd,efd->erf", grad_res, expert_out, preferred_element_type=jnp.float32)
    grad_pre = swiglu_back(expert_pre, FE, grad_hid).astype(jnp.bfloat16)
    grad_expert_in = jnp.einsum(
        "erd,erf->edf", incoming, grad_pre, preferred_element_type=jnp.float32
    )
    grad_incoming = jnp.einsum(
        "erf,edf->erd", grad_pre, expert_in, preferred_element_type=jnp.float32
    ).astype(jnp.bfloat16)
    grad_outgoing = lax.all_to_all(
        grad_incoming, "ctx", split_axis=1, concat_axis=0, tiled=True
    ).reshape(slot_count, model_width)
    expert_grads = (
        lax.psum_scatter(
            grad_expert_in.astype(jnp.bfloat16), "fsdp", scatter_dimension=1, tiled=True
        ).astype(jnp.float32),
        lax.psum_scatter(
            grad_expert_out.astype(jnp.bfloat16), "fsdp", scatter_dimension=1, tiled=True
        ).astype(jnp.float32),
    )
    grad_two = jnp.einsum("tc,cd->td", token_map, grad_outgoing, preferred_element_type=jnp.float32)
    grad_probs = jnp.sum(jnp.where(chosen_mask, grad_gates[..., None], 0.0), axis=1)
    grad_logits = (
        router_probs * (grad_probs - jnp.sum(router_probs * grad_probs, axis=-1, keepdims=True))
    ).astype(jnp.bfloat16)
    grad_router = jnp.einsum("td,te->de", low_two, grad_logits, preferred_element_type=jnp.float32)
    grad_shared_res = (shared_scale[:, None] * grad_out).astype(jnp.bfloat16)
    grad_gate_pre = (
        jnp.sum(grad_out * shared_res, axis=-1) * shared_scale * (1.0 - shared_scale)
    ).astype(jnp.bfloat16)
    grad_shared_out = jnp.einsum(
        "tf,td->fd", shared_hid, grad_shared_res, preferred_element_type=jnp.float32
    )
    grad_shared_hid = jnp.einsum(
        "td,fd->tf", grad_shared_res, shared_out, preferred_element_type=jnp.float32
    )
    grad_shared_pre = swiglu_back(shared_pre, FS, grad_shared_hid).astype(jnp.bfloat16)
    grad_shared_in = jnp.einsum(
        "td,tf->df", low_two, grad_shared_pre, preferred_element_type=jnp.float32
    )
    grad_gate_vector = jnp.einsum(
        "td,t->d", low_two, grad_gate_pre, preferred_element_type=jnp.float32
    )
    grad_two = grad_two + jnp.einsum(
        "te,de->td", grad_logits, router_weight, preferred_element_type=jnp.float32
    )
    grad_two = grad_two + jnp.einsum(
        "tf,df->td", grad_shared_pre, shared_in, preferred_element_type=jnp.float32
    )
    grad_two = (
        grad_two
        + grad_gate_pre.astype(jnp.float32)[:, None] * gate_vector.astype(jnp.float32)[None, :]
    )
    grad_resid_norm, grad_gain_two = rms_back(
        residual, inv_two, ffn_gain.astype(jnp.float32), grad_two
    )
    grad_resid = grad_out + grad_resid_norm
    ffn_grads = (
        lax.psum_scatter(grad_gain_two, ("ctx", "fsdp"), scatter_dimension=0, tiled=True),
        lax.psum_scatter(grad_router, ("ctx", "fsdp"), scatter_dimension=0, tiled=True),
        lax.psum_scatter(grad_gate_vector, ("ctx", "fsdp"), scatter_dimension=0, tiled=True),
        lax.psum_scatter(grad_shared_in, ("ctx", "fsdp"), scatter_dimension=0, tiled=True),
        lax.psum_scatter(grad_shared_out, ("ctx", "fsdp"), scatter_dimension=0, tiled=True),
    )
    grad_mixed = grad_resid.astype(jnp.bfloat16)
    grad_out_weight = jnp.einsum(
        "tc,td->cd", attn_low, grad_mixed, preferred_element_type=jnp.float32
    )
    grad_attn = (
        jnp.einsum("td,cd->tc", grad_mixed, out_weight, preferred_element_type=jnp.float32)
        .astype(jnp.bfloat16)
        .reshape(head_shape)
    )

    def delta_step(summed, key_part):
        key_blk, value_blk, pos_blk, seg_blk = key_part
        weights = jnp.exp(score_block(key_blk, pos_blk, seg_blk)[0] - log_total[..., None])
        grad_weights = jnp.einsum(
            "qhd,khd->hqk", grad_attn, value_blk, preferred_element_type=jnp.float32
        )
        return (summed + jnp.sum(weights * grad_weights, axis=-1), None)

    delta_sum, unused = lax.scan(
        delta_step, jnp.zeros((head_count, token_count), jnp.float32), key_stack
    )

    def grad_step(summed, key_part):
        key_blk, value_blk, pos_blk, seg_blk = key_part
        scores, allowed = score_block(key_blk, pos_blk, seg_blk)
        weights = jnp.exp(scores - log_total[..., None])
        grad_weights = jnp.einsum(
            "qhd,khd->hqk", grad_attn, value_blk, preferred_element_type=jnp.float32
        )
        grad_scores = jnp.where(
            allowed[None], weights * (grad_weights - delta_sum[..., None]), 0.0
        ).astype(jnp.bfloat16)
        summed = (
            summed
            + jnp.einsum("hqk,khd->qhd", grad_scores, key_blk, preferred_element_type=jnp.float32)
            * score_scale
        )
        grad_key = (
            jnp.einsum("hqk,qhd->khd", grad_scores, queries, preferred_element_type=jnp.float32)
            * score_scale
        )
        grad_value = jnp.einsum(
            "hqk,qhd->khd",
            weights.astype(jnp.bfloat16),
            grad_attn,
            preferred_element_type=jnp.float32,
        )
        return (summed, (grad_key, grad_value))

    grad_query, (grad_keys, grad_values) = lax.scan(
        grad_step, jnp.zeros(head_shape, jnp.float32), key_stack
    )
    grad_keys_own, grad_values_own = (
        lax.psum_scatter(
            grad_keys.reshape(2, half_len, model_width).astype(jnp.bfloat16),
            "ctx",
            scatter_dimension=1,
            tiled=True,
        ).astype(jnp.float32),
        lax.psum_scatter(
            grad_values.reshape(2, half_len, model_width).astype(jnp.bfloat16),
            "ctx",
            scatter_dimension=1,
            tiled=True,
        ).astype(jnp.float32),
    )
    grad_q_rows = rotate_back(grad_query, cos_tab, sine_tab).reshape(token_count, model_width)
    grad_k_rows = rotate_back(grad_keys_own.reshape(head_shape), cos_tab, sine_tab).reshape(
        token_count, model_width
    )
    grad_projected = jnp.concatenate(
        [grad_q_rows, grad_k_rows, grad_values_own.reshape(token_count, model_width)], axis=-1
    ).astype(jnp.bfloat16)
    grad_qkv_weight = jnp.einsum(
        "td,te->de", normed_low, grad_projected, preferred_element_type=jnp.float32
    )
    grad_qkv_bias = jnp.sum(grad_projected.astype(jnp.float32), axis=0)
    grad_normed = jnp.einsum(
        "te,de->td", grad_projected, qkv_weight, preferred_element_type=jnp.float32
    )
    grad_inputs_norm, grad_gain_one = rms_back(
        inputs, inv_one, attn_gain.astype(jnp.float32), grad_normed
    )
    grad_tokens = (grad_resid + grad_inputs_norm).reshape(tokens.shape)
    attn_grads = (
        lax.psum_scatter(grad_qkv_weight, ("ctx", "fsdp"), scatter_dimension=0, tiled=True),
        lax.psum_scatter(grad_qkv_bias, ("ctx", "fsdp"), scatter_dimension=0, tiled=True),
        lax.psum_scatter(grad_out_weight, ("ctx", "fsdp"), scatter_dimension=0, tiled=True),
        lax.psum_scatter(grad_gain_one, ("ctx", "fsdp"), scatter_dimension=0, tiled=True),
    )
    return (
        output,
        grad_tokens,
        attn_grads[0],
        attn_grads[1],
        attn_grads[2],
        attn_grads[3],
        ffn_grads[0],
        ffn_grads[1],
        ffn_grads[2],
        ffn_grads[3],
        ffn_grads[4],
        expert_grads[0],
        expert_grads[1],
    )


def solution(mesh):
    in_specs = (
        P("fsdp", None, "ctx", None),
        P("fsdp", None, None),
        P("fsdp", None, "ctx", None),
        P("fsdp", None, "ctx", None),
        P(("ctx", "fsdp"), None),
        P(("ctx", "fsdp")),
        P(("ctx", "fsdp"), None),
        P(("ctx", "fsdp")),
        P(("ctx", "fsdp")),
        P(("ctx", "fsdp"), None),
        P(("ctx", "fsdp")),
        P(("ctx", "fsdp"), None),
        P(("ctx", "fsdp"), None),
        P("ctx", "fsdp", None),
        P("ctx", "fsdp", None),
    )
    out_specs = (
        P("fsdp", None, "ctx", None),
        P("fsdp", None, "ctx", None),
        P(("ctx", "fsdp"), None),
        P(("ctx", "fsdp")),
        P(("ctx", "fsdp"), None),
        P(("ctx", "fsdp")),
        P(("ctx", "fsdp")),
        P(("ctx", "fsdp"), None),
        P(("ctx", "fsdp")),
        P(("ctx", "fsdp"), None),
        P(("ctx", "fsdp"), None),
        P("ctx", "fsdp", None),
        P("ctx", "fsdp", None),
    )
    ctx_size = mesh.shape["ctx"]
    fsdp_size = mesh.shape["fsdp"]

    def local(*arrays):
        if HEADS % ctx_size:
            return local_wide(*arrays)
        return local_split(ctx_size, fsdp_size, *arrays)

    return jax.shard_map(local, mesh=mesh, in_specs=in_specs, out_specs=out_specs, check_vma=False)
```

```python
import jax
import jax.numpy as jnp
from jax import lax
from jax.sharding import PartitionSpec as P

HD = 128
HEADS = 16
FS = 5632
FE = 1408


RMS_EPS = 1e-06
ROPE_THETA = 1000000.0
MASK_FILL = -1e30
HIGHEST = lax.Precision.HIGHEST


def rope_tables(positions, head_dim):
    half_dim = head_dim // 2
    inv_freq = ROPE_THETA ** (-(jnp.arange(half_dim, dtype=jnp.float32) * 2.0 / head_dim))
    angles = positions.astype(jnp.float32)[:, None] * inv_freq[None, :]
    cos_tab = jnp.concatenate([jnp.cos(angles), jnp.cos(angles)], axis=-1)
    sine_tab = jnp.concatenate([jnp.sin(angles), jnp.sin(angles)], axis=-1)
    return (cos_tab, sine_tab)


def rotate(values, cos_tab, sine_tab):
    half_dim = values.shape[-1] // 2
    turned = jnp.concatenate([-values[..., half_dim:], values[..., :half_dim]], axis=-1)
    return values * cos_tab[:, None, :] + turned * sine_tab[:, None, :]


def rotate_back(upstream, cos_tab, sine_tab):
    half_dim = upstream.shape[-1] // 2
    scaled = upstream * sine_tab[:, None, :]
    return upstream * cos_tab[:, None, :] + jnp.concatenate(
        [scaled[..., half_dim:], -scaled[..., :half_dim]], axis=-1
    )


def rms_norm(values, gain_vec):
    inv_rms = lax.rsqrt(jnp.mean(values * values, axis=-1, keepdims=True) + RMS_EPS)
    return (values * inv_rms * gain_vec, inv_rms)


def rms_back(values, inv_rms, gain_vec, upstream):
    weighted = upstream * gain_vec
    inner_mean = jnp.mean(weighted * values, axis=-1, keepdims=True)
    return (
        inv_rms * weighted - values * inv_rms * inv_rms * inv_rms * inner_mean,
        jnp.sum(upstream * values * inv_rms, axis=0),
    )


def swiglu(pre_act, split_at):
    return jax.nn.silu(pre_act[..., :split_at]) * pre_act[..., split_at:]


def swiglu_back(pre_act, split_at, upstream):
    gate_part = pre_act[..., :split_at]
    up_part = pre_act[..., split_at:]
    sigmoid_g = jax.nn.sigmoid(gate_part)
    d_gate = upstream * up_part * sigmoid_g * (1.0 + gate_part * (1.0 - sigmoid_g))
    d_up = upstream * gate_part * sigmoid_g
    return jnp.concatenate([d_gate, d_up], axis=-1)


def ring_order(size):
    return list(range(0, size, 2)) + list(range(size - 1, 0, -2))


def ring_steps(size):
    order = ring_order(size)
    ahead = [(order[i], order[(i + 1) % size]) for i in range(size)]
    back = [(dst, src) for src, dst in ahead]
    return (ahead, back)


def ring_peers(size, ctx_index):
    order = ring_order(size)
    place = {dev: i for i, dev in enumerate(order)}
    table = jnp.array(
        [[order[(place[dev] + k) % size] for k in range(size)] for dev in range(size)], jnp.int32
    )
    row = lax.dynamic_index_in_dim(table, ctx_index, 0, keepdims=False)
    return [row[k] for k in range(size)]


def ring_walk(block, size, ctx_index, out, put):
    rows = block.shape[0]
    ahead, back = ring_steps(size)
    peers = ring_peers(size, ctx_index)
    half = size // 2
    out = put(out, block, ctx_index, 0)
    fore = rear = block
    for k in range(1, half):
        fore = lax.ppermute(fore, "ctx", ahead)
        rear = lax.ppermute(rear, "ctx", back)
        out = put(out, fore, peers[size - k], 0)
        out = put(out, rear, peers[k], 0)
    fore = lax.ppermute(fore[: rows // 2], "ctx", ahead)
    rear = lax.ppermute(rear[rows // 2 :], "ctx", back)
    out = put(out, fore, peers[half], 0)
    return put(out, rear, peers[half], rows // 2)


def ring_gather(block, size, ctx_index):
    rows, width = block.shape

    def put(out, piece, peer, offset):
        return lax.dynamic_update_slice(out, piece, (peer * rows + offset, jnp.zeros_like(peer)))

    return ring_walk(block, size, ctx_index, jnp.zeros((size * rows, width), block.dtype), put)


def ring_gather_columns(block, size, ctx_index):
    rows, width = block.shape

    def put(out, piece, peer, offset):
        return lax.dynamic_update_slice(out, piece, (jnp.full_like(peer, offset), peer * width))

    return ring_walk(block, size, ctx_index, jnp.zeros((rows, size * width), block.dtype), put)


def ring_scatter(parts, size, ctx_index):
    f32 = jnp.float32
    rows = parts.shape[0] // size
    ahead, back = ring_steps(size)
    peers = ring_peers(size, ctx_index)
    half = size // 2

    def own(k, start, count):
        first = (peers[k % size] * rows + start, jnp.zeros_like(peers[0]))
        return lax.dynamic_slice(parts, first, (count, parts.shape[1])).astype(f32)

    def low(values):
        return values.astype(jnp.bfloat16)

    cut = rows // 2
    fore = lax.ppermute(low(own(half, 0, cut)), "ctx", ahead)
    rear = lax.ppermute(low(own(half, cut, cut)), "ctx", back)
    fore = jnp.concatenate(
        [low(fore.astype(f32) + own(half - 1, 0, cut)), low(own(half - 1, cut, cut))], axis=0
    )
    rear = jnp.concatenate(
        [low(own(1 - half, 0, cut)), low(rear.astype(f32) + own(1 - half, cut, cut))], axis=0
    )
    for k in range(half - 1, 0, -1):
        fore = lax.ppermute(fore, "ctx", ahead)
        rear = lax.ppermute(rear, "ctx", back)
        if k > 1:
            fore = low(fore.astype(f32) + own(k - 1, 0, rows))
            rear = low(rear.astype(f32) + own(1 - k, 0, rows))
    return own(0, 0, rows) + fore.astype(f32) + rear.astype(f32)


def other_core(size):
    return [(i, i ^ 1) for i in range(size)]


def other_chip(size):
    return [(i, i ^ 2) for i in range(size)]


def fsdp_gather(shard, size):
    index = lax.axis_index("fsdp")
    far = lax.ppermute(shard, "fsdp", other_chip(size))
    near = lax.ppermute(shard, "fsdp", other_core(size))
    far_near = lax.ppermute(far, "fsdp", other_core(size))
    out = jnp.zeros((size,) + shard.shape, shard.dtype)
    for piece, peer in ((shard, index), (near, index ^ 1), (far, index ^ 2), (far_near, index ^ 3)):
        out = lax.dynamic_update_index_in_dim(out, piece, peer, 0)
    return out


def small_scatter(parts, size, fsdp_size, ctx_index):
    index = lax.axis_index("fsdp")

    def pick(array, at, axis):
        return lax.dynamic_index_in_dim(array, at, axis, keepdims=False)

    halves = parts.reshape(size, fsdp_size // 2, 2, -1)
    core, chip = index % 2, index // 2
    kept = pick(halves, core, 2)
    kept = kept + lax.ppermute(pick(halves, 1 - core, 2), "fsdp", other_core(fsdp_size))
    mine = pick(kept, chip, 1)
    mine = mine + lax.ppermute(pick(kept, 1 - chip, 1), "fsdp", other_chip(fsdp_size))
    rows = mine.reshape(size // 2, 2, -1)
    odd = ctx_index % 2
    row = pick(rows, odd, 1)
    row = row + lax.ppermute(pick(rows, 1 - odd, 1), "ctx", [(i, i ^ 1) for i in range(size)])
    pairs = size // 2
    total = pick(row, ctx_index // 2, 0)
    for k in range(1, pairs):
        total = total + lax.ppermute(
            pick(row, (ctx_index // 2 + k) % pairs, 0),
            "ctx",
            [(i, (i + 2 * k) % size) for i in range(size)],
        )
    return total


def split_columns(weight, groups, size, extra):
    rows = weight.shape[0]
    width = weight.shape[1] // (groups * size)
    pieces = weight.reshape(rows, groups, size, width).transpose(2, 0, 1, 3)
    pieces = pieces.reshape(size, rows, groups * width)
    if extra is not None:
        count = extra.shape[0]
        more = -(-count // (groups * width * 16)) * 16
        extra = jnp.pad(extra, (0, more * groups * width - count))
        extra = jnp.broadcast_to(
            extra.reshape(1, more, groups * width), (size, more, groups * width)
        )
        pieces = jnp.concatenate([pieces, extra], axis=1)
    pieces = lax.all_to_all(pieces, "ctx", split_axis=0, concat_axis=0, tiled=True)
    whole = lax.all_gather(pieces, "fsdp", axis=0, tiled=False)
    whole = whole.transpose(1, 0, 2, 3)
    taken = whole[:, :, :rows].reshape(-1, groups * width)
    if extra is None:
        return taken
    return (taken, whole[:, :, rows:].reshape(-1, more * groups * width)[:, :count])


def merge_columns(grad, groups, size, fsdp_size):
    width = grad.shape[1] // groups
    rows = grad.shape[0] // (size * fsdp_size)
    pieces = grad.reshape(size, fsdp_size, rows, groups * width).transpose(1, 0, 2, 3)
    pieces = pieces.astype(jnp.bfloat16).reshape(grad.shape)
    pieces = lax.psum_scatter(pieces, "fsdp", scatter_dimension=0, tiled=True)
    pieces = pieces.reshape(size, rows, groups * width)
    pieces = lax.all_to_all(pieces, "ctx", split_axis=0, concat_axis=0, tiled=True)
    pieces = pieces.reshape(size, rows, groups, width).transpose(1, 2, 0, 3)
    return pieces.reshape(rows, groups * size * width).astype(jnp.float32)


def local_split(
    ctx_size,
    fsdp_size,
    tokens,
    segments,
    routes,
    cotangent,
    w_qkv,
    b_qkv,
    w_out,
    gain_attn,
    gain_ffn,
    w_router,
    w_shared_gate,
    w_shared_in,
    w_shared_out,
    w_expert_in,
    w_expert_out,
):
    bf16, f32, i32 = jnp.bfloat16, jnp.float32, jnp.int32
    device_count = ctx_size * fsdp_size
    block_len = tokens.shape[2]
    width = tokens.shape[3]
    token_count = 2 * block_len
    top_count = routes.shape[3]
    seq_len = token_count * ctx_size
    ctx_index = lax.axis_index("ctx")
    expert_count = w_router.shape[1]
    capacity = token_count * top_count // expert_count
    own_heads = HEADS // ctx_size
    own_width = own_heads * HD
    fs_own = FS // ctx_size
    score_scale = HD ** (-0.5)

    def dot(a, b):
        return jnp.dot(a, b, preferred_element_type=f32)

    def dot_t(a, b):
        return lax.dot_general(a, b, (((1,), (1,)), ((), ())), preferred_element_type=f32)

    def t_dot(a, b):
        return lax.dot_general(a, b, (((0,), (0,)), ((), ())), preferred_element_type=f32)

    def own_rows(values):
        return lax.dynamic_index_in_dim(
            values.reshape((ctx_size, token_count) + values.shape[1:]), ctx_index, 0, keepdims=False
        )

    def sum_rows(grad):
        return lax.psum_scatter(
            grad.astype(bf16), "fsdp", scatter_dimension=0, tiled=True
        ).astype(f32)

    shard = width // device_count
    small = [gain_attn, gain_ffn, w_shared_gate, w_router.reshape(-1), b_qkv]
    small_size = sum(piece.shape[0] for piece in small)
    small = jnp.concatenate(small + [routes.astype(bf16).reshape(-1)], axis=0)
    token_rows = ring_gather(tokens.reshape(token_count, width), ctx_size, ctx_index)
    qkv_weight, small = split_columns(w_qkv, 3, ctx_size, small)
    attn_gain = small[:, :shard].reshape(width).astype(f32)
    ffn_gain = small[:, shard : 2 * shard].reshape(width).astype(f32)
    gate_vector = small[:, 2 * shard : 3 * shard].reshape(width)
    router_end = 3 * shard + shard * expert_count
    router_weight = small[:, 3 * shard : router_end].reshape(width, expert_count)
    bias = small[:, router_end:small_size].reshape(3, ctx_size, own_width).astype(f32)
    bias = lax.dynamic_index_in_dim(bias, ctx_index, 1, keepdims=False).reshape(3 * own_width)
    route_rows = small[:, small_size:].astype(i32)
    route_rows = lax.dynamic_index_in_dim(
        route_rows.reshape(ctx_size, fsdp_size, -1), lax.axis_index("fsdp"), 1, keepdims=False
    ).reshape(ctx_size, token_count, top_count)

    out_shard, token_rows = lax.optimization_barrier((w_out, token_rows))
    out_weight = fsdp_gather(ring_gather(out_shard, ctx_size, ctx_index), fsdp_size)
    out_weight = out_weight.reshape(fsdp_size, ctx_size, -1, width)
    out_weight = out_weight.transpose(1, 0, 2, 3).reshape(width, width)
    in_shard, token_rows = lax.optimization_barrier((w_shared_in, token_rows))
    shared_in = split_columns(in_shard, 2, ctx_size, None)
    shared_out = lax.all_gather(w_shared_out, "fsdp", axis=0, tiled=True)
    expert_in = lax.all_gather(w_expert_in[0], "fsdp", axis=0, tiled=True)
    expert_out = lax.all_gather(w_expert_out[0], "fsdp", axis=0, tiled=True)

    block_ids = jnp.arange(ctx_size, dtype=i32)[:, None]
    local_index = jnp.arange(block_len, dtype=i32)[None, :]
    positions = jnp.stack(
        [
            block_ids * block_len + local_index,
            seq_len - (block_ids + 1) * block_len + local_index,
        ],
        axis=1,
    ).reshape(seq_len)
    seg_rows = (
        segments.reshape(2, ctx_size, block_len).transpose(1, 0, 2).reshape(seq_len)
    )
    cos_tab, sine_tab = rope_tables(positions, HD)

    inputs = token_rows.astype(f32)
    normed, inv_one_all = rms_norm(inputs, attn_gain)
    normed_low = normed.astype(bf16)
    projected = dot(normed_low, qkv_weight) + bias
    head_shape = (seq_len, own_heads, HD)
    queries = rotate(projected[:, :own_width].reshape(head_shape), cos_tab, sine_tab).astype(bf16)
    keys = rotate(
        projected[:, own_width : 2 * own_width].reshape(head_shape), cos_tab, sine_tab
    ).astype(bf16)
    values = projected[:, 2 * own_width :].reshape(head_shape).astype(bf16)
    allowed = (positions[None, :] <= positions[:, None]) & (seg_rows[None, :] == seg_rows[:, None])
    scores = jnp.einsum("qhd,khd->hqk", queries, keys, preferred_element_type=f32) * score_scale
    scores = jnp.where(allowed[None], scores, MASK_FILL)
    top_score = jnp.max(scores, axis=-1, keepdims=True)
    log_total = top_score + jnp.log(jnp.sum(jnp.exp(scores - top_score), axis=-1, keepdims=True))
    weights = jnp.exp(scores - log_total)
    weights_low = weights.astype(bf16)
    attended = jnp.einsum("hqk,khd->qhd", weights_low, values, preferred_element_type=f32)
    attn_own = attended.astype(bf16).reshape(seq_len, own_width)
    attn_rows = ring_gather_columns(attn_own, ctx_size, ctx_index)
    grad_block, attn_rows = lax.optimization_barrier((cotangent, attn_rows))
    grad_rows = ring_gather(grad_block.reshape(token_count, width), ctx_size, ctx_index)
    residual = inputs + dot(attn_rows, out_weight)

    normed_two, inv_two_all = rms_norm(residual, ffn_gain)
    low_two = normed_two.astype(bf16)
    mixed_weight = jnp.concatenate([router_weight, gate_vector[:, None]], axis=1)
    logits = dot(low_two, mixed_weight)
    probs_all = jax.nn.softmax(logits[:, :expert_count], axis=-1)
    scale_all = jax.nn.sigmoid(logits[:, expert_count])
    gate_all = lax.dynamic_index_in_dim(probs_all, ctx_index, 1, keepdims=False)

    named = jnp.any(route_rows == ctx_index, axis=-1)
    before = jnp.arange(token_count)[:, None] < jnp.arange(token_count)[None, :]
    rank = dot(named.astype(bf16), before.astype(bf16)).astype(i32)
    slot_of = jnp.where(named & (rank < capacity), rank, -1)
    slot_mask = slot_of[:, None, :] == jnp.arange(capacity, dtype=i32)[None, :, None]
    slot_map = slot_mask.astype(bf16)
    blocks_two = low_two.reshape(ctx_size, token_count, width)
    blocks_grad = grad_rows.reshape(ctx_size, token_count, width)
    gate_blocks = gate_all.reshape(ctx_size, token_count)

    def to_slots(blocks):
        picked = jnp.einsum("bmt,btd->bmd", slot_map, blocks, preferred_element_type=f32)
        return picked.reshape(ctx_size * capacity, width)

    def to_tokens(slots):
        spread = jnp.einsum(
            "bmt,bmd->btd",
            slot_map,
            slots.reshape(ctx_size, capacity, width),
            preferred_element_type=f32,
        )
        return spread.reshape(seq_len, width)

    buffer = to_slots(blocks_two).astype(bf16)
    expert_pre = dot(buffer, expert_in)
    expert_hid = swiglu(expert_pre, FE).astype(bf16)
    expert_res = dot(expert_hid, expert_out).astype(bf16)
    routed = gate_all[:, None] * to_tokens(expert_res)

    grad_slots = to_slots(blocks_grad)
    gate_slots = jnp.sum(jnp.where(slot_mask, gate_blocks[:, None, :], 0.0), axis=-1).reshape(-1, 1)
    grad_res = (gate_slots * grad_slots).astype(bf16)
    slot_dots = jnp.sum(grad_slots * expert_res.astype(f32), axis=-1).reshape(ctx_size, capacity, 1)
    grad_gates = jnp.sum(jnp.where(slot_mask, slot_dots, 0.0), axis=1)
    grad_expert_out = t_dot(expert_hid, grad_res)
    grad_hid = dot_t(grad_res, expert_out)
    grad_pre = swiglu_back(expert_pre, FE, grad_hid).astype(bf16)
    grad_expert_in = t_dot(buffer, grad_pre)
    grad_buffer = dot_t(grad_pre, expert_in).astype(bf16)

    grad_expert_in, grad_expert_out, low_shared = lax.optimization_barrier(
        (grad_expert_in.astype(bf16), grad_expert_out.astype(bf16), low_two)
    )
    sum_expert_out = sum_rows(grad_expert_out)
    sum_expert_in = sum_rows(grad_expert_in)

    shared_pre = dot(low_shared, shared_in)
    shared_hid = swiglu(shared_pre, fs_own).astype(bf16)
    shared_res = dot(shared_hid, shared_out)
    out_parts = (scale_all[:, None] * shared_res + routed).astype(bf16)
    out_sum = ring_scatter(out_parts, ctx_size, ctx_index)
    own_residual = own_rows(residual)
    output = (own_residual + out_sum).astype(bf16).reshape(tokens.shape)
    grad_f32 = grad_rows.astype(f32)
    grad_shared_res = (scale_all[:, None] * grad_f32).astype(bf16)
    gate_dots = jnp.sum(grad_f32 * shared_res, axis=-1).reshape(ctx_size, token_count)
    grad_shared_out = t_dot(shared_hid, grad_shared_res)
    grad_shared_hid = dot_t(grad_shared_res, shared_out)
    grad_shared_pre = swiglu_back(shared_pre, fs_own, grad_shared_hid).astype(bf16)
    grad_shared_in = t_dot(low_two, grad_shared_pre)
    two_parts = (dot_t(grad_shared_pre, shared_in) + to_tokens(grad_buffer)).astype(bf16)
    grad_two = ring_scatter(two_parts, ctx_size, ctx_index)

    dots = jnp.stack([grad_gates, gate_dots], axis=1)
    dots = lax.all_to_all(dots, "ctx", split_axis=0, concat_axis=0, tiled=True)
    own_probs = own_rows(probs_all)
    own_scale = own_rows(scale_all)
    own_low = own_rows(low_two)
    own_chosen = routes.reshape(token_count, top_count)
    chosen_mask = jnp.any(
        own_chosen[..., None] == jnp.arange(expert_count, dtype=i32), axis=1
    )
    grad_probs = jnp.where(chosen_mask, dots[:, 0].T, 0.0)
    grad_logits = (
        own_probs * (grad_probs - jnp.sum(own_probs * grad_probs, axis=-1, keepdims=True))
    ).astype(bf16)
    grad_gate_pre = (jnp.sum(dots[:, 1], axis=0) * own_scale * (1.0 - own_scale)).astype(bf16)
    grad_router = t_dot(own_low, grad_logits)
    grad_gate_vector = t_dot(own_low, grad_gate_pre[:, None])
    grad_two = grad_two + dot_t(grad_logits, router_weight)
    grad_two = grad_two + grad_gate_pre.astype(f32)[:, None] * gate_vector.astype(f32)[None, :]
    grad_resid_norm, grad_gain_two = rms_back(
        own_residual, own_rows(inv_two_all), ffn_gain, grad_two
    )
    grad_resid = cotangent.reshape(token_count, width).astype(f32) + grad_resid_norm

    grad_mixed = grad_resid.astype(bf16)
    grad_attn_rows = dot_t(grad_mixed, out_weight).astype(bf16)
    grad_attn = lax.all_to_all(
        grad_attn_rows.reshape(token_count, ctx_size, own_width).transpose(1, 0, 2),
        "ctx",
        split_axis=0,
        concat_axis=0,
        tiled=True,
    ).reshape(head_shape)
    mixed_all = ring_gather(grad_mixed, ctx_size, ctx_index)
    grad_out_weight = t_dot(attn_own, mixed_all)
    grad_weights = jnp.einsum("qhd,khd->hqk", grad_attn, values, preferred_element_type=f32)
    delta = jnp.sum(weights * grad_weights, axis=-1, keepdims=True)
    grad_scores = jnp.where(allowed[None], weights * (grad_weights - delta), 0.0).astype(bf16)
    grad_q = jnp.einsum("hqk,khd->qhd", grad_scores, keys, preferred_element_type=f32) * score_scale
    grad_k = (
        jnp.einsum("hqk,qhd->khd", grad_scores, queries, preferred_element_type=f32) * score_scale
    )
    grad_v = jnp.einsum("hqk,qhd->khd", weights_low, grad_attn, preferred_element_type=f32)
    grad_projected = jnp.concatenate(
        [
            rotate_back(grad_q, cos_tab, sine_tab).reshape(seq_len, own_width),
            rotate_back(grad_k, cos_tab, sine_tab).reshape(seq_len, own_width),
            grad_v.reshape(seq_len, own_width),
        ],
        axis=-1,
    ).astype(bf16)
    one_sums = dot_t(grad_projected, qkv_weight)
    grad_gain_one = jnp.sum(one_sums * inputs * inv_one_all, axis=0)
    one_parts = one_sums.astype(bf16)
    grad_normed = ring_scatter(one_parts, ctx_size, ctx_index)
    grad_inputs_norm, unused = rms_back(
        tokens.reshape(token_count, width).astype(f32),
        own_rows(inv_one_all),
        attn_gain,
        grad_normed,
    )
    grad_tokens = (grad_resid + grad_inputs_norm).reshape(tokens.shape)
    grad_qkv_weight = t_dot(normed_low, grad_projected)
    grad_bias = jnp.sum(grad_projected.astype(f32), axis=0).reshape(3, 1, own_width)
    grad_bias = jnp.where(
        jnp.arange(ctx_size, dtype=i32)[None, :, None] == ctx_index, grad_bias, 0.0
    )

    small_grads = jnp.concatenate(
        [
            piece.reshape(device_count, -1)
            for piece in (grad_gain_one, grad_gain_two, grad_gate_vector, grad_router, grad_bias)
        ],
        axis=1,
    )
    small_grads = small_grads.reshape(ctx_size, fsdp_size, small_size)
    small_grads = small_scatter(small_grads, ctx_size, fsdp_size, ctx_index).reshape(small_size)
    return (
        output,
        grad_tokens,
        merge_columns(grad_qkv_weight, 3, ctx_size, fsdp_size),
        small_grads[router_end:],
        sum_rows(grad_out_weight),
        small_grads[:shard],
        small_grads[shard : 2 * shard],
        small_grads[3 * shard : router_end].reshape(shard, expert_count),
        small_grads[2 * shard : 3 * shard],
        merge_columns(grad_shared_in, 2, ctx_size, fsdp_size),
        sum_rows(grad_shared_out),
        sum_expert_in[None],
        sum_expert_out[None],
    )


def local_wide(
    tokens,
    segments,
    routes,
    cotangent,
    w_qkv,
    b_qkv,
    w_out,
    gain_attn,
    gain_ffn,
    w_router,
    w_shared_gate,
    w_shared_in,
    w_shared_out,
    w_expert_in,
    w_expert_out,
):
    block_len = tokens.shape[2]
    model_width = tokens.shape[3]
    token_count = 2 * block_len
    top_count = routes.shape[3]
    half_len = segments.shape[2]
    seq_len = 2 * half_len
    ctx_index = lax.axis_index("ctx")
    head_count = model_width // HD
    expert_count = w_router.shape[1]
    capacity = token_count * top_count // expert_count
    slot_count = expert_count * capacity
    key_rows = min(512, seq_len)
    key_blocks = seq_len // key_rows
    score_scale = HD ** (-0.5)
    head_shape = (token_count, head_count, HD)
    attn_set = (
        lax.all_gather(w_qkv, ("ctx", "fsdp"), axis=0, tiled=True),
        lax.all_gather(b_qkv, ("ctx", "fsdp"), axis=0, tiled=True),
        lax.all_gather(w_out, ("ctx", "fsdp"), axis=0, tiled=True),
        lax.all_gather(gain_attn, ("ctx", "fsdp"), axis=0, tiled=True),
    )
    qkv_weight, qkv_bias, out_weight, attn_gain = attn_set
    inputs = tokens.reshape(token_count, model_width).astype(jnp.float32)
    normed, inv_one = rms_norm(inputs, attn_gain.astype(jnp.float32))
    normed_low = normed.astype(jnp.bfloat16)
    projected = jnp.dot(
        normed_low, qkv_weight, preferred_element_type=jnp.float32
    ) + qkv_bias.astype(jnp.float32)
    local_index = jnp.arange(block_len, dtype=jnp.int32)
    query_pos = jnp.concatenate(
        [ctx_index * block_len + local_index, seq_len - (ctx_index + 1) * block_len + local_index]
    )
    half_index = jnp.arange(half_len, dtype=jnp.int32)
    key_pos = jnp.concatenate(
        [half_index, seq_len - block_len * (half_index // block_len + 1) + half_index % block_len]
    ).reshape(key_blocks, key_rows)
    key_seg = segments.reshape(key_blocks, key_rows)
    query_seg = lax.dynamic_slice_in_dim(segments[0], ctx_index * block_len, block_len, 1).reshape(
        token_count
    )
    cos_tab, sine_tab = rope_tables(query_pos, HD)
    queries = rotate(projected[:, :model_width].reshape(head_shape), cos_tab, sine_tab).astype(
        jnp.bfloat16
    )
    keys_own = rotate(
        projected[:, model_width : 2 * model_width].reshape(head_shape), cos_tab, sine_tab
    ).astype(jnp.bfloat16)
    values_own = projected[:, 2 * model_width :].astype(jnp.bfloat16)
    keys_all, values_all = (
        lax.all_gather(keys_own.reshape(2, block_len, model_width), "ctx", axis=1, tiled=True),
        lax.all_gather(values_own.reshape(2, block_len, model_width), "ctx", axis=1, tiled=True),
    )
    keys_all = keys_all.reshape(key_blocks, key_rows, head_count, HD)
    values_all = values_all.reshape(key_blocks, key_rows, head_count, HD)

    def score_block(key_blk, pos_blk, seg_blk):
        raw_scores = (
            jnp.einsum("qhd,khd->hqk", queries, key_blk, preferred_element_type=jnp.float32)
            * score_scale
        )
        allowed = (pos_blk[None, :] <= query_pos[:, None]) & (
            seg_blk[None, :] == query_seg[:, None]
        )
        return (jnp.where(allowed[None], raw_scores, MASK_FILL), allowed)

    def total_step(running, key_part):
        run_max, run_sum = running
        scores = score_block(key_part[0], key_part[1], key_part[2])[0]
        new_max = jnp.maximum(run_max, jnp.max(scores, axis=-1))
        run_sum = run_sum * jnp.exp(run_max - new_max) + jnp.sum(
            jnp.exp(scores - new_max[..., None]), axis=-1
        )
        return ((new_max, run_sum), None)

    start_max = jnp.full((head_count, token_count), MASK_FILL, jnp.float32)
    start_sum = jnp.zeros((head_count, token_count), jnp.float32)
    (run_max, run_sum), unused = lax.scan(
        total_step, (start_max, start_sum), (keys_all, key_pos, key_seg)
    )
    log_total = run_max + jnp.log(run_sum)

    def attend_step(summed, key_part):
        key_blk, value_blk, pos_blk, seg_blk = key_part
        scores = score_block(key_blk, pos_blk, seg_blk)[0]
        weights = jnp.exp(scores - log_total[..., None]).astype(jnp.bfloat16)
        return (
            summed
            + jnp.einsum("hqk,khd->qhd", weights, value_blk, preferred_element_type=jnp.float32),
            None,
        )

    key_stack = (keys_all, values_all, key_pos, key_seg)
    attended, unused = lax.scan(attend_step, jnp.zeros(head_shape, jnp.float32), key_stack)
    attn_low = attended.reshape(token_count, model_width).astype(jnp.bfloat16)
    residual = inputs + jnp.dot(attn_low, out_weight, preferred_element_type=jnp.float32)
    ffn_set = (
        lax.all_gather(gain_ffn, ("ctx", "fsdp"), axis=0, tiled=True),
        lax.all_gather(w_router, ("ctx", "fsdp"), axis=0, tiled=True),
        lax.all_gather(w_shared_gate, ("ctx", "fsdp"), axis=0, tiled=True),
        lax.all_gather(w_shared_in, ("ctx", "fsdp"), axis=0, tiled=True),
        lax.all_gather(w_shared_out, ("ctx", "fsdp"), axis=0, tiled=True),
    )
    ffn_gain, router_weight, gate_vector, shared_in, shared_out = ffn_set
    normed_two, inv_two = rms_norm(residual, ffn_gain.astype(jnp.float32))
    low_two = normed_two.astype(jnp.bfloat16)
    logits = jnp.dot(low_two, router_weight, preferred_element_type=jnp.float32)
    router_probs = jax.nn.softmax(logits, axis=-1)
    chosen = routes.reshape(token_count, top_count)
    chosen_mask = chosen[..., None] == jnp.arange(expert_count, dtype=jnp.int32)
    gate_vals = jnp.sum(jnp.where(chosen_mask, router_probs[:, None, :], 0.0), axis=-1)
    shared_scale = jax.nn.sigmoid(jnp.dot(low_two, gate_vector, preferred_element_type=jnp.float32))
    shared_pre = jnp.dot(low_two, shared_in, preferred_element_type=jnp.float32)
    shared_hid = swiglu(shared_pre, FS).astype(jnp.bfloat16)
    shared_res = jnp.dot(shared_hid, shared_out, preferred_element_type=jnp.float32)
    pair_routes = chosen.reshape(token_count * top_count)
    expert_marks = (
        pair_routes[:, None] == jnp.arange(expert_count, dtype=jnp.int32)[None, :]
    ).astype(jnp.int32)
    pair_ranks = jnp.sum((jnp.cumsum(expert_marks, axis=0) - expert_marks) * expert_marks, axis=1)
    pair_target = jnp.where(pair_ranks < capacity, pair_routes * capacity + pair_ranks, -1)
    pair_map = pair_target[:, None] == jnp.arange(slot_count, dtype=jnp.int32)[None, :]
    pair_low = pair_map.astype(jnp.bfloat16)
    token_map = jnp.sum(
        pair_map.reshape(token_count, top_count, slot_count).astype(jnp.int32), axis=1
    ).astype(jnp.bfloat16)
    outgoing = jnp.einsum(
        "tc,td->cd", token_map, low_two, preferred_element_type=jnp.float32
    ).astype(jnp.bfloat16)
    incoming = lax.all_to_all(
        outgoing.reshape(expert_count, capacity, model_width),
        "ctx",
        split_axis=0,
        concat_axis=1,
        tiled=True,
    )
    expert_in, expert_out = (
        lax.all_gather(w_expert_in, "fsdp", axis=1, tiled=True),
        lax.all_gather(w_expert_out, "fsdp", axis=1, tiled=True),
    )
    expert_pre = jnp.einsum("erd,edf->erf", incoming, expert_in, preferred_element_type=jnp.float32)
    expert_hid = swiglu(expert_pre, FE).astype(jnp.bfloat16)
    expert_res = jnp.einsum(
        "erf,efd->erd", expert_hid, expert_out, preferred_element_type=jnp.float32
    ).astype(jnp.bfloat16)
    returned = lax.all_to_all(expert_res, "ctx", split_axis=1, concat_axis=0, tiled=True).reshape(
        slot_count, model_width
    )
    pair_vals = jnp.dot(pair_low, returned, preferred_element_type=jnp.float32).reshape(
        token_count, top_count, model_width
    )
    routed = jnp.sum(gate_vals[..., None] * pair_vals, axis=1)
    output = (
        (residual + shared_scale[:, None] * shared_res + routed)
        .astype(jnp.bfloat16)
        .reshape(tokens.shape)
    )
    grad_out = cotangent.reshape(token_count, model_width).astype(jnp.float32)
    pair_grads = gate_vals[..., None] * grad_out[:, None, :]
    grad_gates = jnp.sum(grad_out[:, None, :] * pair_vals, axis=-1)
    grad_returned = jnp.einsum(
        "pc,pd->cd",
        pair_map.astype(jnp.float32),
        pair_grads.reshape(token_count * top_count, model_width),
        precision=HIGHEST,
    ).astype(jnp.bfloat16)
    grad_res = lax.all_to_all(
        grad_returned.reshape(expert_count, capacity, model_width),
        "ctx",
        split_axis=0,
        concat_axis=1,
        tiled=True,
    )
    grad_expert_out = jnp.einsum(
        "erf,erd->efd", expert_hid, grad_res, preferred_element_type=jnp.float32
    )
    grad_hid = jnp.einsum("erd,efd->erf", grad_res, expert_out, preferred_element_type=jnp.float32)
    grad_pre = swiglu_back(expert_pre, FE, grad_hid).astype(jnp.bfloat16)
    grad_expert_in = jnp.einsum(
        "erd,erf->edf", incoming, grad_pre, preferred_element_type=jnp.float32
    )
    grad_incoming = jnp.einsum(
        "erf,edf->erd", grad_pre, expert_in, preferred_element_type=jnp.float32
    ).astype(jnp.bfloat16)
    grad_outgoing = lax.all_to_all(
        grad_incoming, "ctx", split_axis=1, concat_axis=0, tiled=True
    ).reshape(slot_count, model_width)
    expert_grads = (
        lax.psum_scatter(
            grad_expert_in.astype(jnp.bfloat16), "fsdp", scatter_dimension=1, tiled=True
        ).astype(jnp.float32),
        lax.psum_scatter(
            grad_expert_out.astype(jnp.bfloat16), "fsdp", scatter_dimension=1, tiled=True
        ).astype(jnp.float32),
    )
    grad_two = jnp.einsum("tc,cd->td", token_map, grad_outgoing, preferred_element_type=jnp.float32)
    grad_probs = jnp.sum(jnp.where(chosen_mask, grad_gates[..., None], 0.0), axis=1)
    grad_logits = (
        router_probs * (grad_probs - jnp.sum(router_probs * grad_probs, axis=-1, keepdims=True))
    ).astype(jnp.bfloat16)
    grad_router = jnp.einsum("td,te->de", low_two, grad_logits, preferred_element_type=jnp.float32)
    grad_shared_res = (shared_scale[:, None] * grad_out).astype(jnp.bfloat16)
    grad_gate_pre = (
        jnp.sum(grad_out * shared_res, axis=-1) * shared_scale * (1.0 - shared_scale)
    ).astype(jnp.bfloat16)
    grad_shared_out = jnp.einsum(
        "tf,td->fd", shared_hid, grad_shared_res, preferred_element_type=jnp.float32
    )
    grad_shared_hid = jnp.einsum(
        "td,fd->tf", grad_shared_res, shared_out, preferred_element_type=jnp.float32
    )
    grad_shared_pre = swiglu_back(shared_pre, FS, grad_shared_hid).astype(jnp.bfloat16)
    grad_shared_in = jnp.einsum(
        "td,tf->df", low_two, grad_shared_pre, preferred_element_type=jnp.float32
    )
    grad_gate_vector = jnp.einsum(
        "td,t->d", low_two, grad_gate_pre, preferred_element_type=jnp.float32
    )
    grad_two = grad_two + jnp.einsum(
        "te,de->td", grad_logits, router_weight, preferred_element_type=jnp.float32
    )
    grad_two = grad_two + jnp.einsum(
        "tf,df->td", grad_shared_pre, shared_in, preferred_element_type=jnp.float32
    )
    grad_two = (
        grad_two
        + grad_gate_pre.astype(jnp.float32)[:, None] * gate_vector.astype(jnp.float32)[None, :]
    )
    grad_resid_norm, grad_gain_two = rms_back(
        residual, inv_two, ffn_gain.astype(jnp.float32), grad_two
    )
    grad_resid = grad_out + grad_resid_norm
    ffn_grads = (
        lax.psum_scatter(grad_gain_two, ("ctx", "fsdp"), scatter_dimension=0, tiled=True),
        lax.psum_scatter(grad_router, ("ctx", "fsdp"), scatter_dimension=0, tiled=True),
        lax.psum_scatter(grad_gate_vector, ("ctx", "fsdp"), scatter_dimension=0, tiled=True),
        lax.psum_scatter(grad_shared_in, ("ctx", "fsdp"), scatter_dimension=0, tiled=True),
        lax.psum_scatter(grad_shared_out, ("ctx", "fsdp"), scatter_dimension=0, tiled=True),
    )
    grad_mixed = grad_resid.astype(jnp.bfloat16)
    grad_out_weight = jnp.einsum(
        "tc,td->cd", attn_low, grad_mixed, preferred_element_type=jnp.float32
    )
    grad_attn = (
        jnp.einsum("td,cd->tc", grad_mixed, out_weight, preferred_element_type=jnp.float32)
        .astype(jnp.bfloat16)
        .reshape(head_shape)
    )

    def delta_step(summed, key_part):
        key_blk, value_blk, pos_blk, seg_blk = key_part
        weights = jnp.exp(score_block(key_blk, pos_blk, seg_blk)[0] - log_total[..., None])
        grad_weights = jnp.einsum(
            "qhd,khd->hqk", grad_attn, value_blk, preferred_element_type=jnp.float32
        )
        return (summed + jnp.sum(weights * grad_weights, axis=-1), None)

    delta_sum, unused = lax.scan(
        delta_step, jnp.zeros((head_count, token_count), jnp.float32), key_stack
    )

    def grad_step(summed, key_part):
        key_blk, value_blk, pos_blk, seg_blk = key_part
        scores, allowed = score_block(key_blk, pos_blk, seg_blk)
        weights = jnp.exp(scores - log_total[..., None])
        grad_weights = jnp.einsum(
            "qhd,khd->hqk", grad_attn, value_blk, preferred_element_type=jnp.float32
        )
        grad_scores = jnp.where(
            allowed[None], weights * (grad_weights - delta_sum[..., None]), 0.0
        ).astype(jnp.bfloat16)
        summed = (
            summed
            + jnp.einsum("hqk,khd->qhd", grad_scores, key_blk, preferred_element_type=jnp.float32)
            * score_scale
        )
        grad_key = (
            jnp.einsum("hqk,qhd->khd", grad_scores, queries, preferred_element_type=jnp.float32)
            * score_scale
        )
        grad_value = jnp.einsum(
            "hqk,qhd->khd",
            weights.astype(jnp.bfloat16),
            grad_attn,
            preferred_element_type=jnp.float32,
        )
        return (summed, (grad_key, grad_value))

    grad_query, (grad_keys, grad_values) = lax.scan(
        grad_step, jnp.zeros(head_shape, jnp.float32), key_stack
    )
    grad_keys_own, grad_values_own = (
        lax.psum_scatter(
            grad_keys.reshape(2, half_len, model_width).astype(jnp.bfloat16),
            "ctx",
            scatter_dimension=1,
            tiled=True,
        ).astype(jnp.float32),
        lax.psum_scatter(
            grad_values.reshape(2, half_len, model_width).astype(jnp.bfloat16),
            "ctx",
            scatter_dimension=1,
            tiled=True,
        ).astype(jnp.float32),
    )
    grad_q_rows = rotate_back(grad_query, cos_tab, sine_tab).reshape(token_count, model_width)
    grad_k_rows = rotate_back(grad_keys_own.reshape(head_shape), cos_tab, sine_tab).reshape(
        token_count, model_width
    )
    grad_projected = jnp.concatenate(
        [grad_q_rows, grad_k_rows, grad_values_own.reshape(token_count, model_width)], axis=-1
    ).astype(jnp.bfloat16)
    grad_qkv_weight = jnp.einsum(
        "td,te->de", normed_low, grad_projected, preferred_element_type=jnp.float32
    )
    grad_qkv_bias = jnp.sum(grad_projected.astype(jnp.float32), axis=0)
    grad_normed = jnp.einsum(
        "te,de->td", grad_projected, qkv_weight, preferred_element_type=jnp.float32
    )
    grad_inputs_norm, grad_gain_one = rms_back(
        inputs, inv_one, attn_gain.astype(jnp.float32), grad_normed
    )
    grad_tokens = (grad_resid + grad_inputs_norm).reshape(tokens.shape)
    attn_grads = (
        lax.psum_scatter(grad_qkv_weight, ("ctx", "fsdp"), scatter_dimension=0, tiled=True),
        lax.psum_scatter(grad_qkv_bias, ("ctx", "fsdp"), scatter_dimension=0, tiled=True),
        lax.psum_scatter(grad_out_weight, ("ctx", "fsdp"), scatter_dimension=0, tiled=True),
        lax.psum_scatter(grad_gain_one, ("ctx", "fsdp"), scatter_dimension=0, tiled=True),
    )
    return (
        output,
        grad_tokens,
        attn_grads[0],
        attn_grads[1],
        attn_grads[2],
        attn_grads[3],
        ffn_grads[0],
        ffn_grads[1],
        ffn_grads[2],
        ffn_grads[3],
        ffn_grads[4],
        expert_grads[0],
        expert_grads[1],
    )


def solution(mesh):
    in_specs = (
        P("fsdp", None, "ctx", None),
        P("fsdp", None, None),
        P("fsdp", None, "ctx", None),
        P("fsdp", None, "ctx", None),
        P(("ctx", "fsdp"), None),
        P(("ctx", "fsdp")),
        P(("ctx", "fsdp"), None),
        P(("ctx", "fsdp")),
        P(("ctx", "fsdp")),
        P(("ctx", "fsdp"), None),
        P(("ctx", "fsdp")),
        P(("ctx", "fsdp"), None),
        P(("ctx", "fsdp"), None),
        P("ctx", "fsdp", None),
        P("ctx", "fsdp", None),
    )
    out_specs = (
        P("fsdp", None, "ctx", None),
        P("fsdp", None, "ctx", None),
        P(("ctx", "fsdp"), None),
        P(("ctx", "fsdp")),
        P(("ctx", "fsdp"), None),
        P(("ctx", "fsdp")),
        P(("ctx", "fsdp")),
        P(("ctx", "fsdp"), None),
        P(("ctx", "fsdp")),
        P(("ctx", "fsdp"), None),
        P(("ctx", "fsdp"), None),
        P("ctx", "fsdp", None),
        P("ctx", "fsdp", None),
    )
    ctx_size = mesh.shape["ctx"]
    fsdp_size = mesh.shape["fsdp"]

    def local(*arrays):
        if HEADS % ctx_size:
            return local_wide(*arrays)
        return local_split(ctx_size, fsdp_size, *arrays)

    return jax.shard_map(local, mesh=mesh, in_specs=in_specs, out_specs=out_specs, check_vma=False)
```

```python
import jax
import jax.numpy as jnp
from jax import lax
from jax.sharding import PartitionSpec as P

HD = 128
HEADS = 16
FS = 5632
FE = 1408


RMS_EPS = 1e-06
ROPE_THETA = 1000000.0
MASK_FILL = -1e30
HIGHEST = lax.Precision.HIGHEST


def rope_tables(positions, head_dim):
    half_dim = head_dim // 2
    inv_freq = ROPE_THETA ** (-(jnp.arange(half_dim, dtype=jnp.float32) * 2.0 / head_dim))
    angles = positions.astype(jnp.float32)[:, None] * inv_freq[None, :]
    cos_tab = jnp.concatenate([jnp.cos(angles), jnp.cos(angles)], axis=-1)
    sine_tab = jnp.concatenate([jnp.sin(angles), jnp.sin(angles)], axis=-1)
    return (cos_tab, sine_tab)


def rotate(values, cos_tab, sine_tab):
    half_dim = values.shape[-1] // 2
    turned = jnp.concatenate([-values[..., half_dim:], values[..., :half_dim]], axis=-1)
    return values * cos_tab[:, None, :] + turned * sine_tab[:, None, :]


def rotate_back(upstream, cos_tab, sine_tab):
    half_dim = upstream.shape[-1] // 2
    scaled = upstream * sine_tab[:, None, :]
    return upstream * cos_tab[:, None, :] + jnp.concatenate(
        [scaled[..., half_dim:], -scaled[..., :half_dim]], axis=-1
    )


def rms_norm(values, gain_vec):
    inv_rms = lax.rsqrt(jnp.mean(values * values, axis=-1, keepdims=True) + RMS_EPS)
    return (values * inv_rms * gain_vec, inv_rms)


def rms_back(values, inv_rms, gain_vec, upstream):
    weighted = upstream * gain_vec
    inner_mean = jnp.mean(weighted * values, axis=-1, keepdims=True)
    return (
        inv_rms * weighted - values * inv_rms * inv_rms * inv_rms * inner_mean,
        jnp.sum(upstream * values * inv_rms, axis=0),
    )


def swiglu(pre_act, split_at):
    return jax.nn.silu(pre_act[..., :split_at]) * pre_act[..., split_at:]


def swiglu_back(pre_act, split_at, upstream):
    gate_part = pre_act[..., :split_at]
    up_part = pre_act[..., split_at:]
    sigmoid_g = jax.nn.sigmoid(gate_part)
    d_gate = upstream * up_part * sigmoid_g * (1.0 + gate_part * (1.0 - sigmoid_g))
    d_up = upstream * gate_part * sigmoid_g
    return jnp.concatenate([d_gate, d_up], axis=-1)


def ring_order(size):
    return list(range(0, size, 2)) + list(range(size - 1, 0, -2))


def ring_steps(size):
    order = ring_order(size)
    ahead = [(order[i], order[(i + 1) % size]) for i in range(size)]
    back = [(dst, src) for src, dst in ahead]
    return (ahead, back)


def ring_peers(size, ctx_index):
    order = ring_order(size)
    place = {dev: i for i, dev in enumerate(order)}
    table = jnp.array(
        [[order[(place[dev] + k) % size] for k in range(size)] for dev in range(size)], jnp.int32
    )
    row = lax.dynamic_index_in_dim(table, ctx_index, 0, keepdims=False)
    return [row[k] for k in range(size)]


def ring_walk(block, size, ctx_index, out, put):
    rows = block.shape[0]
    ahead, back = ring_steps(size)
    peers = ring_peers(size, ctx_index)
    half = size // 2
    out = put(out, block, ctx_index, 0)
    fore = rear = block
    for k in range(1, half):
        fore = lax.ppermute(fore, "ctx", ahead)
        rear = lax.ppermute(rear, "ctx", back)
        out = put(out, fore, peers[size - k], 0)
        out = put(out, rear, peers[k], 0)
    fore = lax.ppermute(fore[: rows // 2], "ctx", ahead)
    rear = lax.ppermute(rear[rows // 2 :], "ctx", back)
    out = put(out, fore, peers[half], 0)
    return put(out, rear, peers[half], rows // 2)


def ring_gather(block, size, ctx_index):
    rows, width = block.shape

    def put(out, piece, peer, offset):
        return lax.dynamic_update_slice(out, piece, (peer * rows + offset, jnp.zeros_like(peer)))

    return ring_walk(block, size, ctx_index, jnp.zeros((size * rows, width), block.dtype), put)


def ring_gather_columns(block, size, ctx_index):
    rows, width = block.shape

    def put(out, piece, peer, offset):
        return lax.dynamic_update_slice(out, piece, (jnp.full_like(peer, offset), peer * width))

    return ring_walk(block, size, ctx_index, jnp.zeros((rows, size * width), block.dtype), put)


def ring_scatter(parts, size, ctx_index):
    f32 = jnp.float32
    rows = parts.shape[0] // size
    ahead, back = ring_steps(size)
    peers = ring_peers(size, ctx_index)
    half = size // 2

    def own(k, start, count):
        first = (peers[k % size] * rows + start, jnp.zeros_like(peers[0]))
        return lax.dynamic_slice(parts, first, (count, parts.shape[1])).astype(f32)

    def low(values):
        return values.astype(jnp.bfloat16)

    cut = rows // 2
    fore = lax.ppermute(low(own(half, 0, cut)), "ctx", ahead)
    rear = lax.ppermute(low(own(half, cut, cut)), "ctx", back)
    fore = jnp.concatenate(
        [low(fore.astype(f32) + own(half - 1, 0, cut)), low(own(half - 1, cut, cut))], axis=0
    )
    rear = jnp.concatenate(
        [low(own(1 - half, 0, cut)), low(rear.astype(f32) + own(1 - half, cut, cut))], axis=0
    )
    for k in range(half - 1, 0, -1):
        fore = lax.ppermute(fore, "ctx", ahead)
        rear = lax.ppermute(rear, "ctx", back)
        if k > 1:
            fore = low(fore.astype(f32) + own(k - 1, 0, rows))
            rear = low(rear.astype(f32) + own(1 - k, 0, rows))
    return own(0, 0, rows) + fore.astype(f32) + rear.astype(f32)


def other_core(size):
    return [(i, i ^ 1) for i in range(size)]


def other_chip(size):
    return [(i, i ^ 2) for i in range(size)]


def fsdp_pieces(shard, size):
    far = lax.ppermute(shard, "fsdp", other_chip(size))
    near = lax.ppermute(shard, "fsdp", other_core(size))
    return (far, near)


def fsdp_join(shard, far, near, size):
    index = lax.axis_index("fsdp")
    far_near = lax.ppermute(far, "fsdp", other_core(size))
    out = jnp.zeros((size,) + shard.shape, shard.dtype)
    for piece, peer in ((shard, index), (near, index ^ 1), (far, index ^ 2), (far_near, index ^ 3)):
        out = lax.dynamic_update_index_in_dim(out, piece, peer, 0)
    return out


def after(value, *deps):
    return lax.optimization_barrier((value,) + deps)


def fsdp_scatter(grad, size, axis):
    index = lax.axis_index("fsdp")

    def pick(peer):
        return lax.dynamic_index_in_dim(grad, peer, axis, keepdims=False)

    far_near = lax.ppermute(pick(index ^ 3), "fsdp", other_core(size))
    near = lax.ppermute(pick(index ^ 1), "fsdp", other_core(size))
    far = (pick(index ^ 2).astype(jnp.float32) + far_near.astype(jnp.float32)).astype(jnp.bfloat16)
    far = lax.ppermute(far, "fsdp", other_chip(size))
    return pick(index).astype(jnp.float32) + near.astype(jnp.float32) + far.astype(jnp.float32)


def exchange(pieces, size, ctx_index):
    out = jnp.zeros_like(pieces)
    own = lax.dynamic_index_in_dim(pieces, ctx_index, 0, keepdims=False)
    out = lax.dynamic_update_index_in_dim(out, own, ctx_index, 0)
    for k in range(1, size):
        piece = lax.dynamic_index_in_dim(pieces, (ctx_index + k) % size, 0, keepdims=False)
        piece = lax.ppermute(piece, "ctx", [(i, (i + k) % size) for i in range(size)])
        out = lax.dynamic_update_index_in_dim(out, piece, (ctx_index - k) % size, 0)
    return out


def small_scatter(parts, size, fsdp_size, ctx_index):
    index = lax.axis_index("fsdp")

    def pick(array, at, axis):
        return lax.dynamic_index_in_dim(array, at, axis, keepdims=False)

    halves = parts.reshape(size, fsdp_size // 2, 2, -1)
    core, chip = index % 2, index // 2
    kept = pick(halves, core, 2)
    kept = kept + lax.ppermute(pick(halves, 1 - core, 2), "fsdp", other_core(fsdp_size))
    mine = pick(kept, chip, 1)
    mine = mine + lax.ppermute(pick(kept, 1 - chip, 1), "fsdp", other_chip(fsdp_size))
    rows = mine.reshape(size // 2, 2, -1)
    odd = ctx_index % 2
    row = pick(rows, odd, 1)
    row = row + lax.ppermute(pick(rows, 1 - odd, 1), "ctx", [(i, i ^ 1) for i in range(size)])
    pairs = size // 2
    total = pick(row, ctx_index // 2, 0)
    for k in range(1, pairs):
        total = total + lax.ppermute(
            pick(row, (ctx_index // 2 + k) % pairs, 0),
            "ctx",
            [(i, (i + 2 * k) % size) for i in range(size)],
        )
    return total


def column_pieces(weight, groups, size, ctx_index, extra):
    rows = weight.shape[0]
    width = weight.shape[1] // (groups * size)
    pieces = weight.reshape(rows, groups, size, width).transpose(2, 0, 1, 3)
    pieces = pieces.reshape(size, rows, groups * width)
    if extra is not None:
        count = extra.shape[0]
        more = -(-count // (groups * width * 16)) * 16
        extra = jnp.pad(extra, (0, more * groups * width - count))
        extra = jnp.broadcast_to(
            extra.reshape(1, more, groups * width), (size, more, groups * width)
        )
        pieces = jnp.concatenate([pieces, extra], axis=1)
    return exchange(pieces, size, ctx_index)


def merge_columns(pieces, groups, size):
    rows = pieces.shape[1]
    width = pieces.shape[2] // groups
    pieces = lax.all_to_all(pieces, "ctx", split_axis=0, concat_axis=0, tiled=True)
    pieces = pieces.reshape(size, rows, groups, width).transpose(1, 2, 0, 3)
    return pieces.reshape(rows, groups * size * width).astype(jnp.float32)


def local_split(
    ctx_size,
    fsdp_size,
    tokens,
    segments,
    routes,
    cotangent,
    w_qkv,
    b_qkv,
    w_out,
    gain_attn,
    gain_ffn,
    w_router,
    w_shared_gate,
    w_shared_in,
    w_shared_out,
    w_expert_in,
    w_expert_out,
):
    bf16, f32, i32 = jnp.bfloat16, jnp.float32, jnp.int32
    device_count = ctx_size * fsdp_size
    block_len = tokens.shape[2]
    width = tokens.shape[3]
    token_count = 2 * block_len
    top_count = routes.shape[3]
    seq_len = token_count * ctx_size
    ctx_index = lax.axis_index("ctx")
    expert_count = w_router.shape[1]
    capacity = token_count * top_count // expert_count
    own_heads = HEADS // ctx_size
    own_width = own_heads * HD
    fs_own = FS // ctx_size
    score_scale = HD ** (-0.5)

    def dot(a, b):
        return jnp.dot(a, b, preferred_element_type=f32)

    def dot_t(a, b):
        return lax.dot_general(a, b, (((1,), (1,)), ((), ())), preferred_element_type=f32)

    def t_dot(a, b):
        return lax.dot_general(a, b, (((0,), (0,)), ((), ())), preferred_element_type=f32)

    def own_rows(values):
        return lax.dynamic_index_in_dim(
            values.reshape((ctx_size, token_count) + values.shape[1:]), ctx_index, 0, keepdims=False
        )

    def sum_rows(grad):
        return lax.psum_scatter(
            grad.astype(bf16), "fsdp", scatter_dimension=0, tiled=True
        ).astype(f32)

    shard = width // device_count
    small = [gain_attn, gain_ffn, w_shared_gate, w_router.reshape(-1), b_qkv]
    small_size = sum(piece.shape[0] for piece in small)
    small = jnp.concatenate(small + [routes.astype(bf16).reshape(-1)], axis=0)
    small_count = small.shape[0]
    token_rows = ring_gather(tokens.reshape(token_count, width), ctx_size, ctx_index)
    pieces = column_pieces(w_qkv, 3, ctx_size, ctx_index, small)
    pieces = fsdp_join(pieces, *fsdp_pieces(pieces, fsdp_size), fsdp_size)
    pieces = pieces.transpose(1, 0, 2, 3)
    qkv_weight = pieces[:, :, :shard].reshape(width, 3 * own_width)
    small = pieces[:, :, shard:].reshape(device_count, -1)[:, :small_count]
    attn_gain = small[:, :shard].reshape(width).astype(f32)
    ffn_gain = small[:, shard : 2 * shard].reshape(width).astype(f32)
    gate_vector = small[:, 2 * shard : 3 * shard].reshape(width)
    router_end = 3 * shard + shard * expert_count
    router_weight = small[:, 3 * shard : router_end].reshape(width, expert_count)
    bias = small[:, router_end:small_size].reshape(3, ctx_size, own_width).astype(f32)
    bias = lax.dynamic_index_in_dim(bias, ctx_index, 1, keepdims=False).reshape(3 * own_width)
    route_rows = small[:, small_size:].astype(i32)
    route_rows = lax.dynamic_index_in_dim(
        route_rows.reshape(ctx_size, fsdp_size, -1), lax.axis_index("fsdp"), 1, keepdims=False
    ).reshape(ctx_size, token_count, top_count)

    expert_in = lax.all_gather(w_expert_in[0], "fsdp", axis=0, tiled=True)
    expert_out = lax.all_gather(w_expert_out[0], "fsdp", axis=0, tiled=True)
    out_shard, in_shard, token_rows = after(w_out, w_shared_in, token_rows)
    out_rows = ring_gather(out_shard, ctx_size, ctx_index)
    out_far, out_near = fsdp_pieces(out_rows, fsdp_size)
    shared_in = column_pieces(in_shard, 2, ctx_size, ctx_index, None)
    shared_in = lax.all_gather(shared_in, "fsdp", axis=0, tiled=False)
    shared_out = lax.all_gather(w_shared_out, "fsdp", axis=0, tiled=True)

    block_ids = jnp.arange(ctx_size, dtype=i32)[:, None]
    local_index = jnp.arange(block_len, dtype=i32)[None, :]
    positions = jnp.stack(
        [
            block_ids * block_len + local_index,
            seq_len - (block_ids + 1) * block_len + local_index,
        ],
        axis=1,
    ).reshape(seq_len)
    seg_rows = (
        segments.reshape(2, ctx_size, block_len).transpose(1, 0, 2).reshape(seq_len)
    )
    cos_tab, sine_tab = rope_tables(positions, HD)

    inputs = token_rows.astype(f32)
    normed, inv_one_all = rms_norm(inputs, attn_gain)
    normed_low = normed.astype(bf16)
    projected = dot(normed_low, qkv_weight) + bias
    head_shape = (seq_len, own_heads, HD)
    queries = rotate(projected[:, :own_width].reshape(head_shape), cos_tab, sine_tab).astype(bf16)
    keys = rotate(
        projected[:, own_width : 2 * own_width].reshape(head_shape), cos_tab, sine_tab
    ).astype(bf16)
    values = projected[:, 2 * own_width :].reshape(head_shape).astype(bf16)
    allowed = (positions[None, :] <= positions[:, None]) & (seg_rows[None, :] == seg_rows[:, None])
    scores = jnp.einsum("qhd,khd->hqk", queries, keys, preferred_element_type=f32) * score_scale
    scores = jnp.where(allowed[None], scores, MASK_FILL)
    top_score = jnp.max(scores, axis=-1, keepdims=True)
    log_total = top_score + jnp.log(jnp.sum(jnp.exp(scores - top_score), axis=-1, keepdims=True))
    weights = jnp.exp(scores - log_total)
    weights_low = weights.astype(bf16)
    attended = jnp.einsum("hqk,khd->qhd", weights_low, values, preferred_element_type=f32)
    attn_own = attended.astype(bf16).reshape(seq_len, own_width)
    out_rows, out_far, out_near, attn_own = after(out_rows, out_far, out_near, attn_own)
    out_weight = fsdp_join(out_rows, out_far, out_near, fsdp_size)
    out_weight = out_weight.reshape(fsdp_size, ctx_size, -1, width)
    out_weight = out_weight.transpose(1, 0, 2, 3).reshape(width, width)
    attn_rows = ring_gather_columns(attn_own, ctx_size, ctx_index)
    grad_block, attn_rows = after(cotangent, attn_rows)
    grad_rows = ring_gather(grad_block.reshape(token_count, width), ctx_size, ctx_index)
    residual = inputs + dot(attn_rows, out_weight)

    normed_two, inv_two_all = rms_norm(residual, ffn_gain)
    low_two = normed_two.astype(bf16)
    mixed_weight = jnp.concatenate([router_weight, gate_vector[:, None]], axis=1)
    logits = dot(low_two, mixed_weight)
    probs_all = jax.nn.softmax(logits[:, :expert_count], axis=-1)
    scale_all = jax.nn.sigmoid(logits[:, expert_count])
    gate_all = lax.dynamic_index_in_dim(probs_all, ctx_index, 1, keepdims=False)

    named = jnp.any(route_rows == ctx_index, axis=-1)
    before = jnp.arange(token_count)[:, None] < jnp.arange(token_count)[None, :]
    rank = dot(named.astype(bf16), before.astype(bf16)).astype(i32)
    slot_of = jnp.where(named & (rank < capacity), rank, -1)
    slot_mask = slot_of[:, None, :] == jnp.arange(capacity, dtype=i32)[None, :, None]
    slot_map = slot_mask.astype(bf16)
    blocks_two = low_two.reshape(ctx_size, token_count, width)
    blocks_grad = grad_rows.reshape(ctx_size, token_count, width)
    gate_blocks = gate_all.reshape(ctx_size, token_count)

    def to_slots(blocks):
        picked = jnp.einsum("bmt,btd->bmd", slot_map, blocks, preferred_element_type=f32)
        return picked.reshape(ctx_size * capacity, width)

    def to_tokens(slots):
        spread = jnp.einsum(
            "bmt,bmd->btd",
            slot_map,
            slots.reshape(ctx_size, capacity, width),
            preferred_element_type=f32,
        )
        return spread.reshape(seq_len, width)

    buffer = to_slots(blocks_two).astype(bf16)
    expert_pre = dot(buffer, expert_in)
    expert_hid = swiglu(expert_pre, FE).astype(bf16)
    expert_res = dot(expert_hid, expert_out).astype(bf16)
    routed = gate_all[:, None] * to_tokens(expert_res)

    shared_in, expert_res = after(shared_in, expert_res)
    shared_in = shared_in.transpose(1, 0, 2, 3).reshape(width, 2 * fs_own)
    shared_pre = dot(low_two, shared_in)
    shared_hid = swiglu(shared_pre, fs_own).astype(bf16)
    shared_res = dot(shared_hid, shared_out)
    out_parts = (scale_all[:, None] * shared_res + routed).astype(bf16)
    out_sum = ring_scatter(out_parts, ctx_size, ctx_index)

    grad_slots = to_slots(blocks_grad)
    gate_slots = jnp.sum(jnp.where(slot_mask, gate_blocks[:, None, :], 0.0), axis=-1).reshape(-1, 1)
    grad_res = (gate_slots * grad_slots).astype(bf16)
    slot_dots = jnp.sum(grad_slots * expert_res.astype(f32), axis=-1).reshape(ctx_size, capacity, 1)
    grad_gates = jnp.sum(jnp.where(slot_mask, slot_dots, 0.0), axis=1)
    grad_expert_out = t_dot(expert_hid, grad_res)
    grad_hid = dot_t(grad_res, expert_out)
    grad_pre = swiglu_back(expert_pre, FE, grad_hid).astype(bf16)
    grad_expert_in = t_dot(buffer, grad_pre)
    grad_buffer = dot_t(grad_pre, expert_in).astype(bf16)

    grad_expert_in, grad_expert_out, grad_shared_res = after(
        grad_expert_in.astype(bf16),
        grad_expert_out.astype(bf16),
        (scale_all[:, None] * grad_rows.astype(f32)).astype(bf16),
    )
    sum_expert_out = fsdp_scatter(
        grad_expert_out.reshape(fsdp_size, -1, width), fsdp_size, 0
    )
    sum_expert_in = sum_rows(grad_expert_in)

    grad_f32 = grad_rows.astype(f32)
    gate_dots = jnp.sum(grad_f32 * shared_res, axis=-1).reshape(ctx_size, token_count)
    grad_shared_out = t_dot(shared_hid, grad_shared_res)
    grad_shared_hid = dot_t(grad_shared_res, shared_out)
    grad_shared_pre = swiglu_back(shared_pre, fs_own, grad_shared_hid).astype(bf16)
    grad_shared_in = t_dot(low_two, grad_shared_pre)
    two_parts = (dot_t(grad_shared_pre, shared_in) + to_tokens(grad_buffer)).astype(bf16)
    grad_two = ring_scatter(two_parts, ctx_size, ctx_index)
    grad_two, out_sum = after(grad_two, out_sum)
    own_residual = own_rows(residual)
    output = (own_residual + out_sum).astype(bf16).reshape(tokens.shape)

    dots = jnp.stack([grad_gates, gate_dots], axis=1)
    dots = lax.all_to_all(dots, "ctx", split_axis=0, concat_axis=0, tiled=True)
    own_probs = own_rows(probs_all)
    own_scale = own_rows(scale_all)
    own_low = own_rows(low_two)
    own_chosen = routes.reshape(token_count, top_count)
    chosen_mask = jnp.any(
        own_chosen[..., None] == jnp.arange(expert_count, dtype=i32), axis=1
    )
    grad_probs = jnp.where(chosen_mask, dots[:, 0].T, 0.0)
    grad_logits = (
        own_probs * (grad_probs - jnp.sum(own_probs * grad_probs, axis=-1, keepdims=True))
    ).astype(bf16)
    grad_gate_pre = (jnp.sum(dots[:, 1], axis=0) * own_scale * (1.0 - own_scale)).astype(bf16)
    grad_router = t_dot(own_low, grad_logits)
    grad_gate_vector = t_dot(own_low, grad_gate_pre[:, None])
    grad_two = grad_two + dot_t(grad_logits, router_weight)
    grad_two = grad_two + grad_gate_pre.astype(f32)[:, None] * gate_vector.astype(f32)[None, :]
    grad_resid_norm, grad_gain_two = rms_back(
        own_residual, own_rows(inv_two_all), ffn_gain, grad_two
    )
    grad_resid = cotangent.reshape(token_count, width).astype(f32) + grad_resid_norm

    grad_mixed = grad_resid.astype(bf16)
    grad_attn_rows = dot_t(grad_mixed, out_weight).astype(bf16)
    grad_attn = lax.all_to_all(
        grad_attn_rows.reshape(token_count, ctx_size, own_width).transpose(1, 0, 2),
        "ctx",
        split_axis=0,
        concat_axis=0,
        tiled=True,
    ).reshape(head_shape)
    grad_attn, sum_expert_out = after(grad_attn, sum_expert_out)
    mixed_all = ring_gather(grad_mixed, ctx_size, ctx_index)
    grad_weights = jnp.einsum("qhd,khd->hqk", grad_attn, values, preferred_element_type=f32)
    delta = jnp.sum(weights * grad_weights, axis=-1, keepdims=True)
    grad_scores = jnp.where(allowed[None], weights * (grad_weights - delta), 0.0).astype(bf16)
    grad_q = jnp.einsum("hqk,khd->qhd", grad_scores, keys, preferred_element_type=f32) * score_scale
    grad_k = (
        jnp.einsum("hqk,qhd->khd", grad_scores, queries, preferred_element_type=f32) * score_scale
    )
    grad_v = jnp.einsum("hqk,qhd->khd", weights_low, grad_attn, preferred_element_type=f32)
    grad_projected = jnp.concatenate(
        [
            rotate_back(grad_q, cos_tab, sine_tab).reshape(seq_len, own_width),
            rotate_back(grad_k, cos_tab, sine_tab).reshape(seq_len, own_width),
            grad_v.reshape(seq_len, own_width),
        ],
        axis=-1,
    ).astype(bf16)
    grad_projected, mixed_all, sum_expert_in = after(grad_projected, mixed_all, sum_expert_in)
    one_sums = dot_t(grad_projected, qkv_weight)
    grad_gain_one = jnp.sum(one_sums * inputs * inv_one_all, axis=0)
    one_parts = one_sums.astype(bf16)
    grad_normed = ring_scatter(one_parts, ctx_size, ctx_index)
    grad_inputs_norm, unused = rms_back(
        tokens.reshape(token_count, width).astype(f32),
        own_rows(inv_one_all),
        attn_gain,
        grad_normed,
    )
    grad_tokens = (grad_resid + grad_inputs_norm).reshape(tokens.shape)
    grad_qkv_weight = t_dot(normed_low, grad_projected)
    grad_bias = jnp.sum(grad_projected.astype(f32), axis=0).reshape(3, 1, own_width)
    grad_bias = jnp.where(
        jnp.arange(ctx_size, dtype=i32)[None, :, None] == ctx_index, grad_bias, 0.0
    )

    grad_out_weight = t_dot(attn_own, mixed_all)
    sum_qkv_weight = fsdp_scatter(
        grad_qkv_weight.astype(bf16).reshape(ctx_size, fsdp_size, shard, 3 * own_width),
        fsdp_size,
        1,
    ).astype(bf16)
    sum_shared_in = grad_shared_in.astype(bf16).reshape(ctx_size, fsdp_size, shard, 2 * fs_own)
    sum_shared_in = lax.psum_scatter(
        sum_shared_in.transpose(1, 0, 2, 3).reshape(width, 2 * fs_own),
        "fsdp",
        scatter_dimension=0,
        tiled=True,
    ).reshape(ctx_size, shard, 2 * fs_own)
    small_grads = jnp.concatenate(
        [
            piece.reshape(device_count, -1)
            for piece in (grad_gain_one, grad_gain_two, grad_gate_vector, grad_router, grad_bias)
        ],
        axis=1,
    )
    small_grads = small_grads.reshape(ctx_size, fsdp_size, small_size)
    small_grads = small_scatter(small_grads, ctx_size, fsdp_size, ctx_index).reshape(small_size)
    return (
        output,
        grad_tokens,
        merge_columns(sum_qkv_weight, 3, ctx_size),
        small_grads[router_end:],
        sum_rows(grad_out_weight),
        small_grads[:shard],
        small_grads[shard : 2 * shard],
        small_grads[3 * shard : router_end].reshape(shard, expert_count),
        small_grads[2 * shard : 3 * shard],
        merge_columns(sum_shared_in, 2, ctx_size),
        sum_rows(grad_shared_out),
        sum_expert_in[None],
        sum_expert_out[None],
    )


def local_wide(
    tokens,
    segments,
    routes,
    cotangent,
    w_qkv,
    b_qkv,
    w_out,
    gain_attn,
    gain_ffn,
    w_router,
    w_shared_gate,
    w_shared_in,
    w_shared_out,
    w_expert_in,
    w_expert_out,
):
    block_len = tokens.shape[2]
    model_width = tokens.shape[3]
    token_count = 2 * block_len
    top_count = routes.shape[3]
    half_len = segments.shape[2]
    seq_len = 2 * half_len
    ctx_index = lax.axis_index("ctx")
    head_count = model_width // HD
    expert_count = w_router.shape[1]
    capacity = token_count * top_count // expert_count
    slot_count = expert_count * capacity
    key_rows = min(512, seq_len)
    key_blocks = seq_len // key_rows
    score_scale = HD ** (-0.5)
    head_shape = (token_count, head_count, HD)
    attn_set = (
        lax.all_gather(w_qkv, ("ctx", "fsdp"), axis=0, tiled=True),
        lax.all_gather(b_qkv, ("ctx", "fsdp"), axis=0, tiled=True),
        lax.all_gather(w_out, ("ctx", "fsdp"), axis=0, tiled=True),
        lax.all_gather(gain_attn, ("ctx", "fsdp"), axis=0, tiled=True),
    )
    qkv_weight, qkv_bias, out_weight, attn_gain = attn_set
    inputs = tokens.reshape(token_count, model_width).astype(jnp.float32)
    normed, inv_one = rms_norm(inputs, attn_gain.astype(jnp.float32))
    normed_low = normed.astype(jnp.bfloat16)
    projected = jnp.dot(
        normed_low, qkv_weight, preferred_element_type=jnp.float32
    ) + qkv_bias.astype(jnp.float32)
    local_index = jnp.arange(block_len, dtype=jnp.int32)
    query_pos = jnp.concatenate(
        [ctx_index * block_len + local_index, seq_len - (ctx_index + 1) * block_len + local_index]
    )
    half_index = jnp.arange(half_len, dtype=jnp.int32)
    key_pos = jnp.concatenate(
        [half_index, seq_len - block_len * (half_index // block_len + 1) + half_index % block_len]
    ).reshape(key_blocks, key_rows)
    key_seg = segments.reshape(key_blocks, key_rows)
    query_seg = lax.dynamic_slice_in_dim(segments[0], ctx_index * block_len, block_len, 1).reshape(
        token_count
    )
    cos_tab, sine_tab = rope_tables(query_pos, HD)
    queries = rotate(projected[:, :model_width].reshape(head_shape), cos_tab, sine_tab).astype(
        jnp.bfloat16
    )
    keys_own = rotate(
        projected[:, model_width : 2 * model_width].reshape(head_shape), cos_tab, sine_tab
    ).astype(jnp.bfloat16)
    values_own = projected[:, 2 * model_width :].astype(jnp.bfloat16)
    keys_all, values_all = (
        lax.all_gather(keys_own.reshape(2, block_len, model_width), "ctx", axis=1, tiled=True),
        lax.all_gather(values_own.reshape(2, block_len, model_width), "ctx", axis=1, tiled=True),
    )
    keys_all = keys_all.reshape(key_blocks, key_rows, head_count, HD)
    values_all = values_all.reshape(key_blocks, key_rows, head_count, HD)

    def score_block(key_blk, pos_blk, seg_blk):
        raw_scores = (
            jnp.einsum("qhd,khd->hqk", queries, key_blk, preferred_element_type=jnp.float32)
            * score_scale
        )
        allowed = (pos_blk[None, :] <= query_pos[:, None]) & (
            seg_blk[None, :] == query_seg[:, None]
        )
        return (jnp.where(allowed[None], raw_scores, MASK_FILL), allowed)

    def total_step(running, key_part):
        run_max, run_sum = running
        scores = score_block(key_part[0], key_part[1], key_part[2])[0]
        new_max = jnp.maximum(run_max, jnp.max(scores, axis=-1))
        run_sum = run_sum * jnp.exp(run_max - new_max) + jnp.sum(
            jnp.exp(scores - new_max[..., None]), axis=-1
        )
        return ((new_max, run_sum), None)

    start_max = jnp.full((head_count, token_count), MASK_FILL, jnp.float32)
    start_sum = jnp.zeros((head_count, token_count), jnp.float32)
    (run_max, run_sum), unused = lax.scan(
        total_step, (start_max, start_sum), (keys_all, key_pos, key_seg)
    )
    log_total = run_max + jnp.log(run_sum)

    def attend_step(summed, key_part):
        key_blk, value_blk, pos_blk, seg_blk = key_part
        scores = score_block(key_blk, pos_blk, seg_blk)[0]
        weights = jnp.exp(scores - log_total[..., None]).astype(jnp.bfloat16)
        return (
            summed
            + jnp.einsum("hqk,khd->qhd", weights, value_blk, preferred_element_type=jnp.float32),
            None,
        )

    key_stack = (keys_all, values_all, key_pos, key_seg)
    attended, unused = lax.scan(attend_step, jnp.zeros(head_shape, jnp.float32), key_stack)
    attn_low = attended.reshape(token_count, model_width).astype(jnp.bfloat16)
    residual = inputs + jnp.dot(attn_low, out_weight, preferred_element_type=jnp.float32)
    ffn_set = (
        lax.all_gather(gain_ffn, ("ctx", "fsdp"), axis=0, tiled=True),
        lax.all_gather(w_router, ("ctx", "fsdp"), axis=0, tiled=True),
        lax.all_gather(w_shared_gate, ("ctx", "fsdp"), axis=0, tiled=True),
        lax.all_gather(w_shared_in, ("ctx", "fsdp"), axis=0, tiled=True),
        lax.all_gather(w_shared_out, ("ctx", "fsdp"), axis=0, tiled=True),
    )
    ffn_gain, router_weight, gate_vector, shared_in, shared_out = ffn_set
    normed_two, inv_two = rms_norm(residual, ffn_gain.astype(jnp.float32))
    low_two = normed_two.astype(jnp.bfloat16)
    logits = jnp.dot(low_two, router_weight, preferred_element_type=jnp.float32)
    router_probs = jax.nn.softmax(logits, axis=-1)
    chosen = routes.reshape(token_count, top_count)
    chosen_mask = chosen[..., None] == jnp.arange(expert_count, dtype=jnp.int32)
    gate_vals = jnp.sum(jnp.where(chosen_mask, router_probs[:, None, :], 0.0), axis=-1)
    shared_scale = jax.nn.sigmoid(jnp.dot(low_two, gate_vector, preferred_element_type=jnp.float32))
    shared_pre = jnp.dot(low_two, shared_in, preferred_element_type=jnp.float32)
    shared_hid = swiglu(shared_pre, FS).astype(jnp.bfloat16)
    shared_res = jnp.dot(shared_hid, shared_out, preferred_element_type=jnp.float32)
    pair_routes = chosen.reshape(token_count * top_count)
    expert_marks = (
        pair_routes[:, None] == jnp.arange(expert_count, dtype=jnp.int32)[None, :]
    ).astype(jnp.int32)
    pair_ranks = jnp.sum((jnp.cumsum(expert_marks, axis=0) - expert_marks) * expert_marks, axis=1)
    pair_target = jnp.where(pair_ranks < capacity, pair_routes * capacity + pair_ranks, -1)
    pair_map = pair_target[:, None] == jnp.arange(slot_count, dtype=jnp.int32)[None, :]
    pair_low = pair_map.astype(jnp.bfloat16)
    token_map = jnp.sum(
        pair_map.reshape(token_count, top_count, slot_count).astype(jnp.int32), axis=1
    ).astype(jnp.bfloat16)
    outgoing = jnp.einsum(
        "tc,td->cd", token_map, low_two, preferred_element_type=jnp.float32
    ).astype(jnp.bfloat16)
    incoming = lax.all_to_all(
        outgoing.reshape(expert_count, capacity, model_width),
        "ctx",
        split_axis=0,
        concat_axis=1,
        tiled=True,
    )
    expert_in, expert_out = (
        lax.all_gather(w_expert_in, "fsdp", axis=1, tiled=True),
        lax.all_gather(w_expert_out, "fsdp", axis=1, tiled=True),
    )
    expert_pre = jnp.einsum("erd,edf->erf", incoming, expert_in, preferred_element_type=jnp.float32)
    expert_hid = swiglu(expert_pre, FE).astype(jnp.bfloat16)
    expert_res = jnp.einsum(
        "erf,efd->erd", expert_hid, expert_out, preferred_element_type=jnp.float32
    ).astype(jnp.bfloat16)
    returned = lax.all_to_all(expert_res, "ctx", split_axis=1, concat_axis=0, tiled=True).reshape(
        slot_count, model_width
    )
    pair_vals = jnp.dot(pair_low, returned, preferred_element_type=jnp.float32).reshape(
        token_count, top_count, model_width
    )
    routed = jnp.sum(gate_vals[..., None] * pair_vals, axis=1)
    output = (
        (residual + shared_scale[:, None] * shared_res + routed)
        .astype(jnp.bfloat16)
        .reshape(tokens.shape)
    )
    grad_out = cotangent.reshape(token_count, model_width).astype(jnp.float32)
    pair_grads = gate_vals[..., None] * grad_out[:, None, :]
    grad_gates = jnp.sum(grad_out[:, None, :] * pair_vals, axis=-1)
    grad_returned = jnp.einsum(
        "pc,pd->cd",
        pair_map.astype(jnp.float32),
        pair_grads.reshape(token_count * top_count, model_width),
        precision=HIGHEST,
    ).astype(jnp.bfloat16)
    grad_res = lax.all_to_all(
        grad_returned.reshape(expert_count, capacity, model_width),
        "ctx",
        split_axis=0,
        concat_axis=1,
        tiled=True,
    )
    grad_expert_out = jnp.einsum(
        "erf,erd->efd", expert_hid, grad_res, preferred_element_type=jnp.float32
    )
    grad_hid = jnp.einsum("erd,efd->erf", grad_res, expert_out, preferred_element_type=jnp.float32)
    grad_pre = swiglu_back(expert_pre, FE, grad_hid).astype(jnp.bfloat16)
    grad_expert_in = jnp.einsum(
        "erd,erf->edf", incoming, grad_pre, preferred_element_type=jnp.float32
    )
    grad_incoming = jnp.einsum(
        "erf,edf->erd", grad_pre, expert_in, preferred_element_type=jnp.float32
    ).astype(jnp.bfloat16)
    grad_outgoing = lax.all_to_all(
        grad_incoming, "ctx", split_axis=1, concat_axis=0, tiled=True
    ).reshape(slot_count, model_width)
    expert_grads = (
        lax.psum_scatter(
            grad_expert_in.astype(jnp.bfloat16), "fsdp", scatter_dimension=1, tiled=True
        ).astype(jnp.float32),
        lax.psum_scatter(
            grad_expert_out.astype(jnp.bfloat16), "fsdp", scatter_dimension=1, tiled=True
        ).astype(jnp.float32),
    )
    grad_two = jnp.einsum("tc,cd->td", token_map, grad_outgoing, preferred_element_type=jnp.float32)
    grad_probs = jnp.sum(jnp.where(chosen_mask, grad_gates[..., None], 0.0), axis=1)
    grad_logits = (
        router_probs * (grad_probs - jnp.sum(router_probs * grad_probs, axis=-1, keepdims=True))
    ).astype(jnp.bfloat16)
    grad_router = jnp.einsum("td,te->de", low_two, grad_logits, preferred_element_type=jnp.float32)
    grad_shared_res = (shared_scale[:, None] * grad_out).astype(jnp.bfloat16)
    grad_gate_pre = (
        jnp.sum(grad_out * shared_res, axis=-1) * shared_scale * (1.0 - shared_scale)
    ).astype(jnp.bfloat16)
    grad_shared_out = jnp.einsum(
        "tf,td->fd", shared_hid, grad_shared_res, preferred_element_type=jnp.float32
    )
    grad_shared_hid = jnp.einsum(
        "td,fd->tf", grad_shared_res, shared_out, preferred_element_type=jnp.float32
    )
    grad_shared_pre = swiglu_back(shared_pre, FS, grad_shared_hid).astype(jnp.bfloat16)
    grad_shared_in = jnp.einsum(
        "td,tf->df", low_two, grad_shared_pre, preferred_element_type=jnp.float32
    )
    grad_gate_vector = jnp.einsum(
        "td,t->d", low_two, grad_gate_pre, preferred_element_type=jnp.float32
    )
    grad_two = grad_two + jnp.einsum(
        "te,de->td", grad_logits, router_weight, preferred_element_type=jnp.float32
    )
    grad_two = grad_two + jnp.einsum(
        "tf,df->td", grad_shared_pre, shared_in, preferred_element_type=jnp.float32
    )
    grad_two = (
        grad_two
        + grad_gate_pre.astype(jnp.float32)[:, None] * gate_vector.astype(jnp.float32)[None, :]
    )
    grad_resid_norm, grad_gain_two = rms_back(
        residual, inv_two, ffn_gain.astype(jnp.float32), grad_two
    )
    grad_resid = grad_out + grad_resid_norm
    ffn_grads = (
        lax.psum_scatter(grad_gain_two, ("ctx", "fsdp"), scatter_dimension=0, tiled=True),
        lax.psum_scatter(grad_router, ("ctx", "fsdp"), scatter_dimension=0, tiled=True),
        lax.psum_scatter(grad_gate_vector, ("ctx", "fsdp"), scatter_dimension=0, tiled=True),
        lax.psum_scatter(grad_shared_in, ("ctx", "fsdp"), scatter_dimension=0, tiled=True),
        lax.psum_scatter(grad_shared_out, ("ctx", "fsdp"), scatter_dimension=0, tiled=True),
    )
    grad_mixed = grad_resid.astype(jnp.bfloat16)
    grad_out_weight = jnp.einsum(
        "tc,td->cd", attn_low, grad_mixed, preferred_element_type=jnp.float32
    )
    grad_attn = (
        jnp.einsum("td,cd->tc", grad_mixed, out_weight, preferred_element_type=jnp.float32)
        .astype(jnp.bfloat16)
        .reshape(head_shape)
    )

    def delta_step(summed, key_part):
        key_blk, value_blk, pos_blk, seg_blk = key_part
        weights = jnp.exp(score_block(key_blk, pos_blk, seg_blk)[0] - log_total[..., None])
        grad_weights = jnp.einsum(
            "qhd,khd->hqk", grad_attn, value_blk, preferred_element_type=jnp.float32
        )
        return (summed + jnp.sum(weights * grad_weights, axis=-1), None)

    delta_sum, unused = lax.scan(
        delta_step, jnp.zeros((head_count, token_count), jnp.float32), key_stack
    )

    def grad_step(summed, key_part):
        key_blk, value_blk, pos_blk, seg_blk = key_part
        scores, allowed = score_block(key_blk, pos_blk, seg_blk)
        weights = jnp.exp(scores - log_total[..., None])
        grad_weights = jnp.einsum(
            "qhd,khd->hqk", grad_attn, value_blk, preferred_element_type=jnp.float32
        )
        grad_scores = jnp.where(
            allowed[None], weights * (grad_weights - delta_sum[..., None]), 0.0
        ).astype(jnp.bfloat16)
        summed = (
            summed
            + jnp.einsum("hqk,khd->qhd", grad_scores, key_blk, preferred_element_type=jnp.float32)
            * score_scale
        )
        grad_key = (
            jnp.einsum("hqk,qhd->khd", grad_scores, queries, preferred_element_type=jnp.float32)
            * score_scale
        )
        grad_value = jnp.einsum(
            "hqk,qhd->khd",
            weights.astype(jnp.bfloat16),
            grad_attn,
            preferred_element_type=jnp.float32,
        )
        return (summed, (grad_key, grad_value))

    grad_query, (grad_keys, grad_values) = lax.scan(
        grad_step, jnp.zeros(head_shape, jnp.float32), key_stack
    )
    grad_keys_own, grad_values_own = (
        lax.psum_scatter(
            grad_keys.reshape(2, half_len, model_width).astype(jnp.bfloat16),
            "ctx",
            scatter_dimension=1,
            tiled=True,
        ).astype(jnp.float32),
        lax.psum_scatter(
            grad_values.reshape(2, half_len, model_width).astype(jnp.bfloat16),
            "ctx",
            scatter_dimension=1,
            tiled=True,
        ).astype(jnp.float32),
    )
    grad_q_rows = rotate_back(grad_query, cos_tab, sine_tab).reshape(token_count, model_width)
    grad_k_rows = rotate_back(grad_keys_own.reshape(head_shape), cos_tab, sine_tab).reshape(
        token_count, model_width
    )
    grad_projected = jnp.concatenate(
        [grad_q_rows, grad_k_rows, grad_values_own.reshape(token_count, model_width)], axis=-1
    ).astype(jnp.bfloat16)
    grad_qkv_weight = jnp.einsum(
        "td,te->de", normed_low, grad_projected, preferred_element_type=jnp.float32
    )
    grad_qkv_bias = jnp.sum(grad_projected.astype(jnp.float32), axis=0)
    grad_normed = jnp.einsum(
        "te,de->td", grad_projected, qkv_weight, preferred_element_type=jnp.float32
    )
    grad_inputs_norm, grad_gain_one = rms_back(
        inputs, inv_one, attn_gain.astype(jnp.float32), grad_normed
    )
    grad_tokens = (grad_resid + grad_inputs_norm).reshape(tokens.shape)
    attn_grads = (
        lax.psum_scatter(grad_qkv_weight, ("ctx", "fsdp"), scatter_dimension=0, tiled=True),
        lax.psum_scatter(grad_qkv_bias, ("ctx", "fsdp"), scatter_dimension=0, tiled=True),
        lax.psum_scatter(grad_out_weight, ("ctx", "fsdp"), scatter_dimension=0, tiled=True),
        lax.psum_scatter(grad_gain_one, ("ctx", "fsdp"), scatter_dimension=0, tiled=True),
    )
    return (
        output,
        grad_tokens,
        attn_grads[0],
        attn_grads[1],
        attn_grads[2],
        attn_grads[3],
        ffn_grads[0],
        ffn_grads[1],
        ffn_grads[2],
        ffn_grads[3],
        ffn_grads[4],
        expert_grads[0],
        expert_grads[1],
    )


def solution(mesh):
    in_specs = (
        P("fsdp", None, "ctx", None),
        P("fsdp", None, None),
        P("fsdp", None, "ctx", None),
        P("fsdp", None, "ctx", None),
        P(("ctx", "fsdp"), None),
        P(("ctx", "fsdp")),
        P(("ctx", "fsdp"), None),
        P(("ctx", "fsdp")),
        P(("ctx", "fsdp")),
        P(("ctx", "fsdp"), None),
        P(("ctx", "fsdp")),
        P(("ctx", "fsdp"), None),
        P(("ctx", "fsdp"), None),
        P("ctx", "fsdp", None),
        P("ctx", "fsdp", None),
    )
    out_specs = (
        P("fsdp", None, "ctx", None),
        P("fsdp", None, "ctx", None),
        P(("ctx", "fsdp"), None),
        P(("ctx", "fsdp")),
        P(("ctx", "fsdp"), None),
        P(("ctx", "fsdp")),
        P(("ctx", "fsdp")),
        P(("ctx", "fsdp"), None),
        P(("ctx", "fsdp")),
        P(("ctx", "fsdp"), None),
        P(("ctx", "fsdp"), None),
        P("ctx", "fsdp", None),
        P("ctx", "fsdp", None),
    )
    ctx_size = mesh.shape["ctx"]
    fsdp_size = mesh.shape["fsdp"]

    def local(*arrays):
        if HEADS % ctx_size:
            return local_wide(*arrays)
        return local_split(ctx_size, fsdp_size, *arrays)

    return jax.shard_map(local, mesh=mesh, in_specs=in_specs, out_specs=out_specs, check_vma=False)
```

```python
import jax
import jax.numpy as jnp
from jax import lax
from jax.sharding import PartitionSpec as P

HD = 128
HEADS = 16
FS = 5632
FE = 1408


RMS_EPS = 1e-06
ROPE_THETA = 1000000.0
MASK_FILL = -1e30
HIGHEST = lax.Precision.HIGHEST


def rope_tables(positions, head_dim):
    half_dim = head_dim // 2
    inv_freq = ROPE_THETA ** (-(jnp.arange(half_dim, dtype=jnp.float32) * 2.0 / head_dim))
    angles = positions.astype(jnp.float32)[:, None] * inv_freq[None, :]
    cos_tab = jnp.concatenate([jnp.cos(angles), jnp.cos(angles)], axis=-1)
    sine_tab = jnp.concatenate([jnp.sin(angles), jnp.sin(angles)], axis=-1)
    return (cos_tab, sine_tab)


def rotate(values, cos_tab, sine_tab):
    half_dim = values.shape[-1] // 2
    turned = jnp.concatenate([-values[..., half_dim:], values[..., :half_dim]], axis=-1)
    return values * cos_tab[:, None, :] + turned * sine_tab[:, None, :]


def rotate_back(upstream, cos_tab, sine_tab):
    half_dim = upstream.shape[-1] // 2
    scaled = upstream * sine_tab[:, None, :]
    return upstream * cos_tab[:, None, :] + jnp.concatenate(
        [scaled[..., half_dim:], -scaled[..., :half_dim]], axis=-1
    )


def rms_norm(values, gain_vec):
    inv_rms = lax.rsqrt(jnp.mean(values * values, axis=-1, keepdims=True) + RMS_EPS)
    return (values * inv_rms * gain_vec, inv_rms)


def rms_back(values, inv_rms, gain_vec, upstream):
    weighted = upstream * gain_vec
    inner_mean = jnp.mean(weighted * values, axis=-1, keepdims=True)
    return (
        inv_rms * weighted - values * inv_rms * inv_rms * inv_rms * inner_mean,
        jnp.sum(upstream * values * inv_rms, axis=0),
    )


def swiglu(pre_act, split_at):
    return jax.nn.silu(pre_act[..., :split_at]) * pre_act[..., split_at:]


def swiglu_back(pre_act, split_at, upstream):
    gate_part = pre_act[..., :split_at]
    up_part = pre_act[..., split_at:]
    sigmoid_g = jax.nn.sigmoid(gate_part)
    d_gate = upstream * up_part * sigmoid_g * (1.0 + gate_part * (1.0 - sigmoid_g))
    d_up = upstream * gate_part * sigmoid_g
    return jnp.concatenate([d_gate, d_up], axis=-1)


def ring_order(size):
    return list(range(0, size, 2)) + list(range(size - 1, 0, -2))


def ring_steps(size):
    order = ring_order(size)
    ahead = [(order[i], order[(i + 1) % size]) for i in range(size)]
    back = [(dst, src) for src, dst in ahead]
    return (ahead, back)


def ring_peers(size, ctx_index):
    order = ring_order(size)
    place = {dev: i for i, dev in enumerate(order)}
    table = jnp.array(
        [[order[(place[dev] + k) % size] for k in range(size)] for dev in range(size)], jnp.int32
    )
    row = lax.dynamic_index_in_dim(table, ctx_index, 0, keepdims=False)
    return [row[k] for k in range(size)]


def ring_walk(block, size, ctx_index, out, put):
    rows = block.shape[0]
    ahead, back = ring_steps(size)
    peers = ring_peers(size, ctx_index)
    half = size // 2
    out = put(out, block, ctx_index, 0)
    fore = rear = block
    for k in range(1, half):
        fore = lax.ppermute(fore, "ctx", ahead)
        rear = lax.ppermute(rear, "ctx", back)
        out = put(out, fore, peers[size - k], 0)
        out = put(out, rear, peers[k], 0)
    fore = lax.ppermute(fore[: rows // 2], "ctx", ahead)
    rear = lax.ppermute(rear[rows // 2 :], "ctx", back)
    out = put(out, fore, peers[half], 0)
    return put(out, rear, peers[half], rows // 2)


def ring_gather(block, size, ctx_index):
    rows, width = block.shape

    def put(out, piece, peer, offset):
        return lax.dynamic_update_slice(out, piece, (peer * rows + offset, jnp.zeros_like(peer)))

    return ring_walk(block, size, ctx_index, jnp.zeros((size * rows, width), block.dtype), put)


def ring_gather_columns(block, size, ctx_index):
    rows, width = block.shape

    def put(out, piece, peer, offset):
        return lax.dynamic_update_slice(out, piece, (jnp.full_like(peer, offset), peer * width))

    return ring_walk(block, size, ctx_index, jnp.zeros((rows, size * width), block.dtype), put)


def ring_sums(parts, size, ctx_index):
    f32 = jnp.float32
    rows = parts.shape[0] // size
    ahead, back = ring_steps(size)
    peers = ring_peers(size, ctx_index)
    half = size // 2

    def own(k, start, count):
        first = (peers[k % size] * rows + start, jnp.zeros_like(peers[0]))
        return lax.dynamic_slice(parts, first, (count, parts.shape[1])).astype(f32)

    def low(values):
        return values.astype(jnp.bfloat16)

    cut = rows // 2
    fore = lax.ppermute(low(own(half, 0, cut)), "ctx", ahead)
    rear = lax.ppermute(low(own(half, cut, cut)), "ctx", back)
    fore = jnp.concatenate(
        [low(fore.astype(f32) + own(half - 1, 0, cut)), low(own(half - 1, cut, cut))], axis=0
    )
    rear = jnp.concatenate(
        [low(own(1 - half, 0, cut)), low(rear.astype(f32) + own(1 - half, cut, cut))], axis=0
    )
    for k in range(half - 1, 0, -1):
        fore = lax.ppermute(fore, "ctx", ahead)
        rear = lax.ppermute(rear, "ctx", back)
        if k > 1:
            fore = low(fore.astype(f32) + own(k - 1, 0, rows))
            rear = low(rear.astype(f32) + own(1 - k, 0, rows))
    return (fore, rear)


def ring_scatter(parts, size, ctx_index, kept=None):
    fore, rear = ring_sums(parts, size, ctx_index)
    kept = (parts if kept is None else kept).reshape(size, -1, parts.shape[1])
    kept = lax.dynamic_index_in_dim(kept, ctx_index, 0, keepdims=False)
    return kept.astype(jnp.float32) + fore.astype(jnp.float32) + rear.astype(jnp.float32)


def other_core(size):
    return [(i, i ^ 1) for i in range(size)]


def other_chip(size):
    return [(i, i ^ 2) for i in range(size)]


def fsdp_join(shard, size):
    index = lax.axis_index("fsdp")
    far = lax.ppermute(shard, "fsdp", other_chip(size))
    near = lax.ppermute(shard, "fsdp", other_core(size))
    far_near = lax.ppermute(far, "fsdp", other_core(size))
    out = jnp.zeros((size,) + shard.shape, shard.dtype)
    for piece, peer in ((shard, index), (near, index ^ 1), (far, index ^ 2), (far_near, index ^ 3)):
        out = lax.dynamic_update_index_in_dim(out, piece, peer, 0)
    return out


def after(value, *deps):
    return lax.optimization_barrier((value,) + deps)


def fsdp_scatter(grad, size, axis):
    index = lax.axis_index("fsdp")

    def pick(peer):
        return lax.dynamic_index_in_dim(grad, peer, axis, keepdims=False)

    far_near = lax.ppermute(pick(index ^ 3), "fsdp", other_core(size))
    near = lax.ppermute(pick(index ^ 1), "fsdp", other_core(size))
    far = (pick(index ^ 2).astype(jnp.float32) + far_near.astype(jnp.float32)).astype(jnp.bfloat16)
    far = lax.ppermute(far, "fsdp", other_chip(size))
    return pick(index).astype(jnp.float32) + near.astype(jnp.float32) + far.astype(jnp.float32)


def exchange(pieces, size, ctx_index):
    out = jnp.zeros_like(pieces)
    own = lax.dynamic_index_in_dim(pieces, ctx_index, 0, keepdims=False)
    out = lax.dynamic_update_index_in_dim(out, own, ctx_index, 0)
    for k in range(1, size):
        piece = lax.dynamic_index_in_dim(pieces, (ctx_index + k) % size, 0, keepdims=False)
        piece = lax.ppermute(piece, "ctx", [(i, (i + k) % size) for i in range(size)])
        out = lax.dynamic_update_index_in_dim(out, piece, (ctx_index - k) % size, 0)
    return out


def small_scatter(parts, size, fsdp_size, ctx_index):
    index = lax.axis_index("fsdp")

    def pick(array, at, axis):
        return lax.dynamic_index_in_dim(array, at, axis, keepdims=False)

    halves = parts.reshape(size, fsdp_size // 2, 2, -1)
    core, chip = index % 2, index // 2
    kept = pick(halves, core, 2)
    kept = kept + lax.ppermute(pick(halves, 1 - core, 2), "fsdp", other_core(fsdp_size))
    mine = pick(kept, chip, 1)
    mine = mine + lax.ppermute(pick(kept, 1 - chip, 1), "fsdp", other_chip(fsdp_size))
    rows = mine.reshape(size // 2, 2, -1)
    odd = ctx_index % 2
    row = pick(rows, odd, 1)
    row = row + lax.ppermute(pick(rows, 1 - odd, 1), "ctx", [(i, i ^ 1) for i in range(size)])
    pairs = size // 2
    total = pick(row, ctx_index // 2, 0)
    for k in range(1, pairs):
        total = total + lax.ppermute(
            pick(row, (ctx_index // 2 + k) % pairs, 0),
            "ctx",
            [(i, (i + 2 * k) % size) for i in range(size)],
        )
    return total


def column_pieces(weight, groups, size, ctx_index, extra):
    rows = weight.shape[0]
    width = weight.shape[1] // (groups * size)
    pieces = weight.reshape(rows, groups, size, width).transpose(2, 0, 1, 3)
    pieces = pieces.reshape(size, rows, groups * width)
    if extra is not None:
        count = extra.shape[0]
        more = -(-count // (groups * width * 16)) * 16
        extra = jnp.pad(extra, (0, more * groups * width - count))
        extra = jnp.broadcast_to(
            extra.reshape(1, more, groups * width), (size, more, groups * width)
        )
        pieces = jnp.concatenate([pieces, extra], axis=1)
    return exchange(pieces, size, ctx_index)


def merge_columns(pieces, groups, size):
    rows = pieces.shape[1]
    width = pieces.shape[2] // groups
    pieces = lax.all_to_all(pieces, "ctx", split_axis=0, concat_axis=0, tiled=True)
    pieces = pieces.reshape(size, rows, groups, width).transpose(1, 2, 0, 3)
    return pieces.reshape(rows, groups * size * width).astype(jnp.float32)


def local_split(
    ctx_size,
    fsdp_size,
    tokens,
    segments,
    routes,
    cotangent,
    w_qkv,
    b_qkv,
    w_out,
    gain_attn,
    gain_ffn,
    w_router,
    w_shared_gate,
    w_shared_in,
    w_shared_out,
    w_expert_in,
    w_expert_out,
):
    bf16, f32, i32 = jnp.bfloat16, jnp.float32, jnp.int32
    device_count = ctx_size * fsdp_size
    block_len = tokens.shape[2]
    width = tokens.shape[3]
    token_count = 2 * block_len
    top_count = routes.shape[3]
    seq_len = token_count * ctx_size
    ctx_index = lax.axis_index("ctx")
    expert_count = w_router.shape[1]
    capacity = token_count * top_count // expert_count
    own_heads = HEADS // ctx_size
    own_width = own_heads * HD
    fs_own = FS // ctx_size
    score_scale = HD ** (-0.5)

    def dot(a, b):
        return jnp.dot(a, b, preferred_element_type=f32)

    def dot_t(a, b):
        return lax.dot_general(a, b, (((1,), (1,)), ((), ())), preferred_element_type=f32)

    def t_dot(a, b):
        return lax.dot_general(a, b, (((0,), (0,)), ((), ())), preferred_element_type=f32)

    def own_rows(values):
        return lax.dynamic_index_in_dim(
            values.reshape((ctx_size, token_count) + values.shape[1:]), ctx_index, 0, keepdims=False
        )

    def sum_rows(grad):
        return lax.psum_scatter(grad.astype(bf16), "fsdp", scatter_dimension=0, tiled=True)

    shard = width // device_count
    small = [gain_attn, gain_ffn, w_shared_gate, w_router.reshape(-1), b_qkv]
    small_size = sum(piece.shape[0] for piece in small)
    small = jnp.concatenate(small + [routes.astype(bf16).reshape(-1)], axis=0)
    small_count = small.shape[0]
    pieces = column_pieces(w_qkv, 3, ctx_size, ctx_index, small)
    pieces, token_block, out_shard = after(pieces, tokens.reshape(token_count, width), w_out)
    token_rows = ring_gather(token_block, ctx_size, ctx_index)
    out_far = lax.ppermute(out_shard, "fsdp", other_chip(fsdp_size))
    pieces = fsdp_join(pieces, fsdp_size)
    pieces = pieces.transpose(1, 0, 2, 3)
    qkv_weight = pieces[:, :, :shard].reshape(width, 3 * own_width)
    small = pieces[:, :, shard:].reshape(device_count, -1)[:, :small_count]
    attn_gain = small[:, :shard].reshape(width).astype(f32)
    ffn_gain = small[:, shard : 2 * shard].reshape(width).astype(f32)
    gate_vector = small[:, 2 * shard : 3 * shard].reshape(width)
    router_end = 3 * shard + shard * expert_count
    router_weight = small[:, 3 * shard : router_end].reshape(width, expert_count)
    bias = small[:, router_end:small_size].reshape(3, ctx_size, own_width).astype(f32)
    bias = lax.dynamic_index_in_dim(bias, ctx_index, 1, keepdims=False).reshape(3 * own_width)
    route_rows = small[:, small_size:].astype(i32)
    route_rows = lax.dynamic_index_in_dim(
        route_rows.reshape(ctx_size, fsdp_size, -1), lax.axis_index("fsdp"), 1, keepdims=False
    ).reshape(ctx_size, token_count, top_count)

    expert_in = lax.all_gather(w_expert_in[0], "fsdp", axis=0, tiled=True)
    expert_out = lax.all_gather(w_expert_out[0], "fsdp", axis=0, tiled=True)
    chip = lax.axis_index("fsdp") // 2
    out_block = jnp.where(
        chip == 0,
        jnp.concatenate([out_shard, out_far], axis=0),
        jnp.concatenate([out_far, out_shard], axis=0),
    )
    out_block, in_shard, token_rows, qkv_weight = after(
        out_block, w_shared_in, token_rows, qkv_weight
    )
    out_rows = ring_gather(out_block, ctx_size, ctx_index)
    out_near = lax.ppermute(out_rows, "fsdp", other_core(fsdp_size))
    shared_in = column_pieces(in_shard, 2, ctx_size, ctx_index, None)
    shared_in = lax.all_gather(shared_in, "fsdp", axis=0, tiled=False)
    shared_out = lax.all_gather(w_shared_out, "fsdp", axis=0, tiled=True)

    block_ids = jnp.arange(ctx_size, dtype=i32)[:, None]
    local_index = jnp.arange(block_len, dtype=i32)[None, :]
    positions = jnp.stack(
        [
            block_ids * block_len + local_index,
            seq_len - (block_ids + 1) * block_len + local_index,
        ],
        axis=1,
    ).reshape(seq_len)
    seg_rows = (
        segments.reshape(2, ctx_size, block_len).transpose(1, 0, 2).reshape(seq_len)
    )
    cos_tab, sine_tab = rope_tables(positions, HD)

    inputs = token_rows.astype(f32)
    normed, inv_one_all = rms_norm(inputs, attn_gain)
    normed_low = normed.astype(bf16)
    projected = dot(normed_low, qkv_weight) + bias
    head_shape = (seq_len, own_heads, HD)
    queries = rotate(projected[:, :own_width].reshape(head_shape), cos_tab, sine_tab).astype(bf16)
    keys = rotate(
        projected[:, own_width : 2 * own_width].reshape(head_shape), cos_tab, sine_tab
    ).astype(bf16)
    values = projected[:, 2 * own_width :].reshape(head_shape).astype(bf16)
    allowed = (positions[None, :] <= positions[:, None]) & (seg_rows[None, :] == seg_rows[:, None])
    scores = jnp.einsum("qhd,khd->hqk", queries, keys, preferred_element_type=f32) * score_scale
    scores = jnp.where(allowed[None], scores, MASK_FILL)
    top_score = jnp.max(scores, axis=-1, keepdims=True)
    log_total = top_score + jnp.log(jnp.sum(jnp.exp(scores - top_score), axis=-1, keepdims=True))
    weights = jnp.exp(scores - log_total)
    weights_low = weights.astype(bf16)
    attended = jnp.einsum("hqk,khd->qhd", weights_low, values, preferred_element_type=f32)
    attn_own = attended.astype(bf16).reshape(seq_len, own_width)
    out_rows, out_near, attn_own = after(out_rows, out_near, attn_own)
    core = lax.axis_index("fsdp") % 2
    out_weight = jnp.zeros((ctx_size * fsdp_size // 2, 2, shard, width), bf16)
    for piece, place in ((out_rows, core), (out_near, 1 - core)):
        piece = piece.reshape(-1, shard, width)
        out_weight = lax.dynamic_update_index_in_dim(out_weight, piece, place, 1)
    out_weight = out_weight.reshape(width, width)
    attn_rows = ring_gather_columns(attn_own, ctx_size, ctx_index)
    grad_block, attn_rows = after(cotangent, attn_rows)
    grad_rows = ring_gather(grad_block.reshape(token_count, width), ctx_size, ctx_index)
    residual = inputs + dot(attn_rows, out_weight)

    normed_two, inv_two_all = rms_norm(residual, ffn_gain)
    low_two = normed_two.astype(bf16)
    mixed_weight = jnp.concatenate([router_weight, gate_vector[:, None]], axis=1)
    logits = dot(low_two, mixed_weight)
    probs_all = jax.nn.softmax(logits[:, :expert_count], axis=-1)
    scale_all = jax.nn.sigmoid(logits[:, expert_count])
    gate_all = lax.dynamic_index_in_dim(probs_all, ctx_index, 1, keepdims=False)

    named = jnp.any(route_rows == ctx_index, axis=-1)
    before = jnp.arange(token_count)[:, None] < jnp.arange(token_count)[None, :]
    rank = dot(named.astype(bf16), before.astype(bf16)).astype(i32)
    slot_of = jnp.where(named & (rank < capacity), rank, -1)
    slot_mask = slot_of[:, None, :] == jnp.arange(capacity, dtype=i32)[None, :, None]
    slot_map = slot_mask.astype(bf16)
    blocks_two = low_two.reshape(ctx_size, token_count, width)
    gate_blocks = gate_all.reshape(ctx_size, token_count)

    def to_slots(blocks):
        picked = jnp.einsum("bmt,btd->bmd", slot_map, blocks, preferred_element_type=f32)
        return picked.reshape(ctx_size * capacity, width)

    def to_tokens(slots):
        spread = jnp.einsum(
            "bmt,bmd->btd",
            slot_map,
            slots.reshape(ctx_size, capacity, width),
            preferred_element_type=f32,
        )
        return spread.reshape(seq_len, width)

    buffer = to_slots(blocks_two).astype(bf16)
    expert_pre = dot(buffer, expert_in)
    expert_hid = swiglu(expert_pre, FE).astype(bf16)
    expert_res = dot(expert_hid, expert_out).astype(bf16)
    routed = gate_all[:, None] * to_tokens(expert_res)

    shared_in, grad_rows, expert_res = after(shared_in, grad_rows, expert_res)
    shared_in = shared_in.transpose(1, 0, 2, 3).reshape(width, 2 * fs_own)
    shared_pre = dot(low_two, shared_in)
    shared_hid = swiglu(shared_pre, fs_own).astype(bf16)
    shared_res = dot(shared_hid, shared_out)
    out_parts = (scale_all[:, None] * shared_res + routed).astype(bf16)
    out_sum = ring_scatter(out_parts, ctx_size, ctx_index)

    grad_slots = to_slots(grad_rows.reshape(ctx_size, token_count, width))
    gate_slots = jnp.sum(jnp.where(slot_mask, gate_blocks[:, None, :], 0.0), axis=-1).reshape(-1, 1)
    grad_res = (gate_slots * grad_slots).astype(bf16)
    slot_dots = jnp.sum(grad_slots * expert_res.astype(f32), axis=-1).reshape(ctx_size, capacity, 1)
    grad_gates = jnp.sum(jnp.where(slot_mask, slot_dots, 0.0), axis=1)
    grad_expert_out = t_dot(expert_hid, grad_res)
    grad_hid = dot_t(grad_res, expert_out)
    grad_pre = swiglu_back(expert_pre, FE, grad_hid).astype(bf16)
    grad_expert_in = t_dot(buffer, grad_pre)
    grad_buffer = dot_t(grad_pre, expert_in).astype(bf16)

    grad_expert_in, grad_expert_out, grad_shared_res = after(
        grad_expert_in.astype(bf16),
        grad_expert_out.astype(bf16),
        (scale_all[:, None] * grad_rows.astype(f32)).astype(bf16),
    )
    sum_expert_out = fsdp_scatter(
        grad_expert_out.reshape(fsdp_size, -1, width), fsdp_size, 0
    )
    sum_expert_in = sum_rows(grad_expert_in)

    grad_f32 = grad_rows.astype(f32)
    gate_dots = jnp.sum(grad_f32 * shared_res, axis=-1).reshape(ctx_size, token_count)
    grad_shared_out = t_dot(shared_hid, grad_shared_res)
    grad_shared_hid = dot_t(grad_shared_res, shared_out)
    grad_shared_pre = swiglu_back(shared_pre, fs_own, grad_shared_hid).astype(bf16)
    grad_shared_in = t_dot(low_two, grad_shared_pre)
    grad_shared_pre, out_sum = after(grad_shared_pre, out_sum)
    two_parts = (dot_t(grad_shared_pre, shared_in) + to_tokens(grad_buffer)).astype(bf16)
    grad_two = ring_scatter(two_parts, ctx_size, ctx_index)
    sum_expert_in, grad_shared_in, grad_shared_out = after(
        sum_expert_in, grad_shared_in.astype(bf16), grad_shared_out.astype(bf16)
    )
    sum_shared_in = grad_shared_in.reshape(ctx_size, fsdp_size, shard, 2 * fs_own)
    sum_shared_in = lax.psum_scatter(
        sum_shared_in.transpose(1, 0, 2, 3).reshape(width, 2 * fs_own),
        "fsdp",
        scatter_dimension=0,
        tiled=True,
    ).reshape(ctx_size, shard, 2 * fs_own)
    sum_shared_out = sum_rows(grad_shared_out)
    own_residual = own_rows(residual)
    output = (own_residual + out_sum).astype(bf16).reshape(tokens.shape)

    dots = jnp.stack([grad_gates, gate_dots], axis=1)
    dots = lax.all_to_all(dots, "ctx", split_axis=0, concat_axis=0, tiled=True)
    own_probs = own_rows(probs_all)
    own_scale = own_rows(scale_all)
    own_low = own_rows(low_two)
    own_chosen = routes.reshape(token_count, top_count)
    chosen_mask = jnp.any(
        own_chosen[..., None] == jnp.arange(expert_count, dtype=i32), axis=1
    )
    grad_probs = jnp.where(chosen_mask, dots[:, 0].T, 0.0)
    grad_logits = (
        own_probs * (grad_probs - jnp.sum(own_probs * grad_probs, axis=-1, keepdims=True))
    ).astype(bf16)
    grad_gate_pre = (jnp.sum(dots[:, 1], axis=0) * own_scale * (1.0 - own_scale)).astype(bf16)
    grad_router = t_dot(own_low, grad_logits)
    grad_gate_vector = t_dot(own_low, grad_gate_pre[:, None])
    grad_two = grad_two + dot_t(grad_logits, router_weight)
    grad_two = grad_two + grad_gate_pre.astype(f32)[:, None] * gate_vector.astype(f32)[None, :]
    grad_resid_norm, grad_gain_two = rms_back(
        own_residual, own_rows(inv_two_all), ffn_gain, grad_two
    )
    grad_resid = cotangent.reshape(token_count, width).astype(f32) + grad_resid_norm

    grad_mixed = grad_resid.astype(bf16)
    grad_attn_rows = dot_t(grad_mixed, out_weight).astype(bf16)
    grad_attn = lax.all_to_all(
        grad_attn_rows.reshape(token_count, ctx_size, own_width).transpose(1, 0, 2),
        "ctx",
        split_axis=0,
        concat_axis=0,
        tiled=True,
    ).reshape(head_shape)
    grad_attn, sum_expert_out = after(grad_attn, sum_expert_out)
    mixed_all = ring_gather(grad_mixed, ctx_size, ctx_index)
    grad_weights = jnp.einsum("qhd,khd->hqk", grad_attn, values, preferred_element_type=f32)
    delta = jnp.sum(weights * grad_weights, axis=-1, keepdims=True)
    grad_scores = jnp.where(allowed[None], weights * (grad_weights - delta), 0.0).astype(bf16)
    grad_q = jnp.einsum("hqk,khd->qhd", grad_scores, keys, preferred_element_type=f32) * score_scale
    grad_k = (
        jnp.einsum("hqk,qhd->khd", grad_scores, queries, preferred_element_type=f32) * score_scale
    )
    grad_v = jnp.einsum("hqk,qhd->khd", weights_low, grad_attn, preferred_element_type=f32)
    grad_projected = jnp.concatenate(
        [
            rotate_back(grad_q, cos_tab, sine_tab).reshape(seq_len, own_width),
            rotate_back(grad_k, cos_tab, sine_tab).reshape(seq_len, own_width),
            grad_v.reshape(seq_len, own_width),
        ],
        axis=-1,
    ).astype(bf16)
    grad_projected, mixed_all = after(grad_projected, mixed_all)
    one_sums = dot_t(grad_projected, qkv_weight)
    grad_gain_one = jnp.sum(one_sums * inputs * inv_one_all, axis=0)
    one_parts = one_sums.astype(bf16)
    one_kept, grad_projected = after(one_parts, grad_projected)
    one_kept, sum_shared_in, sum_shared_out, sum_expert_in = after(
        one_kept, sum_shared_in, sum_shared_out, sum_expert_in
    )
    grad_normed = ring_scatter(one_parts, ctx_size, ctx_index, one_kept)
    grad_inputs_norm, unused = rms_back(
        tokens.reshape(token_count, width).astype(f32),
        own_rows(inv_one_all),
        attn_gain,
        grad_normed,
    )
    grad_tokens = (grad_resid + grad_inputs_norm).reshape(tokens.shape)
    grad_qkv_weight = t_dot(normed_low, grad_projected)
    grad_bias = jnp.sum(grad_projected.astype(f32), axis=0).reshape(3, 1, own_width)
    grad_bias = jnp.where(
        jnp.arange(ctx_size, dtype=i32)[None, :, None] == ctx_index, grad_bias, 0.0
    )

    grad_out_weight = t_dot(attn_own, mixed_all)
    sum_qkv_weight = fsdp_scatter(
        grad_qkv_weight.astype(bf16).reshape(ctx_size, fsdp_size, shard, 3 * own_width),
        fsdp_size,
        1,
    ).astype(bf16)
    small_grads = jnp.concatenate(
        [
            piece.reshape(device_count, -1)
            for piece in (grad_gain_one, grad_gain_two, grad_gate_vector, grad_router, grad_bias)
        ],
        axis=1,
    )
    small_grads = small_grads.reshape(ctx_size, fsdp_size, small_size)
    small_grads = small_scatter(small_grads, ctx_size, fsdp_size, ctx_index).reshape(small_size)
    return (
        output,
        grad_tokens,
        merge_columns(sum_qkv_weight, 3, ctx_size),
        small_grads[router_end:],
        sum_rows(grad_out_weight).astype(f32),
        small_grads[:shard],
        small_grads[shard : 2 * shard],
        small_grads[3 * shard : router_end].reshape(shard, expert_count),
        small_grads[2 * shard : 3 * shard],
        merge_columns(sum_shared_in, 2, ctx_size),
        sum_shared_out.astype(f32),
        sum_expert_in.astype(f32)[None],
        sum_expert_out[None],
    )


def local_wide(
    tokens,
    segments,
    routes,
    cotangent,
    w_qkv,
    b_qkv,
    w_out,
    gain_attn,
    gain_ffn,
    w_router,
    w_shared_gate,
    w_shared_in,
    w_shared_out,
    w_expert_in,
    w_expert_out,
):
    block_len = tokens.shape[2]
    model_width = tokens.shape[3]
    token_count = 2 * block_len
    top_count = routes.shape[3]
    half_len = segments.shape[2]
    seq_len = 2 * half_len
    ctx_index = lax.axis_index("ctx")
    head_count = model_width // HD
    expert_count = w_router.shape[1]
    capacity = token_count * top_count // expert_count
    slot_count = expert_count * capacity
    key_rows = min(512, seq_len)
    key_blocks = seq_len // key_rows
    score_scale = HD ** (-0.5)
    head_shape = (token_count, head_count, HD)
    attn_set = (
        lax.all_gather(w_qkv, ("ctx", "fsdp"), axis=0, tiled=True),
        lax.all_gather(b_qkv, ("ctx", "fsdp"), axis=0, tiled=True),
        lax.all_gather(w_out, ("ctx", "fsdp"), axis=0, tiled=True),
        lax.all_gather(gain_attn, ("ctx", "fsdp"), axis=0, tiled=True),
    )
    qkv_weight, qkv_bias, out_weight, attn_gain = attn_set
    inputs = tokens.reshape(token_count, model_width).astype(jnp.float32)
    normed, inv_one = rms_norm(inputs, attn_gain.astype(jnp.float32))
    normed_low = normed.astype(jnp.bfloat16)
    projected = jnp.dot(
        normed_low, qkv_weight, preferred_element_type=jnp.float32
    ) + qkv_bias.astype(jnp.float32)
    local_index = jnp.arange(block_len, dtype=jnp.int32)
    query_pos = jnp.concatenate(
        [ctx_index * block_len + local_index, seq_len - (ctx_index + 1) * block_len + local_index]
    )
    half_index = jnp.arange(half_len, dtype=jnp.int32)
    key_pos = jnp.concatenate(
        [half_index, seq_len - block_len * (half_index // block_len + 1) + half_index % block_len]
    ).reshape(key_blocks, key_rows)
    key_seg = segments.reshape(key_blocks, key_rows)
    query_seg = lax.dynamic_slice_in_dim(segments[0], ctx_index * block_len, block_len, 1).reshape(
        token_count
    )
    cos_tab, sine_tab = rope_tables(query_pos, HD)
    queries = rotate(projected[:, :model_width].reshape(head_shape), cos_tab, sine_tab).astype(
        jnp.bfloat16
    )
    keys_own = rotate(
        projected[:, model_width : 2 * model_width].reshape(head_shape), cos_tab, sine_tab
    ).astype(jnp.bfloat16)
    values_own = projected[:, 2 * model_width :].astype(jnp.bfloat16)
    keys_all, values_all = (
        lax.all_gather(keys_own.reshape(2, block_len, model_width), "ctx", axis=1, tiled=True),
        lax.all_gather(values_own.reshape(2, block_len, model_width), "ctx", axis=1, tiled=True),
    )
    keys_all = keys_all.reshape(key_blocks, key_rows, head_count, HD)
    values_all = values_all.reshape(key_blocks, key_rows, head_count, HD)

    def score_block(key_blk, pos_blk, seg_blk):
        raw_scores = (
            jnp.einsum("qhd,khd->hqk", queries, key_blk, preferred_element_type=jnp.float32)
            * score_scale
        )
        allowed = (pos_blk[None, :] <= query_pos[:, None]) & (
            seg_blk[None, :] == query_seg[:, None]
        )
        return (jnp.where(allowed[None], raw_scores, MASK_FILL), allowed)

    def total_step(running, key_part):
        run_max, run_sum = running
        scores = score_block(key_part[0], key_part[1], key_part[2])[0]
        new_max = jnp.maximum(run_max, jnp.max(scores, axis=-1))
        run_sum = run_sum * jnp.exp(run_max - new_max) + jnp.sum(
            jnp.exp(scores - new_max[..., None]), axis=-1
        )
        return ((new_max, run_sum), None)

    start_max = jnp.full((head_count, token_count), MASK_FILL, jnp.float32)
    start_sum = jnp.zeros((head_count, token_count), jnp.float32)
    (run_max, run_sum), unused = lax.scan(
        total_step, (start_max, start_sum), (keys_all, key_pos, key_seg)
    )
    log_total = run_max + jnp.log(run_sum)

    def attend_step(summed, key_part):
        key_blk, value_blk, pos_blk, seg_blk = key_part
        scores = score_block(key_blk, pos_blk, seg_blk)[0]
        weights = jnp.exp(scores - log_total[..., None]).astype(jnp.bfloat16)
        return (
            summed
            + jnp.einsum("hqk,khd->qhd", weights, value_blk, preferred_element_type=jnp.float32),
            None,
        )

    key_stack = (keys_all, values_all, key_pos, key_seg)
    attended, unused = lax.scan(attend_step, jnp.zeros(head_shape, jnp.float32), key_stack)
    attn_low = attended.reshape(token_count, model_width).astype(jnp.bfloat16)
    residual = inputs + jnp.dot(attn_low, out_weight, preferred_element_type=jnp.float32)
    ffn_set = (
        lax.all_gather(gain_ffn, ("ctx", "fsdp"), axis=0, tiled=True),
        lax.all_gather(w_router, ("ctx", "fsdp"), axis=0, tiled=True),
        lax.all_gather(w_shared_gate, ("ctx", "fsdp"), axis=0, tiled=True),
        lax.all_gather(w_shared_in, ("ctx", "fsdp"), axis=0, tiled=True),
        lax.all_gather(w_shared_out, ("ctx", "fsdp"), axis=0, tiled=True),
    )
    ffn_gain, router_weight, gate_vector, shared_in, shared_out = ffn_set
    normed_two, inv_two = rms_norm(residual, ffn_gain.astype(jnp.float32))
    low_two = normed_two.astype(jnp.bfloat16)
    logits = jnp.dot(low_two, router_weight, preferred_element_type=jnp.float32)
    router_probs = jax.nn.softmax(logits, axis=-1)
    chosen = routes.reshape(token_count, top_count)
    chosen_mask = chosen[..., None] == jnp.arange(expert_count, dtype=jnp.int32)
    gate_vals = jnp.sum(jnp.where(chosen_mask, router_probs[:, None, :], 0.0), axis=-1)
    shared_scale = jax.nn.sigmoid(jnp.dot(low_two, gate_vector, preferred_element_type=jnp.float32))
    shared_pre = jnp.dot(low_two, shared_in, preferred_element_type=jnp.float32)
    shared_hid = swiglu(shared_pre, FS).astype(jnp.bfloat16)
    shared_res = jnp.dot(shared_hid, shared_out, preferred_element_type=jnp.float32)
    pair_routes = chosen.reshape(token_count * top_count)
    expert_marks = (
        pair_routes[:, None] == jnp.arange(expert_count, dtype=jnp.int32)[None, :]
    ).astype(jnp.int32)
    pair_ranks = jnp.sum((jnp.cumsum(expert_marks, axis=0) - expert_marks) * expert_marks, axis=1)
    pair_target = jnp.where(pair_ranks < capacity, pair_routes * capacity + pair_ranks, -1)
    pair_map = pair_target[:, None] == jnp.arange(slot_count, dtype=jnp.int32)[None, :]
    pair_low = pair_map.astype(jnp.bfloat16)
    token_map = jnp.sum(
        pair_map.reshape(token_count, top_count, slot_count).astype(jnp.int32), axis=1
    ).astype(jnp.bfloat16)
    outgoing = jnp.einsum(
        "tc,td->cd", token_map, low_two, preferred_element_type=jnp.float32
    ).astype(jnp.bfloat16)
    incoming = lax.all_to_all(
        outgoing.reshape(expert_count, capacity, model_width),
        "ctx",
        split_axis=0,
        concat_axis=1,
        tiled=True,
    )
    expert_in, expert_out = (
        lax.all_gather(w_expert_in, "fsdp", axis=1, tiled=True),
        lax.all_gather(w_expert_out, "fsdp", axis=1, tiled=True),
    )
    expert_pre = jnp.einsum("erd,edf->erf", incoming, expert_in, preferred_element_type=jnp.float32)
    expert_hid = swiglu(expert_pre, FE).astype(jnp.bfloat16)
    expert_res = jnp.einsum(
        "erf,efd->erd", expert_hid, expert_out, preferred_element_type=jnp.float32
    ).astype(jnp.bfloat16)
    returned = lax.all_to_all(expert_res, "ctx", split_axis=1, concat_axis=0, tiled=True).reshape(
        slot_count, model_width
    )
    pair_vals = jnp.dot(pair_low, returned, preferred_element_type=jnp.float32).reshape(
        token_count, top_count, model_width
    )
    routed = jnp.sum(gate_vals[..., None] * pair_vals, axis=1)
    output = (
        (residual + shared_scale[:, None] * shared_res + routed)
        .astype(jnp.bfloat16)
        .reshape(tokens.shape)
    )
    grad_out = cotangent.reshape(token_count, model_width).astype(jnp.float32)
    pair_grads = gate_vals[..., None] * grad_out[:, None, :]
    grad_gates = jnp.sum(grad_out[:, None, :] * pair_vals, axis=-1)
    grad_returned = jnp.einsum(
        "pc,pd->cd",
        pair_map.astype(jnp.float32),
        pair_grads.reshape(token_count * top_count, model_width),
        precision=HIGHEST,
    ).astype(jnp.bfloat16)
    grad_res = lax.all_to_all(
        grad_returned.reshape(expert_count, capacity, model_width),
        "ctx",
        split_axis=0,
        concat_axis=1,
        tiled=True,
    )
    grad_expert_out = jnp.einsum(
        "erf,erd->efd", expert_hid, grad_res, preferred_element_type=jnp.float32
    )
    grad_hid = jnp.einsum("erd,efd->erf", grad_res, expert_out, preferred_element_type=jnp.float32)
    grad_pre = swiglu_back(expert_pre, FE, grad_hid).astype(jnp.bfloat16)
    grad_expert_in = jnp.einsum(
        "erd,erf->edf", incoming, grad_pre, preferred_element_type=jnp.float32
    )
    grad_incoming = jnp.einsum(
        "erf,edf->erd", grad_pre, expert_in, preferred_element_type=jnp.float32
    ).astype(jnp.bfloat16)
    grad_outgoing = lax.all_to_all(
        grad_incoming, "ctx", split_axis=1, concat_axis=0, tiled=True
    ).reshape(slot_count, model_width)
    expert_grads = (
        lax.psum_scatter(
            grad_expert_in.astype(jnp.bfloat16), "fsdp", scatter_dimension=1, tiled=True
        ).astype(jnp.float32),
        lax.psum_scatter(
            grad_expert_out.astype(jnp.bfloat16), "fsdp", scatter_dimension=1, tiled=True
        ).astype(jnp.float32),
    )
    grad_two = jnp.einsum("tc,cd->td", token_map, grad_outgoing, preferred_element_type=jnp.float32)
    grad_probs = jnp.sum(jnp.where(chosen_mask, grad_gates[..., None], 0.0), axis=1)
    grad_logits = (
        router_probs * (grad_probs - jnp.sum(router_probs * grad_probs, axis=-1, keepdims=True))
    ).astype(jnp.bfloat16)
    grad_router = jnp.einsum("td,te->de", low_two, grad_logits, preferred_element_type=jnp.float32)
    grad_shared_res = (shared_scale[:, None] * grad_out).astype(jnp.bfloat16)
    grad_gate_pre = (
        jnp.sum(grad_out * shared_res, axis=-1) * shared_scale * (1.0 - shared_scale)
    ).astype(jnp.bfloat16)
    grad_shared_out = jnp.einsum(
        "tf,td->fd", shared_hid, grad_shared_res, preferred_element_type=jnp.float32
    )
    grad_shared_hid = jnp.einsum(
        "td,fd->tf", grad_shared_res, shared_out, preferred_element_type=jnp.float32
    )
    grad_shared_pre = swiglu_back(shared_pre, FS, grad_shared_hid).astype(jnp.bfloat16)
    grad_shared_in = jnp.einsum(
        "td,tf->df", low_two, grad_shared_pre, preferred_element_type=jnp.float32
    )
    grad_gate_vector = jnp.einsum(
        "td,t->d", low_two, grad_gate_pre, preferred_element_type=jnp.float32
    )
    grad_two = grad_two + jnp.einsum(
        "te,de->td", grad_logits, router_weight, preferred_element_type=jnp.float32
    )
    grad_two = grad_two + jnp.einsum(
        "tf,df->td", grad_shared_pre, shared_in, preferred_element_type=jnp.float32
    )
    grad_two = (
        grad_two
        + grad_gate_pre.astype(jnp.float32)[:, None] * gate_vector.astype(jnp.float32)[None, :]
    )
    grad_resid_norm, grad_gain_two = rms_back(
        residual, inv_two, ffn_gain.astype(jnp.float32), grad_two
    )
    grad_resid = grad_out + grad_resid_norm
    ffn_grads = (
        lax.psum_scatter(grad_gain_two, ("ctx", "fsdp"), scatter_dimension=0, tiled=True),
        lax.psum_scatter(grad_router, ("ctx", "fsdp"), scatter_dimension=0, tiled=True),
        lax.psum_scatter(grad_gate_vector, ("ctx", "fsdp"), scatter_dimension=0, tiled=True),
        lax.psum_scatter(grad_shared_in, ("ctx", "fsdp"), scatter_dimension=0, tiled=True),
        lax.psum_scatter(grad_shared_out, ("ctx", "fsdp"), scatter_dimension=0, tiled=True),
    )
    grad_mixed = grad_resid.astype(jnp.bfloat16)
    grad_out_weight = jnp.einsum(
        "tc,td->cd", attn_low, grad_mixed, preferred_element_type=jnp.float32
    )
    grad_attn = (
        jnp.einsum("td,cd->tc", grad_mixed, out_weight, preferred_element_type=jnp.float32)
        .astype(jnp.bfloat16)
        .reshape(head_shape)
    )

    def delta_step(summed, key_part):
        key_blk, value_blk, pos_blk, seg_blk = key_part
        weights = jnp.exp(score_block(key_blk, pos_blk, seg_blk)[0] - log_total[..., None])
        grad_weights = jnp.einsum(
            "qhd,khd->hqk", grad_attn, value_blk, preferred_element_type=jnp.float32
        )
        return (summed + jnp.sum(weights * grad_weights, axis=-1), None)

    delta_sum, unused = lax.scan(
        delta_step, jnp.zeros((head_count, token_count), jnp.float32), key_stack
    )

    def grad_step(summed, key_part):
        key_blk, value_blk, pos_blk, seg_blk = key_part
        scores, allowed = score_block(key_blk, pos_blk, seg_blk)
        weights = jnp.exp(scores - log_total[..., None])
        grad_weights = jnp.einsum(
            "qhd,khd->hqk", grad_attn, value_blk, preferred_element_type=jnp.float32
        )
        grad_scores = jnp.where(
            allowed[None], weights * (grad_weights - delta_sum[..., None]), 0.0
        ).astype(jnp.bfloat16)
        summed = (
            summed
            + jnp.einsum("hqk,khd->qhd", grad_scores, key_blk, preferred_element_type=jnp.float32)
            * score_scale
        )
        grad_key = (
            jnp.einsum("hqk,qhd->khd", grad_scores, queries, preferred_element_type=jnp.float32)
            * score_scale
        )
        grad_value = jnp.einsum(
            "hqk,qhd->khd",
            weights.astype(jnp.bfloat16),
            grad_attn,
            preferred_element_type=jnp.float32,
        )
        return (summed, (grad_key, grad_value))

    grad_query, (grad_keys, grad_values) = lax.scan(
        grad_step, jnp.zeros(head_shape, jnp.float32), key_stack
    )
    grad_keys_own, grad_values_own = (
        lax.psum_scatter(
            grad_keys.reshape(2, half_len, model_width).astype(jnp.bfloat16),
            "ctx",
            scatter_dimension=1,
            tiled=True,
        ).astype(jnp.float32),
        lax.psum_scatter(
            grad_values.reshape(2, half_len, model_width).astype(jnp.bfloat16),
            "ctx",
            scatter_dimension=1,
            tiled=True,
        ).astype(jnp.float32),
    )
    grad_q_rows = rotate_back(grad_query, cos_tab, sine_tab).reshape(token_count, model_width)
    grad_k_rows = rotate_back(grad_keys_own.reshape(head_shape), cos_tab, sine_tab).reshape(
        token_count, model_width
    )
    grad_projected = jnp.concatenate(
        [grad_q_rows, grad_k_rows, grad_values_own.reshape(token_count, model_width)], axis=-1
    ).astype(jnp.bfloat16)
    grad_qkv_weight = jnp.einsum(
        "td,te->de", normed_low, grad_projected, preferred_element_type=jnp.float32
    )
    grad_qkv_bias = jnp.sum(grad_projected.astype(jnp.float32), axis=0)
    grad_normed = jnp.einsum(
        "te,de->td", grad_projected, qkv_weight, preferred_element_type=jnp.float32
    )
    grad_inputs_norm, grad_gain_one = rms_back(
        inputs, inv_one, attn_gain.astype(jnp.float32), grad_normed
    )
    grad_tokens = (grad_resid + grad_inputs_norm).reshape(tokens.shape)
    attn_grads = (
        lax.psum_scatter(grad_qkv_weight, ("ctx", "fsdp"), scatter_dimension=0, tiled=True),
        lax.psum_scatter(grad_qkv_bias, ("ctx", "fsdp"), scatter_dimension=0, tiled=True),
        lax.psum_scatter(grad_out_weight, ("ctx", "fsdp"), scatter_dimension=0, tiled=True),
        lax.psum_scatter(grad_gain_one, ("ctx", "fsdp"), scatter_dimension=0, tiled=True),
    )
    return (
        output,
        grad_tokens,
        attn_grads[0],
        attn_grads[1],
        attn_grads[2],
        attn_grads[3],
        ffn_grads[0],
        ffn_grads[1],
        ffn_grads[2],
        ffn_grads[3],
        ffn_grads[4],
        expert_grads[0],
        expert_grads[1],
    )


def solution(mesh):
    in_specs = (
        P("fsdp", None, "ctx", None),
        P("fsdp", None, None),
        P("fsdp", None, "ctx", None),
        P("fsdp", None, "ctx", None),
        P(("ctx", "fsdp"), None),
        P(("ctx", "fsdp")),
        P(("ctx", "fsdp"), None),
        P(("ctx", "fsdp")),
        P(("ctx", "fsdp")),
        P(("ctx", "fsdp"), None),
        P(("ctx", "fsdp")),
        P(("ctx", "fsdp"), None),
        P(("ctx", "fsdp"), None),
        P("ctx", "fsdp", None),
        P("ctx", "fsdp", None),
    )
    out_specs = (
        P("fsdp", None, "ctx", None),
        P("fsdp", None, "ctx", None),
        P(("ctx", "fsdp"), None),
        P(("ctx", "fsdp")),
        P(("ctx", "fsdp"), None),
        P(("ctx", "fsdp")),
        P(("ctx", "fsdp")),
        P(("ctx", "fsdp"), None),
        P(("ctx", "fsdp")),
        P(("ctx", "fsdp"), None),
        P(("ctx", "fsdp"), None),
        P("ctx", "fsdp", None),
        P("ctx", "fsdp", None),
    )
    ctx_size = mesh.shape["ctx"]
    fsdp_size = mesh.shape["fsdp"]

    def local(*arrays):
        if HEADS % ctx_size:
            return local_wide(*arrays)
        return local_split(ctx_size, fsdp_size, *arrays)

    return jax.shard_map(local, mesh=mesh, in_specs=in_specs, out_specs=out_specs, check_vma=False)
```

```python
import jax
import jax.numpy as jnp
from jax import lax
from jax.sharding import PartitionSpec as P

HD = 128
HEADS = 16
FS = 5632
FE = 1408


RMS_EPS = 1e-06
ROPE_THETA = 1000000.0
MASK_FILL = -1e30
HIGHEST = lax.Precision.HIGHEST


def rope_tables(positions, head_dim):
    half_dim = head_dim // 2
    inv_freq = ROPE_THETA ** (-(jnp.arange(half_dim, dtype=jnp.float32) * 2.0 / head_dim))
    angles = positions.astype(jnp.float32)[:, None] * inv_freq[None, :]
    cos_tab = jnp.concatenate([jnp.cos(angles), jnp.cos(angles)], axis=-1)
    sine_tab = jnp.concatenate([jnp.sin(angles), jnp.sin(angles)], axis=-1)
    return (cos_tab, sine_tab)


def rotate(values, cos_tab, sine_tab):
    half_dim = values.shape[-1] // 2
    turned = jnp.concatenate([-values[..., half_dim:], values[..., :half_dim]], axis=-1)
    return values * cos_tab[:, None, :] + turned * sine_tab[:, None, :]


def rotate_back(upstream, cos_tab, sine_tab):
    half_dim = upstream.shape[-1] // 2
    scaled = upstream * sine_tab[:, None, :]
    return upstream * cos_tab[:, None, :] + jnp.concatenate(
        [scaled[..., half_dim:], -scaled[..., :half_dim]], axis=-1
    )


def rms_norm(values, gain_vec):
    inv_rms = lax.rsqrt(jnp.mean(values * values, axis=-1, keepdims=True) + RMS_EPS)
    return (values * inv_rms * gain_vec, inv_rms)


def rms_back(values, inv_rms, gain_vec, upstream):
    weighted = upstream * gain_vec
    inner_mean = jnp.mean(weighted * values, axis=-1, keepdims=True)
    return (
        inv_rms * weighted - values * inv_rms * inv_rms * inv_rms * inner_mean,
        jnp.sum(upstream * values * inv_rms, axis=0),
    )


def swiglu(pre_act, split_at):
    return jax.nn.silu(pre_act[..., :split_at]) * pre_act[..., split_at:]


def swiglu_back(pre_act, split_at, upstream):
    gate_part = pre_act[..., :split_at]
    up_part = pre_act[..., split_at:]
    sigmoid_g = jax.nn.sigmoid(gate_part)
    d_gate = upstream * up_part * sigmoid_g * (1.0 + gate_part * (1.0 - sigmoid_g))
    d_up = upstream * gate_part * sigmoid_g
    return jnp.concatenate([d_gate, d_up], axis=-1)


def ring_order(size):
    return list(range(0, size, 2)) + list(range(size - 1, 0, -2))


def ring_steps(size):
    order = ring_order(size)
    ahead = [(order[i], order[(i + 1) % size]) for i in range(size)]
    back = [(dst, src) for src, dst in ahead]
    return (ahead, back)


def ring_peers(size, ctx_index):
    order = ring_order(size)
    place = {dev: i for i, dev in enumerate(order)}
    table = jnp.array(
        [[order[(place[dev] + k) % size] for k in range(size)] for dev in range(size)], jnp.int32
    )
    row = lax.dynamic_index_in_dim(table, ctx_index, 0, keepdims=False)
    return [row[k] for k in range(size)]


def ring_walk(block, size, ctx_index, out, put):
    rows = block.shape[0]
    ahead, back = ring_steps(size)
    peers = ring_peers(size, ctx_index)
    half = size // 2
    out = put(out, block, ctx_index, 0)
    fore = rear = block
    for k in range(1, half):
        fore = lax.ppermute(fore, "ctx", ahead)
        rear = lax.ppermute(rear, "ctx", back)
        out = put(out, fore, peers[size - k], 0)
        out = put(out, rear, peers[k], 0)
    fore = lax.ppermute(fore[: rows // 2], "ctx", ahead)
    rear = lax.ppermute(rear[rows // 2 :], "ctx", back)
    out = put(out, fore, peers[half], 0)
    return put(out, rear, peers[half], rows // 2)


def ring_gather(block, size, ctx_index):
    rows, width = block.shape

    def put(out, piece, peer, offset):
        return lax.dynamic_update_slice(out, piece, (peer * rows + offset, jnp.zeros_like(peer)))

    return ring_walk(block, size, ctx_index, jnp.zeros((size * rows, width), block.dtype), put)


def ring_sums(parts, size, ctx_index):
    f32 = jnp.float32
    rows = parts.shape[0] // size
    ahead, back = ring_steps(size)
    peers = ring_peers(size, ctx_index)
    half = size // 2

    def own(k, start, count):
        first = (peers[k % size] * rows + start, jnp.zeros_like(peers[0]))
        return lax.dynamic_slice(parts, first, (count, parts.shape[1])).astype(f32)

    def low(values):
        return values.astype(jnp.bfloat16)

    cut = rows // 2
    fore = lax.ppermute(low(own(half, 0, cut)), "ctx", ahead)
    rear = lax.ppermute(low(own(half, cut, cut)), "ctx", back)
    fore = jnp.concatenate(
        [low(fore.astype(f32) + own(half - 1, 0, cut)), low(own(half - 1, cut, cut))], axis=0
    )
    rear = jnp.concatenate(
        [low(own(1 - half, 0, cut)), low(rear.astype(f32) + own(1 - half, cut, cut))], axis=0
    )
    for k in range(half - 1, 0, -1):
        fore = lax.ppermute(fore, "ctx", ahead)
        rear = lax.ppermute(rear, "ctx", back)
        if k > 1:
            fore = low(fore.astype(f32) + own(k - 1, 0, rows))
            rear = low(rear.astype(f32) + own(1 - k, 0, rows))
    return (fore, rear)


def ring_scatter(parts, size, ctx_index, kept=None):
    fore, rear = ring_sums(parts, size, ctx_index)
    kept = (parts if kept is None else kept).reshape(size, -1, parts.shape[1])
    kept = lax.dynamic_index_in_dim(kept, ctx_index, 0, keepdims=False)
    return kept.astype(jnp.float32) + fore.astype(jnp.float32) + rear.astype(jnp.float32)


def other_core(size):
    return [(i, i ^ 1) for i in range(size)]


def other_chip(size):
    return [(i, i ^ 2) for i in range(size)]


def after(value, *deps):
    return lax.optimization_barrier((value,) + deps)


def fsdp_scatter(grad, size, axis):
    index = lax.axis_index("fsdp")

    def pick(peer):
        return lax.dynamic_index_in_dim(grad, peer, axis, keepdims=False)

    far_near = lax.ppermute(pick(index ^ 3), "fsdp", other_core(size))
    near = lax.ppermute(pick(index ^ 1), "fsdp", other_core(size))
    far = (pick(index ^ 2).astype(jnp.float32) + far_near.astype(jnp.float32)).astype(jnp.bfloat16)
    far = lax.ppermute(far, "fsdp", other_chip(size))
    return pick(index).astype(jnp.float32) + near.astype(jnp.float32) + far.astype(jnp.float32)


def column_pieces(weight, groups, size, extra):
    rows = weight.shape[0]
    width = weight.shape[1] // (groups * size)
    pieces = weight.reshape(rows, groups, size, width).transpose(2, 0, 1, 3)
    pieces = pieces.reshape(size, rows, groups * width)
    if extra is not None:
        count = extra.shape[0]
        more = -(-count // (groups * width * 16)) * 16
        extra = jnp.pad(extra, (0, more * groups * width - count))
        extra = jnp.broadcast_to(
            extra.reshape(1, more, groups * width), (size, more, groups * width)
        )
        pieces = jnp.concatenate([pieces, extra], axis=1)
    return lax.all_to_all(pieces, "ctx", split_axis=0, concat_axis=0, tiled=True)


def merge_columns(pieces, groups, size):
    width = pieces.shape[2] // groups
    pieces = lax.all_to_all(pieces, "ctx", split_axis=0, concat_axis=0, tiled=True)
    columns = [
        pieces[peer, :, group * width : (group + 1) * width]
        for group in range(groups)
        for peer in range(size)
    ]
    return jnp.concatenate(columns, axis=1).astype(jnp.float32)


def local_split(
    ctx_size,
    fsdp_size,
    tokens,
    segments,
    routes,
    cotangent,
    w_qkv,
    b_qkv,
    w_out,
    gain_attn,
    gain_ffn,
    w_router,
    w_shared_gate,
    w_shared_in,
    w_shared_out,
    w_expert_in,
    w_expert_out,
):
    bf16, f32, i32 = jnp.bfloat16, jnp.float32, jnp.int32
    device_count = ctx_size * fsdp_size
    block_len = tokens.shape[2]
    width = tokens.shape[3]
    token_count = 2 * block_len
    top_count = routes.shape[3]
    seq_len = token_count * ctx_size
    ctx_index = lax.axis_index("ctx")
    expert_count = w_router.shape[1]
    capacity = token_count * top_count // expert_count
    own_heads = HEADS // ctx_size
    own_width = own_heads * HD
    fs_own = FS // ctx_size
    score_scale = HD ** (-0.5)

    def dot(a, b):
        return jnp.dot(a, b, preferred_element_type=f32)

    def dot_t(a, b):
        return lax.dot_general(a, b, (((1,), (1,)), ((), ())), preferred_element_type=f32)

    def t_dot(a, b):
        return lax.dot_general(a, b, (((0,), (0,)), ((), ())), preferred_element_type=f32)

    def own_rows(values):
        return lax.dynamic_index_in_dim(
            values.reshape((ctx_size, token_count) + values.shape[1:]), ctx_index, 0, keepdims=False
        )

    def sum_rows(grad):
        return lax.psum_scatter(grad.astype(bf16), "fsdp", scatter_dimension=0, tiled=True)

    shard = width // device_count
    small = [gain_attn, gain_ffn, w_shared_gate, w_router.reshape(-1), b_qkv]
    small_size = sum(piece.shape[0] for piece in small)
    small = jnp.concatenate(small + [routes.astype(bf16).reshape(-1)], axis=0)
    small_count = small.shape[0]
    token_rows = ring_gather(tokens.reshape(token_count, width), ctx_size, ctx_index)
    pieces = column_pieces(w_qkv, 3, ctx_size, small)
    pieces = lax.all_gather(pieces, "fsdp", axis=0, tiled=False).transpose(1, 0, 2, 3)
    qkv_weight = pieces[:, :, :shard].reshape(width, 3 * own_width)
    small = pieces[:, :, shard:].reshape(device_count, -1)[:, :small_count]
    attn_gain = small[:, :shard].reshape(width).astype(f32)
    ffn_gain = small[:, shard : 2 * shard].reshape(width).astype(f32)
    gate_vector = small[:, 2 * shard : 3 * shard].reshape(width)
    router_end = 3 * shard + shard * expert_count
    router_weight = small[:, 3 * shard : router_end].reshape(width, expert_count)
    bias = small[:, router_end:small_size].reshape(3, ctx_size, own_width).astype(f32)
    bias = lax.dynamic_index_in_dim(bias, ctx_index, 1, keepdims=False).reshape(3 * own_width)
    route_rows = small[:, small_size:].astype(i32)
    route_rows = lax.dynamic_index_in_dim(
        route_rows.reshape(ctx_size, fsdp_size, -1), lax.axis_index("fsdp"), 1, keepdims=False
    ).reshape(ctx_size, token_count, top_count)

    expert_out = lax.all_gather(w_expert_out[0], "fsdp", axis=0, tiled=True)
    expert_in, token_rows = after(w_expert_in[0], token_rows)
    expert_in = lax.all_gather(expert_in, "fsdp", axis=0, tiled=True)
    out_weight = lax.all_gather(w_out, "fsdp", axis=0, tiled=True)

    block_ids = jnp.arange(ctx_size, dtype=i32)[:, None]
    local_index = jnp.arange(block_len, dtype=i32)[None, :]
    positions = jnp.stack(
        [
            block_ids * block_len + local_index,
            seq_len - (block_ids + 1) * block_len + local_index,
        ],
        axis=1,
    ).reshape(seq_len)
    seg_rows = (
        segments.reshape(2, ctx_size, block_len).transpose(1, 0, 2).reshape(seq_len)
    )
    cos_tab, sine_tab = rope_tables(positions, HD)

    inputs = token_rows.astype(f32)
    normed, inv_one_all = rms_norm(inputs, attn_gain)
    normed_low = normed.astype(bf16)
    projected = dot(normed_low, qkv_weight) + bias
    head_shape = (seq_len, own_heads, HD)
    queries = rotate(projected[:, :own_width].reshape(head_shape), cos_tab, sine_tab).astype(bf16)
    keys = rotate(
        projected[:, own_width : 2 * own_width].reshape(head_shape), cos_tab, sine_tab
    ).astype(bf16)
    values = projected[:, 2 * own_width :].reshape(head_shape).astype(bf16)
    queries, in_shard, out_shard = after(queries, w_shared_in, w_shared_out)
    shared_in = column_pieces(in_shard, 2, ctx_size, None)
    shared_in = lax.all_gather(shared_in, "fsdp", axis=0, tiled=False)
    shared_out = lax.all_gather(out_shard, "fsdp", axis=0, tiled=True)
    allowed = (positions[None, :] <= positions[:, None]) & (seg_rows[None, :] == seg_rows[:, None])
    scores = jnp.einsum("qhd,khd->hqk", queries, keys, preferred_element_type=f32) * score_scale
    scores = jnp.where(allowed[None], scores, MASK_FILL)
    top_score = jnp.max(scores, axis=-1, keepdims=True)
    log_total = top_score + jnp.log(jnp.sum(jnp.exp(scores - top_score), axis=-1, keepdims=True))
    weights = jnp.exp(scores - log_total)
    weights_low = weights.astype(bf16)
    attended = jnp.einsum("hqk,khd->qhd", weights_low, values, preferred_element_type=f32)
    attn_own = attended.astype(bf16).reshape(seq_len, own_width)
    attn_own, grad_block = after(attn_own, cotangent.reshape(token_count, width))
    grad_rows = lax.all_gather(grad_block, "ctx", axis=0, tiled=True)
    attn_parts = dot(attn_own, out_weight).astype(bf16)
    own_tokens = tokens.reshape(token_count, width).astype(f32)
    own_residual = own_tokens + ring_scatter(attn_parts, ctx_size, ctx_index)

    normed_two, inv_two = rms_norm(own_residual, ffn_gain)
    own_low = normed_two.astype(bf16)
    low_two = ring_gather(own_low, ctx_size, ctx_index)
    mixed_weight = jnp.concatenate([router_weight, gate_vector[:, None]], axis=1)
    logits = dot(low_two, mixed_weight)
    probs_all = jax.nn.softmax(logits[:, :expert_count], axis=-1)
    scale_all = jax.nn.sigmoid(logits[:, expert_count])
    gate_all = lax.dynamic_index_in_dim(probs_all, ctx_index, 1, keepdims=False)

    named = jnp.any(route_rows == ctx_index, axis=-1)
    before = jnp.arange(token_count)[:, None] < jnp.arange(token_count)[None, :]
    rank = dot(named.astype(bf16), before.astype(bf16)).astype(i32)
    slot_of = jnp.where(named & (rank < capacity), rank, -1)
    slot_mask = slot_of[:, None, :] == jnp.arange(capacity, dtype=i32)[None, :, None]
    slot_map = slot_mask.astype(bf16)
    blocks_two = low_two.reshape(ctx_size, token_count, width)
    gate_blocks = gate_all.reshape(ctx_size, token_count)

    def to_slots(blocks):
        picked = jnp.einsum("bmt,btd->bmd", slot_map, blocks, preferred_element_type=f32)
        return picked.reshape(ctx_size * capacity, width)

    def to_tokens(slots):
        spread = jnp.einsum(
            "bmt,bmd->btd",
            slot_map,
            slots.reshape(ctx_size, capacity, width),
            preferred_element_type=f32,
        )
        return spread.reshape(seq_len, width)

    buffer = to_slots(blocks_two).astype(bf16)
    expert_pre = dot(buffer, expert_in)
    expert_hid = swiglu(expert_pre, FE).astype(bf16)
    expert_res = dot(expert_hid, expert_out).astype(bf16)
    routed = gate_all[:, None] * to_tokens(expert_res)

    shared_in = shared_in.transpose(1, 0, 2, 3).reshape(width, 2 * fs_own)
    shared_pre = dot(low_two, shared_in)
    shared_hid = swiglu(shared_pre, fs_own).astype(bf16)
    shared_res = dot(shared_hid, shared_out)
    out_parts = (scale_all[:, None] * shared_res + routed).astype(bf16)
    out_sum = ring_scatter(out_parts, ctx_size, ctx_index)

    grad_slots = to_slots(grad_rows.reshape(ctx_size, token_count, width))
    gate_slots = jnp.sum(jnp.where(slot_mask, gate_blocks[:, None, :], 0.0), axis=-1).reshape(-1, 1)
    grad_res = (gate_slots * grad_slots).astype(bf16)
    slot_dots = jnp.sum(grad_slots * expert_res.astype(f32), axis=-1).reshape(ctx_size, capacity, 1)
    grad_gates = jnp.sum(jnp.where(slot_mask, slot_dots, 0.0), axis=1)
    grad_expert_out = t_dot(expert_hid, grad_res)
    grad_hid = dot_t(grad_res, expert_out)
    grad_pre = swiglu_back(expert_pre, FE, grad_hid).astype(bf16)
    grad_expert_in = t_dot(buffer, grad_pre)
    grad_buffer = dot_t(grad_pre, expert_in).astype(bf16)

    grad_expert_in, grad_expert_out, grad_shared_res = after(
        grad_expert_in.astype(bf16),
        grad_expert_out.astype(bf16),
        (scale_all[:, None] * grad_rows.astype(f32)).astype(bf16),
    )
    sum_expert_out = sum_rows(grad_expert_out)
    sum_expert_in = sum_rows(grad_expert_in)

    grad_f32 = grad_rows.astype(f32)
    gate_dots = jnp.sum(grad_f32 * shared_res, axis=-1).reshape(ctx_size, token_count)
    grad_shared_out = t_dot(shared_hid, grad_shared_res)
    grad_shared_hid = dot_t(grad_shared_res, shared_out)
    grad_shared_pre = swiglu_back(shared_pre, fs_own, grad_shared_hid).astype(bf16)
    grad_shared_in = t_dot(low_two, grad_shared_pre)
    grad_shared_pre, out_sum = after(grad_shared_pre, out_sum)
    two_parts = (dot_t(grad_shared_pre, shared_in) + to_tokens(grad_buffer)).astype(bf16)
    grad_two = ring_scatter(two_parts, ctx_size, ctx_index)
    sum_expert_in, grad_shared_in, grad_shared_out = after(
        sum_expert_in, grad_shared_in.astype(bf16), grad_shared_out.astype(bf16)
    )
    sum_shared_in = grad_shared_in.reshape(ctx_size, fsdp_size, shard, 2 * fs_own)
    sum_shared_in = lax.psum_scatter(
        sum_shared_in.transpose(1, 0, 2, 3).reshape(width, 2 * fs_own),
        "fsdp",
        scatter_dimension=0,
        tiled=True,
    ).reshape(ctx_size, shard, 2 * fs_own)
    sum_shared_out = sum_rows(grad_shared_out)
    output = (own_residual + out_sum).astype(bf16).reshape(tokens.shape)

    dots = jnp.stack([grad_gates, gate_dots], axis=1)
    dots = lax.all_to_all(dots, "ctx", split_axis=0, concat_axis=0, tiled=True)
    own_probs = own_rows(probs_all)
    own_scale = own_rows(scale_all)
    own_chosen = routes.reshape(token_count, top_count)
    chosen_mask = jnp.any(
        own_chosen[..., None] == jnp.arange(expert_count, dtype=i32), axis=1
    )
    grad_probs = jnp.where(chosen_mask, dots[:, 0].T, 0.0)
    grad_logits = (
        own_probs * (grad_probs - jnp.sum(own_probs * grad_probs, axis=-1, keepdims=True))
    ).astype(bf16)
    grad_gate_pre = (jnp.sum(dots[:, 1], axis=0) * own_scale * (1.0 - own_scale)).astype(bf16)
    grad_router = t_dot(own_low, grad_logits)
    grad_gate_vector = t_dot(own_low, grad_gate_pre[:, None])
    grad_two = grad_two + dot_t(grad_logits, router_weight)
    grad_two = grad_two + grad_gate_pre.astype(f32)[:, None] * gate_vector.astype(f32)[None, :]
    grad_resid_norm, grad_gain_two = rms_back(
        own_residual, inv_two, ffn_gain, grad_two
    )
    grad_resid = cotangent.reshape(token_count, width).astype(f32) + grad_resid_norm

    grad_mixed = grad_resid.astype(bf16)
    mixed_all = ring_gather(grad_mixed, ctx_size, ctx_index)
    grad_attn = dot_t(mixed_all, out_weight).astype(bf16).reshape(head_shape)
    grad_weights = jnp.einsum("qhd,khd->hqk", grad_attn, values, preferred_element_type=f32)
    delta = jnp.sum(weights * grad_weights, axis=-1, keepdims=True)
    grad_scores = jnp.where(allowed[None], weights * (grad_weights - delta), 0.0).astype(bf16)
    grad_q = jnp.einsum("hqk,khd->qhd", grad_scores, keys, preferred_element_type=f32) * score_scale
    grad_k = (
        jnp.einsum("hqk,qhd->khd", grad_scores, queries, preferred_element_type=f32) * score_scale
    )
    grad_v = jnp.einsum("hqk,qhd->khd", weights_low, grad_attn, preferred_element_type=f32)
    grad_projected = jnp.concatenate(
        [
            rotate_back(grad_q, cos_tab, sine_tab).reshape(seq_len, own_width),
            rotate_back(grad_k, cos_tab, sine_tab).reshape(seq_len, own_width),
            grad_v.reshape(seq_len, own_width),
        ],
        axis=-1,
    ).astype(bf16)
    one_sums = dot_t(grad_projected, qkv_weight)
    grad_gain_one = jnp.sum(one_sums * inputs * inv_one_all, axis=0)
    one_parts = one_sums.astype(bf16)
    one_kept, grad_projected = after(one_parts, grad_projected)
    one_kept, sum_shared_in, sum_shared_out, sum_expert_in = after(
        one_kept, sum_shared_in, sum_shared_out, sum_expert_in
    )
    grad_normed = ring_scatter(one_parts, ctx_size, ctx_index, one_kept)
    grad_inputs_norm, unused = rms_back(
        own_tokens,
        own_rows(inv_one_all),
        attn_gain,
        grad_normed,
    )
    grad_tokens = (grad_resid + grad_inputs_norm).reshape(tokens.shape)
    grad_qkv_weight = t_dot(normed_low, grad_projected)
    grad_bias = jnp.sum(grad_projected.astype(f32), axis=0).reshape(3, 1, own_width)
    grad_bias = jnp.where(
        jnp.arange(ctx_size, dtype=i32)[None, :, None] == ctx_index, grad_bias, 0.0
    )

    grad_out_weight = t_dot(attn_own, mixed_all)
    sum_qkv_weight = fsdp_scatter(
        grad_qkv_weight.astype(bf16).reshape(ctx_size, fsdp_size, shard, 3 * own_width),
        fsdp_size,
        1,
    ).astype(bf16)
    small_grads = jnp.concatenate(
        [
            piece.reshape(device_count, -1)
            for piece in (grad_gain_one, grad_gain_two, grad_gate_vector, grad_router, grad_bias)
        ],
        axis=1,
    )
    small_grads = lax.psum_scatter(
        small_grads, ("ctx", "fsdp"), scatter_dimension=0, tiled=True
    ).reshape(small_size)
    return (
        output,
        grad_tokens,
        merge_columns(sum_qkv_weight, 3, ctx_size),
        small_grads[router_end:],
        sum_rows(grad_out_weight).astype(f32),
        small_grads[:shard],
        small_grads[shard : 2 * shard],
        small_grads[3 * shard : router_end].reshape(shard, expert_count),
        small_grads[2 * shard : 3 * shard],
        merge_columns(sum_shared_in, 2, ctx_size),
        sum_shared_out.astype(f32),
        sum_expert_in.astype(f32)[None],
        sum_expert_out.astype(f32)[None],
    )


def local_wide(
    tokens,
    segments,
    routes,
    cotangent,
    w_qkv,
    b_qkv,
    w_out,
    gain_attn,
    gain_ffn,
    w_router,
    w_shared_gate,
    w_shared_in,
    w_shared_out,
    w_expert_in,
    w_expert_out,
):
    block_len = tokens.shape[2]
    model_width = tokens.shape[3]
    token_count = 2 * block_len
    top_count = routes.shape[3]
    half_len = segments.shape[2]
    seq_len = 2 * half_len
    ctx_index = lax.axis_index("ctx")
    head_count = model_width // HD
    expert_count = w_router.shape[1]
    capacity = token_count * top_count // expert_count
    slot_count = expert_count * capacity
    key_rows = min(512, seq_len)
    key_blocks = seq_len // key_rows
    score_scale = HD ** (-0.5)
    head_shape = (token_count, head_count, HD)
    attn_set = (
        lax.all_gather(w_qkv, ("ctx", "fsdp"), axis=0, tiled=True),
        lax.all_gather(b_qkv, ("ctx", "fsdp"), axis=0, tiled=True),
        lax.all_gather(w_out, ("ctx", "fsdp"), axis=0, tiled=True),
        lax.all_gather(gain_attn, ("ctx", "fsdp"), axis=0, tiled=True),
    )
    qkv_weight, qkv_bias, out_weight, attn_gain = attn_set
    inputs = tokens.reshape(token_count, model_width).astype(jnp.float32)
    normed, inv_one = rms_norm(inputs, attn_gain.astype(jnp.float32))
    normed_low = normed.astype(jnp.bfloat16)
    projected = jnp.dot(
        normed_low, qkv_weight, preferred_element_type=jnp.float32
    ) + qkv_bias.astype(jnp.float32)
    local_index = jnp.arange(block_len, dtype=jnp.int32)
    query_pos = jnp.concatenate(
        [ctx_index * block_len + local_index, seq_len - (ctx_index + 1) * block_len + local_index]
    )
    half_index = jnp.arange(half_len, dtype=jnp.int32)
    key_pos = jnp.concatenate(
        [half_index, seq_len - block_len * (half_index // block_len + 1) + half_index % block_len]
    ).reshape(key_blocks, key_rows)
    key_seg = segments.reshape(key_blocks, key_rows)
    query_seg = lax.dynamic_slice_in_dim(segments[0], ctx_index * block_len, block_len, 1).reshape(
        token_count
    )
    cos_tab, sine_tab = rope_tables(query_pos, HD)
    queries = rotate(projected[:, :model_width].reshape(head_shape), cos_tab, sine_tab).astype(
        jnp.bfloat16
    )
    keys_own = rotate(
        projected[:, model_width : 2 * model_width].reshape(head_shape), cos_tab, sine_tab
    ).astype(jnp.bfloat16)
    values_own = projected[:, 2 * model_width :].astype(jnp.bfloat16)
    keys_all, values_all = (
        lax.all_gather(keys_own.reshape(2, block_len, model_width), "ctx", axis=1, tiled=True),
        lax.all_gather(values_own.reshape(2, block_len, model_width), "ctx", axis=1, tiled=True),
    )
    keys_all = keys_all.reshape(key_blocks, key_rows, head_count, HD)
    values_all = values_all.reshape(key_blocks, key_rows, head_count, HD)

    def score_block(key_blk, pos_blk, seg_blk):
        raw_scores = (
            jnp.einsum("qhd,khd->hqk", queries, key_blk, preferred_element_type=jnp.float32)
            * score_scale
        )
        allowed = (pos_blk[None, :] <= query_pos[:, None]) & (
            seg_blk[None, :] == query_seg[:, None]
        )
        return (jnp.where(allowed[None], raw_scores, MASK_FILL), allowed)

    def total_step(running, key_part):
        run_max, run_sum = running
        scores = score_block(key_part[0], key_part[1], key_part[2])[0]
        new_max = jnp.maximum(run_max, jnp.max(scores, axis=-1))
        run_sum = run_sum * jnp.exp(run_max - new_max) + jnp.sum(
            jnp.exp(scores - new_max[..., None]), axis=-1
        )
        return ((new_max, run_sum), None)

    start_max = jnp.full((head_count, token_count), MASK_FILL, jnp.float32)
    start_sum = jnp.zeros((head_count, token_count), jnp.float32)
    (run_max, run_sum), unused = lax.scan(
        total_step, (start_max, start_sum), (keys_all, key_pos, key_seg)
    )
    log_total = run_max + jnp.log(run_sum)

    def attend_step(summed, key_part):
        key_blk, value_blk, pos_blk, seg_blk = key_part
        scores = score_block(key_blk, pos_blk, seg_blk)[0]
        weights = jnp.exp(scores - log_total[..., None]).astype(jnp.bfloat16)
        return (
            summed
            + jnp.einsum("hqk,khd->qhd", weights, value_blk, preferred_element_type=jnp.float32),
            None,
        )

    key_stack = (keys_all, values_all, key_pos, key_seg)
    attended, unused = lax.scan(attend_step, jnp.zeros(head_shape, jnp.float32), key_stack)
    attn_low = attended.reshape(token_count, model_width).astype(jnp.bfloat16)
    residual = inputs + jnp.dot(attn_low, out_weight, preferred_element_type=jnp.float32)
    ffn_set = (
        lax.all_gather(gain_ffn, ("ctx", "fsdp"), axis=0, tiled=True),
        lax.all_gather(w_router, ("ctx", "fsdp"), axis=0, tiled=True),
        lax.all_gather(w_shared_gate, ("ctx", "fsdp"), axis=0, tiled=True),
        lax.all_gather(w_shared_in, ("ctx", "fsdp"), axis=0, tiled=True),
        lax.all_gather(w_shared_out, ("ctx", "fsdp"), axis=0, tiled=True),
    )
    ffn_gain, router_weight, gate_vector, shared_in, shared_out = ffn_set
    normed_two, inv_two = rms_norm(residual, ffn_gain.astype(jnp.float32))
    low_two = normed_two.astype(jnp.bfloat16)
    logits = jnp.dot(low_two, router_weight, preferred_element_type=jnp.float32)
    router_probs = jax.nn.softmax(logits, axis=-1)
    chosen = routes.reshape(token_count, top_count)
    chosen_mask = chosen[..., None] == jnp.arange(expert_count, dtype=jnp.int32)
    gate_vals = jnp.sum(jnp.where(chosen_mask, router_probs[:, None, :], 0.0), axis=-1)
    shared_scale = jax.nn.sigmoid(jnp.dot(low_two, gate_vector, preferred_element_type=jnp.float32))
    shared_pre = jnp.dot(low_two, shared_in, preferred_element_type=jnp.float32)
    shared_hid = swiglu(shared_pre, FS).astype(jnp.bfloat16)
    shared_res = jnp.dot(shared_hid, shared_out, preferred_element_type=jnp.float32)
    pair_routes = chosen.reshape(token_count * top_count)
    expert_marks = (
        pair_routes[:, None] == jnp.arange(expert_count, dtype=jnp.int32)[None, :]
    ).astype(jnp.int32)
    pair_ranks = jnp.sum((jnp.cumsum(expert_marks, axis=0) - expert_marks) * expert_marks, axis=1)
    pair_target = jnp.where(pair_ranks < capacity, pair_routes * capacity + pair_ranks, -1)
    pair_map = pair_target[:, None] == jnp.arange(slot_count, dtype=jnp.int32)[None, :]
    pair_low = pair_map.astype(jnp.bfloat16)
    token_map = jnp.sum(
        pair_map.reshape(token_count, top_count, slot_count).astype(jnp.int32), axis=1
    ).astype(jnp.bfloat16)
    outgoing = jnp.einsum(
        "tc,td->cd", token_map, low_two, preferred_element_type=jnp.float32
    ).astype(jnp.bfloat16)
    incoming = lax.all_to_all(
        outgoing.reshape(expert_count, capacity, model_width),
        "ctx",
        split_axis=0,
        concat_axis=1,
        tiled=True,
    )
    expert_in, expert_out = (
        lax.all_gather(w_expert_in, "fsdp", axis=1, tiled=True),
        lax.all_gather(w_expert_out, "fsdp", axis=1, tiled=True),
    )
    expert_pre = jnp.einsum("erd,edf->erf", incoming, expert_in, preferred_element_type=jnp.float32)
    expert_hid = swiglu(expert_pre, FE).astype(jnp.bfloat16)
    expert_res = jnp.einsum(
        "erf,efd->erd", expert_hid, expert_out, preferred_element_type=jnp.float32
    ).astype(jnp.bfloat16)
    returned = lax.all_to_all(expert_res, "ctx", split_axis=1, concat_axis=0, tiled=True).reshape(
        slot_count, model_width
    )
    pair_vals = jnp.dot(pair_low, returned, preferred_element_type=jnp.float32).reshape(
        token_count, top_count, model_width
    )
    routed = jnp.sum(gate_vals[..., None] * pair_vals, axis=1)
    output = (
        (residual + shared_scale[:, None] * shared_res + routed)
        .astype(jnp.bfloat16)
        .reshape(tokens.shape)
    )
    grad_out = cotangent.reshape(token_count, model_width).astype(jnp.float32)
    pair_grads = gate_vals[..., None] * grad_out[:, None, :]
    grad_gates = jnp.sum(grad_out[:, None, :] * pair_vals, axis=-1)
    grad_returned = jnp.einsum(
        "pc,pd->cd",
        pair_map.astype(jnp.float32),
        pair_grads.reshape(token_count * top_count, model_width),
        precision=HIGHEST,
    ).astype(jnp.bfloat16)
    grad_res = lax.all_to_all(
        grad_returned.reshape(expert_count, capacity, model_width),
        "ctx",
        split_axis=0,
        concat_axis=1,
        tiled=True,
    )
    grad_expert_out = jnp.einsum(
        "erf,erd->efd", expert_hid, grad_res, preferred_element_type=jnp.float32
    )
    grad_hid = jnp.einsum("erd,efd->erf", grad_res, expert_out, preferred_element_type=jnp.float32)
    grad_pre = swiglu_back(expert_pre, FE, grad_hid).astype(jnp.bfloat16)
    grad_expert_in = jnp.einsum(
        "erd,erf->edf", incoming, grad_pre, preferred_element_type=jnp.float32
    )
    grad_incoming = jnp.einsum(
        "erf,edf->erd", grad_pre, expert_in, preferred_element_type=jnp.float32
    ).astype(jnp.bfloat16)
    grad_outgoing = lax.all_to_all(
        grad_incoming, "ctx", split_axis=1, concat_axis=0, tiled=True
    ).reshape(slot_count, model_width)
    expert_grads = (
        lax.psum_scatter(
            grad_expert_in.astype(jnp.bfloat16), "fsdp", scatter_dimension=1, tiled=True
        ).astype(jnp.float32),
        lax.psum_scatter(
            grad_expert_out.astype(jnp.bfloat16), "fsdp", scatter_dimension=1, tiled=True
        ).astype(jnp.float32),
    )
    grad_two = jnp.einsum("tc,cd->td", token_map, grad_outgoing, preferred_element_type=jnp.float32)
    grad_probs = jnp.sum(jnp.where(chosen_mask, grad_gates[..., None], 0.0), axis=1)
    grad_logits = (
        router_probs * (grad_probs - jnp.sum(router_probs * grad_probs, axis=-1, keepdims=True))
    ).astype(jnp.bfloat16)
    grad_router = jnp.einsum("td,te->de", low_two, grad_logits, preferred_element_type=jnp.float32)
    grad_shared_res = (shared_scale[:, None] * grad_out).astype(jnp.bfloat16)
    grad_gate_pre = (
        jnp.sum(grad_out * shared_res, axis=-1) * shared_scale * (1.0 - shared_scale)
    ).astype(jnp.bfloat16)
    grad_shared_out = jnp.einsum(
        "tf,td->fd", shared_hid, grad_shared_res, preferred_element_type=jnp.float32
    )
    grad_shared_hid = jnp.einsum(
        "td,fd->tf", grad_shared_res, shared_out, preferred_element_type=jnp.float32
    )
    grad_shared_pre = swiglu_back(shared_pre, FS, grad_shared_hid).astype(jnp.bfloat16)
    grad_shared_in = jnp.einsum(
        "td,tf->df", low_two, grad_shared_pre, preferred_element_type=jnp.float32
    )
    grad_gate_vector = jnp.einsum(
        "td,t->d", low_two, grad_gate_pre, preferred_element_type=jnp.float32
    )
    grad_two = grad_two + jnp.einsum(
        "te,de->td", grad_logits, router_weight, preferred_element_type=jnp.float32
    )
    grad_two = grad_two + jnp.einsum(
        "tf,df->td", grad_shared_pre, shared_in, preferred_element_type=jnp.float32
    )
    grad_two = (
        grad_two
        + grad_gate_pre.astype(jnp.float32)[:, None] * gate_vector.astype(jnp.float32)[None, :]
    )
    grad_resid_norm, grad_gain_two = rms_back(
        residual, inv_two, ffn_gain.astype(jnp.float32), grad_two
    )
    grad_resid = grad_out + grad_resid_norm
    ffn_grads = (
        lax.psum_scatter(grad_gain_two, ("ctx", "fsdp"), scatter_dimension=0, tiled=True),
        lax.psum_scatter(grad_router, ("ctx", "fsdp"), scatter_dimension=0, tiled=True),
        lax.psum_scatter(grad_gate_vector, ("ctx", "fsdp"), scatter_dimension=0, tiled=True),
        lax.psum_scatter(grad_shared_in, ("ctx", "fsdp"), scatter_dimension=0, tiled=True),
        lax.psum_scatter(grad_shared_out, ("ctx", "fsdp"), scatter_dimension=0, tiled=True),
    )
    grad_mixed = grad_resid.astype(jnp.bfloat16)
    grad_out_weight = jnp.einsum(
        "tc,td->cd", attn_low, grad_mixed, preferred_element_type=jnp.float32
    )
    grad_attn = (
        jnp.einsum("td,cd->tc", grad_mixed, out_weight, preferred_element_type=jnp.float32)
        .astype(jnp.bfloat16)
        .reshape(head_shape)
    )

    def delta_step(summed, key_part):
        key_blk, value_blk, pos_blk, seg_blk = key_part
        weights = jnp.exp(score_block(key_blk, pos_blk, seg_blk)[0] - log_total[..., None])
        grad_weights = jnp.einsum(
            "qhd,khd->hqk", grad_attn, value_blk, preferred_element_type=jnp.float32
        )
        return (summed + jnp.sum(weights * grad_weights, axis=-1), None)

    delta_sum, unused = lax.scan(
        delta_step, jnp.zeros((head_count, token_count), jnp.float32), key_stack
    )

    def grad_step(summed, key_part):
        key_blk, value_blk, pos_blk, seg_blk = key_part
        scores, allowed = score_block(key_blk, pos_blk, seg_blk)
        weights = jnp.exp(scores - log_total[..., None])
        grad_weights = jnp.einsum(
            "qhd,khd->hqk", grad_attn, value_blk, preferred_element_type=jnp.float32
        )
        grad_scores = jnp.where(
            allowed[None], weights * (grad_weights - delta_sum[..., None]), 0.0
        ).astype(jnp.bfloat16)
        summed = (
            summed
            + jnp.einsum("hqk,khd->qhd", grad_scores, key_blk, preferred_element_type=jnp.float32)
            * score_scale
        )
        grad_key = (
            jnp.einsum("hqk,qhd->khd", grad_scores, queries, preferred_element_type=jnp.float32)
            * score_scale
        )
        grad_value = jnp.einsum(
            "hqk,qhd->khd",
            weights.astype(jnp.bfloat16),
            grad_attn,
            preferred_element_type=jnp.float32,
        )
        return (summed, (grad_key, grad_value))

    grad_query, (grad_keys, grad_values) = lax.scan(
        grad_step, jnp.zeros(head_shape, jnp.float32), key_stack
    )
    grad_keys_own, grad_values_own = (
        lax.psum_scatter(
            grad_keys.reshape(2, half_len, model_width).astype(jnp.bfloat16),
            "ctx",
            scatter_dimension=1,
            tiled=True,
        ).astype(jnp.float32),
        lax.psum_scatter(
            grad_values.reshape(2, half_len, model_width).astype(jnp.bfloat16),
            "ctx",
            scatter_dimension=1,
            tiled=True,
        ).astype(jnp.float32),
    )
    grad_q_rows = rotate_back(grad_query, cos_tab, sine_tab).reshape(token_count, model_width)
    grad_k_rows = rotate_back(grad_keys_own.reshape(head_shape), cos_tab, sine_tab).reshape(
        token_count, model_width
    )
    grad_projected = jnp.concatenate(
        [grad_q_rows, grad_k_rows, grad_values_own.reshape(token_count, model_width)], axis=-1
    ).astype(jnp.bfloat16)
    grad_qkv_weight = jnp.einsum(
        "td,te->de", normed_low, grad_projected, preferred_element_type=jnp.float32
    )
    grad_qkv_bias = jnp.sum(grad_projected.astype(jnp.float32), axis=0)
    grad_normed = jnp.einsum(
        "te,de->td", grad_projected, qkv_weight, preferred_element_type=jnp.float32
    )
    grad_inputs_norm, grad_gain_one = rms_back(
        inputs, inv_one, attn_gain.astype(jnp.float32), grad_normed
    )
    grad_tokens = (grad_resid + grad_inputs_norm).reshape(tokens.shape)
    attn_grads = (
        lax.psum_scatter(grad_qkv_weight, ("ctx", "fsdp"), scatter_dimension=0, tiled=True),
        lax.psum_scatter(grad_qkv_bias, ("ctx", "fsdp"), scatter_dimension=0, tiled=True),
        lax.psum_scatter(grad_out_weight, ("ctx", "fsdp"), scatter_dimension=0, tiled=True),
        lax.psum_scatter(grad_gain_one, ("ctx", "fsdp"), scatter_dimension=0, tiled=True),
    )
    return (
        output,
        grad_tokens,
        attn_grads[0],
        attn_grads[1],
        attn_grads[2],
        attn_grads[3],
        ffn_grads[0],
        ffn_grads[1],
        ffn_grads[2],
        ffn_grads[3],
        ffn_grads[4],
        expert_grads[0],
        expert_grads[1],
    )


def solution(mesh):
    in_specs = (
        P("fsdp", None, "ctx", None),
        P("fsdp", None, None),
        P("fsdp", None, "ctx", None),
        P("fsdp", None, "ctx", None),
        P(("ctx", "fsdp"), None),
        P(("ctx", "fsdp")),
        P(("ctx", "fsdp"), None),
        P(("ctx", "fsdp")),
        P(("ctx", "fsdp")),
        P(("ctx", "fsdp"), None),
        P(("ctx", "fsdp")),
        P(("ctx", "fsdp"), None),
        P(("ctx", "fsdp"), None),
        P("ctx", "fsdp", None),
        P("ctx", "fsdp", None),
    )
    out_specs = (
        P("fsdp", None, "ctx", None),
        P("fsdp", None, "ctx", None),
        P(("ctx", "fsdp"), None),
        P(("ctx", "fsdp")),
        P(("ctx", "fsdp"), None),
        P(("ctx", "fsdp")),
        P(("ctx", "fsdp")),
        P(("ctx", "fsdp"), None),
        P(("ctx", "fsdp")),
        P(("ctx", "fsdp"), None),
        P(("ctx", "fsdp"), None),
        P("ctx", "fsdp", None),
        P("ctx", "fsdp", None),
    )
    ctx_size = mesh.shape["ctx"]
    fsdp_size = mesh.shape["fsdp"]

    def local(*arrays):
        if HEADS % ctx_size:
            return local_wide(*arrays)
        return local_split(ctx_size, fsdp_size, *arrays)

    return jax.shard_map(local, mesh=mesh, in_specs=in_specs, out_specs=out_specs, check_vma=False)
```

```python
import jax
import jax.numpy as jnp
from jax import lax
from jax.sharding import PartitionSpec as P

HD = 128
HEADS = 16
FS = 5632
FE = 1408


RMS_EPS = 1e-06
ROPE_THETA = 1000000.0
MASK_FILL = -1e30
HIGHEST = lax.Precision.HIGHEST


def rope_tables(positions, head_dim):
    half_dim = head_dim // 2
    inv_freq = ROPE_THETA ** (-(jnp.arange(half_dim, dtype=jnp.float32) * 2.0 / head_dim))
    angles = positions.astype(jnp.float32)[:, None] * inv_freq[None, :]
    cos_tab = jnp.concatenate([jnp.cos(angles), jnp.cos(angles)], axis=-1)
    sine_tab = jnp.concatenate([jnp.sin(angles), jnp.sin(angles)], axis=-1)
    return (cos_tab, sine_tab)


def rotate(values, cos_tab, sine_tab):
    half_dim = values.shape[-1] // 2
    turned = jnp.concatenate([-values[..., half_dim:], values[..., :half_dim]], axis=-1)
    return values * cos_tab[:, None, :] + turned * sine_tab[:, None, :]


def rotate_back(upstream, cos_tab, sine_tab):
    half_dim = upstream.shape[-1] // 2
    scaled = upstream * sine_tab[:, None, :]
    return upstream * cos_tab[:, None, :] + jnp.concatenate(
        [scaled[..., half_dim:], -scaled[..., :half_dim]], axis=-1
    )


def rms_norm(values, gain_vec):
    inv_rms = lax.rsqrt(jnp.mean(values * values, axis=-1, keepdims=True) + RMS_EPS)
    return (values * inv_rms * gain_vec, inv_rms)


def rms_back(values, inv_rms, gain_vec, upstream):
    weighted = upstream * gain_vec
    inner_mean = jnp.mean(weighted * values, axis=-1, keepdims=True)
    return (
        inv_rms * weighted - values * inv_rms * inv_rms * inv_rms * inner_mean,
        jnp.sum(upstream * values * inv_rms, axis=0),
    )


def swiglu(pre_act, split_at):
    return jax.nn.silu(pre_act[..., :split_at]) * pre_act[..., split_at:]


def swiglu_back(pre_act, split_at, upstream):
    gate_part = pre_act[..., :split_at]
    up_part = pre_act[..., split_at:]
    sigmoid_g = jax.nn.sigmoid(gate_part)
    d_gate = upstream * up_part * sigmoid_g * (1.0 + gate_part * (1.0 - sigmoid_g))
    d_up = upstream * gate_part * sigmoid_g
    return jnp.concatenate([d_gate, d_up], axis=-1)


def ring_order(size):
    return list(range(0, size, 2)) + list(range(size - 1, 0, -2))


def ring_steps(size):
    order = ring_order(size)
    ahead = [(order[i], order[(i + 1) % size]) for i in range(size)]
    back = [(dst, src) for src, dst in ahead]
    return (ahead, back)


def ring_peers(size, ctx_index):
    order = ring_order(size)
    place = {dev: i for i, dev in enumerate(order)}
    table = jnp.array(
        [[order[(place[dev] + k) % size] for k in range(size)] for dev in range(size)], jnp.int32
    )
    row = lax.dynamic_index_in_dim(table, ctx_index, 0, keepdims=False)
    return [row[k] for k in range(size)]


def ring_walk(block, size, ctx_index, out, put):
    rows = block.shape[0]
    ahead, back = ring_steps(size)
    peers = ring_peers(size, ctx_index)
    half = size // 2
    out = put(out, block, ctx_index, 0)
    fore = rear = block
    for k in range(1, half):
        fore = lax.ppermute(fore, "ctx", ahead)
        rear = lax.ppermute(rear, "ctx", back)
        out = put(out, fore, peers[size - k], 0)
        out = put(out, rear, peers[k], 0)
    fore = lax.ppermute(fore[: rows // 2], "ctx", ahead)
    rear = lax.ppermute(rear[rows // 2 :], "ctx", back)
    out = put(out, fore, peers[half], 0)
    return put(out, rear, peers[half], rows // 2)


def ring_gather(block, size, ctx_index):
    rows, width = block.shape

    def put(out, piece, peer, offset):
        return lax.dynamic_update_slice(out, piece, (peer * rows + offset, jnp.zeros_like(peer)))

    return ring_walk(block, size, ctx_index, jnp.zeros((size * rows, width), block.dtype), put)


def ring_sums(parts, size, ctx_index):
    f32 = jnp.float32
    rows = parts.shape[0] // size
    ahead, back = ring_steps(size)
    peers = ring_peers(size, ctx_index)
    half = size // 2

    def own(k, start, count):
        first = (peers[k % size] * rows + start, jnp.zeros_like(peers[0]))
        return lax.dynamic_slice(parts, first, (count, parts.shape[1])).astype(f32)

    def low(values):
        return values.astype(jnp.bfloat16)

    cut = rows // 2
    fore = lax.ppermute(low(own(half, 0, cut)), "ctx", ahead)
    rear = lax.ppermute(low(own(half, cut, cut)), "ctx", back)
    fore = jnp.concatenate(
        [low(fore.astype(f32) + own(half - 1, 0, cut)), low(own(half - 1, cut, cut))], axis=0
    )
    rear = jnp.concatenate(
        [low(own(1 - half, 0, cut)), low(rear.astype(f32) + own(1 - half, cut, cut))], axis=0
    )
    for k in range(half - 1, 0, -1):
        fore = lax.ppermute(fore, "ctx", ahead)
        rear = lax.ppermute(rear, "ctx", back)
        if k > 1:
            fore = low(fore.astype(f32) + own(k - 1, 0, rows))
            rear = low(rear.astype(f32) + own(1 - k, 0, rows))
    return (fore, rear)


def ring_scatter(parts, size, ctx_index, kept=None):
    fore, rear = ring_sums(parts, size, ctx_index)
    kept = (parts if kept is None else kept).reshape(size, -1, parts.shape[1])
    kept = lax.dynamic_index_in_dim(kept, ctx_index, 0, keepdims=False)
    return kept.astype(jnp.float32) + fore.astype(jnp.float32) + rear.astype(jnp.float32)


def other_core(size):
    return [(i, i ^ 1) for i in range(size)]


def other_chip(size):
    return [(i, i ^ 2) for i in range(size)]


def after(value, *deps):
    return lax.optimization_barrier((value,) + deps)


def fsdp_gather(shard, size):
    index = lax.axis_index("fsdp")
    rows, width = shard.shape
    far = lax.ppermute(shard, "fsdp", other_chip(size))
    pair = jnp.where(
        index < 2, jnp.stack([shard, far], axis=0), jnp.stack([far, shard], axis=0)
    )
    near = lax.ppermute(pair, "fsdp", other_core(size))
    out = jnp.zeros((2, 2, rows, width), shard.dtype)
    out = lax.dynamic_update_index_in_dim(out, pair, index % 2, 1)
    out = lax.dynamic_update_index_in_dim(out, near, 1 - index % 2, 1)
    return out.reshape(size * rows, width)


def fsdp_scatter(grad, size, axis):
    index = lax.axis_index("fsdp")

    def pick(peer):
        return lax.dynamic_index_in_dim(grad, peer, axis, keepdims=False)

    far_near = lax.ppermute(pick(index ^ 3), "fsdp", other_core(size))
    near = lax.ppermute(pick(index ^ 1), "fsdp", other_core(size))
    far = (pick(index ^ 2).astype(jnp.float32) + far_near.astype(jnp.float32)).astype(jnp.bfloat16)
    far = lax.ppermute(far, "fsdp", other_chip(size))
    return pick(index).astype(jnp.float32) + near.astype(jnp.float32) + far.astype(jnp.float32)


def column_pieces(weight, groups, size, extra):
    rows = weight.shape[0]
    width = weight.shape[1] // (groups * size)
    pieces = weight.reshape(rows, groups, size, width).transpose(2, 0, 1, 3)
    pieces = pieces.reshape(size, rows, groups * width)
    if extra is not None:
        count = extra.shape[0]
        more = -(-count // (groups * width * 16)) * 16
        extra = jnp.pad(extra, (0, more * groups * width - count))
        extra = jnp.broadcast_to(
            extra.reshape(1, more, groups * width), (size, more, groups * width)
        )
        pieces = jnp.concatenate([pieces, extra], axis=1)
    return lax.all_to_all(pieces, "ctx", split_axis=0, concat_axis=0, tiled=True)


def merge_columns(pieces, groups, size):
    width = pieces.shape[2] // groups
    columns = [
        pieces[peer, :, group * width : (group + 1) * width]
        for group in range(groups)
        for peer in range(size)
    ]
    return jnp.concatenate(columns, axis=1).astype(jnp.float32)


def local_split(
    ctx_size,
    fsdp_size,
    tokens,
    segments,
    routes,
    cotangent,
    w_qkv,
    b_qkv,
    w_out,
    gain_attn,
    gain_ffn,
    w_router,
    w_shared_gate,
    w_shared_in,
    w_shared_out,
    w_expert_in,
    w_expert_out,
):
    bf16, f32, i32 = jnp.bfloat16, jnp.float32, jnp.int32
    device_count = ctx_size * fsdp_size
    block_len = tokens.shape[2]
    width = tokens.shape[3]
    token_count = 2 * block_len
    top_count = routes.shape[3]
    seq_len = token_count * ctx_size
    ctx_index = lax.axis_index("ctx")
    expert_count = w_router.shape[1]
    capacity = token_count * top_count // expert_count
    own_heads = HEADS // ctx_size
    own_width = own_heads * HD
    fs_own = FS // ctx_size
    score_scale = HD ** (-0.5)

    def dot(a, b):
        return jnp.dot(a, b, preferred_element_type=f32)

    def dot_t(a, b):
        return lax.dot_general(a, b, (((1,), (1,)), ((), ())), preferred_element_type=f32)

    def t_dot(a, b):
        return lax.dot_general(a, b, (((0,), (0,)), ((), ())), preferred_element_type=f32)

    def own_rows(values):
        return lax.dynamic_index_in_dim(
            values.reshape((ctx_size, token_count) + values.shape[1:]), ctx_index, 0, keepdims=False
        )

    def sum_rows(grad):
        return lax.psum_scatter(grad.astype(bf16), "fsdp", scatter_dimension=0, tiled=True)

    shard = width // device_count
    small = [gain_attn, gain_ffn, w_shared_gate, w_router.reshape(-1), b_qkv]
    small_size = sum(piece.shape[0] for piece in small)
    small = jnp.concatenate(small + [routes.astype(bf16).reshape(-1)], axis=0)
    small_count = small.shape[0]
    token_rows = ring_gather(tokens.reshape(token_count, width), ctx_size, ctx_index)
    expert_out = lax.all_gather(w_expert_out[0], "fsdp", axis=0, tiled=True)
    pieces = column_pieces(w_qkv, 3, ctx_size, small)
    pieces, expert_out = after(pieces, expert_out)
    pieces = lax.all_gather(pieces, "fsdp", axis=0, tiled=False).transpose(1, 0, 2, 3)
    qkv_weight = pieces[:, :, :shard].reshape(width, 3 * own_width)
    small = pieces[:, :, shard:].reshape(device_count, -1)[:, :small_count]
    attn_gain = small[:, :shard].reshape(width).astype(f32)
    ffn_gain = small[:, shard : 2 * shard].reshape(width).astype(f32)
    gate_vector = small[:, 2 * shard : 3 * shard].reshape(width)
    router_end = 3 * shard + shard * expert_count
    router_weight = small[:, 3 * shard : router_end].reshape(width, expert_count)
    bias = small[:, router_end:small_size].reshape(3, ctx_size, own_width).astype(f32)
    bias = lax.dynamic_index_in_dim(bias, ctx_index, 1, keepdims=False).reshape(3 * own_width)
    route_rows = small[:, small_size:].astype(i32)
    route_rows = lax.dynamic_index_in_dim(
        route_rows.reshape(ctx_size, fsdp_size, -1), lax.axis_index("fsdp"), 1, keepdims=False
    ).reshape(ctx_size, token_count, top_count)

    expert_in = lax.all_gather(w_expert_in[0], "fsdp", axis=0, tiled=True)
    out_weight = fsdp_gather(w_out, fsdp_size)

    block_ids = jnp.arange(ctx_size, dtype=i32)[:, None]
    local_index = jnp.arange(block_len, dtype=i32)[None, :]
    positions = jnp.stack(
        [
            block_ids * block_len + local_index,
            seq_len - (block_ids + 1) * block_len + local_index,
        ],
        axis=1,
    ).reshape(seq_len)
    seg_rows = (
        segments.reshape(2, ctx_size, block_len).transpose(1, 0, 2).reshape(seq_len)
    )
    cos_tab, sine_tab = rope_tables(positions, HD)

    inputs = token_rows.astype(f32)
    normed, inv_one_all = rms_norm(inputs, attn_gain)
    normed_low = normed.astype(bf16)
    projected = dot(normed_low, qkv_weight) + bias
    head_shape = (seq_len, own_heads, HD)
    queries = rotate(projected[:, :own_width].reshape(head_shape), cos_tab, sine_tab).astype(bf16)
    keys = rotate(
        projected[:, own_width : 2 * own_width].reshape(head_shape), cos_tab, sine_tab
    ).astype(bf16)
    values = projected[:, 2 * own_width :].reshape(head_shape).astype(bf16)
    queries, in_shard, out_shard = after(queries, w_shared_in, w_shared_out)
    shared_in = column_pieces(in_shard, 2, ctx_size, None)
    shared_in = lax.all_gather(shared_in, "fsdp", axis=0, tiled=False)
    shared_out = fsdp_gather(out_shard, fsdp_size)
    allowed = (positions[None, :] <= positions[:, None]) & (seg_rows[None, :] == seg_rows[:, None])
    scores = jnp.einsum("qhd,khd->hqk", queries, keys, preferred_element_type=f32) * score_scale
    scores = jnp.where(allowed[None], scores, MASK_FILL)
    top_score = jnp.max(scores, axis=-1, keepdims=True)
    log_total = top_score + jnp.log(jnp.sum(jnp.exp(scores - top_score), axis=-1, keepdims=True))
    weights = jnp.exp(scores - log_total)
    weights_low = weights.astype(bf16)
    attended = jnp.einsum("hqk,khd->qhd", weights_low, values, preferred_element_type=f32)
    attn_own = attended.astype(bf16).reshape(seq_len, own_width)
    attn_own, grad_block = after(attn_own, cotangent.reshape(token_count, width))
    grad_rows = lax.all_gather(grad_block, "ctx", axis=0, tiled=True)
    attn_parts = dot(attn_own, out_weight).astype(bf16)
    own_tokens = tokens.reshape(token_count, width).astype(f32)
    own_residual = own_tokens + ring_scatter(attn_parts, ctx_size, ctx_index)

    normed_two, inv_two = rms_norm(own_residual, ffn_gain)
    own_low = normed_two.astype(bf16)
    low_two = ring_gather(own_low, ctx_size, ctx_index)
    mixed_weight = jnp.concatenate([router_weight, gate_vector[:, None]], axis=1)
    logits = dot(low_two, mixed_weight)
    probs_all = jax.nn.softmax(logits[:, :expert_count], axis=-1)
    scale_all = jax.nn.sigmoid(logits[:, expert_count])
    gate_all = lax.dynamic_index_in_dim(probs_all, ctx_index, 1, keepdims=False)

    named = jnp.any(route_rows == ctx_index, axis=-1)
    before = jnp.arange(token_count)[:, None] < jnp.arange(token_count)[None, :]
    rank = dot(named.astype(bf16), before.astype(bf16)).astype(i32)
    slot_of = jnp.where(named & (rank < capacity), rank, -1)
    slot_mask = slot_of[:, None, :] == jnp.arange(capacity, dtype=i32)[None, :, None]
    slot_map = slot_mask.astype(bf16)
    blocks_two = low_two.reshape(ctx_size, token_count, width)
    gate_blocks = gate_all.reshape(ctx_size, token_count)

    def to_slots(blocks):
        picked = jnp.einsum("bmt,btd->bmd", slot_map, blocks, preferred_element_type=f32)
        return picked.reshape(ctx_size * capacity, width)

    def to_tokens(slots):
        spread = jnp.einsum(
            "bmt,bmd->btd",
            slot_map,
            slots.reshape(ctx_size, capacity, width),
            preferred_element_type=f32,
        )
        return spread.reshape(seq_len, width)

    buffer = to_slots(blocks_two).astype(bf16)
    expert_pre = dot(buffer, expert_in)
    expert_hid = swiglu(expert_pre, FE).astype(bf16)
    expert_res = dot(expert_hid, expert_out).astype(bf16)
    routed = gate_all[:, None] * to_tokens(expert_res)

    shared_in, expert_res = after(shared_in, expert_res)
    shared_in = shared_in.transpose(1, 0, 2, 3).reshape(width, 2 * fs_own)
    shared_pre = dot(low_two, shared_in)
    shared_hid = swiglu(shared_pre, fs_own).astype(bf16)
    shared_res = dot(shared_hid, shared_out)
    grad_rows, shared_res = after(grad_rows, shared_res)
    out_parts = (scale_all[:, None] * shared_res + routed).astype(bf16)
    out_sum = ring_scatter(out_parts, ctx_size, ctx_index)

    grad_slots = to_slots(grad_rows.reshape(ctx_size, token_count, width))
    gate_slots = jnp.sum(jnp.where(slot_mask, gate_blocks[:, None, :], 0.0), axis=-1).reshape(-1, 1)
    grad_res = (gate_slots * grad_slots).astype(bf16)
    slot_dots = jnp.sum(grad_slots * expert_res.astype(f32), axis=-1).reshape(ctx_size, capacity, 1)
    grad_gates = jnp.sum(jnp.where(slot_mask, slot_dots, 0.0), axis=1)
    grad_expert_out = t_dot(expert_hid, grad_res)
    grad_hid = dot_t(grad_res, expert_out)
    grad_pre = swiglu_back(expert_pre, FE, grad_hid).astype(bf16)
    grad_expert_in = t_dot(buffer, grad_pre)
    grad_buffer = dot_t(grad_pre, expert_in).astype(bf16)

    grad_expert_out = grad_expert_out.astype(bf16)
    grad_expert_in, grad_shared_res = after(
        grad_expert_in.astype(bf16),
        (scale_all[:, None] * grad_rows.astype(f32)).astype(bf16),
    )
    sum_expert_in = sum_rows(grad_expert_in)

    grad_f32 = grad_rows.astype(f32)
    gate_dots = jnp.sum(grad_f32 * shared_res, axis=-1).reshape(ctx_size, token_count)
    grad_shared_out = t_dot(shared_hid, grad_shared_res)
    grad_shared_hid = dot_t(grad_shared_res, shared_out)
    grad_shared_pre = swiglu_back(shared_pre, fs_own, grad_shared_hid).astype(bf16)
    grad_shared_in = t_dot(low_two, grad_shared_pre)
    grad_shared_pre, out_sum = after(grad_shared_pre, out_sum)
    two_parts = (dot_t(grad_shared_pre, shared_in) + to_tokens(grad_buffer)).astype(bf16)
    grad_two = ring_scatter(two_parts, ctx_size, ctx_index)
    grad_two, grad_shared_in, grad_shared_out, grad_expert_out = after(
        grad_two, grad_shared_in.astype(bf16), grad_shared_out.astype(bf16), grad_expert_out
    )
    sum_expert_in, grad_shared_in, grad_shared_out = after(
        sum_expert_in, grad_shared_in, grad_shared_out
    )
    sum_shared_in = grad_shared_in.reshape(ctx_size, fsdp_size, shard, 2 * fs_own)
    sum_shared_in = lax.psum_scatter(
        sum_shared_in.transpose(1, 0, 2, 3).reshape(width, 2 * fs_own),
        "fsdp",
        scatter_dimension=0,
        tiled=True,
    ).reshape(ctx_size, shard, 2 * fs_own)
    sum_shared_out = sum_rows(grad_shared_out)
    sum_expert_in, grad_expert_out = after(sum_expert_in, grad_expert_out)
    sum_expert_out = sum_rows(grad_expert_out)
    output = (own_residual + out_sum).astype(bf16).reshape(tokens.shape)

    dots = jnp.stack([grad_gates, gate_dots], axis=1)
    dots = lax.all_to_all(dots, "ctx", split_axis=0, concat_axis=0, tiled=True)
    own_probs = own_rows(probs_all)
    own_scale = own_rows(scale_all)
    own_chosen = routes.reshape(token_count, top_count)
    chosen_mask = jnp.any(
        own_chosen[..., None] == jnp.arange(expert_count, dtype=i32), axis=1
    )
    grad_probs = jnp.where(chosen_mask, dots[:, 0].T, 0.0)
    grad_logits = (
        own_probs * (grad_probs - jnp.sum(own_probs * grad_probs, axis=-1, keepdims=True))
    ).astype(bf16)
    grad_gate_pre = (jnp.sum(dots[:, 1], axis=0) * own_scale * (1.0 - own_scale)).astype(bf16)
    grad_router = t_dot(own_low, grad_logits)
    grad_gate_vector = t_dot(own_low, grad_gate_pre[:, None])
    grad_two = grad_two + dot_t(grad_logits, router_weight)
    grad_two = grad_two + grad_gate_pre.astype(f32)[:, None] * gate_vector.astype(f32)[None, :]
    grad_resid_norm, grad_gain_two = rms_back(
        own_residual, inv_two, ffn_gain, grad_two
    )
    grad_resid = cotangent.reshape(token_count, width).astype(f32) + grad_resid_norm

    grad_mixed = grad_resid.astype(bf16)
    mixed_all = ring_gather(grad_mixed, ctx_size, ctx_index)
    grad_attn = dot_t(mixed_all, out_weight).astype(bf16).reshape(head_shape)
    grad_attn, sum_expert_in = after(grad_attn, sum_expert_in)
    grad_weights = jnp.einsum("qhd,khd->hqk", grad_attn, values, preferred_element_type=f32)
    delta = jnp.sum(weights * grad_weights, axis=-1, keepdims=True)
    grad_scores = jnp.where(allowed[None], weights * (grad_weights - delta), 0.0).astype(bf16)
    grad_q = jnp.einsum("hqk,khd->qhd", grad_scores, keys, preferred_element_type=f32) * score_scale
    grad_k = (
        jnp.einsum("hqk,qhd->khd", grad_scores, queries, preferred_element_type=f32) * score_scale
    )
    grad_v = jnp.einsum("hqk,qhd->khd", weights_low, grad_attn, preferred_element_type=f32)
    grad_projected = jnp.concatenate(
        [
            rotate_back(grad_q, cos_tab, sine_tab).reshape(seq_len, own_width),
            rotate_back(grad_k, cos_tab, sine_tab).reshape(seq_len, own_width),
            grad_v.reshape(seq_len, own_width),
        ],
        axis=-1,
    ).astype(bf16)
    one_sums = dot_t(grad_projected, qkv_weight)
    grad_gain_one = jnp.sum(one_sums * inputs * inv_one_all, axis=0)
    one_parts = one_sums.astype(bf16)
    one_kept, grad_projected = after(one_parts, grad_projected)
    one_kept, sum_shared_in, sum_shared_out, sum_expert_out = after(
        one_kept, sum_shared_in, sum_shared_out, sum_expert_out
    )
    sum_shared_in = lax.all_to_all(
        sum_shared_in, "ctx", split_axis=0, concat_axis=0, tiled=True
    )
    grad_normed = ring_scatter(one_parts, ctx_size, ctx_index, one_kept)
    grad_inputs_norm, unused = rms_back(
        own_tokens,
        own_rows(inv_one_all),
        attn_gain,
        grad_normed,
    )
    grad_tokens = (grad_resid + grad_inputs_norm).reshape(tokens.shape)
    grad_qkv_weight = t_dot(normed_low, grad_projected)
    grad_bias = jnp.sum(grad_projected.astype(f32), axis=0).reshape(3, 1, own_width)
    grad_bias = jnp.where(
        jnp.arange(ctx_size, dtype=i32)[None, :, None] == ctx_index, grad_bias, 0.0
    )

    grad_out_weight = t_dot(attn_own, mixed_all)
    small_grads = [grad_gain_one, grad_gain_two, grad_gate_vector, grad_router, grad_bias]
    small_grads = jnp.concatenate(
        [piece.reshape(device_count, -1) for piece in small_grads], axis=1
    )
    more = -(-small_size // (3 * own_width * 16)) * 16
    small_grads = jnp.pad(small_grads, ((0, 0), (0, more * 3 * own_width - small_size)))
    pieces = jnp.concatenate(
        [
            grad_qkv_weight.astype(bf16).reshape(ctx_size, fsdp_size, shard, 3 * own_width),
            small_grads.astype(bf16).reshape(ctx_size, fsdp_size, more, 3 * own_width),
        ],
        axis=2,
    )
    pieces = fsdp_scatter(pieces, fsdp_size, 1).astype(bf16)
    pieces = lax.all_to_all(pieces, "ctx", split_axis=0, concat_axis=0, tiled=True)
    small_grads = jnp.sum(pieces[:, shard:].reshape(ctx_size, -1).astype(f32), axis=0)
    return (
        output,
        grad_tokens,
        merge_columns(pieces[:, :shard], 3, ctx_size),
        small_grads[router_end:small_size],
        sum_rows(grad_out_weight).astype(f32),
        small_grads[:shard],
        small_grads[shard : 2 * shard],
        small_grads[3 * shard : router_end].reshape(shard, expert_count),
        small_grads[2 * shard : 3 * shard],
        merge_columns(sum_shared_in, 2, ctx_size),
        sum_shared_out.astype(f32),
        sum_expert_in.astype(f32)[None],
        sum_expert_out.astype(f32)[None],
    )


def local_wide(
    tokens,
    segments,
    routes,
    cotangent,
    w_qkv,
    b_qkv,
    w_out,
    gain_attn,
    gain_ffn,
    w_router,
    w_shared_gate,
    w_shared_in,
    w_shared_out,
    w_expert_in,
    w_expert_out,
):
    block_len = tokens.shape[2]
    model_width = tokens.shape[3]
    token_count = 2 * block_len
    top_count = routes.shape[3]
    half_len = segments.shape[2]
    seq_len = 2 * half_len
    ctx_index = lax.axis_index("ctx")
    head_count = model_width // HD
    expert_count = w_router.shape[1]
    capacity = token_count * top_count // expert_count
    slot_count = expert_count * capacity
    key_rows = min(512, seq_len)
    key_blocks = seq_len // key_rows
    score_scale = HD ** (-0.5)
    head_shape = (token_count, head_count, HD)
    attn_set = (
        lax.all_gather(w_qkv, ("ctx", "fsdp"), axis=0, tiled=True),
        lax.all_gather(b_qkv, ("ctx", "fsdp"), axis=0, tiled=True),
        lax.all_gather(w_out, ("ctx", "fsdp"), axis=0, tiled=True),
        lax.all_gather(gain_attn, ("ctx", "fsdp"), axis=0, tiled=True),
    )
    qkv_weight, qkv_bias, out_weight, attn_gain = attn_set
    inputs = tokens.reshape(token_count, model_width).astype(jnp.float32)
    normed, inv_one = rms_norm(inputs, attn_gain.astype(jnp.float32))
    normed_low = normed.astype(jnp.bfloat16)
    projected = jnp.dot(
        normed_low, qkv_weight, preferred_element_type=jnp.float32
    ) + qkv_bias.astype(jnp.float32)
    local_index = jnp.arange(block_len, dtype=jnp.int32)
    query_pos = jnp.concatenate(
        [ctx_index * block_len + local_index, seq_len - (ctx_index + 1) * block_len + local_index]
    )
    half_index = jnp.arange(half_len, dtype=jnp.int32)
    key_pos = jnp.concatenate(
        [half_index, seq_len - block_len * (half_index // block_len + 1) + half_index % block_len]
    ).reshape(key_blocks, key_rows)
    key_seg = segments.reshape(key_blocks, key_rows)
    query_seg = lax.dynamic_slice_in_dim(segments[0], ctx_index * block_len, block_len, 1).reshape(
        token_count
    )
    cos_tab, sine_tab = rope_tables(query_pos, HD)
    queries = rotate(projected[:, :model_width].reshape(head_shape), cos_tab, sine_tab).astype(
        jnp.bfloat16
    )
    keys_own = rotate(
        projected[:, model_width : 2 * model_width].reshape(head_shape), cos_tab, sine_tab
    ).astype(jnp.bfloat16)
    values_own = projected[:, 2 * model_width :].astype(jnp.bfloat16)
    keys_all, values_all = (
        lax.all_gather(keys_own.reshape(2, block_len, model_width), "ctx", axis=1, tiled=True),
        lax.all_gather(values_own.reshape(2, block_len, model_width), "ctx", axis=1, tiled=True),
    )
    keys_all = keys_all.reshape(key_blocks, key_rows, head_count, HD)
    values_all = values_all.reshape(key_blocks, key_rows, head_count, HD)

    def score_block(key_blk, pos_blk, seg_blk):
        raw_scores = (
            jnp.einsum("qhd,khd->hqk", queries, key_blk, preferred_element_type=jnp.float32)
            * score_scale
        )
        allowed = (pos_blk[None, :] <= query_pos[:, None]) & (
            seg_blk[None, :] == query_seg[:, None]
        )
        return (jnp.where(allowed[None], raw_scores, MASK_FILL), allowed)

    def total_step(running, key_part):
        run_max, run_sum = running
        scores = score_block(key_part[0], key_part[1], key_part[2])[0]
        new_max = jnp.maximum(run_max, jnp.max(scores, axis=-1))
        run_sum = run_sum * jnp.exp(run_max - new_max) + jnp.sum(
            jnp.exp(scores - new_max[..., None]), axis=-1
        )
        return ((new_max, run_sum), None)

    start_max = jnp.full((head_count, token_count), MASK_FILL, jnp.float32)
    start_sum = jnp.zeros((head_count, token_count), jnp.float32)
    (run_max, run_sum), unused = lax.scan(
        total_step, (start_max, start_sum), (keys_all, key_pos, key_seg)
    )
    log_total = run_max + jnp.log(run_sum)

    def attend_step(summed, key_part):
        key_blk, value_blk, pos_blk, seg_blk = key_part
        scores = score_block(key_blk, pos_blk, seg_blk)[0]
        weights = jnp.exp(scores - log_total[..., None]).astype(jnp.bfloat16)
        return (
            summed
            + jnp.einsum("hqk,khd->qhd", weights, value_blk, preferred_element_type=jnp.float32),
            None,
        )

    key_stack = (keys_all, values_all, key_pos, key_seg)
    attended, unused = lax.scan(attend_step, jnp.zeros(head_shape, jnp.float32), key_stack)
    attn_low = attended.reshape(token_count, model_width).astype(jnp.bfloat16)
    residual = inputs + jnp.dot(attn_low, out_weight, preferred_element_type=jnp.float32)
    ffn_set = (
        lax.all_gather(gain_ffn, ("ctx", "fsdp"), axis=0, tiled=True),
        lax.all_gather(w_router, ("ctx", "fsdp"), axis=0, tiled=True),
        lax.all_gather(w_shared_gate, ("ctx", "fsdp"), axis=0, tiled=True),
        lax.all_gather(w_shared_in, ("ctx", "fsdp"), axis=0, tiled=True),
        lax.all_gather(w_shared_out, ("ctx", "fsdp"), axis=0, tiled=True),
    )
    ffn_gain, router_weight, gate_vector, shared_in, shared_out = ffn_set
    normed_two, inv_two = rms_norm(residual, ffn_gain.astype(jnp.float32))
    low_two = normed_two.astype(jnp.bfloat16)
    logits = jnp.dot(low_two, router_weight, preferred_element_type=jnp.float32)
    router_probs = jax.nn.softmax(logits, axis=-1)
    chosen = routes.reshape(token_count, top_count)
    chosen_mask = chosen[..., None] == jnp.arange(expert_count, dtype=jnp.int32)
    gate_vals = jnp.sum(jnp.where(chosen_mask, router_probs[:, None, :], 0.0), axis=-1)
    shared_scale = jax.nn.sigmoid(jnp.dot(low_two, gate_vector, preferred_element_type=jnp.float32))
    shared_pre = jnp.dot(low_two, shared_in, preferred_element_type=jnp.float32)
    shared_hid = swiglu(shared_pre, FS).astype(jnp.bfloat16)
    shared_res = jnp.dot(shared_hid, shared_out, preferred_element_type=jnp.float32)
    pair_routes = chosen.reshape(token_count * top_count)
    expert_marks = (
        pair_routes[:, None] == jnp.arange(expert_count, dtype=jnp.int32)[None, :]
    ).astype(jnp.int32)
    pair_ranks = jnp.sum((jnp.cumsum(expert_marks, axis=0) - expert_marks) * expert_marks, axis=1)
    pair_target = jnp.where(pair_ranks < capacity, pair_routes * capacity + pair_ranks, -1)
    pair_map = pair_target[:, None] == jnp.arange(slot_count, dtype=jnp.int32)[None, :]
    pair_low = pair_map.astype(jnp.bfloat16)
    token_map = jnp.sum(
        pair_map.reshape(token_count, top_count, slot_count).astype(jnp.int32), axis=1
    ).astype(jnp.bfloat16)
    outgoing = jnp.einsum(
        "tc,td->cd", token_map, low_two, preferred_element_type=jnp.float32
    ).astype(jnp.bfloat16)
    incoming = lax.all_to_all(
        outgoing.reshape(expert_count, capacity, model_width),
        "ctx",
        split_axis=0,
        concat_axis=1,
        tiled=True,
    )
    expert_in, expert_out = (
        lax.all_gather(w_expert_in, "fsdp", axis=1, tiled=True),
        lax.all_gather(w_expert_out, "fsdp", axis=1, tiled=True),
    )
    expert_pre = jnp.einsum("erd,edf->erf", incoming, expert_in, preferred_element_type=jnp.float32)
    expert_hid = swiglu(expert_pre, FE).astype(jnp.bfloat16)
    expert_res = jnp.einsum(
        "erf,efd->erd", expert_hid, expert_out, preferred_element_type=jnp.float32
    ).astype(jnp.bfloat16)
    returned = lax.all_to_all(expert_res, "ctx", split_axis=1, concat_axis=0, tiled=True).reshape(
        slot_count, model_width
    )
    pair_vals = jnp.dot(pair_low, returned, preferred_element_type=jnp.float32).reshape(
        token_count, top_count, model_width
    )
    routed = jnp.sum(gate_vals[..., None] * pair_vals, axis=1)
    output = (
        (residual + shared_scale[:, None] * shared_res + routed)
        .astype(jnp.bfloat16)
        .reshape(tokens.shape)
    )
    grad_out = cotangent.reshape(token_count, model_width).astype(jnp.float32)
    pair_grads = gate_vals[..., None] * grad_out[:, None, :]
    grad_gates = jnp.sum(grad_out[:, None, :] * pair_vals, axis=-1)
    grad_returned = jnp.einsum(
        "pc,pd->cd",
        pair_map.astype(jnp.float32),
        pair_grads.reshape(token_count * top_count, model_width),
        precision=HIGHEST,
    ).astype(jnp.bfloat16)
    grad_res = lax.all_to_all(
        grad_returned.reshape(expert_count, capacity, model_width),
        "ctx",
        split_axis=0,
        concat_axis=1,
        tiled=True,
    )
    grad_expert_out = jnp.einsum(
        "erf,erd->efd", expert_hid, grad_res, preferred_element_type=jnp.float32
    )
    grad_hid = jnp.einsum("erd,efd->erf", grad_res, expert_out, preferred_element_type=jnp.float32)
    grad_pre = swiglu_back(expert_pre, FE, grad_hid).astype(jnp.bfloat16)
    grad_expert_in = jnp.einsum(
        "erd,erf->edf", incoming, grad_pre, preferred_element_type=jnp.float32
    )
    grad_incoming = jnp.einsum(
        "erf,edf->erd", grad_pre, expert_in, preferred_element_type=jnp.float32
    ).astype(jnp.bfloat16)
    grad_outgoing = lax.all_to_all(
        grad_incoming, "ctx", split_axis=1, concat_axis=0, tiled=True
    ).reshape(slot_count, model_width)
    expert_grads = (
        lax.psum_scatter(
            grad_expert_in.astype(jnp.bfloat16), "fsdp", scatter_dimension=1, tiled=True
        ).astype(jnp.float32),
        lax.psum_scatter(
            grad_expert_out.astype(jnp.bfloat16), "fsdp", scatter_dimension=1, tiled=True
        ).astype(jnp.float32),
    )
    grad_two = jnp.einsum("tc,cd->td", token_map, grad_outgoing, preferred_element_type=jnp.float32)
    grad_probs = jnp.sum(jnp.where(chosen_mask, grad_gates[..., None], 0.0), axis=1)
    grad_logits = (
        router_probs * (grad_probs - jnp.sum(router_probs * grad_probs, axis=-1, keepdims=True))
    ).astype(jnp.bfloat16)
    grad_router = jnp.einsum("td,te->de", low_two, grad_logits, preferred_element_type=jnp.float32)
    grad_shared_res = (shared_scale[:, None] * grad_out).astype(jnp.bfloat16)
    grad_gate_pre = (
        jnp.sum(grad_out * shared_res, axis=-1) * shared_scale * (1.0 - shared_scale)
    ).astype(jnp.bfloat16)
    grad_shared_out = jnp.einsum(
        "tf,td->fd", shared_hid, grad_shared_res, preferred_element_type=jnp.float32
    )
    grad_shared_hid = jnp.einsum(
        "td,fd->tf", grad_shared_res, shared_out, preferred_element_type=jnp.float32
    )
    grad_shared_pre = swiglu_back(shared_pre, FS, grad_shared_hid).astype(jnp.bfloat16)
    grad_shared_in = jnp.einsum(
        "td,tf->df", low_two, grad_shared_pre, preferred_element_type=jnp.float32
    )
    grad_gate_vector = jnp.einsum(
        "td,t->d", low_two, grad_gate_pre, preferred_element_type=jnp.float32
    )
    grad_two = grad_two + jnp.einsum(
        "te,de->td", grad_logits, router_weight, preferred_element_type=jnp.float32
    )
    grad_two = grad_two + jnp.einsum(
        "tf,df->td", grad_shared_pre, shared_in, preferred_element_type=jnp.float32
    )
    grad_two = (
        grad_two
        + grad_gate_pre.astype(jnp.float32)[:, None] * gate_vector.astype(jnp.float32)[None, :]
    )
    grad_resid_norm, grad_gain_two = rms_back(
        residual, inv_two, ffn_gain.astype(jnp.float32), grad_two
    )
    grad_resid = grad_out + grad_resid_norm
    ffn_grads = (
        lax.psum_scatter(grad_gain_two, ("ctx", "fsdp"), scatter_dimension=0, tiled=True),
        lax.psum_scatter(grad_router, ("ctx", "fsdp"), scatter_dimension=0, tiled=True),
        lax.psum_scatter(grad_gate_vector, ("ctx", "fsdp"), scatter_dimension=0, tiled=True),
        lax.psum_scatter(grad_shared_in, ("ctx", "fsdp"), scatter_dimension=0, tiled=True),
        lax.psum_scatter(grad_shared_out, ("ctx", "fsdp"), scatter_dimension=0, tiled=True),
    )
    grad_mixed = grad_resid.astype(jnp.bfloat16)
    grad_out_weight = jnp.einsum(
        "tc,td->cd", attn_low, grad_mixed, preferred_element_type=jnp.float32
    )
    grad_attn = (
        jnp.einsum("td,cd->tc", grad_mixed, out_weight, preferred_element_type=jnp.float32)
        .astype(jnp.bfloat16)
        .reshape(head_shape)
    )

    def delta_step(summed, key_part):
        key_blk, value_blk, pos_blk, seg_blk = key_part
        weights = jnp.exp(score_block(key_blk, pos_blk, seg_blk)[0] - log_total[..., None])
        grad_weights = jnp.einsum(
            "qhd,khd->hqk", grad_attn, value_blk, preferred_element_type=jnp.float32
        )
        return (summed + jnp.sum(weights * grad_weights, axis=-1), None)

    delta_sum, unused = lax.scan(
        delta_step, jnp.zeros((head_count, token_count), jnp.float32), key_stack
    )

    def grad_step(summed, key_part):
        key_blk, value_blk, pos_blk, seg_blk = key_part
        scores, allowed = score_block(key_blk, pos_blk, seg_blk)
        weights = jnp.exp(scores - log_total[..., None])
        grad_weights = jnp.einsum(
            "qhd,khd->hqk", grad_attn, value_blk, preferred_element_type=jnp.float32
        )
        grad_scores = jnp.where(
            allowed[None], weights * (grad_weights - delta_sum[..., None]), 0.0
        ).astype(jnp.bfloat16)
        summed = (
            summed
            + jnp.einsum("hqk,khd->qhd", grad_scores, key_blk, preferred_element_type=jnp.float32)
            * score_scale
        )
        grad_key = (
            jnp.einsum("hqk,qhd->khd", grad_scores, queries, preferred_element_type=jnp.float32)
            * score_scale
        )
        grad_value = jnp.einsum(
            "hqk,qhd->khd",
            weights.astype(jnp.bfloat16),
            grad_attn,
            preferred_element_type=jnp.float32,
        )
        return (summed, (grad_key, grad_value))

    grad_query, (grad_keys, grad_values) = lax.scan(
        grad_step, jnp.zeros(head_shape, jnp.float32), key_stack
    )
    grad_keys_own, grad_values_own = (
        lax.psum_scatter(
            grad_keys.reshape(2, half_len, model_width).astype(jnp.bfloat16),
            "ctx",
            scatter_dimension=1,
            tiled=True,
        ).astype(jnp.float32),
        lax.psum_scatter(
            grad_values.reshape(2, half_len, model_width).astype(jnp.bfloat16),
            "ctx",
            scatter_dimension=1,
            tiled=True,
        ).astype(jnp.float32),
    )
    grad_q_rows = rotate_back(grad_query, cos_tab, sine_tab).reshape(token_count, model_width)
    grad_k_rows = rotate_back(grad_keys_own.reshape(head_shape), cos_tab, sine_tab).reshape(
        token_count, model_width
    )
    grad_projected = jnp.concatenate(
        [grad_q_rows, grad_k_rows, grad_values_own.reshape(token_count, model_width)], axis=-1
    ).astype(jnp.bfloat16)
    grad_qkv_weight = jnp.einsum(
        "td,te->de", normed_low, grad_projected, preferred_element_type=jnp.float32
    )
    grad_qkv_bias = jnp.sum(grad_projected.astype(jnp.float32), axis=0)
    grad_normed = jnp.einsum(
        "te,de->td", grad_projected, qkv_weight, preferred_element_type=jnp.float32
    )
    grad_inputs_norm, grad_gain_one = rms_back(
        inputs, inv_one, attn_gain.astype(jnp.float32), grad_normed
    )
    grad_tokens = (grad_resid + grad_inputs_norm).reshape(tokens.shape)
    attn_grads = (
        lax.psum_scatter(grad_qkv_weight, ("ctx", "fsdp"), scatter_dimension=0, tiled=True),
        lax.psum_scatter(grad_qkv_bias, ("ctx", "fsdp"), scatter_dimension=0, tiled=True),
        lax.psum_scatter(grad_out_weight, ("ctx", "fsdp"), scatter_dimension=0, tiled=True),
        lax.psum_scatter(grad_gain_one, ("ctx", "fsdp"), scatter_dimension=0, tiled=True),
    )
    return (
        output,
        grad_tokens,
        attn_grads[0],
        attn_grads[1],
        attn_grads[2],
        attn_grads[3],
        ffn_grads[0],
        ffn_grads[1],
        ffn_grads[2],
        ffn_grads[3],
        ffn_grads[4],
        expert_grads[0],
        expert_grads[1],
    )


def solution(mesh):
    in_specs = (
        P("fsdp", None, "ctx", None),
        P("fsdp", None, None),
        P("fsdp", None, "ctx", None),
        P("fsdp", None, "ctx", None),
        P(("ctx", "fsdp"), None),
        P(("ctx", "fsdp")),
        P(("ctx", "fsdp"), None),
        P(("ctx", "fsdp")),
        P(("ctx", "fsdp")),
        P(("ctx", "fsdp"), None),
        P(("ctx", "fsdp")),
        P(("ctx", "fsdp"), None),
        P(("ctx", "fsdp"), None),
        P("ctx", "fsdp", None),
        P("ctx", "fsdp", None),
    )
    out_specs = (
        P("fsdp", None, "ctx", None),
        P("fsdp", None, "ctx", None),
        P(("ctx", "fsdp"), None),
        P(("ctx", "fsdp")),
        P(("ctx", "fsdp"), None),
        P(("ctx", "fsdp")),
        P(("ctx", "fsdp")),
        P(("ctx", "fsdp"), None),
        P(("ctx", "fsdp")),
        P(("ctx", "fsdp"), None),
        P(("ctx", "fsdp"), None),
        P("ctx", "fsdp", None),
        P("ctx", "fsdp", None),
    )
    ctx_size = mesh.shape["ctx"]
    fsdp_size = mesh.shape["fsdp"]

    def local(*arrays):
        if HEADS % ctx_size:
            return local_wide(*arrays)
        return local_split(ctx_size, fsdp_size, *arrays)

    return jax.shard_map(local, mesh=mesh, in_specs=in_specs, out_specs=out_specs, check_vma=False)
```

```python
import jax
import jax.numpy as jnp
from jax import lax
from jax.sharding import PartitionSpec as P

HD = 128
HEADS = 16
FS = 5632
FE = 1408


RMS_EPS = 1e-06
ROPE_THETA = 1000000.0
MASK_FILL = -1e30
HIGHEST = lax.Precision.HIGHEST


def rope_tables(positions, head_dim):
    half_dim = head_dim // 2
    inv_freq = ROPE_THETA ** (-(jnp.arange(half_dim, dtype=jnp.float32) * 2.0 / head_dim))
    angles = positions.astype(jnp.float32)[:, None] * inv_freq[None, :]
    cos_tab = jnp.concatenate([jnp.cos(angles), jnp.cos(angles)], axis=-1)
    sine_tab = jnp.concatenate([jnp.sin(angles), jnp.sin(angles)], axis=-1)
    return (cos_tab, sine_tab)


def rotate(values, cos_tab, sine_tab):
    half_dim = values.shape[-1] // 2
    turned = jnp.concatenate([-values[..., half_dim:], values[..., :half_dim]], axis=-1)
    return values * cos_tab[:, None, :] + turned * sine_tab[:, None, :]


def rotate_back(upstream, cos_tab, sine_tab):
    half_dim = upstream.shape[-1] // 2
    scaled = upstream * sine_tab[:, None, :]
    return upstream * cos_tab[:, None, :] + jnp.concatenate(
        [scaled[..., half_dim:], -scaled[..., :half_dim]], axis=-1
    )


def rms_norm(values, gain_vec):
    inv_rms = lax.rsqrt(jnp.mean(values * values, axis=-1, keepdims=True) + RMS_EPS)
    return (values * inv_rms * gain_vec, inv_rms)


def rms_back(values, inv_rms, gain_vec, upstream):
    weighted = upstream * gain_vec
    inner_mean = jnp.mean(weighted * values, axis=-1, keepdims=True)
    return (
        inv_rms * weighted - values * inv_rms * inv_rms * inv_rms * inner_mean,
        jnp.sum(upstream * values * inv_rms, axis=0),
    )


def swiglu(pre_act, split_at):
    return jax.nn.silu(pre_act[..., :split_at]) * pre_act[..., split_at:]


def swiglu_back(pre_act, split_at, upstream):
    gate_part = pre_act[..., :split_at]
    up_part = pre_act[..., split_at:]
    sigmoid_g = jax.nn.sigmoid(gate_part)
    d_gate = upstream * up_part * sigmoid_g * (1.0 + gate_part * (1.0 - sigmoid_g))
    d_up = upstream * gate_part * sigmoid_g
    return jnp.concatenate([d_gate, d_up], axis=-1)


def ring_order(size):
    return list(range(0, size, 2)) + list(range(size - 1, 0, -2))


def ring_steps(size):
    order = ring_order(size)
    ahead = [(order[i], order[(i + 1) % size]) for i in range(size)]
    back = [(dst, src) for src, dst in ahead]
    return (ahead, back)


def ring_peers(size, ctx_index):
    order = ring_order(size)
    place = {dev: i for i, dev in enumerate(order)}
    table = jnp.array(
        [[order[(place[dev] + k) % size] for k in range(size)] for dev in range(size)], jnp.int32
    )
    row = lax.dynamic_index_in_dim(table, ctx_index, 0, keepdims=False)
    return [row[k] for k in range(size)]


def ring_walk(block, size, ctx_index, out, put):
    rows = block.shape[0]
    ahead, back = ring_steps(size)
    peers = ring_peers(size, ctx_index)
    half = size // 2
    out = put(out, block, ctx_index, 0)
    fore = rear = block
    for k in range(1, half):
        fore = lax.ppermute(fore, "ctx", ahead)
        rear = lax.ppermute(rear, "ctx", back)
        out = put(out, fore, peers[size - k], 0)
        out = put(out, rear, peers[k], 0)
    fore = lax.ppermute(fore[: rows // 2], "ctx", ahead)
    rear = lax.ppermute(rear[rows // 2 :], "ctx", back)
    out = put(out, fore, peers[half], 0)
    return put(out, rear, peers[half], rows // 2)


def ring_gather(block, size, ctx_index):
    rows, width = block.shape

    def put(out, piece, peer, offset):
        return lax.dynamic_update_slice(out, piece, (peer * rows + offset, jnp.zeros_like(peer)))

    return ring_walk(block, size, ctx_index, jnp.zeros((size * rows, width), block.dtype), put)


def ring_sums(parts, size, ctx_index):
    f32 = jnp.float32
    rows = parts.shape[0] // size
    ahead, back = ring_steps(size)
    peers = ring_peers(size, ctx_index)
    half = size // 2

    def own(k, start, count):
        first = (peers[k % size] * rows + start, jnp.zeros_like(peers[0]))
        return lax.dynamic_slice(parts, first, (count, parts.shape[1])).astype(f32)

    def low(values):
        return values.astype(jnp.bfloat16)

    cut = rows // 2
    fore = lax.ppermute(low(own(half, 0, cut)), "ctx", ahead)
    rear = lax.ppermute(low(own(half, cut, cut)), "ctx", back)
    fore = jnp.concatenate(
        [low(fore.astype(f32) + own(half - 1, 0, cut)), low(own(half - 1, cut, cut))], axis=0
    )
    rear = jnp.concatenate(
        [low(own(1 - half, 0, cut)), low(rear.astype(f32) + own(1 - half, cut, cut))], axis=0
    )
    for k in range(half - 1, 0, -1):
        fore = lax.ppermute(fore, "ctx", ahead)
        rear = lax.ppermute(rear, "ctx", back)
        if k > 1:
            fore = low(fore.astype(f32) + own(k - 1, 0, rows))
            rear = low(rear.astype(f32) + own(1 - k, 0, rows))
    return (fore, rear)


def ring_scatter(parts, size, ctx_index, kept=None):
    fore, rear = ring_sums(parts, size, ctx_index)
    kept = (parts if kept is None else kept).reshape(size, -1, parts.shape[1])
    kept = lax.dynamic_index_in_dim(kept, ctx_index, 0, keepdims=False)
    return kept.astype(jnp.float32) + fore.astype(jnp.float32) + rear.astype(jnp.float32)


def other_core(size):
    return [(i, i ^ 1) for i in range(size)]


def other_chip(size):
    return [(i, i ^ 2) for i in range(size)]


def after(value, *deps):
    return lax.optimization_barrier((value,) + deps)


def fsdp_gather(shard, size, hold):
    index = lax.axis_index("fsdp")
    rows, width = shard.shape
    far = lax.ppermute(shard, "fsdp", other_chip(size))
    far, hold = after(far, hold)
    pair = jnp.where(
        index < 2, jnp.stack([shard, far], axis=0), jnp.stack([far, shard], axis=0)
    )
    near = lax.ppermute(pair, "fsdp", other_core(size))
    out = jnp.zeros((2, 2, rows, width), shard.dtype)
    out = lax.dynamic_update_index_in_dim(out, pair, index % 2, 1)
    out = lax.dynamic_update_index_in_dim(out, near, 1 - index % 2, 1)
    return (out.reshape(size * rows, width), hold)


def column_pieces(weight, groups, size, extra):
    rows = weight.shape[0]
    width = weight.shape[1] // (groups * size)
    pieces = weight.reshape(rows, groups, size, width).transpose(2, 0, 1, 3)
    pieces = pieces.reshape(size, rows, groups * width)
    if extra is not None:
        count = extra.shape[0]
        more = -(-count // (groups * width * 16)) * 16
        extra = jnp.pad(extra, (0, more * groups * width - count))
        extra = jnp.broadcast_to(
            extra.reshape(1, more, groups * width), (size, more, groups * width)
        )
        pieces = jnp.concatenate([pieces, extra], axis=1)
    return lax.all_to_all(pieces, "ctx", split_axis=0, concat_axis=0, tiled=True)


def merge_columns(pieces, groups, size):
    width = pieces.shape[2] // groups
    columns = [
        pieces[peer, :, group * width : (group + 1) * width]
        for group in range(groups)
        for peer in range(size)
    ]
    return jnp.concatenate(columns, axis=1).astype(jnp.float32)


def local_split(
    ctx_size,
    fsdp_size,
    tokens,
    segments,
    routes,
    cotangent,
    w_qkv,
    b_qkv,
    w_out,
    gain_attn,
    gain_ffn,
    w_router,
    w_shared_gate,
    w_shared_in,
    w_shared_out,
    w_expert_in,
    w_expert_out,
):
    bf16, f32, i32 = jnp.bfloat16, jnp.float32, jnp.int32
    device_count = ctx_size * fsdp_size
    block_len = tokens.shape[2]
    width = tokens.shape[3]
    token_count = 2 * block_len
    top_count = routes.shape[3]
    seq_len = token_count * ctx_size
    ctx_index = lax.axis_index("ctx")
    expert_count = w_router.shape[1]
    capacity = token_count * top_count // expert_count
    own_heads = HEADS // ctx_size
    own_width = own_heads * HD
    fs_own = FS // ctx_size
    score_scale = HD ** (-0.5)

    def dot(a, b):
        return jnp.dot(a, b, preferred_element_type=f32)

    def dot_t(a, b):
        return lax.dot_general(a, b, (((1,), (1,)), ((), ())), preferred_element_type=f32)

    def t_dot(a, b):
        return lax.dot_general(a, b, (((0,), (0,)), ((), ())), preferred_element_type=f32)

    def own_rows(values):
        return lax.dynamic_index_in_dim(
            values.reshape((ctx_size, token_count) + values.shape[1:]), ctx_index, 0, keepdims=False
        )

    def sum_rows(grad):
        return lax.psum_scatter(grad.astype(bf16), "fsdp", scatter_dimension=0, tiled=True)

    shard = width // device_count
    small = [gain_attn, gain_ffn, w_shared_gate, w_router.reshape(-1), b_qkv]
    small_size = sum(piece.shape[0] for piece in small)
    small = jnp.concatenate(small + [routes.astype(bf16).reshape(-1)], axis=0)
    small_count = small.shape[0]
    token_rows = ring_gather(tokens.reshape(token_count, width), ctx_size, ctx_index)
    expert_out = lax.all_gather(w_expert_out[0], "fsdp", axis=0, tiled=True)
    pieces = column_pieces(w_qkv, 3, ctx_size, small)
    pieces, expert_out = after(pieces, expert_out)
    pieces = lax.all_gather(pieces, "fsdp", axis=0, tiled=False).transpose(1, 0, 2, 3)
    qkv_weight = pieces[:, :, :shard].reshape(width, 3 * own_width)
    small = pieces[:, :, shard:].reshape(device_count, -1)[:, :small_count]
    attn_gain = small[:, :shard].reshape(width).astype(f32)
    ffn_gain = small[:, shard : 2 * shard].reshape(width).astype(f32)
    gate_vector = small[:, 2 * shard : 3 * shard].reshape(width)
    router_end = 3 * shard + shard * expert_count
    router_weight = small[:, 3 * shard : router_end].reshape(width, expert_count)
    bias = small[:, router_end:small_size].reshape(3, ctx_size, own_width).astype(f32)
    bias = lax.dynamic_index_in_dim(bias, ctx_index, 1, keepdims=False).reshape(3 * own_width)
    route_rows = small[:, small_size:].astype(i32)
    route_rows = lax.dynamic_index_in_dim(
        route_rows.reshape(ctx_size, fsdp_size, -1), lax.axis_index("fsdp"), 1, keepdims=False
    ).reshape(ctx_size, token_count, top_count)

    expert_in = lax.all_gather(w_expert_in[0], "fsdp", axis=0, tiled=True)
    grad_rows = lax.all_gather(
        cotangent.reshape(token_count, width), "ctx", axis=0, tiled=True
    )

    block_ids = jnp.arange(ctx_size, dtype=i32)[:, None]
    local_index = jnp.arange(block_len, dtype=i32)[None, :]
    positions = jnp.stack(
        [
            block_ids * block_len + local_index,
            seq_len - (block_ids + 1) * block_len + local_index,
        ],
        axis=1,
    ).reshape(seq_len)
    seg_rows = (
        segments.reshape(2, ctx_size, block_len).transpose(1, 0, 2).reshape(seq_len)
    )
    cos_tab, sine_tab = rope_tables(positions, HD)

    inputs = token_rows.astype(f32)
    normed, inv_one_all = rms_norm(inputs, attn_gain)
    normed_low = normed.astype(bf16)
    projected = dot(normed_low, qkv_weight) + bias
    head_shape = (seq_len, own_heads, HD)
    queries = rotate(projected[:, :own_width].reshape(head_shape), cos_tab, sine_tab).astype(bf16)
    keys = rotate(
        projected[:, own_width : 2 * own_width].reshape(head_shape), cos_tab, sine_tab
    ).astype(bf16)
    values = projected[:, 2 * own_width :].reshape(head_shape).astype(bf16)
    queries, in_shard = after(queries, w_shared_in)
    shared_in = column_pieces(in_shard, 2, ctx_size, None)
    out_weight, queries = fsdp_gather(w_out, fsdp_size, queries)
    allowed = (positions[None, :] <= positions[:, None]) & (seg_rows[None, :] == seg_rows[:, None])
    scores = jnp.einsum("qhd,khd->hqk", queries, keys, preferred_element_type=f32) * score_scale
    scores = jnp.where(allowed[None], scores, MASK_FILL)
    top_score = jnp.max(scores, axis=-1, keepdims=True)
    log_total = top_score + jnp.log(jnp.sum(jnp.exp(scores - top_score), axis=-1, keepdims=True))
    weights = jnp.exp(scores - log_total)
    weights_low = weights.astype(bf16)
    attended = jnp.einsum("hqk,khd->qhd", weights_low, values, preferred_element_type=f32)
    attn_own = attended.astype(bf16).reshape(seq_len, own_width)
    shared_in, attn_own = after(shared_in, attn_own)
    shared_in = lax.all_gather(shared_in, "fsdp", axis=0, tiled=False)
    shared_out, attn_own = fsdp_gather(w_shared_out, fsdp_size, attn_own)
    attn_parts = dot(attn_own, out_weight).astype(bf16)
    own_tokens = tokens.reshape(token_count, width).astype(f32)
    own_residual = own_tokens + ring_scatter(attn_parts, ctx_size, ctx_index)

    normed_two, inv_two = rms_norm(own_residual, ffn_gain)
    own_low = normed_two.astype(bf16)
    low_two = ring_gather(own_low, ctx_size, ctx_index)
    mixed_weight = jnp.concatenate([router_weight, gate_vector[:, None]], axis=1)
    logits = dot(low_two, mixed_weight)
    probs_all = jax.nn.softmax(logits[:, :expert_count], axis=-1)
    scale_all = jax.nn.sigmoid(logits[:, expert_count])
    gate_all = lax.dynamic_index_in_dim(probs_all, ctx_index, 1, keepdims=False)

    named = jnp.any(route_rows == ctx_index, axis=-1)
    before = jnp.arange(token_count)[:, None] < jnp.arange(token_count)[None, :]
    rank = dot(named.astype(bf16), before.astype(bf16)).astype(i32)
    slot_of = jnp.where(named & (rank < capacity), rank, -1)
    slot_mask = slot_of[:, None, :] == jnp.arange(capacity, dtype=i32)[None, :, None]
    slot_map = slot_mask.astype(bf16)
    blocks_two = low_two.reshape(ctx_size, token_count, width)
    gate_blocks = gate_all.reshape(ctx_size, token_count)

    def to_slots(blocks):
        picked = jnp.einsum("bmt,btd->bmd", slot_map, blocks, preferred_element_type=f32)
        return picked.reshape(ctx_size * capacity, width)

    def to_tokens(slots):
        spread = jnp.einsum(
            "bmt,bmd->btd",
            slot_map,
            slots.reshape(ctx_size, capacity, width),
            preferred_element_type=f32,
        )
        return spread.reshape(seq_len, width)

    buffer = to_slots(blocks_two).astype(bf16)
    buffer, grad_rows = after(buffer, grad_rows)
    expert_pre = dot(buffer, expert_in)
    expert_hid = swiglu(expert_pre, FE).astype(bf16)
    expert_res = dot(expert_hid, expert_out).astype(bf16)
    routed = gate_all[:, None] * to_tokens(expert_res)

    shared_in, expert_res = after(shared_in, expert_res)
    shared_in = shared_in.transpose(1, 0, 2, 3).reshape(width, 2 * fs_own)
    shared_pre = dot(low_two, shared_in)
    shared_hid = swiglu(shared_pre, fs_own).astype(bf16)
    shared_res = dot(shared_hid, shared_out)
    grad_rows, shared_res = after(grad_rows, shared_res)
    out_parts = (scale_all[:, None] * shared_res + routed).astype(bf16)
    out_sum = ring_scatter(out_parts, ctx_size, ctx_index)

    grad_slots = to_slots(grad_rows.reshape(ctx_size, token_count, width))
    gate_slots = jnp.sum(jnp.where(slot_mask, gate_blocks[:, None, :], 0.0), axis=-1).reshape(-1, 1)
    grad_res = (gate_slots * grad_slots).astype(bf16)
    slot_dots = jnp.sum(grad_slots * expert_res.astype(f32), axis=-1).reshape(ctx_size, capacity, 1)
    grad_gates = jnp.sum(jnp.where(slot_mask, slot_dots, 0.0), axis=1)
    grad_expert_out = t_dot(expert_hid, grad_res)
    grad_hid = dot_t(grad_res, expert_out)
    grad_pre = swiglu_back(expert_pre, FE, grad_hid).astype(bf16)
    grad_expert_in = t_dot(buffer, grad_pre)
    grad_buffer = dot_t(grad_pre, expert_in).astype(bf16)

    grad_expert_out = grad_expert_out.astype(bf16)
    grad_expert_in, grad_shared_res = after(
        grad_expert_in.astype(bf16),
        (scale_all[:, None] * grad_rows.astype(f32)).astype(bf16),
    )
    sum_expert_in = sum_rows(grad_expert_in)

    grad_f32 = grad_rows.astype(f32)
    gate_dots = jnp.sum(grad_f32 * shared_res, axis=-1).reshape(ctx_size, token_count)
    grad_shared_out = t_dot(shared_hid, grad_shared_res)
    grad_shared_hid = dot_t(grad_shared_res, shared_out)
    grad_shared_pre = swiglu_back(shared_pre, fs_own, grad_shared_hid).astype(bf16)
    grad_shared_in = t_dot(low_two, grad_shared_pre)
    grad_shared_pre, out_sum = after(grad_shared_pre, out_sum)
    two_parts = (dot_t(grad_shared_pre, shared_in) + to_tokens(grad_buffer)).astype(bf16)
    grad_two = ring_scatter(two_parts, ctx_size, ctx_index)
    grad_two, grad_shared_in, grad_shared_out, grad_expert_out = after(
        grad_two, grad_shared_in.astype(bf16), grad_shared_out.astype(bf16), grad_expert_out
    )
    sum_shared_in = grad_shared_in.reshape(ctx_size, fsdp_size, shard, 2 * fs_own)
    sum_shared_in = lax.psum_scatter(
        sum_shared_in.transpose(1, 0, 2, 3).reshape(width, 2 * fs_own),
        "fsdp",
        scatter_dimension=0,
        tiled=True,
    ).reshape(ctx_size, shard, 2 * fs_own)
    sum_shared_out = sum_rows(grad_shared_out)
    sum_expert_out = sum_rows(grad_expert_out)
    output = (own_residual + out_sum).astype(bf16).reshape(tokens.shape)

    dots = jnp.stack([grad_gates, gate_dots], axis=1)
    dots = lax.all_to_all(dots, "ctx", split_axis=0, concat_axis=0, tiled=True)
    own_probs = own_rows(probs_all)
    own_scale = own_rows(scale_all)
    own_chosen = routes.reshape(token_count, top_count)
    chosen_mask = jnp.any(
        own_chosen[..., None] == jnp.arange(expert_count, dtype=i32), axis=1
    )
    grad_probs = jnp.where(chosen_mask, dots[:, 0].T, 0.0)
    grad_logits = (
        own_probs * (grad_probs - jnp.sum(own_probs * grad_probs, axis=-1, keepdims=True))
    ).astype(bf16)
    grad_gate_pre = (jnp.sum(dots[:, 1], axis=0) * own_scale * (1.0 - own_scale)).astype(bf16)
    grad_router = t_dot(own_low, grad_logits)
    grad_gate_vector = t_dot(own_low, grad_gate_pre[:, None])
    grad_two = grad_two + dot_t(grad_logits, router_weight)
    grad_two = grad_two + grad_gate_pre.astype(f32)[:, None] * gate_vector.astype(f32)[None, :]
    grad_resid_norm, grad_gain_two = rms_back(
        own_residual, inv_two, ffn_gain, grad_two
    )
    grad_resid = cotangent.reshape(token_count, width).astype(f32) + grad_resid_norm

    grad_mixed, sum_expert_in = after(grad_resid.astype(bf16), sum_expert_in)
    mixed_all = ring_gather(grad_mixed, ctx_size, ctx_index)
    grad_attn = dot_t(mixed_all, out_weight).astype(bf16).reshape(head_shape)
    grad_attn, sum_shared_in, sum_shared_out = after(grad_attn, sum_shared_in, sum_shared_out)
    grad_weights = jnp.einsum("qhd,khd->hqk", grad_attn, values, preferred_element_type=f32)
    delta = jnp.sum(weights * grad_weights, axis=-1, keepdims=True)
    grad_scores = jnp.where(allowed[None], weights * (grad_weights - delta), 0.0).astype(bf16)
    grad_q = jnp.einsum("hqk,khd->qhd", grad_scores, keys, preferred_element_type=f32) * score_scale
    grad_k = (
        jnp.einsum("hqk,qhd->khd", grad_scores, queries, preferred_element_type=f32) * score_scale
    )
    grad_v = jnp.einsum("hqk,qhd->khd", weights_low, grad_attn, preferred_element_type=f32)
    grad_projected = jnp.concatenate(
        [
            rotate_back(grad_q, cos_tab, sine_tab).reshape(seq_len, own_width),
            rotate_back(grad_k, cos_tab, sine_tab).reshape(seq_len, own_width),
            grad_v.reshape(seq_len, own_width),
        ],
        axis=-1,
    ).astype(bf16)
    grad_projected, sum_expert_out = after(grad_projected, sum_expert_out)
    one_sums = dot_t(grad_projected, qkv_weight)
    grad_gain_one = jnp.sum(one_sums * inputs * inv_one_all, axis=0)
    one_parts = one_sums.astype(bf16)
    one_kept, grad_projected = after(one_parts, grad_projected)
    one_kept, sum_shared_in = after(one_kept, sum_shared_in)
    sum_shared_in = lax.all_to_all(
        sum_shared_in, "ctx", split_axis=0, concat_axis=0, tiled=True
    )
    grad_normed = ring_scatter(one_parts, ctx_size, ctx_index, one_kept)
    grad_inputs_norm, unused = rms_back(
        own_tokens,
        own_rows(inv_one_all),
        attn_gain,
        grad_normed,
    )
    grad_tokens = (grad_resid + grad_inputs_norm).reshape(tokens.shape)
    grad_qkv_weight = t_dot(normed_low, grad_projected)
    grad_bias = jnp.sum(grad_projected.astype(f32), axis=0).reshape(3, 1, own_width)
    grad_bias = jnp.where(
        jnp.arange(ctx_size, dtype=i32)[None, :, None] == ctx_index, grad_bias, 0.0
    )

    grad_out_weight = t_dot(attn_own, mixed_all)
    small_grads = [grad_gain_one, grad_gain_two, grad_gate_vector, grad_router, grad_bias]
    small_grads = jnp.concatenate(
        [piece.reshape(device_count, -1) for piece in small_grads], axis=1
    )
    more = -(-small_size // (3 * own_width * 16)) * 16
    small_grads = jnp.pad(small_grads, ((0, 0), (0, more * 3 * own_width - small_size)))
    pieces = jnp.concatenate(
        [
            grad_qkv_weight.astype(bf16).reshape(ctx_size, fsdp_size, shard, 3 * own_width),
            small_grads.astype(bf16).reshape(ctx_size, fsdp_size, more, 3 * own_width),
        ],
        axis=2,
    )
    pieces = pieces.transpose(1, 0, 2, 3).reshape(-1, 3 * own_width)
    pieces = lax.psum_scatter(pieces, "fsdp", scatter_dimension=0, tiled=True)
    pieces = pieces.reshape(ctx_size, shard + more, 3 * own_width)
    pieces = lax.all_to_all(pieces, "ctx", split_axis=0, concat_axis=0, tiled=True)
    small_grads = jnp.sum(pieces[:, shard:].reshape(ctx_size, -1).astype(f32), axis=0)
    return (
        output,
        grad_tokens,
        merge_columns(pieces[:, :shard], 3, ctx_size),
        small_grads[router_end:small_size],
        sum_rows(grad_out_weight).astype(f32),
        small_grads[:shard],
        small_grads[shard : 2 * shard],
        small_grads[3 * shard : router_end].reshape(shard, expert_count),
        small_grads[2 * shard : 3 * shard],
        merge_columns(sum_shared_in, 2, ctx_size),
        sum_shared_out.astype(f32),
        sum_expert_in.astype(f32)[None],
        sum_expert_out.astype(f32)[None],
    )


def local_wide(
    tokens,
    segments,
    routes,
    cotangent,
    w_qkv,
    b_qkv,
    w_out,
    gain_attn,
    gain_ffn,
    w_router,
    w_shared_gate,
    w_shared_in,
    w_shared_out,
    w_expert_in,
    w_expert_out,
):
    block_len = tokens.shape[2]
    model_width = tokens.shape[3]
    token_count = 2 * block_len
    top_count = routes.shape[3]
    half_len = segments.shape[2]
    seq_len = 2 * half_len
    ctx_index = lax.axis_index("ctx")
    head_count = model_width // HD
    expert_count = w_router.shape[1]
    capacity = token_count * top_count // expert_count
    slot_count = expert_count * capacity
    key_rows = min(512, seq_len)
    key_blocks = seq_len // key_rows
    score_scale = HD ** (-0.5)
    head_shape = (token_count, head_count, HD)
    attn_set = (
        lax.all_gather(w_qkv, ("ctx", "fsdp"), axis=0, tiled=True),
        lax.all_gather(b_qkv, ("ctx", "fsdp"), axis=0, tiled=True),
        lax.all_gather(w_out, ("ctx", "fsdp"), axis=0, tiled=True),
        lax.all_gather(gain_attn, ("ctx", "fsdp"), axis=0, tiled=True),
    )
    qkv_weight, qkv_bias, out_weight, attn_gain = attn_set
    inputs = tokens.reshape(token_count, model_width).astype(jnp.float32)
    normed, inv_one = rms_norm(inputs, attn_gain.astype(jnp.float32))
    normed_low = normed.astype(jnp.bfloat16)
    projected = jnp.dot(
        normed_low, qkv_weight, preferred_element_type=jnp.float32
    ) + qkv_bias.astype(jnp.float32)
    local_index = jnp.arange(block_len, dtype=jnp.int32)
    query_pos = jnp.concatenate(
        [ctx_index * block_len + local_index, seq_len - (ctx_index + 1) * block_len + local_index]
    )
    half_index = jnp.arange(half_len, dtype=jnp.int32)
    key_pos = jnp.concatenate(
        [half_index, seq_len - block_len * (half_index // block_len + 1) + half_index % block_len]
    ).reshape(key_blocks, key_rows)
    key_seg = segments.reshape(key_blocks, key_rows)
    query_seg = lax.dynamic_slice_in_dim(segments[0], ctx_index * block_len, block_len, 1).reshape(
        token_count
    )
    cos_tab, sine_tab = rope_tables(query_pos, HD)
    queries = rotate(projected[:, :model_width].reshape(head_shape), cos_tab, sine_tab).astype(
        jnp.bfloat16
    )
    keys_own = rotate(
        projected[:, model_width : 2 * model_width].reshape(head_shape), cos_tab, sine_tab
    ).astype(jnp.bfloat16)
    values_own = projected[:, 2 * model_width :].astype(jnp.bfloat16)
    keys_all, values_all = (
        lax.all_gather(keys_own.reshape(2, block_len, model_width), "ctx", axis=1, tiled=True),
        lax.all_gather(values_own.reshape(2, block_len, model_width), "ctx", axis=1, tiled=True),
    )
    keys_all = keys_all.reshape(key_blocks, key_rows, head_count, HD)
    values_all = values_all.reshape(key_blocks, key_rows, head_count, HD)

    def score_block(key_blk, pos_blk, seg_blk):
        raw_scores = (
            jnp.einsum("qhd,khd->hqk", queries, key_blk, preferred_element_type=jnp.float32)
            * score_scale
        )
        allowed = (pos_blk[None, :] <= query_pos[:, None]) & (
            seg_blk[None, :] == query_seg[:, None]
        )
        return (jnp.where(allowed[None], raw_scores, MASK_FILL), allowed)

    def total_step(running, key_part):
        run_max, run_sum = running
        scores = score_block(key_part[0], key_part[1], key_part[2])[0]
        new_max = jnp.maximum(run_max, jnp.max(scores, axis=-1))
        run_sum = run_sum * jnp.exp(run_max - new_max) + jnp.sum(
            jnp.exp(scores - new_max[..., None]), axis=-1
        )
        return ((new_max, run_sum), None)

    start_max = jnp.full((head_count, token_count), MASK_FILL, jnp.float32)
    start_sum = jnp.zeros((head_count, token_count), jnp.float32)
    (run_max, run_sum), unused = lax.scan(
        total_step, (start_max, start_sum), (keys_all, key_pos, key_seg)
    )
    log_total = run_max + jnp.log(run_sum)

    def attend_step(summed, key_part):
        key_blk, value_blk, pos_blk, seg_blk = key_part
        scores = score_block(key_blk, pos_blk, seg_blk)[0]
        weights = jnp.exp(scores - log_total[..., None]).astype(jnp.bfloat16)
        return (
            summed
            + jnp.einsum("hqk,khd->qhd", weights, value_blk, preferred_element_type=jnp.float32),
            None,
        )

    key_stack = (keys_all, values_all, key_pos, key_seg)
    attended, unused = lax.scan(attend_step, jnp.zeros(head_shape, jnp.float32), key_stack)
    attn_low = attended.reshape(token_count, model_width).astype(jnp.bfloat16)
    residual = inputs + jnp.dot(attn_low, out_weight, preferred_element_type=jnp.float32)
    ffn_set = (
        lax.all_gather(gain_ffn, ("ctx", "fsdp"), axis=0, tiled=True),
        lax.all_gather(w_router, ("ctx", "fsdp"), axis=0, tiled=True),
        lax.all_gather(w_shared_gate, ("ctx", "fsdp"), axis=0, tiled=True),
        lax.all_gather(w_shared_in, ("ctx", "fsdp"), axis=0, tiled=True),
        lax.all_gather(w_shared_out, ("ctx", "fsdp"), axis=0, tiled=True),
    )
    ffn_gain, router_weight, gate_vector, shared_in, shared_out = ffn_set
    normed_two, inv_two = rms_norm(residual, ffn_gain.astype(jnp.float32))
    low_two = normed_two.astype(jnp.bfloat16)
    logits = jnp.dot(low_two, router_weight, preferred_element_type=jnp.float32)
    router_probs = jax.nn.softmax(logits, axis=-1)
    chosen = routes.reshape(token_count, top_count)
    chosen_mask = chosen[..., None] == jnp.arange(expert_count, dtype=jnp.int32)
    gate_vals = jnp.sum(jnp.where(chosen_mask, router_probs[:, None, :], 0.0), axis=-1)
    shared_scale = jax.nn.sigmoid(jnp.dot(low_two, gate_vector, preferred_element_type=jnp.float32))
    shared_pre = jnp.dot(low_two, shared_in, preferred_element_type=jnp.float32)
    shared_hid = swiglu(shared_pre, FS).astype(jnp.bfloat16)
    shared_res = jnp.dot(shared_hid, shared_out, preferred_element_type=jnp.float32)
    pair_routes = chosen.reshape(token_count * top_count)
    expert_marks = (
        pair_routes[:, None] == jnp.arange(expert_count, dtype=jnp.int32)[None, :]
    ).astype(jnp.int32)
    pair_ranks = jnp.sum((jnp.cumsum(expert_marks, axis=0) - expert_marks) * expert_marks, axis=1)
    pair_target = jnp.where(pair_ranks < capacity, pair_routes * capacity + pair_ranks, -1)
    pair_map = pair_target[:, None] == jnp.arange(slot_count, dtype=jnp.int32)[None, :]
    pair_low = pair_map.astype(jnp.bfloat16)
    token_map = jnp.sum(
        pair_map.reshape(token_count, top_count, slot_count).astype(jnp.int32), axis=1
    ).astype(jnp.bfloat16)
    outgoing = jnp.einsum(
        "tc,td->cd", token_map, low_two, preferred_element_type=jnp.float32
    ).astype(jnp.bfloat16)
    incoming = lax.all_to_all(
        outgoing.reshape(expert_count, capacity, model_width),
        "ctx",
        split_axis=0,
        concat_axis=1,
        tiled=True,
    )
    expert_in, expert_out = (
        lax.all_gather(w_expert_in, "fsdp", axis=1, tiled=True),
        lax.all_gather(w_expert_out, "fsdp", axis=1, tiled=True),
    )
    expert_pre = jnp.einsum("erd,edf->erf", incoming, expert_in, preferred_element_type=jnp.float32)
    expert_hid = swiglu(expert_pre, FE).astype(jnp.bfloat16)
    expert_res = jnp.einsum(
        "erf,efd->erd", expert_hid, expert_out, preferred_element_type=jnp.float32
    ).astype(jnp.bfloat16)
    returned = lax.all_to_all(expert_res, "ctx", split_axis=1, concat_axis=0, tiled=True).reshape(
        slot_count, model_width
    )
    pair_vals = jnp.dot(pair_low, returned, preferred_element_type=jnp.float32).reshape(
        token_count, top_count, model_width
    )
    routed = jnp.sum(gate_vals[..., None] * pair_vals, axis=1)
    output = (
        (residual + shared_scale[:, None] * shared_res + routed)
        .astype(jnp.bfloat16)
        .reshape(tokens.shape)
    )
    grad_out = cotangent.reshape(token_count, model_width).astype(jnp.float32)
    pair_grads = gate_vals[..., None] * grad_out[:, None, :]
    grad_gates = jnp.sum(grad_out[:, None, :] * pair_vals, axis=-1)
    grad_returned = jnp.einsum(
        "pc,pd->cd",
        pair_map.astype(jnp.float32),
        pair_grads.reshape(token_count * top_count, model_width),
        precision=HIGHEST,
    ).astype(jnp.bfloat16)
    grad_res = lax.all_to_all(
        grad_returned.reshape(expert_count, capacity, model_width),
        "ctx",
        split_axis=0,
        concat_axis=1,
        tiled=True,
    )
    grad_expert_out = jnp.einsum(
        "erf,erd->efd", expert_hid, grad_res, preferred_element_type=jnp.float32
    )
    grad_hid = jnp.einsum("erd,efd->erf", grad_res, expert_out, preferred_element_type=jnp.float32)
    grad_pre = swiglu_back(expert_pre, FE, grad_hid).astype(jnp.bfloat16)
    grad_expert_in = jnp.einsum(
        "erd,erf->edf", incoming, grad_pre, preferred_element_type=jnp.float32
    )
    grad_incoming = jnp.einsum(
        "erf,edf->erd", grad_pre, expert_in, preferred_element_type=jnp.float32
    ).astype(jnp.bfloat16)
    grad_outgoing = lax.all_to_all(
        grad_incoming, "ctx", split_axis=1, concat_axis=0, tiled=True
    ).reshape(slot_count, model_width)
    expert_grads = (
        lax.psum_scatter(
            grad_expert_in.astype(jnp.bfloat16), "fsdp", scatter_dimension=1, tiled=True
        ).astype(jnp.float32),
        lax.psum_scatter(
            grad_expert_out.astype(jnp.bfloat16), "fsdp", scatter_dimension=1, tiled=True
        ).astype(jnp.float32),
    )
    grad_two = jnp.einsum("tc,cd->td", token_map, grad_outgoing, preferred_element_type=jnp.float32)
    grad_probs = jnp.sum(jnp.where(chosen_mask, grad_gates[..., None], 0.0), axis=1)
    grad_logits = (
        router_probs * (grad_probs - jnp.sum(router_probs * grad_probs, axis=-1, keepdims=True))
    ).astype(jnp.bfloat16)
    grad_router = jnp.einsum("td,te->de", low_two, grad_logits, preferred_element_type=jnp.float32)
    grad_shared_res = (shared_scale[:, None] * grad_out).astype(jnp.bfloat16)
    grad_gate_pre = (
        jnp.sum(grad_out * shared_res, axis=-1) * shared_scale * (1.0 - shared_scale)
    ).astype(jnp.bfloat16)
    grad_shared_out = jnp.einsum(
        "tf,td->fd", shared_hid, grad_shared_res, preferred_element_type=jnp.float32
    )
    grad_shared_hid = jnp.einsum(
        "td,fd->tf", grad_shared_res, shared_out, preferred_element_type=jnp.float32
    )
    grad_shared_pre = swiglu_back(shared_pre, FS, grad_shared_hid).astype(jnp.bfloat16)
    grad_shared_in = jnp.einsum(
        "td,tf->df", low_two, grad_shared_pre, preferred_element_type=jnp.float32
    )
    grad_gate_vector = jnp.einsum(
        "td,t->d", low_two, grad_gate_pre, preferred_element_type=jnp.float32
    )
    grad_two = grad_two + jnp.einsum(
        "te,de->td", grad_logits, router_weight, preferred_element_type=jnp.float32
    )
    grad_two = grad_two + jnp.einsum(
        "tf,df->td", grad_shared_pre, shared_in, preferred_element_type=jnp.float32
    )
    grad_two = (
        grad_two
        + grad_gate_pre.astype(jnp.float32)[:, None] * gate_vector.astype(jnp.float32)[None, :]
    )
    grad_resid_norm, grad_gain_two = rms_back(
        residual, inv_two, ffn_gain.astype(jnp.float32), grad_two
    )
    grad_resid = grad_out + grad_resid_norm
    ffn_grads = (
        lax.psum_scatter(grad_gain_two, ("ctx", "fsdp"), scatter_dimension=0, tiled=True),
        lax.psum_scatter(grad_router, ("ctx", "fsdp"), scatter_dimension=0, tiled=True),
        lax.psum_scatter(grad_gate_vector, ("ctx", "fsdp"), scatter_dimension=0, tiled=True),
        lax.psum_scatter(grad_shared_in, ("ctx", "fsdp"), scatter_dimension=0, tiled=True),
        lax.psum_scatter(grad_shared_out, ("ctx", "fsdp"), scatter_dimension=0, tiled=True),
    )
    grad_mixed = grad_resid.astype(jnp.bfloat16)
    grad_out_weight = jnp.einsum(
        "tc,td->cd", attn_low, grad_mixed, preferred_element_type=jnp.float32
    )
    grad_attn = (
        jnp.einsum("td,cd->tc", grad_mixed, out_weight, preferred_element_type=jnp.float32)
        .astype(jnp.bfloat16)
        .reshape(head_shape)
    )

    def delta_step(summed, key_part):
        key_blk, value_blk, pos_blk, seg_blk = key_part
        weights = jnp.exp(score_block(key_blk, pos_blk, seg_blk)[0] - log_total[..., None])
        grad_weights = jnp.einsum(
            "qhd,khd->hqk", grad_attn, value_blk, preferred_element_type=jnp.float32
        )
        return (summed + jnp.sum(weights * grad_weights, axis=-1), None)

    delta_sum, unused = lax.scan(
        delta_step, jnp.zeros((head_count, token_count), jnp.float32), key_stack
    )

    def grad_step(summed, key_part):
        key_blk, value_blk, pos_blk, seg_blk = key_part
        scores, allowed = score_block(key_blk, pos_blk, seg_blk)
        weights = jnp.exp(scores - log_total[..., None])
        grad_weights = jnp.einsum(
            "qhd,khd->hqk", grad_attn, value_blk, preferred_element_type=jnp.float32
        )
        grad_scores = jnp.where(
            allowed[None], weights * (grad_weights - delta_sum[..., None]), 0.0
        ).astype(jnp.bfloat16)
        summed = (
            summed
            + jnp.einsum("hqk,khd->qhd", grad_scores, key_blk, preferred_element_type=jnp.float32)
            * score_scale
        )
        grad_key = (
            jnp.einsum("hqk,qhd->khd", grad_scores, queries, preferred_element_type=jnp.float32)
            * score_scale
        )
        grad_value = jnp.einsum(
            "hqk,qhd->khd",
            weights.astype(jnp.bfloat16),
            grad_attn,
            preferred_element_type=jnp.float32,
        )
        return (summed, (grad_key, grad_value))

    grad_query, (grad_keys, grad_values) = lax.scan(
        grad_step, jnp.zeros(head_shape, jnp.float32), key_stack
    )
    grad_keys_own, grad_values_own = (
        lax.psum_scatter(
            grad_keys.reshape(2, half_len, model_width).astype(jnp.bfloat16),
            "ctx",
            scatter_dimension=1,
            tiled=True,
        ).astype(jnp.float32),
        lax.psum_scatter(
            grad_values.reshape(2, half_len, model_width).astype(jnp.bfloat16),
            "ctx",
            scatter_dimension=1,
            tiled=True,
        ).astype(jnp.float32),
    )
    grad_q_rows = rotate_back(grad_query, cos_tab, sine_tab).reshape(token_count, model_width)
    grad_k_rows = rotate_back(grad_keys_own.reshape(head_shape), cos_tab, sine_tab).reshape(
        token_count, model_width
    )
    grad_projected = jnp.concatenate(
        [grad_q_rows, grad_k_rows, grad_values_own.reshape(token_count, model_width)], axis=-1
    ).astype(jnp.bfloat16)
    grad_qkv_weight = jnp.einsum(
        "td,te->de", normed_low, grad_projected, preferred_element_type=jnp.float32
    )
    grad_qkv_bias = jnp.sum(grad_projected.astype(jnp.float32), axis=0)
    grad_normed = jnp.einsum(
        "te,de->td", grad_projected, qkv_weight, preferred_element_type=jnp.float32
    )
    grad_inputs_norm, grad_gain_one = rms_back(
        inputs, inv_one, attn_gain.astype(jnp.float32), grad_normed
    )
    grad_tokens = (grad_resid + grad_inputs_norm).reshape(tokens.shape)
    attn_grads = (
        lax.psum_scatter(grad_qkv_weight, ("ctx", "fsdp"), scatter_dimension=0, tiled=True),
        lax.psum_scatter(grad_qkv_bias, ("ctx", "fsdp"), scatter_dimension=0, tiled=True),
        lax.psum_scatter(grad_out_weight, ("ctx", "fsdp"), scatter_dimension=0, tiled=True),
        lax.psum_scatter(grad_gain_one, ("ctx", "fsdp"), scatter_dimension=0, tiled=True),
    )
    return (
        output,
        grad_tokens,
        attn_grads[0],
        attn_grads[1],
        attn_grads[2],
        attn_grads[3],
        ffn_grads[0],
        ffn_grads[1],
        ffn_grads[2],
        ffn_grads[3],
        ffn_grads[4],
        expert_grads[0],
        expert_grads[1],
    )


def solution(mesh):
    in_specs = (
        P("fsdp", None, "ctx", None),
        P("fsdp", None, None),
        P("fsdp", None, "ctx", None),
        P("fsdp", None, "ctx", None),
        P(("ctx", "fsdp"), None),
        P(("ctx", "fsdp")),
        P(("ctx", "fsdp"), None),
        P(("ctx", "fsdp")),
        P(("ctx", "fsdp")),
        P(("ctx", "fsdp"), None),
        P(("ctx", "fsdp")),
        P(("ctx", "fsdp"), None),
        P(("ctx", "fsdp"), None),
        P("ctx", "fsdp", None),
        P("ctx", "fsdp", None),
    )
    out_specs = (
        P("fsdp", None, "ctx", None),
        P("fsdp", None, "ctx", None),
        P(("ctx", "fsdp"), None),
        P(("ctx", "fsdp")),
        P(("ctx", "fsdp"), None),
        P(("ctx", "fsdp")),
        P(("ctx", "fsdp")),
        P(("ctx", "fsdp"), None),
        P(("ctx", "fsdp")),
        P(("ctx", "fsdp"), None),
        P(("ctx", "fsdp"), None),
        P("ctx", "fsdp", None),
        P("ctx", "fsdp", None),
    )
    ctx_size = mesh.shape["ctx"]
    fsdp_size = mesh.shape["fsdp"]

    def local(*arrays):
        if HEADS % ctx_size:
            return local_wide(*arrays)
        return local_split(ctx_size, fsdp_size, *arrays)

    return jax.shard_map(local, mesh=mesh, in_specs=in_specs, out_specs=out_specs, check_vma=False)
```

```python
import jax
import jax.numpy as jnp
from jax import lax
from jax.sharding import PartitionSpec as P

HD = 128
HEADS = 16
FS = 5632
FE = 1408


RMS_EPS = 1e-06
ROPE_THETA = 1000000.0
MASK_FILL = -1e30
HIGHEST = lax.Precision.HIGHEST


def rope_tables(positions, head_dim):
    half_dim = head_dim // 2
    inv_freq = ROPE_THETA ** (-(jnp.arange(half_dim, dtype=jnp.float32) * 2.0 / head_dim))
    angles = positions.astype(jnp.float32)[:, None] * inv_freq[None, :]
    cos_tab = jnp.concatenate([jnp.cos(angles), jnp.cos(angles)], axis=-1)
    sine_tab = jnp.concatenate([jnp.sin(angles), jnp.sin(angles)], axis=-1)
    return (cos_tab, sine_tab)


def rotate(values, cos_tab, sine_tab):
    half_dim = values.shape[-1] // 2
    turned = jnp.concatenate([-values[..., half_dim:], values[..., :half_dim]], axis=-1)
    return values * cos_tab[:, None, :] + turned * sine_tab[:, None, :]


def rotate_back(upstream, cos_tab, sine_tab):
    half_dim = upstream.shape[-1] // 2
    scaled = upstream * sine_tab[:, None, :]
    return upstream * cos_tab[:, None, :] + jnp.concatenate(
        [scaled[..., half_dim:], -scaled[..., :half_dim]], axis=-1
    )


def rms_norm(values, gain_vec):
    inv_rms = lax.rsqrt(jnp.mean(values * values, axis=-1, keepdims=True) + RMS_EPS)
    return (values * inv_rms * gain_vec, inv_rms)


def rms_back(values, inv_rms, gain_vec, upstream):
    weighted = upstream * gain_vec
    inner_mean = jnp.mean(weighted * values, axis=-1, keepdims=True)
    return (
        inv_rms * weighted - values * inv_rms * inv_rms * inv_rms * inner_mean,
        jnp.sum(upstream * values * inv_rms, axis=0),
    )


def swiglu(pre_act, split_at):
    return jax.nn.silu(pre_act[..., :split_at]) * pre_act[..., split_at:]


def swiglu_back(pre_act, split_at, upstream):
    gate_part = pre_act[..., :split_at]
    up_part = pre_act[..., split_at:]
    sigmoid_g = jax.nn.sigmoid(gate_part)
    d_gate = upstream * up_part * sigmoid_g * (1.0 + gate_part * (1.0 - sigmoid_g))
    d_up = upstream * gate_part * sigmoid_g
    return jnp.concatenate([d_gate, d_up], axis=-1)


def ring_order(size):
    return list(range(0, size, 2)) + list(range(size - 1, 0, -2))


def ring_steps(size):
    order = ring_order(size)
    ahead = [(order[i], order[(i + 1) % size]) for i in range(size)]
    back = [(dst, src) for src, dst in ahead]
    return (ahead, back)


def ring_peers(size, ctx_index):
    order = ring_order(size)
    place = {dev: i for i, dev in enumerate(order)}
    table = jnp.array(
        [[order[(place[dev] + k) % size] for k in range(size)] for dev in range(size)], jnp.int32
    )
    row = lax.dynamic_index_in_dim(table, ctx_index, 0, keepdims=False)
    return [row[k] for k in range(size)]


def ring_walk(block, size, ctx_index, out, put):
    rows = block.shape[0]
    ahead, back = ring_steps(size)
    peers = ring_peers(size, ctx_index)
    half = size // 2
    out = put(out, block, ctx_index, 0)
    fore = rear = block
    for k in range(1, half):
        fore = lax.ppermute(fore, "ctx", ahead)
        rear = lax.ppermute(rear, "ctx", back)
        out = put(out, fore, peers[size - k], 0)
        out = put(out, rear, peers[k], 0)
    fore = lax.ppermute(fore[: rows // 2], "ctx", ahead)
    rear = lax.ppermute(rear[rows // 2 :], "ctx", back)
    out = put(out, fore, peers[half], 0)
    return put(out, rear, peers[half], rows // 2)


def ring_gather(block, size, ctx_index):
    rows, width = block.shape

    def put(out, piece, peer, offset):
        return lax.dynamic_update_slice(out, piece, (peer * rows + offset, jnp.zeros_like(peer)))

    return ring_walk(block, size, ctx_index, jnp.zeros((size * rows, width), block.dtype), put)


def ring_sums(parts, size, ctx_index):
    f32 = jnp.float32
    rows = parts.shape[0] // size
    ahead, back = ring_steps(size)
    peers = ring_peers(size, ctx_index)
    half = size // 2

    def own(k, start, count):
        first = (peers[k % size] * rows + start, jnp.zeros_like(peers[0]))
        return lax.dynamic_slice(parts, first, (count, parts.shape[1])).astype(f32)

    def low(values):
        return values.astype(jnp.bfloat16)

    cut = rows // 2
    fore = lax.ppermute(low(own(half, 0, cut)), "ctx", ahead)
    rear = lax.ppermute(low(own(half, cut, cut)), "ctx", back)
    fore = jnp.concatenate(
        [low(fore.astype(f32) + own(half - 1, 0, cut)), low(own(half - 1, cut, cut))], axis=0
    )
    rear = jnp.concatenate(
        [low(own(1 - half, 0, cut)), low(rear.astype(f32) + own(1 - half, cut, cut))], axis=0
    )
    for k in range(half - 1, 0, -1):
        fore = lax.ppermute(fore, "ctx", ahead)
        rear = lax.ppermute(rear, "ctx", back)
        if k > 1:
            fore = low(fore.astype(f32) + own(k - 1, 0, rows))
            rear = low(rear.astype(f32) + own(1 - k, 0, rows))
    return (fore, rear)


def ring_scatter(parts, size, ctx_index, kept=None):
    fore, rear = ring_sums(parts, size, ctx_index)
    kept = (parts if kept is None else kept).reshape(size, -1, parts.shape[1])
    kept = lax.dynamic_index_in_dim(kept, ctx_index, 0, keepdims=False)
    return kept.astype(jnp.float32) + fore.astype(jnp.float32) + rear.astype(jnp.float32)


def other_core(size):
    return [(i, i ^ 1) for i in range(size)]


def other_chip(size):
    return [(i, i ^ 2) for i in range(size)]


def after(value, *deps):
    return lax.optimization_barrier((value,) + deps)


def fsdp_gather(shard, size, hold):
    index = lax.axis_index("fsdp")
    rows, width = shard.shape
    far = lax.ppermute(shard, "fsdp", other_chip(size))
    far, hold = after(far, hold)
    pair = jnp.where(
        index < 2, jnp.stack([shard, far], axis=0), jnp.stack([far, shard], axis=0)
    )
    near = lax.ppermute(pair, "fsdp", other_core(size))
    out = jnp.zeros((2, 2, rows, width), shard.dtype)
    out = lax.dynamic_update_index_in_dim(out, pair, index % 2, 1)
    out = lax.dynamic_update_index_in_dim(out, near, 1 - index % 2, 1)
    return (out.reshape(size * rows, width), hold)


def column_pieces(weight, groups, size, extra):
    rows = weight.shape[0]
    width = weight.shape[1] // (groups * size)
    pieces = weight.reshape(rows, groups, size, width).transpose(2, 0, 1, 3)
    pieces = pieces.reshape(size, rows, groups * width)
    if extra is not None:
        count = extra.shape[0]
        more = -(-count // (groups * width * 16)) * 16
        extra = jnp.pad(extra, (0, more * groups * width - count))
        extra = jnp.broadcast_to(
            extra.reshape(1, more, groups * width), (size, more, groups * width)
        )
        pieces = jnp.concatenate([pieces, extra], axis=1)
    return lax.all_to_all(pieces, "ctx", split_axis=0, concat_axis=0, tiled=True)


def merge_columns(pieces, groups, size):
    width = pieces.shape[2] // groups
    columns = [
        pieces[peer, :, group * width : (group + 1) * width]
        for group in range(groups)
        for peer in range(size)
    ]
    return jnp.concatenate(columns, axis=1).astype(jnp.float32)


def local_split(
    ctx_size,
    fsdp_size,
    tokens,
    segments,
    routes,
    cotangent,
    w_qkv,
    b_qkv,
    w_out,
    gain_attn,
    gain_ffn,
    w_router,
    w_shared_gate,
    w_shared_in,
    w_shared_out,
    w_expert_in,
    w_expert_out,
):
    bf16, f32, i32 = jnp.bfloat16, jnp.float32, jnp.int32
    device_count = ctx_size * fsdp_size
    block_len = tokens.shape[2]
    width = tokens.shape[3]
    token_count = 2 * block_len
    top_count = routes.shape[3]
    seq_len = token_count * ctx_size
    ctx_index = lax.axis_index("ctx")
    expert_count = w_router.shape[1]
    capacity = token_count * top_count // expert_count
    own_heads = HEADS // ctx_size
    own_width = own_heads * HD
    fs_own = FS // ctx_size
    score_scale = HD ** (-0.5)

    def dot(a, b):
        return jnp.dot(a, b, preferred_element_type=f32)

    def dot_t(a, b):
        return lax.dot_general(a, b, (((1,), (1,)), ((), ())), preferred_element_type=f32)

    def t_dot(a, b):
        return lax.dot_general(a, b, (((0,), (0,)), ((), ())), preferred_element_type=f32)

    def own_rows(values):
        return lax.dynamic_index_in_dim(
            values.reshape((ctx_size, token_count) + values.shape[1:]), ctx_index, 0, keepdims=False
        )

    def sum_rows(grad):
        return lax.psum_scatter(grad.astype(bf16), "fsdp", scatter_dimension=0, tiled=True)

    shard = width // device_count
    small = [gain_attn, gain_ffn, w_shared_gate, w_router.reshape(-1), b_qkv]
    small_size = sum(piece.shape[0] for piece in small)
    small = jnp.concatenate(small + [routes.astype(bf16).reshape(-1)], axis=0)
    small_count = small.shape[0]
    token_rows = ring_gather(tokens.reshape(token_count, width), ctx_size, ctx_index)
    expert_out = lax.all_gather(w_expert_out[0], "fsdp", axis=0, tiled=True)
    pieces = column_pieces(w_qkv, 3, ctx_size, small)
    pieces, expert_out = after(pieces, expert_out)
    pieces = lax.all_gather(pieces, "fsdp", axis=0, tiled=False).transpose(1, 0, 2, 3)
    qkv_weight = pieces[:, :, :shard].reshape(width, 3 * own_width)
    small = pieces[:, :, shard:].reshape(device_count, -1)[:, :small_count]
    attn_gain = small[:, :shard].reshape(width).astype(f32)
    ffn_gain = small[:, shard : 2 * shard].reshape(width).astype(f32)
    gate_vector = small[:, 2 * shard : 3 * shard].reshape(width)
    router_end = 3 * shard + shard * expert_count
    router_weight = small[:, 3 * shard : router_end].reshape(width, expert_count)
    bias = small[:, router_end:small_size].reshape(3, ctx_size, own_width).astype(f32)
    bias = lax.dynamic_index_in_dim(bias, ctx_index, 1, keepdims=False).reshape(3 * own_width)
    route_rows = small[:, small_size:].astype(i32)
    route_rows = lax.dynamic_index_in_dim(
        route_rows.reshape(ctx_size, fsdp_size, -1), lax.axis_index("fsdp"), 1, keepdims=False
    ).reshape(ctx_size, token_count, top_count)

    expert_in = lax.all_gather(w_expert_in[0], "fsdp", axis=0, tiled=True)
    grad_rows = lax.all_gather(
        cotangent.reshape(token_count, width), "ctx", axis=0, tiled=True
    )

    block_ids = jnp.arange(ctx_size, dtype=i32)[:, None]
    local_index = jnp.arange(block_len, dtype=i32)[None, :]
    positions = jnp.stack(
        [
            block_ids * block_len + local_index,
            seq_len - (block_ids + 1) * block_len + local_index,
        ],
        axis=1,
    ).reshape(seq_len)
    seg_rows = (
        segments.reshape(2, ctx_size, block_len).transpose(1, 0, 2).reshape(seq_len)
    )
    cos_tab, sine_tab = rope_tables(positions, HD)

    inputs = token_rows.astype(f32)
    normed, inv_one_all = rms_norm(inputs, attn_gain)
    normed_low = normed.astype(bf16)
    projected = dot(normed_low, qkv_weight) + bias
    head_shape = (seq_len, own_heads, HD)
    queries = rotate(projected[:, :own_width].reshape(head_shape), cos_tab, sine_tab).astype(bf16)
    keys = rotate(
        projected[:, own_width : 2 * own_width].reshape(head_shape), cos_tab, sine_tab
    ).astype(bf16)
    values = projected[:, 2 * own_width :].reshape(head_shape).astype(bf16)
    queries, in_shard = after(queries, w_shared_in)
    shared_in = column_pieces(in_shard, 2, ctx_size, None)
    out_weight, queries = fsdp_gather(w_out, fsdp_size, queries)
    allowed = (positions[None, :] <= positions[:, None]) & (seg_rows[None, :] == seg_rows[:, None])
    scores = jnp.einsum("qhd,khd->hqk", queries, keys, preferred_element_type=f32) * score_scale
    scores = jnp.where(allowed[None], scores, MASK_FILL)
    top_score = jnp.max(scores, axis=-1, keepdims=True)
    log_total = top_score + jnp.log(jnp.sum(jnp.exp(scores - top_score), axis=-1, keepdims=True))
    weights = jnp.exp(scores - log_total)
    weights_low = weights.astype(bf16)
    attended = jnp.einsum("hqk,khd->qhd", weights_low, values, preferred_element_type=f32)
    attn_own = attended.astype(bf16).reshape(seq_len, own_width)
    shared_out, attn_own = fsdp_gather(w_shared_out, fsdp_size, attn_own)
    attn_parts = dot(attn_own, out_weight).astype(bf16)
    own_tokens = tokens.reshape(token_count, width).astype(f32)
    own_residual = own_tokens + ring_scatter(attn_parts, ctx_size, ctx_index)

    normed_two, inv_two = rms_norm(own_residual, ffn_gain)
    own_low = normed_two.astype(bf16)
    shared_in, own_low = after(shared_in, own_low)
    shared_in = lax.all_gather(shared_in, "fsdp", axis=0, tiled=False)
    low_two = ring_gather(own_low, ctx_size, ctx_index)
    mixed_weight = jnp.concatenate([router_weight, gate_vector[:, None]], axis=1)
    logits = dot(low_two, mixed_weight)
    probs_all = jax.nn.softmax(logits[:, :expert_count], axis=-1)
    scale_all = jax.nn.sigmoid(logits[:, expert_count])
    gate_all = lax.dynamic_index_in_dim(probs_all, ctx_index, 1, keepdims=False)

    named = jnp.any(route_rows == ctx_index, axis=-1)
    before = jnp.arange(token_count)[:, None] < jnp.arange(token_count)[None, :]
    rank = dot(named.astype(bf16), before.astype(bf16)).astype(i32)
    slot_of = jnp.where(named & (rank < capacity), rank, -1)
    slot_mask = slot_of[:, None, :] == jnp.arange(capacity, dtype=i32)[None, :, None]
    slot_map = slot_mask.astype(bf16)
    blocks_two = low_two.reshape(ctx_size, token_count, width)
    gate_blocks = gate_all.reshape(ctx_size, token_count)

    def to_slots(blocks):
        picked = jnp.einsum("bmt,btd->bmd", slot_map, blocks, preferred_element_type=f32)
        return picked.reshape(ctx_size * capacity, width)

    def to_tokens(slots):
        spread = jnp.einsum(
            "bmt,bmd->btd",
            slot_map,
            slots.reshape(ctx_size, capacity, width),
            preferred_element_type=f32,
        )
        return spread.reshape(seq_len, width)

    buffer = to_slots(blocks_two).astype(bf16)
    buffer, grad_rows = after(buffer, grad_rows)
    expert_pre = dot(buffer, expert_in)
    expert_hid = swiglu(expert_pre, FE).astype(bf16)
    expert_res = dot(expert_hid, expert_out).astype(bf16)
    routed = gate_all[:, None] * to_tokens(expert_res)

    grad_slots = to_slots(grad_rows.reshape(ctx_size, token_count, width))
    gate_slots = jnp.sum(jnp.where(slot_mask, gate_blocks[:, None, :], 0.0), axis=-1).reshape(-1, 1)
    grad_res = (gate_slots * grad_slots).astype(bf16)
    slot_dots = jnp.sum(grad_slots * expert_res.astype(f32), axis=-1).reshape(ctx_size, capacity, 1)
    grad_gates = jnp.sum(jnp.where(slot_mask, slot_dots, 0.0), axis=1)
    grad_hid = dot_t(grad_res, expert_out)
    grad_pre = swiglu_back(expert_pre, FE, grad_hid).astype(bf16)
    grad_pre, shared_in = after(grad_pre, shared_in)
    grad_expert_in = t_dot(buffer, grad_pre)
    grad_buffer = dot_t(grad_pre, expert_in).astype(bf16)

    grad_expert_in, low_shared = after(grad_expert_in.astype(bf16), low_two)
    sum_expert_in = sum_rows(grad_expert_in)

    shared_in = shared_in.transpose(1, 0, 2, 3).reshape(width, 2 * fs_own)
    shared_pre = dot(low_shared, shared_in)
    shared_hid = swiglu(shared_pre, fs_own).astype(bf16)
    shared_res = dot(shared_hid, shared_out)
    out_parts = (scale_all[:, None] * shared_res + routed).astype(bf16)

    grad_f32 = grad_rows.astype(f32)
    gate_dots = jnp.sum(grad_f32 * shared_res, axis=-1).reshape(ctx_size, token_count)
    grad_shared_res = (scale_all[:, None] * grad_f32).astype(bf16)
    grad_shared_hid = dot_t(grad_shared_res, shared_out)
    grad_shared_pre = swiglu_back(shared_pre, fs_own, grad_shared_hid).astype(bf16)
    two_parts = (dot_t(grad_shared_pre, shared_in) + to_tokens(grad_buffer)).astype(bf16)
    two_parts, expert_hid, shared_hid, grad_shared_pre = after(
        two_parts, expert_hid, shared_hid, grad_shared_pre
    )
    grad_expert_out = t_dot(expert_hid, grad_res).astype(bf16)
    grad_shared_out = t_dot(shared_hid, grad_shared_res).astype(bf16)
    grad_shared_in = t_dot(low_two, grad_shared_pre).astype(bf16)
    grad_two = ring_scatter(two_parts, ctx_size, ctx_index)
    grad_two, grad_shared_in, grad_shared_out, grad_expert_out = after(
        grad_two, grad_shared_in, grad_shared_out, grad_expert_out
    )
    sum_shared_in = grad_shared_in.reshape(ctx_size, fsdp_size, shard, 2 * fs_own)
    sum_shared_in = lax.psum_scatter(
        sum_shared_in.transpose(1, 0, 2, 3).reshape(width, 2 * fs_own),
        "fsdp",
        scatter_dimension=0,
        tiled=True,
    ).reshape(ctx_size, shard, 2 * fs_own)
    sum_shared_out = sum_rows(grad_shared_out)
    sum_expert_out = sum_rows(grad_expert_out)
    dots = jnp.stack([grad_gates, gate_dots], axis=1)
    dots = lax.all_to_all(dots, "ctx", split_axis=0, concat_axis=0, tiled=True)
    own_probs = own_rows(probs_all)
    own_scale = own_rows(scale_all)
    own_chosen = routes.reshape(token_count, top_count)
    chosen_mask = jnp.any(
        own_chosen[..., None] == jnp.arange(expert_count, dtype=i32), axis=1
    )
    grad_probs = jnp.where(chosen_mask, dots[:, 0].T, 0.0)
    grad_logits = (
        own_probs * (grad_probs - jnp.sum(own_probs * grad_probs, axis=-1, keepdims=True))
    ).astype(bf16)
    grad_gate_pre = (jnp.sum(dots[:, 1], axis=0) * own_scale * (1.0 - own_scale)).astype(bf16)
    grad_router = t_dot(own_low, grad_logits)
    grad_gate_vector = t_dot(own_low, grad_gate_pre[:, None])
    grad_two = grad_two + dot_t(grad_logits, router_weight)
    grad_two = grad_two + grad_gate_pre.astype(f32)[:, None] * gate_vector.astype(f32)[None, :]
    grad_resid_norm, grad_gain_two = rms_back(
        own_residual, inv_two, ffn_gain, grad_two
    )
    grad_resid = cotangent.reshape(token_count, width).astype(f32) + grad_resid_norm

    grad_mixed, sum_expert_in = after(grad_resid.astype(bf16), sum_expert_in)
    mixed_all = ring_gather(grad_mixed, ctx_size, ctx_index)
    grad_attn = dot_t(mixed_all, out_weight).astype(bf16).reshape(head_shape)
    grad_attn, sum_shared_in, sum_shared_out = after(grad_attn, sum_shared_in, sum_shared_out)
    sum_shared_in = lax.all_to_all(
        sum_shared_in, "ctx", split_axis=0, concat_axis=0, tiled=True
    )
    grad_weights = jnp.einsum("qhd,khd->hqk", grad_attn, values, preferred_element_type=f32)
    delta = jnp.sum(weights * grad_weights, axis=-1, keepdims=True)
    grad_scores = jnp.where(allowed[None], weights * (grad_weights - delta), 0.0).astype(bf16)
    grad_q = jnp.einsum("hqk,khd->qhd", grad_scores, keys, preferred_element_type=f32) * score_scale
    grad_k = (
        jnp.einsum("hqk,qhd->khd", grad_scores, queries, preferred_element_type=f32) * score_scale
    )
    grad_v = jnp.einsum("hqk,qhd->khd", weights_low, grad_attn, preferred_element_type=f32)
    grad_projected = jnp.concatenate(
        [
            rotate_back(grad_q, cos_tab, sine_tab).reshape(seq_len, own_width),
            rotate_back(grad_k, cos_tab, sine_tab).reshape(seq_len, own_width),
            grad_v.reshape(seq_len, own_width),
        ],
        axis=-1,
    ).astype(bf16)
    grad_projected, sum_expert_out, sum_shared_in = after(
        grad_projected, sum_expert_out, sum_shared_in
    )
    one_sums = dot_t(grad_projected, qkv_weight)
    grad_gain_one = jnp.sum(one_sums * inputs * inv_one_all, axis=0)
    one_parts = one_sums.astype(bf16)
    one_kept, grad_projected = after(one_parts, grad_projected)
    one_kept, out_parts = after(one_kept, out_parts)
    output = own_residual + ring_scatter(out_parts, ctx_size, ctx_index)
    output = output.astype(bf16).reshape(tokens.shape)
    grad_normed = ring_scatter(one_parts, ctx_size, ctx_index, one_kept)
    grad_inputs_norm, unused = rms_back(
        own_tokens,
        own_rows(inv_one_all),
        attn_gain,
        grad_normed,
    )
    grad_tokens = (grad_resid + grad_inputs_norm).reshape(tokens.shape)
    grad_qkv_weight = t_dot(normed_low, grad_projected)
    grad_bias = jnp.sum(grad_projected.astype(f32), axis=0).reshape(3, 1, own_width)
    grad_bias = jnp.where(
        jnp.arange(ctx_size, dtype=i32)[None, :, None] == ctx_index, grad_bias, 0.0
    )

    grad_out_weight = t_dot(attn_own, mixed_all)
    small_grads = [grad_gain_one, grad_gain_two, grad_gate_vector, grad_router, grad_bias]
    small_grads = jnp.concatenate(
        [piece.reshape(device_count, -1) for piece in small_grads], axis=1
    )
    more = -(-small_size // (3 * own_width * 16)) * 16
    small_grads = jnp.pad(small_grads, ((0, 0), (0, more * 3 * own_width - small_size)))
    pieces = jnp.concatenate(
        [
            grad_qkv_weight.astype(bf16).reshape(ctx_size, fsdp_size, shard, 3 * own_width),
            small_grads.astype(bf16).reshape(ctx_size, fsdp_size, more, 3 * own_width),
        ],
        axis=2,
    )
    pieces = pieces.transpose(1, 0, 2, 3).reshape(-1, 3 * own_width)
    pieces = lax.psum_scatter(pieces, "fsdp", scatter_dimension=0, tiled=True)
    pieces = pieces.reshape(ctx_size, shard + more, 3 * own_width)
    pieces = lax.all_to_all(pieces, "ctx", split_axis=0, concat_axis=0, tiled=True)
    small_grads = jnp.sum(pieces[:, shard:].reshape(ctx_size, -1).astype(f32), axis=0)
    return (
        output,
        grad_tokens,
        merge_columns(pieces[:, :shard], 3, ctx_size),
        small_grads[router_end:small_size],
        sum_rows(grad_out_weight).astype(f32),
        small_grads[:shard],
        small_grads[shard : 2 * shard],
        small_grads[3 * shard : router_end].reshape(shard, expert_count),
        small_grads[2 * shard : 3 * shard],
        merge_columns(sum_shared_in, 2, ctx_size),
        sum_shared_out.astype(f32),
        sum_expert_in.astype(f32)[None],
        sum_expert_out.astype(f32)[None],
    )


def local_wide(
    tokens,
    segments,
    routes,
    cotangent,
    w_qkv,
    b_qkv,
    w_out,
    gain_attn,
    gain_ffn,
    w_router,
    w_shared_gate,
    w_shared_in,
    w_shared_out,
    w_expert_in,
    w_expert_out,
):
    block_len = tokens.shape[2]
    model_width = tokens.shape[3]
    token_count = 2 * block_len
    top_count = routes.shape[3]
    half_len = segments.shape[2]
    seq_len = 2 * half_len
    ctx_index = lax.axis_index("ctx")
    head_count = model_width // HD
    expert_count = w_router.shape[1]
    capacity = token_count * top_count // expert_count
    slot_count = expert_count * capacity
    key_rows = min(512, seq_len)
    key_blocks = seq_len // key_rows
    score_scale = HD ** (-0.5)
    head_shape = (token_count, head_count, HD)
    attn_set = (
        lax.all_gather(w_qkv, ("ctx", "fsdp"), axis=0, tiled=True),
        lax.all_gather(b_qkv, ("ctx", "fsdp"), axis=0, tiled=True),
        lax.all_gather(w_out, ("ctx", "fsdp"), axis=0, tiled=True),
        lax.all_gather(gain_attn, ("ctx", "fsdp"), axis=0, tiled=True),
    )
    qkv_weight, qkv_bias, out_weight, attn_gain = attn_set
    inputs = tokens.reshape(token_count, model_width).astype(jnp.float32)
    normed, inv_one = rms_norm(inputs, attn_gain.astype(jnp.float32))
    normed_low = normed.astype(jnp.bfloat16)
    projected = jnp.dot(
        normed_low, qkv_weight, preferred_element_type=jnp.float32
    ) + qkv_bias.astype(jnp.float32)
    local_index = jnp.arange(block_len, dtype=jnp.int32)
    query_pos = jnp.concatenate(
        [ctx_index * block_len + local_index, seq_len - (ctx_index + 1) * block_len + local_index]
    )
    half_index = jnp.arange(half_len, dtype=jnp.int32)
    key_pos = jnp.concatenate(
        [half_index, seq_len - block_len * (half_index // block_len + 1) + half_index % block_len]
    ).reshape(key_blocks, key_rows)
    key_seg = segments.reshape(key_blocks, key_rows)
    query_seg = lax.dynamic_slice_in_dim(segments[0], ctx_index * block_len, block_len, 1).reshape(
        token_count
    )
    cos_tab, sine_tab = rope_tables(query_pos, HD)
    queries = rotate(projected[:, :model_width].reshape(head_shape), cos_tab, sine_tab).astype(
        jnp.bfloat16
    )
    keys_own = rotate(
        projected[:, model_width : 2 * model_width].reshape(head_shape), cos_tab, sine_tab
    ).astype(jnp.bfloat16)
    values_own = projected[:, 2 * model_width :].astype(jnp.bfloat16)
    keys_all, values_all = (
        lax.all_gather(keys_own.reshape(2, block_len, model_width), "ctx", axis=1, tiled=True),
        lax.all_gather(values_own.reshape(2, block_len, model_width), "ctx", axis=1, tiled=True),
    )
    keys_all = keys_all.reshape(key_blocks, key_rows, head_count, HD)
    values_all = values_all.reshape(key_blocks, key_rows, head_count, HD)

    def score_block(key_blk, pos_blk, seg_blk):
        raw_scores = (
            jnp.einsum("qhd,khd->hqk", queries, key_blk, preferred_element_type=jnp.float32)
            * score_scale
        )
        allowed = (pos_blk[None, :] <= query_pos[:, None]) & (
            seg_blk[None, :] == query_seg[:, None]
        )
        return (jnp.where(allowed[None], raw_scores, MASK_FILL), allowed)

    def total_step(running, key_part):
        run_max, run_sum = running
        scores = score_block(key_part[0], key_part[1], key_part[2])[0]
        new_max = jnp.maximum(run_max, jnp.max(scores, axis=-1))
        run_sum = run_sum * jnp.exp(run_max - new_max) + jnp.sum(
            jnp.exp(scores - new_max[..., None]), axis=-1
        )
        return ((new_max, run_sum), None)

    start_max = jnp.full((head_count, token_count), MASK_FILL, jnp.float32)
    start_sum = jnp.zeros((head_count, token_count), jnp.float32)
    (run_max, run_sum), unused = lax.scan(
        total_step, (start_max, start_sum), (keys_all, key_pos, key_seg)
    )
    log_total = run_max + jnp.log(run_sum)

    def attend_step(summed, key_part):
        key_blk, value_blk, pos_blk, seg_blk = key_part
        scores = score_block(key_blk, pos_blk, seg_blk)[0]
        weights = jnp.exp(scores - log_total[..., None]).astype(jnp.bfloat16)
        return (
            summed
            + jnp.einsum("hqk,khd->qhd", weights, value_blk, preferred_element_type=jnp.float32),
            None,
        )

    key_stack = (keys_all, values_all, key_pos, key_seg)
    attended, unused = lax.scan(attend_step, jnp.zeros(head_shape, jnp.float32), key_stack)
    attn_low = attended.reshape(token_count, model_width).astype(jnp.bfloat16)
    residual = inputs + jnp.dot(attn_low, out_weight, preferred_element_type=jnp.float32)
    ffn_set = (
        lax.all_gather(gain_ffn, ("ctx", "fsdp"), axis=0, tiled=True),
        lax.all_gather(w_router, ("ctx", "fsdp"), axis=0, tiled=True),
        lax.all_gather(w_shared_gate, ("ctx", "fsdp"), axis=0, tiled=True),
        lax.all_gather(w_shared_in, ("ctx", "fsdp"), axis=0, tiled=True),
        lax.all_gather(w_shared_out, ("ctx", "fsdp"), axis=0, tiled=True),
    )
    ffn_gain, router_weight, gate_vector, shared_in, shared_out = ffn_set
    normed_two, inv_two = rms_norm(residual, ffn_gain.astype(jnp.float32))
    low_two = normed_two.astype(jnp.bfloat16)
    logits = jnp.dot(low_two, router_weight, preferred_element_type=jnp.float32)
    router_probs = jax.nn.softmax(logits, axis=-1)
    chosen = routes.reshape(token_count, top_count)
    chosen_mask = chosen[..., None] == jnp.arange(expert_count, dtype=jnp.int32)
    gate_vals = jnp.sum(jnp.where(chosen_mask, router_probs[:, None, :], 0.0), axis=-1)
    shared_scale = jax.nn.sigmoid(jnp.dot(low_two, gate_vector, preferred_element_type=jnp.float32))
    shared_pre = jnp.dot(low_two, shared_in, preferred_element_type=jnp.float32)
    shared_hid = swiglu(shared_pre, FS).astype(jnp.bfloat16)
    shared_res = jnp.dot(shared_hid, shared_out, preferred_element_type=jnp.float32)
    pair_routes = chosen.reshape(token_count * top_count)
    expert_marks = (
        pair_routes[:, None] == jnp.arange(expert_count, dtype=jnp.int32)[None, :]
    ).astype(jnp.int32)
    pair_ranks = jnp.sum((jnp.cumsum(expert_marks, axis=0) - expert_marks) * expert_marks, axis=1)
    pair_target = jnp.where(pair_ranks < capacity, pair_routes * capacity + pair_ranks, -1)
    pair_map = pair_target[:, None] == jnp.arange(slot_count, dtype=jnp.int32)[None, :]
    pair_low = pair_map.astype(jnp.bfloat16)
    token_map = jnp.sum(
        pair_map.reshape(token_count, top_count, slot_count).astype(jnp.int32), axis=1
    ).astype(jnp.bfloat16)
    outgoing = jnp.einsum(
        "tc,td->cd", token_map, low_two, preferred_element_type=jnp.float32
    ).astype(jnp.bfloat16)
    incoming = lax.all_to_all(
        outgoing.reshape(expert_count, capacity, model_width),
        "ctx",
        split_axis=0,
        concat_axis=1,
        tiled=True,
    )
    expert_in, expert_out = (
        lax.all_gather(w_expert_in, "fsdp", axis=1, tiled=True),
        lax.all_gather(w_expert_out, "fsdp", axis=1, tiled=True),
    )
    expert_pre = jnp.einsum("erd,edf->erf", incoming, expert_in, preferred_element_type=jnp.float32)
    expert_hid = swiglu(expert_pre, FE).astype(jnp.bfloat16)
    expert_res = jnp.einsum(
        "erf,efd->erd", expert_hid, expert_out, preferred_element_type=jnp.float32
    ).astype(jnp.bfloat16)
    returned = lax.all_to_all(expert_res, "ctx", split_axis=1, concat_axis=0, tiled=True).reshape(
        slot_count, model_width
    )
    pair_vals = jnp.dot(pair_low, returned, preferred_element_type=jnp.float32).reshape(
        token_count, top_count, model_width
    )
    routed = jnp.sum(gate_vals[..., None] * pair_vals, axis=1)
    output = (
        (residual + shared_scale[:, None] * shared_res + routed)
        .astype(jnp.bfloat16)
        .reshape(tokens.shape)
    )
    grad_out = cotangent.reshape(token_count, model_width).astype(jnp.float32)
    pair_grads = gate_vals[..., None] * grad_out[:, None, :]
    grad_gates = jnp.sum(grad_out[:, None, :] * pair_vals, axis=-1)
    grad_returned = jnp.einsum(
        "pc,pd->cd",
        pair_map.astype(jnp.float32),
        pair_grads.reshape(token_count * top_count, model_width),
        precision=HIGHEST,
    ).astype(jnp.bfloat16)
    grad_res = lax.all_to_all(
        grad_returned.reshape(expert_count, capacity, model_width),
        "ctx",
        split_axis=0,
        concat_axis=1,
        tiled=True,
    )
    grad_expert_out = jnp.einsum(
        "erf,erd->efd", expert_hid, grad_res, preferred_element_type=jnp.float32
    )
    grad_hid = jnp.einsum("erd,efd->erf", grad_res, expert_out, preferred_element_type=jnp.float32)
    grad_pre = swiglu_back(expert_pre, FE, grad_hid).astype(jnp.bfloat16)
    grad_expert_in = jnp.einsum(
        "erd,erf->edf", incoming, grad_pre, preferred_element_type=jnp.float32
    )
    grad_incoming = jnp.einsum(
        "erf,edf->erd", grad_pre, expert_in, preferred_element_type=jnp.float32
    ).astype(jnp.bfloat16)
    grad_outgoing = lax.all_to_all(
        grad_incoming, "ctx", split_axis=1, concat_axis=0, tiled=True
    ).reshape(slot_count, model_width)
    expert_grads = (
        lax.psum_scatter(
            grad_expert_in.astype(jnp.bfloat16), "fsdp", scatter_dimension=1, tiled=True
        ).astype(jnp.float32),
        lax.psum_scatter(
            grad_expert_out.astype(jnp.bfloat16), "fsdp", scatter_dimension=1, tiled=True
        ).astype(jnp.float32),
    )
    grad_two = jnp.einsum("tc,cd->td", token_map, grad_outgoing, preferred_element_type=jnp.float32)
    grad_probs = jnp.sum(jnp.where(chosen_mask, grad_gates[..., None], 0.0), axis=1)
    grad_logits = (
        router_probs * (grad_probs - jnp.sum(router_probs * grad_probs, axis=-1, keepdims=True))
    ).astype(jnp.bfloat16)
    grad_router = jnp.einsum("td,te->de", low_two, grad_logits, preferred_element_type=jnp.float32)
    grad_shared_res = (shared_scale[:, None] * grad_out).astype(jnp.bfloat16)
    grad_gate_pre = (
        jnp.sum(grad_out * shared_res, axis=-1) * shared_scale * (1.0 - shared_scale)
    ).astype(jnp.bfloat16)
    grad_shared_out = jnp.einsum(
        "tf,td->fd", shared_hid, grad_shared_res, preferred_element_type=jnp.float32
    )
    grad_shared_hid = jnp.einsum(
        "td,fd->tf", grad_shared_res, shared_out, preferred_element_type=jnp.float32
    )
    grad_shared_pre = swiglu_back(shared_pre, FS, grad_shared_hid).astype(jnp.bfloat16)
    grad_shared_in = jnp.einsum(
        "td,tf->df", low_two, grad_shared_pre, preferred_element_type=jnp.float32
    )
    grad_gate_vector = jnp.einsum(
        "td,t->d", low_two, grad_gate_pre, preferred_element_type=jnp.float32
    )
    grad_two = grad_two + jnp.einsum(
        "te,de->td", grad_logits, router_weight, preferred_element_type=jnp.float32
    )
    grad_two = grad_two + jnp.einsum(
        "tf,df->td", grad_shared_pre, shared_in, preferred_element_type=jnp.float32
    )
    grad_two = (
        grad_two
        + grad_gate_pre.astype(jnp.float32)[:, None] * gate_vector.astype(jnp.float32)[None, :]
    )
    grad_resid_norm, grad_gain_two = rms_back(
        residual, inv_two, ffn_gain.astype(jnp.float32), grad_two
    )
    grad_resid = grad_out + grad_resid_norm
    ffn_grads = (
        lax.psum_scatter(grad_gain_two, ("ctx", "fsdp"), scatter_dimension=0, tiled=True),
        lax.psum_scatter(grad_router, ("ctx", "fsdp"), scatter_dimension=0, tiled=True),
        lax.psum_scatter(grad_gate_vector, ("ctx", "fsdp"), scatter_dimension=0, tiled=True),
        lax.psum_scatter(grad_shared_in, ("ctx", "fsdp"), scatter_dimension=0, tiled=True),
        lax.psum_scatter(grad_shared_out, ("ctx", "fsdp"), scatter_dimension=0, tiled=True),
    )
    grad_mixed = grad_resid.astype(jnp.bfloat16)
    grad_out_weight = jnp.einsum(
        "tc,td->cd", attn_low, grad_mixed, preferred_element_type=jnp.float32
    )
    grad_attn = (
        jnp.einsum("td,cd->tc", grad_mixed, out_weight, preferred_element_type=jnp.float32)
        .astype(jnp.bfloat16)
        .reshape(head_shape)
    )

    def delta_step(summed, key_part):
        key_blk, value_blk, pos_blk, seg_blk = key_part
        weights = jnp.exp(score_block(key_blk, pos_blk, seg_blk)[0] - log_total[..., None])
        grad_weights = jnp.einsum(
            "qhd,khd->hqk", grad_attn, value_blk, preferred_element_type=jnp.float32
        )
        return (summed + jnp.sum(weights * grad_weights, axis=-1), None)

    delta_sum, unused = lax.scan(
        delta_step, jnp.zeros((head_count, token_count), jnp.float32), key_stack
    )

    def grad_step(summed, key_part):
        key_blk, value_blk, pos_blk, seg_blk = key_part
        scores, allowed = score_block(key_blk, pos_blk, seg_blk)
        weights = jnp.exp(scores - log_total[..., None])
        grad_weights = jnp.einsum(
            "qhd,khd->hqk", grad_attn, value_blk, preferred_element_type=jnp.float32
        )
        grad_scores = jnp.where(
            allowed[None], weights * (grad_weights - delta_sum[..., None]), 0.0
        ).astype(jnp.bfloat16)
        summed = (
            summed
            + jnp.einsum("hqk,khd->qhd", grad_scores, key_blk, preferred_element_type=jnp.float32)
            * score_scale
        )
        grad_key = (
            jnp.einsum("hqk,qhd->khd", grad_scores, queries, preferred_element_type=jnp.float32)
            * score_scale
        )
        grad_value = jnp.einsum(
            "hqk,qhd->khd",
            weights.astype(jnp.bfloat16),
            grad_attn,
            preferred_element_type=jnp.float32,
        )
        return (summed, (grad_key, grad_value))

    grad_query, (grad_keys, grad_values) = lax.scan(
        grad_step, jnp.zeros(head_shape, jnp.float32), key_stack
    )
    grad_keys_own, grad_values_own = (
        lax.psum_scatter(
            grad_keys.reshape(2, half_len, model_width).astype(jnp.bfloat16),
            "ctx",
            scatter_dimension=1,
            tiled=True,
        ).astype(jnp.float32),
        lax.psum_scatter(
            grad_values.reshape(2, half_len, model_width).astype(jnp.bfloat16),
            "ctx",
            scatter_dimension=1,
            tiled=True,
        ).astype(jnp.float32),
    )
    grad_q_rows = rotate_back(grad_query, cos_tab, sine_tab).reshape(token_count, model_width)
    grad_k_rows = rotate_back(grad_keys_own.reshape(head_shape), cos_tab, sine_tab).reshape(
        token_count, model_width
    )
    grad_projected = jnp.concatenate(
        [grad_q_rows, grad_k_rows, grad_values_own.reshape(token_count, model_width)], axis=-1
    ).astype(jnp.bfloat16)
    grad_qkv_weight = jnp.einsum(
        "td,te->de", normed_low, grad_projected, preferred_element_type=jnp.float32
    )
    grad_qkv_bias = jnp.sum(grad_projected.astype(jnp.float32), axis=0)
    grad_normed = jnp.einsum(
        "te,de->td", grad_projected, qkv_weight, preferred_element_type=jnp.float32
    )
    grad_inputs_norm, grad_gain_one = rms_back(
        inputs, inv_one, attn_gain.astype(jnp.float32), grad_normed
    )
    grad_tokens = (grad_resid + grad_inputs_norm).reshape(tokens.shape)
    attn_grads = (
        lax.psum_scatter(grad_qkv_weight, ("ctx", "fsdp"), scatter_dimension=0, tiled=True),
        lax.psum_scatter(grad_qkv_bias, ("ctx", "fsdp"), scatter_dimension=0, tiled=True),
        lax.psum_scatter(grad_out_weight, ("ctx", "fsdp"), scatter_dimension=0, tiled=True),
        lax.psum_scatter(grad_gain_one, ("ctx", "fsdp"), scatter_dimension=0, tiled=True),
    )
    return (
        output,
        grad_tokens,
        attn_grads[0],
        attn_grads[1],
        attn_grads[2],
        attn_grads[3],
        ffn_grads[0],
        ffn_grads[1],
        ffn_grads[2],
        ffn_grads[3],
        ffn_grads[4],
        expert_grads[0],
        expert_grads[1],
    )


def solution(mesh):
    in_specs = (
        P("fsdp", None, "ctx", None),
        P("fsdp", None, None),
        P("fsdp", None, "ctx", None),
        P("fsdp", None, "ctx", None),
        P(("ctx", "fsdp"), None),
        P(("ctx", "fsdp")),
        P(("ctx", "fsdp"), None),
        P(("ctx", "fsdp")),
        P(("ctx", "fsdp")),
        P(("ctx", "fsdp"), None),
        P(("ctx", "fsdp")),
        P(("ctx", "fsdp"), None),
        P(("ctx", "fsdp"), None),
        P("ctx", "fsdp", None),
        P("ctx", "fsdp", None),
    )
    out_specs = (
        P("fsdp", None, "ctx", None),
        P("fsdp", None, "ctx", None),
        P(("ctx", "fsdp"), None),
        P(("ctx", "fsdp")),
        P(("ctx", "fsdp"), None),
        P(("ctx", "fsdp")),
        P(("ctx", "fsdp")),
        P(("ctx", "fsdp"), None),
        P(("ctx", "fsdp")),
        P(("ctx", "fsdp"), None),
        P(("ctx", "fsdp"), None),
        P("ctx", "fsdp", None),
        P("ctx", "fsdp", None),
    )
    ctx_size = mesh.shape["ctx"]
    fsdp_size = mesh.shape["fsdp"]

    def local(*arrays):
        if HEADS % ctx_size:
            return local_wide(*arrays)
        return local_split(ctx_size, fsdp_size, *arrays)

    return jax.shard_map(local, mesh=mesh, in_specs=in_specs, out_specs=out_specs, check_vma=False)
```

```python
import jax
import jax.numpy as jnp
from jax import lax
from jax.sharding import PartitionSpec as P

HD = 128
HEADS = 16
FS = 5632
FE = 1408


RMS_EPS = 1e-06
ROPE_THETA = 1000000.0
MASK_FILL = -1e30
HIGHEST = lax.Precision.HIGHEST


def rope_tables(positions, head_dim):
    half_dim = head_dim // 2
    inv_freq = ROPE_THETA ** (-(jnp.arange(half_dim, dtype=jnp.float32) * 2.0 / head_dim))
    angles = positions.astype(jnp.float32)[:, None] * inv_freq[None, :]
    cos_tab = jnp.concatenate([jnp.cos(angles), jnp.cos(angles)], axis=-1)
    sine_tab = jnp.concatenate([jnp.sin(angles), jnp.sin(angles)], axis=-1)
    return (cos_tab, sine_tab)


def rotate(values, cos_tab, sine_tab):
    half_dim = values.shape[-1] // 2
    turned = jnp.concatenate([-values[..., half_dim:], values[..., :half_dim]], axis=-1)
    return values * cos_tab[:, None, :] + turned * sine_tab[:, None, :]


def rotate_back(upstream, cos_tab, sine_tab):
    half_dim = upstream.shape[-1] // 2
    scaled = upstream * sine_tab[:, None, :]
    return upstream * cos_tab[:, None, :] + jnp.concatenate(
        [scaled[..., half_dim:], -scaled[..., :half_dim]], axis=-1
    )


def rms_norm(values, gain_vec):
    inv_rms = lax.rsqrt(jnp.mean(values * values, axis=-1, keepdims=True) + RMS_EPS)
    return (values * inv_rms * gain_vec, inv_rms)


def rms_back(values, inv_rms, gain_vec, upstream):
    weighted = upstream * gain_vec
    inner_mean = jnp.mean(weighted * values, axis=-1, keepdims=True)
    return (
        inv_rms * weighted - values * inv_rms * inv_rms * inv_rms * inner_mean,
        jnp.sum(upstream * values * inv_rms, axis=0),
    )


def swiglu(pre_act, split_at):
    return jax.nn.silu(pre_act[..., :split_at]) * pre_act[..., split_at:]


def swiglu_back(pre_act, split_at, upstream):
    gate_part = pre_act[..., :split_at]
    up_part = pre_act[..., split_at:]
    sigmoid_g = jax.nn.sigmoid(gate_part)
    d_gate = upstream * up_part * sigmoid_g * (1.0 + gate_part * (1.0 - sigmoid_g))
    d_up = upstream * gate_part * sigmoid_g
    return jnp.concatenate([d_gate, d_up], axis=-1)


def ring_order(size):
    return list(range(0, size, 2)) + list(range(size - 1, 0, -2))


def ring_steps(size):
    order = ring_order(size)
    ahead = [(order[i], order[(i + 1) % size]) for i in range(size)]
    back = [(dst, src) for src, dst in ahead]
    return (ahead, back)


def ring_peers(size, ctx_index):
    order = ring_order(size)
    place = {dev: i for i, dev in enumerate(order)}
    table = jnp.array(
        [[order[(place[dev] + k) % size] for k in range(size)] for dev in range(size)], jnp.int32
    )
    row = lax.dynamic_index_in_dim(table, ctx_index, 0, keepdims=False)
    return [row[k] for k in range(size)]


def after(value, *deps):
    return lax.optimization_barrier((value,) + deps)


def ring_gather(block, size, ctx_index, rider=None):
    rows, width = block.shape

    def put(out, piece, peer, offset):
        return lax.dynamic_update_slice(out, piece, (peer * rows + offset, jnp.zeros_like(peer)))

    out = jnp.zeros((size * rows, width), block.dtype)
    ahead, back = ring_steps(size)
    peers = ring_peers(size, ctx_index)
    half = size // 2
    out = put(out, block, ctx_index, 0)
    fore = rear = block
    for k in range(1, half):
        fore = lax.ppermute(fore, "ctx", ahead)
        rear = lax.ppermute(rear, "ctx", back)
        if rider is not None and k == 2:
            fore, rider = after(fore, rider)
        out = put(out, fore, peers[size - k], 0)
        out = put(out, rear, peers[k], 0)
    fore = lax.ppermute(fore[: rows // 2], "ctx", ahead)
    rear = lax.ppermute(rear[rows // 2 :], "ctx", back)
    out = put(out, fore, peers[half], 0)
    out = put(out, rear, peers[half], rows // 2)
    return out if rider is None else (out, rider)


def ring_sums(parts, size, ctx_index):
    f32 = jnp.float32
    rows = parts.shape[0] // size
    ahead, back = ring_steps(size)
    peers = ring_peers(size, ctx_index)
    half = size // 2

    def own(k, start, count):
        first = (peers[k % size] * rows + start, jnp.zeros_like(peers[0]))
        return lax.dynamic_slice(parts, first, (count, parts.shape[1])).astype(f32)

    def low(values):
        return values.astype(jnp.bfloat16)

    cut = rows // 2
    fore = lax.ppermute(low(own(half, 0, cut)), "ctx", ahead)
    rear = lax.ppermute(low(own(half, cut, cut)), "ctx", back)
    fore = jnp.concatenate(
        [low(fore.astype(f32) + own(half - 1, 0, cut)), low(own(half - 1, cut, cut))], axis=0
    )
    rear = jnp.concatenate(
        [low(own(1 - half, 0, cut)), low(rear.astype(f32) + own(1 - half, cut, cut))], axis=0
    )
    for k in range(half - 1, 0, -1):
        fore = lax.ppermute(fore, "ctx", ahead)
        rear = lax.ppermute(rear, "ctx", back)
        if k > 1:
            fore = low(fore.astype(f32) + own(k - 1, 0, rows))
            rear = low(rear.astype(f32) + own(1 - k, 0, rows))
    return (fore, rear)


def ring_scatter(parts, size, ctx_index, kept=None):
    fore, rear = ring_sums(parts, size, ctx_index)
    kept = (parts if kept is None else kept).reshape(size, -1, parts.shape[1])
    kept = lax.dynamic_index_in_dim(kept, ctx_index, 0, keepdims=False)
    return kept.astype(jnp.float32) + fore.astype(jnp.float32) + rear.astype(jnp.float32)


def other_core(size):
    return [(i, i ^ 1) for i in range(size)]


def other_chip(size):
    return [(i, i ^ 2) for i in range(size)]


def fsdp_gather(shard, size, hold):
    index = lax.axis_index("fsdp")
    rows, width = shard.shape
    far = lax.ppermute(shard, "fsdp", other_chip(size))
    far, hold = after(far, hold)
    pair = jnp.where(
        index < 2, jnp.stack([shard, far], axis=0), jnp.stack([far, shard], axis=0)
    )
    near = lax.ppermute(pair, "fsdp", other_core(size))
    out = jnp.zeros((2, 2, rows, width), shard.dtype)
    out = lax.dynamic_update_index_in_dim(out, pair, index % 2, 1)
    out = lax.dynamic_update_index_in_dim(out, near, 1 - index % 2, 1)
    return (out.reshape(size * rows, width), hold)


def column_pieces(weight, groups, size, extra):
    rows = weight.shape[0]
    width = weight.shape[1] // (groups * size)
    pieces = weight.reshape(rows, groups, size, width).transpose(2, 0, 1, 3)
    pieces = pieces.reshape(size, rows, groups * width)
    if extra is not None:
        count = extra.shape[0]
        more = -(-count // (groups * width * 16)) * 16
        extra = jnp.pad(extra, (0, more * groups * width - count))
        extra = jnp.broadcast_to(
            extra.reshape(1, more, groups * width), (size, more, groups * width)
        )
        pieces = jnp.concatenate([pieces, extra], axis=1)
    return lax.all_to_all(pieces, "ctx", split_axis=0, concat_axis=0, tiled=True)


def merge_columns(pieces, groups, size):
    width = pieces.shape[2] // groups
    if width % 128 == 0:
        pieces = pieces.reshape(size, -1, groups, width).transpose(1, 2, 0, 3)
        return pieces.reshape(-1, groups * size * width).astype(jnp.float32)
    columns = [
        pieces[peer, :, group * width : (group + 1) * width]
        for group in range(groups)
        for peer in range(size)
    ]
    return jnp.concatenate(columns, axis=1).astype(jnp.float32)


def local_split(
    ctx_size,
    fsdp_size,
    tokens,
    segments,
    routes,
    cotangent,
    w_qkv,
    b_qkv,
    w_out,
    gain_attn,
    gain_ffn,
    w_router,
    w_shared_gate,
    w_shared_in,
    w_shared_out,
    w_expert_in,
    w_expert_out,
):
    bf16, f32, i32 = jnp.bfloat16, jnp.float32, jnp.int32
    device_count = ctx_size * fsdp_size
    block_len = tokens.shape[2]
    width = tokens.shape[3]
    token_count = 2 * block_len
    top_count = routes.shape[3]
    seq_len = token_count * ctx_size
    ctx_index = lax.axis_index("ctx")
    expert_count = w_router.shape[1]
    capacity = token_count * top_count // expert_count
    own_heads = HEADS // ctx_size
    own_width = own_heads * HD
    fs_own = FS // ctx_size
    score_scale = HD ** (-0.5)

    def dot(a, b):
        return jnp.dot(a, b, preferred_element_type=f32)

    def dot_t(a, b):
        return lax.dot_general(a, b, (((1,), (1,)), ((), ())), preferred_element_type=f32)

    def t_dot(a, b):
        return lax.dot_general(a, b, (((0,), (0,)), ((), ())), preferred_element_type=f32)

    def own_rows(values):
        return lax.dynamic_index_in_dim(
            values.reshape((ctx_size, token_count) + values.shape[1:]), ctx_index, 0, keepdims=False
        )

    def sum_rows(grad):
        return lax.psum_scatter(grad.astype(bf16), "fsdp", scatter_dimension=0, tiled=True)

    shard = width // device_count
    small = [gain_attn, gain_ffn, w_shared_gate, w_router.reshape(-1), b_qkv]
    small_size = sum(piece.shape[0] for piece in small)
    small = jnp.concatenate(small + [routes.astype(bf16).reshape(-1)], axis=0)
    small_count = small.shape[0]
    own_tokens = tokens.reshape(token_count, width).astype(f32)
    own_scaled, inv_one = rms_norm(own_tokens, 1.0)
    scaled_rows = ring_gather(own_scaled.astype(bf16), ctx_size, ctx_index)
    expert_out = lax.all_gather(w_expert_out[0], "fsdp", axis=0, tiled=True)
    pieces = column_pieces(w_qkv, 3, ctx_size, small)
    pieces = lax.all_gather(pieces, "fsdp", axis=0, tiled=False).transpose(1, 0, 2, 3)
    qkv_weight = pieces[:, :, :shard].reshape(width, 3 * own_width)
    small = pieces[:, :, shard:].reshape(device_count, -1)[:, :small_count]
    attn_gain = small[:, :shard].reshape(width).astype(f32)
    ffn_gain = small[:, shard : 2 * shard].reshape(width).astype(f32)
    gate_vector = small[:, 2 * shard : 3 * shard].reshape(width)
    router_end = 3 * shard + shard * expert_count
    router_weight = small[:, 3 * shard : router_end].reshape(width, expert_count)
    bias = small[:, router_end:small_size].reshape(3, ctx_size, own_width).astype(f32)
    bias = lax.dynamic_index_in_dim(bias, ctx_index, 1, keepdims=False).reshape(3 * own_width)
    route_rows = small[:, small_size:].astype(i32)
    route_rows = lax.dynamic_index_in_dim(
        route_rows.reshape(ctx_size, fsdp_size, -1), lax.axis_index("fsdp"), 1, keepdims=False
    ).reshape(ctx_size, token_count, top_count)

    expert_in = lax.all_gather(w_expert_in[0], "fsdp", axis=0, tiled=True)

    block_ids = jnp.arange(ctx_size, dtype=i32)[:, None]
    local_index = jnp.arange(block_len, dtype=i32)[None, :]
    positions = jnp.stack(
        [
            block_ids * block_len + local_index,
            seq_len - (block_ids + 1) * block_len + local_index,
        ],
        axis=1,
    ).reshape(seq_len)
    seg_rows = (
        segments.reshape(2, ctx_size, block_len).transpose(1, 0, 2).reshape(seq_len)
    )
    cos_tab, sine_tab = rope_tables(positions, HD)

    normed_low = (scaled_rows.astype(f32) * attn_gain).astype(bf16)
    projected = dot(normed_low, qkv_weight) + bias
    head_shape = (seq_len, own_heads, HD)
    queries = rotate(projected[:, :own_width].reshape(head_shape), cos_tab, sine_tab).astype(bf16)
    keys = rotate(
        projected[:, own_width : 2 * own_width].reshape(head_shape), cos_tab, sine_tab
    ).astype(bf16)
    values = projected[:, 2 * own_width :].reshape(head_shape).astype(bf16)
    queries, in_shard = after(queries, w_shared_in)
    shared_in = column_pieces(in_shard, 2, ctx_size, None)
    out_weight, queries = fsdp_gather(w_out, fsdp_size, queries)
    allowed = (positions[None, :] <= positions[:, None]) & (seg_rows[None, :] == seg_rows[:, None])
    scores = jnp.einsum("qhd,khd->hqk", queries, keys, preferred_element_type=f32) * score_scale
    scores = jnp.where(allowed[None], scores, MASK_FILL)
    top_score = jnp.max(scores, axis=-1, keepdims=True)
    log_total = top_score + jnp.log(jnp.sum(jnp.exp(scores - top_score), axis=-1, keepdims=True))
    weights = jnp.exp(scores - log_total)
    weights_low = weights.astype(bf16)
    attended = jnp.einsum("hqk,khd->qhd", weights_low, values, preferred_element_type=f32)
    attn_own = attended.astype(bf16).reshape(seq_len, own_width)
    shared_out, attn_own = fsdp_gather(w_shared_out, fsdp_size, attn_own)
    attn_parts, shared_in = after(dot(attn_own, out_weight).astype(bf16), shared_in)
    shared_in = lax.all_gather(shared_in, "fsdp", axis=0, tiled=False)
    own_residual = own_tokens + ring_scatter(attn_parts, ctx_size, ctx_index)

    normed_two, inv_two = rms_norm(own_residual, ffn_gain)
    own_low = normed_two.astype(bf16)
    low_two, grad_rows = ring_gather(
        own_low, ctx_size, ctx_index, cotangent.reshape(token_count, width)
    )
    grad_rows = lax.all_gather(grad_rows, "ctx", axis=0, tiled=True)
    mixed_weight = jnp.concatenate([router_weight, gate_vector[:, None]], axis=1)
    logits = dot(low_two, mixed_weight)
    probs_all = jax.nn.softmax(logits[:, :expert_count], axis=-1)
    scale_all = jax.nn.sigmoid(logits[:, expert_count])
    gate_all = lax.dynamic_index_in_dim(probs_all, ctx_index, 1, keepdims=False)

    named = jnp.any(route_rows == ctx_index, axis=-1)
    before = jnp.arange(token_count)[:, None] < jnp.arange(token_count)[None, :]
    rank = dot(named.astype(bf16), before.astype(bf16)).astype(i32)
    slot_of = jnp.where(named & (rank < capacity), rank, -1)
    slot_mask = slot_of[:, None, :] == jnp.arange(capacity, dtype=i32)[None, :, None]
    slot_map = slot_mask.astype(bf16)
    blocks_two = low_two.reshape(ctx_size, token_count, width)
    gate_blocks = gate_all.reshape(ctx_size, token_count)

    def to_slots(blocks):
        picked = jnp.einsum("bmt,btd->bmd", slot_map, blocks, preferred_element_type=f32)
        return picked.reshape(ctx_size * capacity, width)

    def to_tokens(slots):
        spread = jnp.einsum(
            "bmt,bmd->btd",
            slot_map,
            slots.reshape(ctx_size, capacity, width),
            preferred_element_type=f32,
        )
        return spread.reshape(seq_len, width)

    buffer = to_slots(blocks_two).astype(bf16)
    expert_pre = dot(buffer, expert_in)
    expert_hid = swiglu(expert_pre, FE).astype(bf16)
    expert_res = dot(expert_hid, expert_out).astype(bf16)
    routed = gate_all[:, None] * to_tokens(expert_res)

    shared_in, expert_res = after(shared_in, expert_res)
    shared_in = shared_in.transpose(1, 0, 2, 3).reshape(width, 2 * fs_own)
    shared_pre = dot(low_two, shared_in)
    shared_hid = swiglu(shared_pre, fs_own).astype(bf16)
    shared_res = dot(shared_hid, shared_out)
    grad_rows, shared_res = after(grad_rows, shared_res)
    out_parts = (scale_all[:, None] * shared_res + routed).astype(bf16)

    grad_slots = to_slots(grad_rows.reshape(ctx_size, token_count, width))
    gate_slots = jnp.sum(jnp.where(slot_mask, gate_blocks[:, None, :], 0.0), axis=-1).reshape(-1, 1)
    grad_res = (gate_slots * grad_slots).astype(bf16)
    slot_dots = jnp.sum(grad_slots * expert_res.astype(f32), axis=-1).reshape(ctx_size, capacity, 1)
    grad_gates = jnp.sum(jnp.where(slot_mask, slot_dots, 0.0), axis=1)
    grad_hid = dot_t(grad_res, expert_out)
    grad_pre = swiglu_back(expert_pre, FE, grad_hid).astype(bf16)
    grad_expert_in = t_dot(buffer, grad_pre)
    grad_buffer = dot_t(grad_pre, expert_in).astype(bf16)

    grad_f32 = grad_rows.astype(f32)
    grad_expert_in, grad_shared_res = after(
        grad_expert_in.astype(bf16), (scale_all[:, None] * grad_f32).astype(bf16)
    )
    sum_expert_in = sum_rows(grad_expert_in)

    gate_dots = jnp.sum(grad_f32 * shared_res, axis=-1).reshape(ctx_size, token_count)
    grad_shared_hid = dot_t(grad_shared_res, shared_out)
    grad_shared_pre = swiglu_back(shared_pre, fs_own, grad_shared_hid).astype(bf16)
    two_parts = (dot_t(grad_shared_pre, shared_in) + to_tokens(grad_buffer)).astype(bf16)
    two_parts, expert_hid, shared_hid, grad_shared_pre = after(
        two_parts, expert_hid, shared_hid, grad_shared_pre
    )
    grad_expert_out = t_dot(expert_hid, grad_res).astype(bf16)
    grad_shared_out = t_dot(shared_hid, grad_shared_res).astype(bf16)
    grad_shared_in = t_dot(low_two, grad_shared_pre).astype(bf16)
    grad_two = ring_scatter(two_parts, ctx_size, ctx_index)
    dots = jnp.stack([grad_gates, gate_dots], axis=1)
    dots = lax.all_to_all(dots, "ctx", split_axis=0, concat_axis=0, tiled=True)
    grad_two, grad_shared_in, grad_shared_out, grad_expert_out, dots = after(
        grad_two, grad_shared_in, grad_shared_out, grad_expert_out, dots
    )
    sum_shared_in = grad_shared_in.reshape(ctx_size, fsdp_size, shard, 2 * fs_own)
    sum_shared_in = lax.psum_scatter(
        sum_shared_in.transpose(1, 0, 2, 3).reshape(width, 2 * fs_own),
        "fsdp",
        scatter_dimension=0,
        tiled=True,
    ).reshape(ctx_size, shard, 2 * fs_own)
    sum_shared_out = sum_rows(grad_shared_out)
    sum_expert_out = sum_rows(grad_expert_out)
    own_probs = own_rows(probs_all)
    own_scale = own_rows(scale_all)
    own_chosen = routes.reshape(token_count, top_count)
    chosen_mask = jnp.any(
        own_chosen[..., None] == jnp.arange(expert_count, dtype=i32), axis=1
    )
    grad_probs = jnp.where(chosen_mask, dots[:, 0].T, 0.0)
    grad_logits = (
        own_probs * (grad_probs - jnp.sum(own_probs * grad_probs, axis=-1, keepdims=True))
    ).astype(bf16)
    grad_gate_pre = (jnp.sum(dots[:, 1], axis=0) * own_scale * (1.0 - own_scale)).astype(bf16)
    grad_router = t_dot(own_low, grad_logits)
    grad_gate_vector = t_dot(own_low, grad_gate_pre[:, None])
    grad_two = grad_two + dot_t(grad_logits, router_weight)
    grad_two = grad_two + grad_gate_pre.astype(f32)[:, None] * gate_vector.astype(f32)[None, :]
    grad_resid_norm, grad_gain_two = rms_back(
        own_residual, inv_two, ffn_gain, grad_two
    )
    grad_resid = cotangent.reshape(token_count, width).astype(f32) + grad_resid_norm

    grad_mixed, sum_expert_in = after(grad_resid.astype(bf16), sum_expert_in)
    mixed_all = ring_gather(grad_mixed, ctx_size, ctx_index)
    grad_attn = dot_t(mixed_all, out_weight).astype(bf16).reshape(head_shape)
    grad_attn, sum_shared_in, sum_shared_out = after(grad_attn, sum_shared_in, sum_shared_out)
    sum_shared_in = lax.all_to_all(
        sum_shared_in, "ctx", split_axis=0, concat_axis=0, tiled=True
    )
    grad_weights = jnp.einsum("qhd,khd->hqk", grad_attn, values, preferred_element_type=f32)
    delta = jnp.sum(weights * grad_weights, axis=-1, keepdims=True)
    grad_scores = jnp.where(allowed[None], weights * (grad_weights - delta), 0.0).astype(bf16)
    grad_q = jnp.einsum("hqk,khd->qhd", grad_scores, keys, preferred_element_type=f32) * score_scale
    grad_k = (
        jnp.einsum("hqk,qhd->khd", grad_scores, queries, preferred_element_type=f32) * score_scale
    )
    grad_v = jnp.einsum("hqk,qhd->khd", weights_low, grad_attn, preferred_element_type=f32)
    grad_projected = jnp.concatenate(
        [
            rotate_back(grad_q, cos_tab, sine_tab).reshape(seq_len, own_width),
            rotate_back(grad_k, cos_tab, sine_tab).reshape(seq_len, own_width),
            grad_v.reshape(seq_len, own_width),
        ],
        axis=-1,
    ).astype(bf16)
    grad_projected, sum_expert_out, sum_shared_in = after(
        grad_projected, sum_expert_out, sum_shared_in
    )
    one_sums = dot_t(grad_projected, qkv_weight)
    grad_gain_one = jnp.sum(one_sums * scaled_rows.astype(f32), axis=0)
    one_parts = one_sums.astype(bf16)
    one_kept, grad_projected = after(one_parts, grad_projected)
    one_kept, out_parts = after(one_kept, out_parts)
    output = own_residual + ring_scatter(out_parts, ctx_size, ctx_index)
    output = output.astype(bf16).reshape(tokens.shape)
    grad_normed = ring_scatter(one_parts, ctx_size, ctx_index, one_kept)
    grad_inputs_norm, unused = rms_back(
        own_tokens,
        inv_one,
        attn_gain,
        grad_normed,
    )
    grad_tokens = (grad_resid + grad_inputs_norm).reshape(tokens.shape)
    grad_qkv_weight = t_dot(normed_low, grad_projected)
    grad_bias = jnp.sum(grad_projected.astype(f32), axis=0).reshape(3, 1, own_width)
    grad_bias = jnp.where(
        jnp.arange(ctx_size, dtype=i32)[None, :, None] == ctx_index, grad_bias, 0.0
    )

    grad_out_weight = t_dot(attn_own, mixed_all)
    small_grads = [grad_gain_one, grad_gain_two, grad_gate_vector, grad_router, grad_bias]
    small_grads = jnp.concatenate(
        [piece.reshape(device_count, -1) for piece in small_grads], axis=1
    )
    more = -(-small_size // (3 * own_width * 16)) * 16
    small_grads = jnp.pad(small_grads, ((0, 0), (0, more * 3 * own_width - small_size)))
    pieces = jnp.concatenate(
        [
            grad_qkv_weight.astype(bf16).reshape(ctx_size, fsdp_size, shard, 3 * own_width),
            small_grads.astype(bf16).reshape(ctx_size, fsdp_size, more, 3 * own_width),
        ],
        axis=2,
    )
    pieces = pieces.transpose(1, 0, 2, 3).reshape(-1, 3 * own_width)
    pieces = lax.psum_scatter(pieces, "fsdp", scatter_dimension=0, tiled=True)
    pieces = pieces.reshape(ctx_size, shard + more, 3 * own_width)
    pieces = lax.all_to_all(pieces, "ctx", split_axis=0, concat_axis=0, tiled=True)
    small_grads = jnp.sum(pieces[:, shard:].reshape(ctx_size, -1).astype(f32), axis=0)
    return (
        output,
        grad_tokens,
        merge_columns(pieces[:, :shard], 3, ctx_size),
        small_grads[router_end:small_size],
        sum_rows(grad_out_weight).astype(f32),
        small_grads[:shard],
        small_grads[shard : 2 * shard],
        small_grads[3 * shard : router_end].reshape(shard, expert_count),
        small_grads[2 * shard : 3 * shard],
        merge_columns(sum_shared_in, 2, ctx_size),
        sum_shared_out.astype(f32),
        sum_expert_in.astype(f32)[None],
        sum_expert_out.astype(f32)[None],
    )


def local_wide(
    tokens,
    segments,
    routes,
    cotangent,
    w_qkv,
    b_qkv,
    w_out,
    gain_attn,
    gain_ffn,
    w_router,
    w_shared_gate,
    w_shared_in,
    w_shared_out,
    w_expert_in,
    w_expert_out,
):
    block_len = tokens.shape[2]
    model_width = tokens.shape[3]
    token_count = 2 * block_len
    top_count = routes.shape[3]
    half_len = segments.shape[2]
    seq_len = 2 * half_len
    ctx_index = lax.axis_index("ctx")
    head_count = model_width // HD
    expert_count = w_router.shape[1]
    capacity = token_count * top_count // expert_count
    slot_count = expert_count * capacity
    key_rows = min(512, seq_len)
    key_blocks = seq_len // key_rows
    score_scale = HD ** (-0.5)
    head_shape = (token_count, head_count, HD)
    attn_set = (
        lax.all_gather(w_qkv, ("ctx", "fsdp"), axis=0, tiled=True),
        lax.all_gather(b_qkv, ("ctx", "fsdp"), axis=0, tiled=True),
        lax.all_gather(w_out, ("ctx", "fsdp"), axis=0, tiled=True),
        lax.all_gather(gain_attn, ("ctx", "fsdp"), axis=0, tiled=True),
    )
    qkv_weight, qkv_bias, out_weight, attn_gain = attn_set
    inputs = tokens.reshape(token_count, model_width).astype(jnp.float32)
    normed, inv_one = rms_norm(inputs, attn_gain.astype(jnp.float32))
    normed_low = normed.astype(jnp.bfloat16)
    projected = jnp.dot(
        normed_low, qkv_weight, preferred_element_type=jnp.float32
    ) + qkv_bias.astype(jnp.float32)
    local_index = jnp.arange(block_len, dtype=jnp.int32)
    query_pos = jnp.concatenate(
        [ctx_index * block_len + local_index, seq_len - (ctx_index + 1) * block_len + local_index]
    )
    half_index = jnp.arange(half_len, dtype=jnp.int32)
    key_pos = jnp.concatenate(
        [half_index, seq_len - block_len * (half_index // block_len + 1) + half_index % block_len]
    ).reshape(key_blocks, key_rows)
    key_seg = segments.reshape(key_blocks, key_rows)
    query_seg = lax.dynamic_slice_in_dim(segments[0], ctx_index * block_len, block_len, 1).reshape(
        token_count
    )
    cos_tab, sine_tab = rope_tables(query_pos, HD)
    queries = rotate(projected[:, :model_width].reshape(head_shape), cos_tab, sine_tab).astype(
        jnp.bfloat16
    )
    keys_own = rotate(
        projected[:, model_width : 2 * model_width].reshape(head_shape), cos_tab, sine_tab
    ).astype(jnp.bfloat16)
    values_own = projected[:, 2 * model_width :].astype(jnp.bfloat16)
    keys_all, values_all = (
        lax.all_gather(keys_own.reshape(2, block_len, model_width), "ctx", axis=1, tiled=True),
        lax.all_gather(values_own.reshape(2, block_len, model_width), "ctx", axis=1, tiled=True),
    )
    keys_all = keys_all.reshape(key_blocks, key_rows, head_count, HD)
    values_all = values_all.reshape(key_blocks, key_rows, head_count, HD)

    def score_block(key_blk, pos_blk, seg_blk):
        raw_scores = (
            jnp.einsum("qhd,khd->hqk", queries, key_blk, preferred_element_type=jnp.float32)
            * score_scale
        )
        allowed = (pos_blk[None, :] <= query_pos[:, None]) & (
            seg_blk[None, :] == query_seg[:, None]
        )
        return (jnp.where(allowed[None], raw_scores, MASK_FILL), allowed)

    def total_step(running, key_part):
        run_max, run_sum = running
        scores = score_block(key_part[0], key_part[1], key_part[2])[0]
        new_max = jnp.maximum(run_max, jnp.max(scores, axis=-1))
        run_sum = run_sum * jnp.exp(run_max - new_max) + jnp.sum(
            jnp.exp(scores - new_max[..., None]), axis=-1
        )
        return ((new_max, run_sum), None)

    start_max = jnp.full((head_count, token_count), MASK_FILL, jnp.float32)
    start_sum = jnp.zeros((head_count, token_count), jnp.float32)
    (run_max, run_sum), unused = lax.scan(
        total_step, (start_max, start_sum), (keys_all, key_pos, key_seg)
    )
    log_total = run_max + jnp.log(run_sum)

    def attend_step(summed, key_part):
        key_blk, value_blk, pos_blk, seg_blk = key_part
        scores = score_block(key_blk, pos_blk, seg_blk)[0]
        weights = jnp.exp(scores - log_total[..., None]).astype(jnp.bfloat16)
        return (
            summed
            + jnp.einsum("hqk,khd->qhd", weights, value_blk, preferred_element_type=jnp.float32),
            None,
        )

    key_stack = (keys_all, values_all, key_pos, key_seg)
    attended, unused = lax.scan(attend_step, jnp.zeros(head_shape, jnp.float32), key_stack)
    attn_low = attended.reshape(token_count, model_width).astype(jnp.bfloat16)
    residual = inputs + jnp.dot(attn_low, out_weight, preferred_element_type=jnp.float32)
    ffn_set = (
        lax.all_gather(gain_ffn, ("ctx", "fsdp"), axis=0, tiled=True),
        lax.all_gather(w_router, ("ctx", "fsdp"), axis=0, tiled=True),
        lax.all_gather(w_shared_gate, ("ctx", "fsdp"), axis=0, tiled=True),
        lax.all_gather(w_shared_in, ("ctx", "fsdp"), axis=0, tiled=True),
        lax.all_gather(w_shared_out, ("ctx", "fsdp"), axis=0, tiled=True),
    )
    ffn_gain, router_weight, gate_vector, shared_in, shared_out = ffn_set
    normed_two, inv_two = rms_norm(residual, ffn_gain.astype(jnp.float32))
    low_two = normed_two.astype(jnp.bfloat16)
    logits = jnp.dot(low_two, router_weight, preferred_element_type=jnp.float32)
    router_probs = jax.nn.softmax(logits, axis=-1)
    chosen = routes.reshape(token_count, top_count)
    chosen_mask = chosen[..., None] == jnp.arange(expert_count, dtype=jnp.int32)
    gate_vals = jnp.sum(jnp.where(chosen_mask, router_probs[:, None, :], 0.0), axis=-1)
    shared_scale = jax.nn.sigmoid(jnp.dot(low_two, gate_vector, preferred_element_type=jnp.float32))
    shared_pre = jnp.dot(low_two, shared_in, preferred_element_type=jnp.float32)
    shared_hid = swiglu(shared_pre, FS).astype(jnp.bfloat16)
    shared_res = jnp.dot(shared_hid, shared_out, preferred_element_type=jnp.float32)
    pair_routes = chosen.reshape(token_count * top_count)
    expert_marks = (
        pair_routes[:, None] == jnp.arange(expert_count, dtype=jnp.int32)[None, :]
    ).astype(jnp.int32)
    pair_ranks = jnp.sum((jnp.cumsum(expert_marks, axis=0) - expert_marks) * expert_marks, axis=1)
    pair_target = jnp.where(pair_ranks < capacity, pair_routes * capacity + pair_ranks, -1)
    pair_map = pair_target[:, None] == jnp.arange(slot_count, dtype=jnp.int32)[None, :]
    pair_low = pair_map.astype(jnp.bfloat16)
    token_map = jnp.sum(
        pair_map.reshape(token_count, top_count, slot_count).astype(jnp.int32), axis=1
    ).astype(jnp.bfloat16)
    outgoing = jnp.einsum(
        "tc,td->cd", token_map, low_two, preferred_element_type=jnp.float32
    ).astype(jnp.bfloat16)
    incoming = lax.all_to_all(
        outgoing.reshape(expert_count, capacity, model_width),
        "ctx",
        split_axis=0,
        concat_axis=1,
        tiled=True,
    )
    expert_in, expert_out = (
        lax.all_gather(w_expert_in, "fsdp", axis=1, tiled=True),
        lax.all_gather(w_expert_out, "fsdp", axis=1, tiled=True),
    )
    expert_pre = jnp.einsum("erd,edf->erf", incoming, expert_in, preferred_element_type=jnp.float32)
    expert_hid = swiglu(expert_pre, FE).astype(jnp.bfloat16)
    expert_res = jnp.einsum(
        "erf,efd->erd", expert_hid, expert_out, preferred_element_type=jnp.float32
    ).astype(jnp.bfloat16)
    returned = lax.all_to_all(expert_res, "ctx", split_axis=1, concat_axis=0, tiled=True).reshape(
        slot_count, model_width
    )
    pair_vals = jnp.dot(pair_low, returned, preferred_element_type=jnp.float32).reshape(
        token_count, top_count, model_width
    )
    routed = jnp.sum(gate_vals[..., None] * pair_vals, axis=1)
    output = (
        (residual + shared_scale[:, None] * shared_res + routed)
        .astype(jnp.bfloat16)
        .reshape(tokens.shape)
    )
    grad_out = cotangent.reshape(token_count, model_width).astype(jnp.float32)
    pair_grads = gate_vals[..., None] * grad_out[:, None, :]
    grad_gates = jnp.sum(grad_out[:, None, :] * pair_vals, axis=-1)
    grad_returned = jnp.einsum(
        "pc,pd->cd",
        pair_map.astype(jnp.float32),
        pair_grads.reshape(token_count * top_count, model_width),
        precision=HIGHEST,
    ).astype(jnp.bfloat16)
    grad_res = lax.all_to_all(
        grad_returned.reshape(expert_count, capacity, model_width),
        "ctx",
        split_axis=0,
        concat_axis=1,
        tiled=True,
    )
    grad_expert_out = jnp.einsum(
        "erf,erd->efd", expert_hid, grad_res, preferred_element_type=jnp.float32
    )
    grad_hid = jnp.einsum("erd,efd->erf", grad_res, expert_out, preferred_element_type=jnp.float32)
    grad_pre = swiglu_back(expert_pre, FE, grad_hid).astype(jnp.bfloat16)
    grad_expert_in = jnp.einsum(
        "erd,erf->edf", incoming, grad_pre, preferred_element_type=jnp.float32
    )
    grad_incoming = jnp.einsum(
        "erf,edf->erd", grad_pre, expert_in, preferred_element_type=jnp.float32
    ).astype(jnp.bfloat16)
    grad_outgoing = lax.all_to_all(
        grad_incoming, "ctx", split_axis=1, concat_axis=0, tiled=True
    ).reshape(slot_count, model_width)
    expert_grads = (
        lax.psum_scatter(
            grad_expert_in.astype(jnp.bfloat16), "fsdp", scatter_dimension=1, tiled=True
        ).astype(jnp.float32),
        lax.psum_scatter(
            grad_expert_out.astype(jnp.bfloat16), "fsdp", scatter_dimension=1, tiled=True
        ).astype(jnp.float32),
    )
    grad_two = jnp.einsum("tc,cd->td", token_map, grad_outgoing, preferred_element_type=jnp.float32)
    grad_probs = jnp.sum(jnp.where(chosen_mask, grad_gates[..., None], 0.0), axis=1)
    grad_logits = (
        router_probs * (grad_probs - jnp.sum(router_probs * grad_probs, axis=-1, keepdims=True))
    ).astype(jnp.bfloat16)
    grad_router = jnp.einsum("td,te->de", low_two, grad_logits, preferred_element_type=jnp.float32)
    grad_shared_res = (shared_scale[:, None] * grad_out).astype(jnp.bfloat16)
    grad_gate_pre = (
        jnp.sum(grad_out * shared_res, axis=-1) * shared_scale * (1.0 - shared_scale)
    ).astype(jnp.bfloat16)
    grad_shared_out = jnp.einsum(
        "tf,td->fd", shared_hid, grad_shared_res, preferred_element_type=jnp.float32
    )
    grad_shared_hid = jnp.einsum(
        "td,fd->tf", grad_shared_res, shared_out, preferred_element_type=jnp.float32
    )
    grad_shared_pre = swiglu_back(shared_pre, FS, grad_shared_hid).astype(jnp.bfloat16)
    grad_shared_in = jnp.einsum(
        "td,tf->df", low_two, grad_shared_pre, preferred_element_type=jnp.float32
    )
    grad_gate_vector = jnp.einsum(
        "td,t->d", low_two, grad_gate_pre, preferred_element_type=jnp.float32
    )
    grad_two = grad_two + jnp.einsum(
        "te,de->td", grad_logits, router_weight, preferred_element_type=jnp.float32
    )
    grad_two = grad_two + jnp.einsum(
        "tf,df->td", grad_shared_pre, shared_in, preferred_element_type=jnp.float32
    )
    grad_two = (
        grad_two
        + grad_gate_pre.astype(jnp.float32)[:, None] * gate_vector.astype(jnp.float32)[None, :]
    )
    grad_resid_norm, grad_gain_two = rms_back(
        residual, inv_two, ffn_gain.astype(jnp.float32), grad_two
    )
    grad_resid = grad_out + grad_resid_norm
    ffn_grads = (
        lax.psum_scatter(grad_gain_two, ("ctx", "fsdp"), scatter_dimension=0, tiled=True),
        lax.psum_scatter(grad_router, ("ctx", "fsdp"), scatter_dimension=0, tiled=True),
        lax.psum_scatter(grad_gate_vector, ("ctx", "fsdp"), scatter_dimension=0, tiled=True),
        lax.psum_scatter(grad_shared_in, ("ctx", "fsdp"), scatter_dimension=0, tiled=True),
        lax.psum_scatter(grad_shared_out, ("ctx", "fsdp"), scatter_dimension=0, tiled=True),
    )
    grad_mixed = grad_resid.astype(jnp.bfloat16)
    grad_out_weight = jnp.einsum(
        "tc,td->cd", attn_low, grad_mixed, preferred_element_type=jnp.float32
    )
    grad_attn = (
        jnp.einsum("td,cd->tc", grad_mixed, out_weight, preferred_element_type=jnp.float32)
        .astype(jnp.bfloat16)
        .reshape(head_shape)
    )

    def delta_step(summed, key_part):
        key_blk, value_blk, pos_blk, seg_blk = key_part
        weights = jnp.exp(score_block(key_blk, pos_blk, seg_blk)[0] - log_total[..., None])
        grad_weights = jnp.einsum(
            "qhd,khd->hqk", grad_attn, value_blk, preferred_element_type=jnp.float32
        )
        return (summed + jnp.sum(weights * grad_weights, axis=-1), None)

    delta_sum, unused = lax.scan(
        delta_step, jnp.zeros((head_count, token_count), jnp.float32), key_stack
    )

    def grad_step(summed, key_part):
        key_blk, value_blk, pos_blk, seg_blk = key_part
        scores, allowed = score_block(key_blk, pos_blk, seg_blk)
        weights = jnp.exp(scores - log_total[..., None])
        grad_weights = jnp.einsum(
            "qhd,khd->hqk", grad_attn, value_blk, preferred_element_type=jnp.float32
        )
        grad_scores = jnp.where(
            allowed[None], weights * (grad_weights - delta_sum[..., None]), 0.0
        ).astype(jnp.bfloat16)
        summed = (
            summed
            + jnp.einsum("hqk,khd->qhd", grad_scores, key_blk, preferred_element_type=jnp.float32)
            * score_scale
        )
        grad_key = (
            jnp.einsum("hqk,qhd->khd", grad_scores, queries, preferred_element_type=jnp.float32)
            * score_scale
        )
        grad_value = jnp.einsum(
            "hqk,qhd->khd",
            weights.astype(jnp.bfloat16),
            grad_attn,
            preferred_element_type=jnp.float32,
        )
        return (summed, (grad_key, grad_value))

    grad_query, (grad_keys, grad_values) = lax.scan(
        grad_step, jnp.zeros(head_shape, jnp.float32), key_stack
    )
    grad_keys_own, grad_values_own = (
        lax.psum_scatter(
            grad_keys.reshape(2, half_len, model_width).astype(jnp.bfloat16),
            "ctx",
            scatter_dimension=1,
            tiled=True,
        ).astype(jnp.float32),
        lax.psum_scatter(
            grad_values.reshape(2, half_len, model_width).astype(jnp.bfloat16),
            "ctx",
            scatter_dimension=1,
            tiled=True,
        ).astype(jnp.float32),
    )
    grad_q_rows = rotate_back(grad_query, cos_tab, sine_tab).reshape(token_count, model_width)
    grad_k_rows = rotate_back(grad_keys_own.reshape(head_shape), cos_tab, sine_tab).reshape(
        token_count, model_width
    )
    grad_projected = jnp.concatenate(
        [grad_q_rows, grad_k_rows, grad_values_own.reshape(token_count, model_width)], axis=-1
    ).astype(jnp.bfloat16)
    grad_qkv_weight = jnp.einsum(
        "td,te->de", normed_low, grad_projected, preferred_element_type=jnp.float32
    )
    grad_qkv_bias = jnp.sum(grad_projected.astype(jnp.float32), axis=0)
    grad_normed = jnp.einsum(
        "te,de->td", grad_projected, qkv_weight, preferred_element_type=jnp.float32
    )
    grad_inputs_norm, grad_gain_one = rms_back(
        inputs, inv_one, attn_gain.astype(jnp.float32), grad_normed
    )
    grad_tokens = (grad_resid + grad_inputs_norm).reshape(tokens.shape)
    attn_grads = (
        lax.psum_scatter(grad_qkv_weight, ("ctx", "fsdp"), scatter_dimension=0, tiled=True),
        lax.psum_scatter(grad_qkv_bias, ("ctx", "fsdp"), scatter_dimension=0, tiled=True),
        lax.psum_scatter(grad_out_weight, ("ctx", "fsdp"), scatter_dimension=0, tiled=True),
        lax.psum_scatter(grad_gain_one, ("ctx", "fsdp"), scatter_dimension=0, tiled=True),
    )
    return (
        output,
        grad_tokens,
        attn_grads[0],
        attn_grads[1],
        attn_grads[2],
        attn_grads[3],
        ffn_grads[0],
        ffn_grads[1],
        ffn_grads[2],
        ffn_grads[3],
        ffn_grads[4],
        expert_grads[0],
        expert_grads[1],
    )


def solution(mesh):
    in_specs = (
        P("fsdp", None, "ctx", None),
        P("fsdp", None, None),
        P("fsdp", None, "ctx", None),
        P("fsdp", None, "ctx", None),
        P(("ctx", "fsdp"), None),
        P(("ctx", "fsdp")),
        P(("ctx", "fsdp"), None),
        P(("ctx", "fsdp")),
        P(("ctx", "fsdp")),
        P(("ctx", "fsdp"), None),
        P(("ctx", "fsdp")),
        P(("ctx", "fsdp"), None),
        P(("ctx", "fsdp"), None),
        P("ctx", "fsdp", None),
        P("ctx", "fsdp", None),
    )
    out_specs = (
        P("fsdp", None, "ctx", None),
        P("fsdp", None, "ctx", None),
        P(("ctx", "fsdp"), None),
        P(("ctx", "fsdp")),
        P(("ctx", "fsdp"), None),
        P(("ctx", "fsdp")),
        P(("ctx", "fsdp")),
        P(("ctx", "fsdp"), None),
        P(("ctx", "fsdp")),
        P(("ctx", "fsdp"), None),
        P(("ctx", "fsdp"), None),
        P("ctx", "fsdp", None),
        P("ctx", "fsdp", None),
    )
    ctx_size = mesh.shape["ctx"]
    fsdp_size = mesh.shape["fsdp"]

    def local(*arrays):
        if HEADS % ctx_size:
            return local_wide(*arrays)
        return local_split(ctx_size, fsdp_size, *arrays)

    return jax.shard_map(local, mesh=mesh, in_specs=in_specs, out_specs=out_specs, check_vma=False)
```

```python
import jax
import jax.numpy as jnp
from jax import lax
from jax.sharding import PartitionSpec as P

HD = 128
HEADS = 16
FS = 5632
FE = 1408


RMS_EPS = 1e-06
ROPE_THETA = 1000000.0
MASK_FILL = -1e30
HIGHEST = lax.Precision.HIGHEST


def rope_tables(positions, head_dim):
    half_dim = head_dim // 2
    inv_freq = ROPE_THETA ** (-(jnp.arange(half_dim, dtype=jnp.float32) * 2.0 / head_dim))
    angles = positions.astype(jnp.float32)[:, None] * inv_freq[None, :]
    cos_tab = jnp.concatenate([jnp.cos(angles), jnp.cos(angles)], axis=-1)
    sine_tab = jnp.concatenate([jnp.sin(angles), jnp.sin(angles)], axis=-1)
    return (cos_tab, sine_tab)


def rotate(values, cos_tab, sine_tab):
    half_dim = values.shape[-1] // 2
    turned = jnp.concatenate([-values[..., half_dim:], values[..., :half_dim]], axis=-1)
    return values * cos_tab[:, None, :] + turned * sine_tab[:, None, :]


def rotate_back(upstream, cos_tab, sine_tab):
    half_dim = upstream.shape[-1] // 2
    scaled = upstream * sine_tab[:, None, :]
    return upstream * cos_tab[:, None, :] + jnp.concatenate(
        [scaled[..., half_dim:], -scaled[..., :half_dim]], axis=-1
    )


def rms_norm(values, gain_vec):
    inv_rms = lax.rsqrt(jnp.mean(values * values, axis=-1, keepdims=True) + RMS_EPS)
    return (values * inv_rms * gain_vec, inv_rms)


def rms_back(values, inv_rms, gain_vec, upstream):
    weighted = upstream * gain_vec
    inner_mean = jnp.mean(weighted * values, axis=-1, keepdims=True)
    return (
        inv_rms * weighted - values * inv_rms * inv_rms * inv_rms * inner_mean,
        jnp.sum(upstream * values * inv_rms, axis=0),
    )


def swiglu(pre_act, split_at):
    return jax.nn.silu(pre_act[..., :split_at]) * pre_act[..., split_at:]


def swiglu_back(pre_act, split_at, upstream):
    gate_part = pre_act[..., :split_at]
    up_part = pre_act[..., split_at:]
    sigmoid_g = jax.nn.sigmoid(gate_part)
    d_gate = upstream * up_part * sigmoid_g * (1.0 + gate_part * (1.0 - sigmoid_g))
    d_up = upstream * gate_part * sigmoid_g
    return jnp.concatenate([d_gate, d_up], axis=-1)


def ring_order(size):
    return list(range(0, size, 2)) + list(range(size - 1, 0, -2))


def ring_steps(size):
    order = ring_order(size)
    ahead = [(order[i], order[(i + 1) % size]) for i in range(size)]
    back = [(dst, src) for src, dst in ahead]
    return (ahead, back)


def ring_peers(size, ctx_index):
    order = ring_order(size)
    place = {dev: i for i, dev in enumerate(order)}
    table = jnp.array(
        [[order[(place[dev] + k) % size] for k in range(size)] for dev in range(size)], jnp.int32
    )
    row = lax.dynamic_index_in_dim(table, ctx_index, 0, keepdims=False)
    return [row[k] for k in range(size)]


def after(value, *deps):
    return lax.optimization_barrier((value,) + deps)


def ring_gather(block, size, ctx_index, rider=None):
    rows, width = block.shape

    def put(out, piece, peer, offset):
        return lax.dynamic_update_slice(out, piece, (peer * rows + offset, jnp.zeros_like(peer)))

    out = jnp.zeros((size * rows, width), block.dtype)
    ahead, back = ring_steps(size)
    peers = ring_peers(size, ctx_index)
    half = size // 2
    out = put(out, block, ctx_index, 0)
    fore = rear = block
    for k in range(1, half):
        fore = lax.ppermute(fore, "ctx", ahead)
        rear = lax.ppermute(rear, "ctx", back)
        if rider is not None and k == 2:
            fore, rider = after(fore, rider)
        out = put(out, fore, peers[size - k], 0)
        out = put(out, rear, peers[k], 0)
    fore = lax.ppermute(fore[: rows // 2], "ctx", ahead)
    rear = lax.ppermute(rear[rows // 2 :], "ctx", back)
    out = put(out, fore, peers[half], 0)
    out = put(out, rear, peers[half], rows // 2)
    return out if rider is None else (out, rider)


def ring_sums(parts, size, ctx_index):
    f32 = jnp.float32
    rows = parts.shape[0] // size
    ahead, back = ring_steps(size)
    peers = ring_peers(size, ctx_index)
    half = size // 2

    def own(k, start, count):
        first = (peers[k % size] * rows + start, jnp.zeros_like(peers[0]))
        return lax.dynamic_slice(parts, first, (count, parts.shape[1])).astype(f32)

    def low(values):
        return values.astype(jnp.bfloat16)

    cut = rows // 2
    fore = lax.ppermute(low(own(half, 0, cut)), "ctx", ahead)
    rear = lax.ppermute(low(own(half, cut, cut)), "ctx", back)
    fore = jnp.concatenate(
        [low(fore.astype(f32) + own(half - 1, 0, cut)), low(own(half - 1, cut, cut))], axis=0
    )
    rear = jnp.concatenate(
        [low(own(1 - half, 0, cut)), low(rear.astype(f32) + own(1 - half, cut, cut))], axis=0
    )
    for k in range(half - 1, 0, -1):
        fore = lax.ppermute(fore, "ctx", ahead)
        rear = lax.ppermute(rear, "ctx", back)
        if k > 1:
            fore = low(fore.astype(f32) + own(k - 1, 0, rows))
            rear = low(rear.astype(f32) + own(1 - k, 0, rows))
    return (fore, rear)


def ring_scatter(parts, size, ctx_index, kept=None):
    fore, rear = ring_sums(parts, size, ctx_index)
    kept = (parts if kept is None else kept).reshape(size, -1, parts.shape[1])
    kept = lax.dynamic_index_in_dim(kept, ctx_index, 0, keepdims=False)
    return kept.astype(jnp.float32) + fore.astype(jnp.float32) + rear.astype(jnp.float32)


def other_core(size):
    return [(i, i ^ 1) for i in range(size)]


def other_chip(size):
    return [(i, i ^ 2) for i in range(size)]


def fsdp_gather(shard, size, hold):
    index = lax.axis_index("fsdp")
    rows, width = shard.shape
    far = lax.ppermute(shard, "fsdp", other_chip(size))
    far, hold = after(far, hold)
    pair = jnp.where(
        index < 2, jnp.stack([shard, far], axis=0), jnp.stack([far, shard], axis=0)
    )
    near = lax.ppermute(pair, "fsdp", other_core(size))
    out = jnp.zeros((2, 2, rows, width), shard.dtype)
    out = lax.dynamic_update_index_in_dim(out, pair, index % 2, 1)
    out = lax.dynamic_update_index_in_dim(out, near, 1 - index % 2, 1)
    return (out.reshape(size * rows, width), hold)


def column_pieces(weight, groups, size, extra):
    rows = weight.shape[0]
    width = weight.shape[1] // (groups * size)
    pieces = weight.reshape(rows, groups, size, width).transpose(2, 0, 1, 3)
    pieces = pieces.reshape(size, rows, groups * width)
    if extra is not None:
        count = extra.shape[0]
        more = -(-count // (groups * width * 16)) * 16
        extra = jnp.pad(extra, (0, more * groups * width - count))
        extra = jnp.broadcast_to(
            extra.reshape(1, more, groups * width), (size, more, groups * width)
        )
        pieces = jnp.concatenate([pieces, extra], axis=1)
    return pieces


def merge_columns(pieces, groups, size):
    width = pieces.shape[2] // groups
    if width % 128 == 0:
        pieces = pieces.reshape(size, -1, groups, width).transpose(1, 2, 0, 3)
        return pieces.reshape(-1, groups * size * width).astype(jnp.float32)
    columns = [
        pieces[peer, :, group * width : (group + 1) * width]
        for group in range(groups)
        for peer in range(size)
    ]
    return jnp.concatenate(columns, axis=1).astype(jnp.float32)


def local_split(
    ctx_size,
    fsdp_size,
    tokens,
    segments,
    routes,
    cotangent,
    w_qkv,
    b_qkv,
    w_out,
    gain_attn,
    gain_ffn,
    w_router,
    w_shared_gate,
    w_shared_in,
    w_shared_out,
    w_expert_in,
    w_expert_out,
):
    bf16, f32, i32 = jnp.bfloat16, jnp.float32, jnp.int32
    device_count = ctx_size * fsdp_size
    block_len = tokens.shape[2]
    width = tokens.shape[3]
    token_count = 2 * block_len
    top_count = routes.shape[3]
    seq_len = token_count * ctx_size
    ctx_index = lax.axis_index("ctx")
    expert_count = w_router.shape[1]
    capacity = token_count * top_count // expert_count
    own_heads = HEADS // ctx_size
    own_width = own_heads * HD
    fs_own = FS // ctx_size
    score_scale = HD ** (-0.5)

    def dot(a, b):
        return jnp.dot(a, b, preferred_element_type=f32)

    def dot_t(a, b):
        return lax.dot_general(a, b, (((1,), (1,)), ((), ())), preferred_element_type=f32)

    def t_dot(a, b):
        return lax.dot_general(a, b, (((0,), (0,)), ((), ())), preferred_element_type=f32)

    def own_rows(values):
        return lax.dynamic_index_in_dim(
            values.reshape((ctx_size, token_count) + values.shape[1:]), ctx_index, 0, keepdims=False
        )

    def sum_rows(grad):
        return lax.psum_scatter(grad.astype(bf16), "fsdp", scatter_dimension=0, tiled=True)

    shard = width // device_count
    small = [gain_attn, gain_ffn, w_shared_gate, w_router.reshape(-1), b_qkv]
    small_size = sum(piece.shape[0] for piece in small)
    small = jnp.concatenate(small + [routes.astype(bf16).reshape(-1)], axis=0)
    small_count = small.shape[0]
    own_tokens = tokens.reshape(token_count, width).astype(f32)
    own_scaled, inv_one = rms_norm(own_tokens, 1.0)
    scaled_rows = ring_gather(own_scaled.astype(bf16), ctx_size, ctx_index)
    pieces = column_pieces(w_qkv, 3, ctx_size, small)
    pieces = lax.all_to_all(pieces, "ctx", split_axis=0, concat_axis=0, tiled=True)
    shared_in = column_pieces(w_shared_in, 2, ctx_size, None)
    shared_in, scaled_rows = after(shared_in, scaled_rows)
    shared_in = lax.all_to_all(shared_in, "ctx", split_axis=0, concat_axis=0, tiled=True)
    pieces = lax.all_gather(pieces, "fsdp", axis=0, tiled=False).transpose(1, 0, 2, 3)
    qkv_weight = pieces[:, :, :shard].reshape(width, 3 * own_width)
    small = pieces[:, :, shard:].reshape(device_count, -1)[:, :small_count]
    attn_gain = small[:, :shard].reshape(width).astype(f32)
    ffn_gain = small[:, shard : 2 * shard].reshape(width).astype(f32)
    gate_vector = small[:, 2 * shard : 3 * shard].reshape(width)
    router_end = 3 * shard + shard * expert_count
    router_weight = small[:, 3 * shard : router_end].reshape(width, expert_count)
    bias = small[:, router_end:small_size].reshape(3, ctx_size, own_width).astype(f32)
    bias = lax.dynamic_index_in_dim(bias, ctx_index, 1, keepdims=False).reshape(3 * own_width)
    route_rows = small[:, small_size:].astype(i32)
    route_rows = lax.dynamic_index_in_dim(
        route_rows.reshape(ctx_size, fsdp_size, -1), lax.axis_index("fsdp"), 1, keepdims=False
    ).reshape(ctx_size, token_count, top_count)

    expert_in = lax.all_gather(w_expert_in[0], "fsdp", axis=0, tiled=True)

    block_ids = jnp.arange(ctx_size, dtype=i32)[:, None]
    local_index = jnp.arange(block_len, dtype=i32)[None, :]
    positions = jnp.stack(
        [
            block_ids * block_len + local_index,
            seq_len - (block_ids + 1) * block_len + local_index,
        ],
        axis=1,
    ).reshape(seq_len)
    seg_rows = (
        segments.reshape(2, ctx_size, block_len).transpose(1, 0, 2).reshape(seq_len)
    )
    cos_tab, sine_tab = rope_tables(positions, HD)

    normed_low = (scaled_rows.astype(f32) * attn_gain).astype(bf16)
    projected = dot(normed_low, qkv_weight) + bias
    head_shape = (seq_len, own_heads, HD)
    queries = rotate(projected[:, :own_width].reshape(head_shape), cos_tab, sine_tab).astype(bf16)
    keys = rotate(
        projected[:, own_width : 2 * own_width].reshape(head_shape), cos_tab, sine_tab
    ).astype(bf16)
    values = projected[:, 2 * own_width :].reshape(head_shape).astype(bf16)
    out_weight, queries = fsdp_gather(w_out, fsdp_size, queries)
    allowed = (positions[None, :] <= positions[:, None]) & (seg_rows[None, :] == seg_rows[:, None])
    scores = jnp.einsum("qhd,khd->hqk", queries, keys, preferred_element_type=f32) * score_scale
    scores = jnp.where(allowed[None], scores, MASK_FILL)
    top_score = jnp.max(scores, axis=-1, keepdims=True)
    log_total = top_score + jnp.log(jnp.sum(jnp.exp(scores - top_score), axis=-1, keepdims=True))
    weights = jnp.exp(scores - log_total)
    weights_low = weights.astype(bf16)
    attended = jnp.einsum("hqk,khd->qhd", weights_low, values, preferred_element_type=f32)
    attn_own = attended.astype(bf16).reshape(seq_len, own_width)
    shared_out, attn_own = fsdp_gather(w_shared_out, fsdp_size, attn_own)
    expert_out, attn_own = fsdp_gather(w_expert_out[0], fsdp_size, attn_own)
    attn_parts, shared_in = after(dot(attn_own, out_weight).astype(bf16), shared_in)
    shared_in = lax.all_gather(shared_in, "fsdp", axis=0, tiled=False)
    own_residual = own_tokens + ring_scatter(attn_parts, ctx_size, ctx_index)

    normed_two, inv_two = rms_norm(own_residual, ffn_gain)
    own_low = normed_two.astype(bf16)
    low_two, grad_rows = ring_gather(
        own_low, ctx_size, ctx_index, cotangent.reshape(token_count, width)
    )
    grad_rows = lax.all_gather(grad_rows, "ctx", axis=0, tiled=True)
    mixed_weight = jnp.concatenate([router_weight, gate_vector[:, None]], axis=1)
    logits = dot(low_two, mixed_weight)
    probs_all = jax.nn.softmax(logits[:, :expert_count], axis=-1)
    scale_all = jax.nn.sigmoid(logits[:, expert_count])
    gate_all = lax.dynamic_index_in_dim(probs_all, ctx_index, 1, keepdims=False)

    named = jnp.any(route_rows == ctx_index, axis=-1)
    before = jnp.arange(token_count)[:, None] < jnp.arange(token_count)[None, :]
    rank = dot(named.astype(bf16), before.astype(bf16)).astype(i32)
    slot_of = jnp.where(named & (rank < capacity), rank, -1)
    slot_mask = slot_of[:, None, :] == jnp.arange(capacity, dtype=i32)[None, :, None]
    slot_map = slot_mask.astype(bf16)
    blocks_two = low_two.reshape(ctx_size, token_count, width)
    gate_blocks = gate_all.reshape(ctx_size, token_count)

    def to_slots(blocks):
        picked = jnp.einsum("bmt,btd->bmd", slot_map, blocks, preferred_element_type=f32)
        return picked.reshape(ctx_size * capacity, width)

    def to_tokens(slots):
        spread = jnp.einsum(
            "bmt,bmd->btd",
            slot_map,
            slots.reshape(ctx_size, capacity, width),
            preferred_element_type=f32,
        )
        return spread.reshape(seq_len, width)

    buffer = to_slots(blocks_two).astype(bf16)
    expert_pre = dot(buffer, expert_in)
    expert_hid = swiglu(expert_pre, FE).astype(bf16)
    expert_res = dot(expert_hid, expert_out).astype(bf16)
    routed = gate_all[:, None] * to_tokens(expert_res)

    shared_in, expert_res = after(shared_in, expert_res)
    shared_in = shared_in.transpose(1, 0, 2, 3).reshape(width, 2 * fs_own)
    shared_pre = dot(low_two, shared_in)
    shared_hid = swiglu(shared_pre, fs_own).astype(bf16)
    shared_res = dot(shared_hid, shared_out)
    out_parts = (scale_all[:, None] * shared_res + routed).astype(bf16)
    grad_rows, out_parts = after(grad_rows, out_parts)
    out_sum = lax.psum_scatter(out_parts, "ctx", scatter_dimension=0, tiled=True)

    grad_slots = to_slots(grad_rows.reshape(ctx_size, token_count, width))
    gate_slots = jnp.sum(jnp.where(slot_mask, gate_blocks[:, None, :], 0.0), axis=-1).reshape(-1, 1)
    grad_res = (gate_slots * grad_slots).astype(bf16)
    grad_hid = dot_t(grad_res, expert_out)
    slot_terms = jnp.sum(expert_hid.astype(f32) * grad_hid, axis=-1)
    slot_terms = slot_terms.reshape(ctx_size, capacity, 1)
    gate_terms = jnp.sum(jnp.where(slot_mask, slot_terms, 0.0), axis=1)
    grad_pre = swiglu_back(expert_pre, FE, grad_hid).astype(bf16)
    grad_expert_in = t_dot(buffer, grad_pre)
    grad_buffer = dot_t(grad_pre, expert_in).astype(bf16)

    grad_f32 = grad_rows.astype(f32)
    grad_expert_in, grad_shared_res = after(
        grad_expert_in.astype(bf16), (scale_all[:, None] * grad_f32).astype(bf16)
    )
    sum_expert_in = sum_rows(grad_expert_in)

    grad_shared_hid = dot_t(grad_shared_res, shared_out)
    scale_terms = jnp.sum(shared_hid.astype(f32) * grad_shared_hid, axis=-1)
    grad_shared_pre = swiglu_back(shared_pre, fs_own, grad_shared_hid).astype(bf16)
    two_parts = (dot_t(grad_shared_pre, shared_in) + to_tokens(grad_buffer)).astype(bf16)
    two_parts, expert_hid, shared_hid, grad_shared_pre = after(
        two_parts, expert_hid, shared_hid, grad_shared_pre
    )
    grad_expert_out = t_dot(expert_hid, grad_res).astype(bf16)
    grad_shared_out = t_dot(shared_hid, grad_shared_res).astype(bf16)
    grad_shared_in = t_dot(low_two, grad_shared_pre).astype(bf16)
    grad_two = ring_scatter(two_parts, ctx_size, ctx_index)
    dots = jnp.stack([gate_terms, scale_terms.reshape(ctx_size, token_count)], axis=1)
    dots = lax.all_to_all(dots, "ctx", split_axis=0, concat_axis=0, tiled=True)
    grad_two, grad_shared_in, grad_shared_out, grad_expert_out, dots, out_sum = after(
        grad_two, grad_shared_in, grad_shared_out, grad_expert_out, dots, out_sum
    )
    output = (own_residual + out_sum.astype(f32)).astype(bf16).reshape(tokens.shape)
    sum_shared_in = grad_shared_in.reshape(ctx_size, fsdp_size, shard, 2 * fs_own)
    sum_shared_in = lax.psum_scatter(
        sum_shared_in.transpose(1, 0, 2, 3).reshape(width, 2 * fs_own),
        "fsdp",
        scatter_dimension=0,
        tiled=True,
    ).reshape(ctx_size, shard, 2 * fs_own)
    sum_shared_out = sum_rows(grad_shared_out)
    sum_expert_out = sum_rows(grad_expert_out)
    own_probs = own_rows(probs_all)
    own_scale = own_rows(scale_all)
    own_chosen = routes.reshape(token_count, top_count)
    chosen_mask = jnp.any(
        own_chosen[..., None] == jnp.arange(expert_count, dtype=i32), axis=1
    )
    prob_terms = jnp.where(chosen_mask, dots[:, 0].T, 0.0)
    grad_logits = (
        prob_terms - own_probs * jnp.sum(prob_terms, axis=-1, keepdims=True)
    ).astype(bf16)
    grad_gate_pre = (jnp.sum(dots[:, 1], axis=0) * (1.0 - own_scale)).astype(bf16)
    grad_router = t_dot(own_low, grad_logits)
    grad_gate_vector = t_dot(own_low, grad_gate_pre[:, None])
    grad_two = grad_two + dot_t(grad_logits, router_weight)
    grad_two = grad_two + grad_gate_pre.astype(f32)[:, None] * gate_vector.astype(f32)[None, :]
    grad_resid_norm, grad_gain_two = rms_back(
        own_residual, inv_two, ffn_gain, grad_two
    )
    grad_resid = cotangent.reshape(token_count, width).astype(f32) + grad_resid_norm

    grad_mixed, sum_expert_in = after(grad_resid.astype(bf16), sum_expert_in)
    mixed_all = ring_gather(grad_mixed, ctx_size, ctx_index)
    grad_attn = dot_t(mixed_all, out_weight).astype(bf16).reshape(head_shape)
    grad_weights = jnp.einsum("qhd,khd->hqk", grad_attn, values, preferred_element_type=f32)
    delta = jnp.sum(weights * grad_weights, axis=-1, keepdims=True)
    grad_scores = jnp.where(allowed[None], weights * (grad_weights - delta), 0.0).astype(bf16)
    grad_scores, sum_shared_in = after(grad_scores, sum_shared_in)
    sum_shared_in = lax.all_to_all(
        sum_shared_in, "ctx", split_axis=0, concat_axis=0, tiled=True
    )
    grad_q = jnp.einsum("hqk,khd->qhd", grad_scores, keys, preferred_element_type=f32) * score_scale
    grad_k = (
        jnp.einsum("hqk,qhd->khd", grad_scores, queries, preferred_element_type=f32) * score_scale
    )
    grad_v = jnp.einsum("hqk,qhd->khd", weights_low, grad_attn, preferred_element_type=f32)
    grad_projected = jnp.concatenate(
        [
            rotate_back(grad_q, cos_tab, sine_tab).reshape(seq_len, own_width),
            rotate_back(grad_k, cos_tab, sine_tab).reshape(seq_len, own_width),
            grad_v.reshape(seq_len, own_width),
        ],
        axis=-1,
    ).astype(bf16)
    grad_projected, sum_shared_out, sum_shared_in = after(
        grad_projected, sum_shared_out, sum_shared_in
    )
    one_sums = dot_t(grad_projected, qkv_weight)
    grad_gain_one = jnp.sum(one_sums * scaled_rows.astype(f32), axis=0)
    one_parts = one_sums.astype(bf16)
    one_kept, grad_projected = after(one_parts, grad_projected)
    one_kept, sum_expert_out = after(one_kept, sum_expert_out)
    grad_normed = ring_scatter(one_parts, ctx_size, ctx_index, one_kept)
    grad_inputs_norm, unused = rms_back(
        own_tokens,
        inv_one,
        attn_gain,
        grad_normed,
    )
    grad_tokens = (grad_resid + grad_inputs_norm).reshape(tokens.shape)
    grad_qkv_weight = t_dot(normed_low, grad_projected)
    grad_bias = jnp.sum(grad_projected.astype(f32), axis=0).reshape(3, 1, own_width)
    grad_bias = jnp.where(
        jnp.arange(ctx_size, dtype=i32)[None, :, None] == ctx_index, grad_bias, 0.0
    )

    grad_out_weight = t_dot(attn_own, mixed_all)
    small_grads = [grad_gain_one, grad_gain_two, grad_gate_vector, grad_router, grad_bias]
    small_grads = jnp.concatenate(
        [piece.reshape(device_count, -1) for piece in small_grads], axis=1
    )
    more = -(-small_size // (3 * own_width * 16)) * 16
    small_grads = jnp.pad(small_grads, ((0, 0), (0, more * 3 * own_width - small_size)))
    pieces = jnp.concatenate(
        [
            grad_qkv_weight.astype(bf16).reshape(ctx_size, fsdp_size, shard, 3 * own_width),
            small_grads.astype(bf16).reshape(ctx_size, fsdp_size, more, 3 * own_width),
        ],
        axis=2,
    )
    pieces = pieces.transpose(1, 0, 2, 3).reshape(-1, 3 * own_width)
    pieces = lax.psum_scatter(pieces, "fsdp", scatter_dimension=0, tiled=True)
    pieces = pieces.reshape(ctx_size, shard + more, 3 * own_width)
    pieces = lax.all_to_all(pieces, "ctx", split_axis=0, concat_axis=0, tiled=True)
    small_grads = jnp.sum(pieces[:, shard:].reshape(ctx_size, -1).astype(f32), axis=0)
    return (
        output,
        grad_tokens,
        merge_columns(pieces[:, :shard], 3, ctx_size),
        small_grads[router_end:small_size],
        sum_rows(grad_out_weight).astype(f32),
        small_grads[:shard],
        small_grads[shard : 2 * shard],
        small_grads[3 * shard : router_end].reshape(shard, expert_count),
        small_grads[2 * shard : 3 * shard],
        merge_columns(sum_shared_in, 2, ctx_size),
        sum_shared_out.astype(f32),
        sum_expert_in.astype(f32)[None],
        sum_expert_out.astype(f32)[None],
    )


def local_wide(
    tokens,
    segments,
    routes,
    cotangent,
    w_qkv,
    b_qkv,
    w_out,
    gain_attn,
    gain_ffn,
    w_router,
    w_shared_gate,
    w_shared_in,
    w_shared_out,
    w_expert_in,
    w_expert_out,
):
    block_len = tokens.shape[2]
    model_width = tokens.shape[3]
    token_count = 2 * block_len
    top_count = routes.shape[3]
    half_len = segments.shape[2]
    seq_len = 2 * half_len
    ctx_index = lax.axis_index("ctx")
    head_count = model_width // HD
    expert_count = w_router.shape[1]
    capacity = token_count * top_count // expert_count
    slot_count = expert_count * capacity
    key_rows = min(512, seq_len)
    key_blocks = seq_len // key_rows
    score_scale = HD ** (-0.5)
    head_shape = (token_count, head_count, HD)
    attn_set = (
        lax.all_gather(w_qkv, ("ctx", "fsdp"), axis=0, tiled=True),
        lax.all_gather(b_qkv, ("ctx", "fsdp"), axis=0, tiled=True),
        lax.all_gather(w_out, ("ctx", "fsdp"), axis=0, tiled=True),
        lax.all_gather(gain_attn, ("ctx", "fsdp"), axis=0, tiled=True),
    )
    qkv_weight, qkv_bias, out_weight, attn_gain = attn_set
    inputs = tokens.reshape(token_count, model_width).astype(jnp.float32)
    normed, inv_one = rms_norm(inputs, attn_gain.astype(jnp.float32))
    normed_low = normed.astype(jnp.bfloat16)
    projected = jnp.dot(
        normed_low, qkv_weight, preferred_element_type=jnp.float32
    ) + qkv_bias.astype(jnp.float32)
    local_index = jnp.arange(block_len, dtype=jnp.int32)
    query_pos = jnp.concatenate(
        [ctx_index * block_len + local_index, seq_len - (ctx_index + 1) * block_len + local_index]
    )
    half_index = jnp.arange(half_len, dtype=jnp.int32)
    key_pos = jnp.concatenate(
        [half_index, seq_len - block_len * (half_index // block_len + 1) + half_index % block_len]
    ).reshape(key_blocks, key_rows)
    key_seg = segments.reshape(key_blocks, key_rows)
    query_seg = lax.dynamic_slice_in_dim(segments[0], ctx_index * block_len, block_len, 1).reshape(
        token_count
    )
    cos_tab, sine_tab = rope_tables(query_pos, HD)
    queries = rotate(projected[:, :model_width].reshape(head_shape), cos_tab, sine_tab).astype(
        jnp.bfloat16
    )
    keys_own = rotate(
        projected[:, model_width : 2 * model_width].reshape(head_shape), cos_tab, sine_tab
    ).astype(jnp.bfloat16)
    values_own = projected[:, 2 * model_width :].astype(jnp.bfloat16)
    keys_all, values_all = (
        lax.all_gather(keys_own.reshape(2, block_len, model_width), "ctx", axis=1, tiled=True),
        lax.all_gather(values_own.reshape(2, block_len, model_width), "ctx", axis=1, tiled=True),
    )
    keys_all = keys_all.reshape(key_blocks, key_rows, head_count, HD)
    values_all = values_all.reshape(key_blocks, key_rows, head_count, HD)

    def score_block(key_blk, pos_blk, seg_blk):
        raw_scores = (
            jnp.einsum("qhd,khd->hqk", queries, key_blk, preferred_element_type=jnp.float32)
            * score_scale
        )
        allowed = (pos_blk[None, :] <= query_pos[:, None]) & (
            seg_blk[None, :] == query_seg[:, None]
        )
        return (jnp.where(allowed[None], raw_scores, MASK_FILL), allowed)

    def total_step(running, key_part):
        run_max, run_sum = running
        scores = score_block(key_part[0], key_part[1], key_part[2])[0]
        new_max = jnp.maximum(run_max, jnp.max(scores, axis=-1))
        run_sum = run_sum * jnp.exp(run_max - new_max) + jnp.sum(
            jnp.exp(scores - new_max[..., None]), axis=-1
        )
        return ((new_max, run_sum), None)

    start_max = jnp.full((head_count, token_count), MASK_FILL, jnp.float32)
    start_sum = jnp.zeros((head_count, token_count), jnp.float32)
    (run_max, run_sum), unused = lax.scan(
        total_step, (start_max, start_sum), (keys_all, key_pos, key_seg)
    )
    log_total = run_max + jnp.log(run_sum)

    def attend_step(summed, key_part):
        key_blk, value_blk, pos_blk, seg_blk = key_part
        scores = score_block(key_blk, pos_blk, seg_blk)[0]
        weights = jnp.exp(scores - log_total[..., None]).astype(jnp.bfloat16)
        return (
            summed
            + jnp.einsum("hqk,khd->qhd", weights, value_blk, preferred_element_type=jnp.float32),
            None,
        )

    key_stack = (keys_all, values_all, key_pos, key_seg)
    attended, unused = lax.scan(attend_step, jnp.zeros(head_shape, jnp.float32), key_stack)
    attn_low = attended.reshape(token_count, model_width).astype(jnp.bfloat16)
    residual = inputs + jnp.dot(attn_low, out_weight, preferred_element_type=jnp.float32)
    ffn_set = (
        lax.all_gather(gain_ffn, ("ctx", "fsdp"), axis=0, tiled=True),
        lax.all_gather(w_router, ("ctx", "fsdp"), axis=0, tiled=True),
        lax.all_gather(w_shared_gate, ("ctx", "fsdp"), axis=0, tiled=True),
        lax.all_gather(w_shared_in, ("ctx", "fsdp"), axis=0, tiled=True),
        lax.all_gather(w_shared_out, ("ctx", "fsdp"), axis=0, tiled=True),
    )
    ffn_gain, router_weight, gate_vector, shared_in, shared_out = ffn_set
    normed_two, inv_two = rms_norm(residual, ffn_gain.astype(jnp.float32))
    low_two = normed_two.astype(jnp.bfloat16)
    logits = jnp.dot(low_two, router_weight, preferred_element_type=jnp.float32)
    router_probs = jax.nn.softmax(logits, axis=-1)
    chosen = routes.reshape(token_count, top_count)
    chosen_mask = chosen[..., None] == jnp.arange(expert_count, dtype=jnp.int32)
    gate_vals = jnp.sum(jnp.where(chosen_mask, router_probs[:, None, :], 0.0), axis=-1)
    shared_scale = jax.nn.sigmoid(jnp.dot(low_two, gate_vector, preferred_element_type=jnp.float32))
    shared_pre = jnp.dot(low_two, shared_in, preferred_element_type=jnp.float32)
    shared_hid = swiglu(shared_pre, FS).astype(jnp.bfloat16)
    shared_res = jnp.dot(shared_hid, shared_out, preferred_element_type=jnp.float32)
    pair_routes = chosen.reshape(token_count * top_count)
    expert_marks = (
        pair_routes[:, None] == jnp.arange(expert_count, dtype=jnp.int32)[None, :]
    ).astype(jnp.int32)
    pair_ranks = jnp.sum((jnp.cumsum(expert_marks, axis=0) - expert_marks) * expert_marks, axis=1)
    pair_target = jnp.where(pair_ranks < capacity, pair_routes * capacity + pair_ranks, -1)
    pair_map = pair_target[:, None] == jnp.arange(slot_count, dtype=jnp.int32)[None, :]
    pair_low = pair_map.astype(jnp.bfloat16)
    token_map = jnp.sum(
        pair_map.reshape(token_count, top_count, slot_count).astype(jnp.int32), axis=1
    ).astype(jnp.bfloat16)
    outgoing = jnp.einsum(
        "tc,td->cd", token_map, low_two, preferred_element_type=jnp.float32
    ).astype(jnp.bfloat16)
    incoming = lax.all_to_all(
        outgoing.reshape(expert_count, capacity, model_width),
        "ctx",
        split_axis=0,
        concat_axis=1,
        tiled=True,
    )
    expert_in, expert_out = (
        lax.all_gather(w_expert_in, "fsdp", axis=1, tiled=True),
        lax.all_gather(w_expert_out, "fsdp", axis=1, tiled=True),
    )
    expert_pre = jnp.einsum("erd,edf->erf", incoming, expert_in, preferred_element_type=jnp.float32)
    expert_hid = swiglu(expert_pre, FE).astype(jnp.bfloat16)
    expert_res = jnp.einsum(
        "erf,efd->erd", expert_hid, expert_out, preferred_element_type=jnp.float32
    ).astype(jnp.bfloat16)
    returned = lax.all_to_all(expert_res, "ctx", split_axis=1, concat_axis=0, tiled=True).reshape(
        slot_count, model_width
    )
    pair_vals = jnp.dot(pair_low, returned, preferred_element_type=jnp.float32).reshape(
        token_count, top_count, model_width
    )
    routed = jnp.sum(gate_vals[..., None] * pair_vals, axis=1)
    output = (
        (residual + shared_scale[:, None] * shared_res + routed)
        .astype(jnp.bfloat16)
        .reshape(tokens.shape)
    )
    grad_out = cotangent.reshape(token_count, model_width).astype(jnp.float32)
    pair_grads = gate_vals[..., None] * grad_out[:, None, :]
    grad_gates = jnp.sum(grad_out[:, None, :] * pair_vals, axis=-1)
    grad_returned = jnp.einsum(
        "pc,pd->cd",
        pair_map.astype(jnp.float32),
        pair_grads.reshape(token_count * top_count, model_width),
        precision=HIGHEST,
    ).astype(jnp.bfloat16)
    grad_res = lax.all_to_all(
        grad_returned.reshape(expert_count, capacity, model_width),
        "ctx",
        split_axis=0,
        concat_axis=1,
        tiled=True,
    )
    grad_expert_out = jnp.einsum(
        "erf,erd->efd", expert_hid, grad_res, preferred_element_type=jnp.float32
    )
    grad_hid = jnp.einsum("erd,efd->erf", grad_res, expert_out, preferred_element_type=jnp.float32)
    grad_pre = swiglu_back(expert_pre, FE, grad_hid).astype(jnp.bfloat16)
    grad_expert_in = jnp.einsum(
        "erd,erf->edf", incoming, grad_pre, preferred_element_type=jnp.float32
    )
    grad_incoming = jnp.einsum(
        "erf,edf->erd", grad_pre, expert_in, preferred_element_type=jnp.float32
    ).astype(jnp.bfloat16)
    grad_outgoing = lax.all_to_all(
        grad_incoming, "ctx", split_axis=1, concat_axis=0, tiled=True
    ).reshape(slot_count, model_width)
    expert_grads = (
        lax.psum_scatter(
            grad_expert_in.astype(jnp.bfloat16), "fsdp", scatter_dimension=1, tiled=True
        ).astype(jnp.float32),
        lax.psum_scatter(
            grad_expert_out.astype(jnp.bfloat16), "fsdp", scatter_dimension=1, tiled=True
        ).astype(jnp.float32),
    )
    grad_two = jnp.einsum("tc,cd->td", token_map, grad_outgoing, preferred_element_type=jnp.float32)
    grad_probs = jnp.sum(jnp.where(chosen_mask, grad_gates[..., None], 0.0), axis=1)
    grad_logits = (
        router_probs * (grad_probs - jnp.sum(router_probs * grad_probs, axis=-1, keepdims=True))
    ).astype(jnp.bfloat16)
    grad_router = jnp.einsum("td,te->de", low_two, grad_logits, preferred_element_type=jnp.float32)
    grad_shared_res = (shared_scale[:, None] * grad_out).astype(jnp.bfloat16)
    grad_gate_pre = (
        jnp.sum(grad_out * shared_res, axis=-1) * shared_scale * (1.0 - shared_scale)
    ).astype(jnp.bfloat16)
    grad_shared_out = jnp.einsum(
        "tf,td->fd", shared_hid, grad_shared_res, preferred_element_type=jnp.float32
    )
    grad_shared_hid = jnp.einsum(
        "td,fd->tf", grad_shared_res, shared_out, preferred_element_type=jnp.float32
    )
    grad_shared_pre = swiglu_back(shared_pre, FS, grad_shared_hid).astype(jnp.bfloat16)
    grad_shared_in = jnp.einsum(
        "td,tf->df", low_two, grad_shared_pre, preferred_element_type=jnp.float32
    )
    grad_gate_vector = jnp.einsum(
        "td,t->d", low_two, grad_gate_pre, preferred_element_type=jnp.float32
    )
    grad_two = grad_two + jnp.einsum(
        "te,de->td", grad_logits, router_weight, preferred_element_type=jnp.float32
    )
    grad_two = grad_two + jnp.einsum(
        "tf,df->td", grad_shared_pre, shared_in, preferred_element_type=jnp.float32
    )
    grad_two = (
        grad_two
        + grad_gate_pre.astype(jnp.float32)[:, None] * gate_vector.astype(jnp.float32)[None, :]
    )
    grad_resid_norm, grad_gain_two = rms_back(
        residual, inv_two, ffn_gain.astype(jnp.float32), grad_two
    )
    grad_resid = grad_out + grad_resid_norm
    ffn_grads = (
        lax.psum_scatter(grad_gain_two, ("ctx", "fsdp"), scatter_dimension=0, tiled=True),
        lax.psum_scatter(grad_router, ("ctx", "fsdp"), scatter_dimension=0, tiled=True),
        lax.psum_scatter(grad_gate_vector, ("ctx", "fsdp"), scatter_dimension=0, tiled=True),
        lax.psum_scatter(grad_shared_in, ("ctx", "fsdp"), scatter_dimension=0, tiled=True),
        lax.psum_scatter(grad_shared_out, ("ctx", "fsdp"), scatter_dimension=0, tiled=True),
    )
    grad_mixed = grad_resid.astype(jnp.bfloat16)
    grad_out_weight = jnp.einsum(
        "tc,td->cd", attn_low, grad_mixed, preferred_element_type=jnp.float32
    )
    grad_attn = (
        jnp.einsum("td,cd->tc", grad_mixed, out_weight, preferred_element_type=jnp.float32)
        .astype(jnp.bfloat16)
        .reshape(head_shape)
    )

    def delta_step(summed, key_part):
        key_blk, value_blk, pos_blk, seg_blk = key_part
        weights = jnp.exp(score_block(key_blk, pos_blk, seg_blk)[0] - log_total[..., None])
        grad_weights = jnp.einsum(
            "qhd,khd->hqk", grad_attn, value_blk, preferred_element_type=jnp.float32
        )
        return (summed + jnp.sum(weights * grad_weights, axis=-1), None)

    delta_sum, unused = lax.scan(
        delta_step, jnp.zeros((head_count, token_count), jnp.float32), key_stack
    )

    def grad_step(summed, key_part):
        key_blk, value_blk, pos_blk, seg_blk = key_part
        scores, allowed = score_block(key_blk, pos_blk, seg_blk)
        weights = jnp.exp(scores - log_total[..., None])
        grad_weights = jnp.einsum(
            "qhd,khd->hqk", grad_attn, value_blk, preferred_element_type=jnp.float32
        )
        grad_scores = jnp.where(
            allowed[None], weights * (grad_weights - delta_sum[..., None]), 0.0
        ).astype(jnp.bfloat16)
        summed = (
            summed
            + jnp.einsum("hqk,khd->qhd", grad_scores, key_blk, preferred_element_type=jnp.float32)
            * score_scale
        )
        grad_key = (
            jnp.einsum("hqk,qhd->khd", grad_scores, queries, preferred_element_type=jnp.float32)
            * score_scale
        )
        grad_value = jnp.einsum(
            "hqk,qhd->khd",
            weights.astype(jnp.bfloat16),
            grad_attn,
            preferred_element_type=jnp.float32,
        )
        return (summed, (grad_key, grad_value))

    grad_query, (grad_keys, grad_values) = lax.scan(
        grad_step, jnp.zeros(head_shape, jnp.float32), key_stack
    )
    grad_keys_own, grad_values_own = (
        lax.psum_scatter(
            grad_keys.reshape(2, half_len, model_width).astype(jnp.bfloat16),
            "ctx",
            scatter_dimension=1,
            tiled=True,
        ).astype(jnp.float32),
        lax.psum_scatter(
            grad_values.reshape(2, half_len, model_width).astype(jnp.bfloat16),
            "ctx",
            scatter_dimension=1,
            tiled=True,
        ).astype(jnp.float32),
    )
    grad_q_rows = rotate_back(grad_query, cos_tab, sine_tab).reshape(token_count, model_width)
    grad_k_rows = rotate_back(grad_keys_own.reshape(head_shape), cos_tab, sine_tab).reshape(
        token_count, model_width
    )
    grad_projected = jnp.concatenate(
        [grad_q_rows, grad_k_rows, grad_values_own.reshape(token_count, model_width)], axis=-1
    ).astype(jnp.bfloat16)
    grad_qkv_weight = jnp.einsum(
        "td,te->de", normed_low, grad_projected, preferred_element_type=jnp.float32
    )
    grad_qkv_bias = jnp.sum(grad_projected.astype(jnp.float32), axis=0)
    grad_normed = jnp.einsum(
        "te,de->td", grad_projected, qkv_weight, preferred_element_type=jnp.float32
    )
    grad_inputs_norm, grad_gain_one = rms_back(
        inputs, inv_one, attn_gain.astype(jnp.float32), grad_normed
    )
    grad_tokens = (grad_resid + grad_inputs_norm).reshape(tokens.shape)
    attn_grads = (
        lax.psum_scatter(grad_qkv_weight, ("ctx", "fsdp"), scatter_dimension=0, tiled=True),
        lax.psum_scatter(grad_qkv_bias, ("ctx", "fsdp"), scatter_dimension=0, tiled=True),
        lax.psum_scatter(grad_out_weight, ("ctx", "fsdp"), scatter_dimension=0, tiled=True),
        lax.psum_scatter(grad_gain_one, ("ctx", "fsdp"), scatter_dimension=0, tiled=True),
    )
    return (
        output,
        grad_tokens,
        attn_grads[0],
        attn_grads[1],
        attn_grads[2],
        attn_grads[3],
        ffn_grads[0],
        ffn_grads[1],
        ffn_grads[2],
        ffn_grads[3],
        ffn_grads[4],
        expert_grads[0],
        expert_grads[1],
    )


def solution(mesh):
    in_specs = (
        P("fsdp", None, "ctx", None),
        P("fsdp", None, None),
        P("fsdp", None, "ctx", None),
        P("fsdp", None, "ctx", None),
        P(("ctx", "fsdp"), None),
        P(("ctx", "fsdp")),
        P(("ctx", "fsdp"), None),
        P(("ctx", "fsdp")),
        P(("ctx", "fsdp")),
        P(("ctx", "fsdp"), None),
        P(("ctx", "fsdp")),
        P(("ctx", "fsdp"), None),
        P(("ctx", "fsdp"), None),
        P("ctx", "fsdp", None),
        P("ctx", "fsdp", None),
    )
    out_specs = (
        P("fsdp", None, "ctx", None),
        P("fsdp", None, "ctx", None),
        P(("ctx", "fsdp"), None),
        P(("ctx", "fsdp")),
        P(("ctx", "fsdp"), None),
        P(("ctx", "fsdp")),
        P(("ctx", "fsdp")),
        P(("ctx", "fsdp"), None),
        P(("ctx", "fsdp")),
        P(("ctx", "fsdp"), None),
        P(("ctx", "fsdp"), None),
        P("ctx", "fsdp", None),
        P("ctx", "fsdp", None),
    )
    ctx_size = mesh.shape["ctx"]
    fsdp_size = mesh.shape["fsdp"]

    def local(*arrays):
        if HEADS % ctx_size:
            return local_wide(*arrays)
        return local_split(ctx_size, fsdp_size, *arrays)

    return jax.shard_map(local, mesh=mesh, in_specs=in_specs, out_specs=out_specs, check_vma=False)
```

```python
import jax
import jax.numpy as jnp
from jax import lax
from jax.sharding import PartitionSpec as P

HD = 128
HEADS = 16
FS = 5632
FE = 1408


RMS_EPS = 1e-06
ROPE_THETA = 1000000.0
MASK_FILL = -1e30
HIGHEST = lax.Precision.HIGHEST


def rope_tables(positions, head_dim):
    half_dim = head_dim // 2
    inv_freq = ROPE_THETA ** (-(jnp.arange(half_dim, dtype=jnp.float32) * 2.0 / head_dim))
    angles = positions.astype(jnp.float32)[:, None] * inv_freq[None, :]
    cos_tab = jnp.concatenate([jnp.cos(angles), jnp.cos(angles)], axis=-1)
    sine_tab = jnp.concatenate([jnp.sin(angles), jnp.sin(angles)], axis=-1)
    return (cos_tab, sine_tab)


def rotate(values, cos_tab, sine_tab):
    half_dim = values.shape[-1] // 2
    turned = jnp.concatenate([-values[..., half_dim:], values[..., :half_dim]], axis=-1)
    return values * cos_tab[:, None, :] + turned * sine_tab[:, None, :]


def rotate_back(upstream, cos_tab, sine_tab):
    half_dim = upstream.shape[-1] // 2
    scaled = upstream * sine_tab[:, None, :]
    return upstream * cos_tab[:, None, :] + jnp.concatenate(
        [scaled[..., half_dim:], -scaled[..., :half_dim]], axis=-1
    )


def rms_norm(values, gain_vec):
    inv_rms = lax.rsqrt(jnp.mean(values * values, axis=-1, keepdims=True) + RMS_EPS)
    return (values * inv_rms * gain_vec, inv_rms)


def rms_back(values, inv_rms, gain_vec, upstream):
    weighted = upstream * gain_vec
    inner_mean = jnp.mean(weighted * values, axis=-1, keepdims=True)
    return (
        inv_rms * weighted - values * inv_rms * inv_rms * inv_rms * inner_mean,
        jnp.sum(upstream * values * inv_rms, axis=0),
    )


def swiglu(pre_act, split_at):
    return jax.nn.silu(pre_act[..., :split_at]) * pre_act[..., split_at:]


def swiglu_back(pre_act, split_at, upstream):
    gate_part = pre_act[..., :split_at]
    up_part = pre_act[..., split_at:]
    sigmoid_g = jax.nn.sigmoid(gate_part)
    d_gate = upstream * up_part * sigmoid_g * (1.0 + gate_part * (1.0 - sigmoid_g))
    d_up = upstream * gate_part * sigmoid_g
    return jnp.concatenate([d_gate, d_up], axis=-1)


def ring_order(size):
    return list(range(0, size, 2)) + list(range(size - 1, 0, -2))


def ring_steps(size):
    order = ring_order(size)
    ahead = [(order[i], order[(i + 1) % size]) for i in range(size)]
    back = [(dst, src) for src, dst in ahead]
    return (ahead, back)


def ring_peers(size, ctx_index):
    order = ring_order(size)
    place = {dev: i for i, dev in enumerate(order)}
    table = jnp.array(
        [[order[(place[dev] + k) % size] for k in range(size)] for dev in range(size)], jnp.int32
    )
    row = lax.dynamic_index_in_dim(table, ctx_index, 0, keepdims=False)
    return [row[k] for k in range(size)]


def after(value, *deps):
    return lax.optimization_barrier((value,) + deps)


def ring_gather(block, size, ctx_index, rider=None):
    rows, width = block.shape

    def put(out, piece, peer, offset):
        return lax.dynamic_update_slice(out, piece, (peer * rows + offset, jnp.zeros_like(peer)))

    out = jnp.zeros((size * rows, width), block.dtype)
    ahead, back = ring_steps(size)
    peers = ring_peers(size, ctx_index)
    half = size // 2
    out = put(out, block, ctx_index, 0)
    fore = rear = block
    for k in range(1, half):
        fore = lax.ppermute(fore, "ctx", ahead)
        rear = lax.ppermute(rear, "ctx", back)
        if rider is not None and k == 2:
            fore, rider = after(fore, rider)
        out = put(out, fore, peers[size - k], 0)
        out = put(out, rear, peers[k], 0)
    fore = lax.ppermute(fore[: rows // 2], "ctx", ahead)
    rear = lax.ppermute(rear[rows // 2 :], "ctx", back)
    out = put(out, fore, peers[half], 0)
    out = put(out, rear, peers[half], rows // 2)
    return out if rider is None else (out, rider)


def ring_sums(parts, size, ctx_index):
    f32 = jnp.float32
    rows = parts.shape[0] // size
    ahead, back = ring_steps(size)
    peers = ring_peers(size, ctx_index)
    half = size // 2

    def own(k, start, count):
        first = (peers[k % size] * rows + start, jnp.zeros_like(peers[0]))
        return lax.dynamic_slice(parts, first, (count, parts.shape[1])).astype(f32)

    def low(values):
        return values.astype(jnp.bfloat16)

    cut = rows // 2
    fore = lax.ppermute(low(own(half, 0, cut)), "ctx", ahead)
    rear = lax.ppermute(low(own(half, cut, cut)), "ctx", back)
    fore = jnp.concatenate(
        [low(fore.astype(f32) + own(half - 1, 0, cut)), low(own(half - 1, cut, cut))], axis=0
    )
    rear = jnp.concatenate(
        [low(own(1 - half, 0, cut)), low(rear.astype(f32) + own(1 - half, cut, cut))], axis=0
    )
    for k in range(half - 1, 0, -1):
        fore = lax.ppermute(fore, "ctx", ahead)
        rear = lax.ppermute(rear, "ctx", back)
        if k > 1:
            fore = low(fore.astype(f32) + own(k - 1, 0, rows))
            rear = low(rear.astype(f32) + own(1 - k, 0, rows))
    return (fore, rear)


def ring_scatter(parts, size, ctx_index, kept=None):
    fore, rear = ring_sums(parts, size, ctx_index)
    kept = (parts if kept is None else kept).reshape(size, -1, parts.shape[1])
    kept = lax.dynamic_index_in_dim(kept, ctx_index, 0, keepdims=False)
    return kept.astype(jnp.float32) + fore.astype(jnp.float32) + rear.astype(jnp.float32)


def other_core(size):
    return [(i, i ^ 1) for i in range(size)]


def other_chip(size):
    return [(i, i ^ 2) for i in range(size)]


def fsdp_gather(shard, size, hold):
    index = lax.axis_index("fsdp")
    rows, width = shard.shape
    far = lax.ppermute(shard, "fsdp", other_chip(size))
    far, hold = after(far, hold)
    pair = jnp.where(
        index < 2, jnp.stack([shard, far], axis=0), jnp.stack([far, shard], axis=0)
    )
    near = lax.ppermute(pair, "fsdp", other_core(size))
    out = jnp.zeros((2, 2, rows, width), shard.dtype)
    out = lax.dynamic_update_index_in_dim(out, pair, index % 2, 1)
    out = lax.dynamic_update_index_in_dim(out, near, 1 - index % 2, 1)
    return (out.reshape(size * rows, width), hold)


def fsdp_scatter(grad, size):
    index = lax.axis_index("fsdp")
    core, chip = index % 2, index // 2
    grad = grad.reshape((2, 2) + grad.shape[1:])

    def pick(array, at, axis):
        return lax.dynamic_index_in_dim(array, at, axis, keepdims=False)

    near = lax.ppermute(pick(grad, 1 - core, 1), "fsdp", other_core(size))
    mine = (pick(grad, core, 1).astype(jnp.float32) + near.astype(jnp.float32)).astype(grad.dtype)
    far = lax.ppermute(pick(mine, 1 - chip, 0), "fsdp", other_chip(size))
    return pick(mine, chip, 0).astype(jnp.float32) + far.astype(jnp.float32)


def column_pieces(weight, groups, size, extra):
    rows = weight.shape[0]
    width = weight.shape[1] // (groups * size)
    pieces = weight.reshape(rows, groups, size, width).transpose(2, 0, 1, 3)
    pieces = pieces.reshape(size, rows, groups * width)
    if extra is not None:
        count = extra.shape[0]
        more = -(-count // (groups * width * 16)) * 16
        extra = jnp.pad(extra, (0, more * groups * width - count))
        extra = jnp.broadcast_to(
            extra.reshape(1, more, groups * width), (size, more, groups * width)
        )
        pieces = jnp.concatenate([pieces, extra], axis=1)
    return pieces


def merge_columns(pieces, groups, size):
    width = pieces.shape[2] // groups
    if width % 128 == 0:
        pieces = pieces.reshape(size, -1, groups, width).transpose(1, 2, 0, 3)
        return pieces.reshape(-1, groups * size * width).astype(jnp.float32)
    columns = [
        pieces[peer, :, group * width : (group + 1) * width]
        for group in range(groups)
        for peer in range(size)
    ]
    return jnp.concatenate(columns, axis=1).astype(jnp.float32)


def local_split(
    ctx_size,
    fsdp_size,
    tokens,
    segments,
    routes,
    cotangent,
    w_qkv,
    b_qkv,
    w_out,
    gain_attn,
    gain_ffn,
    w_router,
    w_shared_gate,
    w_shared_in,
    w_shared_out,
    w_expert_in,
    w_expert_out,
):
    bf16, f32, i32 = jnp.bfloat16, jnp.float32, jnp.int32
    device_count = ctx_size * fsdp_size
    block_len = tokens.shape[2]
    width = tokens.shape[3]
    token_count = 2 * block_len
    top_count = routes.shape[3]
    seq_len = token_count * ctx_size
    ctx_index = lax.axis_index("ctx")
    expert_count = w_router.shape[1]
    capacity = token_count * top_count // expert_count
    own_heads = HEADS // ctx_size
    own_width = own_heads * HD
    fs_own = FS // ctx_size
    score_scale = HD ** (-0.5)

    def dot(a, b):
        return jnp.dot(a, b, preferred_element_type=f32)

    def dot_t(a, b):
        return lax.dot_general(a, b, (((1,), (1,)), ((), ())), preferred_element_type=f32)

    def t_dot(a, b):
        return lax.dot_general(a, b, (((0,), (0,)), ((), ())), preferred_element_type=f32)

    def own_rows(values):
        return lax.dynamic_index_in_dim(
            values.reshape((ctx_size, token_count) + values.shape[1:]), ctx_index, 0, keepdims=False
        )

    def sum_rows(grad):
        return lax.psum_scatter(grad.astype(bf16), "fsdp", scatter_dimension=0, tiled=True)

    shard = width // device_count
    small = [gain_attn, gain_ffn, w_shared_gate, w_router.reshape(-1), b_qkv]
    small_size = sum(piece.shape[0] for piece in small)
    small = jnp.concatenate(small + [routes.astype(bf16).reshape(-1)], axis=0)
    small_count = small.shape[0]
    own_tokens = tokens.reshape(token_count, width).astype(f32)
    own_scaled, inv_one = rms_norm(own_tokens, 1.0)
    scaled_rows = ring_gather(own_scaled.astype(bf16), ctx_size, ctx_index)
    pieces = column_pieces(w_qkv, 3, ctx_size, small)
    pieces = lax.all_to_all(pieces, "ctx", split_axis=0, concat_axis=0, tiled=True)
    shared_in = column_pieces(w_shared_in, 2, ctx_size, None)
    shared_in, scaled_rows = after(shared_in, scaled_rows)
    shared_in = lax.all_to_all(shared_in, "ctx", split_axis=0, concat_axis=0, tiled=True)
    pieces = lax.all_gather(pieces, "fsdp", axis=0, tiled=False).transpose(1, 0, 2, 3)
    qkv_weight = pieces[:, :, :shard].reshape(width, 3 * own_width)
    small = pieces[:, :, shard:].reshape(device_count, -1)[:, :small_count]
    attn_gain = small[:, :shard].reshape(width).astype(f32)
    ffn_gain = small[:, shard : 2 * shard].reshape(width).astype(f32)
    gate_vector = small[:, 2 * shard : 3 * shard].reshape(width)
    router_end = 3 * shard + shard * expert_count
    router_weight = small[:, 3 * shard : router_end].reshape(width, expert_count)
    bias = small[:, router_end:small_size].reshape(3, ctx_size, own_width).astype(f32)
    bias = lax.dynamic_index_in_dim(bias, ctx_index, 1, keepdims=False).reshape(3 * own_width)
    route_rows = small[:, small_size:].astype(i32)
    route_rows = lax.dynamic_index_in_dim(
        route_rows.reshape(ctx_size, fsdp_size, -1), lax.axis_index("fsdp"), 1, keepdims=False
    ).reshape(ctx_size, token_count, top_count)

    expert_in = lax.all_gather(w_expert_in[0], "fsdp", axis=0, tiled=True)

    block_ids = jnp.arange(ctx_size, dtype=i32)[:, None]
    local_index = jnp.arange(block_len, dtype=i32)[None, :]
    positions = jnp.stack(
        [
            block_ids * block_len + local_index,
            seq_len - (block_ids + 1) * block_len + local_index,
        ],
        axis=1,
    ).reshape(seq_len)
    seg_rows = (
        segments.reshape(2, ctx_size, block_len).transpose(1, 0, 2).reshape(seq_len)
    )
    cos_tab, sine_tab = rope_tables(positions, HD)

    normed_low = (scaled_rows.astype(f32) * attn_gain).astype(bf16)
    projected = dot(normed_low, qkv_weight) + bias
    head_shape = (seq_len, own_heads, HD)
    queries = rotate(projected[:, :own_width].reshape(head_shape), cos_tab, sine_tab).astype(bf16)
    keys = rotate(
        projected[:, own_width : 2 * own_width].reshape(head_shape), cos_tab, sine_tab
    ).astype(bf16)
    values = projected[:, 2 * own_width :].reshape(head_shape).astype(bf16)
    out_weight, queries = fsdp_gather(w_out, fsdp_size, queries)
    allowed = (positions[None, :] <= positions[:, None]) & (seg_rows[None, :] == seg_rows[:, None])
    scores = jnp.einsum("qhd,khd->hqk", queries, keys, preferred_element_type=f32) * score_scale
    scores = jnp.where(allowed[None], scores, MASK_FILL)
    top_score = jnp.max(scores, axis=-1, keepdims=True)
    log_total = top_score + jnp.log(jnp.sum(jnp.exp(scores - top_score), axis=-1, keepdims=True))
    weights = jnp.exp(scores - log_total)
    weights_low = weights.astype(bf16)
    attended = jnp.einsum("hqk,khd->qhd", weights_low, values, preferred_element_type=f32)
    attn_own = attended.astype(bf16).reshape(seq_len, own_width)
    shared_out, attn_own = fsdp_gather(w_shared_out, fsdp_size, attn_own)
    expert_out, attn_own = fsdp_gather(w_expert_out[0], fsdp_size, attn_own)
    attn_parts, shared_in = after(dot(attn_own, out_weight).astype(bf16), shared_in)
    shared_in = lax.all_gather(shared_in, "fsdp", axis=0, tiled=False)
    own_residual = own_tokens + ring_scatter(attn_parts, ctx_size, ctx_index)

    normed_two, inv_two = rms_norm(own_residual, ffn_gain)
    own_low = normed_two.astype(bf16)
    low_two, grad_rows = ring_gather(
        own_low, ctx_size, ctx_index, cotangent.reshape(token_count, width)
    )
    grad_rows = lax.all_gather(grad_rows, "ctx", axis=0, tiled=True)
    mixed_weight = jnp.concatenate([router_weight, gate_vector[:, None]], axis=1)
    logits = dot(low_two, mixed_weight)
    probs_all = jax.nn.softmax(logits[:, :expert_count], axis=-1)
    scale_all = jax.nn.sigmoid(logits[:, expert_count])
    gate_all = lax.dynamic_index_in_dim(probs_all, ctx_index, 1, keepdims=False)

    named = jnp.any(route_rows == ctx_index, axis=-1)
    before = jnp.arange(token_count)[:, None] < jnp.arange(token_count)[None, :]
    rank = dot(named.astype(bf16), before.astype(bf16)).astype(i32)
    slot_of = jnp.where(named & (rank < capacity), rank, -1)
    slot_mask = slot_of[:, None, :] == jnp.arange(capacity, dtype=i32)[None, :, None]
    slot_map = slot_mask.astype(bf16)
    blocks_two = low_two.reshape(ctx_size, token_count, width)
    gate_blocks = gate_all.reshape(ctx_size, token_count)

    def to_slots(blocks):
        picked = jnp.einsum("bmt,btd->bmd", slot_map, blocks, preferred_element_type=f32)
        return picked.reshape(ctx_size * capacity, width)

    def to_tokens(slots):
        spread = jnp.einsum(
            "bmt,bmd->btd",
            slot_map,
            slots.reshape(ctx_size, capacity, width),
            preferred_element_type=f32,
        )
        return spread.reshape(seq_len, width)

    buffer = to_slots(blocks_two).astype(bf16)
    expert_pre = dot(buffer, expert_in)
    expert_hid = swiglu(expert_pre, FE).astype(bf16)
    expert_res = dot(expert_hid, expert_out).astype(bf16)
    routed = gate_all[:, None] * to_tokens(expert_res)

    shared_in, expert_res = after(shared_in, expert_res)
    shared_in = shared_in.transpose(1, 0, 2, 3).reshape(width, 2 * fs_own)
    shared_pre = dot(low_two, shared_in)
    shared_hid = swiglu(shared_pre, fs_own).astype(bf16)
    shared_res = dot(shared_hid, shared_out)
    out_parts = (scale_all[:, None] * shared_res + routed).astype(bf16)
    grad_rows, out_parts = after(grad_rows, out_parts)
    out_sum = lax.psum_scatter(out_parts, "ctx", scatter_dimension=0, tiled=True)

    grad_slots = to_slots(grad_rows.reshape(ctx_size, token_count, width))
    gate_slots = jnp.sum(jnp.where(slot_mask, gate_blocks[:, None, :], 0.0), axis=-1).reshape(-1, 1)
    grad_res = (gate_slots * grad_slots).astype(bf16)
    grad_hid = dot_t(grad_res, expert_out)
    slot_terms = jnp.sum(expert_hid.astype(f32) * grad_hid, axis=-1)
    slot_terms = slot_terms.reshape(ctx_size, capacity, 1)
    gate_terms = jnp.sum(jnp.where(slot_mask, slot_terms, 0.0), axis=1)
    grad_pre = swiglu_back(expert_pre, FE, grad_hid).astype(bf16)
    grad_expert_in = t_dot(buffer, grad_pre)
    grad_buffer = dot_t(grad_pre, expert_in).astype(bf16)

    grad_f32 = grad_rows.astype(f32)
    grad_expert_in, grad_shared_res = after(
        grad_expert_in.astype(bf16), (scale_all[:, None] * grad_f32).astype(bf16)
    )
    sum_expert_in = sum_rows(grad_expert_in)

    grad_shared_hid = dot_t(grad_shared_res, shared_out)
    scale_terms = jnp.sum(shared_hid.astype(f32) * grad_shared_hid, axis=-1)
    grad_shared_pre = swiglu_back(shared_pre, fs_own, grad_shared_hid).astype(bf16)
    two_parts = (dot_t(grad_shared_pre, shared_in) + to_tokens(grad_buffer)).astype(bf16)
    two_parts, expert_hid, shared_hid, grad_shared_pre = after(
        two_parts, expert_hid, shared_hid, grad_shared_pre
    )
    grad_expert_out = t_dot(expert_hid, grad_res).astype(bf16)
    grad_shared_out = t_dot(shared_hid, grad_shared_res).astype(bf16)
    grad_shared_in = t_dot(low_two, grad_shared_pre).astype(bf16)
    grad_two = ring_scatter(two_parts, ctx_size, ctx_index)
    dots = jnp.stack([gate_terms, scale_terms.reshape(ctx_size, token_count)], axis=1)
    dots = lax.all_to_all(dots, "ctx", split_axis=0, concat_axis=0, tiled=True)
    grad_two, grad_shared_in, grad_shared_out, grad_expert_out, dots = after(
        grad_two, grad_shared_in, grad_shared_out, grad_expert_out, dots
    )
    sum_shared_in = grad_shared_in.reshape(ctx_size, fsdp_size, shard, 2 * fs_own)
    sum_shared_in = lax.psum_scatter(
        sum_shared_in.transpose(1, 0, 2, 3).reshape(width, 2 * fs_own),
        "fsdp",
        scatter_dimension=0,
        tiled=True,
    ).reshape(ctx_size, shard, 2 * fs_own)
    sum_expert_out = fsdp_scatter(grad_expert_out.reshape(fsdp_size, -1, width), fsdp_size)
    own_probs = own_rows(probs_all)
    own_scale = own_rows(scale_all)
    own_chosen = routes.reshape(token_count, top_count)
    chosen_mask = jnp.any(
        own_chosen[..., None] == jnp.arange(expert_count, dtype=i32), axis=1
    )
    prob_terms = jnp.where(chosen_mask, dots[:, 0].T, 0.0)
    grad_logits = (
        prob_terms - own_probs * jnp.sum(prob_terms, axis=-1, keepdims=True)
    ).astype(bf16)
    grad_gate_pre = (jnp.sum(dots[:, 1], axis=0) * (1.0 - own_scale)).astype(bf16)
    grad_router = t_dot(own_low, grad_logits)
    grad_gate_vector = t_dot(own_low, grad_gate_pre[:, None])
    grad_two = grad_two + dot_t(grad_logits, router_weight)
    grad_two = grad_two + grad_gate_pre.astype(f32)[:, None] * gate_vector.astype(f32)[None, :]
    grad_resid_norm, grad_gain_two = rms_back(
        own_residual, inv_two, ffn_gain, grad_two
    )
    grad_resid = cotangent.reshape(token_count, width).astype(f32) + grad_resid_norm

    grad_mixed, sum_expert_in = after(grad_resid.astype(bf16), sum_expert_in)
    mixed_all = ring_gather(grad_mixed, ctx_size, ctx_index)
    grad_attn = dot_t(mixed_all, out_weight).astype(bf16).reshape(head_shape)
    grad_attn, sum_shared_in = after(grad_attn, sum_shared_in)
    sum_shared_in = lax.all_to_all(
        sum_shared_in, "ctx", split_axis=0, concat_axis=0, tiled=True
    )
    grad_weights = jnp.einsum("qhd,khd->hqk", grad_attn, values, preferred_element_type=f32)
    delta = jnp.sum(weights * grad_weights, axis=-1, keepdims=True)
    grad_scores = jnp.where(allowed[None], weights * (grad_weights - delta), 0.0).astype(bf16)
    grad_q = jnp.einsum("hqk,khd->qhd", grad_scores, keys, preferred_element_type=f32) * score_scale
    grad_k = (
        jnp.einsum("hqk,qhd->khd", grad_scores, queries, preferred_element_type=f32) * score_scale
    )
    grad_v = jnp.einsum("hqk,qhd->khd", weights_low, grad_attn, preferred_element_type=f32)
    grad_projected = jnp.concatenate(
        [
            rotate_back(grad_q, cos_tab, sine_tab).reshape(seq_len, own_width),
            rotate_back(grad_k, cos_tab, sine_tab).reshape(seq_len, own_width),
            grad_v.reshape(seq_len, own_width),
        ],
        axis=-1,
    ).astype(bf16)
    grad_projected, out_sum, sum_expert_out = after(grad_projected, out_sum, sum_expert_out)
    output = (own_residual + out_sum.astype(f32)).astype(bf16).reshape(tokens.shape)
    one_sums = dot_t(grad_projected, qkv_weight)
    grad_gain_one = jnp.sum(one_sums * scaled_rows.astype(f32), axis=0)
    one_parts = one_sums.astype(bf16)
    one_kept, grad_projected = after(one_parts, grad_projected)
    one_kept, sum_shared_in = after(one_kept, sum_shared_in)
    grad_normed = ring_scatter(one_parts, ctx_size, ctx_index, one_kept)
    grad_inputs_norm, unused = rms_back(
        own_tokens,
        inv_one,
        attn_gain,
        grad_normed,
    )
    grad_tokens = (grad_resid + grad_inputs_norm).reshape(tokens.shape)
    grad_qkv_weight = t_dot(normed_low, grad_projected)
    grad_bias = jnp.sum(grad_projected.astype(f32), axis=0).reshape(3, 1, own_width)
    grad_bias = jnp.where(
        jnp.arange(ctx_size, dtype=i32)[None, :, None] == ctx_index, grad_bias, 0.0
    )

    grad_out_weight = t_dot(attn_own, mixed_all)
    small_grads = [grad_gain_one, grad_gain_two, grad_gate_vector, grad_router, grad_bias]
    small_grads = jnp.concatenate(
        [piece.reshape(device_count, -1) for piece in small_grads], axis=1
    )
    more = -(-small_size // (3 * own_width * 16)) * 16
    small_grads = jnp.pad(small_grads, ((0, 0), (0, more * 3 * own_width - small_size)))
    pieces = jnp.concatenate(
        [
            grad_qkv_weight.astype(bf16).reshape(ctx_size, fsdp_size, shard, 3 * own_width),
            small_grads.astype(bf16).reshape(ctx_size, fsdp_size, more, 3 * own_width),
        ],
        axis=2,
    )
    pieces = pieces.transpose(1, 0, 2, 3).reshape(-1, 3 * own_width)
    pieces = lax.psum_scatter(pieces, "fsdp", scatter_dimension=0, tiled=True)
    pieces, grad_shared_out = after(pieces, grad_shared_out)
    sum_shared_out = sum_rows(grad_shared_out)
    pieces = pieces.reshape(ctx_size, shard + more, 3 * own_width)
    pieces = lax.all_to_all(pieces, "ctx", split_axis=0, concat_axis=0, tiled=True)
    small_grads = jnp.sum(pieces[:, shard:].reshape(ctx_size, -1).astype(f32), axis=0)
    return (
        output,
        grad_tokens,
        merge_columns(pieces[:, :shard], 3, ctx_size),
        small_grads[router_end:small_size],
        sum_rows(grad_out_weight).astype(f32),
        small_grads[:shard],
        small_grads[shard : 2 * shard],
        small_grads[3 * shard : router_end].reshape(shard, expert_count),
        small_grads[2 * shard : 3 * shard],
        merge_columns(sum_shared_in, 2, ctx_size),
        sum_shared_out.astype(f32),
        sum_expert_in.astype(f32)[None],
        sum_expert_out[None],
    )


def local_wide(
    tokens,
    segments,
    routes,
    cotangent,
    w_qkv,
    b_qkv,
    w_out,
    gain_attn,
    gain_ffn,
    w_router,
    w_shared_gate,
    w_shared_in,
    w_shared_out,
    w_expert_in,
    w_expert_out,
):
    block_len = tokens.shape[2]
    model_width = tokens.shape[3]
    token_count = 2 * block_len
    top_count = routes.shape[3]
    half_len = segments.shape[2]
    seq_len = 2 * half_len
    ctx_index = lax.axis_index("ctx")
    head_count = model_width // HD
    expert_count = w_router.shape[1]
    capacity = token_count * top_count // expert_count
    slot_count = expert_count * capacity
    key_rows = min(512, seq_len)
    key_blocks = seq_len // key_rows
    score_scale = HD ** (-0.5)
    head_shape = (token_count, head_count, HD)
    attn_set = (
        lax.all_gather(w_qkv, ("ctx", "fsdp"), axis=0, tiled=True),
        lax.all_gather(b_qkv, ("ctx", "fsdp"), axis=0, tiled=True),
        lax.all_gather(w_out, ("ctx", "fsdp"), axis=0, tiled=True),
        lax.all_gather(gain_attn, ("ctx", "fsdp"), axis=0, tiled=True),
    )
    qkv_weight, qkv_bias, out_weight, attn_gain = attn_set
    inputs = tokens.reshape(token_count, model_width).astype(jnp.float32)
    normed, inv_one = rms_norm(inputs, attn_gain.astype(jnp.float32))
    normed_low = normed.astype(jnp.bfloat16)
    projected = jnp.dot(
        normed_low, qkv_weight, preferred_element_type=jnp.float32
    ) + qkv_bias.astype(jnp.float32)
    local_index = jnp.arange(block_len, dtype=jnp.int32)
    query_pos = jnp.concatenate(
        [ctx_index * block_len + local_index, seq_len - (ctx_index + 1) * block_len + local_index]
    )
    half_index = jnp.arange(half_len, dtype=jnp.int32)
    key_pos = jnp.concatenate(
        [half_index, seq_len - block_len * (half_index // block_len + 1) + half_index % block_len]
    ).reshape(key_blocks, key_rows)
    key_seg = segments.reshape(key_blocks, key_rows)
    query_seg = lax.dynamic_slice_in_dim(segments[0], ctx_index * block_len, block_len, 1).reshape(
        token_count
    )
    cos_tab, sine_tab = rope_tables(query_pos, HD)
    queries = rotate(projected[:, :model_width].reshape(head_shape), cos_tab, sine_tab).astype(
        jnp.bfloat16
    )
    keys_own = rotate(
        projected[:, model_width : 2 * model_width].reshape(head_shape), cos_tab, sine_tab
    ).astype(jnp.bfloat16)
    values_own = projected[:, 2 * model_width :].astype(jnp.bfloat16)
    keys_all, values_all = (
        lax.all_gather(keys_own.reshape(2, block_len, model_width), "ctx", axis=1, tiled=True),
        lax.all_gather(values_own.reshape(2, block_len, model_width), "ctx", axis=1, tiled=True),
    )
    keys_all = keys_all.reshape(key_blocks, key_rows, head_count, HD)
    values_all = values_all.reshape(key_blocks, key_rows, head_count, HD)

    def score_block(key_blk, pos_blk, seg_blk):
        raw_scores = (
            jnp.einsum("qhd,khd->hqk", queries, key_blk, preferred_element_type=jnp.float32)
            * score_scale
        )
        allowed = (pos_blk[None, :] <= query_pos[:, None]) & (
            seg_blk[None, :] == query_seg[:, None]
        )
        return (jnp.where(allowed[None], raw_scores, MASK_FILL), allowed)

    def total_step(running, key_part):
        run_max, run_sum = running
        scores = score_block(key_part[0], key_part[1], key_part[2])[0]
        new_max = jnp.maximum(run_max, jnp.max(scores, axis=-1))
        run_sum = run_sum * jnp.exp(run_max - new_max) + jnp.sum(
            jnp.exp(scores - new_max[..., None]), axis=-1
        )
        return ((new_max, run_sum), None)

    start_max = jnp.full((head_count, token_count), MASK_FILL, jnp.float32)
    start_sum = jnp.zeros((head_count, token_count), jnp.float32)
    (run_max, run_sum), unused = lax.scan(
        total_step, (start_max, start_sum), (keys_all, key_pos, key_seg)
    )
    log_total = run_max + jnp.log(run_sum)

    def attend_step(summed, key_part):
        key_blk, value_blk, pos_blk, seg_blk = key_part
        scores = score_block(key_blk, pos_blk, seg_blk)[0]
        weights = jnp.exp(scores - log_total[..., None]).astype(jnp.bfloat16)
        return (
            summed
            + jnp.einsum("hqk,khd->qhd", weights, value_blk, preferred_element_type=jnp.float32),
            None,
        )

    key_stack = (keys_all, values_all, key_pos, key_seg)
    attended, unused = lax.scan(attend_step, jnp.zeros(head_shape, jnp.float32), key_stack)
    attn_low = attended.reshape(token_count, model_width).astype(jnp.bfloat16)
    residual = inputs + jnp.dot(attn_low, out_weight, preferred_element_type=jnp.float32)
    ffn_set = (
        lax.all_gather(gain_ffn, ("ctx", "fsdp"), axis=0, tiled=True),
        lax.all_gather(w_router, ("ctx", "fsdp"), axis=0, tiled=True),
        lax.all_gather(w_shared_gate, ("ctx", "fsdp"), axis=0, tiled=True),
        lax.all_gather(w_shared_in, ("ctx", "fsdp"), axis=0, tiled=True),
        lax.all_gather(w_shared_out, ("ctx", "fsdp"), axis=0, tiled=True),
    )
    ffn_gain, router_weight, gate_vector, shared_in, shared_out = ffn_set
    normed_two, inv_two = rms_norm(residual, ffn_gain.astype(jnp.float32))
    low_two = normed_two.astype(jnp.bfloat16)
    logits = jnp.dot(low_two, router_weight, preferred_element_type=jnp.float32)
    router_probs = jax.nn.softmax(logits, axis=-1)
    chosen = routes.reshape(token_count, top_count)
    chosen_mask = chosen[..., None] == jnp.arange(expert_count, dtype=jnp.int32)
    gate_vals = jnp.sum(jnp.where(chosen_mask, router_probs[:, None, :], 0.0), axis=-1)
    shared_scale = jax.nn.sigmoid(jnp.dot(low_two, gate_vector, preferred_element_type=jnp.float32))
    shared_pre = jnp.dot(low_two, shared_in, preferred_element_type=jnp.float32)
    shared_hid = swiglu(shared_pre, FS).astype(jnp.bfloat16)
    shared_res = jnp.dot(shared_hid, shared_out, preferred_element_type=jnp.float32)
    pair_routes = chosen.reshape(token_count * top_count)
    expert_marks = (
        pair_routes[:, None] == jnp.arange(expert_count, dtype=jnp.int32)[None, :]
    ).astype(jnp.int32)
    pair_ranks = jnp.sum((jnp.cumsum(expert_marks, axis=0) - expert_marks) * expert_marks, axis=1)
    pair_target = jnp.where(pair_ranks < capacity, pair_routes * capacity + pair_ranks, -1)
    pair_map = pair_target[:, None] == jnp.arange(slot_count, dtype=jnp.int32)[None, :]
    pair_low = pair_map.astype(jnp.bfloat16)
    token_map = jnp.sum(
        pair_map.reshape(token_count, top_count, slot_count).astype(jnp.int32), axis=1
    ).astype(jnp.bfloat16)
    outgoing = jnp.einsum(
        "tc,td->cd", token_map, low_two, preferred_element_type=jnp.float32
    ).astype(jnp.bfloat16)
    incoming = lax.all_to_all(
        outgoing.reshape(expert_count, capacity, model_width),
        "ctx",
        split_axis=0,
        concat_axis=1,
        tiled=True,
    )
    expert_in, expert_out = (
        lax.all_gather(w_expert_in, "fsdp", axis=1, tiled=True),
        lax.all_gather(w_expert_out, "fsdp", axis=1, tiled=True),
    )
    expert_pre = jnp.einsum("erd,edf->erf", incoming, expert_in, preferred_element_type=jnp.float32)
    expert_hid = swiglu(expert_pre, FE).astype(jnp.bfloat16)
    expert_res = jnp.einsum(
        "erf,efd->erd", expert_hid, expert_out, preferred_element_type=jnp.float32
    ).astype(jnp.bfloat16)
    returned = lax.all_to_all(expert_res, "ctx", split_axis=1, concat_axis=0, tiled=True).reshape(
        slot_count, model_width
    )
    pair_vals = jnp.dot(pair_low, returned, preferred_element_type=jnp.float32).reshape(
        token_count, top_count, model_width
    )
    routed = jnp.sum(gate_vals[..., None] * pair_vals, axis=1)
    output = (
        (residual + shared_scale[:, None] * shared_res + routed)
        .astype(jnp.bfloat16)
        .reshape(tokens.shape)
    )
    grad_out = cotangent.reshape(token_count, model_width).astype(jnp.float32)
    pair_grads = gate_vals[..., None] * grad_out[:, None, :]
    grad_gates = jnp.sum(grad_out[:, None, :] * pair_vals, axis=-1)
    grad_returned = jnp.einsum(
        "pc,pd->cd",
        pair_map.astype(jnp.float32),
        pair_grads.reshape(token_count * top_count, model_width),
        precision=HIGHEST,
    ).astype(jnp.bfloat16)
    grad_res = lax.all_to_all(
        grad_returned.reshape(expert_count, capacity, model_width),
        "ctx",
        split_axis=0,
        concat_axis=1,
        tiled=True,
    )
    grad_expert_out = jnp.einsum(
        "erf,erd->efd", expert_hid, grad_res, preferred_element_type=jnp.float32
    )
    grad_hid = jnp.einsum("erd,efd->erf", grad_res, expert_out, preferred_element_type=jnp.float32)
    grad_pre = swiglu_back(expert_pre, FE, grad_hid).astype(jnp.bfloat16)
    grad_expert_in = jnp.einsum(
        "erd,erf->edf", incoming, grad_pre, preferred_element_type=jnp.float32
    )
    grad_incoming = jnp.einsum(
        "erf,edf->erd", grad_pre, expert_in, preferred_element_type=jnp.float32
    ).astype(jnp.bfloat16)
    grad_outgoing = lax.all_to_all(
        grad_incoming, "ctx", split_axis=1, concat_axis=0, tiled=True
    ).reshape(slot_count, model_width)
    expert_grads = (
        lax.psum_scatter(
            grad_expert_in.astype(jnp.bfloat16), "fsdp", scatter_dimension=1, tiled=True
        ).astype(jnp.float32),
        lax.psum_scatter(
            grad_expert_out.astype(jnp.bfloat16), "fsdp", scatter_dimension=1, tiled=True
        ).astype(jnp.float32),
    )
    grad_two = jnp.einsum("tc,cd->td", token_map, grad_outgoing, preferred_element_type=jnp.float32)
    grad_probs = jnp.sum(jnp.where(chosen_mask, grad_gates[..., None], 0.0), axis=1)
    grad_logits = (
        router_probs * (grad_probs - jnp.sum(router_probs * grad_probs, axis=-1, keepdims=True))
    ).astype(jnp.bfloat16)
    grad_router = jnp.einsum("td,te->de", low_two, grad_logits, preferred_element_type=jnp.float32)
    grad_shared_res = (shared_scale[:, None] * grad_out).astype(jnp.bfloat16)
    grad_gate_pre = (
        jnp.sum(grad_out * shared_res, axis=-1) * shared_scale * (1.0 - shared_scale)
    ).astype(jnp.bfloat16)
    grad_shared_out = jnp.einsum(
        "tf,td->fd", shared_hid, grad_shared_res, preferred_element_type=jnp.float32
    )
    grad_shared_hid = jnp.einsum(
        "td,fd->tf", grad_shared_res, shared_out, preferred_element_type=jnp.float32
    )
    grad_shared_pre = swiglu_back(shared_pre, FS, grad_shared_hid).astype(jnp.bfloat16)
    grad_shared_in = jnp.einsum(
        "td,tf->df", low_two, grad_shared_pre, preferred_element_type=jnp.float32
    )
    grad_gate_vector = jnp.einsum(
        "td,t->d", low_two, grad_gate_pre, preferred_element_type=jnp.float32
    )
    grad_two = grad_two + jnp.einsum(
        "te,de->td", grad_logits, router_weight, preferred_element_type=jnp.float32
    )
    grad_two = grad_two + jnp.einsum(
        "tf,df->td", grad_shared_pre, shared_in, preferred_element_type=jnp.float32
    )
    grad_two = (
        grad_two
        + grad_gate_pre.astype(jnp.float32)[:, None] * gate_vector.astype(jnp.float32)[None, :]
    )
    grad_resid_norm, grad_gain_two = rms_back(
        residual, inv_two, ffn_gain.astype(jnp.float32), grad_two
    )
    grad_resid = grad_out + grad_resid_norm
    ffn_grads = (
        lax.psum_scatter(grad_gain_two, ("ctx", "fsdp"), scatter_dimension=0, tiled=True),
        lax.psum_scatter(grad_router, ("ctx", "fsdp"), scatter_dimension=0, tiled=True),
        lax.psum_scatter(grad_gate_vector, ("ctx", "fsdp"), scatter_dimension=0, tiled=True),
        lax.psum_scatter(grad_shared_in, ("ctx", "fsdp"), scatter_dimension=0, tiled=True),
        lax.psum_scatter(grad_shared_out, ("ctx", "fsdp"), scatter_dimension=0, tiled=True),
    )
    grad_mixed = grad_resid.astype(jnp.bfloat16)
    grad_out_weight = jnp.einsum(
        "tc,td->cd", attn_low, grad_mixed, preferred_element_type=jnp.float32
    )
    grad_attn = (
        jnp.einsum("td,cd->tc", grad_mixed, out_weight, preferred_element_type=jnp.float32)
        .astype(jnp.bfloat16)
        .reshape(head_shape)
    )

    def delta_step(summed, key_part):
        key_blk, value_blk, pos_blk, seg_blk = key_part
        weights = jnp.exp(score_block(key_blk, pos_blk, seg_blk)[0] - log_total[..., None])
        grad_weights = jnp.einsum(
            "qhd,khd->hqk", grad_attn, value_blk, preferred_element_type=jnp.float32
        )
        return (summed + jnp.sum(weights * grad_weights, axis=-1), None)

    delta_sum, unused = lax.scan(
        delta_step, jnp.zeros((head_count, token_count), jnp.float32), key_stack
    )

    def grad_step(summed, key_part):
        key_blk, value_blk, pos_blk, seg_blk = key_part
        scores, allowed = score_block(key_blk, pos_blk, seg_blk)
        weights = jnp.exp(scores - log_total[..., None])
        grad_weights = jnp.einsum(
            "qhd,khd->hqk", grad_attn, value_blk, preferred_element_type=jnp.float32
        )
        grad_scores = jnp.where(
            allowed[None], weights * (grad_weights - delta_sum[..., None]), 0.0
        ).astype(jnp.bfloat16)
        summed = (
            summed
            + jnp.einsum("hqk,khd->qhd", grad_scores, key_blk, preferred_element_type=jnp.float32)
            * score_scale
        )
        grad_key = (
            jnp.einsum("hqk,qhd->khd", grad_scores, queries, preferred_element_type=jnp.float32)
            * score_scale
        )
        grad_value = jnp.einsum(
            "hqk,qhd->khd",
            weights.astype(jnp.bfloat16),
            grad_attn,
            preferred_element_type=jnp.float32,
        )
        return (summed, (grad_key, grad_value))

    grad_query, (grad_keys, grad_values) = lax.scan(
        grad_step, jnp.zeros(head_shape, jnp.float32), key_stack
    )
    grad_keys_own, grad_values_own = (
        lax.psum_scatter(
            grad_keys.reshape(2, half_len, model_width).astype(jnp.bfloat16),
            "ctx",
            scatter_dimension=1,
            tiled=True,
        ).astype(jnp.float32),
        lax.psum_scatter(
            grad_values.reshape(2, half_len, model_width).astype(jnp.bfloat16),
            "ctx",
            scatter_dimension=1,
            tiled=True,
        ).astype(jnp.float32),
    )
    grad_q_rows = rotate_back(grad_query, cos_tab, sine_tab).reshape(token_count, model_width)
    grad_k_rows = rotate_back(grad_keys_own.reshape(head_shape), cos_tab, sine_tab).reshape(
        token_count, model_width
    )
    grad_projected = jnp.concatenate(
        [grad_q_rows, grad_k_rows, grad_values_own.reshape(token_count, model_width)], axis=-1
    ).astype(jnp.bfloat16)
    grad_qkv_weight = jnp.einsum(
        "td,te->de", normed_low, grad_projected, preferred_element_type=jnp.float32
    )
    grad_qkv_bias = jnp.sum(grad_projected.astype(jnp.float32), axis=0)
    grad_normed = jnp.einsum(
        "te,de->td", grad_projected, qkv_weight, preferred_element_type=jnp.float32
    )
    grad_inputs_norm, grad_gain_one = rms_back(
        inputs, inv_one, attn_gain.astype(jnp.float32), grad_normed
    )
    grad_tokens = (grad_resid + grad_inputs_norm).reshape(tokens.shape)
    attn_grads = (
        lax.psum_scatter(grad_qkv_weight, ("ctx", "fsdp"), scatter_dimension=0, tiled=True),
        lax.psum_scatter(grad_qkv_bias, ("ctx", "fsdp"), scatter_dimension=0, tiled=True),
        lax.psum_scatter(grad_out_weight, ("ctx", "fsdp"), scatter_dimension=0, tiled=True),
        lax.psum_scatter(grad_gain_one, ("ctx", "fsdp"), scatter_dimension=0, tiled=True),
    )
    return (
        output,
        grad_tokens,
        attn_grads[0],
        attn_grads[1],
        attn_grads[2],
        attn_grads[3],
        ffn_grads[0],
        ffn_grads[1],
        ffn_grads[2],
        ffn_grads[3],
        ffn_grads[4],
        expert_grads[0],
        expert_grads[1],
    )


def solution(mesh):
    in_specs = (
        P("fsdp", None, "ctx", None),
        P("fsdp", None, None),
        P("fsdp", None, "ctx", None),
        P("fsdp", None, "ctx", None),
        P(("ctx", "fsdp"), None),
        P(("ctx", "fsdp")),
        P(("ctx", "fsdp"), None),
        P(("ctx", "fsdp")),
        P(("ctx", "fsdp")),
        P(("ctx", "fsdp"), None),
        P(("ctx", "fsdp")),
        P(("ctx", "fsdp"), None),
        P(("ctx", "fsdp"), None),
        P("ctx", "fsdp", None),
        P("ctx", "fsdp", None),
    )
    out_specs = (
        P("fsdp", None, "ctx", None),
        P("fsdp", None, "ctx", None),
        P(("ctx", "fsdp"), None),
        P(("ctx", "fsdp")),
        P(("ctx", "fsdp"), None),
        P(("ctx", "fsdp")),
        P(("ctx", "fsdp")),
        P(("ctx", "fsdp"), None),
        P(("ctx", "fsdp")),
        P(("ctx", "fsdp"), None),
        P(("ctx", "fsdp"), None),
        P("ctx", "fsdp", None),
        P("ctx", "fsdp", None),
    )
    ctx_size = mesh.shape["ctx"]
    fsdp_size = mesh.shape["fsdp"]

    def local(*arrays):
        if HEADS % ctx_size:
            return local_wide(*arrays)
        return local_split(ctx_size, fsdp_size, *arrays)

    return jax.shard_map(local, mesh=mesh, in_specs=in_specs, out_specs=out_specs, check_vma=False)
```

```python
import jax
import jax.numpy as jnp
from jax import lax
from jax.sharding import PartitionSpec as P

HD = 128
HEADS = 16
FS = 5632
FE = 1408


RMS_EPS = 1e-06
ROPE_THETA = 1000000.0
MASK_FILL = -1e30
HIGHEST = lax.Precision.HIGHEST


def rope_tables(positions, head_dim):
    half_dim = head_dim // 2
    inv_freq = ROPE_THETA ** (-(jnp.arange(half_dim, dtype=jnp.float32) * 2.0 / head_dim))
    angles = positions.astype(jnp.float32)[:, None] * inv_freq[None, :]
    cos_tab = jnp.concatenate([jnp.cos(angles), jnp.cos(angles)], axis=-1)
    sine_tab = jnp.concatenate([jnp.sin(angles), jnp.sin(angles)], axis=-1)
    return (cos_tab, sine_tab)


def rotate(values, cos_tab, sine_tab):
    half_dim = values.shape[-1] // 2
    turned = jnp.concatenate([-values[..., half_dim:], values[..., :half_dim]], axis=-1)
    return values * cos_tab[:, None, :] + turned * sine_tab[:, None, :]


def rotate_back(upstream, cos_tab, sine_tab):
    half_dim = upstream.shape[-1] // 2
    scaled = upstream * sine_tab[:, None, :]
    return upstream * cos_tab[:, None, :] + jnp.concatenate(
        [scaled[..., half_dim:], -scaled[..., :half_dim]], axis=-1
    )


def rms_norm(values, gain_vec):
    inv_rms = lax.rsqrt(jnp.mean(values * values, axis=-1, keepdims=True) + RMS_EPS)
    return (values * inv_rms * gain_vec, inv_rms)


def rms_back(values, inv_rms, gain_vec, upstream):
    weighted = upstream * gain_vec
    inner_mean = jnp.mean(weighted * values, axis=-1, keepdims=True)
    return (
        inv_rms * weighted - values * inv_rms * inv_rms * inv_rms * inner_mean,
        jnp.sum(upstream * values * inv_rms, axis=0),
    )


def swiglu(pre_act, split_at):
    return jax.nn.silu(pre_act[..., :split_at]) * pre_act[..., split_at:]


def swiglu_back(pre_act, split_at, upstream):
    gate_part = pre_act[..., :split_at]
    up_part = pre_act[..., split_at:]
    sigmoid_g = jax.nn.sigmoid(gate_part)
    d_gate = upstream * up_part * sigmoid_g * (1.0 + gate_part * (1.0 - sigmoid_g))
    d_up = upstream * gate_part * sigmoid_g
    return jnp.concatenate([d_gate, d_up], axis=-1)


def ring_order(size):
    return list(range(0, size, 2)) + list(range(size - 1, 0, -2))


def ring_steps(size):
    order = ring_order(size)
    ahead = [(order[i], order[(i + 1) % size]) for i in range(size)]
    back = [(dst, src) for src, dst in ahead]
    return (ahead, back)


def ring_peers(size, ctx_index):
    order = ring_order(size)
    place = {dev: i for i, dev in enumerate(order)}
    table = jnp.array(
        [[order[(place[dev] + k) % size] for k in range(size)] for dev in range(size)], jnp.int32
    )
    row = lax.dynamic_index_in_dim(table, ctx_index, 0, keepdims=False)
    return [row[k] for k in range(size)]


def after(value, *deps):
    return lax.optimization_barrier((value,) + deps)


def ring_gather(block, size, ctx_index, rider=None):
    rows, width = block.shape

    def put(out, piece, peer, offset):
        return lax.dynamic_update_slice(out, piece, (peer * rows + offset, jnp.zeros_like(peer)))

    out = jnp.zeros((size * rows, width), block.dtype)
    ahead, back = ring_steps(size)
    peers = ring_peers(size, ctx_index)
    half = size // 2
    out = put(out, block, ctx_index, 0)
    fore = rear = block
    for k in range(1, half):
        fore = lax.ppermute(fore, "ctx", ahead)
        rear = lax.ppermute(rear, "ctx", back)
        if rider is not None and k == 2:
            fore, rider = after(fore, rider)
        out = put(out, fore, peers[size - k], 0)
        out = put(out, rear, peers[k], 0)
    fore = lax.ppermute(fore[: rows // 2], "ctx", ahead)
    rear = lax.ppermute(rear[rows // 2 :], "ctx", back)
    out = put(out, fore, peers[half], 0)
    out = put(out, rear, peers[half], rows // 2)
    return out if rider is None else (out, rider)


def ring_sums(parts, size, ctx_index):
    f32 = jnp.float32
    rows = parts.shape[0] // size
    ahead, back = ring_steps(size)
    peers = ring_peers(size, ctx_index)
    half = size // 2

    def own(k, start, count):
        first = (peers[k % size] * rows + start, jnp.zeros_like(peers[0]))
        return lax.dynamic_slice(parts, first, (count, parts.shape[1])).astype(f32)

    def low(values):
        return values.astype(jnp.bfloat16)

    cut = rows // 2
    fore = lax.ppermute(low(own(half, 0, cut)), "ctx", ahead)
    rear = lax.ppermute(low(own(half, cut, cut)), "ctx", back)
    fore = jnp.concatenate(
        [low(fore.astype(f32) + own(half - 1, 0, cut)), low(own(half - 1, cut, cut))], axis=0
    )
    rear = jnp.concatenate(
        [low(own(1 - half, 0, cut)), low(rear.astype(f32) + own(1 - half, cut, cut))], axis=0
    )
    for k in range(half - 1, 0, -1):
        fore = lax.ppermute(fore, "ctx", ahead)
        rear = lax.ppermute(rear, "ctx", back)
        if k > 1:
            fore = low(fore.astype(f32) + own(k - 1, 0, rows))
            rear = low(rear.astype(f32) + own(1 - k, 0, rows))
    return (fore, rear)


def ring_scatter(parts, size, ctx_index, kept=None):
    fore, rear = ring_sums(parts, size, ctx_index)
    kept = (parts if kept is None else kept).reshape(size, -1, parts.shape[1])
    kept = lax.dynamic_index_in_dim(kept, ctx_index, 0, keepdims=False)
    return kept.astype(jnp.float32) + fore.astype(jnp.float32) + rear.astype(jnp.float32)


def other_core(size):
    return [(i, i ^ 1) for i in range(size)]


def other_chip(size):
    return [(i, i ^ 2) for i in range(size)]


def fsdp_gather(shard, size, hold):
    index = lax.axis_index("fsdp")
    rows, width = shard.shape
    far = lax.ppermute(shard, "fsdp", other_chip(size))
    far, hold = after(far, hold)
    pair = jnp.where(
        index < 2, jnp.stack([shard, far], axis=0), jnp.stack([far, shard], axis=0)
    )
    near = lax.ppermute(pair, "fsdp", other_core(size))
    out = jnp.zeros((2, 2, rows, width), shard.dtype)
    out = lax.dynamic_update_index_in_dim(out, pair, index % 2, 1)
    out = lax.dynamic_update_index_in_dim(out, near, 1 - index % 2, 1)
    return (out.reshape(size * rows, width), hold)


def column_pieces(weight, groups, size, extra):
    rows = weight.shape[0]
    width = weight.shape[1] // (groups * size)
    pieces = weight.reshape(rows, groups, size, width).transpose(2, 0, 1, 3)
    pieces = pieces.reshape(size, rows, groups * width)
    if extra is not None:
        count = extra.shape[0]
        more = -(-count // (groups * width * 16)) * 16
        extra = jnp.pad(extra, (0, more * groups * width - count))
        extra = jnp.broadcast_to(
            extra.reshape(1, more, groups * width), (size, more, groups * width)
        )
        pieces = jnp.concatenate([pieces, extra], axis=1)
    return pieces


def merge_columns(pieces, groups, size):
    width = pieces.shape[2] // groups
    if width % 128 == 0:
        pieces = pieces.reshape(size, -1, groups, width).transpose(1, 2, 0, 3)
        return pieces.reshape(-1, groups * size * width).astype(jnp.float32)
    columns = [
        pieces[peer, :, group * width : (group + 1) * width]
        for group in range(groups)
        for peer in range(size)
    ]
    return jnp.concatenate(columns, axis=1).astype(jnp.float32)


def local_split(
    ctx_size,
    fsdp_size,
    tokens,
    segments,
    routes,
    cotangent,
    w_qkv,
    b_qkv,
    w_out,
    gain_attn,
    gain_ffn,
    w_router,
    w_shared_gate,
    w_shared_in,
    w_shared_out,
    w_expert_in,
    w_expert_out,
):
    bf16, f32, i32 = jnp.bfloat16, jnp.float32, jnp.int32
    device_count = ctx_size * fsdp_size
    block_len = tokens.shape[2]
    width = tokens.shape[3]
    token_count = 2 * block_len
    top_count = routes.shape[3]
    seq_len = token_count * ctx_size
    ctx_index = lax.axis_index("ctx")
    expert_count = w_router.shape[1]
    capacity = token_count * top_count // expert_count
    own_heads = HEADS // ctx_size
    own_width = own_heads * HD
    fs_own = FS // ctx_size
    score_scale = HD ** (-0.5)

    def dot(a, b):
        return jnp.dot(a, b, preferred_element_type=f32)

    def dot_t(a, b):
        return lax.dot_general(a, b, (((1,), (1,)), ((), ())), preferred_element_type=f32)

    def t_dot(a, b):
        return lax.dot_general(a, b, (((0,), (0,)), ((), ())), preferred_element_type=f32)

    def own_rows(values):
        return lax.dynamic_index_in_dim(
            values.reshape((ctx_size, token_count) + values.shape[1:]), ctx_index, 0, keepdims=False
        )

    def sum_rows(grad):
        return lax.psum_scatter(grad.astype(bf16), "fsdp", scatter_dimension=0, tiled=True)

    shard = width // device_count
    small = [gain_attn, gain_ffn, w_shared_gate, w_router.reshape(-1), b_qkv]
    small_size = sum(piece.shape[0] for piece in small)
    small = jnp.concatenate(small + [routes.astype(bf16).reshape(-1)], axis=0)
    small_count = small.shape[0]
    own_tokens = tokens.reshape(token_count, width).astype(f32)
    own_scaled, inv_one = rms_norm(own_tokens, 1.0)
    scaled_rows = ring_gather(own_scaled.astype(bf16), ctx_size, ctx_index)
    pieces = column_pieces(w_qkv, 3, ctx_size, small)
    pieces = lax.all_to_all(pieces, "ctx", split_axis=0, concat_axis=0, tiled=True)
    shared_in = column_pieces(w_shared_in, 2, ctx_size, None)
    shared_in, scaled_rows = after(shared_in, scaled_rows)
    shared_in = lax.all_to_all(shared_in, "ctx", split_axis=0, concat_axis=0, tiled=True)
    pieces = lax.all_gather(pieces, "fsdp", axis=0, tiled=False).transpose(1, 0, 2, 3)
    qkv_weight = pieces[:, :, :shard].reshape(width, 3 * own_width)
    small = pieces[:, :, shard:].reshape(device_count, -1)[:, :small_count]
    attn_gain = small[:, :shard].reshape(width).astype(f32)
    ffn_gain = small[:, shard : 2 * shard].reshape(width).astype(f32)
    gate_vector = small[:, 2 * shard : 3 * shard].reshape(width)
    router_end = 3 * shard + shard * expert_count
    router_weight = small[:, 3 * shard : router_end].reshape(width, expert_count)
    bias = small[:, router_end:small_size].reshape(3, ctx_size, own_width).astype(f32)
    bias = lax.dynamic_index_in_dim(bias, ctx_index, 1, keepdims=False).reshape(3 * own_width)
    route_rows = small[:, small_size:].astype(i32)
    route_rows = lax.dynamic_index_in_dim(
        route_rows.reshape(ctx_size, fsdp_size, -1), lax.axis_index("fsdp"), 1, keepdims=False
    ).reshape(ctx_size, token_count, top_count)

    expert_in = lax.all_gather(w_expert_in[0], "fsdp", axis=0, tiled=True)

    block_ids = jnp.arange(ctx_size, dtype=i32)[:, None]
    local_index = jnp.arange(block_len, dtype=i32)[None, :]
    positions = jnp.stack(
        [
            block_ids * block_len + local_index,
            seq_len - (block_ids + 1) * block_len + local_index,
        ],
        axis=1,
    ).reshape(seq_len)
    seg_rows = (
        segments.reshape(2, ctx_size, block_len).transpose(1, 0, 2).reshape(seq_len)
    )
    cos_tab, sine_tab = rope_tables(positions, HD)

    normed_low = (scaled_rows.astype(f32) * attn_gain).astype(bf16)
    projected = dot(normed_low, qkv_weight) + bias
    head_shape = (seq_len, own_heads, HD)
    queries = rotate(projected[:, :own_width].reshape(head_shape), cos_tab, sine_tab).astype(bf16)
    keys = rotate(
        projected[:, own_width : 2 * own_width].reshape(head_shape), cos_tab, sine_tab
    ).astype(bf16)
    values = projected[:, 2 * own_width :].reshape(head_shape).astype(bf16)
    out_weight, queries = fsdp_gather(w_out, fsdp_size, queries)
    allowed = (positions[None, :] <= positions[:, None]) & (seg_rows[None, :] == seg_rows[:, None])
    scores = jnp.einsum("qhd,khd->hqk", queries, keys, preferred_element_type=f32) * score_scale
    scores = jnp.where(allowed[None], scores, MASK_FILL)
    top_score = jnp.max(scores, axis=-1, keepdims=True)
    log_total = top_score + jnp.log(jnp.sum(jnp.exp(scores - top_score), axis=-1, keepdims=True))
    weights = jnp.exp(scores - log_total)
    weights_low = weights.astype(bf16)
    attended = jnp.einsum("hqk,khd->qhd", weights_low, values, preferred_element_type=f32)
    attn_own = attended.astype(bf16).reshape(seq_len, own_width)
    shared_out, attn_own = fsdp_gather(w_shared_out, fsdp_size, attn_own)
    expert_out, attn_own = fsdp_gather(w_expert_out[0], fsdp_size, attn_own)
    attn_parts, shared_in = after(dot(attn_own, out_weight).astype(bf16), shared_in)
    shared_in = lax.all_gather(shared_in, "fsdp", axis=0, tiled=False)
    own_residual = own_tokens + ring_scatter(attn_parts, ctx_size, ctx_index)

    normed_two, inv_two = rms_norm(own_residual, ffn_gain)
    own_low = normed_two.astype(bf16)
    low_two, grad_rows = ring_gather(
        own_low, ctx_size, ctx_index, cotangent.reshape(token_count, width)
    )
    grad_rows = lax.all_gather(grad_rows, "ctx", axis=0, tiled=True)
    mixed_weight = jnp.concatenate([router_weight, gate_vector[:, None]], axis=1)
    logits = dot(low_two, mixed_weight)
    probs_all = jax.nn.softmax(logits[:, :expert_count], axis=-1)
    scale_all = jax.nn.sigmoid(logits[:, expert_count])
    gate_all = lax.dynamic_index_in_dim(probs_all, ctx_index, 1, keepdims=False)

    named = jnp.any(route_rows == ctx_index, axis=-1)
    before = jnp.arange(token_count)[:, None] < jnp.arange(token_count)[None, :]
    rank = dot(named.astype(bf16), before.astype(bf16)).astype(i32)
    slot_of = jnp.where(named & (rank < capacity), rank, -1)
    slot_mask = slot_of[:, None, :] == jnp.arange(capacity, dtype=i32)[None, :, None]
    slot_map = slot_mask.astype(bf16)
    blocks_two = low_two.reshape(ctx_size, token_count, width)
    gate_blocks = gate_all.reshape(ctx_size, token_count)

    def to_slots(blocks):
        picked = jnp.einsum("bmt,btd->bmd", slot_map, blocks, preferred_element_type=f32)
        return picked.reshape(ctx_size * capacity, width)

    def to_tokens(slots):
        spread = jnp.einsum(
            "bmt,bmd->btd",
            slot_map,
            slots.reshape(ctx_size, capacity, width),
            preferred_element_type=f32,
        )
        return spread.reshape(seq_len, width)

    buffer = to_slots(blocks_two).astype(bf16)
    expert_pre = dot(buffer, expert_in)
    expert_hid = swiglu(expert_pre, FE).astype(bf16)
    expert_res = dot(expert_hid, expert_out).astype(bf16)
    routed = gate_all[:, None] * to_tokens(expert_res)

    shared_in, expert_res = after(shared_in, expert_res)
    shared_in = shared_in.transpose(1, 0, 2, 3).reshape(width, 2 * fs_own)
    shared_pre = dot(low_two, shared_in)
    shared_hid = swiglu(shared_pre, fs_own).astype(bf16)
    shared_res = dot(shared_hid, shared_out)
    out_parts = (scale_all[:, None] * shared_res + routed).astype(bf16)
    grad_rows, out_parts = after(grad_rows, out_parts)

    grad_slots = to_slots(grad_rows.reshape(ctx_size, token_count, width))
    gate_slots = jnp.sum(jnp.where(slot_mask, gate_blocks[:, None, :], 0.0), axis=-1).reshape(-1, 1)
    grad_res = (gate_slots * grad_slots).astype(bf16)
    grad_hid = dot_t(grad_res, expert_out)
    slot_terms = jnp.sum(expert_hid.astype(f32) * grad_hid, axis=-1)
    slot_terms = slot_terms.reshape(ctx_size, capacity, 1)
    gate_terms = jnp.sum(jnp.where(slot_mask, slot_terms, 0.0), axis=1)
    grad_pre = swiglu_back(expert_pre, FE, grad_hid).astype(bf16)
    grad_expert_in = t_dot(buffer, grad_pre)
    grad_buffer = dot_t(grad_pre, expert_in).astype(bf16)

    grad_f32 = grad_rows.astype(f32)
    grad_expert_in, grad_shared_res = after(
        grad_expert_in.astype(bf16), (scale_all[:, None] * grad_f32).astype(bf16)
    )
    sum_expert_in = sum_rows(grad_expert_in)

    grad_shared_hid = dot_t(grad_shared_res, shared_out)
    scale_terms = jnp.sum(shared_hid.astype(f32) * grad_shared_hid, axis=-1)
    grad_shared_pre = swiglu_back(shared_pre, fs_own, grad_shared_hid).astype(bf16)
    two_parts = (dot_t(grad_shared_pre, shared_in) + to_tokens(grad_buffer)).astype(bf16)
    two_parts, expert_hid, shared_hid, grad_shared_pre = after(
        two_parts, expert_hid, shared_hid, grad_shared_pre
    )
    grad_expert_out = t_dot(expert_hid, grad_res).astype(bf16)
    grad_shared_out = t_dot(shared_hid, grad_shared_res).astype(bf16)
    grad_shared_in = t_dot(low_two, grad_shared_pre).astype(bf16)
    grad_two = ring_scatter(two_parts, ctx_size, ctx_index)
    dots = jnp.stack([gate_terms, scale_terms.reshape(ctx_size, token_count)], axis=1)
    dots = lax.all_to_all(dots, "ctx", split_axis=0, concat_axis=0, tiled=True)
    grad_two, grad_shared_in, grad_shared_out, grad_expert_out, dots = after(
        grad_two, grad_shared_in, grad_shared_out, grad_expert_out, dots
    )
    sum_shared_in = grad_shared_in.reshape(ctx_size, fsdp_size, shard, 2 * fs_own)
    sum_shared_in = lax.psum_scatter(
        sum_shared_in.transpose(1, 0, 2, 3).reshape(width, 2 * fs_own),
        "fsdp",
        scatter_dimension=0,
        tiled=True,
    ).reshape(ctx_size, shard, 2 * fs_own)
    sum_expert_out = sum_rows(grad_expert_out)
    own_probs = own_rows(probs_all)
    own_scale = own_rows(scale_all)
    own_chosen = routes.reshape(token_count, top_count)
    chosen_mask = jnp.any(
        own_chosen[..., None] == jnp.arange(expert_count, dtype=i32), axis=1
    )
    prob_terms = jnp.where(chosen_mask, dots[:, 0].T, 0.0)
    grad_logits = (
        prob_terms - own_probs * jnp.sum(prob_terms, axis=-1, keepdims=True)
    ).astype(bf16)
    grad_gate_pre = (jnp.sum(dots[:, 1], axis=0) * (1.0 - own_scale)).astype(bf16)
    grad_router = t_dot(own_low, grad_logits)
    grad_gate_vector = t_dot(own_low, grad_gate_pre[:, None])
    grad_two = grad_two + dot_t(grad_logits, router_weight)
    grad_two = grad_two + grad_gate_pre.astype(f32)[:, None] * gate_vector.astype(f32)[None, :]
    grad_resid_norm, grad_gain_two = rms_back(
        own_residual, inv_two, ffn_gain, grad_two
    )
    grad_resid = cotangent.reshape(token_count, width).astype(f32) + grad_resid_norm

    grad_mixed, sum_expert_in = after(grad_resid.astype(bf16), sum_expert_in)
    mixed_all = ring_gather(grad_mixed, ctx_size, ctx_index)
    grad_attn = dot_t(mixed_all, out_weight).astype(bf16).reshape(head_shape)
    grad_attn, sum_shared_in = after(grad_attn, sum_shared_in)
    sum_shared_in = lax.all_to_all(
        sum_shared_in, "ctx", split_axis=0, concat_axis=0, tiled=True
    )
    grad_weights = jnp.einsum("qhd,khd->hqk", grad_attn, values, preferred_element_type=f32)
    delta = jnp.sum(weights * grad_weights, axis=-1, keepdims=True)
    grad_scores = jnp.where(allowed[None], weights * (grad_weights - delta), 0.0).astype(bf16)
    grad_q = jnp.einsum("hqk,khd->qhd", grad_scores, keys, preferred_element_type=f32) * score_scale
    grad_k = (
        jnp.einsum("hqk,qhd->khd", grad_scores, queries, preferred_element_type=f32) * score_scale
    )
    grad_v = jnp.einsum("hqk,qhd->khd", weights_low, grad_attn, preferred_element_type=f32)
    grad_projected = jnp.concatenate(
        [
            rotate_back(grad_q, cos_tab, sine_tab).reshape(seq_len, own_width),
            rotate_back(grad_k, cos_tab, sine_tab).reshape(seq_len, own_width),
            grad_v.reshape(seq_len, own_width),
        ],
        axis=-1,
    ).astype(bf16)
    grad_projected, sum_expert_out, sum_shared_in = after(
        grad_projected, sum_expert_out, sum_shared_in
    )
    one_sums = dot_t(grad_projected, qkv_weight)
    grad_gain_one = jnp.sum(one_sums * scaled_rows.astype(f32), axis=0)
    one_parts = one_sums.astype(bf16)
    one_kept, grad_projected = after(one_parts, grad_projected)
    one_kept, out_parts = after(one_kept, out_parts)
    output = own_residual + ring_scatter(out_parts, ctx_size, ctx_index)
    output = output.astype(bf16).reshape(tokens.shape)
    grad_qkv_weight = t_dot(normed_low, grad_projected)
    grad_bias = jnp.sum(grad_projected.astype(f32), axis=0).reshape(3, 1, own_width)
    grad_bias = jnp.where(
        jnp.arange(ctx_size, dtype=i32)[None, :, None] == ctx_index, grad_bias, 0.0
    )

    grad_out_weight = t_dot(attn_own, mixed_all)
    small_grads = [grad_gain_one, grad_gain_two, grad_gate_vector, grad_router, grad_bias]
    small_grads = jnp.concatenate(
        [piece.reshape(device_count, -1) for piece in small_grads], axis=1
    )
    more = -(-small_size // (3 * own_width * 16)) * 16
    small_grads = jnp.pad(small_grads, ((0, 0), (0, more * 3 * own_width - small_size)))
    pieces = jnp.concatenate(
        [
            grad_qkv_weight.astype(bf16).reshape(ctx_size, fsdp_size, shard, 3 * own_width),
            small_grads.astype(bf16).reshape(ctx_size, fsdp_size, more, 3 * own_width),
        ],
        axis=2,
    )
    pieces = pieces.transpose(1, 0, 2, 3).reshape(-1, 3 * own_width)
    pieces = lax.psum_scatter(pieces, "fsdp", scatter_dimension=0, tiled=True)
    pieces, grad_shared_out = after(pieces, grad_shared_out)
    sum_shared_out = sum_rows(grad_shared_out)
    pieces = pieces.reshape(ctx_size, shard + more, 3 * own_width)
    pieces = lax.all_to_all(pieces, "ctx", split_axis=0, concat_axis=0, tiled=True)
    one_kept, pieces = after(one_kept, pieces)
    grad_normed = ring_scatter(one_parts, ctx_size, ctx_index, one_kept)
    grad_inputs_norm, unused = rms_back(
        own_tokens,
        inv_one,
        attn_gain,
        grad_normed,
    )
    grad_tokens = (grad_resid + grad_inputs_norm).reshape(tokens.shape)
    small_grads = jnp.sum(pieces[:, shard:].reshape(ctx_size, -1).astype(f32), axis=0)
    return (
        output,
        grad_tokens,
        merge_columns(pieces[:, :shard], 3, ctx_size),
        small_grads[router_end:small_size],
        sum_rows(grad_out_weight).astype(f32),
        small_grads[:shard],
        small_grads[shard : 2 * shard],
        small_grads[3 * shard : router_end].reshape(shard, expert_count),
        small_grads[2 * shard : 3 * shard],
        merge_columns(sum_shared_in, 2, ctx_size),
        sum_shared_out.astype(f32),
        sum_expert_in.astype(f32)[None],
        sum_expert_out.astype(f32)[None],
    )


def local_wide(
    tokens,
    segments,
    routes,
    cotangent,
    w_qkv,
    b_qkv,
    w_out,
    gain_attn,
    gain_ffn,
    w_router,
    w_shared_gate,
    w_shared_in,
    w_shared_out,
    w_expert_in,
    w_expert_out,
):
    block_len = tokens.shape[2]
    model_width = tokens.shape[3]
    token_count = 2 * block_len
    top_count = routes.shape[3]
    half_len = segments.shape[2]
    seq_len = 2 * half_len
    ctx_index = lax.axis_index("ctx")
    head_count = model_width // HD
    expert_count = w_router.shape[1]
    capacity = token_count * top_count // expert_count
    slot_count = expert_count * capacity
    key_rows = min(512, seq_len)
    key_blocks = seq_len // key_rows
    score_scale = HD ** (-0.5)
    head_shape = (token_count, head_count, HD)
    attn_set = (
        lax.all_gather(w_qkv, ("ctx", "fsdp"), axis=0, tiled=True),
        lax.all_gather(b_qkv, ("ctx", "fsdp"), axis=0, tiled=True),
        lax.all_gather(w_out, ("ctx", "fsdp"), axis=0, tiled=True),
        lax.all_gather(gain_attn, ("ctx", "fsdp"), axis=0, tiled=True),
    )
    qkv_weight, qkv_bias, out_weight, attn_gain = attn_set
    inputs = tokens.reshape(token_count, model_width).astype(jnp.float32)
    normed, inv_one = rms_norm(inputs, attn_gain.astype(jnp.float32))
    normed_low = normed.astype(jnp.bfloat16)
    projected = jnp.dot(
        normed_low, qkv_weight, preferred_element_type=jnp.float32
    ) + qkv_bias.astype(jnp.float32)
    local_index = jnp.arange(block_len, dtype=jnp.int32)
    query_pos = jnp.concatenate(
        [ctx_index * block_len + local_index, seq_len - (ctx_index + 1) * block_len + local_index]
    )
    half_index = jnp.arange(half_len, dtype=jnp.int32)
    key_pos = jnp.concatenate(
        [half_index, seq_len - block_len * (half_index // block_len + 1) + half_index % block_len]
    ).reshape(key_blocks, key_rows)
    key_seg = segments.reshape(key_blocks, key_rows)
    query_seg = lax.dynamic_slice_in_dim(segments[0], ctx_index * block_len, block_len, 1).reshape(
        token_count
    )
    cos_tab, sine_tab = rope_tables(query_pos, HD)
    queries = rotate(projected[:, :model_width].reshape(head_shape), cos_tab, sine_tab).astype(
        jnp.bfloat16
    )
    keys_own = rotate(
        projected[:, model_width : 2 * model_width].reshape(head_shape), cos_tab, sine_tab
    ).astype(jnp.bfloat16)
    values_own = projected[:, 2 * model_width :].astype(jnp.bfloat16)
    keys_all, values_all = (
        lax.all_gather(keys_own.reshape(2, block_len, model_width), "ctx", axis=1, tiled=True),
        lax.all_gather(values_own.reshape(2, block_len, model_width), "ctx", axis=1, tiled=True),
    )
    keys_all = keys_all.reshape(key_blocks, key_rows, head_count, HD)
    values_all = values_all.reshape(key_blocks, key_rows, head_count, HD)

    def score_block(key_blk, pos_blk, seg_blk):
        raw_scores = (
            jnp.einsum("qhd,khd->hqk", queries, key_blk, preferred_element_type=jnp.float32)
            * score_scale
        )
        allowed = (pos_blk[None, :] <= query_pos[:, None]) & (
            seg_blk[None, :] == query_seg[:, None]
        )
        return (jnp.where(allowed[None], raw_scores, MASK_FILL), allowed)

    def total_step(running, key_part):
        run_max, run_sum = running
        scores = score_block(key_part[0], key_part[1], key_part[2])[0]
        new_max = jnp.maximum(run_max, jnp.max(scores, axis=-1))
        run_sum = run_sum * jnp.exp(run_max - new_max) + jnp.sum(
            jnp.exp(scores - new_max[..., None]), axis=-1
        )
        return ((new_max, run_sum), None)

    start_max = jnp.full((head_count, token_count), MASK_FILL, jnp.float32)
    start_sum = jnp.zeros((head_count, token_count), jnp.float32)
    (run_max, run_sum), unused = lax.scan(
        total_step, (start_max, start_sum), (keys_all, key_pos, key_seg)
    )
    log_total = run_max + jnp.log(run_sum)

    def attend_step(summed, key_part):
        key_blk, value_blk, pos_blk, seg_blk = key_part
        scores = score_block(key_blk, pos_blk, seg_blk)[0]
        weights = jnp.exp(scores - log_total[..., None]).astype(jnp.bfloat16)
        return (
            summed
            + jnp.einsum("hqk,khd->qhd", weights, value_blk, preferred_element_type=jnp.float32),
            None,
        )

    key_stack = (keys_all, values_all, key_pos, key_seg)
    attended, unused = lax.scan(attend_step, jnp.zeros(head_shape, jnp.float32), key_stack)
    attn_low = attended.reshape(token_count, model_width).astype(jnp.bfloat16)
    residual = inputs + jnp.dot(attn_low, out_weight, preferred_element_type=jnp.float32)
    ffn_set = (
        lax.all_gather(gain_ffn, ("ctx", "fsdp"), axis=0, tiled=True),
        lax.all_gather(w_router, ("ctx", "fsdp"), axis=0, tiled=True),
        lax.all_gather(w_shared_gate, ("ctx", "fsdp"), axis=0, tiled=True),
        lax.all_gather(w_shared_in, ("ctx", "fsdp"), axis=0, tiled=True),
        lax.all_gather(w_shared_out, ("ctx", "fsdp"), axis=0, tiled=True),
    )
    ffn_gain, router_weight, gate_vector, shared_in, shared_out = ffn_set
    normed_two, inv_two = rms_norm(residual, ffn_gain.astype(jnp.float32))
    low_two = normed_two.astype(jnp.bfloat16)
    logits = jnp.dot(low_two, router_weight, preferred_element_type=jnp.float32)
    router_probs = jax.nn.softmax(logits, axis=-1)
    chosen = routes.reshape(token_count, top_count)
    chosen_mask = chosen[..., None] == jnp.arange(expert_count, dtype=jnp.int32)
    gate_vals = jnp.sum(jnp.where(chosen_mask, router_probs[:, None, :], 0.0), axis=-1)
    shared_scale = jax.nn.sigmoid(jnp.dot(low_two, gate_vector, preferred_element_type=jnp.float32))
    shared_pre = jnp.dot(low_two, shared_in, preferred_element_type=jnp.float32)
    shared_hid = swiglu(shared_pre, FS).astype(jnp.bfloat16)
    shared_res = jnp.dot(shared_hid, shared_out, preferred_element_type=jnp.float32)
    pair_routes = chosen.reshape(token_count * top_count)
    expert_marks = (
        pair_routes[:, None] == jnp.arange(expert_count, dtype=jnp.int32)[None, :]
    ).astype(jnp.int32)
    pair_ranks = jnp.sum((jnp.cumsum(expert_marks, axis=0) - expert_marks) * expert_marks, axis=1)
    pair_target = jnp.where(pair_ranks < capacity, pair_routes * capacity + pair_ranks, -1)
    pair_map = pair_target[:, None] == jnp.arange(slot_count, dtype=jnp.int32)[None, :]
    pair_low = pair_map.astype(jnp.bfloat16)
    token_map = jnp.sum(
        pair_map.reshape(token_count, top_count, slot_count).astype(jnp.int32), axis=1
    ).astype(jnp.bfloat16)
    outgoing = jnp.einsum(
        "tc,td->cd", token_map, low_two, preferred_element_type=jnp.float32
    ).astype(jnp.bfloat16)
    incoming = lax.all_to_all(
        outgoing.reshape(expert_count, capacity, model_width),
        "ctx",
        split_axis=0,
        concat_axis=1,
        tiled=True,
    )
    expert_in, expert_out = (
        lax.all_gather(w_expert_in, "fsdp", axis=1, tiled=True),
        lax.all_gather(w_expert_out, "fsdp", axis=1, tiled=True),
    )
    expert_pre = jnp.einsum("erd,edf->erf", incoming, expert_in, preferred_element_type=jnp.float32)
    expert_hid = swiglu(expert_pre, FE).astype(jnp.bfloat16)
    expert_res = jnp.einsum(
        "erf,efd->erd", expert_hid, expert_out, preferred_element_type=jnp.float32
    ).astype(jnp.bfloat16)
    returned = lax.all_to_all(expert_res, "ctx", split_axis=1, concat_axis=0, tiled=True).reshape(
        slot_count, model_width
    )
    pair_vals = jnp.dot(pair_low, returned, preferred_element_type=jnp.float32).reshape(
        token_count, top_count, model_width
    )
    routed = jnp.sum(gate_vals[..., None] * pair_vals, axis=1)
    output = (
        (residual + shared_scale[:, None] * shared_res + routed)
        .astype(jnp.bfloat16)
        .reshape(tokens.shape)
    )
    grad_out = cotangent.reshape(token_count, model_width).astype(jnp.float32)
    pair_grads = gate_vals[..., None] * grad_out[:, None, :]
    grad_gates = jnp.sum(grad_out[:, None, :] * pair_vals, axis=-1)
    grad_returned = jnp.einsum(
        "pc,pd->cd",
        pair_map.astype(jnp.float32),
        pair_grads.reshape(token_count * top_count, model_width),
        precision=HIGHEST,
    ).astype(jnp.bfloat16)
    grad_res = lax.all_to_all(
        grad_returned.reshape(expert_count, capacity, model_width),
        "ctx",
        split_axis=0,
        concat_axis=1,
        tiled=True,
    )
    grad_expert_out = jnp.einsum(
        "erf,erd->efd", expert_hid, grad_res, preferred_element_type=jnp.float32
    )
    grad_hid = jnp.einsum("erd,efd->erf", grad_res, expert_out, preferred_element_type=jnp.float32)
    grad_pre = swiglu_back(expert_pre, FE, grad_hid).astype(jnp.bfloat16)
    grad_expert_in = jnp.einsum(
        "erd,erf->edf", incoming, grad_pre, preferred_element_type=jnp.float32
    )
    grad_incoming = jnp.einsum(
        "erf,edf->erd", grad_pre, expert_in, preferred_element_type=jnp.float32
    ).astype(jnp.bfloat16)
    grad_outgoing = lax.all_to_all(
        grad_incoming, "ctx", split_axis=1, concat_axis=0, tiled=True
    ).reshape(slot_count, model_width)
    expert_grads = (
        lax.psum_scatter(
            grad_expert_in.astype(jnp.bfloat16), "fsdp", scatter_dimension=1, tiled=True
        ).astype(jnp.float32),
        lax.psum_scatter(
            grad_expert_out.astype(jnp.bfloat16), "fsdp", scatter_dimension=1, tiled=True
        ).astype(jnp.float32),
    )
    grad_two = jnp.einsum("tc,cd->td", token_map, grad_outgoing, preferred_element_type=jnp.float32)
    grad_probs = jnp.sum(jnp.where(chosen_mask, grad_gates[..., None], 0.0), axis=1)
    grad_logits = (
        router_probs * (grad_probs - jnp.sum(router_probs * grad_probs, axis=-1, keepdims=True))
    ).astype(jnp.bfloat16)
    grad_router = jnp.einsum("td,te->de", low_two, grad_logits, preferred_element_type=jnp.float32)
    grad_shared_res = (shared_scale[:, None] * grad_out).astype(jnp.bfloat16)
    grad_gate_pre = (
        jnp.sum(grad_out * shared_res, axis=-1) * shared_scale * (1.0 - shared_scale)
    ).astype(jnp.bfloat16)
    grad_shared_out = jnp.einsum(
        "tf,td->fd", shared_hid, grad_shared_res, preferred_element_type=jnp.float32
    )
    grad_shared_hid = jnp.einsum(
        "td,fd->tf", grad_shared_res, shared_out, preferred_element_type=jnp.float32
    )
    grad_shared_pre = swiglu_back(shared_pre, FS, grad_shared_hid).astype(jnp.bfloat16)
    grad_shared_in = jnp.einsum(
        "td,tf->df", low_two, grad_shared_pre, preferred_element_type=jnp.float32
    )
    grad_gate_vector = jnp.einsum(
        "td,t->d", low_two, grad_gate_pre, preferred_element_type=jnp.float32
    )
    grad_two = grad_two + jnp.einsum(
        "te,de->td", grad_logits, router_weight, preferred_element_type=jnp.float32
    )
    grad_two = grad_two + jnp.einsum(
        "tf,df->td", grad_shared_pre, shared_in, preferred_element_type=jnp.float32
    )
    grad_two = (
        grad_two
        + grad_gate_pre.astype(jnp.float32)[:, None] * gate_vector.astype(jnp.float32)[None, :]
    )
    grad_resid_norm, grad_gain_two = rms_back(
        residual, inv_two, ffn_gain.astype(jnp.float32), grad_two
    )
    grad_resid = grad_out + grad_resid_norm
    ffn_grads = (
        lax.psum_scatter(grad_gain_two, ("ctx", "fsdp"), scatter_dimension=0, tiled=True),
        lax.psum_scatter(grad_router, ("ctx", "fsdp"), scatter_dimension=0, tiled=True),
        lax.psum_scatter(grad_gate_vector, ("ctx", "fsdp"), scatter_dimension=0, tiled=True),
        lax.psum_scatter(grad_shared_in, ("ctx", "fsdp"), scatter_dimension=0, tiled=True),
        lax.psum_scatter(grad_shared_out, ("ctx", "fsdp"), scatter_dimension=0, tiled=True),
    )
    grad_mixed = grad_resid.astype(jnp.bfloat16)
    grad_out_weight = jnp.einsum(
        "tc,td->cd", attn_low, grad_mixed, preferred_element_type=jnp.float32
    )
    grad_attn = (
        jnp.einsum("td,cd->tc", grad_mixed, out_weight, preferred_element_type=jnp.float32)
        .astype(jnp.bfloat16)
        .reshape(head_shape)
    )

    def delta_step(summed, key_part):
        key_blk, value_blk, pos_blk, seg_blk = key_part
        weights = jnp.exp(score_block(key_blk, pos_blk, seg_blk)[0] - log_total[..., None])
        grad_weights = jnp.einsum(
            "qhd,khd->hqk", grad_attn, value_blk, preferred_element_type=jnp.float32
        )
        return (summed + jnp.sum(weights * grad_weights, axis=-1), None)

    delta_sum, unused = lax.scan(
        delta_step, jnp.zeros((head_count, token_count), jnp.float32), key_stack
    )

    def grad_step(summed, key_part):
        key_blk, value_blk, pos_blk, seg_blk = key_part
        scores, allowed = score_block(key_blk, pos_blk, seg_blk)
        weights = jnp.exp(scores - log_total[..., None])
        grad_weights = jnp.einsum(
            "qhd,khd->hqk", grad_attn, value_blk, preferred_element_type=jnp.float32
        )
        grad_scores = jnp.where(
            allowed[None], weights * (grad_weights - delta_sum[..., None]), 0.0
        ).astype(jnp.bfloat16)
        summed = (
            summed
            + jnp.einsum("hqk,khd->qhd", grad_scores, key_blk, preferred_element_type=jnp.float32)
            * score_scale
        )
        grad_key = (
            jnp.einsum("hqk,qhd->khd", grad_scores, queries, preferred_element_type=jnp.float32)
            * score_scale
        )
        grad_value = jnp.einsum(
            "hqk,qhd->khd",
            weights.astype(jnp.bfloat16),
            grad_attn,
            preferred_element_type=jnp.float32,
        )
        return (summed, (grad_key, grad_value))

    grad_query, (grad_keys, grad_values) = lax.scan(
        grad_step, jnp.zeros(head_shape, jnp.float32), key_stack
    )
    grad_keys_own, grad_values_own = (
        lax.psum_scatter(
            grad_keys.reshape(2, half_len, model_width).astype(jnp.bfloat16),
            "ctx",
            scatter_dimension=1,
            tiled=True,
        ).astype(jnp.float32),
        lax.psum_scatter(
            grad_values.reshape(2, half_len, model_width).astype(jnp.bfloat16),
            "ctx",
            scatter_dimension=1,
            tiled=True,
        ).astype(jnp.float32),
    )
    grad_q_rows = rotate_back(grad_query, cos_tab, sine_tab).reshape(token_count, model_width)
    grad_k_rows = rotate_back(grad_keys_own.reshape(head_shape), cos_tab, sine_tab).reshape(
        token_count, model_width
    )
    grad_projected = jnp.concatenate(
        [grad_q_rows, grad_k_rows, grad_values_own.reshape(token_count, model_width)], axis=-1
    ).astype(jnp.bfloat16)
    grad_qkv_weight = jnp.einsum(
        "td,te->de", normed_low, grad_projected, preferred_element_type=jnp.float32
    )
    grad_qkv_bias = jnp.sum(grad_projected.astype(jnp.float32), axis=0)
    grad_normed = jnp.einsum(
        "te,de->td", grad_projected, qkv_weight, preferred_element_type=jnp.float32
    )
    grad_inputs_norm, grad_gain_one = rms_back(
        inputs, inv_one, attn_gain.astype(jnp.float32), grad_normed
    )
    grad_tokens = (grad_resid + grad_inputs_norm).reshape(tokens.shape)
    attn_grads = (
        lax.psum_scatter(grad_qkv_weight, ("ctx", "fsdp"), scatter_dimension=0, tiled=True),
        lax.psum_scatter(grad_qkv_bias, ("ctx", "fsdp"), scatter_dimension=0, tiled=True),
        lax.psum_scatter(grad_out_weight, ("ctx", "fsdp"), scatter_dimension=0, tiled=True),
        lax.psum_scatter(grad_gain_one, ("ctx", "fsdp"), scatter_dimension=0, tiled=True),
    )
    return (
        output,
        grad_tokens,
        attn_grads[0],
        attn_grads[1],
        attn_grads[2],
        attn_grads[3],
        ffn_grads[0],
        ffn_grads[1],
        ffn_grads[2],
        ffn_grads[3],
        ffn_grads[4],
        expert_grads[0],
        expert_grads[1],
    )


def solution(mesh):
    in_specs = (
        P("fsdp", None, "ctx", None),
        P("fsdp", None, None),
        P("fsdp", None, "ctx", None),
        P("fsdp", None, "ctx", None),
        P(("ctx", "fsdp"), None),
        P(("ctx", "fsdp")),
        P(("ctx", "fsdp"), None),
        P(("ctx", "fsdp")),
        P(("ctx", "fsdp")),
        P(("ctx", "fsdp"), None),
        P(("ctx", "fsdp")),
        P(("ctx", "fsdp"), None),
        P(("ctx", "fsdp"), None),
        P("ctx", "fsdp", None),
        P("ctx", "fsdp", None),
    )
    out_specs = (
        P("fsdp", None, "ctx", None),
        P("fsdp", None, "ctx", None),
        P(("ctx", "fsdp"), None),
        P(("ctx", "fsdp")),
        P(("ctx", "fsdp"), None),
        P(("ctx", "fsdp")),
        P(("ctx", "fsdp")),
        P(("ctx", "fsdp"), None),
        P(("ctx", "fsdp")),
        P(("ctx", "fsdp"), None),
        P(("ctx", "fsdp"), None),
        P("ctx", "fsdp", None),
        P("ctx", "fsdp", None),
    )
    ctx_size = mesh.shape["ctx"]
    fsdp_size = mesh.shape["fsdp"]

    def local(*arrays):
        if HEADS % ctx_size:
            return local_wide(*arrays)
        return local_split(ctx_size, fsdp_size, *arrays)

    return jax.shard_map(local, mesh=mesh, in_specs=in_specs, out_specs=out_specs, check_vma=False)
```

```python
import jax
import jax.numpy as jnp
from jax import lax
from jax.sharding import PartitionSpec as P

HD = 128
HEADS = 16
FS = 5632
FE = 1408


RMS_EPS = 1e-06
ROPE_THETA = 1000000.0
MASK_FILL = -1e30
HIGHEST = lax.Precision.HIGHEST


def rope_tables(positions, head_dim):
    half_dim = head_dim // 2
    inv_freq = ROPE_THETA ** (-(jnp.arange(half_dim, dtype=jnp.float32) * 2.0 / head_dim))
    angles = positions.astype(jnp.float32)[:, None] * inv_freq[None, :]
    cos_tab = jnp.concatenate([jnp.cos(angles), jnp.cos(angles)], axis=-1)
    sine_tab = jnp.concatenate([jnp.sin(angles), jnp.sin(angles)], axis=-1)
    return (cos_tab, sine_tab)


def rotate(values, cos_tab, sine_tab):
    half_dim = values.shape[-1] // 2
    turned = jnp.concatenate([-values[..., half_dim:], values[..., :half_dim]], axis=-1)
    return values * cos_tab[:, None, :] + turned * sine_tab[:, None, :]


def rotate_back(upstream, cos_tab, sine_tab):
    half_dim = upstream.shape[-1] // 2
    scaled = upstream * sine_tab[:, None, :]
    return upstream * cos_tab[:, None, :] + jnp.concatenate(
        [scaled[..., half_dim:], -scaled[..., :half_dim]], axis=-1
    )


def rms_norm(values, gain_vec):
    inv_rms = lax.rsqrt(jnp.mean(values * values, axis=-1, keepdims=True) + RMS_EPS)
    return (values * inv_rms * gain_vec, inv_rms)


def rms_back(values, inv_rms, gain_vec, upstream):
    weighted = upstream * gain_vec
    inner_mean = jnp.mean(weighted * values, axis=-1, keepdims=True)
    return (
        inv_rms * weighted - values * inv_rms * inv_rms * inv_rms * inner_mean,
        jnp.sum(upstream * values * inv_rms, axis=0),
    )


def swiglu(pre_act, split_at):
    return jax.nn.silu(pre_act[..., :split_at]) * pre_act[..., split_at:]


def swiglu_back(pre_act, split_at, upstream):
    gate_part = pre_act[..., :split_at]
    up_part = pre_act[..., split_at:]
    sigmoid_g = jax.nn.sigmoid(gate_part)
    d_gate = upstream * up_part * sigmoid_g * (1.0 + gate_part * (1.0 - sigmoid_g))
    d_up = upstream * gate_part * sigmoid_g
    return jnp.concatenate([d_gate, d_up], axis=-1)


def ring_order(size):
    return list(range(0, size, 2)) + list(range(size - 1, 0, -2))


def ring_steps(size):
    order = ring_order(size)
    ahead = [(order[i], order[(i + 1) % size]) for i in range(size)]
    back = [(dst, src) for src, dst in ahead]
    return (ahead, back)


def ring_peers(size, ctx_index):
    order = ring_order(size)
    place = {dev: i for i, dev in enumerate(order)}
    table = jnp.array(
        [[order[(place[dev] + k) % size] for k in range(size)] for dev in range(size)], jnp.int32
    )
    row = lax.dynamic_index_in_dim(table, ctx_index, 0, keepdims=False)
    return [row[k] for k in range(size)]


def after(value, *deps):
    return lax.optimization_barrier((value,) + deps)


def ring_gather(block, size, ctx_index, rider=None):
    rows, width = block.shape

    def put(out, piece, peer, offset):
        return lax.dynamic_update_slice(out, piece, (peer * rows + offset, jnp.zeros_like(peer)))

    out = jnp.zeros((size * rows, width), block.dtype)
    ahead, back = ring_steps(size)
    peers = ring_peers(size, ctx_index)
    half = size // 2
    out = put(out, block, ctx_index, 0)
    fore = rear = block
    for k in range(1, half):
        fore = lax.ppermute(fore, "ctx", ahead)
        rear = lax.ppermute(rear, "ctx", back)
        if rider is not None and k == 2:
            fore, rider = after(fore, rider)
        out = put(out, fore, peers[size - k], 0)
        out = put(out, rear, peers[k], 0)
    fore = lax.ppermute(fore[: rows // 2], "ctx", ahead)
    rear = lax.ppermute(rear[rows // 2 :], "ctx", back)
    out = put(out, fore, peers[half], 0)
    out = put(out, rear, peers[half], rows // 2)
    return out if rider is None else (out, rider)


def ring_sums(parts, size, ctx_index):
    f32 = jnp.float32
    rows = parts.shape[0] // size
    ahead, back = ring_steps(size)
    peers = ring_peers(size, ctx_index)
    half = size // 2

    def own(k, start, count):
        first = (peers[k % size] * rows + start, jnp.zeros_like(peers[0]))
        return lax.dynamic_slice(parts, first, (count, parts.shape[1])).astype(f32)

    def low(values):
        return values.astype(jnp.bfloat16)

    cut = rows // 2
    fore = lax.ppermute(low(own(half, 0, cut)), "ctx", ahead)
    rear = lax.ppermute(low(own(half, cut, cut)), "ctx", back)
    fore = jnp.concatenate(
        [low(fore.astype(f32) + own(half - 1, 0, cut)), low(own(half - 1, cut, cut))], axis=0
    )
    rear = jnp.concatenate(
        [low(own(1 - half, 0, cut)), low(rear.astype(f32) + own(1 - half, cut, cut))], axis=0
    )
    for k in range(half - 1, 0, -1):
        fore = lax.ppermute(fore, "ctx", ahead)
        rear = lax.ppermute(rear, "ctx", back)
        if k > 1:
            fore = low(fore.astype(f32) + own(k - 1, 0, rows))
            rear = low(rear.astype(f32) + own(1 - k, 0, rows))
    return (fore, rear)


def ring_scatter(parts, size, ctx_index, kept=None):
    fore, rear = ring_sums(parts, size, ctx_index)
    kept = (parts if kept is None else kept).reshape(size, -1, parts.shape[1])
    kept = lax.dynamic_index_in_dim(kept, ctx_index, 0, keepdims=False)
    return kept.astype(jnp.float32) + fore.astype(jnp.float32) + rear.astype(jnp.float32)


def other_core(size):
    return [(i, i ^ 1) for i in range(size)]


def other_chip(size):
    return [(i, i ^ 2) for i in range(size)]


def fsdp_gather(shard, size, hold):
    index = lax.axis_index("fsdp")
    rows, width = shard.shape
    far = lax.ppermute(shard, "fsdp", other_chip(size))
    far, hold = after(far, hold)
    pair = jnp.where(
        index < 2, jnp.stack([shard, far], axis=0), jnp.stack([far, shard], axis=0)
    )
    near = lax.ppermute(pair, "fsdp", other_core(size))
    out = jnp.zeros((2, 2, rows, width), shard.dtype)
    out = lax.dynamic_update_index_in_dim(out, pair, index % 2, 1)
    out = lax.dynamic_update_index_in_dim(out, near, 1 - index % 2, 1)
    return (out.reshape(size * rows, width), hold)


def column_pieces(weight, groups, size, extra):
    rows = weight.shape[0]
    width = weight.shape[1] // (groups * size)
    pieces = weight.reshape(rows, groups, size, width).transpose(2, 0, 1, 3)
    pieces = pieces.reshape(size, rows, groups * width)
    if extra is not None:
        count = extra.shape[0]
        more = -(-count // (groups * width * 16)) * 16
        extra = jnp.pad(extra, (0, more * groups * width - count))
        extra = jnp.broadcast_to(
            extra.reshape(1, more, groups * width), (size, more, groups * width)
        )
        pieces = jnp.concatenate([pieces, extra], axis=1)
    return pieces


def merge_columns(pieces, groups, size):
    width = pieces.shape[2] // groups
    if width % 128 == 0:
        pieces = pieces.reshape(size, -1, groups, width).transpose(1, 2, 0, 3)
        return pieces.reshape(-1, groups * size * width).astype(jnp.float32)
    columns = [
        pieces[peer, :, group * width : (group + 1) * width]
        for group in range(groups)
        for peer in range(size)
    ]
    return jnp.concatenate(columns, axis=1).astype(jnp.float32)


def local_split(
    ctx_size,
    fsdp_size,
    tokens,
    segments,
    routes,
    cotangent,
    w_qkv,
    b_qkv,
    w_out,
    gain_attn,
    gain_ffn,
    w_router,
    w_shared_gate,
    w_shared_in,
    w_shared_out,
    w_expert_in,
    w_expert_out,
):
    bf16, f32, i32 = jnp.bfloat16, jnp.float32, jnp.int32
    device_count = ctx_size * fsdp_size
    block_len = tokens.shape[2]
    width = tokens.shape[3]
    token_count = 2 * block_len
    top_count = routes.shape[3]
    seq_len = token_count * ctx_size
    ctx_index = lax.axis_index("ctx")
    expert_count = w_router.shape[1]
    capacity = token_count * top_count // expert_count
    own_heads = HEADS // ctx_size
    own_width = own_heads * HD
    fs_own = FS // ctx_size
    score_scale = HD ** (-0.5)

    def dot(a, b):
        return jnp.dot(a, b, preferred_element_type=f32)

    def dot_t(a, b):
        return lax.dot_general(a, b, (((1,), (1,)), ((), ())), preferred_element_type=f32)

    def t_dot(a, b):
        return lax.dot_general(a, b, (((0,), (0,)), ((), ())), preferred_element_type=f32)

    def own_rows(values):
        return lax.dynamic_index_in_dim(
            values.reshape((ctx_size, token_count) + values.shape[1:]), ctx_index, 0, keepdims=False
        )

    def sum_rows(grad):
        return lax.psum_scatter(grad.astype(bf16), "fsdp", scatter_dimension=0, tiled=True)

    shard = width // device_count
    small = [gain_attn, gain_ffn, w_shared_gate, w_router.reshape(-1), b_qkv]
    small_size = sum(piece.shape[0] for piece in small)
    small = jnp.concatenate(small + [routes.astype(bf16).reshape(-1)], axis=0)
    small_count = small.shape[0]
    own_tokens = tokens.reshape(token_count, width).astype(f32)
    own_scaled, inv_one = rms_norm(own_tokens, 1.0)
    scaled_rows = ring_gather(own_scaled.astype(bf16), ctx_size, ctx_index)
    pieces = column_pieces(w_qkv, 3, ctx_size, small)
    pieces = lax.all_to_all(pieces, "ctx", split_axis=0, concat_axis=0, tiled=True)
    shared_in = column_pieces(w_shared_in, 2, ctx_size, None)
    shared_in, scaled_rows = after(shared_in, scaled_rows)
    shared_in = lax.all_to_all(shared_in, "ctx", split_axis=0, concat_axis=0, tiled=True)
    pieces = lax.all_gather(pieces, "fsdp", axis=0, tiled=False).transpose(1, 0, 2, 3)
    qkv_weight = pieces[:, :, :shard].reshape(width, 3 * own_width)
    small = pieces[:, :, shard:].reshape(device_count, -1)[:, :small_count]
    attn_gain = small[:, :shard].reshape(width).astype(f32)
    ffn_gain = small[:, shard : 2 * shard].reshape(width).astype(f32)
    gate_vector = small[:, 2 * shard : 3 * shard].reshape(width)
    router_end = 3 * shard + shard * expert_count
    router_weight = small[:, 3 * shard : router_end].reshape(width, expert_count)
    bias = small[:, router_end:small_size].reshape(3, ctx_size, own_width).astype(f32)
    bias = lax.dynamic_index_in_dim(bias, ctx_index, 1, keepdims=False).reshape(3 * own_width)
    route_rows = small[:, small_size:].astype(i32)
    route_rows = lax.dynamic_index_in_dim(
        route_rows.reshape(ctx_size, fsdp_size, -1), lax.axis_index("fsdp"), 1, keepdims=False
    ).reshape(ctx_size, token_count, top_count)

    expert_in = lax.all_gather(w_expert_in[0], "fsdp", axis=0, tiled=True)

    block_ids = jnp.arange(ctx_size, dtype=i32)[:, None]
    local_index = jnp.arange(block_len, dtype=i32)[None, :]
    positions = jnp.stack(
        [
            block_ids * block_len + local_index,
            seq_len - (block_ids + 1) * block_len + local_index,
        ],
        axis=1,
    ).reshape(seq_len)
    seg_rows = (
        segments.reshape(2, ctx_size, block_len).transpose(1, 0, 2).reshape(seq_len)
    )
    cos_tab, sine_tab = rope_tables(positions, HD)

    normed_low = (scaled_rows.astype(f32) * attn_gain).astype(bf16)
    projected = dot(normed_low, qkv_weight) + bias
    head_shape = (seq_len, own_heads, HD)
    queries = rotate(projected[:, :own_width].reshape(head_shape), cos_tab, sine_tab).astype(bf16)
    keys = rotate(
        projected[:, own_width : 2 * own_width].reshape(head_shape), cos_tab, sine_tab
    ).astype(bf16)
    values = projected[:, 2 * own_width :].reshape(head_shape).astype(bf16)
    out_weight, queries = fsdp_gather(w_out, fsdp_size, queries)
    allowed = (positions[None, :] <= positions[:, None]) & (seg_rows[None, :] == seg_rows[:, None])
    scores = jnp.einsum("qhd,khd->hqk", queries, keys, preferred_element_type=f32) * score_scale
    scores = jnp.where(allowed[None], scores, MASK_FILL)
    top_score = jnp.max(scores, axis=-1, keepdims=True)
    log_total = top_score + jnp.log(jnp.sum(jnp.exp(scores - top_score), axis=-1, keepdims=True))
    weights = jnp.exp(scores - log_total)
    weights_low = weights.astype(bf16)
    attended = jnp.einsum("hqk,khd->qhd", weights_low, values, preferred_element_type=f32)
    attn_own = attended.astype(bf16).reshape(seq_len, own_width)
    shared_out, attn_own = fsdp_gather(w_shared_out, fsdp_size, attn_own)
    expert_out, attn_own = fsdp_gather(w_expert_out[0], fsdp_size, attn_own)
    attn_parts, shared_in = after(dot(attn_own, out_weight).astype(bf16), shared_in)
    shared_in = lax.all_gather(shared_in, "fsdp", axis=0, tiled=False)
    own_residual = own_tokens + ring_scatter(attn_parts, ctx_size, ctx_index)

    normed_two, inv_two = rms_norm(own_residual, ffn_gain)
    own_low = normed_two.astype(bf16)
    low_two, grad_rows = ring_gather(
        own_low, ctx_size, ctx_index, cotangent.reshape(token_count, width)
    )
    grad_rows = lax.all_gather(grad_rows, "ctx", axis=0, tiled=True)
    mixed_weight = jnp.concatenate([router_weight, gate_vector[:, None]], axis=1)
    logits = dot(low_two, mixed_weight)
    probs_all = jax.nn.softmax(logits[:, :expert_count], axis=-1)
    scale_all = jax.nn.sigmoid(logits[:, expert_count])
    gate_all = lax.dynamic_index_in_dim(probs_all, ctx_index, 1, keepdims=False)

    named = jnp.any(route_rows == ctx_index, axis=-1)
    before = jnp.arange(token_count)[:, None] < jnp.arange(token_count)[None, :]
    rank = dot(named.astype(bf16), before.astype(bf16)).astype(i32)
    slot_of = jnp.where(named & (rank < capacity), rank, -1)
    slot_mask = slot_of[:, None, :] == jnp.arange(capacity, dtype=i32)[None, :, None]
    slot_map = slot_mask.astype(bf16)
    blocks_two = low_two.reshape(ctx_size, token_count, width)
    gate_blocks = gate_all.reshape(ctx_size, token_count)

    def to_slots(blocks):
        picked = jnp.einsum("bmt,btd->bmd", slot_map, blocks, preferred_element_type=f32)
        return picked.reshape(ctx_size * capacity, width)

    def to_tokens(slots):
        spread = jnp.einsum(
            "bmt,bmd->btd",
            slot_map,
            slots.reshape(ctx_size, capacity, width),
            preferred_element_type=f32,
        )
        return spread.reshape(seq_len, width)

    buffer = to_slots(blocks_two).astype(bf16)
    expert_pre = dot(buffer, expert_in)
    expert_hid = swiglu(expert_pre, FE).astype(bf16)
    expert_res = dot(expert_hid, expert_out).astype(bf16)
    routed = gate_all[:, None] * to_tokens(expert_res)

    shared_in, expert_res = after(shared_in, expert_res)
    shared_in = shared_in.transpose(1, 0, 2, 3).reshape(width, 2 * fs_own)
    shared_pre = dot(low_two, shared_in)
    shared_hid = swiglu(shared_pre, fs_own).astype(bf16)
    shared_res = dot(shared_hid, shared_out)
    out_parts = (scale_all[:, None] * shared_res + routed).astype(bf16)
    grad_rows, out_parts = after(grad_rows, out_parts)

    grad_slots = to_slots(grad_rows.reshape(ctx_size, token_count, width))
    gate_slots = jnp.sum(jnp.where(slot_mask, gate_blocks[:, None, :], 0.0), axis=-1).reshape(-1, 1)
    grad_res = (gate_slots * grad_slots).astype(bf16)
    grad_hid = dot_t(grad_res, expert_out)
    slot_terms = jnp.sum(expert_hid.astype(f32) * grad_hid, axis=-1)
    slot_terms = slot_terms.reshape(ctx_size, capacity, 1)
    gate_terms = jnp.sum(jnp.where(slot_mask, slot_terms, 0.0), axis=1)
    grad_pre = swiglu_back(expert_pre, FE, grad_hid).astype(bf16)
    grad_expert_in = t_dot(buffer, grad_pre)
    grad_buffer = dot_t(grad_pre, expert_in).astype(bf16)

    grad_f32 = grad_rows.astype(f32)
    grad_expert_in, grad_shared_res = after(
        grad_expert_in.astype(bf16), (scale_all[:, None] * grad_f32).astype(bf16)
    )
    sum_expert_in = sum_rows(grad_expert_in)

    grad_shared_hid = dot_t(grad_shared_res, shared_out)
    scale_terms = jnp.sum(shared_hid.astype(f32) * grad_shared_hid, axis=-1)
    grad_shared_pre = swiglu_back(shared_pre, fs_own, grad_shared_hid).astype(bf16)
    two_parts = (dot_t(grad_shared_pre, shared_in) + to_tokens(grad_buffer)).astype(bf16)
    two_parts, expert_hid, shared_hid, grad_shared_pre = after(
        two_parts, expert_hid, shared_hid, grad_shared_pre
    )
    grad_expert_out = t_dot(expert_hid, grad_res).astype(bf16)
    grad_shared_out = t_dot(shared_hid, grad_shared_res).astype(bf16)
    grad_shared_in = t_dot(low_two, grad_shared_pre).astype(bf16)
    grad_two = ring_scatter(two_parts, ctx_size, ctx_index)
    dots = jnp.stack([gate_terms, scale_terms.reshape(ctx_size, token_count)], axis=1)
    dots = lax.all_to_all(dots, "ctx", split_axis=0, concat_axis=0, tiled=True)
    grad_two, grad_shared_in, grad_shared_out, grad_expert_out, dots = after(
        grad_two, grad_shared_in, grad_shared_out, grad_expert_out, dots
    )
    sum_shared_in = grad_shared_in.reshape(ctx_size, fsdp_size, shard, 2 * fs_own)
    sum_shared_in = lax.psum_scatter(
        sum_shared_in.transpose(1, 0, 2, 3).reshape(width, 2 * fs_own),
        "fsdp",
        scatter_dimension=0,
        tiled=True,
    ).reshape(ctx_size, shard, 2 * fs_own)
    sum_expert_out = sum_rows(grad_expert_out)
    own_probs = own_rows(probs_all)
    own_scale = own_rows(scale_all)
    own_chosen = routes.reshape(token_count, top_count)
    chosen_mask = jnp.any(
        own_chosen[..., None] == jnp.arange(expert_count, dtype=i32), axis=1
    )
    prob_terms = jnp.where(chosen_mask, dots[:, 0].T, 0.0)
    grad_logits = (
        prob_terms - own_probs * jnp.sum(prob_terms, axis=-1, keepdims=True)
    ).astype(bf16)
    grad_gate_pre = (jnp.sum(dots[:, 1], axis=0) * (1.0 - own_scale)).astype(bf16)
    grad_router = t_dot(own_low, grad_logits)
    grad_gate_vector = t_dot(own_low, grad_gate_pre[:, None])
    grad_two = grad_two + dot_t(grad_logits, router_weight)
    grad_two = grad_two + grad_gate_pre.astype(f32)[:, None] * gate_vector.astype(f32)[None, :]
    grad_resid_norm, grad_gain_two = rms_back(
        own_residual, inv_two, ffn_gain, grad_two
    )
    grad_resid = cotangent.reshape(token_count, width).astype(f32) + grad_resid_norm

    grad_mixed, sum_expert_in = after(grad_resid.astype(bf16), sum_expert_in)
    mixed_all = ring_gather(grad_mixed, ctx_size, ctx_index)
    grad_attn = dot_t(mixed_all, out_weight).astype(bf16).reshape(head_shape)
    grad_attn, sum_shared_in = after(grad_attn, sum_shared_in)
    sum_shared_in = lax.all_to_all(
        sum_shared_in, "ctx", split_axis=0, concat_axis=0, tiled=True
    )
    grad_weights = jnp.einsum("qhd,khd->hqk", grad_attn, values, preferred_element_type=f32)
    delta = jnp.sum(weights * grad_weights, axis=-1, keepdims=True)
    grad_scores = jnp.where(allowed[None], weights * (grad_weights - delta), 0.0).astype(bf16)
    grad_q = jnp.einsum("hqk,khd->qhd", grad_scores, keys, preferred_element_type=f32) * score_scale
    grad_k = (
        jnp.einsum("hqk,qhd->khd", grad_scores, queries, preferred_element_type=f32) * score_scale
    )
    grad_v = jnp.einsum("hqk,qhd->khd", weights_low, grad_attn, preferred_element_type=f32)
    grad_projected = jnp.concatenate(
        [
            rotate_back(grad_q, cos_tab, sine_tab).reshape(seq_len, own_width),
            rotate_back(grad_k, cos_tab, sine_tab).reshape(seq_len, own_width),
            grad_v.reshape(seq_len, own_width),
        ],
        axis=-1,
    ).astype(bf16)
    grad_projected, sum_expert_out, sum_shared_in = after(
        grad_projected, sum_expert_out, sum_shared_in
    )
    one_sums = dot_t(grad_projected, qkv_weight)
    grad_gain_one = jnp.sum(one_sums * scaled_rows.astype(f32), axis=0)
    one_parts = one_sums.astype(bf16)
    one_kept, grad_projected = after(one_parts, grad_projected)
    one_kept, attn_own = after(one_kept, attn_own)
    grad_normed = ring_scatter(one_parts, ctx_size, ctx_index, one_kept)
    grad_qkv_weight = t_dot(normed_low, grad_projected)
    grad_bias = jnp.sum(grad_projected.astype(f32), axis=0).reshape(3, 1, own_width)
    grad_bias = jnp.where(
        jnp.arange(ctx_size, dtype=i32)[None, :, None] == ctx_index, grad_bias, 0.0
    )

    grad_out_weight = t_dot(attn_own, mixed_all)
    small_grads = [grad_gain_one, grad_gain_two, grad_gate_vector, grad_router, grad_bias]
    small_grads = jnp.concatenate(
        [piece.reshape(device_count, -1) for piece in small_grads], axis=1
    )
    more = -(-small_size // (3 * own_width * 16)) * 16
    small_grads = jnp.pad(small_grads, ((0, 0), (0, more * 3 * own_width - small_size)))
    pieces = jnp.concatenate(
        [
            grad_qkv_weight.astype(bf16).reshape(ctx_size, fsdp_size, shard, 3 * own_width),
            small_grads.astype(bf16).reshape(ctx_size, fsdp_size, more, 3 * own_width),
        ],
        axis=2,
    )
    pieces = pieces.transpose(1, 0, 2, 3).reshape(-1, 3 * own_width)
    pieces = lax.psum_scatter(pieces, "fsdp", scatter_dimension=0, tiled=True)
    grad_normed, pieces, out_parts, grad_shared_out, grad_out_weight = after(
        grad_normed, pieces, out_parts, grad_shared_out, grad_out_weight.astype(bf16)
    )
    sum_shared_out = sum_rows(grad_shared_out)
    sum_out_weight = sum_rows(grad_out_weight)
    output = own_residual + ring_scatter(out_parts, ctx_size, ctx_index)
    output = output.astype(bf16).reshape(tokens.shape)
    pieces = pieces.reshape(ctx_size, shard + more, 3 * own_width)
    pieces = lax.all_to_all(pieces, "ctx", split_axis=0, concat_axis=0, tiled=True)
    grad_inputs_norm, unused = rms_back(
        own_tokens,
        inv_one,
        attn_gain,
        grad_normed,
    )
    grad_tokens = (grad_resid + grad_inputs_norm).reshape(tokens.shape)
    small_grads = jnp.sum(pieces[:, shard:].reshape(ctx_size, -1).astype(f32), axis=0)
    return (
        output,
        grad_tokens,
        merge_columns(pieces[:, :shard], 3, ctx_size),
        small_grads[router_end:small_size],
        sum_out_weight.astype(f32),
        small_grads[:shard],
        small_grads[shard : 2 * shard],
        small_grads[3 * shard : router_end].reshape(shard, expert_count),
        small_grads[2 * shard : 3 * shard],
        merge_columns(sum_shared_in, 2, ctx_size),
        sum_shared_out.astype(f32),
        sum_expert_in.astype(f32)[None],
        sum_expert_out.astype(f32)[None],
    )


def local_wide(
    tokens,
    segments,
    routes,
    cotangent,
    w_qkv,
    b_qkv,
    w_out,
    gain_attn,
    gain_ffn,
    w_router,
    w_shared_gate,
    w_shared_in,
    w_shared_out,
    w_expert_in,
    w_expert_out,
):
    block_len = tokens.shape[2]
    model_width = tokens.shape[3]
    token_count = 2 * block_len
    top_count = routes.shape[3]
    half_len = segments.shape[2]
    seq_len = 2 * half_len
    ctx_index = lax.axis_index("ctx")
    head_count = model_width // HD
    expert_count = w_router.shape[1]
    capacity = token_count * top_count // expert_count
    slot_count = expert_count * capacity
    key_rows = min(512, seq_len)
    key_blocks = seq_len // key_rows
    score_scale = HD ** (-0.5)
    head_shape = (token_count, head_count, HD)
    attn_set = (
        lax.all_gather(w_qkv, ("ctx", "fsdp"), axis=0, tiled=True),
        lax.all_gather(b_qkv, ("ctx", "fsdp"), axis=0, tiled=True),
        lax.all_gather(w_out, ("ctx", "fsdp"), axis=0, tiled=True),
        lax.all_gather(gain_attn, ("ctx", "fsdp"), axis=0, tiled=True),
    )
    qkv_weight, qkv_bias, out_weight, attn_gain = attn_set
    inputs = tokens.reshape(token_count, model_width).astype(jnp.float32)
    normed, inv_one = rms_norm(inputs, attn_gain.astype(jnp.float32))
    normed_low = normed.astype(jnp.bfloat16)
    projected = jnp.dot(
        normed_low, qkv_weight, preferred_element_type=jnp.float32
    ) + qkv_bias.astype(jnp.float32)
    local_index = jnp.arange(block_len, dtype=jnp.int32)
    query_pos = jnp.concatenate(
        [ctx_index * block_len + local_index, seq_len - (ctx_index + 1) * block_len + local_index]
    )
    half_index = jnp.arange(half_len, dtype=jnp.int32)
    key_pos = jnp.concatenate(
        [half_index, seq_len - block_len * (half_index // block_len + 1) + half_index % block_len]
    ).reshape(key_blocks, key_rows)
    key_seg = segments.reshape(key_blocks, key_rows)
    query_seg = lax.dynamic_slice_in_dim(segments[0], ctx_index * block_len, block_len, 1).reshape(
        token_count
    )
    cos_tab, sine_tab = rope_tables(query_pos, HD)
    queries = rotate(projected[:, :model_width].reshape(head_shape), cos_tab, sine_tab).astype(
        jnp.bfloat16
    )
    keys_own = rotate(
        projected[:, model_width : 2 * model_width].reshape(head_shape), cos_tab, sine_tab
    ).astype(jnp.bfloat16)
    values_own = projected[:, 2 * model_width :].astype(jnp.bfloat16)
    keys_all, values_all = (
        lax.all_gather(keys_own.reshape(2, block_len, model_width), "ctx", axis=1, tiled=True),
        lax.all_gather(values_own.reshape(2, block_len, model_width), "ctx", axis=1, tiled=True),
    )
    keys_all = keys_all.reshape(key_blocks, key_rows, head_count, HD)
    values_all = values_all.reshape(key_blocks, key_rows, head_count, HD)

    def score_block(key_blk, pos_blk, seg_blk):
        raw_scores = (
            jnp.einsum("qhd,khd->hqk", queries, key_blk, preferred_element_type=jnp.float32)
            * score_scale
        )
        allowed = (pos_blk[None, :] <= query_pos[:, None]) & (
            seg_blk[None, :] == query_seg[:, None]
        )
        return (jnp.where(allowed[None], raw_scores, MASK_FILL), allowed)

    def total_step(running, key_part):
        run_max, run_sum = running
        scores = score_block(key_part[0], key_part[1], key_part[2])[0]
        new_max = jnp.maximum(run_max, jnp.max(scores, axis=-1))
        run_sum = run_sum * jnp.exp(run_max - new_max) + jnp.sum(
            jnp.exp(scores - new_max[..., None]), axis=-1
        )
        return ((new_max, run_sum), None)

    start_max = jnp.full((head_count, token_count), MASK_FILL, jnp.float32)
    start_sum = jnp.zeros((head_count, token_count), jnp.float32)
    (run_max, run_sum), unused = lax.scan(
        total_step, (start_max, start_sum), (keys_all, key_pos, key_seg)
    )
    log_total = run_max + jnp.log(run_sum)

    def attend_step(summed, key_part):
        key_blk, value_blk, pos_blk, seg_blk = key_part
        scores = score_block(key_blk, pos_blk, seg_blk)[0]
        weights = jnp.exp(scores - log_total[..., None]).astype(jnp.bfloat16)
        return (
            summed
            + jnp.einsum("hqk,khd->qhd", weights, value_blk, preferred_element_type=jnp.float32),
            None,
        )

    key_stack = (keys_all, values_all, key_pos, key_seg)
    attended, unused = lax.scan(attend_step, jnp.zeros(head_shape, jnp.float32), key_stack)
    attn_low = attended.reshape(token_count, model_width).astype(jnp.bfloat16)
    residual = inputs + jnp.dot(attn_low, out_weight, preferred_element_type=jnp.float32)
    ffn_set = (
        lax.all_gather(gain_ffn, ("ctx", "fsdp"), axis=0, tiled=True),
        lax.all_gather(w_router, ("ctx", "fsdp"), axis=0, tiled=True),
        lax.all_gather(w_shared_gate, ("ctx", "fsdp"), axis=0, tiled=True),
        lax.all_gather(w_shared_in, ("ctx", "fsdp"), axis=0, tiled=True),
        lax.all_gather(w_shared_out, ("ctx", "fsdp"), axis=0, tiled=True),
    )
    ffn_gain, router_weight, gate_vector, shared_in, shared_out = ffn_set
    normed_two, inv_two = rms_norm(residual, ffn_gain.astype(jnp.float32))
    low_two = normed_two.astype(jnp.bfloat16)
    logits = jnp.dot(low_two, router_weight, preferred_element_type=jnp.float32)
    router_probs = jax.nn.softmax(logits, axis=-1)
    chosen = routes.reshape(token_count, top_count)
    chosen_mask = chosen[..., None] == jnp.arange(expert_count, dtype=jnp.int32)
    gate_vals = jnp.sum(jnp.where(chosen_mask, router_probs[:, None, :], 0.0), axis=-1)
    shared_scale = jax.nn.sigmoid(jnp.dot(low_two, gate_vector, preferred_element_type=jnp.float32))
    shared_pre = jnp.dot(low_two, shared_in, preferred_element_type=jnp.float32)
    shared_hid = swiglu(shared_pre, FS).astype(jnp.bfloat16)
    shared_res = jnp.dot(shared_hid, shared_out, preferred_element_type=jnp.float32)
    pair_routes = chosen.reshape(token_count * top_count)
    expert_marks = (
        pair_routes[:, None] == jnp.arange(expert_count, dtype=jnp.int32)[None, :]
    ).astype(jnp.int32)
    pair_ranks = jnp.sum((jnp.cumsum(expert_marks, axis=0) - expert_marks) * expert_marks, axis=1)
    pair_target = jnp.where(pair_ranks < capacity, pair_routes * capacity + pair_ranks, -1)
    pair_map = pair_target[:, None] == jnp.arange(slot_count, dtype=jnp.int32)[None, :]
    pair_low = pair_map.astype(jnp.bfloat16)
    token_map = jnp.sum(
        pair_map.reshape(token_count, top_count, slot_count).astype(jnp.int32), axis=1
    ).astype(jnp.bfloat16)
    outgoing = jnp.einsum(
        "tc,td->cd", token_map, low_two, preferred_element_type=jnp.float32
    ).astype(jnp.bfloat16)
    incoming = lax.all_to_all(
        outgoing.reshape(expert_count, capacity, model_width),
        "ctx",
        split_axis=0,
        concat_axis=1,
        tiled=True,
    )
    expert_in, expert_out = (
        lax.all_gather(w_expert_in, "fsdp", axis=1, tiled=True),
        lax.all_gather(w_expert_out, "fsdp", axis=1, tiled=True),
    )
    expert_pre = jnp.einsum("erd,edf->erf", incoming, expert_in, preferred_element_type=jnp.float32)
    expert_hid = swiglu(expert_pre, FE).astype(jnp.bfloat16)
    expert_res = jnp.einsum(
        "erf,efd->erd", expert_hid, expert_out, preferred_element_type=jnp.float32
    ).astype(jnp.bfloat16)
    returned = lax.all_to_all(expert_res, "ctx", split_axis=1, concat_axis=0, tiled=True).reshape(
        slot_count, model_width
    )
    pair_vals = jnp.dot(pair_low, returned, preferred_element_type=jnp.float32).reshape(
        token_count, top_count, model_width
    )
    routed = jnp.sum(gate_vals[..., None] * pair_vals, axis=1)
    output = (
        (residual + shared_scale[:, None] * shared_res + routed)
        .astype(jnp.bfloat16)
        .reshape(tokens.shape)
    )
    grad_out = cotangent.reshape(token_count, model_width).astype(jnp.float32)
    pair_grads = gate_vals[..., None] * grad_out[:, None, :]
    grad_gates = jnp.sum(grad_out[:, None, :] * pair_vals, axis=-1)
    grad_returned = jnp.einsum(
        "pc,pd->cd",
        pair_map.astype(jnp.float32),
        pair_grads.reshape(token_count * top_count, model_width),
        precision=HIGHEST,
    ).astype(jnp.bfloat16)
    grad_res = lax.all_to_all(
        grad_returned.reshape(expert_count, capacity, model_width),
        "ctx",
        split_axis=0,
        concat_axis=1,
        tiled=True,
    )
    grad_expert_out = jnp.einsum(
        "erf,erd->efd", expert_hid, grad_res, preferred_element_type=jnp.float32
    )
    grad_hid = jnp.einsum("erd,efd->erf", grad_res, expert_out, preferred_element_type=jnp.float32)
    grad_pre = swiglu_back(expert_pre, FE, grad_hid).astype(jnp.bfloat16)
    grad_expert_in = jnp.einsum(
        "erd,erf->edf", incoming, grad_pre, preferred_element_type=jnp.float32
    )
    grad_incoming = jnp.einsum(
        "erf,edf->erd", grad_pre, expert_in, preferred_element_type=jnp.float32
    ).astype(jnp.bfloat16)
    grad_outgoing = lax.all_to_all(
        grad_incoming, "ctx", split_axis=1, concat_axis=0, tiled=True
    ).reshape(slot_count, model_width)
    expert_grads = (
        lax.psum_scatter(
            grad_expert_in.astype(jnp.bfloat16), "fsdp", scatter_dimension=1, tiled=True
        ).astype(jnp.float32),
        lax.psum_scatter(
            grad_expert_out.astype(jnp.bfloat16), "fsdp", scatter_dimension=1, tiled=True
        ).astype(jnp.float32),
    )
    grad_two = jnp.einsum("tc,cd->td", token_map, grad_outgoing, preferred_element_type=jnp.float32)
    grad_probs = jnp.sum(jnp.where(chosen_mask, grad_gates[..., None], 0.0), axis=1)
    grad_logits = (
        router_probs * (grad_probs - jnp.sum(router_probs * grad_probs, axis=-1, keepdims=True))
    ).astype(jnp.bfloat16)
    grad_router = jnp.einsum("td,te->de", low_two, grad_logits, preferred_element_type=jnp.float32)
    grad_shared_res = (shared_scale[:, None] * grad_out).astype(jnp.bfloat16)
    grad_gate_pre = (
        jnp.sum(grad_out * shared_res, axis=-1) * shared_scale * (1.0 - shared_scale)
    ).astype(jnp.bfloat16)
    grad_shared_out = jnp.einsum(
        "tf,td->fd", shared_hid, grad_shared_res, preferred_element_type=jnp.float32
    )
    grad_shared_hid = jnp.einsum(
        "td,fd->tf", grad_shared_res, shared_out, preferred_element_type=jnp.float32
    )
    grad_shared_pre = swiglu_back(shared_pre, FS, grad_shared_hid).astype(jnp.bfloat16)
    grad_shared_in = jnp.einsum(
        "td,tf->df", low_two, grad_shared_pre, preferred_element_type=jnp.float32
    )
    grad_gate_vector = jnp.einsum(
        "td,t->d", low_two, grad_gate_pre, preferred_element_type=jnp.float32
    )
    grad_two = grad_two + jnp.einsum(
        "te,de->td", grad_logits, router_weight, preferred_element_type=jnp.float32
    )
    grad_two = grad_two + jnp.einsum(
        "tf,df->td", grad_shared_pre, shared_in, preferred_element_type=jnp.float32
    )
    grad_two = (
        grad_two
        + grad_gate_pre.astype(jnp.float32)[:, None] * gate_vector.astype(jnp.float32)[None, :]
    )
    grad_resid_norm, grad_gain_two = rms_back(
        residual, inv_two, ffn_gain.astype(jnp.float32), grad_two
    )
    grad_resid = grad_out + grad_resid_norm
    ffn_grads = (
        lax.psum_scatter(grad_gain_two, ("ctx", "fsdp"), scatter_dimension=0, tiled=True),
        lax.psum_scatter(grad_router, ("ctx", "fsdp"), scatter_dimension=0, tiled=True),
        lax.psum_scatter(grad_gate_vector, ("ctx", "fsdp"), scatter_dimension=0, tiled=True),
        lax.psum_scatter(grad_shared_in, ("ctx", "fsdp"), scatter_dimension=0, tiled=True),
        lax.psum_scatter(grad_shared_out, ("ctx", "fsdp"), scatter_dimension=0, tiled=True),
    )
    grad_mixed = grad_resid.astype(jnp.bfloat16)
    grad_out_weight = jnp.einsum(
        "tc,td->cd", attn_low, grad_mixed, preferred_element_type=jnp.float32
    )
    grad_attn = (
        jnp.einsum("td,cd->tc", grad_mixed, out_weight, preferred_element_type=jnp.float32)
        .astype(jnp.bfloat16)
        .reshape(head_shape)
    )

    def delta_step(summed, key_part):
        key_blk, value_blk, pos_blk, seg_blk = key_part
        weights = jnp.exp(score_block(key_blk, pos_blk, seg_blk)[0] - log_total[..., None])
        grad_weights = jnp.einsum(
            "qhd,khd->hqk", grad_attn, value_blk, preferred_element_type=jnp.float32
        )
        return (summed + jnp.sum(weights * grad_weights, axis=-1), None)

    delta_sum, unused = lax.scan(
        delta_step, jnp.zeros((head_count, token_count), jnp.float32), key_stack
    )

    def grad_step(summed, key_part):
        key_blk, value_blk, pos_blk, seg_blk = key_part
        scores, allowed = score_block(key_blk, pos_blk, seg_blk)
        weights = jnp.exp(scores - log_total[..., None])
        grad_weights = jnp.einsum(
            "qhd,khd->hqk", grad_attn, value_blk, preferred_element_type=jnp.float32
        )
        grad_scores = jnp.where(
            allowed[None], weights * (grad_weights - delta_sum[..., None]), 0.0
        ).astype(jnp.bfloat16)
        summed = (
            summed
            + jnp.einsum("hqk,khd->qhd", grad_scores, key_blk, preferred_element_type=jnp.float32)
            * score_scale
        )
        grad_key = (
            jnp.einsum("hqk,qhd->khd", grad_scores, queries, preferred_element_type=jnp.float32)
            * score_scale
        )
        grad_value = jnp.einsum(
            "hqk,qhd->khd",
            weights.astype(jnp.bfloat16),
            grad_attn,
            preferred_element_type=jnp.float32,
        )
        return (summed, (grad_key, grad_value))

    grad_query, (grad_keys, grad_values) = lax.scan(
        grad_step, jnp.zeros(head_shape, jnp.float32), key_stack
    )
    grad_keys_own, grad_values_own = (
        lax.psum_scatter(
            grad_keys.reshape(2, half_len, model_width).astype(jnp.bfloat16),
            "ctx",
            scatter_dimension=1,
            tiled=True,
        ).astype(jnp.float32),
        lax.psum_scatter(
            grad_values.reshape(2, half_len, model_width).astype(jnp.bfloat16),
            "ctx",
            scatter_dimension=1,
            tiled=True,
        ).astype(jnp.float32),
    )
    grad_q_rows = rotate_back(grad_query, cos_tab, sine_tab).reshape(token_count, model_width)
    grad_k_rows = rotate_back(grad_keys_own.reshape(head_shape), cos_tab, sine_tab).reshape(
        token_count, model_width
    )
    grad_projected = jnp.concatenate(
        [grad_q_rows, grad_k_rows, grad_values_own.reshape(token_count, model_width)], axis=-1
    ).astype(jnp.bfloat16)
    grad_qkv_weight = jnp.einsum(
        "td,te->de", normed_low, grad_projected, preferred_element_type=jnp.float32
    )
    grad_qkv_bias = jnp.sum(grad_projected.astype(jnp.float32), axis=0)
    grad_normed = jnp.einsum(
        "te,de->td", grad_projected, qkv_weight, preferred_element_type=jnp.float32
    )
    grad_inputs_norm, grad_gain_one = rms_back(
        inputs, inv_one, attn_gain.astype(jnp.float32), grad_normed
    )
    grad_tokens = (grad_resid + grad_inputs_norm).reshape(tokens.shape)
    attn_grads = (
        lax.psum_scatter(grad_qkv_weight, ("ctx", "fsdp"), scatter_dimension=0, tiled=True),
        lax.psum_scatter(grad_qkv_bias, ("ctx", "fsdp"), scatter_dimension=0, tiled=True),
        lax.psum_scatter(grad_out_weight, ("ctx", "fsdp"), scatter_dimension=0, tiled=True),
        lax.psum_scatter(grad_gain_one, ("ctx", "fsdp"), scatter_dimension=0, tiled=True),
    )
    return (
        output,
        grad_tokens,
        attn_grads[0],
        attn_grads[1],
        attn_grads[2],
        attn_grads[3],
        ffn_grads[0],
        ffn_grads[1],
        ffn_grads[2],
        ffn_grads[3],
        ffn_grads[4],
        expert_grads[0],
        expert_grads[1],
    )


def solution(mesh):
    in_specs = (
        P("fsdp", None, "ctx", None),
        P("fsdp", None, None),
        P("fsdp", None, "ctx", None),
        P("fsdp", None, "ctx", None),
        P(("ctx", "fsdp"), None),
        P(("ctx", "fsdp")),
        P(("ctx", "fsdp"), None),
        P(("ctx", "fsdp")),
        P(("ctx", "fsdp")),
        P(("ctx", "fsdp"), None),
        P(("ctx", "fsdp")),
        P(("ctx", "fsdp"), None),
        P(("ctx", "fsdp"), None),
        P("ctx", "fsdp", None),
        P("ctx", "fsdp", None),
    )
    out_specs = (
        P("fsdp", None, "ctx", None),
        P("fsdp", None, "ctx", None),
        P(("ctx", "fsdp"), None),
        P(("ctx", "fsdp")),
        P(("ctx", "fsdp"), None),
        P(("ctx", "fsdp")),
        P(("ctx", "fsdp")),
        P(("ctx", "fsdp"), None),
        P(("ctx", "fsdp")),
        P(("ctx", "fsdp"), None),
        P(("ctx", "fsdp"), None),
        P("ctx", "fsdp", None),
        P("ctx", "fsdp", None),
    )
    ctx_size = mesh.shape["ctx"]
    fsdp_size = mesh.shape["fsdp"]

    def local(*arrays):
        if HEADS % ctx_size:
            return local_wide(*arrays)
        return local_split(ctx_size, fsdp_size, *arrays)

    return jax.shard_map(local, mesh=mesh, in_specs=in_specs, out_specs=out_specs, check_vma=False)
```

```python
import functools

import jax
import jax.numpy as jnp
from jax import lax
from jax.experimental import pallas as pl
from jax.experimental.pallas import tpu as pltpu
from jax.sharding import PartitionSpec as P

HD = 128
HEADS = 16
FS = 5632
FE = 1408


RMS_EPS = 1e-06
ROPE_THETA = 1000000.0
MASK_FILL = -1e30
HIGHEST = lax.Precision.HIGHEST


def rope_tables(positions, head_dim):
    half_dim = head_dim // 2
    inv_freq = ROPE_THETA ** (-(jnp.arange(half_dim, dtype=jnp.float32) * 2.0 / head_dim))
    angles = positions.astype(jnp.float32)[:, None] * inv_freq[None, :]
    cos_tab = jnp.concatenate([jnp.cos(angles), jnp.cos(angles)], axis=-1)
    sine_tab = jnp.concatenate([jnp.sin(angles), jnp.sin(angles)], axis=-1)
    return (cos_tab, sine_tab)


def rotate(values, cos_tab, sine_tab):
    half_dim = values.shape[-1] // 2
    turned = jnp.concatenate([-values[..., half_dim:], values[..., :half_dim]], axis=-1)
    return values * cos_tab[:, None, :] + turned * sine_tab[:, None, :]


def rotate_back(upstream, cos_tab, sine_tab):
    half_dim = upstream.shape[-1] // 2
    scaled = upstream * sine_tab[:, None, :]
    return upstream * cos_tab[:, None, :] + jnp.concatenate(
        [scaled[..., half_dim:], -scaled[..., :half_dim]], axis=-1
    )


def rms_norm(values, gain_vec):
    inv_rms = lax.rsqrt(jnp.mean(values * values, axis=-1, keepdims=True) + RMS_EPS)
    return (values * inv_rms * gain_vec, inv_rms)


def rms_back(values, inv_rms, gain_vec, upstream):
    weighted = upstream * gain_vec
    inner_mean = jnp.mean(weighted * values, axis=-1, keepdims=True)
    return (
        inv_rms * weighted - values * inv_rms * inv_rms * inv_rms * inner_mean,
        jnp.sum(upstream * values * inv_rms, axis=0),
    )


def swiglu(pre_act, split_at):
    return jax.nn.silu(pre_act[..., :split_at]) * pre_act[..., split_at:]


def swiglu_back(pre_act, split_at, upstream):
    gate_part = pre_act[..., :split_at]
    up_part = pre_act[..., split_at:]
    sigmoid_g = jax.nn.sigmoid(gate_part)
    d_gate = upstream * up_part * sigmoid_g * (1.0 + gate_part * (1.0 - sigmoid_g))
    d_up = upstream * gate_part * sigmoid_g
    return jnp.concatenate([d_gate, d_up], axis=-1)


def ring_order(size):
    return list(range(0, size, 2)) + list(range(size - 1, 0, -2))


def ring_steps(size):
    order = ring_order(size)
    ahead = [(order[i], order[(i + 1) % size]) for i in range(size)]
    back = [(dst, src) for src, dst in ahead]
    return (ahead, back)


def ring_peers(size, ctx_index):
    order = ring_order(size)
    place = {dev: i for i, dev in enumerate(order)}
    table = jnp.array(
        [[order[(place[dev] + k) % size] for k in range(size)] for dev in range(size)], jnp.int32
    )
    row = lax.dynamic_index_in_dim(table, ctx_index, 0, keepdims=False)
    return [row[k] for k in range(size)]


def after(value, *deps):
    return lax.optimization_barrier((value,) + deps)


def ring_gather(block, size, ctx_index, rider=None):
    rows, width = block.shape

    def put(out, piece, peer, offset):
        return lax.dynamic_update_slice(out, piece, (peer * rows + offset, jnp.zeros_like(peer)))

    out = jnp.zeros((size * rows, width), block.dtype)
    ahead, back = ring_steps(size)
    peers = ring_peers(size, ctx_index)
    half = size // 2
    out = put(out, block, ctx_index, 0)
    fore = rear = block
    for k in range(1, half):
        fore = lax.ppermute(fore, "ctx", ahead)
        rear = lax.ppermute(rear, "ctx", back)
        if rider is not None and k == 2:
            fore, rider = after(fore, rider)
        out = put(out, fore, peers[size - k], 0)
        out = put(out, rear, peers[k], 0)
    fore = lax.ppermute(fore[: rows // 2], "ctx", ahead)
    rear = lax.ppermute(rear[rows // 2 :], "ctx", back)
    out = put(out, fore, peers[half], 0)
    out = put(out, rear, peers[half], rows // 2)
    return out if rider is None else (out, rider)


def ring_sums(parts, size, ctx_index):
    f32 = jnp.float32
    rows = parts.shape[0] // size
    ahead, back = ring_steps(size)
    peers = ring_peers(size, ctx_index)
    half = size // 2

    def own(k, start, count):
        first = (peers[k % size] * rows + start, jnp.zeros_like(peers[0]))
        return lax.dynamic_slice(parts, first, (count, parts.shape[1])).astype(f32)

    def low(values):
        return values.astype(jnp.bfloat16)

    cut = rows // 2
    fore = lax.ppermute(low(own(half, 0, cut)), "ctx", ahead)
    rear = lax.ppermute(low(own(half, cut, cut)), "ctx", back)
    fore = jnp.concatenate(
        [low(fore.astype(f32) + own(half - 1, 0, cut)), low(own(half - 1, cut, cut))], axis=0
    )
    rear = jnp.concatenate(
        [low(own(1 - half, 0, cut)), low(rear.astype(f32) + own(1 - half, cut, cut))], axis=0
    )
    for k in range(half - 1, 0, -1):
        fore = lax.ppermute(fore, "ctx", ahead)
        rear = lax.ppermute(rear, "ctx", back)
        if k > 1:
            fore = low(fore.astype(f32) + own(k - 1, 0, rows))
            rear = low(rear.astype(f32) + own(1 - k, 0, rows))
    return (fore, rear)


def ring_scatter(parts, size, ctx_index, kept=None):
    fore, rear = ring_sums(parts, size, ctx_index)
    kept = (parts if kept is None else kept).reshape(size, -1, parts.shape[1])
    kept = lax.dynamic_index_in_dim(kept, ctx_index, 0, keepdims=False)
    return kept.astype(jnp.float32) + fore.astype(jnp.float32) + rear.astype(jnp.float32)


def other_core(size):
    return [(i, i ^ 1) for i in range(size)]


def other_chip(size):
    return [(i, i ^ 2) for i in range(size)]


def fsdp_gather(shard, size, hold):
    index = lax.axis_index("fsdp")
    rows, width = shard.shape
    far = lax.ppermute(shard, "fsdp", other_chip(size))
    far, hold = after(far, hold)
    pair = jnp.where(
        index < 2, jnp.stack([shard, far], axis=0), jnp.stack([far, shard], axis=0)
    )
    near = lax.ppermute(pair, "fsdp", other_core(size))
    out = jnp.zeros((2, 2, rows, width), shard.dtype)
    out = lax.dynamic_update_index_in_dim(out, pair, index % 2, 1)
    out = lax.dynamic_update_index_in_dim(out, near, 1 - index % 2, 1)
    return (out.reshape(size * rows, width), hold)


def column_pieces(weight, groups, size, extra):
    rows = weight.shape[0]
    width = weight.shape[1] // (groups * size)
    pieces = weight.reshape(rows, groups, size, width).transpose(2, 0, 1, 3)
    pieces = pieces.reshape(size, rows, groups * width)
    if extra is not None:
        count = extra.shape[0]
        more = -(-count // (groups * width * 16)) * 16
        extra = jnp.pad(extra, (0, more * groups * width - count))
        extra = jnp.broadcast_to(
            extra.reshape(1, more, groups * width), (size, more, groups * width)
        )
        pieces = jnp.concatenate([pieces, extra], axis=1)
    return pieces


def merge_columns(pieces, groups, size):
    width = pieces.shape[2] // groups
    if width % 128 == 0:
        pieces = pieces.reshape(size, -1, groups, width).transpose(1, 2, 0, 3)
        return pieces.reshape(-1, groups * size * width).astype(jnp.float32)
    columns = [
        pieces[peer, :, group * width : (group + 1) * width]
        for group in range(groups)
        for peer in range(size)
    ]
    return jnp.concatenate(columns, axis=1).astype(jnp.float32)


def attention_back_kernel(
    q_ref, k_ref, v_ref, do_ref, lse_ref, key_ref, query_ref, dq_ref, dk_ref, dv_ref, *, rows
):
    f32, bf16 = jnp.float32, jnp.bfloat16
    scale = HD ** (-0.5)
    keys, values = k_ref[...], v_ref[...]
    key_pos, key_seg = key_ref[:, 0:1], key_ref[:, 1:2]

    def pair(a, b, dims):
        return lax.dot_general(a, b, (dims, ((), ())), preferred_element_type=f32)

    for start in range(0, q_ref.shape[0], rows):
        here = slice(start, start + rows)
        queries, upstream = q_ref[here, :], do_ref[here, :]
        allowed = (key_pos <= query_ref[0:1, here]) & (key_seg == query_ref[1:2, here])
        scores = jnp.where(allowed, pair(keys, queries, ((1,), (1,))) * scale, MASK_FILL)
        weights = jnp.exp(scores - lse_ref[0, :, here])
        grads = pair(values, upstream, ((1,), (1,)))
        delta = jnp.sum(weights * grads, axis=0, keepdims=True)
        grads = jnp.where(allowed, weights * (grads - delta), 0.0).astype(bf16)
        part_v = pair(weights.astype(bf16), upstream, ((1,), (0,)))
        part_k = pair(grads, queries, ((1,), (0,))) * scale
        if start == 0:
            dv_ref[...] = part_v
            dk_ref[...] = part_k
        else:
            dv_ref[...] += part_v
            dk_ref[...] += part_k
        dq_ref[here, :] = pair(grads, keys, ((0,), (0,))) * scale


def attention_back(queries, keys, values, upstream, log_total, positions, seg_rows):
    tokens, width = queries.shape
    heads = width // HD
    marks = jnp.stack([positions, seg_rows], axis=0)
    by_head = pl.BlockSpec((tokens, HD), lambda h: (0, h))
    return pl.pallas_call(
        functools.partial(attention_back_kernel, rows=min(256, tokens)),
        grid=(heads,),
        in_specs=[by_head] * 4
        + [
            pl.BlockSpec((1, 1, tokens), lambda h: (h, 0, 0)),
            pl.BlockSpec((tokens, 2), lambda h: (0, 0)),
            pl.BlockSpec((2, tokens), lambda h: (0, 0)),
        ],
        out_specs=[by_head] * 3,
        out_shape=[jax.ShapeDtypeStruct((tokens, width), jnp.float32)] * 3,
        compiler_params=pltpu.CompilerParams(vmem_limit_bytes=40 * 1024 * 1024),
        cost_estimate=pl.CostEstimate(
            flops=10 * tokens * tokens * width,
            bytes_accessed=20 * tokens * width,
            transcendentals=tokens * tokens * heads,
        ),
    )(queries, keys, values, upstream, log_total.reshape(heads, 1, tokens), marks.T, marks)


def local_split(
    ctx_size,
    fsdp_size,
    tokens,
    segments,
    routes,
    cotangent,
    w_qkv,
    b_qkv,
    w_out,
    gain_attn,
    gain_ffn,
    w_router,
    w_shared_gate,
    w_shared_in,
    w_shared_out,
    w_expert_in,
    w_expert_out,
):
    bf16, f32, i32 = jnp.bfloat16, jnp.float32, jnp.int32
    device_count = ctx_size * fsdp_size
    block_len = tokens.shape[2]
    width = tokens.shape[3]
    token_count = 2 * block_len
    top_count = routes.shape[3]
    seq_len = token_count * ctx_size
    ctx_index = lax.axis_index("ctx")
    expert_count = w_router.shape[1]
    capacity = token_count * top_count // expert_count
    own_heads = HEADS // ctx_size
    own_width = own_heads * HD
    fs_own = FS // ctx_size
    score_scale = HD ** (-0.5)

    def dot(a, b):
        return jnp.dot(a, b, preferred_element_type=f32)

    def dot_t(a, b):
        return lax.dot_general(a, b, (((1,), (1,)), ((), ())), preferred_element_type=f32)

    def t_dot(a, b):
        return lax.dot_general(a, b, (((0,), (0,)), ((), ())), preferred_element_type=f32)

    def own_rows(values):
        return lax.dynamic_index_in_dim(
            values.reshape((ctx_size, token_count) + values.shape[1:]), ctx_index, 0, keepdims=False
        )

    def sum_rows(grad):
        return lax.psum_scatter(grad.astype(bf16), "fsdp", scatter_dimension=0, tiled=True)

    shard = width // device_count
    small = [gain_attn, gain_ffn, w_shared_gate, w_router.reshape(-1), b_qkv]
    small_size = sum(piece.shape[0] for piece in small)
    small = jnp.concatenate(small + [routes.astype(bf16).reshape(-1)], axis=0)
    small_count = small.shape[0]
    own_tokens = tokens.reshape(token_count, width).astype(f32)
    own_scaled, inv_one = rms_norm(own_tokens, 1.0)
    scaled_rows = ring_gather(own_scaled.astype(bf16), ctx_size, ctx_index)
    pieces = column_pieces(w_qkv, 3, ctx_size, small)
    pieces = lax.all_to_all(pieces, "ctx", split_axis=0, concat_axis=0, tiled=True)
    shared_in = column_pieces(w_shared_in, 2, ctx_size, None)
    shared_in, scaled_rows = after(shared_in, scaled_rows)
    shared_in = lax.all_to_all(shared_in, "ctx", split_axis=0, concat_axis=0, tiled=True)
    pieces = lax.all_gather(pieces, "fsdp", axis=0, tiled=False).transpose(1, 0, 2, 3)
    qkv_weight = pieces[:, :, :shard].reshape(width, 3 * own_width)
    small = pieces[:, :, shard:].reshape(device_count, -1)[:, :small_count]
    attn_gain = small[:, :shard].reshape(width).astype(f32)
    ffn_gain = small[:, shard : 2 * shard].reshape(width).astype(f32)
    gate_vector = small[:, 2 * shard : 3 * shard].reshape(width)
    router_end = 3 * shard + shard * expert_count
    router_weight = small[:, 3 * shard : router_end].reshape(width, expert_count)
    bias = small[:, router_end:small_size].reshape(3, ctx_size, own_width).astype(f32)
    bias = lax.dynamic_index_in_dim(bias, ctx_index, 1, keepdims=False).reshape(3 * own_width)
    route_rows = small[:, small_size:].astype(i32)
    route_rows = lax.dynamic_index_in_dim(
        route_rows.reshape(ctx_size, fsdp_size, -1), lax.axis_index("fsdp"), 1, keepdims=False
    ).reshape(ctx_size, token_count, top_count)

    expert_in = lax.all_gather(w_expert_in[0], "fsdp", axis=0, tiled=True)

    block_ids = jnp.arange(ctx_size, dtype=i32)[:, None]
    local_index = jnp.arange(block_len, dtype=i32)[None, :]
    positions = jnp.stack(
        [
            block_ids * block_len + local_index,
            seq_len - (block_ids + 1) * block_len + local_index,
        ],
        axis=1,
    ).reshape(seq_len)
    seg_rows = (
        segments.reshape(2, ctx_size, block_len).transpose(1, 0, 2).reshape(seq_len)
    )
    cos_tab, sine_tab = rope_tables(positions, HD)

    normed_low = (scaled_rows.astype(f32) * attn_gain).astype(bf16)
    projected = dot(normed_low, qkv_weight) + bias
    head_shape = (seq_len, own_heads, HD)
    queries = rotate(projected[:, :own_width].reshape(head_shape), cos_tab, sine_tab).astype(bf16)
    keys = rotate(
        projected[:, own_width : 2 * own_width].reshape(head_shape), cos_tab, sine_tab
    ).astype(bf16)
    values = projected[:, 2 * own_width :].reshape(head_shape).astype(bf16)
    out_weight, queries = fsdp_gather(w_out, fsdp_size, queries)
    allowed = (positions[None, :] <= positions[:, None]) & (seg_rows[None, :] == seg_rows[:, None])
    scores = jnp.einsum("qhd,khd->hqk", queries, keys, preferred_element_type=f32) * score_scale
    scores = jnp.where(allowed[None], scores, MASK_FILL)
    top_score = jnp.max(scores, axis=-1, keepdims=True)
    log_total = top_score + jnp.log(jnp.sum(jnp.exp(scores - top_score), axis=-1, keepdims=True))
    weights = jnp.exp(scores - log_total)
    weights_low = weights.astype(bf16)
    attended = jnp.einsum("hqk,khd->qhd", weights_low, values, preferred_element_type=f32)
    attn_own = attended.astype(bf16).reshape(seq_len, own_width)
    shared_out, attn_own = fsdp_gather(w_shared_out, fsdp_size, attn_own)
    expert_out, attn_own = fsdp_gather(w_expert_out[0], fsdp_size, attn_own)
    attn_parts, shared_in = after(dot(attn_own, out_weight).astype(bf16), shared_in)
    shared_in = lax.all_gather(shared_in, "fsdp", axis=0, tiled=False)
    own_residual = own_tokens + ring_scatter(attn_parts, ctx_size, ctx_index)

    normed_two, inv_two = rms_norm(own_residual, ffn_gain)
    own_low = normed_two.astype(bf16)
    low_two, grad_rows = ring_gather(
        own_low, ctx_size, ctx_index, cotangent.reshape(token_count, width)
    )
    grad_rows = lax.all_gather(grad_rows, "ctx", axis=0, tiled=True)
    mixed_weight = jnp.concatenate([router_weight, gate_vector[:, None]], axis=1)
    logits = dot(low_two, mixed_weight)
    probs_all = jax.nn.softmax(logits[:, :expert_count], axis=-1)
    scale_all = jax.nn.sigmoid(logits[:, expert_count])
    gate_all = lax.dynamic_index_in_dim(probs_all, ctx_index, 1, keepdims=False)

    named = jnp.any(route_rows == ctx_index, axis=-1)
    before = jnp.arange(token_count)[:, None] < jnp.arange(token_count)[None, :]
    rank = dot(named.astype(bf16), before.astype(bf16)).astype(i32)
    slot_of = jnp.where(named & (rank < capacity), rank, -1)
    slot_mask = slot_of[:, None, :] == jnp.arange(capacity, dtype=i32)[None, :, None]
    slot_map = slot_mask.astype(bf16)
    blocks_two = low_two.reshape(ctx_size, token_count, width)
    gate_blocks = gate_all.reshape(ctx_size, token_count)

    def to_slots(blocks):
        picked = jnp.einsum("bmt,btd->bmd", slot_map, blocks, preferred_element_type=f32)
        return picked.reshape(ctx_size * capacity, width)

    def to_tokens(slots):
        spread = jnp.einsum(
            "bmt,bmd->btd",
            slot_map,
            slots.reshape(ctx_size, capacity, width),
            preferred_element_type=f32,
        )
        return spread.reshape(seq_len, width)

    buffer = to_slots(blocks_two).astype(bf16)
    expert_pre = dot(buffer, expert_in)
    expert_hid = swiglu(expert_pre, FE).astype(bf16)
    expert_res = dot(expert_hid, expert_out).astype(bf16)
    routed = gate_all[:, None] * to_tokens(expert_res)

    shared_in, expert_res = after(shared_in, expert_res)
    shared_in = shared_in.transpose(1, 0, 2, 3).reshape(width, 2 * fs_own)
    shared_pre = dot(low_two, shared_in)
    shared_hid = swiglu(shared_pre, fs_own).astype(bf16)
    shared_res = dot(shared_hid, shared_out)
    out_parts = (scale_all[:, None] * shared_res + routed).astype(bf16)
    grad_rows, out_parts = after(grad_rows, out_parts)

    grad_slots = to_slots(grad_rows.reshape(ctx_size, token_count, width))
    gate_slots = jnp.sum(jnp.where(slot_mask, gate_blocks[:, None, :], 0.0), axis=-1).reshape(-1, 1)
    grad_res = (gate_slots * grad_slots).astype(bf16)
    grad_hid = dot_t(grad_res, expert_out)
    slot_terms = jnp.sum(expert_hid.astype(f32) * grad_hid, axis=-1)
    slot_terms = slot_terms.reshape(ctx_size, capacity, 1)
    gate_terms = jnp.sum(jnp.where(slot_mask, slot_terms, 0.0), axis=1)
    grad_pre = swiglu_back(expert_pre, FE, grad_hid).astype(bf16)
    grad_expert_in = t_dot(buffer, grad_pre)
    grad_buffer = dot_t(grad_pre, expert_in).astype(bf16)

    grad_f32 = grad_rows.astype(f32)
    grad_expert_in, grad_shared_res = after(
        grad_expert_in.astype(bf16), (scale_all[:, None] * grad_f32).astype(bf16)
    )
    sum_expert_in = sum_rows(grad_expert_in)

    grad_shared_hid = dot_t(grad_shared_res, shared_out)
    scale_terms = jnp.sum(shared_hid.astype(f32) * grad_shared_hid, axis=-1)
    grad_shared_pre = swiglu_back(shared_pre, fs_own, grad_shared_hid).astype(bf16)
    two_parts = (dot_t(grad_shared_pre, shared_in) + to_tokens(grad_buffer)).astype(bf16)
    two_parts, expert_hid, shared_hid, grad_shared_pre = after(
        two_parts, expert_hid, shared_hid, grad_shared_pre
    )
    grad_expert_out = t_dot(expert_hid, grad_res).astype(bf16)
    grad_shared_out = t_dot(shared_hid, grad_shared_res).astype(bf16)
    grad_shared_in = t_dot(low_two, grad_shared_pre).astype(bf16)
    grad_two = ring_scatter(two_parts, ctx_size, ctx_index)
    dots = jnp.stack([gate_terms, scale_terms.reshape(ctx_size, token_count)], axis=1)
    dots = lax.all_to_all(dots, "ctx", split_axis=0, concat_axis=0, tiled=True)
    grad_two, grad_shared_in, grad_shared_out, grad_expert_out, dots = after(
        grad_two, grad_shared_in, grad_shared_out, grad_expert_out, dots
    )
    sum_shared_in = grad_shared_in.reshape(ctx_size, fsdp_size, shard, 2 * fs_own)
    sum_shared_in = lax.psum_scatter(
        sum_shared_in.transpose(1, 0, 2, 3).reshape(width, 2 * fs_own),
        "fsdp",
        scatter_dimension=0,
        tiled=True,
    ).reshape(ctx_size, shard, 2 * fs_own)
    sum_expert_out = sum_rows(grad_expert_out)
    own_probs = own_rows(probs_all)
    own_scale = own_rows(scale_all)
    own_chosen = routes.reshape(token_count, top_count)
    chosen_mask = jnp.any(
        own_chosen[..., None] == jnp.arange(expert_count, dtype=i32), axis=1
    )
    prob_terms = jnp.where(chosen_mask, dots[:, 0].T, 0.0)
    grad_logits = (
        prob_terms - own_probs * jnp.sum(prob_terms, axis=-1, keepdims=True)
    ).astype(bf16)
    grad_gate_pre = (jnp.sum(dots[:, 1], axis=0) * (1.0 - own_scale)).astype(bf16)
    grad_router = t_dot(own_low, grad_logits)
    grad_gate_vector = t_dot(own_low, grad_gate_pre[:, None])
    grad_two = grad_two + dot_t(grad_logits, router_weight)
    grad_two = grad_two + grad_gate_pre.astype(f32)[:, None] * gate_vector.astype(f32)[None, :]
    grad_resid_norm, grad_gain_two = rms_back(
        own_residual, inv_two, ffn_gain, grad_two
    )
    grad_resid = cotangent.reshape(token_count, width).astype(f32) + grad_resid_norm

    grad_mixed, sum_expert_in = after(grad_resid.astype(bf16), sum_expert_in)
    mixed_all = ring_gather(grad_mixed, ctx_size, ctx_index)
    grad_attn = dot_t(mixed_all, out_weight).astype(bf16)
    grad_attn, sum_shared_in = after(grad_attn, sum_shared_in)
    sum_shared_in = lax.all_to_all(
        sum_shared_in, "ctx", split_axis=0, concat_axis=0, tiled=True
    )
    grad_q, grad_k, grad_v = attention_back(
        queries.reshape(seq_len, own_width),
        keys.reshape(seq_len, own_width),
        values.reshape(seq_len, own_width),
        grad_attn,
        log_total,
        positions,
        seg_rows,
    )
    grad_projected = jnp.concatenate(
        [
            rotate_back(grad_q.reshape(head_shape), cos_tab, sine_tab).reshape(seq_len, own_width),
            rotate_back(grad_k.reshape(head_shape), cos_tab, sine_tab).reshape(seq_len, own_width),
            grad_v,
        ],
        axis=-1,
    ).astype(bf16)
    one_sums = dot_t(grad_projected, qkv_weight)
    grad_gain_one = jnp.sum(one_sums * scaled_rows.astype(f32), axis=0)
    one_parts, sum_expert_out, sum_shared_in = after(
        one_sums.astype(bf16), sum_expert_out, sum_shared_in
    )
    one_kept, grad_projected = after(one_parts, grad_projected)
    one_kept, attn_own = after(one_kept, attn_own)
    grad_normed = ring_scatter(one_parts, ctx_size, ctx_index, one_kept)
    grad_qkv_weight = t_dot(normed_low, grad_projected)
    grad_bias = jnp.sum(grad_projected.astype(f32), axis=0).reshape(3, 1, own_width)
    grad_bias = jnp.where(
        jnp.arange(ctx_size, dtype=i32)[None, :, None] == ctx_index, grad_bias, 0.0
    )

    grad_out_weight = t_dot(attn_own, mixed_all)
    small_grads = [grad_gain_one, grad_gain_two, grad_gate_vector, grad_router, grad_bias]
    small_grads = jnp.concatenate(
        [piece.reshape(device_count, -1) for piece in small_grads], axis=1
    )
    more = -(-small_size // (3 * own_width * 16)) * 16
    small_grads = jnp.pad(small_grads, ((0, 0), (0, more * 3 * own_width - small_size)))
    pieces = jnp.concatenate(
        [
            grad_qkv_weight.astype(bf16).reshape(ctx_size, fsdp_size, shard, 3 * own_width),
            small_grads.astype(bf16).reshape(ctx_size, fsdp_size, more, 3 * own_width),
        ],
        axis=2,
    )
    pieces = pieces.transpose(1, 0, 2, 3).reshape(-1, 3 * own_width)
    pieces = lax.psum_scatter(pieces, "fsdp", scatter_dimension=0, tiled=True)
    grad_normed, pieces, out_parts, grad_shared_out, grad_out_weight = after(
        grad_normed, pieces, out_parts, grad_shared_out, grad_out_weight.astype(bf16)
    )
    sum_shared_out = sum_rows(grad_shared_out)
    sum_out_weight = sum_rows(grad_out_weight)
    output = own_residual + ring_scatter(out_parts, ctx_size, ctx_index)
    output = output.astype(bf16).reshape(tokens.shape)
    pieces = pieces.reshape(ctx_size, shard + more, 3 * own_width)
    pieces = lax.all_to_all(pieces, "ctx", split_axis=0, concat_axis=0, tiled=True)
    grad_inputs_norm, unused = rms_back(
        own_tokens,
        inv_one,
        attn_gain,
        grad_normed,
    )
    grad_tokens = (grad_resid + grad_inputs_norm).reshape(tokens.shape)
    small_grads = jnp.sum(pieces[:, shard:].reshape(ctx_size, -1).astype(f32), axis=0)
    return (
        output,
        grad_tokens,
        merge_columns(pieces[:, :shard], 3, ctx_size),
        small_grads[router_end:small_size],
        sum_out_weight.astype(f32),
        small_grads[:shard],
        small_grads[shard : 2 * shard],
        small_grads[3 * shard : router_end].reshape(shard, expert_count),
        small_grads[2 * shard : 3 * shard],
        merge_columns(sum_shared_in, 2, ctx_size),
        sum_shared_out.astype(f32),
        sum_expert_in.astype(f32)[None],
        sum_expert_out.astype(f32)[None],
    )


def local_wide(
    tokens,
    segments,
    routes,
    cotangent,
    w_qkv,
    b_qkv,
    w_out,
    gain_attn,
    gain_ffn,
    w_router,
    w_shared_gate,
    w_shared_in,
    w_shared_out,
    w_expert_in,
    w_expert_out,
):
    block_len = tokens.shape[2]
    model_width = tokens.shape[3]
    token_count = 2 * block_len
    top_count = routes.shape[3]
    half_len = segments.shape[2]
    seq_len = 2 * half_len
    ctx_index = lax.axis_index("ctx")
    head_count = model_width // HD
    expert_count = w_router.shape[1]
    capacity = token_count * top_count // expert_count
    slot_count = expert_count * capacity
    key_rows = min(512, seq_len)
    key_blocks = seq_len // key_rows
    score_scale = HD ** (-0.5)
    head_shape = (token_count, head_count, HD)
    attn_set = (
        lax.all_gather(w_qkv, ("ctx", "fsdp"), axis=0, tiled=True),
        lax.all_gather(b_qkv, ("ctx", "fsdp"), axis=0, tiled=True),
        lax.all_gather(w_out, ("ctx", "fsdp"), axis=0, tiled=True),
        lax.all_gather(gain_attn, ("ctx", "fsdp"), axis=0, tiled=True),
    )
    qkv_weight, qkv_bias, out_weight, attn_gain = attn_set
    inputs = tokens.reshape(token_count, model_width).astype(jnp.float32)
    normed, inv_one = rms_norm(inputs, attn_gain.astype(jnp.float32))
    normed_low = normed.astype(jnp.bfloat16)
    projected = jnp.dot(
        normed_low, qkv_weight, preferred_element_type=jnp.float32
    ) + qkv_bias.astype(jnp.float32)
    local_index = jnp.arange(block_len, dtype=jnp.int32)
    query_pos = jnp.concatenate(
        [ctx_index * block_len + local_index, seq_len - (ctx_index + 1) * block_len + local_index]
    )
    half_index = jnp.arange(half_len, dtype=jnp.int32)
    key_pos = jnp.concatenate(
        [half_index, seq_len - block_len * (half_index // block_len + 1) + half_index % block_len]
    ).reshape(key_blocks, key_rows)
    key_seg = segments.reshape(key_blocks, key_rows)
    query_seg = lax.dynamic_slice_in_dim(segments[0], ctx_index * block_len, block_len, 1).reshape(
        token_count
    )
    cos_tab, sine_tab = rope_tables(query_pos, HD)
    queries = rotate(projected[:, :model_width].reshape(head_shape), cos_tab, sine_tab).astype(
        jnp.bfloat16
    )
    keys_own = rotate(
        projected[:, model_width : 2 * model_width].reshape(head_shape), cos_tab, sine_tab
    ).astype(jnp.bfloat16)
    values_own = projected[:, 2 * model_width :].astype(jnp.bfloat16)
    keys_all, values_all = (
        lax.all_gather(keys_own.reshape(2, block_len, model_width), "ctx", axis=1, tiled=True),
        lax.all_gather(values_own.reshape(2, block_len, model_width), "ctx", axis=1, tiled=True),
    )
    keys_all = keys_all.reshape(key_blocks, key_rows, head_count, HD)
    values_all = values_all.reshape(key_blocks, key_rows, head_count, HD)

    def score_block(key_blk, pos_blk, seg_blk):
        raw_scores = (
            jnp.einsum("qhd,khd->hqk", queries, key_blk, preferred_element_type=jnp.float32)
            * score_scale
        )
        allowed = (pos_blk[None, :] <= query_pos[:, None]) & (
            seg_blk[None, :] == query_seg[:, None]
        )
        return (jnp.where(allowed[None], raw_scores, MASK_FILL), allowed)

    def total_step(running, key_part):
        run_max, run_sum = running
        scores = score_block(key_part[0], key_part[1], key_part[2])[0]
        new_max = jnp.maximum(run_max, jnp.max(scores, axis=-1))
        run_sum = run_sum * jnp.exp(run_max - new_max) + jnp.sum(
            jnp.exp(scores - new_max[..., None]), axis=-1
        )
        return ((new_max, run_sum), None)

    start_max = jnp.full((head_count, token_count), MASK_FILL, jnp.float32)
    start_sum = jnp.zeros((head_count, token_count), jnp.float32)
    (run_max, run_sum), unused = lax.scan(
        total_step, (start_max, start_sum), (keys_all, key_pos, key_seg)
    )
    log_total = run_max + jnp.log(run_sum)

    def attend_step(summed, key_part):
        key_blk, value_blk, pos_blk, seg_blk = key_part
        scores = score_block(key_blk, pos_blk, seg_blk)[0]
        weights = jnp.exp(scores - log_total[..., None]).astype(jnp.bfloat16)
        return (
            summed
            + jnp.einsum("hqk,khd->qhd", weights, value_blk, preferred_element_type=jnp.float32),
            None,
        )

    key_stack = (keys_all, values_all, key_pos, key_seg)
    attended, unused = lax.scan(attend_step, jnp.zeros(head_shape, jnp.float32), key_stack)
    attn_low = attended.reshape(token_count, model_width).astype(jnp.bfloat16)
    residual = inputs + jnp.dot(attn_low, out_weight, preferred_element_type=jnp.float32)
    ffn_set = (
        lax.all_gather(gain_ffn, ("ctx", "fsdp"), axis=0, tiled=True),
        lax.all_gather(w_router, ("ctx", "fsdp"), axis=0, tiled=True),
        lax.all_gather(w_shared_gate, ("ctx", "fsdp"), axis=0, tiled=True),
        lax.all_gather(w_shared_in, ("ctx", "fsdp"), axis=0, tiled=True),
        lax.all_gather(w_shared_out, ("ctx", "fsdp"), axis=0, tiled=True),
    )
    ffn_gain, router_weight, gate_vector, shared_in, shared_out = ffn_set
    normed_two, inv_two = rms_norm(residual, ffn_gain.astype(jnp.float32))
    low_two = normed_two.astype(jnp.bfloat16)
    logits = jnp.dot(low_two, router_weight, preferred_element_type=jnp.float32)
    router_probs = jax.nn.softmax(logits, axis=-1)
    chosen = routes.reshape(token_count, top_count)
    chosen_mask = chosen[..., None] == jnp.arange(expert_count, dtype=jnp.int32)
    gate_vals = jnp.sum(jnp.where(chosen_mask, router_probs[:, None, :], 0.0), axis=-1)
    shared_scale = jax.nn.sigmoid(jnp.dot(low_two, gate_vector, preferred_element_type=jnp.float32))
    shared_pre = jnp.dot(low_two, shared_in, preferred_element_type=jnp.float32)
    shared_hid = swiglu(shared_pre, FS).astype(jnp.bfloat16)
    shared_res = jnp.dot(shared_hid, shared_out, preferred_element_type=jnp.float32)
    pair_routes = chosen.reshape(token_count * top_count)
    expert_marks = (
        pair_routes[:, None] == jnp.arange(expert_count, dtype=jnp.int32)[None, :]
    ).astype(jnp.int32)
    pair_ranks = jnp.sum((jnp.cumsum(expert_marks, axis=0) - expert_marks) * expert_marks, axis=1)
    pair_target = jnp.where(pair_ranks < capacity, pair_routes * capacity + pair_ranks, -1)
    pair_map = pair_target[:, None] == jnp.arange(slot_count, dtype=jnp.int32)[None, :]
    pair_low = pair_map.astype(jnp.bfloat16)
    token_map = jnp.sum(
        pair_map.reshape(token_count, top_count, slot_count).astype(jnp.int32), axis=1
    ).astype(jnp.bfloat16)
    outgoing = jnp.einsum(
        "tc,td->cd", token_map, low_two, preferred_element_type=jnp.float32
    ).astype(jnp.bfloat16)
    incoming = lax.all_to_all(
        outgoing.reshape(expert_count, capacity, model_width),
        "ctx",
        split_axis=0,
        concat_axis=1,
        tiled=True,
    )
    expert_in, expert_out = (
        lax.all_gather(w_expert_in, "fsdp", axis=1, tiled=True),
        lax.all_gather(w_expert_out, "fsdp", axis=1, tiled=True),
    )
    expert_pre = jnp.einsum("erd,edf->erf", incoming, expert_in, preferred_element_type=jnp.float32)
    expert_hid = swiglu(expert_pre, FE).astype(jnp.bfloat16)
    expert_res = jnp.einsum(
        "erf,efd->erd", expert_hid, expert_out, preferred_element_type=jnp.float32
    ).astype(jnp.bfloat16)
    returned = lax.all_to_all(expert_res, "ctx", split_axis=1, concat_axis=0, tiled=True).reshape(
        slot_count, model_width
    )
    pair_vals = jnp.dot(pair_low, returned, preferred_element_type=jnp.float32).reshape(
        token_count, top_count, model_width
    )
    routed = jnp.sum(gate_vals[..., None] * pair_vals, axis=1)
    output = (
        (residual + shared_scale[:, None] * shared_res + routed)
        .astype(jnp.bfloat16)
        .reshape(tokens.shape)
    )
    grad_out = cotangent.reshape(token_count, model_width).astype(jnp.float32)
    pair_grads = gate_vals[..., None] * grad_out[:, None, :]
    grad_gates = jnp.sum(grad_out[:, None, :] * pair_vals, axis=-1)
    grad_returned = jnp.einsum(
        "pc,pd->cd",
        pair_map.astype(jnp.float32),
        pair_grads.reshape(token_count * top_count, model_width),
        precision=HIGHEST,
    ).astype(jnp.bfloat16)
    grad_res = lax.all_to_all(
        grad_returned.reshape(expert_count, capacity, model_width),
        "ctx",
        split_axis=0,
        concat_axis=1,
        tiled=True,
    )
    grad_expert_out = jnp.einsum(
        "erf,erd->efd", expert_hid, grad_res, preferred_element_type=jnp.float32
    )
    grad_hid = jnp.einsum("erd,efd->erf", grad_res, expert_out, preferred_element_type=jnp.float32)
    grad_pre = swiglu_back(expert_pre, FE, grad_hid).astype(jnp.bfloat16)
    grad_expert_in = jnp.einsum(
        "erd,erf->edf", incoming, grad_pre, preferred_element_type=jnp.float32
    )
    grad_incoming = jnp.einsum(
        "erf,edf->erd", grad_pre, expert_in, preferred_element_type=jnp.float32
    ).astype(jnp.bfloat16)
    grad_outgoing = lax.all_to_all(
        grad_incoming, "ctx", split_axis=1, concat_axis=0, tiled=True
    ).reshape(slot_count, model_width)
    expert_grads = (
        lax.psum_scatter(
            grad_expert_in.astype(jnp.bfloat16), "fsdp", scatter_dimension=1, tiled=True
        ).astype(jnp.float32),
        lax.psum_scatter(
            grad_expert_out.astype(jnp.bfloat16), "fsdp", scatter_dimension=1, tiled=True
        ).astype(jnp.float32),
    )
    grad_two = jnp.einsum("tc,cd->td", token_map, grad_outgoing, preferred_element_type=jnp.float32)
    grad_probs = jnp.sum(jnp.where(chosen_mask, grad_gates[..., None], 0.0), axis=1)
    grad_logits = (
        router_probs * (grad_probs - jnp.sum(router_probs * grad_probs, axis=-1, keepdims=True))
    ).astype(jnp.bfloat16)
    grad_router = jnp.einsum("td,te->de", low_two, grad_logits, preferred_element_type=jnp.float32)
    grad_shared_res = (shared_scale[:, None] * grad_out).astype(jnp.bfloat16)
    grad_gate_pre = (
        jnp.sum(grad_out * shared_res, axis=-1) * shared_scale * (1.0 - shared_scale)
    ).astype(jnp.bfloat16)
    grad_shared_out = jnp.einsum(
        "tf,td->fd", shared_hid, grad_shared_res, preferred_element_type=jnp.float32
    )
    grad_shared_hid = jnp.einsum(
        "td,fd->tf", grad_shared_res, shared_out, preferred_element_type=jnp.float32
    )
    grad_shared_pre = swiglu_back(shared_pre, FS, grad_shared_hid).astype(jnp.bfloat16)
    grad_shared_in = jnp.einsum(
        "td,tf->df", low_two, grad_shared_pre, preferred_element_type=jnp.float32
    )
    grad_gate_vector = jnp.einsum(
        "td,t->d", low_two, grad_gate_pre, preferred_element_type=jnp.float32
    )
    grad_two = grad_two + jnp.einsum(
        "te,de->td", grad_logits, router_weight, preferred_element_type=jnp.float32
    )
    grad_two = grad_two + jnp.einsum(
        "tf,df->td", grad_shared_pre, shared_in, preferred_element_type=jnp.float32
    )
    grad_two = (
        grad_two
        + grad_gate_pre.astype(jnp.float32)[:, None] * gate_vector.astype(jnp.float32)[None, :]
    )
    grad_resid_norm, grad_gain_two = rms_back(
        residual, inv_two, ffn_gain.astype(jnp.float32), grad_two
    )
    grad_resid = grad_out + grad_resid_norm
    ffn_grads = (
        lax.psum_scatter(grad_gain_two, ("ctx", "fsdp"), scatter_dimension=0, tiled=True),
        lax.psum_scatter(grad_router, ("ctx", "fsdp"), scatter_dimension=0, tiled=True),
        lax.psum_scatter(grad_gate_vector, ("ctx", "fsdp"), scatter_dimension=0, tiled=True),
        lax.psum_scatter(grad_shared_in, ("ctx", "fsdp"), scatter_dimension=0, tiled=True),
        lax.psum_scatter(grad_shared_out, ("ctx", "fsdp"), scatter_dimension=0, tiled=True),
    )
    grad_mixed = grad_resid.astype(jnp.bfloat16)
    grad_out_weight = jnp.einsum(
        "tc,td->cd", attn_low, grad_mixed, preferred_element_type=jnp.float32
    )
    grad_attn = (
        jnp.einsum("td,cd->tc", grad_mixed, out_weight, preferred_element_type=jnp.float32)
        .astype(jnp.bfloat16)
        .reshape(head_shape)
    )

    def delta_step(summed, key_part):
        key_blk, value_blk, pos_blk, seg_blk = key_part
        weights = jnp.exp(score_block(key_blk, pos_blk, seg_blk)[0] - log_total[..., None])
        grad_weights = jnp.einsum(
            "qhd,khd->hqk", grad_attn, value_blk, preferred_element_type=jnp.float32
        )
        return (summed + jnp.sum(weights * grad_weights, axis=-1), None)

    delta_sum, unused = lax.scan(
        delta_step, jnp.zeros((head_count, token_count), jnp.float32), key_stack
    )

    def grad_step(summed, key_part):
        key_blk, value_blk, pos_blk, seg_blk = key_part
        scores, allowed = score_block(key_blk, pos_blk, seg_blk)
        weights = jnp.exp(scores - log_total[..., None])
        grad_weights = jnp.einsum(
            "qhd,khd->hqk", grad_attn, value_blk, preferred_element_type=jnp.float32
        )
        grad_scores = jnp.where(
            allowed[None], weights * (grad_weights - delta_sum[..., None]), 0.0
        ).astype(jnp.bfloat16)
        summed = (
            summed
            + jnp.einsum("hqk,khd->qhd", grad_scores, key_blk, preferred_element_type=jnp.float32)
            * score_scale
        )
        grad_key = (
            jnp.einsum("hqk,qhd->khd", grad_scores, queries, preferred_element_type=jnp.float32)
            * score_scale
        )
        grad_value = jnp.einsum(
            "hqk,qhd->khd",
            weights.astype(jnp.bfloat16),
            grad_attn,
            preferred_element_type=jnp.float32,
        )
        return (summed, (grad_key, grad_value))

    grad_query, (grad_keys, grad_values) = lax.scan(
        grad_step, jnp.zeros(head_shape, jnp.float32), key_stack
    )
    grad_keys_own, grad_values_own = (
        lax.psum_scatter(
            grad_keys.reshape(2, half_len, model_width).astype(jnp.bfloat16),
            "ctx",
            scatter_dimension=1,
            tiled=True,
        ).astype(jnp.float32),
        lax.psum_scatter(
            grad_values.reshape(2, half_len, model_width).astype(jnp.bfloat16),
            "ctx",
            scatter_dimension=1,
            tiled=True,
        ).astype(jnp.float32),
    )
    grad_q_rows = rotate_back(grad_query, cos_tab, sine_tab).reshape(token_count, model_width)
    grad_k_rows = rotate_back(grad_keys_own.reshape(head_shape), cos_tab, sine_tab).reshape(
        token_count, model_width
    )
    grad_projected = jnp.concatenate(
        [grad_q_rows, grad_k_rows, grad_values_own.reshape(token_count, model_width)], axis=-1
    ).astype(jnp.bfloat16)
    grad_qkv_weight = jnp.einsum(
        "td,te->de", normed_low, grad_projected, preferred_element_type=jnp.float32
    )
    grad_qkv_bias = jnp.sum(grad_projected.astype(jnp.float32), axis=0)
    grad_normed = jnp.einsum(
        "te,de->td", grad_projected, qkv_weight, preferred_element_type=jnp.float32
    )
    grad_inputs_norm, grad_gain_one = rms_back(
        inputs, inv_one, attn_gain.astype(jnp.float32), grad_normed
    )
    grad_tokens = (grad_resid + grad_inputs_norm).reshape(tokens.shape)
    attn_grads = (
        lax.psum_scatter(grad_qkv_weight, ("ctx", "fsdp"), scatter_dimension=0, tiled=True),
        lax.psum_scatter(grad_qkv_bias, ("ctx", "fsdp"), scatter_dimension=0, tiled=True),
        lax.psum_scatter(grad_out_weight, ("ctx", "fsdp"), scatter_dimension=0, tiled=True),
        lax.psum_scatter(grad_gain_one, ("ctx", "fsdp"), scatter_dimension=0, tiled=True),
    )
    return (
        output,
        grad_tokens,
        attn_grads[0],
        attn_grads[1],
        attn_grads[2],
        attn_grads[3],
        ffn_grads[0],
        ffn_grads[1],
        ffn_grads[2],
        ffn_grads[3],
        ffn_grads[4],
        expert_grads[0],
        expert_grads[1],
    )


def solution(mesh):
    in_specs = (
        P("fsdp", None, "ctx", None),
        P("fsdp", None, None),
        P("fsdp", None, "ctx", None),
        P("fsdp", None, "ctx", None),
        P(("ctx", "fsdp"), None),
        P(("ctx", "fsdp")),
        P(("ctx", "fsdp"), None),
        P(("ctx", "fsdp")),
        P(("ctx", "fsdp")),
        P(("ctx", "fsdp"), None),
        P(("ctx", "fsdp")),
        P(("ctx", "fsdp"), None),
        P(("ctx", "fsdp"), None),
        P("ctx", "fsdp", None),
        P("ctx", "fsdp", None),
    )
    out_specs = (
        P("fsdp", None, "ctx", None),
        P("fsdp", None, "ctx", None),
        P(("ctx", "fsdp"), None),
        P(("ctx", "fsdp")),
        P(("ctx", "fsdp"), None),
        P(("ctx", "fsdp")),
        P(("ctx", "fsdp")),
        P(("ctx", "fsdp"), None),
        P(("ctx", "fsdp")),
        P(("ctx", "fsdp"), None),
        P(("ctx", "fsdp"), None),
        P("ctx", "fsdp", None),
        P("ctx", "fsdp", None),
    )
    ctx_size = mesh.shape["ctx"]
    fsdp_size = mesh.shape["fsdp"]

    def local(*arrays):
        if HEADS % ctx_size:
            return local_wide(*arrays)
        return local_split(ctx_size, fsdp_size, *arrays)

    return jax.shard_map(local, mesh=mesh, in_specs=in_specs, out_specs=out_specs, check_vma=False)
```

```python
import functools

import jax
import jax.numpy as jnp
from jax import lax
from jax.experimental import pallas as pl
from jax.experimental.pallas import tpu as pltpu
from jax.sharding import PartitionSpec as P

HD = 128
HEADS = 16
FS = 5632
FE = 1408


RMS_EPS = 1e-06
ROPE_THETA = 1000000.0
MASK_FILL = -1e30
HIGHEST = lax.Precision.HIGHEST


def rope_tables(positions, head_dim):
    half_dim = head_dim // 2
    inv_freq = ROPE_THETA ** (-(jnp.arange(half_dim, dtype=jnp.float32) * 2.0 / head_dim))
    angles = positions.astype(jnp.float32)[:, None] * inv_freq[None, :]
    cos_tab = jnp.concatenate([jnp.cos(angles), jnp.cos(angles)], axis=-1)
    sine_tab = jnp.concatenate([jnp.sin(angles), jnp.sin(angles)], axis=-1)
    return (cos_tab, sine_tab)


def rotate(values, cos_tab, sine_tab):
    half_dim = values.shape[-1] // 2
    turned = jnp.concatenate([-values[..., half_dim:], values[..., :half_dim]], axis=-1)
    return values * cos_tab[:, None, :] + turned * sine_tab[:, None, :]


def rotate_back(upstream, cos_tab, sine_tab):
    half_dim = upstream.shape[-1] // 2
    scaled = upstream * sine_tab[:, None, :]
    return upstream * cos_tab[:, None, :] + jnp.concatenate(
        [scaled[..., half_dim:], -scaled[..., :half_dim]], axis=-1
    )


def rms_norm(values, gain_vec):
    inv_rms = lax.rsqrt(jnp.mean(values * values, axis=-1, keepdims=True) + RMS_EPS)
    return (values * inv_rms * gain_vec, inv_rms)


def rms_back(values, inv_rms, gain_vec, upstream):
    weighted = upstream * gain_vec
    inner_mean = jnp.mean(weighted * values, axis=-1, keepdims=True)
    return (
        inv_rms * weighted - values * inv_rms * inv_rms * inv_rms * inner_mean,
        jnp.sum(upstream * values * inv_rms, axis=0),
    )


def swiglu(pre_act, split_at):
    return jax.nn.silu(pre_act[..., :split_at]) * pre_act[..., split_at:]


def swiglu_back(pre_act, split_at, upstream):
    gate_part = pre_act[..., :split_at]
    up_part = pre_act[..., split_at:]
    sigmoid_g = jax.nn.sigmoid(gate_part)
    d_gate = upstream * up_part * sigmoid_g * (1.0 + gate_part * (1.0 - sigmoid_g))
    d_up = upstream * gate_part * sigmoid_g
    return jnp.concatenate([d_gate, d_up], axis=-1)


def ring_order(size):
    return list(range(0, size, 2)) + list(range(size - 1, 0, -2))


def ring_steps(size):
    order = ring_order(size)
    ahead = [(order[i], order[(i + 1) % size]) for i in range(size)]
    back = [(dst, src) for src, dst in ahead]
    return (ahead, back)


def ring_peers(size, ctx_index):
    order = ring_order(size)
    place = {dev: i for i, dev in enumerate(order)}
    table = jnp.array(
        [[order[(place[dev] + k) % size] for k in range(size)] for dev in range(size)], jnp.int32
    )
    row = lax.dynamic_index_in_dim(table, ctx_index, 0, keepdims=False)
    return [row[k] for k in range(size)]


def after(value, *deps):
    return lax.optimization_barrier((value,) + deps)


def ring_gather(block, size, ctx_index, rider=None):
    rows, width = block.shape

    def put(out, piece, peer, offset):
        return lax.dynamic_update_slice(out, piece, (peer * rows + offset, jnp.zeros_like(peer)))

    out = jnp.zeros((size * rows, width), block.dtype)
    ahead, back = ring_steps(size)
    peers = ring_peers(size, ctx_index)
    half = size // 2
    out = put(out, block, ctx_index, 0)
    fore = rear = block
    for k in range(1, half):
        fore = lax.ppermute(fore, "ctx", ahead)
        rear = lax.ppermute(rear, "ctx", back)
        if rider is not None and k == 2:
            fore, rider = after(fore, rider)
        out = put(out, fore, peers[size - k], 0)
        out = put(out, rear, peers[k], 0)
    fore = lax.ppermute(fore[: rows // 2], "ctx", ahead)
    rear = lax.ppermute(rear[rows // 2 :], "ctx", back)
    out = put(out, fore, peers[half], 0)
    out = put(out, rear, peers[half], rows // 2)
    return out if rider is None else (out, rider)


def ring_sums(parts, size, ctx_index, riders):
    f32 = jnp.float32
    rows = parts.shape[0] // size
    ahead, back = ring_steps(size)
    peers = ring_peers(size, ctx_index)
    half = size // 2

    def own(k, start, count):
        first = (peers[k % size] * rows + start, jnp.zeros_like(peers[0]))
        return lax.dynamic_slice(parts, first, (count, parts.shape[1])).astype(f32)

    def low(values):
        return values.astype(jnp.bfloat16)

    cut = rows // 2
    fore = lax.ppermute(low(own(half, 0, cut)), "ctx", ahead)
    rear = lax.ppermute(low(own(half, cut, cut)), "ctx", back)
    fore = jnp.concatenate(
        [low(fore.astype(f32) + own(half - 1, 0, cut)), low(own(half - 1, cut, cut))], axis=0
    )
    rear = jnp.concatenate(
        [low(own(1 - half, 0, cut)), low(rear.astype(f32) + own(1 - half, cut, cut))], axis=0
    )
    for k in range(half - 1, 0, -1):
        fore = lax.ppermute(fore, "ctx", ahead)
        rear = lax.ppermute(rear, "ctx", back)
        if riders and k == half - 1:
            fore, *riders = after(fore, *riders)
        if k > 1:
            fore = low(fore.astype(f32) + own(k - 1, 0, rows))
            rear = low(rear.astype(f32) + own(1 - k, 0, rows))
    return (fore, rear, riders)


def ring_scatter(parts, size, ctx_index, kept=None, riders=()):
    fore, rear, riders = ring_sums(parts, size, ctx_index, riders)
    kept = (parts if kept is None else kept).reshape(size, -1, parts.shape[1])
    kept = lax.dynamic_index_in_dim(kept, ctx_index, 0, keepdims=False)
    total = kept.astype(jnp.float32) + fore.astype(jnp.float32) + rear.astype(jnp.float32)
    return (total, *riders) if riders else total


def other_core(size):
    return [(i, i ^ 1) for i in range(size)]


def other_chip(size):
    return [(i, i ^ 2) for i in range(size)]


def fsdp_gather(shard, size, hold):
    index = lax.axis_index("fsdp")
    rows, width = shard.shape
    far = lax.ppermute(shard, "fsdp", other_chip(size))
    far, hold = after(far, hold)
    pair = jnp.where(
        index < 2, jnp.stack([shard, far], axis=0), jnp.stack([far, shard], axis=0)
    )
    near = lax.ppermute(pair, "fsdp", other_core(size))
    out = jnp.zeros((2, 2, rows, width), shard.dtype)
    out = lax.dynamic_update_index_in_dim(out, pair, index % 2, 1)
    out = lax.dynamic_update_index_in_dim(out, near, 1 - index % 2, 1)
    return (out.reshape(size * rows, width), hold)


def fsdp_scatter(grad, size):
    index = lax.axis_index("fsdp")
    core, chip = index % 2, index // 2
    grad = grad.reshape((2, 2) + grad.shape[1:])

    def pick(array, at, axis):
        return lax.dynamic_index_in_dim(array, at, axis, keepdims=False)

    near = lax.ppermute(pick(grad, 1 - core, 1), "fsdp", other_core(size))
    mine = (pick(grad, core, 1).astype(jnp.float32) + near.astype(jnp.float32)).astype(grad.dtype)
    far = lax.ppermute(pick(mine, 1 - chip, 0), "fsdp", other_chip(size))
    return pick(mine, chip, 0).astype(jnp.float32) + far.astype(jnp.float32)


def column_pieces(weight, groups, size, extra):
    rows = weight.shape[0]
    width = weight.shape[1] // (groups * size)
    pieces = weight.reshape(rows, groups, size, width).transpose(2, 0, 1, 3)
    pieces = pieces.reshape(size, rows, groups * width)
    if extra is not None:
        count = extra.shape[0]
        more = -(-count // (groups * width * 16)) * 16
        extra = jnp.pad(extra, (0, more * groups * width - count))
        extra = jnp.broadcast_to(
            extra.reshape(1, more, groups * width), (size, more, groups * width)
        )
        pieces = jnp.concatenate([pieces, extra], axis=1)
    return pieces


def merge_columns(pieces, groups, size):
    width = pieces.shape[2] // groups
    if width % 128 == 0:
        pieces = pieces.reshape(size, -1, groups, width).transpose(1, 2, 0, 3)
        return pieces.reshape(-1, groups * size * width).astype(jnp.float32)
    columns = [
        pieces[peer, :, group * width : (group + 1) * width]
        for group in range(groups)
        for peer in range(size)
    ]
    return jnp.concatenate(columns, axis=1).astype(jnp.float32)


def attention_back_kernel(
    q_ref, k_ref, v_ref, do_ref, lse_ref, key_ref, query_ref, dq_ref, dk_ref, dv_ref, *, rows
):
    f32, bf16 = jnp.float32, jnp.bfloat16
    scale = HD ** (-0.5)
    keys, values = k_ref[...], v_ref[...]
    key_pos, key_seg = key_ref[:, 0:1], key_ref[:, 1:2]

    def pair(a, b, dims):
        return lax.dot_general(a, b, (dims, ((), ())), preferred_element_type=f32)

    for start in range(0, q_ref.shape[0], rows):
        here = slice(start, start + rows)
        queries, upstream = q_ref[here, :], do_ref[here, :]
        allowed = (key_pos <= query_ref[0:1, here]) & (key_seg == query_ref[1:2, here])
        scores = jnp.where(allowed, pair(keys, queries, ((1,), (1,))) * scale, MASK_FILL)
        weights = jnp.exp(scores - lse_ref[0, :, here])
        grads = pair(values, upstream, ((1,), (1,)))
        delta = jnp.sum(weights * grads, axis=0, keepdims=True)
        grads = jnp.where(allowed, weights * (grads - delta), 0.0).astype(bf16)
        part_v = pair(weights.astype(bf16), upstream, ((1,), (0,)))
        part_k = pair(grads, queries, ((1,), (0,))) * scale
        if start == 0:
            dv_ref[...] = part_v
            dk_ref[...] = part_k
        else:
            dv_ref[...] += part_v
            dk_ref[...] += part_k
        dq_ref[here, :] = pair(grads, keys, ((0,), (0,))) * scale


def attention_back(queries, keys, values, upstream, log_total, positions, seg_rows):
    tokens, width = queries.shape
    heads = width // HD
    marks = jnp.stack([positions, seg_rows], axis=0)
    by_head = pl.BlockSpec((tokens, HD), lambda h: (0, h))
    return pl.pallas_call(
        functools.partial(attention_back_kernel, rows=min(256, tokens)),
        grid=(heads,),
        in_specs=[by_head] * 4
        + [
            pl.BlockSpec((1, 1, tokens), lambda h: (h, 0, 0)),
            pl.BlockSpec((tokens, 2), lambda h: (0, 0)),
            pl.BlockSpec((2, tokens), lambda h: (0, 0)),
        ],
        out_specs=[by_head] * 3,
        out_shape=[jax.ShapeDtypeStruct((tokens, width), jnp.float32)] * 3,
        compiler_params=pltpu.CompilerParams(vmem_limit_bytes=40 * 1024 * 1024),
        cost_estimate=pl.CostEstimate(
            flops=10 * tokens * tokens * width,
            bytes_accessed=20 * tokens * width,
            transcendentals=tokens * tokens * heads,
        ),
    )(queries, keys, values, upstream, log_total.reshape(heads, 1, tokens), marks.T, marks)


def local_split(
    ctx_size,
    fsdp_size,
    tokens,
    segments,
    routes,
    cotangent,
    w_qkv,
    b_qkv,
    w_out,
    gain_attn,
    gain_ffn,
    w_router,
    w_shared_gate,
    w_shared_in,
    w_shared_out,
    w_expert_in,
    w_expert_out,
):
    bf16, f32, i32 = jnp.bfloat16, jnp.float32, jnp.int32
    device_count = ctx_size * fsdp_size
    block_len = tokens.shape[2]
    width = tokens.shape[3]
    token_count = 2 * block_len
    top_count = routes.shape[3]
    seq_len = token_count * ctx_size
    ctx_index = lax.axis_index("ctx")
    expert_count = w_router.shape[1]
    capacity = token_count * top_count // expert_count
    own_heads = HEADS // ctx_size
    own_width = own_heads * HD
    fs_own = FS // ctx_size
    score_scale = HD ** (-0.5)

    def dot(a, b):
        return jnp.dot(a, b, preferred_element_type=f32)

    def dot_t(a, b):
        return lax.dot_general(a, b, (((1,), (1,)), ((), ())), preferred_element_type=f32)

    def t_dot(a, b):
        return lax.dot_general(a, b, (((0,), (0,)), ((), ())), preferred_element_type=f32)

    def own_rows(values):
        return lax.dynamic_index_in_dim(
            values.reshape((ctx_size, token_count) + values.shape[1:]), ctx_index, 0, keepdims=False
        )

    def sum_rows(grad):
        return lax.psum_scatter(grad.astype(bf16), "fsdp", scatter_dimension=0, tiled=True)

    shard = width // device_count
    small = [gain_attn, gain_ffn, w_shared_gate, w_router.reshape(-1), b_qkv]
    small_size = sum(piece.shape[0] for piece in small)
    small = jnp.concatenate(small + [routes.astype(bf16).reshape(-1)], axis=0)
    small_count = small.shape[0]
    own_tokens = tokens.reshape(token_count, width).astype(f32)
    own_scaled, inv_one = rms_norm(own_tokens, 1.0)
    scaled_rows = ring_gather(own_scaled.astype(bf16), ctx_size, ctx_index)
    pieces = column_pieces(w_qkv, 3, ctx_size, small)
    pieces = lax.all_to_all(pieces, "ctx", split_axis=0, concat_axis=0, tiled=True)
    shared_in = column_pieces(w_shared_in, 2, ctx_size, None)
    shared_in, scaled_rows = after(shared_in, scaled_rows)
    shared_in = lax.all_to_all(shared_in, "ctx", split_axis=0, concat_axis=0, tiled=True)
    pieces = lax.all_gather(pieces, "fsdp", axis=0, tiled=False).transpose(1, 0, 2, 3)
    qkv_weight = pieces[:, :, :shard].reshape(width, 3 * own_width)
    small = pieces[:, :, shard:].reshape(device_count, -1)[:, :small_count]
    attn_gain = small[:, :shard].reshape(width).astype(f32)
    ffn_gain = small[:, shard : 2 * shard].reshape(width).astype(f32)
    gate_vector = small[:, 2 * shard : 3 * shard].reshape(width)
    router_end = 3 * shard + shard * expert_count
    router_weight = small[:, 3 * shard : router_end].reshape(width, expert_count)
    bias = small[:, router_end:small_size].reshape(3, ctx_size, own_width).astype(f32)
    bias = lax.dynamic_index_in_dim(bias, ctx_index, 1, keepdims=False).reshape(3 * own_width)
    route_rows = small[:, small_size:].astype(i32)
    route_rows = lax.dynamic_index_in_dim(
        route_rows.reshape(ctx_size, fsdp_size, -1), lax.axis_index("fsdp"), 1, keepdims=False
    ).reshape(ctx_size, token_count, top_count)

    expert_in = lax.all_gather(w_expert_in[0], "fsdp", axis=0, tiled=True)

    block_ids = jnp.arange(ctx_size, dtype=i32)[:, None]
    local_index = jnp.arange(block_len, dtype=i32)[None, :]
    positions = jnp.stack(
        [
            block_ids * block_len + local_index,
            seq_len - (block_ids + 1) * block_len + local_index,
        ],
        axis=1,
    ).reshape(seq_len)
    seg_rows = (
        segments.reshape(2, ctx_size, block_len).transpose(1, 0, 2).reshape(seq_len)
    )
    cos_tab, sine_tab = rope_tables(positions, HD)

    normed_low = (scaled_rows.astype(f32) * attn_gain).astype(bf16)
    projected = dot(normed_low, qkv_weight) + bias
    head_shape = (seq_len, own_heads, HD)
    queries = rotate(projected[:, :own_width].reshape(head_shape), cos_tab, sine_tab).astype(bf16)
    keys = rotate(
        projected[:, own_width : 2 * own_width].reshape(head_shape), cos_tab, sine_tab
    ).astype(bf16)
    values = projected[:, 2 * own_width :].reshape(head_shape).astype(bf16)
    out_weight, queries = fsdp_gather(w_out, fsdp_size, queries)
    allowed = (positions[None, :] <= positions[:, None]) & (seg_rows[None, :] == seg_rows[:, None])
    scores = jnp.einsum("qhd,khd->hqk", queries, keys, preferred_element_type=f32) * score_scale
    scores = jnp.where(allowed[None], scores, MASK_FILL)
    top_score = jnp.max(scores, axis=-1, keepdims=True)
    log_total = top_score + jnp.log(jnp.sum(jnp.exp(scores - top_score), axis=-1, keepdims=True))
    weights = jnp.exp(scores - log_total)
    weights_low = weights.astype(bf16)
    attended = jnp.einsum("hqk,khd->qhd", weights_low, values, preferred_element_type=f32)
    attn_own = attended.astype(bf16).reshape(seq_len, own_width)
    shared_out, attn_own = fsdp_gather(w_shared_out, fsdp_size, attn_own)
    expert_out, attn_own = fsdp_gather(w_expert_out[0], fsdp_size, attn_own)
    attn_parts, shared_in = after(dot(attn_own, out_weight).astype(bf16), shared_in)
    shared_in = lax.all_gather(shared_in, "fsdp", axis=0, tiled=False)
    own_residual = own_tokens + ring_scatter(attn_parts, ctx_size, ctx_index)

    normed_two, inv_two = rms_norm(own_residual, ffn_gain)
    own_low = normed_two.astype(bf16)
    low_two, grad_rows = ring_gather(
        own_low, ctx_size, ctx_index, cotangent.reshape(token_count, width)
    )
    grad_rows = lax.all_gather(grad_rows, "ctx", axis=0, tiled=True)
    mixed_weight = jnp.concatenate([router_weight, gate_vector[:, None]], axis=1)
    logits = dot(low_two, mixed_weight)
    probs_all = jax.nn.softmax(logits[:, :expert_count], axis=-1)
    scale_all = jax.nn.sigmoid(logits[:, expert_count])
    gate_all = lax.dynamic_index_in_dim(probs_all, ctx_index, 1, keepdims=False)

    named = jnp.any(route_rows == ctx_index, axis=-1)
    before = jnp.arange(token_count)[:, None] < jnp.arange(token_count)[None, :]
    rank = dot(named.astype(bf16), before.astype(bf16)).astype(i32)
    slot_of = jnp.where(named & (rank < capacity), rank, -1)
    slot_mask = slot_of[:, None, :] == jnp.arange(capacity, dtype=i32)[None, :, None]
    slot_map = slot_mask.astype(bf16)
    blocks_two = low_two.reshape(ctx_size, token_count, width)
    gate_blocks = gate_all.reshape(ctx_size, token_count)

    def to_slots(blocks):
        picked = jnp.einsum("bmt,btd->bmd", slot_map, blocks, preferred_element_type=f32)
        return picked.reshape(ctx_size * capacity, width)

    def to_tokens(slots):
        spread = jnp.einsum(
            "bmt,bmd->btd",
            slot_map,
            slots.reshape(ctx_size, capacity, width),
            preferred_element_type=f32,
        )
        return spread.reshape(seq_len, width)

    buffer = to_slots(blocks_two).astype(bf16)
    expert_pre = dot(buffer, expert_in)
    expert_hid = swiglu(expert_pre, FE).astype(bf16)
    expert_res = dot(expert_hid, expert_out).astype(bf16)
    routed = gate_all[:, None] * to_tokens(expert_res)

    shared_in, expert_res = after(shared_in, expert_res)
    shared_in = shared_in.transpose(1, 0, 2, 3).reshape(width, 2 * fs_own)
    shared_pre = dot(low_two, shared_in)
    shared_hid = swiglu(shared_pre, fs_own).astype(bf16)
    shared_res = dot(shared_hid, shared_out)
    out_parts = (scale_all[:, None] * shared_res + routed).astype(bf16)
    grad_rows, out_parts = after(grad_rows, out_parts)

    grad_slots = to_slots(grad_rows.reshape(ctx_size, token_count, width))
    gate_slots = jnp.sum(jnp.where(slot_mask, gate_blocks[:, None, :], 0.0), axis=-1).reshape(-1, 1)
    grad_res = (gate_slots * grad_slots).astype(bf16)
    grad_hid = dot_t(grad_res, expert_out)
    slot_terms = jnp.sum(expert_hid.astype(f32) * grad_hid, axis=-1)
    slot_terms = slot_terms.reshape(ctx_size, capacity, 1)
    gate_terms = jnp.sum(jnp.where(slot_mask, slot_terms, 0.0), axis=1)
    grad_pre = swiglu_back(expert_pre, FE, grad_hid).astype(bf16)
    grad_expert_in = t_dot(buffer, grad_pre)
    grad_buffer = dot_t(grad_pre, expert_in).astype(bf16)

    grad_f32 = grad_rows.astype(f32)
    grad_expert_in, grad_shared_res = after(
        grad_expert_in.astype(bf16), (scale_all[:, None] * grad_f32).astype(bf16)
    )
    sum_expert_in = sum_rows(grad_expert_in)

    grad_shared_hid = dot_t(grad_shared_res, shared_out)
    scale_terms = jnp.sum(shared_hid.astype(f32) * grad_shared_hid, axis=-1)
    grad_shared_pre = swiglu_back(shared_pre, fs_own, grad_shared_hid).astype(bf16)
    two_parts = (dot_t(grad_shared_pre, shared_in) + to_tokens(grad_buffer)).astype(bf16)
    two_parts, expert_hid, shared_hid, grad_shared_pre = after(
        two_parts, expert_hid, shared_hid, grad_shared_pre
    )
    grad_expert_out = t_dot(expert_hid, grad_res).astype(bf16)
    grad_shared_out = t_dot(shared_hid, grad_shared_res).astype(bf16)
    grad_shared_in = t_dot(low_two, grad_shared_pre).astype(bf16)
    grad_two = ring_scatter(two_parts, ctx_size, ctx_index)
    dots = jnp.stack([gate_terms, scale_terms.reshape(ctx_size, token_count)], axis=1)
    dots = lax.all_to_all(dots, "ctx", split_axis=0, concat_axis=0, tiled=True)
    grad_two, grad_shared_in, grad_shared_out, grad_expert_out, dots = after(
        grad_two, grad_shared_in, grad_shared_out, grad_expert_out, dots
    )
    sum_shared_in = grad_shared_in.reshape(ctx_size, fsdp_size, shard, 2 * fs_own)
    sum_shared_in = lax.psum_scatter(
        sum_shared_in.transpose(1, 0, 2, 3).reshape(width, 2 * fs_own),
        "fsdp",
        scatter_dimension=0,
        tiled=True,
    ).reshape(ctx_size, shard, 2 * fs_own)
    sum_expert_out = sum_rows(grad_expert_out)
    own_probs = own_rows(probs_all)
    own_scale = own_rows(scale_all)
    own_chosen = routes.reshape(token_count, top_count)
    chosen_mask = jnp.any(
        own_chosen[..., None] == jnp.arange(expert_count, dtype=i32), axis=1
    )
    prob_terms = jnp.where(chosen_mask, dots[:, 0].T, 0.0)
    grad_logits = (
        prob_terms - own_probs * jnp.sum(prob_terms, axis=-1, keepdims=True)
    ).astype(bf16)
    grad_gate_pre = (jnp.sum(dots[:, 1], axis=0) * (1.0 - own_scale)).astype(bf16)
    grad_router = t_dot(own_low, grad_logits)
    grad_gate_vector = t_dot(own_low, grad_gate_pre[:, None])
    grad_two = grad_two + dot_t(grad_logits, router_weight)
    grad_two = grad_two + grad_gate_pre.astype(f32)[:, None] * gate_vector.astype(f32)[None, :]
    grad_resid_norm, grad_gain_two = rms_back(
        own_residual, inv_two, ffn_gain, grad_two
    )
    grad_resid = cotangent.reshape(token_count, width).astype(f32) + grad_resid_norm

    grad_mixed, sum_expert_in = after(grad_resid.astype(bf16), sum_expert_in)
    mixed_all = ring_gather(grad_mixed, ctx_size, ctx_index)
    grad_attn = dot_t(mixed_all, out_weight).astype(bf16)
    grad_attn, sum_shared_in = after(grad_attn, sum_shared_in)
    sum_shared_in = lax.all_to_all(
        sum_shared_in, "ctx", split_axis=0, concat_axis=0, tiled=True
    )
    grad_q, grad_k, grad_v = attention_back(
        queries.reshape(seq_len, own_width),
        keys.reshape(seq_len, own_width),
        values.reshape(seq_len, own_width),
        grad_attn,
        log_total,
        positions,
        seg_rows,
    )
    grad_projected = jnp.concatenate(
        [
            rotate_back(grad_q.reshape(head_shape), cos_tab, sine_tab).reshape(seq_len, own_width),
            rotate_back(grad_k.reshape(head_shape), cos_tab, sine_tab).reshape(seq_len, own_width),
            grad_v,
        ],
        axis=-1,
    ).astype(bf16)
    one_sums = dot_t(grad_projected, qkv_weight)
    grad_gain_one = jnp.sum(one_sums * scaled_rows.astype(f32), axis=0)
    one_parts = one_sums.astype(bf16)
    one_kept, grad_projected = after(one_parts, grad_projected)
    one_kept, attn_own = after(one_kept, attn_own)
    grad_normed, sum_expert_out, sum_shared_in = ring_scatter(
        one_parts, ctx_size, ctx_index, one_kept, (sum_expert_out, sum_shared_in)
    )
    grad_qkv_weight = t_dot(normed_low, grad_projected)
    grad_bias = jnp.sum(grad_projected.astype(f32), axis=0).reshape(3, 1, own_width)
    grad_bias = jnp.where(
        jnp.arange(ctx_size, dtype=i32)[None, :, None] == ctx_index, grad_bias, 0.0
    )

    grad_out_weight = t_dot(attn_own, mixed_all)
    small_grads = [grad_gain_one, grad_gain_two, grad_gate_vector, grad_router, grad_bias]
    small_grads = jnp.concatenate(
        [piece.reshape(device_count, -1) for piece in small_grads], axis=1
    )
    more = -(-small_size // (3 * own_width * 16)) * 16
    small_grads = jnp.pad(small_grads, ((0, 0), (0, more * 3 * own_width - small_size)))
    pieces = jnp.concatenate(
        [
            grad_qkv_weight.astype(bf16).reshape(ctx_size, fsdp_size, shard, 3 * own_width),
            small_grads.astype(bf16).reshape(ctx_size, fsdp_size, more, 3 * own_width),
        ],
        axis=2,
    )
    pieces = pieces.transpose(1, 0, 2, 3).reshape(-1, 3 * own_width)
    pieces = lax.psum_scatter(pieces, "fsdp", scatter_dimension=0, tiled=True)
    grad_normed, pieces, out_parts, grad_shared_out, grad_out_weight = after(
        grad_normed, pieces, out_parts, grad_shared_out, grad_out_weight.astype(bf16)
    )
    sum_shared_out = fsdp_scatter(grad_shared_out.reshape(fsdp_size, -1, width), fsdp_size)
    sum_out_weight = sum_rows(grad_out_weight)
    out_sum, sum_shared_out, sum_out_weight = ring_scatter(
        out_parts, ctx_size, ctx_index, riders=(sum_shared_out, sum_out_weight)
    )
    output = own_residual + out_sum
    output = output.astype(bf16).reshape(tokens.shape)
    pieces = pieces.reshape(ctx_size, shard + more, 3 * own_width)
    pieces = lax.all_to_all(pieces, "ctx", split_axis=0, concat_axis=0, tiled=True)
    grad_inputs_norm, unused = rms_back(
        own_tokens,
        inv_one,
        attn_gain,
        grad_normed,
    )
    grad_tokens = (grad_resid + grad_inputs_norm).reshape(tokens.shape)
    small_grads = jnp.sum(pieces[:, shard:].reshape(ctx_size, -1).astype(f32), axis=0)
    return (
        output,
        grad_tokens,
        merge_columns(pieces[:, :shard], 3, ctx_size),
        small_grads[router_end:small_size],
        sum_out_weight.astype(f32),
        small_grads[:shard],
        small_grads[shard : 2 * shard],
        small_grads[3 * shard : router_end].reshape(shard, expert_count),
        small_grads[2 * shard : 3 * shard],
        merge_columns(sum_shared_in, 2, ctx_size),
        sum_shared_out,
        sum_expert_in.astype(f32)[None],
        sum_expert_out.astype(f32)[None],
    )


def local_wide(
    tokens,
    segments,
    routes,
    cotangent,
    w_qkv,
    b_qkv,
    w_out,
    gain_attn,
    gain_ffn,
    w_router,
    w_shared_gate,
    w_shared_in,
    w_shared_out,
    w_expert_in,
    w_expert_out,
):
    block_len = tokens.shape[2]
    model_width = tokens.shape[3]
    token_count = 2 * block_len
    top_count = routes.shape[3]
    half_len = segments.shape[2]
    seq_len = 2 * half_len
    ctx_index = lax.axis_index("ctx")
    head_count = model_width // HD
    expert_count = w_router.shape[1]
    capacity = token_count * top_count // expert_count
    slot_count = expert_count * capacity
    key_rows = min(512, seq_len)
    key_blocks = seq_len // key_rows
    score_scale = HD ** (-0.5)
    head_shape = (token_count, head_count, HD)
    attn_set = (
        lax.all_gather(w_qkv, ("ctx", "fsdp"), axis=0, tiled=True),
        lax.all_gather(b_qkv, ("ctx", "fsdp"), axis=0, tiled=True),
        lax.all_gather(w_out, ("ctx", "fsdp"), axis=0, tiled=True),
        lax.all_gather(gain_attn, ("ctx", "fsdp"), axis=0, tiled=True),
    )
    qkv_weight, qkv_bias, out_weight, attn_gain = attn_set
    inputs = tokens.reshape(token_count, model_width).astype(jnp.float32)
    normed, inv_one = rms_norm(inputs, attn_gain.astype(jnp.float32))
    normed_low = normed.astype(jnp.bfloat16)
    projected = jnp.dot(
        normed_low, qkv_weight, preferred_element_type=jnp.float32
    ) + qkv_bias.astype(jnp.float32)
    local_index = jnp.arange(block_len, dtype=jnp.int32)
    query_pos = jnp.concatenate(
        [ctx_index * block_len + local_index, seq_len - (ctx_index + 1) * block_len + local_index]
    )
    half_index = jnp.arange(half_len, dtype=jnp.int32)
    key_pos = jnp.concatenate(
        [half_index, seq_len - block_len * (half_index // block_len + 1) + half_index % block_len]
    ).reshape(key_blocks, key_rows)
    key_seg = segments.reshape(key_blocks, key_rows)
    query_seg = lax.dynamic_slice_in_dim(segments[0], ctx_index * block_len, block_len, 1).reshape(
        token_count
    )
    cos_tab, sine_tab = rope_tables(query_pos, HD)
    queries = rotate(projected[:, :model_width].reshape(head_shape), cos_tab, sine_tab).astype(
        jnp.bfloat16
    )
    keys_own = rotate(
        projected[:, model_width : 2 * model_width].reshape(head_shape), cos_tab, sine_tab
    ).astype(jnp.bfloat16)
    values_own = projected[:, 2 * model_width :].astype(jnp.bfloat16)
    keys_all, values_all = (
        lax.all_gather(keys_own.reshape(2, block_len, model_width), "ctx", axis=1, tiled=True),
        lax.all_gather(values_own.reshape(2, block_len, model_width), "ctx", axis=1, tiled=True),
    )
    keys_all = keys_all.reshape(key_blocks, key_rows, head_count, HD)
    values_all = values_all.reshape(key_blocks, key_rows, head_count, HD)

    def score_block(key_blk, pos_blk, seg_blk):
        raw_scores = (
            jnp.einsum("qhd,khd->hqk", queries, key_blk, preferred_element_type=jnp.float32)
            * score_scale
        )
        allowed = (pos_blk[None, :] <= query_pos[:, None]) & (
            seg_blk[None, :] == query_seg[:, None]
        )
        return (jnp.where(allowed[None], raw_scores, MASK_FILL), allowed)

    def total_step(running, key_part):
        run_max, run_sum = running
        scores = score_block(key_part[0], key_part[1], key_part[2])[0]
        new_max = jnp.maximum(run_max, jnp.max(scores, axis=-1))
        run_sum = run_sum * jnp.exp(run_max - new_max) + jnp.sum(
            jnp.exp(scores - new_max[..., None]), axis=-1
        )
        return ((new_max, run_sum), None)

    start_max = jnp.full((head_count, token_count), MASK_FILL, jnp.float32)
    start_sum = jnp.zeros((head_count, token_count), jnp.float32)
    (run_max, run_sum), unused = lax.scan(
        total_step, (start_max, start_sum), (keys_all, key_pos, key_seg)
    )
    log_total = run_max + jnp.log(run_sum)

    def attend_step(summed, key_part):
        key_blk, value_blk, pos_blk, seg_blk = key_part
        scores = score_block(key_blk, pos_blk, seg_blk)[0]
        weights = jnp.exp(scores - log_total[..., None]).astype(jnp.bfloat16)
        return (
            summed
            + jnp.einsum("hqk,khd->qhd", weights, value_blk, preferred_element_type=jnp.float32),
            None,
        )

    key_stack = (keys_all, values_all, key_pos, key_seg)
    attended, unused = lax.scan(attend_step, jnp.zeros(head_shape, jnp.float32), key_stack)
    attn_low = attended.reshape(token_count, model_width).astype(jnp.bfloat16)
    residual = inputs + jnp.dot(attn_low, out_weight, preferred_element_type=jnp.float32)
    ffn_set = (
        lax.all_gather(gain_ffn, ("ctx", "fsdp"), axis=0, tiled=True),
        lax.all_gather(w_router, ("ctx", "fsdp"), axis=0, tiled=True),
        lax.all_gather(w_shared_gate, ("ctx", "fsdp"), axis=0, tiled=True),
        lax.all_gather(w_shared_in, ("ctx", "fsdp"), axis=0, tiled=True),
        lax.all_gather(w_shared_out, ("ctx", "fsdp"), axis=0, tiled=True),
    )
    ffn_gain, router_weight, gate_vector, shared_in, shared_out = ffn_set
    normed_two, inv_two = rms_norm(residual, ffn_gain.astype(jnp.float32))
    low_two = normed_two.astype(jnp.bfloat16)
    logits = jnp.dot(low_two, router_weight, preferred_element_type=jnp.float32)
    router_probs = jax.nn.softmax(logits, axis=-1)
    chosen = routes.reshape(token_count, top_count)
    chosen_mask = chosen[..., None] == jnp.arange(expert_count, dtype=jnp.int32)
    gate_vals = jnp.sum(jnp.where(chosen_mask, router_probs[:, None, :], 0.0), axis=-1)
    shared_scale = jax.nn.sigmoid(jnp.dot(low_two, gate_vector, preferred_element_type=jnp.float32))
    shared_pre = jnp.dot(low_two, shared_in, preferred_element_type=jnp.float32)
    shared_hid = swiglu(shared_pre, FS).astype(jnp.bfloat16)
    shared_res = jnp.dot(shared_hid, shared_out, preferred_element_type=jnp.float32)
    pair_routes = chosen.reshape(token_count * top_count)
    expert_marks = (
        pair_routes[:, None] == jnp.arange(expert_count, dtype=jnp.int32)[None, :]
    ).astype(jnp.int32)
    pair_ranks = jnp.sum((jnp.cumsum(expert_marks, axis=0) - expert_marks) * expert_marks, axis=1)
    pair_target = jnp.where(pair_ranks < capacity, pair_routes * capacity + pair_ranks, -1)
    pair_map = pair_target[:, None] == jnp.arange(slot_count, dtype=jnp.int32)[None, :]
    pair_low = pair_map.astype(jnp.bfloat16)
    token_map = jnp.sum(
        pair_map.reshape(token_count, top_count, slot_count).astype(jnp.int32), axis=1
    ).astype(jnp.bfloat16)
    outgoing = jnp.einsum(
        "tc,td->cd", token_map, low_two, preferred_element_type=jnp.float32
    ).astype(jnp.bfloat16)
    incoming = lax.all_to_all(
        outgoing.reshape(expert_count, capacity, model_width),
        "ctx",
        split_axis=0,
        concat_axis=1,
        tiled=True,
    )
    expert_in, expert_out = (
        lax.all_gather(w_expert_in, "fsdp", axis=1, tiled=True),
        lax.all_gather(w_expert_out, "fsdp", axis=1, tiled=True),
    )
    expert_pre = jnp.einsum("erd,edf->erf", incoming, expert_in, preferred_element_type=jnp.float32)
    expert_hid = swiglu(expert_pre, FE).astype(jnp.bfloat16)
    expert_res = jnp.einsum(
        "erf,efd->erd", expert_hid, expert_out, preferred_element_type=jnp.float32
    ).astype(jnp.bfloat16)
    returned = lax.all_to_all(expert_res, "ctx", split_axis=1, concat_axis=0, tiled=True).reshape(
        slot_count, model_width
    )
    pair_vals = jnp.dot(pair_low, returned, preferred_element_type=jnp.float32).reshape(
        token_count, top_count, model_width
    )
    routed = jnp.sum(gate_vals[..., None] * pair_vals, axis=1)
    output = (
        (residual + shared_scale[:, None] * shared_res + routed)
        .astype(jnp.bfloat16)
        .reshape(tokens.shape)
    )
    grad_out = cotangent.reshape(token_count, model_width).astype(jnp.float32)
    pair_grads = gate_vals[..., None] * grad_out[:, None, :]
    grad_gates = jnp.sum(grad_out[:, None, :] * pair_vals, axis=-1)
    grad_returned = jnp.einsum(
        "pc,pd->cd",
        pair_map.astype(jnp.float32),
        pair_grads.reshape(token_count * top_count, model_width),
        precision=HIGHEST,
    ).astype(jnp.bfloat16)
    grad_res = lax.all_to_all(
        grad_returned.reshape(expert_count, capacity, model_width),
        "ctx",
        split_axis=0,
        concat_axis=1,
        tiled=True,
    )
    grad_expert_out = jnp.einsum(
        "erf,erd->efd", expert_hid, grad_res, preferred_element_type=jnp.float32
    )
    grad_hid = jnp.einsum("erd,efd->erf", grad_res, expert_out, preferred_element_type=jnp.float32)
    grad_pre = swiglu_back(expert_pre, FE, grad_hid).astype(jnp.bfloat16)
    grad_expert_in = jnp.einsum(
        "erd,erf->edf", incoming, grad_pre, preferred_element_type=jnp.float32
    )
    grad_incoming = jnp.einsum(
        "erf,edf->erd", grad_pre, expert_in, preferred_element_type=jnp.float32
    ).astype(jnp.bfloat16)
    grad_outgoing = lax.all_to_all(
        grad_incoming, "ctx", split_axis=1, concat_axis=0, tiled=True
    ).reshape(slot_count, model_width)
    expert_grads = (
        lax.psum_scatter(
            grad_expert_in.astype(jnp.bfloat16), "fsdp", scatter_dimension=1, tiled=True
        ).astype(jnp.float32),
        lax.psum_scatter(
            grad_expert_out.astype(jnp.bfloat16), "fsdp", scatter_dimension=1, tiled=True
        ).astype(jnp.float32),
    )
    grad_two = jnp.einsum("tc,cd->td", token_map, grad_outgoing, preferred_element_type=jnp.float32)
    grad_probs = jnp.sum(jnp.where(chosen_mask, grad_gates[..., None], 0.0), axis=1)
    grad_logits = (
        router_probs * (grad_probs - jnp.sum(router_probs * grad_probs, axis=-1, keepdims=True))
    ).astype(jnp.bfloat16)
    grad_router = jnp.einsum("td,te->de", low_two, grad_logits, preferred_element_type=jnp.float32)
    grad_shared_res = (shared_scale[:, None] * grad_out).astype(jnp.bfloat16)
    grad_gate_pre = (
        jnp.sum(grad_out * shared_res, axis=-1) * shared_scale * (1.0 - shared_scale)
    ).astype(jnp.bfloat16)
    grad_shared_out = jnp.einsum(
        "tf,td->fd", shared_hid, grad_shared_res, preferred_element_type=jnp.float32
    )
    grad_shared_hid = jnp.einsum(
        "td,fd->tf", grad_shared_res, shared_out, preferred_element_type=jnp.float32
    )
    grad_shared_pre = swiglu_back(shared_pre, FS, grad_shared_hid).astype(jnp.bfloat16)
    grad_shared_in = jnp.einsum(
        "td,tf->df", low_two, grad_shared_pre, preferred_element_type=jnp.float32
    )
    grad_gate_vector = jnp.einsum(
        "td,t->d", low_two, grad_gate_pre, preferred_element_type=jnp.float32
    )
    grad_two = grad_two + jnp.einsum(
        "te,de->td", grad_logits, router_weight, preferred_element_type=jnp.float32
    )
    grad_two = grad_two + jnp.einsum(
        "tf,df->td", grad_shared_pre, shared_in, preferred_element_type=jnp.float32
    )
    grad_two = (
        grad_two
        + grad_gate_pre.astype(jnp.float32)[:, None] * gate_vector.astype(jnp.float32)[None, :]
    )
    grad_resid_norm, grad_gain_two = rms_back(
        residual, inv_two, ffn_gain.astype(jnp.float32), grad_two
    )
    grad_resid = grad_out + grad_resid_norm
    ffn_grads = (
        lax.psum_scatter(grad_gain_two, ("ctx", "fsdp"), scatter_dimension=0, tiled=True),
        lax.psum_scatter(grad_router, ("ctx", "fsdp"), scatter_dimension=0, tiled=True),
        lax.psum_scatter(grad_gate_vector, ("ctx", "fsdp"), scatter_dimension=0, tiled=True),
        lax.psum_scatter(grad_shared_in, ("ctx", "fsdp"), scatter_dimension=0, tiled=True),
        lax.psum_scatter(grad_shared_out, ("ctx", "fsdp"), scatter_dimension=0, tiled=True),
    )
    grad_mixed = grad_resid.astype(jnp.bfloat16)
    grad_out_weight = jnp.einsum(
        "tc,td->cd", attn_low, grad_mixed, preferred_element_type=jnp.float32
    )
    grad_attn = (
        jnp.einsum("td,cd->tc", grad_mixed, out_weight, preferred_element_type=jnp.float32)
        .astype(jnp.bfloat16)
        .reshape(head_shape)
    )

    def delta_step(summed, key_part):
        key_blk, value_blk, pos_blk, seg_blk = key_part
        weights = jnp.exp(score_block(key_blk, pos_blk, seg_blk)[0] - log_total[..., None])
        grad_weights = jnp.einsum(
            "qhd,khd->hqk", grad_attn, value_blk, preferred_element_type=jnp.float32
        )
        return (summed + jnp.sum(weights * grad_weights, axis=-1), None)

    delta_sum, unused = lax.scan(
        delta_step, jnp.zeros((head_count, token_count), jnp.float32), key_stack
    )

    def grad_step(summed, key_part):
        key_blk, value_blk, pos_blk, seg_blk = key_part
        scores, allowed = score_block(key_blk, pos_blk, seg_blk)
        weights = jnp.exp(scores - log_total[..., None])
        grad_weights = jnp.einsum(
            "qhd,khd->hqk", grad_attn, value_blk, preferred_element_type=jnp.float32
        )
        grad_scores = jnp.where(
            allowed[None], weights * (grad_weights - delta_sum[..., None]), 0.0
        ).astype(jnp.bfloat16)
        summed = (
            summed
            + jnp.einsum("hqk,khd->qhd", grad_scores, key_blk, preferred_element_type=jnp.float32)
            * score_scale
        )
        grad_key = (
            jnp.einsum("hqk,qhd->khd", grad_scores, queries, preferred_element_type=jnp.float32)
            * score_scale
        )
        grad_value = jnp.einsum(
            "hqk,qhd->khd",
            weights.astype(jnp.bfloat16),
            grad_attn,
            preferred_element_type=jnp.float32,
        )
        return (summed, (grad_key, grad_value))

    grad_query, (grad_keys, grad_values) = lax.scan(
        grad_step, jnp.zeros(head_shape, jnp.float32), key_stack
    )
    grad_keys_own, grad_values_own = (
        lax.psum_scatter(
            grad_keys.reshape(2, half_len, model_width).astype(jnp.bfloat16),
            "ctx",
            scatter_dimension=1,
            tiled=True,
        ).astype(jnp.float32),
        lax.psum_scatter(
            grad_values.reshape(2, half_len, model_width).astype(jnp.bfloat16),
            "ctx",
            scatter_dimension=1,
            tiled=True,
        ).astype(jnp.float32),
    )
    grad_q_rows = rotate_back(grad_query, cos_tab, sine_tab).reshape(token_count, model_width)
    grad_k_rows = rotate_back(grad_keys_own.reshape(head_shape), cos_tab, sine_tab).reshape(
        token_count, model_width
    )
    grad_projected = jnp.concatenate(
        [grad_q_rows, grad_k_rows, grad_values_own.reshape(token_count, model_width)], axis=-1
    ).astype(jnp.bfloat16)
    grad_qkv_weight = jnp.einsum(
        "td,te->de", normed_low, grad_projected, preferred_element_type=jnp.float32
    )
    grad_qkv_bias = jnp.sum(grad_projected.astype(jnp.float32), axis=0)
    grad_normed = jnp.einsum(
        "te,de->td", grad_projected, qkv_weight, preferred_element_type=jnp.float32
    )
    grad_inputs_norm, grad_gain_one = rms_back(
        inputs, inv_one, attn_gain.astype(jnp.float32), grad_normed
    )
    grad_tokens = (grad_resid + grad_inputs_norm).reshape(tokens.shape)
    attn_grads = (
        lax.psum_scatter(grad_qkv_weight, ("ctx", "fsdp"), scatter_dimension=0, tiled=True),
        lax.psum_scatter(grad_qkv_bias, ("ctx", "fsdp"), scatter_dimension=0, tiled=True),
        lax.psum_scatter(grad_out_weight, ("ctx", "fsdp"), scatter_dimension=0, tiled=True),
        lax.psum_scatter(grad_gain_one, ("ctx", "fsdp"), scatter_dimension=0, tiled=True),
    )
    return (
        output,
        grad_tokens,
        attn_grads[0],
        attn_grads[1],
        attn_grads[2],
        attn_grads[3],
        ffn_grads[0],
        ffn_grads[1],
        ffn_grads[2],
        ffn_grads[3],
        ffn_grads[4],
        expert_grads[0],
        expert_grads[1],
    )


def solution(mesh):
    in_specs = (
        P("fsdp", None, "ctx", None),
        P("fsdp", None, None),
        P("fsdp", None, "ctx", None),
        P("fsdp", None, "ctx", None),
        P(("ctx", "fsdp"), None),
        P(("ctx", "fsdp")),
        P(("ctx", "fsdp"), None),
        P(("ctx", "fsdp")),
        P(("ctx", "fsdp")),
        P(("ctx", "fsdp"), None),
        P(("ctx", "fsdp")),
        P(("ctx", "fsdp"), None),
        P(("ctx", "fsdp"), None),
        P("ctx", "fsdp", None),
        P("ctx", "fsdp", None),
    )
    out_specs = (
        P("fsdp", None, "ctx", None),
        P("fsdp", None, "ctx", None),
        P(("ctx", "fsdp"), None),
        P(("ctx", "fsdp")),
        P(("ctx", "fsdp"), None),
        P(("ctx", "fsdp")),
        P(("ctx", "fsdp")),
        P(("ctx", "fsdp"), None),
        P(("ctx", "fsdp")),
        P(("ctx", "fsdp"), None),
        P(("ctx", "fsdp"), None),
        P("ctx", "fsdp", None),
        P("ctx", "fsdp", None),
    )
    ctx_size = mesh.shape["ctx"]
    fsdp_size = mesh.shape["fsdp"]

    def local(*arrays):
        if HEADS % ctx_size:
            return local_wide(*arrays)
        return local_split(ctx_size, fsdp_size, *arrays)

    return jax.shard_map(local, mesh=mesh, in_specs=in_specs, out_specs=out_specs, check_vma=False)
```

```python
import functools

import jax
import jax.numpy as jnp
from jax import lax
from jax.experimental import pallas as pl
from jax.experimental.pallas import tpu as pltpu
from jax.sharding import PartitionSpec as P

HD = 128
HEADS = 16
FS = 5632
FE = 1408


RMS_EPS = 1e-06
ROPE_THETA = 1000000.0
MASK_FILL = -1e30
HIGHEST = lax.Precision.HIGHEST


def rope_tables(positions, head_dim):
    half_dim = head_dim // 2
    inv_freq = ROPE_THETA ** (-(jnp.arange(half_dim, dtype=jnp.float32) * 2.0 / head_dim))
    angles = positions.astype(jnp.float32)[:, None] * inv_freq[None, :]
    cos_tab = jnp.concatenate([jnp.cos(angles), jnp.cos(angles)], axis=-1)
    sine_tab = jnp.concatenate([jnp.sin(angles), jnp.sin(angles)], axis=-1)
    return (cos_tab, sine_tab)


def rotate(values, cos_tab, sine_tab):
    half_dim = values.shape[-1] // 2
    turned = jnp.concatenate([-values[..., half_dim:], values[..., :half_dim]], axis=-1)
    return values * cos_tab[:, None, :] + turned * sine_tab[:, None, :]


def rotate_back(upstream, cos_tab, sine_tab):
    half_dim = upstream.shape[-1] // 2
    scaled = upstream * sine_tab[:, None, :]
    return upstream * cos_tab[:, None, :] + jnp.concatenate(
        [scaled[..., half_dim:], -scaled[..., :half_dim]], axis=-1
    )


def rms_norm(values, gain_vec):
    inv_rms = lax.rsqrt(jnp.mean(values * values, axis=-1, keepdims=True) + RMS_EPS)
    return (values * inv_rms * gain_vec, inv_rms)


def rms_back(values, inv_rms, gain_vec, upstream):
    weighted = upstream * gain_vec
    inner_mean = jnp.mean(weighted * values, axis=-1, keepdims=True)
    return (
        inv_rms * weighted - values * inv_rms * inv_rms * inv_rms * inner_mean,
        jnp.sum(upstream * values * inv_rms, axis=0),
    )


def swiglu(pre_act, split_at):
    return jax.nn.silu(pre_act[..., :split_at]) * pre_act[..., split_at:]


def swiglu_back(pre_act, split_at, upstream):
    gate_part = pre_act[..., :split_at]
    up_part = pre_act[..., split_at:]
    sigmoid_g = jax.nn.sigmoid(gate_part)
    d_gate = upstream * up_part * sigmoid_g * (1.0 + gate_part * (1.0 - sigmoid_g))
    d_up = upstream * gate_part * sigmoid_g
    return jnp.concatenate([d_gate, d_up], axis=-1)


def ring_order(size):
    return list(range(0, size, 2)) + list(range(size - 1, 0, -2))


def ring_steps(size):
    order = ring_order(size)
    ahead = [(order[i], order[(i + 1) % size]) for i in range(size)]
    back = [(dst, src) for src, dst in ahead]
    return (ahead, back)


def ring_peers(size, ctx_index):
    order = ring_order(size)
    place = {dev: i for i, dev in enumerate(order)}
    table = jnp.array(
        [[order[(place[dev] + k) % size] for k in range(size)] for dev in range(size)], jnp.int32
    )
    row = lax.dynamic_index_in_dim(table, ctx_index, 0, keepdims=False)
    return [row[k] for k in range(size)]


def after(value, *deps):
    return lax.optimization_barrier((value,) + deps)


def ring_gather(block, size, ctx_index, rider=None):
    rows, width = block.shape

    def put(out, piece, peer, offset):
        return lax.dynamic_update_slice(out, piece, (peer * rows + offset, jnp.zeros_like(peer)))

    out = jnp.zeros((size * rows, width), block.dtype)
    ahead, back = ring_steps(size)
    peers = ring_peers(size, ctx_index)
    half = size // 2
    out = put(out, block, ctx_index, 0)
    fore = rear = block
    for k in range(1, half):
        fore = lax.ppermute(fore, "ctx", ahead)
        rear = lax.ppermute(rear, "ctx", back)
        if rider is not None and k == 2:
            fore, rider = after(fore, rider)
        out = put(out, fore, peers[size - k], 0)
        out = put(out, rear, peers[k], 0)
    fore = lax.ppermute(fore[: rows // 2], "ctx", ahead)
    rear = lax.ppermute(rear[rows // 2 :], "ctx", back)
    out = put(out, fore, peers[half], 0)
    out = put(out, rear, peers[half], rows // 2)
    return out if rider is None else (out, rider)


def ring_sums(parts, size, ctx_index, riders):
    f32 = jnp.float32
    rows = parts.shape[0] // size
    ahead, back = ring_steps(size)
    peers = ring_peers(size, ctx_index)
    half = size // 2

    def own(k, start, count):
        first = (peers[k % size] * rows + start, jnp.zeros_like(peers[0]))
        return lax.dynamic_slice(parts, first, (count, parts.shape[1])).astype(f32)

    def low(values):
        return values.astype(jnp.bfloat16)

    cut = rows // 2
    fore = lax.ppermute(low(own(half, 0, cut)), "ctx", ahead)
    rear = lax.ppermute(low(own(half, cut, cut)), "ctx", back)
    fore = jnp.concatenate(
        [low(fore.astype(f32) + own(half - 1, 0, cut)), low(own(half - 1, cut, cut))], axis=0
    )
    rear = jnp.concatenate(
        [low(own(1 - half, 0, cut)), low(rear.astype(f32) + own(1 - half, cut, cut))], axis=0
    )
    for k in range(half - 1, 0, -1):
        fore = lax.ppermute(fore, "ctx", ahead)
        rear = lax.ppermute(rear, "ctx", back)
        if riders and k == half - 1:
            fore, *riders = after(fore, *riders)
        if k > 1:
            fore = low(fore.astype(f32) + own(k - 1, 0, rows))
            rear = low(rear.astype(f32) + own(1 - k, 0, rows))
    return (fore, rear, riders)


def ring_scatter(parts, size, ctx_index, kept=None, riders=()):
    fore, rear, riders = ring_sums(parts, size, ctx_index, riders)
    kept = (parts if kept is None else kept).reshape(size, -1, parts.shape[1])
    kept = lax.dynamic_index_in_dim(kept, ctx_index, 0, keepdims=False)
    total = kept.astype(jnp.float32) + fore.astype(jnp.float32) + rear.astype(jnp.float32)
    return (total, *riders) if riders else total


def other_core(size):
    return [(i, i ^ 1) for i in range(size)]


def other_chip(size):
    return [(i, i ^ 2) for i in range(size)]


def fsdp_gather(shard, size, hold):
    index = lax.axis_index("fsdp")
    rows, width = shard.shape
    far = lax.ppermute(shard, "fsdp", other_chip(size))
    far, hold = after(far, hold)
    pair = jnp.where(
        index < 2, jnp.stack([shard, far], axis=0), jnp.stack([far, shard], axis=0)
    )
    near = lax.ppermute(pair, "fsdp", other_core(size))
    out = jnp.zeros((2, 2, rows, width), shard.dtype)
    out = lax.dynamic_update_index_in_dim(out, pair, index % 2, 1)
    out = lax.dynamic_update_index_in_dim(out, near, 1 - index % 2, 1)
    return (out.reshape(size * rows, width), hold)


def column_pieces(weight, groups, size, extra):
    rows = weight.shape[0]
    width = weight.shape[1] // (groups * size)
    pieces = weight.reshape(rows, groups, size, width).transpose(2, 0, 1, 3)
    pieces = pieces.reshape(size, rows, groups * width)
    if extra is not None:
        count = extra.shape[0]
        more = -(-count // (groups * width * 16)) * 16
        extra = jnp.pad(extra, (0, more * groups * width - count))
        extra = jnp.broadcast_to(
            extra.reshape(1, more, groups * width), (size, more, groups * width)
        )
        pieces = jnp.concatenate([pieces, extra], axis=1)
    return pieces


def merge_columns(pieces, groups, size):
    width = pieces.shape[2] // groups
    if width % 128 == 0:
        pieces = pieces.reshape(size, -1, groups, width).transpose(1, 2, 0, 3)
        return pieces.reshape(-1, groups * size * width).astype(jnp.float32)
    columns = [
        pieces[peer, :, group * width : (group + 1) * width]
        for group in range(groups)
        for peer in range(size)
    ]
    return jnp.concatenate(columns, axis=1).astype(jnp.float32)


def attention_back_kernel(
    q_ref, k_ref, v_ref, do_ref, lse_ref, key_ref, query_ref, dq_ref, dk_ref, dv_ref, *, rows
):
    f32, bf16 = jnp.float32, jnp.bfloat16
    scale = HD ** (-0.5)
    keys, values = k_ref[...], v_ref[...]
    key_pos, key_seg = key_ref[:, 0:1], key_ref[:, 1:2]

    def pair(a, b, dims):
        return lax.dot_general(a, b, (dims, ((), ())), preferred_element_type=f32)

    for start in range(0, q_ref.shape[0], rows):
        here = slice(start, start + rows)
        queries, upstream = q_ref[here, :], do_ref[here, :]
        allowed = (key_pos <= query_ref[0:1, here]) & (key_seg == query_ref[1:2, here])
        scores = jnp.where(allowed, pair(keys, queries, ((1,), (1,))) * scale, MASK_FILL)
        weights = jnp.exp(scores - lse_ref[0, :, here])
        grads = pair(values, upstream, ((1,), (1,)))
        delta = jnp.sum(weights * grads, axis=0, keepdims=True)
        grads = jnp.where(allowed, weights * (grads - delta), 0.0).astype(bf16)
        part_v = pair(weights.astype(bf16), upstream, ((1,), (0,)))
        part_k = pair(grads, queries, ((1,), (0,))) * scale
        if start == 0:
            dv_ref[...] = part_v
            dk_ref[...] = part_k
        else:
            dv_ref[...] += part_v
            dk_ref[...] += part_k
        dq_ref[here, :] = pair(grads, keys, ((0,), (0,))) * scale


def attention_back(queries, keys, values, upstream, log_total, positions, seg_rows):
    tokens, width = queries.shape
    heads = width // HD
    marks = jnp.stack([positions, seg_rows], axis=0)
    by_head = pl.BlockSpec((tokens, HD), lambda h: (0, h))
    return pl.pallas_call(
        functools.partial(attention_back_kernel, rows=min(256, tokens)),
        grid=(heads,),
        in_specs=[by_head] * 4
        + [
            pl.BlockSpec((1, 1, tokens), lambda h: (h, 0, 0)),
            pl.BlockSpec((tokens, 2), lambda h: (0, 0)),
            pl.BlockSpec((2, tokens), lambda h: (0, 0)),
        ],
        out_specs=[by_head] * 3,
        out_shape=[jax.ShapeDtypeStruct((tokens, width), jnp.float32)] * 3,
        compiler_params=pltpu.CompilerParams(vmem_limit_bytes=40 * 1024 * 1024),
        cost_estimate=pl.CostEstimate(
            flops=10 * tokens * tokens * width,
            bytes_accessed=20 * tokens * width,
            transcendentals=tokens * tokens * heads,
        ),
    )(queries, keys, values, upstream, log_total.reshape(heads, 1, tokens), marks.T, marks)


def local_split(
    ctx_size,
    fsdp_size,
    tokens,
    segments,
    routes,
    cotangent,
    w_qkv,
    b_qkv,
    w_out,
    gain_attn,
    gain_ffn,
    w_router,
    w_shared_gate,
    w_shared_in,
    w_shared_out,
    w_expert_in,
    w_expert_out,
):
    bf16, f32, i32 = jnp.bfloat16, jnp.float32, jnp.int32
    device_count = ctx_size * fsdp_size
    block_len = tokens.shape[2]
    width = tokens.shape[3]
    token_count = 2 * block_len
    top_count = routes.shape[3]
    seq_len = token_count * ctx_size
    ctx_index = lax.axis_index("ctx")
    expert_count = w_router.shape[1]
    capacity = token_count * top_count // expert_count
    own_heads = HEADS // ctx_size
    own_width = own_heads * HD
    fs_own = FS // ctx_size
    score_scale = HD ** (-0.5)

    def dot(a, b):
        return jnp.dot(a, b, preferred_element_type=f32)

    def dot_t(a, b):
        return lax.dot_general(a, b, (((1,), (1,)), ((), ())), preferred_element_type=f32)

    def t_dot(a, b):
        return lax.dot_general(a, b, (((0,), (0,)), ((), ())), preferred_element_type=f32)

    def own_rows(values):
        return lax.dynamic_index_in_dim(
            values.reshape((ctx_size, token_count) + values.shape[1:]), ctx_index, 0, keepdims=False
        )

    def sum_rows(grad):
        return lax.psum_scatter(grad.astype(bf16), "fsdp", scatter_dimension=0, tiled=True)

    shard = width // device_count
    small = [gain_attn, gain_ffn, w_shared_gate, w_router.reshape(-1), b_qkv]
    small_size = sum(piece.shape[0] for piece in small)
    small = jnp.concatenate(small + [routes.astype(bf16).reshape(-1)], axis=0)
    small_count = small.shape[0]
    own_tokens = tokens.reshape(token_count, width).astype(f32)
    own_scaled, inv_one = rms_norm(own_tokens, 1.0)
    scaled_rows = ring_gather(own_scaled.astype(bf16), ctx_size, ctx_index)
    pieces = column_pieces(w_qkv, 3, ctx_size, small)
    pieces = lax.all_to_all(pieces, "ctx", split_axis=0, concat_axis=0, tiled=True)
    shared_in = column_pieces(w_shared_in, 2, ctx_size, None)
    shared_in, scaled_rows = after(shared_in, scaled_rows)
    shared_in = lax.all_to_all(shared_in, "ctx", split_axis=0, concat_axis=0, tiled=True)
    pieces = lax.all_gather(pieces, "fsdp", axis=0, tiled=False).transpose(1, 0, 2, 3)
    qkv_weight = pieces[:, :, :shard].reshape(width, 3 * own_width)
    small = pieces[:, :, shard:].reshape(device_count, -1)[:, :small_count]
    attn_gain = small[:, :shard].reshape(width).astype(f32)
    ffn_gain = small[:, shard : 2 * shard].reshape(width).astype(f32)
    gate_vector = small[:, 2 * shard : 3 * shard].reshape(width)
    router_end = 3 * shard + shard * expert_count
    router_weight = small[:, 3 * shard : router_end].reshape(width, expert_count)
    bias = small[:, router_end:small_size].reshape(3, ctx_size, own_width).astype(f32)
    bias = lax.dynamic_index_in_dim(bias, ctx_index, 1, keepdims=False).reshape(3 * own_width)
    route_rows = small[:, small_size:].astype(i32)
    route_rows = lax.dynamic_index_in_dim(
        route_rows.reshape(ctx_size, fsdp_size, -1), lax.axis_index("fsdp"), 1, keepdims=False
    ).reshape(ctx_size, token_count, top_count)

    expert_in = lax.all_gather(w_expert_in[0], "fsdp", axis=0, tiled=True)

    block_ids = jnp.arange(ctx_size, dtype=i32)[:, None]
    local_index = jnp.arange(block_len, dtype=i32)[None, :]
    positions = jnp.stack(
        [
            block_ids * block_len + local_index,
            seq_len - (block_ids + 1) * block_len + local_index,
        ],
        axis=1,
    ).reshape(seq_len)
    seg_rows = (
        segments.reshape(2, ctx_size, block_len).transpose(1, 0, 2).reshape(seq_len)
    )
    cos_tab, sine_tab = rope_tables(positions, HD)

    normed_low = (scaled_rows.astype(f32) * attn_gain).astype(bf16)
    projected = dot(normed_low, qkv_weight) + bias
    head_shape = (seq_len, own_heads, HD)
    queries = rotate(projected[:, :own_width].reshape(head_shape), cos_tab, sine_tab).astype(bf16)
    keys = rotate(
        projected[:, own_width : 2 * own_width].reshape(head_shape), cos_tab, sine_tab
    ).astype(bf16)
    values = projected[:, 2 * own_width :].reshape(head_shape).astype(bf16)
    out_weight, queries = fsdp_gather(w_out, fsdp_size, queries)
    allowed = (positions[None, :] <= positions[:, None]) & (seg_rows[None, :] == seg_rows[:, None])
    scores = jnp.einsum("qhd,khd->hqk", queries, keys, preferred_element_type=f32) * score_scale
    scores = jnp.where(allowed[None], scores, MASK_FILL)
    top_score = jnp.max(scores, axis=-1, keepdims=True)
    log_total = top_score + jnp.log(jnp.sum(jnp.exp(scores - top_score), axis=-1, keepdims=True))
    weights = jnp.exp(scores - log_total)
    weights_low = weights.astype(bf16)
    attended = jnp.einsum("hqk,khd->qhd", weights_low, values, preferred_element_type=f32)
    attn_own = attended.astype(bf16).reshape(seq_len, own_width)
    shared_out, attn_own = fsdp_gather(w_shared_out, fsdp_size, attn_own)
    expert_out, attn_own = fsdp_gather(w_expert_out[0], fsdp_size, attn_own)
    attn_parts, shared_in = after(dot(attn_own, out_weight).astype(bf16), shared_in)
    shared_in = lax.all_gather(shared_in, "fsdp", axis=0, tiled=False)
    own_residual = own_tokens + ring_scatter(attn_parts, ctx_size, ctx_index)

    normed_two, inv_two = rms_norm(own_residual, ffn_gain)
    own_low = normed_two.astype(bf16)
    low_two, grad_rows = ring_gather(
        own_low, ctx_size, ctx_index, cotangent.reshape(token_count, width)
    )
    grad_rows = lax.all_gather(grad_rows, "ctx", axis=0, tiled=True)
    mixed_weight = jnp.concatenate([router_weight, gate_vector[:, None]], axis=1)
    logits = dot(low_two, mixed_weight)
    probs_all = jax.nn.softmax(logits[:, :expert_count], axis=-1)
    scale_all = jax.nn.sigmoid(logits[:, expert_count])
    gate_all = lax.dynamic_index_in_dim(probs_all, ctx_index, 1, keepdims=False)

    named = jnp.any(route_rows == ctx_index, axis=-1)
    before = jnp.arange(token_count)[:, None] < jnp.arange(token_count)[None, :]
    rank = dot(named.astype(bf16), before.astype(bf16)).astype(i32)
    slot_of = jnp.where(named & (rank < capacity), rank, -1)
    slot_mask = slot_of[:, None, :] == jnp.arange(capacity, dtype=i32)[None, :, None]
    slot_map = slot_mask.astype(bf16)
    blocks_two = low_two.reshape(ctx_size, token_count, width)
    gate_blocks = gate_all.reshape(ctx_size, token_count)

    def to_slots(blocks):
        picked = jnp.einsum("bmt,btd->bmd", slot_map, blocks, preferred_element_type=f32)
        return picked.reshape(ctx_size * capacity, width)

    def to_tokens(slots):
        spread = jnp.einsum(
            "bmt,bmd->btd",
            slot_map,
            slots.reshape(ctx_size, capacity, width),
            preferred_element_type=f32,
        )
        return spread.reshape(seq_len, width)

    buffer = to_slots(blocks_two).astype(bf16)
    expert_pre = dot(buffer, expert_in)
    expert_hid = swiglu(expert_pre, FE).astype(bf16)
    expert_res = dot(expert_hid, expert_out).astype(bf16)
    routed = gate_all[:, None] * to_tokens(expert_res)

    shared_in, expert_res = after(shared_in, expert_res)
    shared_in = shared_in.transpose(1, 0, 2, 3).reshape(width, 2 * fs_own)
    shared_pre = dot(low_two, shared_in)
    shared_hid = swiglu(shared_pre, fs_own).astype(bf16)
    shared_res = dot(shared_hid, shared_out)
    out_parts = (scale_all[:, None] * shared_res + routed).astype(bf16)
    grad_rows, out_parts = after(grad_rows, out_parts)

    grad_slots = to_slots(grad_rows.reshape(ctx_size, token_count, width))
    gate_slots = jnp.sum(jnp.where(slot_mask, gate_blocks[:, None, :], 0.0), axis=-1).reshape(-1, 1)
    grad_res = (gate_slots * grad_slots).astype(bf16)
    grad_hid = dot_t(grad_res, expert_out)
    slot_terms = jnp.sum(expert_hid.astype(f32) * grad_hid, axis=-1)
    slot_terms = slot_terms.reshape(ctx_size, capacity, 1)
    gate_terms = jnp.sum(jnp.where(slot_mask, slot_terms, 0.0), axis=1)
    grad_pre = swiglu_back(expert_pre, FE, grad_hid).astype(bf16)
    grad_expert_in = t_dot(buffer, grad_pre)
    grad_buffer = dot_t(grad_pre, expert_in).astype(bf16)

    grad_f32 = grad_rows.astype(f32)
    grad_expert_in, grad_shared_res = after(
        grad_expert_in.astype(bf16), (scale_all[:, None] * grad_f32).astype(bf16)
    )
    sum_expert_in = sum_rows(grad_expert_in)

    grad_shared_hid = dot_t(grad_shared_res, shared_out)
    scale_terms = jnp.sum(shared_hid.astype(f32) * grad_shared_hid, axis=-1)
    grad_shared_pre = swiglu_back(shared_pre, fs_own, grad_shared_hid).astype(bf16)
    two_parts = (dot_t(grad_shared_pre, shared_in) + to_tokens(grad_buffer)).astype(bf16)
    two_parts, expert_hid, shared_hid, grad_shared_pre = after(
        two_parts, expert_hid, shared_hid, grad_shared_pre
    )
    grad_expert_out = t_dot(expert_hid, grad_res).astype(bf16)
    grad_shared_out = t_dot(shared_hid, grad_shared_res).astype(bf16)
    grad_shared_in = t_dot(low_two, grad_shared_pre).astype(bf16)
    grad_two = ring_scatter(two_parts, ctx_size, ctx_index)
    dots = jnp.stack([gate_terms, scale_terms.reshape(ctx_size, token_count)], axis=1)
    dots = lax.all_to_all(dots, "ctx", split_axis=0, concat_axis=0, tiled=True)
    grad_two, grad_shared_in, grad_shared_out, grad_expert_out, dots = after(
        grad_two, grad_shared_in, grad_shared_out, grad_expert_out, dots
    )
    sum_shared_in = grad_shared_in.reshape(ctx_size, fsdp_size, shard, 2 * fs_own)
    sum_shared_in = lax.psum_scatter(
        sum_shared_in.transpose(1, 0, 2, 3).reshape(width, 2 * fs_own),
        "fsdp",
        scatter_dimension=0,
        tiled=True,
    ).reshape(ctx_size, shard, 2 * fs_own)
    sum_expert_out = sum_rows(grad_expert_out)
    own_probs = own_rows(probs_all)
    own_scale = own_rows(scale_all)
    own_chosen = routes.reshape(token_count, top_count)
    chosen_mask = jnp.any(
        own_chosen[..., None] == jnp.arange(expert_count, dtype=i32), axis=1
    )
    prob_terms = jnp.where(chosen_mask, dots[:, 0].T, 0.0)
    grad_logits = (
        prob_terms - own_probs * jnp.sum(prob_terms, axis=-1, keepdims=True)
    ).astype(bf16)
    grad_gate_pre = (jnp.sum(dots[:, 1], axis=0) * (1.0 - own_scale)).astype(bf16)
    grad_router = t_dot(own_low, grad_logits)
    grad_gate_vector = t_dot(own_low, grad_gate_pre[:, None])
    grad_two = grad_two + dot_t(grad_logits, router_weight)
    grad_two = grad_two + grad_gate_pre.astype(f32)[:, None] * gate_vector.astype(f32)[None, :]
    grad_resid_norm, grad_gain_two = rms_back(
        own_residual, inv_two, ffn_gain, grad_two
    )
    grad_resid = cotangent.reshape(token_count, width).astype(f32) + grad_resid_norm

    grad_mixed, sum_expert_in = after(grad_resid.astype(bf16), sum_expert_in)
    mixed_all = ring_gather(grad_mixed, ctx_size, ctx_index)
    grad_attn = dot_t(mixed_all, out_weight).astype(bf16)
    grad_attn, sum_shared_in = after(grad_attn, sum_shared_in)
    sum_shared_in = lax.all_to_all(
        sum_shared_in, "ctx", split_axis=0, concat_axis=0, tiled=True
    )
    grad_q, grad_k, grad_v = attention_back(
        queries.reshape(seq_len, own_width),
        keys.reshape(seq_len, own_width),
        values.reshape(seq_len, own_width),
        grad_attn,
        log_total,
        positions,
        seg_rows,
    )
    grad_projected = jnp.concatenate(
        [
            rotate_back(grad_q.reshape(head_shape), cos_tab, sine_tab).reshape(seq_len, own_width),
            rotate_back(grad_k.reshape(head_shape), cos_tab, sine_tab).reshape(seq_len, own_width),
            grad_v,
        ],
        axis=-1,
    ).astype(bf16)
    one_sums = dot_t(grad_projected, qkv_weight)
    grad_gain_one = jnp.sum(one_sums * scaled_rows.astype(f32), axis=0)
    one_parts = one_sums.astype(bf16)
    one_kept, grad_projected = after(one_parts, grad_projected)
    one_kept, attn_own = after(one_kept, attn_own)
    one_parts, sum_shared_in = after(one_parts, sum_shared_in)
    grad_normed, sum_expert_out = ring_scatter(
        one_parts, ctx_size, ctx_index, one_kept, (sum_expert_out,)
    )
    grad_qkv_weight = t_dot(normed_low, grad_projected)
    grad_bias = jnp.sum(grad_projected.astype(f32), axis=0).reshape(3, 1, own_width)
    grad_bias = jnp.where(
        jnp.arange(ctx_size, dtype=i32)[None, :, None] == ctx_index, grad_bias, 0.0
    )

    grad_out_weight = t_dot(attn_own, mixed_all)
    small_grads = [grad_gain_one, grad_gain_two, grad_gate_vector, grad_router, grad_bias]
    small_grads = jnp.concatenate(
        [piece.reshape(device_count, -1) for piece in small_grads], axis=1
    )
    more = -(-small_size // (3 * own_width * 16)) * 16
    small_grads = jnp.pad(small_grads, ((0, 0), (0, more * 3 * own_width - small_size)))
    pieces = jnp.concatenate(
        [
            grad_qkv_weight.astype(bf16).reshape(ctx_size, fsdp_size, shard, 3 * own_width),
            small_grads.astype(bf16).reshape(ctx_size, fsdp_size, more, 3 * own_width),
        ],
        axis=2,
    )
    pieces = pieces.transpose(1, 0, 2, 3).reshape(-1, 3 * own_width)
    pieces = lax.psum_scatter(pieces, "fsdp", scatter_dimension=0, tiled=True)
    grad_normed, pieces, out_parts, grad_shared_out, grad_out_weight = after(
        grad_normed, pieces, out_parts, grad_shared_out, grad_out_weight.astype(bf16)
    )
    sum_shared_out = sum_rows(grad_shared_out)
    sum_out_weight = sum_rows(grad_out_weight)
    output = own_residual + ring_scatter(out_parts, ctx_size, ctx_index)
    output = output.astype(bf16).reshape(tokens.shape)
    pieces = pieces.reshape(ctx_size, shard + more, 3 * own_width)
    pieces = lax.all_to_all(pieces, "ctx", split_axis=0, concat_axis=0, tiled=True)
    grad_inputs_norm, unused = rms_back(
        own_tokens,
        inv_one,
        attn_gain,
        grad_normed,
    )
    grad_tokens = (grad_resid + grad_inputs_norm).reshape(tokens.shape)
    small_grads = jnp.sum(pieces[:, shard:].reshape(ctx_size, -1).astype(f32), axis=0)
    return (
        output,
        grad_tokens,
        merge_columns(pieces[:, :shard], 3, ctx_size),
        small_grads[router_end:small_size],
        sum_out_weight.astype(f32),
        small_grads[:shard],
        small_grads[shard : 2 * shard],
        small_grads[3 * shard : router_end].reshape(shard, expert_count),
        small_grads[2 * shard : 3 * shard],
        merge_columns(sum_shared_in, 2, ctx_size),
        sum_shared_out.astype(f32),
        sum_expert_in.astype(f32)[None],
        sum_expert_out.astype(f32)[None],
    )


def local_wide(
    tokens,
    segments,
    routes,
    cotangent,
    w_qkv,
    b_qkv,
    w_out,
    gain_attn,
    gain_ffn,
    w_router,
    w_shared_gate,
    w_shared_in,
    w_shared_out,
    w_expert_in,
    w_expert_out,
):
    block_len = tokens.shape[2]
    model_width = tokens.shape[3]
    token_count = 2 * block_len
    top_count = routes.shape[3]
    half_len = segments.shape[2]
    seq_len = 2 * half_len
    ctx_index = lax.axis_index("ctx")
    head_count = model_width // HD
    expert_count = w_router.shape[1]
    capacity = token_count * top_count // expert_count
    slot_count = expert_count * capacity
    key_rows = min(512, seq_len)
    key_blocks = seq_len // key_rows
    score_scale = HD ** (-0.5)
    head_shape = (token_count, head_count, HD)
    attn_set = (
        lax.all_gather(w_qkv, ("ctx", "fsdp"), axis=0, tiled=True),
        lax.all_gather(b_qkv, ("ctx", "fsdp"), axis=0, tiled=True),
        lax.all_gather(w_out, ("ctx", "fsdp"), axis=0, tiled=True),
        lax.all_gather(gain_attn, ("ctx", "fsdp"), axis=0, tiled=True),
    )
    qkv_weight, qkv_bias, out_weight, attn_gain = attn_set
    inputs = tokens.reshape(token_count, model_width).astype(jnp.float32)
    normed, inv_one = rms_norm(inputs, attn_gain.astype(jnp.float32))
    normed_low = normed.astype(jnp.bfloat16)
    projected = jnp.dot(
        normed_low, qkv_weight, preferred_element_type=jnp.float32
    ) + qkv_bias.astype(jnp.float32)
    local_index = jnp.arange(block_len, dtype=jnp.int32)
    query_pos = jnp.concatenate(
        [ctx_index * block_len + local_index, seq_len - (ctx_index + 1) * block_len + local_index]
    )
    half_index = jnp.arange(half_len, dtype=jnp.int32)
    key_pos = jnp.concatenate(
        [half_index, seq_len - block_len * (half_index // block_len + 1) + half_index % block_len]
    ).reshape(key_blocks, key_rows)
    key_seg = segments.reshape(key_blocks, key_rows)
    query_seg = lax.dynamic_slice_in_dim(segments[0], ctx_index * block_len, block_len, 1).reshape(
        token_count
    )
    cos_tab, sine_tab = rope_tables(query_pos, HD)
    queries = rotate(projected[:, :model_width].reshape(head_shape), cos_tab, sine_tab).astype(
        jnp.bfloat16
    )
    keys_own = rotate(
        projected[:, model_width : 2 * model_width].reshape(head_shape), cos_tab, sine_tab
    ).astype(jnp.bfloat16)
    values_own = projected[:, 2 * model_width :].astype(jnp.bfloat16)
    keys_all, values_all = (
        lax.all_gather(keys_own.reshape(2, block_len, model_width), "ctx", axis=1, tiled=True),
        lax.all_gather(values_own.reshape(2, block_len, model_width), "ctx", axis=1, tiled=True),
    )
    keys_all = keys_all.reshape(key_blocks, key_rows, head_count, HD)
    values_all = values_all.reshape(key_blocks, key_rows, head_count, HD)

    def score_block(key_blk, pos_blk, seg_blk):
        raw_scores = (
            jnp.einsum("qhd,khd->hqk", queries, key_blk, preferred_element_type=jnp.float32)
            * score_scale
        )
        allowed = (pos_blk[None, :] <= query_pos[:, None]) & (
            seg_blk[None, :] == query_seg[:, None]
        )
        return (jnp.where(allowed[None], raw_scores, MASK_FILL), allowed)

    def total_step(running, key_part):
        run_max, run_sum = running
        scores = score_block(key_part[0], key_part[1], key_part[2])[0]
        new_max = jnp.maximum(run_max, jnp.max(scores, axis=-1))
        run_sum = run_sum * jnp.exp(run_max - new_max) + jnp.sum(
            jnp.exp(scores - new_max[..., None]), axis=-1
        )
        return ((new_max, run_sum), None)

    start_max = jnp.full((head_count, token_count), MASK_FILL, jnp.float32)
    start_sum = jnp.zeros((head_count, token_count), jnp.float32)
    (run_max, run_sum), unused = lax.scan(
        total_step, (start_max, start_sum), (keys_all, key_pos, key_seg)
    )
    log_total = run_max + jnp.log(run_sum)

    def attend_step(summed, key_part):
        key_blk, value_blk, pos_blk, seg_blk = key_part
        scores = score_block(key_blk, pos_blk, seg_blk)[0]
        weights = jnp.exp(scores - log_total[..., None]).astype(jnp.bfloat16)
        return (
            summed
            + jnp.einsum("hqk,khd->qhd", weights, value_blk, preferred_element_type=jnp.float32),
            None,
        )

    key_stack = (keys_all, values_all, key_pos, key_seg)
    attended, unused = lax.scan(attend_step, jnp.zeros(head_shape, jnp.float32), key_stack)
    attn_low = attended.reshape(token_count, model_width).astype(jnp.bfloat16)
    residual = inputs + jnp.dot(attn_low, out_weight, preferred_element_type=jnp.float32)
    ffn_set = (
        lax.all_gather(gain_ffn, ("ctx", "fsdp"), axis=0, tiled=True),
        lax.all_gather(w_router, ("ctx", "fsdp"), axis=0, tiled=True),
        lax.all_gather(w_shared_gate, ("ctx", "fsdp"), axis=0, tiled=True),
        lax.all_gather(w_shared_in, ("ctx", "fsdp"), axis=0, tiled=True),
        lax.all_gather(w_shared_out, ("ctx", "fsdp"), axis=0, tiled=True),
    )
    ffn_gain, router_weight, gate_vector, shared_in, shared_out = ffn_set
    normed_two, inv_two = rms_norm(residual, ffn_gain.astype(jnp.float32))
    low_two = normed_two.astype(jnp.bfloat16)
    logits = jnp.dot(low_two, router_weight, preferred_element_type=jnp.float32)
    router_probs = jax.nn.softmax(logits, axis=-1)
    chosen = routes.reshape(token_count, top_count)
    chosen_mask = chosen[..., None] == jnp.arange(expert_count, dtype=jnp.int32)
    gate_vals = jnp.sum(jnp.where(chosen_mask, router_probs[:, None, :], 0.0), axis=-1)
    shared_scale = jax.nn.sigmoid(jnp.dot(low_two, gate_vector, preferred_element_type=jnp.float32))
    shared_pre = jnp.dot(low_two, shared_in, preferred_element_type=jnp.float32)
    shared_hid = swiglu(shared_pre, FS).astype(jnp.bfloat16)
    shared_res = jnp.dot(shared_hid, shared_out, preferred_element_type=jnp.float32)
    pair_routes = chosen.reshape(token_count * top_count)
    expert_marks = (
        pair_routes[:, None] == jnp.arange(expert_count, dtype=jnp.int32)[None, :]
    ).astype(jnp.int32)
    pair_ranks = jnp.sum((jnp.cumsum(expert_marks, axis=0) - expert_marks) * expert_marks, axis=1)
    pair_target = jnp.where(pair_ranks < capacity, pair_routes * capacity + pair_ranks, -1)
    pair_map = pair_target[:, None] == jnp.arange(slot_count, dtype=jnp.int32)[None, :]
    pair_low = pair_map.astype(jnp.bfloat16)
    token_map = jnp.sum(
        pair_map.reshape(token_count, top_count, slot_count).astype(jnp.int32), axis=1
    ).astype(jnp.bfloat16)
    outgoing = jnp.einsum(
        "tc,td->cd", token_map, low_two, preferred_element_type=jnp.float32
    ).astype(jnp.bfloat16)
    incoming = lax.all_to_all(
        outgoing.reshape(expert_count, capacity, model_width),
        "ctx",
        split_axis=0,
        concat_axis=1,
        tiled=True,
    )
    expert_in, expert_out = (
        lax.all_gather(w_expert_in, "fsdp", axis=1, tiled=True),
        lax.all_gather(w_expert_out, "fsdp", axis=1, tiled=True),
    )
    expert_pre = jnp.einsum("erd,edf->erf", incoming, expert_in, preferred_element_type=jnp.float32)
    expert_hid = swiglu(expert_pre, FE).astype(jnp.bfloat16)
    expert_res = jnp.einsum(
        "erf,efd->erd", expert_hid, expert_out, preferred_element_type=jnp.float32
    ).astype(jnp.bfloat16)
    returned = lax.all_to_all(expert_res, "ctx", split_axis=1, concat_axis=0, tiled=True).reshape(
        slot_count, model_width
    )
    pair_vals = jnp.dot(pair_low, returned, preferred_element_type=jnp.float32).reshape(
        token_count, top_count, model_width
    )
    routed = jnp.sum(gate_vals[..., None] * pair_vals, axis=1)
    output = (
        (residual + shared_scale[:, None] * shared_res + routed)
        .astype(jnp.bfloat16)
        .reshape(tokens.shape)
    )
    grad_out = cotangent.reshape(token_count, model_width).astype(jnp.float32)
    pair_grads = gate_vals[..., None] * grad_out[:, None, :]
    grad_gates = jnp.sum(grad_out[:, None, :] * pair_vals, axis=-1)
    grad_returned = jnp.einsum(
        "pc,pd->cd",
        pair_map.astype(jnp.float32),
        pair_grads.reshape(token_count * top_count, model_width),
        precision=HIGHEST,
    ).astype(jnp.bfloat16)
    grad_res = lax.all_to_all(
        grad_returned.reshape(expert_count, capacity, model_width),
        "ctx",
        split_axis=0,
        concat_axis=1,
        tiled=True,
    )
    grad_expert_out = jnp.einsum(
        "erf,erd->efd", expert_hid, grad_res, preferred_element_type=jnp.float32
    )
    grad_hid = jnp.einsum("erd,efd->erf", grad_res, expert_out, preferred_element_type=jnp.float32)
    grad_pre = swiglu_back(expert_pre, FE, grad_hid).astype(jnp.bfloat16)
    grad_expert_in = jnp.einsum(
        "erd,erf->edf", incoming, grad_pre, preferred_element_type=jnp.float32
    )
    grad_incoming = jnp.einsum(
        "erf,edf->erd", grad_pre, expert_in, preferred_element_type=jnp.float32
    ).astype(jnp.bfloat16)
    grad_outgoing = lax.all_to_all(
        grad_incoming, "ctx", split_axis=1, concat_axis=0, tiled=True
    ).reshape(slot_count, model_width)
    expert_grads = (
        lax.psum_scatter(
            grad_expert_in.astype(jnp.bfloat16), "fsdp", scatter_dimension=1, tiled=True
        ).astype(jnp.float32),
        lax.psum_scatter(
            grad_expert_out.astype(jnp.bfloat16), "fsdp", scatter_dimension=1, tiled=True
        ).astype(jnp.float32),
    )
    grad_two = jnp.einsum("tc,cd->td", token_map, grad_outgoing, preferred_element_type=jnp.float32)
    grad_probs = jnp.sum(jnp.where(chosen_mask, grad_gates[..., None], 0.0), axis=1)
    grad_logits = (
        router_probs * (grad_probs - jnp.sum(router_probs * grad_probs, axis=-1, keepdims=True))
    ).astype(jnp.bfloat16)
    grad_router = jnp.einsum("td,te->de", low_two, grad_logits, preferred_element_type=jnp.float32)
    grad_shared_res = (shared_scale[:, None] * grad_out).astype(jnp.bfloat16)
    grad_gate_pre = (
        jnp.sum(grad_out * shared_res, axis=-1) * shared_scale * (1.0 - shared_scale)
    ).astype(jnp.bfloat16)
    grad_shared_out = jnp.einsum(
        "tf,td->fd", shared_hid, grad_shared_res, preferred_element_type=jnp.float32
    )
    grad_shared_hid = jnp.einsum(
        "td,fd->tf", grad_shared_res, shared_out, preferred_element_type=jnp.float32
    )
    grad_shared_pre = swiglu_back(shared_pre, FS, grad_shared_hid).astype(jnp.bfloat16)
    grad_shared_in = jnp.einsum(
        "td,tf->df", low_two, grad_shared_pre, preferred_element_type=jnp.float32
    )
    grad_gate_vector = jnp.einsum(
        "td,t->d", low_two, grad_gate_pre, preferred_element_type=jnp.float32
    )
    grad_two = grad_two + jnp.einsum(
        "te,de->td", grad_logits, router_weight, preferred_element_type=jnp.float32
    )
    grad_two = grad_two + jnp.einsum(
        "tf,df->td", grad_shared_pre, shared_in, preferred_element_type=jnp.float32
    )
    grad_two = (
        grad_two
        + grad_gate_pre.astype(jnp.float32)[:, None] * gate_vector.astype(jnp.float32)[None, :]
    )
    grad_resid_norm, grad_gain_two = rms_back(
        residual, inv_two, ffn_gain.astype(jnp.float32), grad_two
    )
    grad_resid = grad_out + grad_resid_norm
    ffn_grads = (
        lax.psum_scatter(grad_gain_two, ("ctx", "fsdp"), scatter_dimension=0, tiled=True),
        lax.psum_scatter(grad_router, ("ctx", "fsdp"), scatter_dimension=0, tiled=True),
        lax.psum_scatter(grad_gate_vector, ("ctx", "fsdp"), scatter_dimension=0, tiled=True),
        lax.psum_scatter(grad_shared_in, ("ctx", "fsdp"), scatter_dimension=0, tiled=True),
        lax.psum_scatter(grad_shared_out, ("ctx", "fsdp"), scatter_dimension=0, tiled=True),
    )
    grad_mixed = grad_resid.astype(jnp.bfloat16)
    grad_out_weight = jnp.einsum(
        "tc,td->cd", attn_low, grad_mixed, preferred_element_type=jnp.float32
    )
    grad_attn = (
        jnp.einsum("td,cd->tc", grad_mixed, out_weight, preferred_element_type=jnp.float32)
        .astype(jnp.bfloat16)
        .reshape(head_shape)
    )

    def delta_step(summed, key_part):
        key_blk, value_blk, pos_blk, seg_blk = key_part
        weights = jnp.exp(score_block(key_blk, pos_blk, seg_blk)[0] - log_total[..., None])
        grad_weights = jnp.einsum(
            "qhd,khd->hqk", grad_attn, value_blk, preferred_element_type=jnp.float32
        )
        return (summed + jnp.sum(weights * grad_weights, axis=-1), None)

    delta_sum, unused = lax.scan(
        delta_step, jnp.zeros((head_count, token_count), jnp.float32), key_stack
    )

    def grad_step(summed, key_part):
        key_blk, value_blk, pos_blk, seg_blk = key_part
        scores, allowed = score_block(key_blk, pos_blk, seg_blk)
        weights = jnp.exp(scores - log_total[..., None])
        grad_weights = jnp.einsum(
            "qhd,khd->hqk", grad_attn, value_blk, preferred_element_type=jnp.float32
        )
        grad_scores = jnp.where(
            allowed[None], weights * (grad_weights - delta_sum[..., None]), 0.0
        ).astype(jnp.bfloat16)
        summed = (
            summed
            + jnp.einsum("hqk,khd->qhd", grad_scores, key_blk, preferred_element_type=jnp.float32)
            * score_scale
        )
        grad_key = (
            jnp.einsum("hqk,qhd->khd", grad_scores, queries, preferred_element_type=jnp.float32)
            * score_scale
        )
        grad_value = jnp.einsum(
            "hqk,qhd->khd",
            weights.astype(jnp.bfloat16),
            grad_attn,
            preferred_element_type=jnp.float32,
        )
        return (summed, (grad_key, grad_value))

    grad_query, (grad_keys, grad_values) = lax.scan(
        grad_step, jnp.zeros(head_shape, jnp.float32), key_stack
    )
    grad_keys_own, grad_values_own = (
        lax.psum_scatter(
            grad_keys.reshape(2, half_len, model_width).astype(jnp.bfloat16),
            "ctx",
            scatter_dimension=1,
            tiled=True,
        ).astype(jnp.float32),
        lax.psum_scatter(
            grad_values.reshape(2, half_len, model_width).astype(jnp.bfloat16),
            "ctx",
            scatter_dimension=1,
            tiled=True,
        ).astype(jnp.float32),
    )
    grad_q_rows = rotate_back(grad_query, cos_tab, sine_tab).reshape(token_count, model_width)
    grad_k_rows = rotate_back(grad_keys_own.reshape(head_shape), cos_tab, sine_tab).reshape(
        token_count, model_width
    )
    grad_projected = jnp.concatenate(
        [grad_q_rows, grad_k_rows, grad_values_own.reshape(token_count, model_width)], axis=-1
    ).astype(jnp.bfloat16)
    grad_qkv_weight = jnp.einsum(
        "td,te->de", normed_low, grad_projected, preferred_element_type=jnp.float32
    )
    grad_qkv_bias = jnp.sum(grad_projected.astype(jnp.float32), axis=0)
    grad_normed = jnp.einsum(
        "te,de->td", grad_projected, qkv_weight, preferred_element_type=jnp.float32
    )
    grad_inputs_norm, grad_gain_one = rms_back(
        inputs, inv_one, attn_gain.astype(jnp.float32), grad_normed
    )
    grad_tokens = (grad_resid + grad_inputs_norm).reshape(tokens.shape)
    attn_grads = (
        lax.psum_scatter(grad_qkv_weight, ("ctx", "fsdp"), scatter_dimension=0, tiled=True),
        lax.psum_scatter(grad_qkv_bias, ("ctx", "fsdp"), scatter_dimension=0, tiled=True),
        lax.psum_scatter(grad_out_weight, ("ctx", "fsdp"), scatter_dimension=0, tiled=True),
        lax.psum_scatter(grad_gain_one, ("ctx", "fsdp"), scatter_dimension=0, tiled=True),
    )
    return (
        output,
        grad_tokens,
        attn_grads[0],
        attn_grads[1],
        attn_grads[2],
        attn_grads[3],
        ffn_grads[0],
        ffn_grads[1],
        ffn_grads[2],
        ffn_grads[3],
        ffn_grads[4],
        expert_grads[0],
        expert_grads[1],
    )


def solution(mesh):
    in_specs = (
        P("fsdp", None, "ctx", None),
        P("fsdp", None, None),
        P("fsdp", None, "ctx", None),
        P("fsdp", None, "ctx", None),
        P(("ctx", "fsdp"), None),
        P(("ctx", "fsdp")),
        P(("ctx", "fsdp"), None),
        P(("ctx", "fsdp")),
        P(("ctx", "fsdp")),
        P(("ctx", "fsdp"), None),
        P(("ctx", "fsdp")),
        P(("ctx", "fsdp"), None),
        P(("ctx", "fsdp"), None),
        P("ctx", "fsdp", None),
        P("ctx", "fsdp", None),
    )
    out_specs = (
        P("fsdp", None, "ctx", None),
        P("fsdp", None, "ctx", None),
        P(("ctx", "fsdp"), None),
        P(("ctx", "fsdp")),
        P(("ctx", "fsdp"), None),
        P(("ctx", "fsdp")),
        P(("ctx", "fsdp")),
        P(("ctx", "fsdp"), None),
        P(("ctx", "fsdp")),
        P(("ctx", "fsdp"), None),
        P(("ctx", "fsdp"), None),
        P("ctx", "fsdp", None),
        P("ctx", "fsdp", None),
    )
    ctx_size = mesh.shape["ctx"]
    fsdp_size = mesh.shape["fsdp"]

    def local(*arrays):
        if HEADS % ctx_size:
            return local_wide(*arrays)
        return local_split(ctx_size, fsdp_size, *arrays)

    return jax.shard_map(local, mesh=mesh, in_specs=in_specs, out_specs=out_specs, check_vma=False)
```

```python
import functools

import jax
import jax.numpy as jnp
from jax import lax
from jax.experimental import pallas as pl
from jax.experimental.pallas import tpu as pltpu
from jax.sharding import PartitionSpec as P

HD = 128
HEADS = 16
FS = 5632
FE = 1408


RMS_EPS = 1e-06
ROPE_THETA = 1000000.0
MASK_FILL = -1e30
HIGHEST = lax.Precision.HIGHEST


def rope_tables(positions, head_dim):
    half_dim = head_dim // 2
    inv_freq = ROPE_THETA ** (-(jnp.arange(half_dim, dtype=jnp.float32) * 2.0 / head_dim))
    angles = positions.astype(jnp.float32)[:, None] * inv_freq[None, :]
    cos_tab = jnp.concatenate([jnp.cos(angles), jnp.cos(angles)], axis=-1)
    sine_tab = jnp.concatenate([jnp.sin(angles), jnp.sin(angles)], axis=-1)
    return (cos_tab, sine_tab)


def rotate(values, cos_tab, sine_tab):
    half_dim = values.shape[-1] // 2
    turned = jnp.concatenate([-values[..., half_dim:], values[..., :half_dim]], axis=-1)
    return values * cos_tab[:, None, :] + turned * sine_tab[:, None, :]


def rotate_back(upstream, cos_tab, sine_tab):
    half_dim = upstream.shape[-1] // 2
    scaled = upstream * sine_tab[:, None, :]
    return upstream * cos_tab[:, None, :] + jnp.concatenate(
        [scaled[..., half_dim:], -scaled[..., :half_dim]], axis=-1
    )


def rms_norm(values, gain_vec):
    inv_rms = lax.rsqrt(jnp.mean(values * values, axis=-1, keepdims=True) + RMS_EPS)
    return (values * inv_rms * gain_vec, inv_rms)


def rms_back(values, inv_rms, gain_vec, upstream):
    weighted = upstream * gain_vec
    inner_mean = jnp.mean(weighted * values, axis=-1, keepdims=True)
    return (
        inv_rms * weighted - values * inv_rms * inv_rms * inv_rms * inner_mean,
        jnp.sum(upstream * values * inv_rms, axis=0),
    )


def swiglu(pre_act, split_at):
    return jax.nn.silu(pre_act[..., :split_at]) * pre_act[..., split_at:]


def swiglu_back(pre_act, split_at, upstream):
    gate_part = pre_act[..., :split_at]
    up_part = pre_act[..., split_at:]
    sigmoid_g = jax.nn.sigmoid(gate_part)
    d_gate = upstream * up_part * sigmoid_g * (1.0 + gate_part * (1.0 - sigmoid_g))
    d_up = upstream * gate_part * sigmoid_g
    return jnp.concatenate([d_gate, d_up], axis=-1)


def ring_order(size):
    return list(range(0, size, 2)) + list(range(size - 1, 0, -2))


def ring_steps(size):
    order = ring_order(size)
    ahead = [(order[i], order[(i + 1) % size]) for i in range(size)]
    back = [(dst, src) for src, dst in ahead]
    return (ahead, back)


def ring_peers(size, ctx_index):
    order = ring_order(size)
    place = {dev: i for i, dev in enumerate(order)}
    table = jnp.array(
        [[order[(place[dev] + k) % size] for k in range(size)] for dev in range(size)], jnp.int32
    )
    row = lax.dynamic_index_in_dim(table, ctx_index, 0, keepdims=False)
    return [row[k] for k in range(size)]


def after(value, *deps):
    return lax.optimization_barrier((value,) + deps)


def ring_gather(block, size, ctx_index, rider=None):
    rows, width = block.shape

    def put(out, piece, peer, offset):
        return lax.dynamic_update_slice(out, piece, (peer * rows + offset, jnp.zeros_like(peer)))

    out = jnp.zeros((size * rows, width), block.dtype)
    ahead, back = ring_steps(size)
    peers = ring_peers(size, ctx_index)
    half = size // 2
    out = put(out, block, ctx_index, 0)
    fore = rear = block
    for k in range(1, half):
        fore = lax.ppermute(fore, "ctx", ahead)
        rear = lax.ppermute(rear, "ctx", back)
        if rider is not None and k == 2:
            fore, rider = after(fore, rider)
        out = put(out, fore, peers[size - k], 0)
        out = put(out, rear, peers[k], 0)
    fore = lax.ppermute(fore[: rows // 2], "ctx", ahead)
    rear = lax.ppermute(rear[rows // 2 :], "ctx", back)
    out = put(out, fore, peers[half], 0)
    out = put(out, rear, peers[half], rows // 2)
    return out if rider is None else (out, rider)


def ring_sums(parts, size, ctx_index, riders):
    f32 = jnp.float32
    rows = parts.shape[0] // size
    ahead, back = ring_steps(size)
    peers = ring_peers(size, ctx_index)
    half = size // 2

    def own(k, start, count):
        first = (peers[k % size] * rows + start, jnp.zeros_like(peers[0]))
        return lax.dynamic_slice(parts, first, (count, parts.shape[1])).astype(f32)

    def low(values):
        return values.astype(jnp.bfloat16)

    cut = rows // 2
    fore = lax.ppermute(low(own(half, 0, cut)), "ctx", ahead)
    rear = lax.ppermute(low(own(half, cut, cut)), "ctx", back)
    fore = jnp.concatenate(
        [low(fore.astype(f32) + own(half - 1, 0, cut)), low(own(half - 1, cut, cut))], axis=0
    )
    rear = jnp.concatenate(
        [low(own(1 - half, 0, cut)), low(rear.astype(f32) + own(1 - half, cut, cut))], axis=0
    )
    for k in range(half - 1, 0, -1):
        fore = lax.ppermute(fore, "ctx", ahead)
        rear = lax.ppermute(rear, "ctx", back)
        if riders and k == half - 1:
            fore, *riders = after(fore, *riders)
        if k > 1:
            fore = low(fore.astype(f32) + own(k - 1, 0, rows))
            rear = low(rear.astype(f32) + own(1 - k, 0, rows))
    return (fore, rear, riders)


def ring_scatter(parts, size, ctx_index, kept=None, riders=()):
    fore, rear, riders = ring_sums(parts, size, ctx_index, riders)
    kept = (parts if kept is None else kept).reshape(size, -1, parts.shape[1])
    kept = lax.dynamic_index_in_dim(kept, ctx_index, 0, keepdims=False)
    total = kept.astype(jnp.float32) + fore.astype(jnp.float32) + rear.astype(jnp.float32)
    return (total, *riders) if riders else total


def other_core(size):
    return [(i, i ^ 1) for i in range(size)]


def other_chip(size):
    return [(i, i ^ 2) for i in range(size)]


def fsdp_gather(shard, size, hold):
    index = lax.axis_index("fsdp")
    rows, width = shard.shape
    far = lax.ppermute(shard, "fsdp", other_chip(size))
    far, hold = after(far, hold)
    pair = jnp.where(
        index < 2, jnp.stack([shard, far], axis=0), jnp.stack([far, shard], axis=0)
    )
    near = lax.ppermute(pair, "fsdp", other_core(size))
    out = jnp.zeros((2, 2, rows, width), shard.dtype)
    out = lax.dynamic_update_index_in_dim(out, pair, index % 2, 1)
    out = lax.dynamic_update_index_in_dim(out, near, 1 - index % 2, 1)
    return (out.reshape(size * rows, width), hold)


def column_pieces(weight, groups, size, extra):
    rows = weight.shape[0]
    width = weight.shape[1] // (groups * size)
    pieces = weight.reshape(rows, groups, size, width).transpose(2, 0, 1, 3)
    pieces = pieces.reshape(size, rows, groups * width)
    if extra is not None:
        count = extra.shape[0]
        more = -(-count // (groups * width * 16)) * 16
        extra = jnp.pad(extra, (0, more * groups * width - count))
        extra = jnp.broadcast_to(
            extra.reshape(1, more, groups * width), (size, more, groups * width)
        )
        pieces = jnp.concatenate([pieces, extra], axis=1)
    return pieces


def merge_columns(pieces, groups, size):
    width = pieces.shape[2] // groups
    if width % 128 == 0:
        pieces = pieces.reshape(size, -1, groups, width).transpose(1, 2, 0, 3)
        return pieces.reshape(-1, groups * size * width).astype(jnp.float32)
    columns = [
        pieces[peer, :, group * width : (group + 1) * width]
        for group in range(groups)
        for peer in range(size)
    ]
    return jnp.concatenate(columns, axis=1).astype(jnp.float32)


def attention_back_kernel(
    q_ref, k_ref, v_ref, do_ref, lse_ref, key_ref, query_ref, dq_ref, dk_ref, dv_ref, *, rows
):
    f32, bf16 = jnp.float32, jnp.bfloat16
    scale = HD ** (-0.5)
    keys, values = k_ref[...], v_ref[...]
    key_pos, key_seg = key_ref[:, 0:1], key_ref[:, 1:2]

    def pair(a, b, dims):
        return lax.dot_general(a, b, (dims, ((), ())), preferred_element_type=f32)

    for start in range(0, q_ref.shape[0], rows):
        here = slice(start, start + rows)
        queries, upstream = q_ref[here, :], do_ref[here, :]
        allowed = (key_pos <= query_ref[0:1, here]) & (key_seg == query_ref[1:2, here])
        scores = jnp.where(allowed, pair(keys, queries, ((1,), (1,))) * scale, MASK_FILL)
        weights = jnp.exp(scores - lse_ref[0, :, here])
        grads = pair(values, upstream, ((1,), (1,)))
        delta = jnp.sum(weights * grads, axis=0, keepdims=True)
        grads = jnp.where(allowed, weights * (grads - delta), 0.0).astype(bf16)
        part_v = pair(weights.astype(bf16), upstream, ((1,), (0,)))
        part_k = pair(grads, queries, ((1,), (0,))) * scale
        if start == 0:
            dv_ref[...] = part_v
            dk_ref[...] = part_k
        else:
            dv_ref[...] += part_v
            dk_ref[...] += part_k
        dq_ref[here, :] = pair(grads, keys, ((0,), (0,))) * scale


def attention_back(queries, keys, values, upstream, log_total, positions, seg_rows):
    tokens, width = queries.shape
    heads = width // HD
    marks = jnp.stack([positions, seg_rows], axis=0)
    by_head = pl.BlockSpec((tokens, HD), lambda h: (0, h))
    return pl.pallas_call(
        functools.partial(attention_back_kernel, rows=min(256, tokens)),
        grid=(heads,),
        in_specs=[by_head] * 4
        + [
            pl.BlockSpec((1, 1, tokens), lambda h: (h, 0, 0)),
            pl.BlockSpec((tokens, 2), lambda h: (0, 0)),
            pl.BlockSpec((2, tokens), lambda h: (0, 0)),
        ],
        out_specs=[by_head] * 3,
        out_shape=[jax.ShapeDtypeStruct((tokens, width), jnp.float32)] * 3,
        compiler_params=pltpu.CompilerParams(vmem_limit_bytes=40 * 1024 * 1024),
        cost_estimate=pl.CostEstimate(
            flops=10 * tokens * tokens * width,
            bytes_accessed=20 * tokens * width,
            transcendentals=tokens * tokens * heads,
        ),
    )(queries, keys, values, upstream, log_total.reshape(heads, 1, tokens), marks.T, marks)


def local_split(
    ctx_size,
    fsdp_size,
    tokens,
    segments,
    routes,
    cotangent,
    w_qkv,
    b_qkv,
    w_out,
    gain_attn,
    gain_ffn,
    w_router,
    w_shared_gate,
    w_shared_in,
    w_shared_out,
    w_expert_in,
    w_expert_out,
):
    bf16, f32, i32 = jnp.bfloat16, jnp.float32, jnp.int32
    device_count = ctx_size * fsdp_size
    block_len = tokens.shape[2]
    width = tokens.shape[3]
    token_count = 2 * block_len
    top_count = routes.shape[3]
    seq_len = token_count * ctx_size
    ctx_index = lax.axis_index("ctx")
    expert_count = w_router.shape[1]
    capacity = token_count * top_count // expert_count
    own_heads = HEADS // ctx_size
    own_width = own_heads * HD
    fs_own = FS // ctx_size
    score_scale = HD ** (-0.5)

    def dot(a, b):
        return jnp.dot(a, b, preferred_element_type=f32)

    def dot_t(a, b):
        return lax.dot_general(a, b, (((1,), (1,)), ((), ())), preferred_element_type=f32)

    def t_dot(a, b):
        return lax.dot_general(a, b, (((0,), (0,)), ((), ())), preferred_element_type=f32)

    def own_rows(values):
        return lax.dynamic_index_in_dim(
            values.reshape((ctx_size, token_count) + values.shape[1:]), ctx_index, 0, keepdims=False
        )

    def sum_rows(grad):
        return lax.psum_scatter(grad.astype(bf16), "fsdp", scatter_dimension=0, tiled=True)

    shard = width // device_count
    small = [gain_attn, gain_ffn, w_shared_gate, w_router.reshape(-1), b_qkv]
    small_size = sum(piece.shape[0] for piece in small)
    small = jnp.concatenate(small + [routes.astype(bf16).reshape(-1)], axis=0)
    small_count = small.shape[0]
    own_tokens = tokens.reshape(token_count, width).astype(f32)
    own_scaled, inv_one = rms_norm(own_tokens, 1.0)
    scaled_rows = ring_gather(own_scaled.astype(bf16), ctx_size, ctx_index)
    pieces = column_pieces(w_qkv, 3, ctx_size, small)
    pieces = lax.all_to_all(pieces, "ctx", split_axis=0, concat_axis=0, tiled=True)
    shared_in = column_pieces(w_shared_in, 2, ctx_size, None)
    shared_in, scaled_rows = after(shared_in, scaled_rows)
    shared_in = lax.all_to_all(shared_in, "ctx", split_axis=0, concat_axis=0, tiled=True)
    pieces = lax.all_gather(pieces, "fsdp", axis=0, tiled=False).transpose(1, 0, 2, 3)
    qkv_weight = pieces[:, :, :shard].reshape(width, 3 * own_width)
    small = pieces[:, :, shard:].reshape(device_count, -1)[:, :small_count]
    attn_gain = small[:, :shard].reshape(width).astype(f32)
    ffn_gain = small[:, shard : 2 * shard].reshape(width).astype(f32)
    gate_vector = small[:, 2 * shard : 3 * shard].reshape(width)
    router_end = 3 * shard + shard * expert_count
    router_weight = small[:, 3 * shard : router_end].reshape(width, expert_count)
    bias = small[:, router_end:small_size].reshape(3, ctx_size, own_width).astype(f32)
    bias = lax.dynamic_index_in_dim(bias, ctx_index, 1, keepdims=False).reshape(3 * own_width)
    route_rows = small[:, small_size:].astype(i32)
    route_rows = lax.dynamic_index_in_dim(
        route_rows.reshape(ctx_size, fsdp_size, -1), lax.axis_index("fsdp"), 1, keepdims=False
    ).reshape(ctx_size, token_count, top_count)

    expert_in = lax.all_gather(w_expert_in[0], "fsdp", axis=0, tiled=True)

    block_ids = jnp.arange(ctx_size, dtype=i32)[:, None]
    local_index = jnp.arange(block_len, dtype=i32)[None, :]
    positions = jnp.stack(
        [
            block_ids * block_len + local_index,
            seq_len - (block_ids + 1) * block_len + local_index,
        ],
        axis=1,
    ).reshape(seq_len)
    seg_rows = (
        segments.reshape(2, ctx_size, block_len).transpose(1, 0, 2).reshape(seq_len)
    )
    cos_tab, sine_tab = rope_tables(positions, HD)

    normed_low = (scaled_rows.astype(f32) * attn_gain).astype(bf16)
    projected = dot(normed_low, qkv_weight) + bias
    head_shape = (seq_len, own_heads, HD)
    queries = rotate(projected[:, :own_width].reshape(head_shape), cos_tab, sine_tab).astype(bf16)
    keys = rotate(
        projected[:, own_width : 2 * own_width].reshape(head_shape), cos_tab, sine_tab
    ).astype(bf16)
    values = projected[:, 2 * own_width :].reshape(head_shape).astype(bf16)
    out_weight, queries = fsdp_gather(w_out, fsdp_size, queries)
    allowed = (positions[None, :] <= positions[:, None]) & (seg_rows[None, :] == seg_rows[:, None])
    scores = jnp.einsum("qhd,khd->hqk", queries, keys, preferred_element_type=f32) * score_scale
    scores = jnp.where(allowed[None], scores, MASK_FILL)
    top_score = jnp.max(scores, axis=-1, keepdims=True)
    log_total = top_score + jnp.log(jnp.sum(jnp.exp(scores - top_score), axis=-1, keepdims=True))
    weights = jnp.exp(scores - log_total)
    weights_low = weights.astype(bf16)
    attended = jnp.einsum("hqk,khd->qhd", weights_low, values, preferred_element_type=f32)
    attn_own = attended.astype(bf16).reshape(seq_len, own_width)
    shared_out, attn_own = fsdp_gather(w_shared_out, fsdp_size, attn_own)
    expert_out, attn_own = fsdp_gather(w_expert_out[0], fsdp_size, attn_own)
    attn_parts, shared_in = after(dot(attn_own, out_weight).astype(bf16), shared_in)
    shared_in = lax.all_gather(shared_in, "fsdp", axis=0, tiled=False)
    own_residual = own_tokens + ring_scatter(attn_parts, ctx_size, ctx_index)

    normed_two, inv_two = rms_norm(own_residual, ffn_gain)
    own_low = normed_two.astype(bf16)
    low_two, grad_rows = ring_gather(
        own_low, ctx_size, ctx_index, cotangent.reshape(token_count, width)
    )
    grad_rows = lax.all_gather(grad_rows, "ctx", axis=0, tiled=True)
    mixed_weight = jnp.concatenate([router_weight, gate_vector[:, None]], axis=1)
    logits = dot(low_two, mixed_weight)
    probs_all = jax.nn.softmax(logits[:, :expert_count], axis=-1)
    scale_all = jax.nn.sigmoid(logits[:, expert_count])
    gate_all = lax.dynamic_index_in_dim(probs_all, ctx_index, 1, keepdims=False)

    named = jnp.any(route_rows == ctx_index, axis=-1)
    before = jnp.arange(token_count)[:, None] < jnp.arange(token_count)[None, :]
    rank = dot(named.astype(bf16), before.astype(bf16)).astype(i32)
    slot_of = jnp.where(named & (rank < capacity), rank, -1)
    slot_mask = slot_of[:, None, :] == jnp.arange(capacity, dtype=i32)[None, :, None]
    slot_map = slot_mask.astype(bf16)
    blocks_two = low_two.reshape(ctx_size, token_count, width)
    gate_blocks = gate_all.reshape(ctx_size, token_count)

    def to_slots(blocks):
        picked = jnp.einsum("bmt,btd->bmd", slot_map, blocks, preferred_element_type=f32)
        return picked.reshape(ctx_size * capacity, width)

    def to_tokens(slots):
        spread = jnp.einsum(
            "bmt,bmd->btd",
            slot_map,
            slots.reshape(ctx_size, capacity, width),
            preferred_element_type=f32,
        )
        return spread.reshape(seq_len, width)

    buffer = to_slots(blocks_two).astype(bf16)
    expert_pre = dot(buffer, expert_in)
    expert_hid = swiglu(expert_pre, FE).astype(bf16)
    expert_res = dot(expert_hid, expert_out).astype(bf16)
    routed = gate_all[:, None] * to_tokens(expert_res)

    shared_in, expert_res = after(shared_in, expert_res)
    shared_in = shared_in.transpose(1, 0, 2, 3).reshape(width, 2 * fs_own)
    shared_pre = dot(low_two, shared_in)
    shared_hid = swiglu(shared_pre, fs_own).astype(bf16)
    shared_res = dot(shared_hid, shared_out)
    out_parts = (scale_all[:, None] * shared_res + routed).astype(bf16)
    grad_rows, out_parts = after(grad_rows, out_parts)

    grad_slots = to_slots(grad_rows.reshape(ctx_size, token_count, width))
    gate_slots = jnp.sum(jnp.where(slot_mask, gate_blocks[:, None, :], 0.0), axis=-1).reshape(-1, 1)
    grad_res = (gate_slots * grad_slots).astype(bf16)
    grad_hid = dot_t(grad_res, expert_out)
    slot_terms = jnp.sum(expert_hid.astype(f32) * grad_hid, axis=-1)
    slot_terms = slot_terms.reshape(ctx_size, capacity, 1)
    gate_terms = jnp.sum(jnp.where(slot_mask, slot_terms, 0.0), axis=1)
    grad_pre = swiglu_back(expert_pre, FE, grad_hid).astype(bf16)
    grad_expert_in = t_dot(buffer, grad_pre)
    grad_buffer = dot_t(grad_pre, expert_in).astype(bf16)

    grad_f32 = grad_rows.astype(f32)
    grad_expert_in, grad_shared_res = after(
        grad_expert_in.astype(bf16), (scale_all[:, None] * grad_f32).astype(bf16)
    )
    sum_expert_in = sum_rows(grad_expert_in)

    grad_shared_hid = dot_t(grad_shared_res, shared_out)
    scale_terms = jnp.sum(shared_hid.astype(f32) * grad_shared_hid, axis=-1)
    grad_shared_pre = swiglu_back(shared_pre, fs_own, grad_shared_hid).astype(bf16)
    two_parts = (dot_t(grad_shared_pre, shared_in) + to_tokens(grad_buffer)).astype(bf16)
    two_parts, expert_hid, shared_hid, grad_shared_pre = after(
        two_parts, expert_hid, shared_hid, grad_shared_pre
    )
    grad_expert_out = t_dot(expert_hid, grad_res).astype(bf16)
    grad_shared_out = t_dot(shared_hid, grad_shared_res).astype(bf16)
    grad_shared_in = t_dot(low_two, grad_shared_pre).astype(bf16)
    grad_two = ring_scatter(two_parts, ctx_size, ctx_index)
    dots = jnp.stack([gate_terms, scale_terms.reshape(ctx_size, token_count)], axis=1)
    dots = lax.all_to_all(dots, "ctx", split_axis=0, concat_axis=0, tiled=True)
    grad_two, grad_shared_in, grad_shared_out, grad_expert_out, dots = after(
        grad_two, grad_shared_in, grad_shared_out, grad_expert_out, dots
    )
    sum_shared_in = grad_shared_in.reshape(ctx_size, fsdp_size, shard, 2 * fs_own)
    sum_shared_in = lax.psum_scatter(
        sum_shared_in.transpose(1, 0, 2, 3).reshape(width, 2 * fs_own),
        "fsdp",
        scatter_dimension=0,
        tiled=True,
    ).reshape(ctx_size, shard, 2 * fs_own)
    sum_expert_out = sum_rows(grad_expert_out)
    own_probs = own_rows(probs_all)
    own_scale = own_rows(scale_all)
    own_chosen = routes.reshape(token_count, top_count)
    chosen_mask = jnp.any(
        own_chosen[..., None] == jnp.arange(expert_count, dtype=i32), axis=1
    )
    prob_terms = jnp.where(chosen_mask, dots[:, 0].T, 0.0)
    grad_logits = (
        prob_terms - own_probs * jnp.sum(prob_terms, axis=-1, keepdims=True)
    ).astype(bf16)
    grad_gate_pre = (jnp.sum(dots[:, 1], axis=0) * (1.0 - own_scale)).astype(bf16)
    grad_router = t_dot(own_low, grad_logits)
    grad_gate_vector = t_dot(own_low, grad_gate_pre[:, None])
    grad_two = grad_two + dot_t(grad_logits, router_weight)
    grad_two = grad_two + grad_gate_pre.astype(f32)[:, None] * gate_vector.astype(f32)[None, :]
    grad_resid_norm, grad_gain_two = rms_back(
        own_residual, inv_two, ffn_gain, grad_two
    )
    grad_resid = cotangent.reshape(token_count, width).astype(f32) + grad_resid_norm

    grad_mixed, sum_expert_in = after(grad_resid.astype(bf16), sum_expert_in)
    mixed_all = ring_gather(grad_mixed, ctx_size, ctx_index)
    grad_attn = dot_t(mixed_all, out_weight).astype(bf16)
    grad_attn, sum_shared_in = after(grad_attn, sum_shared_in)
    sum_shared_in = lax.all_to_all(
        sum_shared_in, "ctx", split_axis=0, concat_axis=0, tiled=True
    )
    grad_q, grad_k, grad_v = attention_back(
        queries.reshape(seq_len, own_width),
        keys.reshape(seq_len, own_width),
        values.reshape(seq_len, own_width),
        grad_attn,
        log_total,
        positions,
        seg_rows,
    )
    grad_projected = jnp.concatenate(
        [
            rotate_back(grad_q.reshape(head_shape), cos_tab, sine_tab).reshape(seq_len, own_width),
            rotate_back(grad_k.reshape(head_shape), cos_tab, sine_tab).reshape(seq_len, own_width),
            grad_v,
        ],
        axis=-1,
    ).astype(bf16)
    one_sums = dot_t(grad_projected, qkv_weight)
    grad_gain_one = jnp.sum(one_sums * scaled_rows.astype(f32), axis=0)
    one_parts, sum_shared_in = after(one_sums.astype(bf16), sum_shared_in)
    one_kept, grad_projected = after(one_parts, grad_projected)
    one_kept, attn_own = after(one_kept, attn_own)
    grad_normed, sum_expert_out = ring_scatter(
        one_parts, ctx_size, ctx_index, one_kept, (sum_expert_out,)
    )
    grad_qkv_weight = t_dot(normed_low, grad_projected)
    grad_bias = jnp.sum(grad_projected.astype(f32), axis=0).reshape(3, 1, own_width)
    grad_bias = jnp.where(
        jnp.arange(ctx_size, dtype=i32)[None, :, None] == ctx_index, grad_bias, 0.0
    )

    grad_out_weight = t_dot(attn_own, mixed_all)
    small_grads = [grad_gain_one, grad_gain_two, grad_gate_vector, grad_router, grad_bias]
    small_grads = jnp.concatenate(
        [piece.reshape(device_count, -1) for piece in small_grads], axis=1
    )
    more = -(-small_size // (3 * own_width * 16)) * 16
    small_grads = jnp.pad(small_grads, ((0, 0), (0, more * 3 * own_width - small_size)))
    pieces = jnp.concatenate(
        [
            grad_qkv_weight.astype(bf16).reshape(ctx_size, fsdp_size, shard, 3 * own_width),
            small_grads.astype(bf16).reshape(ctx_size, fsdp_size, more, 3 * own_width),
        ],
        axis=2,
    )
    pieces = pieces.transpose(1, 0, 2, 3).reshape(-1, 3 * own_width)
    pieces = lax.psum_scatter(pieces, "fsdp", scatter_dimension=0, tiled=True)
    grad_normed, pieces, out_parts, grad_shared_out, grad_out_weight = after(
        grad_normed, pieces, out_parts, grad_shared_out, grad_out_weight.astype(bf16)
    )
    sum_shared_out = sum_rows(grad_shared_out)
    sum_out_weight = sum_rows(grad_out_weight)
    output = own_residual + ring_scatter(out_parts, ctx_size, ctx_index)
    output = output.astype(bf16).reshape(tokens.shape)
    pieces = pieces.reshape(ctx_size, shard + more, 3 * own_width)
    pieces = lax.all_to_all(pieces, "ctx", split_axis=0, concat_axis=0, tiled=True)
    grad_inputs_norm, unused = rms_back(
        own_tokens,
        inv_one,
        attn_gain,
        grad_normed,
    )
    grad_tokens = (grad_resid + grad_inputs_norm).reshape(tokens.shape)
    small_grads = jnp.sum(pieces[:, shard:].reshape(ctx_size, -1).astype(f32), axis=0)
    return (
        output,
        grad_tokens,
        merge_columns(pieces[:, :shard], 3, ctx_size),
        small_grads[router_end:small_size],
        sum_out_weight.astype(f32),
        small_grads[:shard],
        small_grads[shard : 2 * shard],
        small_grads[3 * shard : router_end].reshape(shard, expert_count),
        small_grads[2 * shard : 3 * shard],
        merge_columns(sum_shared_in, 2, ctx_size),
        sum_shared_out.astype(f32),
        sum_expert_in.astype(f32)[None],
        sum_expert_out.astype(f32)[None],
    )


def local_wide(
    tokens,
    segments,
    routes,
    cotangent,
    w_qkv,
    b_qkv,
    w_out,
    gain_attn,
    gain_ffn,
    w_router,
    w_shared_gate,
    w_shared_in,
    w_shared_out,
    w_expert_in,
    w_expert_out,
):
    block_len = tokens.shape[2]
    model_width = tokens.shape[3]
    token_count = 2 * block_len
    top_count = routes.shape[3]
    half_len = segments.shape[2]
    seq_len = 2 * half_len
    ctx_index = lax.axis_index("ctx")
    head_count = model_width // HD
    expert_count = w_router.shape[1]
    capacity = token_count * top_count // expert_count
    slot_count = expert_count * capacity
    key_rows = min(512, seq_len)
    key_blocks = seq_len // key_rows
    score_scale = HD ** (-0.5)
    head_shape = (token_count, head_count, HD)
    attn_set = (
        lax.all_gather(w_qkv, ("ctx", "fsdp"), axis=0, tiled=True),
        lax.all_gather(b_qkv, ("ctx", "fsdp"), axis=0, tiled=True),
        lax.all_gather(w_out, ("ctx", "fsdp"), axis=0, tiled=True),
        lax.all_gather(gain_attn, ("ctx", "fsdp"), axis=0, tiled=True),
    )
    qkv_weight, qkv_bias, out_weight, attn_gain = attn_set
    inputs = tokens.reshape(token_count, model_width).astype(jnp.float32)
    normed, inv_one = rms_norm(inputs, attn_gain.astype(jnp.float32))
    normed_low = normed.astype(jnp.bfloat16)
    projected = jnp.dot(
        normed_low, qkv_weight, preferred_element_type=jnp.float32
    ) + qkv_bias.astype(jnp.float32)
    local_index = jnp.arange(block_len, dtype=jnp.int32)
    query_pos = jnp.concatenate(
        [ctx_index * block_len + local_index, seq_len - (ctx_index + 1) * block_len + local_index]
    )
    half_index = jnp.arange(half_len, dtype=jnp.int32)
    key_pos = jnp.concatenate(
        [half_index, seq_len - block_len * (half_index // block_len + 1) + half_index % block_len]
    ).reshape(key_blocks, key_rows)
    key_seg = segments.reshape(key_blocks, key_rows)
    query_seg = lax.dynamic_slice_in_dim(segments[0], ctx_index * block_len, block_len, 1).reshape(
        token_count
    )
    cos_tab, sine_tab = rope_tables(query_pos, HD)
    queries = rotate(projected[:, :model_width].reshape(head_shape), cos_tab, sine_tab).astype(
        jnp.bfloat16
    )
    keys_own = rotate(
        projected[:, model_width : 2 * model_width].reshape(head_shape), cos_tab, sine_tab
    ).astype(jnp.bfloat16)
    values_own = projected[:, 2 * model_width :].astype(jnp.bfloat16)
    keys_all, values_all = (
        lax.all_gather(keys_own.reshape(2, block_len, model_width), "ctx", axis=1, tiled=True),
        lax.all_gather(values_own.reshape(2, block_len, model_width), "ctx", axis=1, tiled=True),
    )
    keys_all = keys_all.reshape(key_blocks, key_rows, head_count, HD)
    values_all = values_all.reshape(key_blocks, key_rows, head_count, HD)

    def score_block(key_blk, pos_blk, seg_blk):
        raw_scores = (
            jnp.einsum("qhd,khd->hqk", queries, key_blk, preferred_element_type=jnp.float32)
            * score_scale
        )
        allowed = (pos_blk[None, :] <= query_pos[:, None]) & (
            seg_blk[None, :] == query_seg[:, None]
        )
        return (jnp.where(allowed[None], raw_scores, MASK_FILL), allowed)

    def total_step(running, key_part):
        run_max, run_sum = running
        scores = score_block(key_part[0], key_part[1], key_part[2])[0]
        new_max = jnp.maximum(run_max, jnp.max(scores, axis=-1))
        run_sum = run_sum * jnp.exp(run_max - new_max) + jnp.sum(
            jnp.exp(scores - new_max[..., None]), axis=-1
        )
        return ((new_max, run_sum), None)

    start_max = jnp.full((head_count, token_count), MASK_FILL, jnp.float32)
    start_sum = jnp.zeros((head_count, token_count), jnp.float32)
    (run_max, run_sum), unused = lax.scan(
        total_step, (start_max, start_sum), (keys_all, key_pos, key_seg)
    )
    log_total = run_max + jnp.log(run_sum)

    def attend_step(summed, key_part):
        key_blk, value_blk, pos_blk, seg_blk = key_part
        scores = score_block(key_blk, pos_blk, seg_blk)[0]
        weights = jnp.exp(scores - log_total[..., None]).astype(jnp.bfloat16)
        return (
            summed
            + jnp.einsum("hqk,khd->qhd", weights, value_blk, preferred_element_type=jnp.float32),
            None,
        )

    key_stack = (keys_all, values_all, key_pos, key_seg)
    attended, unused = lax.scan(attend_step, jnp.zeros(head_shape, jnp.float32), key_stack)
    attn_low = attended.reshape(token_count, model_width).astype(jnp.bfloat16)
    residual = inputs + jnp.dot(attn_low, out_weight, preferred_element_type=jnp.float32)
    ffn_set = (
        lax.all_gather(gain_ffn, ("ctx", "fsdp"), axis=0, tiled=True),
        lax.all_gather(w_router, ("ctx", "fsdp"), axis=0, tiled=True),
        lax.all_gather(w_shared_gate, ("ctx", "fsdp"), axis=0, tiled=True),
        lax.all_gather(w_shared_in, ("ctx", "fsdp"), axis=0, tiled=True),
        lax.all_gather(w_shared_out, ("ctx", "fsdp"), axis=0, tiled=True),
    )
    ffn_gain, router_weight, gate_vector, shared_in, shared_out = ffn_set
    normed_two, inv_two = rms_norm(residual, ffn_gain.astype(jnp.float32))
    low_two = normed_two.astype(jnp.bfloat16)
    logits = jnp.dot(low_two, router_weight, preferred_element_type=jnp.float32)
    router_probs = jax.nn.softmax(logits, axis=-1)
    chosen = routes.reshape(token_count, top_count)
    chosen_mask = chosen[..., None] == jnp.arange(expert_count, dtype=jnp.int32)
    gate_vals = jnp.sum(jnp.where(chosen_mask, router_probs[:, None, :], 0.0), axis=-1)
    shared_scale = jax.nn.sigmoid(jnp.dot(low_two, gate_vector, preferred_element_type=jnp.float32))
    shared_pre = jnp.dot(low_two, shared_in, preferred_element_type=jnp.float32)
    shared_hid = swiglu(shared_pre, FS).astype(jnp.bfloat16)
    shared_res = jnp.dot(shared_hid, shared_out, preferred_element_type=jnp.float32)
    pair_routes = chosen.reshape(token_count * top_count)
    expert_marks = (
        pair_routes[:, None] == jnp.arange(expert_count, dtype=jnp.int32)[None, :]
    ).astype(jnp.int32)
    pair_ranks = jnp.sum((jnp.cumsum(expert_marks, axis=0) - expert_marks) * expert_marks, axis=1)
    pair_target = jnp.where(pair_ranks < capacity, pair_routes * capacity + pair_ranks, -1)
    pair_map = pair_target[:, None] == jnp.arange(slot_count, dtype=jnp.int32)[None, :]
    pair_low = pair_map.astype(jnp.bfloat16)
    token_map = jnp.sum(
        pair_map.reshape(token_count, top_count, slot_count).astype(jnp.int32), axis=1
    ).astype(jnp.bfloat16)
    outgoing = jnp.einsum(
        "tc,td->cd", token_map, low_two, preferred_element_type=jnp.float32
    ).astype(jnp.bfloat16)
    incoming = lax.all_to_all(
        outgoing.reshape(expert_count, capacity, model_width),
        "ctx",
        split_axis=0,
        concat_axis=1,
        tiled=True,
    )
    expert_in, expert_out = (
        lax.all_gather(w_expert_in, "fsdp", axis=1, tiled=True),
        lax.all_gather(w_expert_out, "fsdp", axis=1, tiled=True),
    )
    expert_pre = jnp.einsum("erd,edf->erf", incoming, expert_in, preferred_element_type=jnp.float32)
    expert_hid = swiglu(expert_pre, FE).astype(jnp.bfloat16)
    expert_res = jnp.einsum(
        "erf,efd->erd", expert_hid, expert_out, preferred_element_type=jnp.float32
    ).astype(jnp.bfloat16)
    returned = lax.all_to_all(expert_res, "ctx", split_axis=1, concat_axis=0, tiled=True).reshape(
        slot_count, model_width
    )
    pair_vals = jnp.dot(pair_low, returned, preferred_element_type=jnp.float32).reshape(
        token_count, top_count, model_width
    )
    routed = jnp.sum(gate_vals[..., None] * pair_vals, axis=1)
    output = (
        (residual + shared_scale[:, None] * shared_res + routed)
        .astype(jnp.bfloat16)
        .reshape(tokens.shape)
    )
    grad_out = cotangent.reshape(token_count, model_width).astype(jnp.float32)
    pair_grads = gate_vals[..., None] * grad_out[:, None, :]
    grad_gates = jnp.sum(grad_out[:, None, :] * pair_vals, axis=-1)
    grad_returned = jnp.einsum(
        "pc,pd->cd",
        pair_map.astype(jnp.float32),
        pair_grads.reshape(token_count * top_count, model_width),
        precision=HIGHEST,
    ).astype(jnp.bfloat16)
    grad_res = lax.all_to_all(
        grad_returned.reshape(expert_count, capacity, model_width),
        "ctx",
        split_axis=0,
        concat_axis=1,
        tiled=True,
    )
    grad_expert_out = jnp.einsum(
        "erf,erd->efd", expert_hid, grad_res, preferred_element_type=jnp.float32
    )
    grad_hid = jnp.einsum("erd,efd->erf", grad_res, expert_out, preferred_element_type=jnp.float32)
    grad_pre = swiglu_back(expert_pre, FE, grad_hid).astype(jnp.bfloat16)
    grad_expert_in = jnp.einsum(
        "erd,erf->edf", incoming, grad_pre, preferred_element_type=jnp.float32
    )
    grad_incoming = jnp.einsum(
        "erf,edf->erd", grad_pre, expert_in, preferred_element_type=jnp.float32
    ).astype(jnp.bfloat16)
    grad_outgoing = lax.all_to_all(
        grad_incoming, "ctx", split_axis=1, concat_axis=0, tiled=True
    ).reshape(slot_count, model_width)
    expert_grads = (
        lax.psum_scatter(
            grad_expert_in.astype(jnp.bfloat16), "fsdp", scatter_dimension=1, tiled=True
        ).astype(jnp.float32),
        lax.psum_scatter(
            grad_expert_out.astype(jnp.bfloat16), "fsdp", scatter_dimension=1, tiled=True
        ).astype(jnp.float32),
    )
    grad_two = jnp.einsum("tc,cd->td", token_map, grad_outgoing, preferred_element_type=jnp.float32)
    grad_probs = jnp.sum(jnp.where(chosen_mask, grad_gates[..., None], 0.0), axis=1)
    grad_logits = (
        router_probs * (grad_probs - jnp.sum(router_probs * grad_probs, axis=-1, keepdims=True))
    ).astype(jnp.bfloat16)
    grad_router = jnp.einsum("td,te->de", low_two, grad_logits, preferred_element_type=jnp.float32)
    grad_shared_res = (shared_scale[:, None] * grad_out).astype(jnp.bfloat16)
    grad_gate_pre = (
        jnp.sum(grad_out * shared_res, axis=-1) * shared_scale * (1.0 - shared_scale)
    ).astype(jnp.bfloat16)
    grad_shared_out = jnp.einsum(
        "tf,td->fd", shared_hid, grad_shared_res, preferred_element_type=jnp.float32
    )
    grad_shared_hid = jnp.einsum(
        "td,fd->tf", grad_shared_res, shared_out, preferred_element_type=jnp.float32
    )
    grad_shared_pre = swiglu_back(shared_pre, FS, grad_shared_hid).astype(jnp.bfloat16)
    grad_shared_in = jnp.einsum(
        "td,tf->df", low_two, grad_shared_pre, preferred_element_type=jnp.float32
    )
    grad_gate_vector = jnp.einsum(
        "td,t->d", low_two, grad_gate_pre, preferred_element_type=jnp.float32
    )
    grad_two = grad_two + jnp.einsum(
        "te,de->td", grad_logits, router_weight, preferred_element_type=jnp.float32
    )
    grad_two = grad_two + jnp.einsum(
        "tf,df->td", grad_shared_pre, shared_in, preferred_element_type=jnp.float32
    )
    grad_two = (
        grad_two
        + grad_gate_pre.astype(jnp.float32)[:, None] * gate_vector.astype(jnp.float32)[None, :]
    )
    grad_resid_norm, grad_gain_two = rms_back(
        residual, inv_two, ffn_gain.astype(jnp.float32), grad_two
    )
    grad_resid = grad_out + grad_resid_norm
    ffn_grads = (
        lax.psum_scatter(grad_gain_two, ("ctx", "fsdp"), scatter_dimension=0, tiled=True),
        lax.psum_scatter(grad_router, ("ctx", "fsdp"), scatter_dimension=0, tiled=True),
        lax.psum_scatter(grad_gate_vector, ("ctx", "fsdp"), scatter_dimension=0, tiled=True),
        lax.psum_scatter(grad_shared_in, ("ctx", "fsdp"), scatter_dimension=0, tiled=True),
        lax.psum_scatter(grad_shared_out, ("ctx", "fsdp"), scatter_dimension=0, tiled=True),
    )
    grad_mixed = grad_resid.astype(jnp.bfloat16)
    grad_out_weight = jnp.einsum(
        "tc,td->cd", attn_low, grad_mixed, preferred_element_type=jnp.float32
    )
    grad_attn = (
        jnp.einsum("td,cd->tc", grad_mixed, out_weight, preferred_element_type=jnp.float32)
        .astype(jnp.bfloat16)
        .reshape(head_shape)
    )

    def delta_step(summed, key_part):
        key_blk, value_blk, pos_blk, seg_blk = key_part
        weights = jnp.exp(score_block(key_blk, pos_blk, seg_blk)[0] - log_total[..., None])
        grad_weights = jnp.einsum(
            "qhd,khd->hqk", grad_attn, value_blk, preferred_element_type=jnp.float32
        )
        return (summed + jnp.sum(weights * grad_weights, axis=-1), None)

    delta_sum, unused = lax.scan(
        delta_step, jnp.zeros((head_count, token_count), jnp.float32), key_stack
    )

    def grad_step(summed, key_part):
        key_blk, value_blk, pos_blk, seg_blk = key_part
        scores, allowed = score_block(key_blk, pos_blk, seg_blk)
        weights = jnp.exp(scores - log_total[..., None])
        grad_weights = jnp.einsum(
            "qhd,khd->hqk", grad_attn, value_blk, preferred_element_type=jnp.float32
        )
        grad_scores = jnp.where(
            allowed[None], weights * (grad_weights - delta_sum[..., None]), 0.0
        ).astype(jnp.bfloat16)
        summed = (
            summed
            + jnp.einsum("hqk,khd->qhd", grad_scores, key_blk, preferred_element_type=jnp.float32)
            * score_scale
        )
        grad_key = (
            jnp.einsum("hqk,qhd->khd", grad_scores, queries, preferred_element_type=jnp.float32)
            * score_scale
        )
        grad_value = jnp.einsum(
            "hqk,qhd->khd",
            weights.astype(jnp.bfloat16),
            grad_attn,
            preferred_element_type=jnp.float32,
        )
        return (summed, (grad_key, grad_value))

    grad_query, (grad_keys, grad_values) = lax.scan(
        grad_step, jnp.zeros(head_shape, jnp.float32), key_stack
    )
    grad_keys_own, grad_values_own = (
        lax.psum_scatter(
            grad_keys.reshape(2, half_len, model_width).astype(jnp.bfloat16),
            "ctx",
            scatter_dimension=1,
            tiled=True,
        ).astype(jnp.float32),
        lax.psum_scatter(
            grad_values.reshape(2, half_len, model_width).astype(jnp.bfloat16),
            "ctx",
            scatter_dimension=1,
            tiled=True,
        ).astype(jnp.float32),
    )
    grad_q_rows = rotate_back(grad_query, cos_tab, sine_tab).reshape(token_count, model_width)
    grad_k_rows = rotate_back(grad_keys_own.reshape(head_shape), cos_tab, sine_tab).reshape(
        token_count, model_width
    )
    grad_projected = jnp.concatenate(
        [grad_q_rows, grad_k_rows, grad_values_own.reshape(token_count, model_width)], axis=-1
    ).astype(jnp.bfloat16)
    grad_qkv_weight = jnp.einsum(
        "td,te->de", normed_low, grad_projected, preferred_element_type=jnp.float32
    )
    grad_qkv_bias = jnp.sum(grad_projected.astype(jnp.float32), axis=0)
    grad_normed = jnp.einsum(
        "te,de->td", grad_projected, qkv_weight, preferred_element_type=jnp.float32
    )
    grad_inputs_norm, grad_gain_one = rms_back(
        inputs, inv_one, attn_gain.astype(jnp.float32), grad_normed
    )
    grad_tokens = (grad_resid + grad_inputs_norm).reshape(tokens.shape)
    attn_grads = (
        lax.psum_scatter(grad_qkv_weight, ("ctx", "fsdp"), scatter_dimension=0, tiled=True),
        lax.psum_scatter(grad_qkv_bias, ("ctx", "fsdp"), scatter_dimension=0, tiled=True),
        lax.psum_scatter(grad_out_weight, ("ctx", "fsdp"), scatter_dimension=0, tiled=True),
        lax.psum_scatter(grad_gain_one, ("ctx", "fsdp"), scatter_dimension=0, tiled=True),
    )
    return (
        output,
        grad_tokens,
        attn_grads[0],
        attn_grads[1],
        attn_grads[2],
        attn_grads[3],
        ffn_grads[0],
        ffn_grads[1],
        ffn_grads[2],
        ffn_grads[3],
        ffn_grads[4],
        expert_grads[0],
        expert_grads[1],
    )


def solution(mesh):
    in_specs = (
        P("fsdp", None, "ctx", None),
        P("fsdp", None, None),
        P("fsdp", None, "ctx", None),
        P("fsdp", None, "ctx", None),
        P(("ctx", "fsdp"), None),
        P(("ctx", "fsdp")),
        P(("ctx", "fsdp"), None),
        P(("ctx", "fsdp")),
        P(("ctx", "fsdp")),
        P(("ctx", "fsdp"), None),
        P(("ctx", "fsdp")),
        P(("ctx", "fsdp"), None),
        P(("ctx", "fsdp"), None),
        P("ctx", "fsdp", None),
        P("ctx", "fsdp", None),
    )
    out_specs = (
        P("fsdp", None, "ctx", None),
        P("fsdp", None, "ctx", None),
        P(("ctx", "fsdp"), None),
        P(("ctx", "fsdp")),
        P(("ctx", "fsdp"), None),
        P(("ctx", "fsdp")),
        P(("ctx", "fsdp")),
        P(("ctx", "fsdp"), None),
        P(("ctx", "fsdp")),
        P(("ctx", "fsdp"), None),
        P(("ctx", "fsdp"), None),
        P("ctx", "fsdp", None),
        P("ctx", "fsdp", None),
    )
    ctx_size = mesh.shape["ctx"]
    fsdp_size = mesh.shape["fsdp"]

    def local(*arrays):
        if HEADS % ctx_size:
            return local_wide(*arrays)
        return local_split(ctx_size, fsdp_size, *arrays)

    return jax.shard_map(local, mesh=mesh, in_specs=in_specs, out_specs=out_specs, check_vma=False)
```

```python
import functools

import jax
import jax.numpy as jnp
from jax import lax
from jax.experimental import pallas as pl
from jax.experimental.pallas import tpu as pltpu
from jax.sharding import PartitionSpec as P

HD = 128
HEADS = 16
FS = 5632
FE = 1408


RMS_EPS = 1e-06
ROPE_THETA = 1000000.0
MASK_FILL = -1e30
HIGHEST = lax.Precision.HIGHEST


def rope_tables(positions, head_dim):
    half_dim = head_dim // 2
    inv_freq = ROPE_THETA ** (-(jnp.arange(half_dim, dtype=jnp.float32) * 2.0 / head_dim))
    angles = positions.astype(jnp.float32)[:, None] * inv_freq[None, :]
    cos_tab = jnp.concatenate([jnp.cos(angles), jnp.cos(angles)], axis=-1)
    sine_tab = jnp.concatenate([jnp.sin(angles), jnp.sin(angles)], axis=-1)
    return (cos_tab, sine_tab)


def rotate(values, cos_tab, sine_tab):
    half_dim = values.shape[-1] // 2
    turned = jnp.concatenate([-values[..., half_dim:], values[..., :half_dim]], axis=-1)
    return values * cos_tab[:, None, :] + turned * sine_tab[:, None, :]


def rotate_back(upstream, cos_tab, sine_tab):
    half_dim = upstream.shape[-1] // 2
    scaled = upstream * sine_tab[:, None, :]
    return upstream * cos_tab[:, None, :] + jnp.concatenate(
        [scaled[..., half_dim:], -scaled[..., :half_dim]], axis=-1
    )


def rms_norm(values, gain_vec):
    inv_rms = lax.rsqrt(jnp.mean(values * values, axis=-1, keepdims=True) + RMS_EPS)
    return (values * inv_rms * gain_vec, inv_rms)


def rms_back(values, inv_rms, gain_vec, upstream):
    weighted = upstream * gain_vec
    inner_mean = jnp.mean(weighted * values, axis=-1, keepdims=True)
    return (
        inv_rms * weighted - values * inv_rms * inv_rms * inv_rms * inner_mean,
        jnp.sum(upstream * values * inv_rms, axis=0),
    )


def swiglu(pre_act, split_at):
    return jax.nn.silu(pre_act[..., :split_at]) * pre_act[..., split_at:]


def swiglu_back(pre_act, split_at, upstream):
    gate_part = pre_act[..., :split_at]
    up_part = pre_act[..., split_at:]
    sigmoid_g = jax.nn.sigmoid(gate_part)
    d_gate = upstream * up_part * sigmoid_g * (1.0 + gate_part * (1.0 - sigmoid_g))
    d_up = upstream * gate_part * sigmoid_g
    return jnp.concatenate([d_gate, d_up], axis=-1)


def ring_order(size):
    return list(range(0, size, 2)) + list(range(size - 1, 0, -2))


def ring_steps(size):
    order = ring_order(size)
    ahead = [(order[i], order[(i + 1) % size]) for i in range(size)]
    back = [(dst, src) for src, dst in ahead]
    return (ahead, back)


def ring_peers(size, ctx_index):
    order = ring_order(size)
    place = {dev: i for i, dev in enumerate(order)}
    table = jnp.array(
        [[order[(place[dev] + k) % size] for k in range(size)] for dev in range(size)], jnp.int32
    )
    row = lax.dynamic_index_in_dim(table, ctx_index, 0, keepdims=False)
    return [row[k] for k in range(size)]


def after(value, *deps):
    return lax.optimization_barrier((value,) + deps)


def ring_gather(block, size, ctx_index, rider=None):
    rows, width = block.shape

    def put(out, piece, peer, offset):
        return lax.dynamic_update_slice(out, piece, (peer * rows + offset, jnp.zeros_like(peer)))

    out = jnp.zeros((size * rows, width), block.dtype)
    ahead, back = ring_steps(size)
    peers = ring_peers(size, ctx_index)
    half = size // 2
    out = put(out, block, ctx_index, 0)
    fore = rear = block
    for k in range(1, half):
        fore = lax.ppermute(fore, "ctx", ahead)
        rear = lax.ppermute(rear, "ctx", back)
        if rider is not None and k == 2:
            fore, rider = after(fore, rider)
        out = put(out, fore, peers[size - k], 0)
        out = put(out, rear, peers[k], 0)
    fore = lax.ppermute(fore[: rows // 2], "ctx", ahead)
    rear = lax.ppermute(rear[rows // 2 :], "ctx", back)
    out = put(out, fore, peers[half], 0)
    out = put(out, rear, peers[half], rows // 2)
    return out if rider is None else (out, rider)


def ring_sums(parts, size, ctx_index, riders):
    f32 = jnp.float32
    rows = parts.shape[0] // size
    ahead, back = ring_steps(size)
    peers = ring_peers(size, ctx_index)
    half = size // 2

    def own(k, start, count):
        first = (peers[k % size] * rows + start, jnp.zeros_like(peers[0]))
        return lax.dynamic_slice(parts, first, (count, parts.shape[1])).astype(f32)

    def low(values):
        return values.astype(jnp.bfloat16)

    cut = rows // 2
    fore = lax.ppermute(low(own(half, 0, cut)), "ctx", ahead)
    rear = lax.ppermute(low(own(half, cut, cut)), "ctx", back)
    fore = jnp.concatenate(
        [low(fore.astype(f32) + own(half - 1, 0, cut)), low(own(half - 1, cut, cut))], axis=0
    )
    rear = jnp.concatenate(
        [low(own(1 - half, 0, cut)), low(rear.astype(f32) + own(1 - half, cut, cut))], axis=0
    )
    for k in range(half - 1, 0, -1):
        fore = lax.ppermute(fore, "ctx", ahead)
        rear = lax.ppermute(rear, "ctx", back)
        if riders and k == half - 1:
            fore, *riders = after(fore, *riders)
        if k > 1:
            fore = low(fore.astype(f32) + own(k - 1, 0, rows))
            rear = low(rear.astype(f32) + own(1 - k, 0, rows))
    return (fore, rear, riders)


def ring_scatter(parts, size, ctx_index, kept=None, riders=()):
    fore, rear, riders = ring_sums(parts, size, ctx_index, riders)
    kept = (parts if kept is None else kept).reshape(size, -1, parts.shape[1])
    kept = lax.dynamic_index_in_dim(kept, ctx_index, 0, keepdims=False)
    total = kept.astype(jnp.float32) + fore.astype(jnp.float32) + rear.astype(jnp.float32)
    return (total, *riders) if riders else total


def other_core(size):
    return [(i, i ^ 1) for i in range(size)]


def other_chip(size):
    return [(i, i ^ 2) for i in range(size)]


def fsdp_gather(shard, size, hold):
    index = lax.axis_index("fsdp")
    rows, width = shard.shape
    far = lax.ppermute(shard, "fsdp", other_chip(size))
    far, hold = after(far, hold)
    pair = jnp.where(
        index < 2, jnp.stack([shard, far], axis=0), jnp.stack([far, shard], axis=0)
    )
    near = lax.ppermute(pair, "fsdp", other_core(size))
    out = jnp.zeros((2, 2, rows, width), shard.dtype)
    out = lax.dynamic_update_index_in_dim(out, pair, index % 2, 1)
    out = lax.dynamic_update_index_in_dim(out, near, 1 - index % 2, 1)
    return (out.reshape(size * rows, width), hold)


def column_pieces(weight, groups, size, extra):
    rows = weight.shape[0]
    width = weight.shape[1] // (groups * size)
    pieces = weight.reshape(rows, groups, size, width).transpose(2, 0, 1, 3)
    pieces = pieces.reshape(size, rows, groups * width)
    if extra is not None:
        count = extra.shape[0]
        more = -(-count // (groups * width * 16)) * 16
        extra = jnp.pad(extra, (0, more * groups * width - count))
        extra = jnp.broadcast_to(
            extra.reshape(1, more, groups * width), (size, more, groups * width)
        )
        pieces = jnp.concatenate([pieces, extra], axis=1)
    return pieces


def merge_columns(pieces, groups, size):
    width = pieces.shape[2] // groups
    if width % 128 == 0:
        pieces = pieces.reshape(size, -1, groups, width).transpose(1, 2, 0, 3)
        return pieces.reshape(-1, groups * size * width).astype(jnp.float32)
    columns = [
        pieces[peer, :, group * width : (group + 1) * width]
        for group in range(groups)
        for peer in range(size)
    ]
    return jnp.concatenate(columns, axis=1).astype(jnp.float32)


def attention_back_kernel(
    q_ref, k_ref, v_ref, do_ref, lse_ref, key_ref, query_ref, dq_ref, dk_ref, dv_ref, *, rows
):
    f32, bf16 = jnp.float32, jnp.bfloat16
    scale = HD ** (-0.5)
    keys, values = k_ref[...], v_ref[...]
    key_pos, key_seg = key_ref[:, 0:1], key_ref[:, 1:2]

    def pair(a, b, dims):
        return lax.dot_general(a, b, (dims, ((), ())), preferred_element_type=f32)

    for start in range(0, q_ref.shape[0], rows):
        here = slice(start, start + rows)
        queries, upstream = q_ref[here, :], do_ref[here, :]
        allowed = (key_pos <= query_ref[0:1, here]) & (key_seg == query_ref[1:2, here])
        scores = jnp.where(allowed, pair(keys, queries, ((1,), (1,))) * scale, MASK_FILL)
        weights = jnp.exp(scores - lse_ref[0, :, here])
        grads = pair(values, upstream, ((1,), (1,)))
        delta = jnp.sum(weights * grads, axis=0, keepdims=True)
        grads = jnp.where(allowed, weights * (grads - delta), 0.0).astype(bf16)
        part_v = pair(weights.astype(bf16), upstream, ((1,), (0,)))
        part_k = pair(grads, queries, ((1,), (0,))) * scale
        if start == 0:
            dv_ref[...] = part_v
            dk_ref[...] = part_k
        else:
            dv_ref[...] += part_v
            dk_ref[...] += part_k
        dq_ref[here, :] = pair(grads, keys, ((0,), (0,))) * scale


def attention_back(queries, keys, values, upstream, log_total, positions, seg_rows):
    tokens, width = queries.shape
    heads = width // HD
    marks = jnp.stack([positions, seg_rows], axis=0)
    by_head = pl.BlockSpec((tokens, HD), lambda h: (0, h))
    return pl.pallas_call(
        functools.partial(attention_back_kernel, rows=min(256, tokens)),
        grid=(heads,),
        in_specs=[by_head] * 4
        + [
            pl.BlockSpec((1, 1, tokens), lambda h: (h, 0, 0)),
            pl.BlockSpec((tokens, 2), lambda h: (0, 0)),
            pl.BlockSpec((2, tokens), lambda h: (0, 0)),
        ],
        out_specs=[by_head] * 3,
        out_shape=[jax.ShapeDtypeStruct((tokens, width), jnp.float32)] * 3,
        compiler_params=pltpu.CompilerParams(vmem_limit_bytes=40 * 1024 * 1024),
        cost_estimate=pl.CostEstimate(
            flops=10 * tokens * tokens * width,
            bytes_accessed=20 * tokens * width,
            transcendentals=tokens * tokens * heads,
        ),
    )(queries, keys, values, upstream, log_total.reshape(heads, 1, tokens), marks.T, marks)


def local_split(
    ctx_size,
    fsdp_size,
    tokens,
    segments,
    routes,
    cotangent,
    w_qkv,
    b_qkv,
    w_out,
    gain_attn,
    gain_ffn,
    w_router,
    w_shared_gate,
    w_shared_in,
    w_shared_out,
    w_expert_in,
    w_expert_out,
):
    bf16, f32, i32 = jnp.bfloat16, jnp.float32, jnp.int32
    device_count = ctx_size * fsdp_size
    block_len = tokens.shape[2]
    width = tokens.shape[3]
    token_count = 2 * block_len
    top_count = routes.shape[3]
    seq_len = token_count * ctx_size
    ctx_index = lax.axis_index("ctx")
    expert_count = w_router.shape[1]
    capacity = token_count * top_count // expert_count
    own_heads = HEADS // ctx_size
    own_width = own_heads * HD
    fs_own = FS // ctx_size
    score_scale = HD ** (-0.5)

    def dot(a, b):
        return jnp.dot(a, b, preferred_element_type=f32)

    def dot_t(a, b):
        return lax.dot_general(a, b, (((1,), (1,)), ((), ())), preferred_element_type=f32)

    def t_dot(a, b):
        return lax.dot_general(a, b, (((0,), (0,)), ((), ())), preferred_element_type=f32)

    def own_rows(values):
        return lax.dynamic_index_in_dim(
            values.reshape((ctx_size, token_count) + values.shape[1:]), ctx_index, 0, keepdims=False
        )

    def sum_rows(grad):
        return lax.psum_scatter(grad.astype(bf16), "fsdp", scatter_dimension=0, tiled=True)

    shard = width // device_count
    small = [gain_attn, gain_ffn, w_shared_gate, w_router.reshape(-1), b_qkv]
    small_size = sum(piece.shape[0] for piece in small)
    small = jnp.concatenate(small + [routes.astype(bf16).reshape(-1)], axis=0)
    small_count = small.shape[0]
    own_tokens = tokens.reshape(token_count, width).astype(f32)
    own_scaled, inv_one = rms_norm(own_tokens, 1.0)
    scaled_rows = ring_gather(own_scaled.astype(bf16), ctx_size, ctx_index)
    pieces = column_pieces(w_qkv, 3, ctx_size, small)
    pieces = lax.all_to_all(pieces, "ctx", split_axis=0, concat_axis=0, tiled=True)
    shared_in = column_pieces(w_shared_in, 2, ctx_size, None)
    shared_in, scaled_rows = after(shared_in, scaled_rows)
    shared_in = lax.all_to_all(shared_in, "ctx", split_axis=0, concat_axis=0, tiled=True)
    pieces = lax.all_gather(pieces, "fsdp", axis=0, tiled=False).transpose(1, 0, 2, 3)
    qkv_weight = pieces[:, :, :shard].reshape(width, 3 * own_width)
    small = pieces[:, :, shard:].reshape(device_count, -1)[:, :small_count]
    attn_gain = small[:, :shard].reshape(width).astype(f32)
    ffn_gain = small[:, shard : 2 * shard].reshape(width).astype(f32)
    gate_vector = small[:, 2 * shard : 3 * shard].reshape(width)
    router_end = 3 * shard + shard * expert_count
    router_weight = small[:, 3 * shard : router_end].reshape(width, expert_count)
    bias = small[:, router_end:small_size].reshape(3, ctx_size, own_width).astype(f32)
    bias = lax.dynamic_index_in_dim(bias, ctx_index, 1, keepdims=False).reshape(3 * own_width)
    route_rows = small[:, small_size:].astype(i32)
    route_rows = lax.dynamic_index_in_dim(
        route_rows.reshape(ctx_size, fsdp_size, -1), lax.axis_index("fsdp"), 1, keepdims=False
    ).reshape(ctx_size, token_count, top_count)

    expert_in = lax.all_gather(w_expert_in[0], "fsdp", axis=0, tiled=True)

    block_ids = jnp.arange(ctx_size, dtype=i32)[:, None]
    local_index = jnp.arange(block_len, dtype=i32)[None, :]
    positions = jnp.stack(
        [
            block_ids * block_len + local_index,
            seq_len - (block_ids + 1) * block_len + local_index,
        ],
        axis=1,
    ).reshape(seq_len)
    seg_rows = (
        segments.reshape(2, ctx_size, block_len).transpose(1, 0, 2).reshape(seq_len)
    )
    cos_tab, sine_tab = rope_tables(positions, HD)

    normed_low = (scaled_rows.astype(f32) * attn_gain).astype(bf16)
    projected = dot(normed_low, qkv_weight) + bias
    head_shape = (seq_len, own_heads, HD)
    queries = rotate(projected[:, :own_width].reshape(head_shape), cos_tab, sine_tab).astype(bf16)
    keys = rotate(
        projected[:, own_width : 2 * own_width].reshape(head_shape), cos_tab, sine_tab
    ).astype(bf16)
    values = projected[:, 2 * own_width :].reshape(head_shape).astype(bf16)
    out_weight, queries = fsdp_gather(w_out, fsdp_size, queries)
    allowed = (positions[None, :] <= positions[:, None]) & (seg_rows[None, :] == seg_rows[:, None])
    scores = jnp.einsum("qhd,khd->hqk", queries, keys, preferred_element_type=f32) * score_scale
    scores = jnp.where(allowed[None], scores, MASK_FILL)
    top_score = jnp.max(scores, axis=-1, keepdims=True)
    log_total = top_score + jnp.log(jnp.sum(jnp.exp(scores - top_score), axis=-1, keepdims=True))
    weights = jnp.exp(scores - log_total)
    weights_low = weights.astype(bf16)
    attended = jnp.einsum("hqk,khd->qhd", weights_low, values, preferred_element_type=f32)
    attn_own = attended.astype(bf16).reshape(seq_len, own_width)
    shared_out, attn_own = fsdp_gather(w_shared_out, fsdp_size, attn_own)
    expert_out, attn_own = fsdp_gather(w_expert_out[0], fsdp_size, attn_own)
    attn_parts, shared_in = after(dot(attn_own, out_weight).astype(bf16), shared_in)
    shared_in = lax.all_gather(shared_in, "fsdp", axis=0, tiled=False)
    own_residual = own_tokens + ring_scatter(attn_parts, ctx_size, ctx_index)

    normed_two, inv_two = rms_norm(own_residual, ffn_gain)
    own_low = normed_two.astype(bf16)
    low_two, grad_rows = ring_gather(
        own_low, ctx_size, ctx_index, cotangent.reshape(token_count, width)
    )
    grad_rows = lax.all_gather(grad_rows, "ctx", axis=0, tiled=True)
    mixed_weight = jnp.concatenate([router_weight, gate_vector[:, None]], axis=1)
    logits = dot(low_two, mixed_weight)
    probs_all = jax.nn.softmax(logits[:, :expert_count], axis=-1)
    scale_all = jax.nn.sigmoid(logits[:, expert_count])
    gate_all = lax.dynamic_index_in_dim(probs_all, ctx_index, 1, keepdims=False)

    named = jnp.any(route_rows == ctx_index, axis=-1)
    before = jnp.arange(token_count)[:, None] < jnp.arange(token_count)[None, :]
    rank = dot(named.astype(bf16), before.astype(bf16)).astype(i32)
    slot_of = jnp.where(named & (rank < capacity), rank, -1)
    slot_mask = slot_of[:, None, :] == jnp.arange(capacity, dtype=i32)[None, :, None]
    slot_map = slot_mask.astype(bf16)
    blocks_two = low_two.reshape(ctx_size, token_count, width)
    gate_blocks = gate_all.reshape(ctx_size, token_count)

    def to_slots(blocks):
        picked = jnp.einsum("bmt,btd->bmd", slot_map, blocks, preferred_element_type=f32)
        return picked.reshape(ctx_size * capacity, width)

    def to_tokens(slots):
        spread = jnp.einsum(
            "bmt,bmd->btd",
            slot_map,
            slots.reshape(ctx_size, capacity, width),
            preferred_element_type=f32,
        )
        return spread.reshape(seq_len, width)

    buffer = to_slots(blocks_two).astype(bf16)
    expert_pre = dot(buffer, expert_in)
    expert_hid = swiglu(expert_pre, FE).astype(bf16)
    expert_res = dot(expert_hid, expert_out).astype(bf16)
    routed = gate_all[:, None] * to_tokens(expert_res)

    shared_in, expert_res = after(shared_in, expert_res)
    shared_in = shared_in.transpose(1, 0, 2, 3).reshape(width, 2 * fs_own)
    shared_pre = dot(low_two, shared_in)
    shared_hid = swiglu(shared_pre, fs_own).astype(bf16)
    shared_res = dot(shared_hid, shared_out)
    out_parts = (scale_all[:, None] * shared_res + routed).astype(bf16)
    grad_rows, out_parts = after(grad_rows, out_parts)

    grad_slots = to_slots(grad_rows.reshape(ctx_size, token_count, width))
    gate_slots = jnp.sum(jnp.where(slot_mask, gate_blocks[:, None, :], 0.0), axis=-1).reshape(-1, 1)
    grad_res = (gate_slots * grad_slots).astype(bf16)
    grad_hid = dot_t(grad_res, expert_out)
    slot_terms = jnp.sum(expert_hid.astype(f32) * grad_hid, axis=-1)
    slot_terms = slot_terms.reshape(ctx_size, capacity, 1)
    gate_terms = jnp.sum(jnp.where(slot_mask, slot_terms, 0.0), axis=1)
    grad_pre = swiglu_back(expert_pre, FE, grad_hid).astype(bf16)
    grad_expert_in = t_dot(buffer, grad_pre)
    grad_buffer = dot_t(grad_pre, expert_in).astype(bf16)

    grad_f32 = grad_rows.astype(f32)
    grad_expert_in, grad_shared_res = after(
        grad_expert_in.astype(bf16), (scale_all[:, None] * grad_f32).astype(bf16)
    )
    sum_expert_in = sum_rows(grad_expert_in)

    grad_shared_hid = dot_t(grad_shared_res, shared_out)
    scale_terms = jnp.sum(shared_hid.astype(f32) * grad_shared_hid, axis=-1)
    grad_shared_pre = swiglu_back(shared_pre, fs_own, grad_shared_hid).astype(bf16)
    two_parts = (dot_t(grad_shared_pre, shared_in) + to_tokens(grad_buffer)).astype(bf16)
    two_parts, expert_hid, shared_hid, grad_shared_pre = after(
        two_parts, expert_hid, shared_hid, grad_shared_pre
    )
    grad_expert_out = t_dot(expert_hid, grad_res).astype(bf16)
    grad_shared_out = t_dot(shared_hid, grad_shared_res).astype(bf16)
    grad_shared_in = t_dot(low_two, grad_shared_pre).astype(bf16)
    grad_two = ring_scatter(two_parts, ctx_size, ctx_index)
    dots = jnp.stack([gate_terms, scale_terms.reshape(ctx_size, token_count)], axis=1)
    dots = lax.all_to_all(dots, "ctx", split_axis=0, concat_axis=0, tiled=True)
    grad_two, grad_shared_in, grad_shared_out, grad_expert_out, dots = after(
        grad_two, grad_shared_in, grad_shared_out, grad_expert_out, dots
    )
    sum_shared_in = grad_shared_in.reshape(ctx_size, fsdp_size, shard, 2 * fs_own)
    sum_shared_in = lax.psum_scatter(
        sum_shared_in.transpose(1, 0, 2, 3).reshape(width, 2 * fs_own),
        "fsdp",
        scatter_dimension=0,
        tiled=True,
    ).reshape(ctx_size, shard, 2 * fs_own)
    sum_expert_out = sum_rows(grad_expert_out)
    own_probs = own_rows(probs_all)
    own_scale = own_rows(scale_all)
    own_chosen = routes.reshape(token_count, top_count)
    chosen_mask = jnp.any(
        own_chosen[..., None] == jnp.arange(expert_count, dtype=i32), axis=1
    )
    prob_terms = jnp.where(chosen_mask, dots[:, 0].T, 0.0)
    grad_logits = (
        prob_terms - own_probs * jnp.sum(prob_terms, axis=-1, keepdims=True)
    ).astype(bf16)
    grad_gate_pre = (jnp.sum(dots[:, 1], axis=0) * (1.0 - own_scale)).astype(bf16)
    grad_router = t_dot(own_low, grad_logits)
    grad_gate_vector = t_dot(own_low, grad_gate_pre[:, None])
    grad_two = grad_two + dot_t(grad_logits, router_weight)
    grad_two = grad_two + grad_gate_pre.astype(f32)[:, None] * gate_vector.astype(f32)[None, :]
    grad_resid_norm, grad_gain_two = rms_back(
        own_residual, inv_two, ffn_gain, grad_two
    )
    grad_resid = cotangent.reshape(token_count, width).astype(f32) + grad_resid_norm

    grad_mixed, sum_expert_in = after(grad_resid.astype(bf16), sum_expert_in)
    mixed_all = ring_gather(grad_mixed, ctx_size, ctx_index)
    grad_attn = dot_t(mixed_all, out_weight).astype(bf16)
    grad_attn, sum_shared_in = after(grad_attn, sum_shared_in)
    sum_shared_in = lax.all_to_all(
        sum_shared_in, "ctx", split_axis=0, concat_axis=0, tiled=True
    )
    grad_q, grad_k, grad_v = attention_back(
        queries.reshape(seq_len, own_width),
        keys.reshape(seq_len, own_width),
        values.reshape(seq_len, own_width),
        grad_attn,
        log_total,
        positions,
        seg_rows,
    )
    grad_projected = jnp.concatenate(
        [
            rotate_back(grad_q.reshape(head_shape), cos_tab, sine_tab).reshape(seq_len, own_width),
            rotate_back(grad_k.reshape(head_shape), cos_tab, sine_tab).reshape(seq_len, own_width),
            grad_v,
        ],
        axis=-1,
    ).astype(bf16)
    one_sums = dot_t(grad_projected, qkv_weight)
    grad_gain_one = jnp.sum(one_sums * scaled_rows.astype(f32), axis=0)
    one_parts, sum_shared_in = after(one_sums.astype(bf16), sum_shared_in)
    one_kept, grad_projected = after(one_parts, grad_projected)
    one_kept, attn_own = after(one_kept, attn_own)
    grad_normed, sum_expert_out = ring_scatter(
        one_parts, ctx_size, ctx_index, one_kept, (sum_expert_out,)
    )
    grad_qkv_weight = t_dot(normed_low, grad_projected)
    grad_bias = jnp.sum(grad_projected.astype(f32), axis=0).reshape(3, 1, own_width)
    grad_bias = jnp.where(
        jnp.arange(ctx_size, dtype=i32)[None, :, None] == ctx_index, grad_bias, 0.0
    )

    grad_out_weight = t_dot(attn_own, mixed_all)
    small_grads = [grad_gain_one, grad_gain_two, grad_gate_vector, grad_router, grad_bias]
    small_grads = jnp.concatenate(
        [piece.reshape(device_count, -1) for piece in small_grads], axis=1
    )
    more = -(-small_size // (3 * own_width * 16)) * 16
    small_grads = jnp.pad(small_grads, ((0, 0), (0, more * 3 * own_width - small_size)))
    pieces = jnp.concatenate(
        [
            grad_qkv_weight.astype(bf16).reshape(ctx_size, fsdp_size, shard, 3 * own_width),
            small_grads.astype(bf16).reshape(ctx_size, fsdp_size, more, 3 * own_width),
        ],
        axis=2,
    )
    pieces = pieces.transpose(1, 0, 2, 3).reshape(-1, 3 * own_width)
    pieces = lax.psum_scatter(pieces, "fsdp", scatter_dimension=0, tiled=True)
    grad_normed, pieces, out_parts, grad_shared_out, grad_out_weight = after(
        grad_normed, pieces, out_parts, grad_shared_out, grad_out_weight.astype(bf16)
    )
    sum_shared_out = sum_rows(grad_shared_out)
    sum_out_weight = sum_rows(grad_out_weight)
    pieces = pieces.reshape(ctx_size, shard + more, 3 * own_width)
    pieces = lax.all_to_all(pieces, "ctx", split_axis=0, concat_axis=0, tiled=True)
    out_sum, pieces = ring_scatter(out_parts, ctx_size, ctx_index, riders=(pieces,))
    output = (own_residual + out_sum).astype(bf16).reshape(tokens.shape)
    grad_inputs_norm, unused = rms_back(
        own_tokens,
        inv_one,
        attn_gain,
        grad_normed,
    )
    grad_tokens = (grad_resid + grad_inputs_norm).reshape(tokens.shape)
    small_grads = jnp.sum(pieces[:, shard:].reshape(ctx_size, -1).astype(f32), axis=0)
    return (
        output,
        grad_tokens,
        merge_columns(pieces[:, :shard], 3, ctx_size),
        small_grads[router_end:small_size],
        sum_out_weight.astype(f32),
        small_grads[:shard],
        small_grads[shard : 2 * shard],
        small_grads[3 * shard : router_end].reshape(shard, expert_count),
        small_grads[2 * shard : 3 * shard],
        merge_columns(sum_shared_in, 2, ctx_size),
        sum_shared_out.astype(f32),
        sum_expert_in.astype(f32)[None],
        sum_expert_out.astype(f32)[None],
    )


def local_wide(
    tokens,
    segments,
    routes,
    cotangent,
    w_qkv,
    b_qkv,
    w_out,
    gain_attn,
    gain_ffn,
    w_router,
    w_shared_gate,
    w_shared_in,
    w_shared_out,
    w_expert_in,
    w_expert_out,
):
    block_len = tokens.shape[2]
    model_width = tokens.shape[3]
    token_count = 2 * block_len
    top_count = routes.shape[3]
    half_len = segments.shape[2]
    seq_len = 2 * half_len
    ctx_index = lax.axis_index("ctx")
    head_count = model_width // HD
    expert_count = w_router.shape[1]
    capacity = token_count * top_count // expert_count
    slot_count = expert_count * capacity
    key_rows = min(512, seq_len)
    key_blocks = seq_len // key_rows
    score_scale = HD ** (-0.5)
    head_shape = (token_count, head_count, HD)
    attn_set = (
        lax.all_gather(w_qkv, ("ctx", "fsdp"), axis=0, tiled=True),
        lax.all_gather(b_qkv, ("ctx", "fsdp"), axis=0, tiled=True),
        lax.all_gather(w_out, ("ctx", "fsdp"), axis=0, tiled=True),
        lax.all_gather(gain_attn, ("ctx", "fsdp"), axis=0, tiled=True),
    )
    qkv_weight, qkv_bias, out_weight, attn_gain = attn_set
    inputs = tokens.reshape(token_count, model_width).astype(jnp.float32)
    normed, inv_one = rms_norm(inputs, attn_gain.astype(jnp.float32))
    normed_low = normed.astype(jnp.bfloat16)
    projected = jnp.dot(
        normed_low, qkv_weight, preferred_element_type=jnp.float32
    ) + qkv_bias.astype(jnp.float32)
    local_index = jnp.arange(block_len, dtype=jnp.int32)
    query_pos = jnp.concatenate(
        [ctx_index * block_len + local_index, seq_len - (ctx_index + 1) * block_len + local_index]
    )
    half_index = jnp.arange(half_len, dtype=jnp.int32)
    key_pos = jnp.concatenate(
        [half_index, seq_len - block_len * (half_index // block_len + 1) + half_index % block_len]
    ).reshape(key_blocks, key_rows)
    key_seg = segments.reshape(key_blocks, key_rows)
    query_seg = lax.dynamic_slice_in_dim(segments[0], ctx_index * block_len, block_len, 1).reshape(
        token_count
    )
    cos_tab, sine_tab = rope_tables(query_pos, HD)
    queries = rotate(projected[:, :model_width].reshape(head_shape), cos_tab, sine_tab).astype(
        jnp.bfloat16
    )
    keys_own = rotate(
        projected[:, model_width : 2 * model_width].reshape(head_shape), cos_tab, sine_tab
    ).astype(jnp.bfloat16)
    values_own = projected[:, 2 * model_width :].astype(jnp.bfloat16)
    keys_all, values_all = (
        lax.all_gather(keys_own.reshape(2, block_len, model_width), "ctx", axis=1, tiled=True),
        lax.all_gather(values_own.reshape(2, block_len, model_width), "ctx", axis=1, tiled=True),
    )
    keys_all = keys_all.reshape(key_blocks, key_rows, head_count, HD)
    values_all = values_all.reshape(key_blocks, key_rows, head_count, HD)

    def score_block(key_blk, pos_blk, seg_blk):
        raw_scores = (
            jnp.einsum("qhd,khd->hqk", queries, key_blk, preferred_element_type=jnp.float32)
            * score_scale
        )
        allowed = (pos_blk[None, :] <= query_pos[:, None]) & (
            seg_blk[None, :] == query_seg[:, None]
        )
        return (jnp.where(allowed[None], raw_scores, MASK_FILL), allowed)

    def total_step(running, key_part):
        run_max, run_sum = running
        scores = score_block(key_part[0], key_part[1], key_part[2])[0]
        new_max = jnp.maximum(run_max, jnp.max(scores, axis=-1))
        run_sum = run_sum * jnp.exp(run_max - new_max) + jnp.sum(
            jnp.exp(scores - new_max[..., None]), axis=-1
        )
        return ((new_max, run_sum), None)

    start_max = jnp.full((head_count, token_count), MASK_FILL, jnp.float32)
    start_sum = jnp.zeros((head_count, token_count), jnp.float32)
    (run_max, run_sum), unused = lax.scan(
        total_step, (start_max, start_sum), (keys_all, key_pos, key_seg)
    )
    log_total = run_max + jnp.log(run_sum)

    def attend_step(summed, key_part):
        key_blk, value_blk, pos_blk, seg_blk = key_part
        scores = score_block(key_blk, pos_blk, seg_blk)[0]
        weights = jnp.exp(scores - log_total[..., None]).astype(jnp.bfloat16)
        return (
            summed
            + jnp.einsum("hqk,khd->qhd", weights, value_blk, preferred_element_type=jnp.float32),
            None,
        )

    key_stack = (keys_all, values_all, key_pos, key_seg)
    attended, unused = lax.scan(attend_step, jnp.zeros(head_shape, jnp.float32), key_stack)
    attn_low = attended.reshape(token_count, model_width).astype(jnp.bfloat16)
    residual = inputs + jnp.dot(attn_low, out_weight, preferred_element_type=jnp.float32)
    ffn_set = (
        lax.all_gather(gain_ffn, ("ctx", "fsdp"), axis=0, tiled=True),
        lax.all_gather(w_router, ("ctx", "fsdp"), axis=0, tiled=True),
        lax.all_gather(w_shared_gate, ("ctx", "fsdp"), axis=0, tiled=True),
        lax.all_gather(w_shared_in, ("ctx", "fsdp"), axis=0, tiled=True),
        lax.all_gather(w_shared_out, ("ctx", "fsdp"), axis=0, tiled=True),
    )
    ffn_gain, router_weight, gate_vector, shared_in, shared_out = ffn_set
    normed_two, inv_two = rms_norm(residual, ffn_gain.astype(jnp.float32))
    low_two = normed_two.astype(jnp.bfloat16)
    logits = jnp.dot(low_two, router_weight, preferred_element_type=jnp.float32)
    router_probs = jax.nn.softmax(logits, axis=-1)
    chosen = routes.reshape(token_count, top_count)
    chosen_mask = chosen[..., None] == jnp.arange(expert_count, dtype=jnp.int32)
    gate_vals = jnp.sum(jnp.where(chosen_mask, router_probs[:, None, :], 0.0), axis=-1)
    shared_scale = jax.nn.sigmoid(jnp.dot(low_two, gate_vector, preferred_element_type=jnp.float32))
    shared_pre = jnp.dot(low_two, shared_in, preferred_element_type=jnp.float32)
    shared_hid = swiglu(shared_pre, FS).astype(jnp.bfloat16)
    shared_res = jnp.dot(shared_hid, shared_out, preferred_element_type=jnp.float32)
    pair_routes = chosen.reshape(token_count * top_count)
    expert_marks = (
        pair_routes[:, None] == jnp.arange(expert_count, dtype=jnp.int32)[None, :]
    ).astype(jnp.int32)
    pair_ranks = jnp.sum((jnp.cumsum(expert_marks, axis=0) - expert_marks) * expert_marks, axis=1)
    pair_target = jnp.where(pair_ranks < capacity, pair_routes * capacity + pair_ranks, -1)
    pair_map = pair_target[:, None] == jnp.arange(slot_count, dtype=jnp.int32)[None, :]
    pair_low = pair_map.astype(jnp.bfloat16)
    token_map = jnp.sum(
        pair_map.reshape(token_count, top_count, slot_count).astype(jnp.int32), axis=1
    ).astype(jnp.bfloat16)
    outgoing = jnp.einsum(
        "tc,td->cd", token_map, low_two, preferred_element_type=jnp.float32
    ).astype(jnp.bfloat16)
    incoming = lax.all_to_all(
        outgoing.reshape(expert_count, capacity, model_width),
        "ctx",
        split_axis=0,
        concat_axis=1,
        tiled=True,
    )
    expert_in, expert_out = (
        lax.all_gather(w_expert_in, "fsdp", axis=1, tiled=True),
        lax.all_gather(w_expert_out, "fsdp", axis=1, tiled=True),
    )
    expert_pre = jnp.einsum("erd,edf->erf", incoming, expert_in, preferred_element_type=jnp.float32)
    expert_hid = swiglu(expert_pre, FE).astype(jnp.bfloat16)
    expert_res = jnp.einsum(
        "erf,efd->erd", expert_hid, expert_out, preferred_element_type=jnp.float32
    ).astype(jnp.bfloat16)
    returned = lax.all_to_all(expert_res, "ctx", split_axis=1, concat_axis=0, tiled=True).reshape(
        slot_count, model_width
    )
    pair_vals = jnp.dot(pair_low, returned, preferred_element_type=jnp.float32).reshape(
        token_count, top_count, model_width
    )
    routed = jnp.sum(gate_vals[..., None] * pair_vals, axis=1)
    output = (
        (residual + shared_scale[:, None] * shared_res + routed)
        .astype(jnp.bfloat16)
        .reshape(tokens.shape)
    )
    grad_out = cotangent.reshape(token_count, model_width).astype(jnp.float32)
    pair_grads = gate_vals[..., None] * grad_out[:, None, :]
    grad_gates = jnp.sum(grad_out[:, None, :] * pair_vals, axis=-1)
    grad_returned = jnp.einsum(
        "pc,pd->cd",
        pair_map.astype(jnp.float32),
        pair_grads.reshape(token_count * top_count, model_width),
        precision=HIGHEST,
    ).astype(jnp.bfloat16)
    grad_res = lax.all_to_all(
        grad_returned.reshape(expert_count, capacity, model_width),
        "ctx",
        split_axis=0,
        concat_axis=1,
        tiled=True,
    )
    grad_expert_out = jnp.einsum(
        "erf,erd->efd", expert_hid, grad_res, preferred_element_type=jnp.float32
    )
    grad_hid = jnp.einsum("erd,efd->erf", grad_res, expert_out, preferred_element_type=jnp.float32)
    grad_pre = swiglu_back(expert_pre, FE, grad_hid).astype(jnp.bfloat16)
    grad_expert_in = jnp.einsum(
        "erd,erf->edf", incoming, grad_pre, preferred_element_type=jnp.float32
    )
    grad_incoming = jnp.einsum(
        "erf,edf->erd", grad_pre, expert_in, preferred_element_type=jnp.float32
    ).astype(jnp.bfloat16)
    grad_outgoing = lax.all_to_all(
        grad_incoming, "ctx", split_axis=1, concat_axis=0, tiled=True
    ).reshape(slot_count, model_width)
    expert_grads = (
        lax.psum_scatter(
            grad_expert_in.astype(jnp.bfloat16), "fsdp", scatter_dimension=1, tiled=True
        ).astype(jnp.float32),
        lax.psum_scatter(
            grad_expert_out.astype(jnp.bfloat16), "fsdp", scatter_dimension=1, tiled=True
        ).astype(jnp.float32),
    )
    grad_two = jnp.einsum("tc,cd->td", token_map, grad_outgoing, preferred_element_type=jnp.float32)
    grad_probs = jnp.sum(jnp.where(chosen_mask, grad_gates[..., None], 0.0), axis=1)
    grad_logits = (
        router_probs * (grad_probs - jnp.sum(router_probs * grad_probs, axis=-1, keepdims=True))
    ).astype(jnp.bfloat16)
    grad_router = jnp.einsum("td,te->de", low_two, grad_logits, preferred_element_type=jnp.float32)
    grad_shared_res = (shared_scale[:, None] * grad_out).astype(jnp.bfloat16)
    grad_gate_pre = (
        jnp.sum(grad_out * shared_res, axis=-1) * shared_scale * (1.0 - shared_scale)
    ).astype(jnp.bfloat16)
    grad_shared_out = jnp.einsum(
        "tf,td->fd", shared_hid, grad_shared_res, preferred_element_type=jnp.float32
    )
    grad_shared_hid = jnp.einsum(
        "td,fd->tf", grad_shared_res, shared_out, preferred_element_type=jnp.float32
    )
    grad_shared_pre = swiglu_back(shared_pre, FS, grad_shared_hid).astype(jnp.bfloat16)
    grad_shared_in = jnp.einsum(
        "td,tf->df", low_two, grad_shared_pre, preferred_element_type=jnp.float32
    )
    grad_gate_vector = jnp.einsum(
        "td,t->d", low_two, grad_gate_pre, preferred_element_type=jnp.float32
    )
    grad_two = grad_two + jnp.einsum(
        "te,de->td", grad_logits, router_weight, preferred_element_type=jnp.float32
    )
    grad_two = grad_two + jnp.einsum(
        "tf,df->td", grad_shared_pre, shared_in, preferred_element_type=jnp.float32
    )
    grad_two = (
        grad_two
        + grad_gate_pre.astype(jnp.float32)[:, None] * gate_vector.astype(jnp.float32)[None, :]
    )
    grad_resid_norm, grad_gain_two = rms_back(
        residual, inv_two, ffn_gain.astype(jnp.float32), grad_two
    )
    grad_resid = grad_out + grad_resid_norm
    ffn_grads = (
        lax.psum_scatter(grad_gain_two, ("ctx", "fsdp"), scatter_dimension=0, tiled=True),
        lax.psum_scatter(grad_router, ("ctx", "fsdp"), scatter_dimension=0, tiled=True),
        lax.psum_scatter(grad_gate_vector, ("ctx", "fsdp"), scatter_dimension=0, tiled=True),
        lax.psum_scatter(grad_shared_in, ("ctx", "fsdp"), scatter_dimension=0, tiled=True),
        lax.psum_scatter(grad_shared_out, ("ctx", "fsdp"), scatter_dimension=0, tiled=True),
    )
    grad_mixed = grad_resid.astype(jnp.bfloat16)
    grad_out_weight = jnp.einsum(
        "tc,td->cd", attn_low, grad_mixed, preferred_element_type=jnp.float32
    )
    grad_attn = (
        jnp.einsum("td,cd->tc", grad_mixed, out_weight, preferred_element_type=jnp.float32)
        .astype(jnp.bfloat16)
        .reshape(head_shape)
    )

    def delta_step(summed, key_part):
        key_blk, value_blk, pos_blk, seg_blk = key_part
        weights = jnp.exp(score_block(key_blk, pos_blk, seg_blk)[0] - log_total[..., None])
        grad_weights = jnp.einsum(
            "qhd,khd->hqk", grad_attn, value_blk, preferred_element_type=jnp.float32
        )
        return (summed + jnp.sum(weights * grad_weights, axis=-1), None)

    delta_sum, unused = lax.scan(
        delta_step, jnp.zeros((head_count, token_count), jnp.float32), key_stack
    )

    def grad_step(summed, key_part):
        key_blk, value_blk, pos_blk, seg_blk = key_part
        scores, allowed = score_block(key_blk, pos_blk, seg_blk)
        weights = jnp.exp(scores - log_total[..., None])
        grad_weights = jnp.einsum(
            "qhd,khd->hqk", grad_attn, value_blk, preferred_element_type=jnp.float32
        )
        grad_scores = jnp.where(
            allowed[None], weights * (grad_weights - delta_sum[..., None]), 0.0
        ).astype(jnp.bfloat16)
        summed = (
            summed
            + jnp.einsum("hqk,khd->qhd", grad_scores, key_blk, preferred_element_type=jnp.float32)
            * score_scale
        )
        grad_key = (
            jnp.einsum("hqk,qhd->khd", grad_scores, queries, preferred_element_type=jnp.float32)
            * score_scale
        )
        grad_value = jnp.einsum(
            "hqk,qhd->khd",
            weights.astype(jnp.bfloat16),
            grad_attn,
            preferred_element_type=jnp.float32,
        )
        return (summed, (grad_key, grad_value))

    grad_query, (grad_keys, grad_values) = lax.scan(
        grad_step, jnp.zeros(head_shape, jnp.float32), key_stack
    )
    grad_keys_own, grad_values_own = (
        lax.psum_scatter(
            grad_keys.reshape(2, half_len, model_width).astype(jnp.bfloat16),
            "ctx",
            scatter_dimension=1,
            tiled=True,
        ).astype(jnp.float32),
        lax.psum_scatter(
            grad_values.reshape(2, half_len, model_width).astype(jnp.bfloat16),
            "ctx",
            scatter_dimension=1,
            tiled=True,
        ).astype(jnp.float32),
    )
    grad_q_rows = rotate_back(grad_query, cos_tab, sine_tab).reshape(token_count, model_width)
    grad_k_rows = rotate_back(grad_keys_own.reshape(head_shape), cos_tab, sine_tab).reshape(
        token_count, model_width
    )
    grad_projected = jnp.concatenate(
        [grad_q_rows, grad_k_rows, grad_values_own.reshape(token_count, model_width)], axis=-1
    ).astype(jnp.bfloat16)
    grad_qkv_weight = jnp.einsum(
        "td,te->de", normed_low, grad_projected, preferred_element_type=jnp.float32
    )
    grad_qkv_bias = jnp.sum(grad_projected.astype(jnp.float32), axis=0)
    grad_normed = jnp.einsum(
        "te,de->td", grad_projected, qkv_weight, preferred_element_type=jnp.float32
    )
    grad_inputs_norm, grad_gain_one = rms_back(
        inputs, inv_one, attn_gain.astype(jnp.float32), grad_normed
    )
    grad_tokens = (grad_resid + grad_inputs_norm).reshape(tokens.shape)
    attn_grads = (
        lax.psum_scatter(grad_qkv_weight, ("ctx", "fsdp"), scatter_dimension=0, tiled=True),
        lax.psum_scatter(grad_qkv_bias, ("ctx", "fsdp"), scatter_dimension=0, tiled=True),
        lax.psum_scatter(grad_out_weight, ("ctx", "fsdp"), scatter_dimension=0, tiled=True),
        lax.psum_scatter(grad_gain_one, ("ctx", "fsdp"), scatter_dimension=0, tiled=True),
    )
    return (
        output,
        grad_tokens,
        attn_grads[0],
        attn_grads[1],
        attn_grads[2],
        attn_grads[3],
        ffn_grads[0],
        ffn_grads[1],
        ffn_grads[2],
        ffn_grads[3],
        ffn_grads[4],
        expert_grads[0],
        expert_grads[1],
    )


def solution(mesh):
    in_specs = (
        P("fsdp", None, "ctx", None),
        P("fsdp", None, None),
        P("fsdp", None, "ctx", None),
        P("fsdp", None, "ctx", None),
        P(("ctx", "fsdp"), None),
        P(("ctx", "fsdp")),
        P(("ctx", "fsdp"), None),
        P(("ctx", "fsdp")),
        P(("ctx", "fsdp")),
        P(("ctx", "fsdp"), None),
        P(("ctx", "fsdp")),
        P(("ctx", "fsdp"), None),
        P(("ctx", "fsdp"), None),
        P("ctx", "fsdp", None),
        P("ctx", "fsdp", None),
    )
    out_specs = (
        P("fsdp", None, "ctx", None),
        P("fsdp", None, "ctx", None),
        P(("ctx", "fsdp"), None),
        P(("ctx", "fsdp")),
        P(("ctx", "fsdp"), None),
        P(("ctx", "fsdp")),
        P(("ctx", "fsdp")),
        P(("ctx", "fsdp"), None),
        P(("ctx", "fsdp")),
        P(("ctx", "fsdp"), None),
        P(("ctx", "fsdp"), None),
        P("ctx", "fsdp", None),
        P("ctx", "fsdp", None),
    )
    ctx_size = mesh.shape["ctx"]
    fsdp_size = mesh.shape["fsdp"]

    def local(*arrays):
        if HEADS % ctx_size:
            return local_wide(*arrays)
        return local_split(ctx_size, fsdp_size, *arrays)

    return jax.shard_map(local, mesh=mesh, in_specs=in_specs, out_specs=out_specs, check_vma=False)
```

```python
import functools

import jax
import jax.numpy as jnp
from jax import lax
from jax.experimental import pallas as pl
from jax.experimental.pallas import tpu as pltpu
from jax.sharding import PartitionSpec as P

HD = 128
HEADS = 16
FS = 5632
FE = 1408


RMS_EPS = 1e-06
ROPE_THETA = 1000000.0
MASK_FILL = -1e30
HIGHEST = lax.Precision.HIGHEST


def rope_tables(positions, head_dim):
    half_dim = head_dim // 2
    inv_freq = ROPE_THETA ** (-(jnp.arange(half_dim, dtype=jnp.float32) * 2.0 / head_dim))
    angles = positions.astype(jnp.float32)[:, None] * inv_freq[None, :]
    cos_tab = jnp.concatenate([jnp.cos(angles), jnp.cos(angles)], axis=-1)
    sine_tab = jnp.concatenate([jnp.sin(angles), jnp.sin(angles)], axis=-1)
    return (cos_tab, sine_tab)


def rotate(values, cos_tab, sine_tab):
    half_dim = values.shape[-1] // 2
    turned = jnp.concatenate([-values[..., half_dim:], values[..., :half_dim]], axis=-1)
    return values * cos_tab[:, None, :] + turned * sine_tab[:, None, :]


def rotate_back(upstream, cos_tab, sine_tab):
    half_dim = upstream.shape[-1] // 2
    scaled = upstream * sine_tab[:, None, :]
    return upstream * cos_tab[:, None, :] + jnp.concatenate(
        [scaled[..., half_dim:], -scaled[..., :half_dim]], axis=-1
    )


def rms_norm(values, gain_vec):
    inv_rms = lax.rsqrt(jnp.mean(values * values, axis=-1, keepdims=True) + RMS_EPS)
    return (values * inv_rms * gain_vec, inv_rms)


def rms_back(values, inv_rms, gain_vec, upstream):
    weighted = upstream * gain_vec
    inner_mean = jnp.mean(weighted * values, axis=-1, keepdims=True)
    return (
        inv_rms * weighted - values * inv_rms * inv_rms * inv_rms * inner_mean,
        jnp.sum(upstream * values * inv_rms, axis=0),
    )


def swiglu(pre_act, split_at):
    return jax.nn.silu(pre_act[..., :split_at]) * pre_act[..., split_at:]


def swiglu_back(pre_act, split_at, upstream):
    gate_part = pre_act[..., :split_at]
    up_part = pre_act[..., split_at:]
    sigmoid_g = jax.nn.sigmoid(gate_part)
    d_gate = upstream * up_part * sigmoid_g * (1.0 + gate_part * (1.0 - sigmoid_g))
    d_up = upstream * gate_part * sigmoid_g
    return jnp.concatenate([d_gate, d_up], axis=-1)


def ring_order(size):
    return list(range(0, size, 2)) + list(range(size - 1, 0, -2))


def ring_steps(size):
    order = ring_order(size)
    ahead = [(order[i], order[(i + 1) % size]) for i in range(size)]
    back = [(dst, src) for src, dst in ahead]
    return (ahead, back)


def ring_peers(size, ctx_index):
    order = ring_order(size)
    place = {dev: i for i, dev in enumerate(order)}
    table = jnp.array(
        [[order[(place[dev] + k) % size] for k in range(size)] for dev in range(size)], jnp.int32
    )
    row = lax.dynamic_index_in_dim(table, ctx_index, 0, keepdims=False)
    return [row[k] for k in range(size)]


def after(value, *deps):
    return lax.optimization_barrier((value,) + deps)


def ring_gather(block, size, ctx_index, rider=None):
    rows, width = block.shape

    def put(out, piece, peer, offset):
        return lax.dynamic_update_slice(out, piece, (peer * rows + offset, jnp.zeros_like(peer)))

    out = jnp.zeros((size * rows, width), block.dtype)
    ahead, back = ring_steps(size)
    peers = ring_peers(size, ctx_index)
    half = size // 2
    out = put(out, block, ctx_index, 0)
    fore = rear = block
    for k in range(1, half):
        fore = lax.ppermute(fore, "ctx", ahead)
        rear = lax.ppermute(rear, "ctx", back)
        if rider is not None and k == 2:
            fore, rider = after(fore, rider)
        out = put(out, fore, peers[size - k], 0)
        out = put(out, rear, peers[k], 0)
    fore = lax.ppermute(fore[: rows // 2], "ctx", ahead)
    rear = lax.ppermute(rear[rows // 2 :], "ctx", back)
    out = put(out, fore, peers[half], 0)
    out = put(out, rear, peers[half], rows // 2)
    return out if rider is None else (out, rider)


def ring_sums(parts, size, ctx_index, riders):
    f32 = jnp.float32
    rows = parts.shape[0] // size
    ahead, back = ring_steps(size)
    peers = ring_peers(size, ctx_index)
    half = size // 2

    def own(k, start, count):
        first = (peers[k % size] * rows + start, jnp.zeros_like(peers[0]))
        return lax.dynamic_slice(parts, first, (count, parts.shape[1])).astype(f32)

    def low(values):
        return values.astype(jnp.bfloat16)

    cut = rows // 2
    fore = lax.ppermute(low(own(half, 0, cut)), "ctx", ahead)
    rear = lax.ppermute(low(own(half, cut, cut)), "ctx", back)
    fore = jnp.concatenate(
        [low(fore.astype(f32) + own(half - 1, 0, cut)), low(own(half - 1, cut, cut))], axis=0
    )
    rear = jnp.concatenate(
        [low(own(1 - half, 0, cut)), low(rear.astype(f32) + own(1 - half, cut, cut))], axis=0
    )
    for k in range(half - 1, 0, -1):
        fore = lax.ppermute(fore, "ctx", ahead)
        rear = lax.ppermute(rear, "ctx", back)
        if riders and k == half - 1:
            fore, *riders = after(fore, *riders)
        if k > 1:
            fore = low(fore.astype(f32) + own(k - 1, 0, rows))
            rear = low(rear.astype(f32) + own(1 - k, 0, rows))
    return (fore, rear, riders)


def ring_scatter(parts, size, ctx_index, kept=None, riders=()):
    fore, rear, riders = ring_sums(parts, size, ctx_index, riders)
    kept = (parts if kept is None else kept).reshape(size, -1, parts.shape[1])
    kept = lax.dynamic_index_in_dim(kept, ctx_index, 0, keepdims=False)
    total = kept.astype(jnp.float32) + fore.astype(jnp.float32) + rear.astype(jnp.float32)
    return (total, *riders) if riders else total


def other_core(size):
    return [(i, i ^ 1) for i in range(size)]


def other_chip(size):
    return [(i, i ^ 2) for i in range(size)]


def fsdp_gather(shard, size, hold):
    index = lax.axis_index("fsdp")
    rows, width = shard.shape
    far = lax.ppermute(shard, "fsdp", other_chip(size))
    far, hold = after(far, hold)
    pair = jnp.where(
        index < 2, jnp.stack([shard, far], axis=0), jnp.stack([far, shard], axis=0)
    )
    near = lax.ppermute(pair, "fsdp", other_core(size))
    out = jnp.zeros((2, 2, rows, width), shard.dtype)
    out = lax.dynamic_update_index_in_dim(out, pair, index % 2, 1)
    out = lax.dynamic_update_index_in_dim(out, near, 1 - index % 2, 1)
    return (out.reshape(size * rows, width), hold)


def column_pieces(weight, groups, size, extra):
    rows = weight.shape[0]
    width = weight.shape[1] // (groups * size)
    pieces = weight.reshape(rows, groups, size, width).transpose(2, 0, 1, 3)
    pieces = pieces.reshape(size, rows, groups * width)
    if extra is not None:
        count = extra.shape[0]
        more = -(-count // (groups * width * 16)) * 16
        extra = jnp.pad(extra, (0, more * groups * width - count))
        extra = jnp.broadcast_to(
            extra.reshape(1, more, groups * width), (size, more, groups * width)
        )
        pieces = jnp.concatenate([pieces, extra], axis=1)
    return pieces


def merge_columns(pieces, groups, size):
    width = pieces.shape[2] // groups
    if width % 128 == 0:
        pieces = pieces.reshape(size, -1, groups, width).transpose(1, 2, 0, 3)
        return pieces.reshape(-1, groups * size * width).astype(jnp.float32)
    columns = [
        pieces[peer, :, group * width : (group + 1) * width]
        for group in range(groups)
        for peer in range(size)
    ]
    return jnp.concatenate(columns, axis=1).astype(jnp.float32)


def attention_back_kernel(
    q_ref, k_ref, v_ref, do_ref, lse_ref, key_ref, query_ref, dq_ref, dk_ref, dv_ref, *, rows
):
    f32, bf16 = jnp.float32, jnp.bfloat16
    scale = HD ** (-0.5)
    keys, values = k_ref[...], v_ref[...]
    key_pos, key_seg = key_ref[:, 0:1], key_ref[:, 1:2]

    def pair(a, b, dims):
        return lax.dot_general(a, b, (dims, ((), ())), preferred_element_type=f32)

    for start in range(0, q_ref.shape[0], rows):
        here = slice(start, start + rows)
        queries, upstream = q_ref[here, :], do_ref[here, :]
        allowed = (key_pos <= query_ref[0:1, here]) & (key_seg == query_ref[1:2, here])
        scores = jnp.where(allowed, pair(keys, queries, ((1,), (1,))) * scale, MASK_FILL)
        weights = jnp.exp(scores - lse_ref[0, :, here])
        grads = pair(values, upstream, ((1,), (1,)))
        delta = jnp.sum(weights * grads, axis=0, keepdims=True)
        grads = jnp.where(allowed, weights * (grads - delta), 0.0).astype(bf16)
        part_v = pair(weights.astype(bf16), upstream, ((1,), (0,)))
        part_k = pair(grads, queries, ((1,), (0,))) * scale
        if start == 0:
            dv_ref[...] = part_v
            dk_ref[...] = part_k
        else:
            dv_ref[...] += part_v
            dk_ref[...] += part_k
        dq_ref[here, :] = pair(grads, keys, ((0,), (0,))) * scale


def attention_back(queries, keys, values, upstream, log_total, positions, seg_rows):
    tokens, width = queries.shape
    heads = width // HD
    marks = jnp.stack([positions, seg_rows], axis=0)
    by_head = pl.BlockSpec((tokens, HD), lambda h: (0, h))
    return pl.pallas_call(
        functools.partial(attention_back_kernel, rows=min(256, tokens)),
        grid=(heads,),
        in_specs=[by_head] * 4
        + [
            pl.BlockSpec((1, 1, tokens), lambda h: (h, 0, 0)),
            pl.BlockSpec((tokens, 2), lambda h: (0, 0)),
            pl.BlockSpec((2, tokens), lambda h: (0, 0)),
        ],
        out_specs=[by_head] * 3,
        out_shape=[jax.ShapeDtypeStruct((tokens, width), jnp.float32)] * 3,
        compiler_params=pltpu.CompilerParams(vmem_limit_bytes=40 * 1024 * 1024),
        cost_estimate=pl.CostEstimate(
            flops=10 * tokens * tokens * width,
            bytes_accessed=20 * tokens * width,
            transcendentals=tokens * tokens * heads,
        ),
    )(queries, keys, values, upstream, log_total.reshape(heads, 1, tokens), marks.T, marks)


def local_split(
    ctx_size,
    fsdp_size,
    tokens,
    segments,
    routes,
    cotangent,
    w_qkv,
    b_qkv,
    w_out,
    gain_attn,
    gain_ffn,
    w_router,
    w_shared_gate,
    w_shared_in,
    w_shared_out,
    w_expert_in,
    w_expert_out,
):
    bf16, f32, i32 = jnp.bfloat16, jnp.float32, jnp.int32
    device_count = ctx_size * fsdp_size
    block_len = tokens.shape[2]
    width = tokens.shape[3]
    token_count = 2 * block_len
    top_count = routes.shape[3]
    seq_len = token_count * ctx_size
    ctx_index = lax.axis_index("ctx")
    expert_count = w_router.shape[1]
    capacity = token_count * top_count // expert_count
    own_heads = HEADS // ctx_size
    own_width = own_heads * HD
    fs_own = FS // ctx_size
    score_scale = HD ** (-0.5)

    def dot(a, b):
        return jnp.dot(a, b, preferred_element_type=f32)

    def dot_t(a, b):
        return lax.dot_general(a, b, (((1,), (1,)), ((), ())), preferred_element_type=f32)

    def t_dot(a, b):
        return lax.dot_general(a, b, (((0,), (0,)), ((), ())), preferred_element_type=f32)

    def own_rows(values):
        return lax.dynamic_index_in_dim(
            values.reshape((ctx_size, token_count) + values.shape[1:]), ctx_index, 0, keepdims=False
        )

    def sum_rows(grad):
        return lax.psum_scatter(grad.astype(bf16), "fsdp", scatter_dimension=0, tiled=True)

    shard = width // device_count
    small = [gain_attn, gain_ffn, w_shared_gate, w_router.reshape(-1), b_qkv]
    small_size = sum(piece.shape[0] for piece in small)
    small = jnp.concatenate(small + [routes.astype(bf16).reshape(-1)], axis=0)
    small_count = small.shape[0]
    own_tokens = tokens.reshape(token_count, width).astype(f32)
    own_scaled, inv_one = rms_norm(own_tokens, 1.0)
    scaled_rows = ring_gather(own_scaled.astype(bf16), ctx_size, ctx_index)
    pieces = column_pieces(w_qkv, 3, ctx_size, small)
    pieces = lax.all_to_all(pieces, "ctx", split_axis=0, concat_axis=0, tiled=True)
    shared_in = column_pieces(w_shared_in, 2, ctx_size, None)
    shared_in, scaled_rows = after(shared_in, scaled_rows)
    shared_in = lax.all_to_all(shared_in, "ctx", split_axis=0, concat_axis=0, tiled=True)
    pieces = lax.all_gather(pieces, "fsdp", axis=0, tiled=False).transpose(1, 0, 2, 3)
    qkv_weight = pieces[:, :, :shard].reshape(width, 3 * own_width)
    small = pieces[:, :, shard:].reshape(device_count, -1)[:, :small_count]
    attn_gain = small[:, :shard].reshape(width).astype(f32)
    ffn_gain = small[:, shard : 2 * shard].reshape(width).astype(f32)
    gate_vector = small[:, 2 * shard : 3 * shard].reshape(width)
    router_end = 3 * shard + shard * expert_count
    router_weight = small[:, 3 * shard : router_end].reshape(width, expert_count)
    bias = small[:, router_end:small_size].reshape(3, ctx_size, own_width).astype(f32)
    bias = lax.dynamic_index_in_dim(bias, ctx_index, 1, keepdims=False).reshape(3 * own_width)
    route_rows = small[:, small_size:].astype(i32)
    route_rows = lax.dynamic_index_in_dim(
        route_rows.reshape(ctx_size, fsdp_size, -1), lax.axis_index("fsdp"), 1, keepdims=False
    ).reshape(ctx_size, token_count, top_count)

    expert_in = lax.all_gather(w_expert_in[0], "fsdp", axis=0, tiled=True)

    block_ids = jnp.arange(ctx_size, dtype=i32)[:, None]
    local_index = jnp.arange(block_len, dtype=i32)[None, :]
    positions = jnp.stack(
        [
            block_ids * block_len + local_index,
            seq_len - (block_ids + 1) * block_len + local_index,
        ],
        axis=1,
    ).reshape(seq_len)
    seg_rows = (
        segments.reshape(2, ctx_size, block_len).transpose(1, 0, 2).reshape(seq_len)
    )
    cos_tab, sine_tab = rope_tables(positions, HD)

    normed_low = (scaled_rows.astype(f32) * attn_gain).astype(bf16)
    projected = dot(normed_low, qkv_weight) + bias
    head_shape = (seq_len, own_heads, HD)
    queries = rotate(projected[:, :own_width].reshape(head_shape), cos_tab, sine_tab).astype(bf16)
    keys = rotate(
        projected[:, own_width : 2 * own_width].reshape(head_shape), cos_tab, sine_tab
    ).astype(bf16)
    values = projected[:, 2 * own_width :].reshape(head_shape).astype(bf16)
    out_weight, queries = fsdp_gather(w_out, fsdp_size, queries)
    allowed = (positions[None, :] <= positions[:, None]) & (seg_rows[None, :] == seg_rows[:, None])
    scores = jnp.einsum("qhd,khd->hqk", queries, keys, preferred_element_type=f32) * score_scale
    scores = jnp.where(allowed[None], scores, MASK_FILL)
    top_score = jnp.max(scores, axis=-1, keepdims=True)
    log_total = top_score + jnp.log(jnp.sum(jnp.exp(scores - top_score), axis=-1, keepdims=True))
    weights = jnp.exp(scores - log_total)
    weights_low = weights.astype(bf16)
    attended = jnp.einsum("hqk,khd->qhd", weights_low, values, preferred_element_type=f32)
    attn_own = attended.astype(bf16).reshape(seq_len, own_width)
    shared_out, attn_own = fsdp_gather(w_shared_out, fsdp_size, attn_own)
    expert_out, attn_own = fsdp_gather(w_expert_out[0], fsdp_size, attn_own)
    attn_parts, shared_in = after(dot(attn_own, out_weight).astype(bf16), shared_in)
    shared_in = lax.all_gather(shared_in, "fsdp", axis=0, tiled=False)
    own_residual = own_tokens + ring_scatter(attn_parts, ctx_size, ctx_index)

    normed_two, inv_two = rms_norm(own_residual, ffn_gain)
    own_low = normed_two.astype(bf16)
    low_two, grad_rows = ring_gather(
        own_low, ctx_size, ctx_index, cotangent.reshape(token_count, width)
    )
    grad_rows = lax.all_gather(grad_rows, "ctx", axis=0, tiled=True)
    mixed_weight = jnp.concatenate([router_weight, gate_vector[:, None]], axis=1)
    logits = dot(low_two, mixed_weight)
    probs_all = jax.nn.softmax(logits[:, :expert_count], axis=-1)
    scale_all = jax.nn.sigmoid(logits[:, expert_count])
    gate_all = lax.dynamic_index_in_dim(probs_all, ctx_index, 1, keepdims=False)

    named = jnp.any(route_rows == ctx_index, axis=-1)
    before = jnp.arange(token_count)[:, None] < jnp.arange(token_count)[None, :]
    rank = dot(named.astype(bf16), before.astype(bf16)).astype(i32)
    slot_of = jnp.where(named & (rank < capacity), rank, -1)
    slot_mask = slot_of[:, None, :] == jnp.arange(capacity, dtype=i32)[None, :, None]
    slot_map = slot_mask.astype(bf16)
    blocks_two = low_two.reshape(ctx_size, token_count, width)
    gate_blocks = gate_all.reshape(ctx_size, token_count)

    def to_slots(blocks):
        picked = jnp.einsum("bmt,btd->bmd", slot_map, blocks, preferred_element_type=f32)
        return picked.reshape(ctx_size * capacity, width)

    def to_tokens(slots):
        spread = jnp.einsum(
            "bmt,bmd->btd",
            slot_map,
            slots.reshape(ctx_size, capacity, width),
            preferred_element_type=f32,
        )
        return spread.reshape(seq_len, width)

    buffer = to_slots(blocks_two).astype(bf16)
    expert_pre = dot(buffer, expert_in)
    expert_hid = swiglu(expert_pre, FE).astype(bf16)
    expert_res = dot(expert_hid, expert_out).astype(bf16)
    routed = gate_all[:, None] * to_tokens(expert_res)

    shared_in, expert_res = after(shared_in, expert_res)
    shared_in = shared_in.transpose(1, 0, 2, 3).reshape(width, 2 * fs_own)
    shared_pre = dot(low_two, shared_in)
    shared_hid = swiglu(shared_pre, fs_own).astype(bf16)
    shared_res = dot(shared_hid, shared_out)
    out_parts = (scale_all[:, None] * shared_res + routed).astype(bf16)
    grad_rows, out_parts = after(grad_rows, out_parts)

    grad_slots = to_slots(grad_rows.reshape(ctx_size, token_count, width))
    gate_slots = jnp.sum(jnp.where(slot_mask, gate_blocks[:, None, :], 0.0), axis=-1).reshape(-1, 1)
    grad_res = (gate_slots * grad_slots).astype(bf16)
    grad_hid = dot_t(grad_res, expert_out)
    slot_terms = jnp.sum(expert_hid.astype(f32) * grad_hid, axis=-1)
    slot_terms = slot_terms.reshape(ctx_size, capacity, 1)
    gate_terms = jnp.sum(jnp.where(slot_mask, slot_terms, 0.0), axis=1)
    grad_pre = swiglu_back(expert_pre, FE, grad_hid).astype(bf16)
    grad_expert_in = t_dot(buffer, grad_pre)
    grad_buffer = dot_t(grad_pre, expert_in).astype(bf16)

    grad_f32 = grad_rows.astype(f32)
    grad_expert_in, grad_shared_res = after(
        grad_expert_in.astype(bf16), (scale_all[:, None] * grad_f32).astype(bf16)
    )
    sum_expert_in = sum_rows(grad_expert_in)

    grad_shared_hid = dot_t(grad_shared_res, shared_out)
    scale_terms = jnp.sum(shared_hid.astype(f32) * grad_shared_hid, axis=-1)
    grad_shared_pre = swiglu_back(shared_pre, fs_own, grad_shared_hid).astype(bf16)
    two_parts = (dot_t(grad_shared_pre, shared_in) + to_tokens(grad_buffer)).astype(bf16)
    two_parts, expert_hid, shared_hid, grad_shared_pre = after(
        two_parts, expert_hid, shared_hid, grad_shared_pre
    )
    grad_expert_out = t_dot(expert_hid, grad_res).astype(bf16)
    grad_shared_out = t_dot(shared_hid, grad_shared_res).astype(bf16)
    grad_shared_in = t_dot(low_two, grad_shared_pre).astype(bf16)
    grad_two = ring_scatter(two_parts, ctx_size, ctx_index)
    dots = jnp.stack([gate_terms, scale_terms.reshape(ctx_size, token_count)], axis=1)
    dots = lax.all_to_all(dots, "ctx", split_axis=0, concat_axis=0, tiled=True)
    grad_two, grad_shared_in, grad_shared_out, grad_expert_out, dots = after(
        grad_two, grad_shared_in, grad_shared_out, grad_expert_out, dots
    )
    sum_shared_in = grad_shared_in.reshape(ctx_size, fsdp_size, shard, 2 * fs_own)
    sum_shared_in = lax.psum_scatter(
        sum_shared_in.transpose(1, 0, 2, 3).reshape(width, 2 * fs_own),
        "fsdp",
        scatter_dimension=0,
        tiled=True,
    ).reshape(ctx_size, shard, 2 * fs_own)
    sum_expert_out = sum_rows(grad_expert_out)
    own_probs = own_rows(probs_all)
    own_scale = own_rows(scale_all)
    own_chosen = routes.reshape(token_count, top_count)
    chosen_mask = jnp.any(
        own_chosen[..., None] == jnp.arange(expert_count, dtype=i32), axis=1
    )
    prob_terms = jnp.where(chosen_mask, dots[:, 0].T, 0.0)
    grad_logits = (
        prob_terms - own_probs * jnp.sum(prob_terms, axis=-1, keepdims=True)
    ).astype(bf16)
    grad_gate_pre = (jnp.sum(dots[:, 1], axis=0) * (1.0 - own_scale)).astype(bf16)
    grad_router = t_dot(own_low, grad_logits)
    grad_gate_vector = t_dot(own_low, grad_gate_pre[:, None])
    grad_two = grad_two + dot_t(grad_logits, router_weight)
    grad_two = grad_two + grad_gate_pre.astype(f32)[:, None] * gate_vector.astype(f32)[None, :]
    grad_resid_norm, grad_gain_two = rms_back(
        own_residual, inv_two, ffn_gain, grad_two
    )
    grad_resid = cotangent.reshape(token_count, width).astype(f32) + grad_resid_norm

    grad_mixed, sum_expert_in = after(grad_resid.astype(bf16), sum_expert_in)
    mixed_all = ring_gather(grad_mixed, ctx_size, ctx_index)
    grad_attn = dot_t(mixed_all, out_weight).astype(bf16)
    grad_attn, sum_shared_in = after(grad_attn, sum_shared_in)
    sum_shared_in = lax.all_to_all(
        sum_shared_in, "ctx", split_axis=0, concat_axis=0, tiled=True
    )
    grad_q, grad_k, grad_v = attention_back(
        queries.reshape(seq_len, own_width),
        keys.reshape(seq_len, own_width),
        values.reshape(seq_len, own_width),
        grad_attn,
        log_total,
        positions,
        seg_rows,
    )
    grad_projected = jnp.concatenate(
        [
            rotate_back(grad_q.reshape(head_shape), cos_tab, sine_tab).reshape(seq_len, own_width),
            rotate_back(grad_k.reshape(head_shape), cos_tab, sine_tab).reshape(seq_len, own_width),
            grad_v,
        ],
        axis=-1,
    ).astype(bf16)
    one_sums = dot_t(grad_projected, qkv_weight)
    grad_gain_one = jnp.sum(one_sums * scaled_rows.astype(f32), axis=0)
    one_parts, sum_shared_in = after(one_sums.astype(bf16), sum_shared_in)
    one_kept, grad_projected = after(one_parts, grad_projected)
    one_kept, attn_own = after(one_kept, attn_own)
    grad_normed, sum_expert_out, out_parts = ring_scatter(
        one_parts, ctx_size, ctx_index, one_kept, (sum_expert_out, out_parts)
    )
    grad_qkv_weight = t_dot(normed_low, grad_projected)
    grad_bias = jnp.sum(grad_projected.astype(f32), axis=0).reshape(3, 1, own_width)
    grad_bias = jnp.where(
        jnp.arange(ctx_size, dtype=i32)[None, :, None] == ctx_index, grad_bias, 0.0
    )

    grad_out_weight = t_dot(attn_own, mixed_all)
    small_grads = [grad_gain_one, grad_gain_two, grad_gate_vector, grad_router, grad_bias]
    small_grads = jnp.concatenate(
        [piece.reshape(device_count, -1) for piece in small_grads], axis=1
    )
    more = -(-small_size // (3 * own_width * 16)) * 16
    small_grads = jnp.pad(small_grads, ((0, 0), (0, more * 3 * own_width - small_size)))
    pieces = jnp.concatenate(
        [
            grad_qkv_weight.astype(bf16).reshape(ctx_size, fsdp_size, shard, 3 * own_width),
            small_grads.astype(bf16).reshape(ctx_size, fsdp_size, more, 3 * own_width),
        ],
        axis=2,
    )
    pieces = pieces.transpose(1, 0, 2, 3).reshape(-1, 3 * own_width)
    pieces = lax.psum_scatter(pieces, "fsdp", scatter_dimension=0, tiled=True)
    grad_normed, pieces, grad_shared_out, grad_out_weight = after(
        grad_normed, pieces, grad_shared_out, grad_out_weight.astype(bf16)
    )
    sum_shared_out = sum_rows(grad_shared_out)
    sum_out_weight = sum_rows(grad_out_weight)
    pieces = pieces.reshape(ctx_size, shard + more, 3 * own_width)
    pieces = lax.all_to_all(pieces, "ctx", split_axis=0, concat_axis=0, tiled=True)
    out_sum, pieces = ring_scatter(out_parts, ctx_size, ctx_index, riders=(pieces,))
    output = (own_residual + out_sum).astype(bf16).reshape(tokens.shape)
    grad_inputs_norm, unused = rms_back(
        own_tokens,
        inv_one,
        attn_gain,
        grad_normed,
    )
    grad_tokens = (grad_resid + grad_inputs_norm).reshape(tokens.shape)
    small_grads = jnp.sum(pieces[:, shard:].reshape(ctx_size, -1).astype(f32), axis=0)
    return (
        output,
        grad_tokens,
        merge_columns(pieces[:, :shard], 3, ctx_size),
        small_grads[router_end:small_size],
        sum_out_weight.astype(f32),
        small_grads[:shard],
        small_grads[shard : 2 * shard],
        small_grads[3 * shard : router_end].reshape(shard, expert_count),
        small_grads[2 * shard : 3 * shard],
        merge_columns(sum_shared_in, 2, ctx_size),
        sum_shared_out.astype(f32),
        sum_expert_in.astype(f32)[None],
        sum_expert_out.astype(f32)[None],
    )


def local_wide(
    tokens,
    segments,
    routes,
    cotangent,
    w_qkv,
    b_qkv,
    w_out,
    gain_attn,
    gain_ffn,
    w_router,
    w_shared_gate,
    w_shared_in,
    w_shared_out,
    w_expert_in,
    w_expert_out,
):
    block_len = tokens.shape[2]
    model_width = tokens.shape[3]
    token_count = 2 * block_len
    top_count = routes.shape[3]
    half_len = segments.shape[2]
    seq_len = 2 * half_len
    ctx_index = lax.axis_index("ctx")
    head_count = model_width // HD
    expert_count = w_router.shape[1]
    capacity = token_count * top_count // expert_count
    slot_count = expert_count * capacity
    key_rows = min(512, seq_len)
    key_blocks = seq_len // key_rows
    score_scale = HD ** (-0.5)
    head_shape = (token_count, head_count, HD)
    attn_set = (
        lax.all_gather(w_qkv, ("ctx", "fsdp"), axis=0, tiled=True),
        lax.all_gather(b_qkv, ("ctx", "fsdp"), axis=0, tiled=True),
        lax.all_gather(w_out, ("ctx", "fsdp"), axis=0, tiled=True),
        lax.all_gather(gain_attn, ("ctx", "fsdp"), axis=0, tiled=True),
    )
    qkv_weight, qkv_bias, out_weight, attn_gain = attn_set
    inputs = tokens.reshape(token_count, model_width).astype(jnp.float32)
    normed, inv_one = rms_norm(inputs, attn_gain.astype(jnp.float32))
    normed_low = normed.astype(jnp.bfloat16)
    projected = jnp.dot(
        normed_low, qkv_weight, preferred_element_type=jnp.float32
    ) + qkv_bias.astype(jnp.float32)
    local_index = jnp.arange(block_len, dtype=jnp.int32)
    query_pos = jnp.concatenate(
        [ctx_index * block_len + local_index, seq_len - (ctx_index + 1) * block_len + local_index]
    )
    half_index = jnp.arange(half_len, dtype=jnp.int32)
    key_pos = jnp.concatenate(
        [half_index, seq_len - block_len * (half_index // block_len + 1) + half_index % block_len]
    ).reshape(key_blocks, key_rows)
    key_seg = segments.reshape(key_blocks, key_rows)
    query_seg = lax.dynamic_slice_in_dim(segments[0], ctx_index * block_len, block_len, 1).reshape(
        token_count
    )
    cos_tab, sine_tab = rope_tables(query_pos, HD)
    queries = rotate(projected[:, :model_width].reshape(head_shape), cos_tab, sine_tab).astype(
        jnp.bfloat16
    )
    keys_own = rotate(
        projected[:, model_width : 2 * model_width].reshape(head_shape), cos_tab, sine_tab
    ).astype(jnp.bfloat16)
    values_own = projected[:, 2 * model_width :].astype(jnp.bfloat16)
    keys_all, values_all = (
        lax.all_gather(keys_own.reshape(2, block_len, model_width), "ctx", axis=1, tiled=True),
        lax.all_gather(values_own.reshape(2, block_len, model_width), "ctx", axis=1, tiled=True),
    )
    keys_all = keys_all.reshape(key_blocks, key_rows, head_count, HD)
    values_all = values_all.reshape(key_blocks, key_rows, head_count, HD)

    def score_block(key_blk, pos_blk, seg_blk):
        raw_scores = (
            jnp.einsum("qhd,khd->hqk", queries, key_blk, preferred_element_type=jnp.float32)
            * score_scale
        )
        allowed = (pos_blk[None, :] <= query_pos[:, None]) & (
            seg_blk[None, :] == query_seg[:, None]
        )
        return (jnp.where(allowed[None], raw_scores, MASK_FILL), allowed)

    def total_step(running, key_part):
        run_max, run_sum = running
        scores = score_block(key_part[0], key_part[1], key_part[2])[0]
        new_max = jnp.maximum(run_max, jnp.max(scores, axis=-1))
        run_sum = run_sum * jnp.exp(run_max - new_max) + jnp.sum(
            jnp.exp(scores - new_max[..., None]), axis=-1
        )
        return ((new_max, run_sum), None)

    start_max = jnp.full((head_count, token_count), MASK_FILL, jnp.float32)
    start_sum = jnp.zeros((head_count, token_count), jnp.float32)
    (run_max, run_sum), unused = lax.scan(
        total_step, (start_max, start_sum), (keys_all, key_pos, key_seg)
    )
    log_total = run_max + jnp.log(run_sum)

    def attend_step(summed, key_part):
        key_blk, value_blk, pos_blk, seg_blk = key_part
        scores = score_block(key_blk, pos_blk, seg_blk)[0]
        weights = jnp.exp(scores - log_total[..., None]).astype(jnp.bfloat16)
        return (
            summed
            + jnp.einsum("hqk,khd->qhd", weights, value_blk, preferred_element_type=jnp.float32),
            None,
        )

    key_stack = (keys_all, values_all, key_pos, key_seg)
    attended, unused = lax.scan(attend_step, jnp.zeros(head_shape, jnp.float32), key_stack)
    attn_low = attended.reshape(token_count, model_width).astype(jnp.bfloat16)
    residual = inputs + jnp.dot(attn_low, out_weight, preferred_element_type=jnp.float32)
    ffn_set = (
        lax.all_gather(gain_ffn, ("ctx", "fsdp"), axis=0, tiled=True),
        lax.all_gather(w_router, ("ctx", "fsdp"), axis=0, tiled=True),
        lax.all_gather(w_shared_gate, ("ctx", "fsdp"), axis=0, tiled=True),
        lax.all_gather(w_shared_in, ("ctx", "fsdp"), axis=0, tiled=True),
        lax.all_gather(w_shared_out, ("ctx", "fsdp"), axis=0, tiled=True),
    )
    ffn_gain, router_weight, gate_vector, shared_in, shared_out = ffn_set
    normed_two, inv_two = rms_norm(residual, ffn_gain.astype(jnp.float32))
    low_two = normed_two.astype(jnp.bfloat16)
    logits = jnp.dot(low_two, router_weight, preferred_element_type=jnp.float32)
    router_probs = jax.nn.softmax(logits, axis=-1)
    chosen = routes.reshape(token_count, top_count)
    chosen_mask = chosen[..., None] == jnp.arange(expert_count, dtype=jnp.int32)
    gate_vals = jnp.sum(jnp.where(chosen_mask, router_probs[:, None, :], 0.0), axis=-1)
    shared_scale = jax.nn.sigmoid(jnp.dot(low_two, gate_vector, preferred_element_type=jnp.float32))
    shared_pre = jnp.dot(low_two, shared_in, preferred_element_type=jnp.float32)
    shared_hid = swiglu(shared_pre, FS).astype(jnp.bfloat16)
    shared_res = jnp.dot(shared_hid, shared_out, preferred_element_type=jnp.float32)
    pair_routes = chosen.reshape(token_count * top_count)
    expert_marks = (
        pair_routes[:, None] == jnp.arange(expert_count, dtype=jnp.int32)[None, :]
    ).astype(jnp.int32)
    pair_ranks = jnp.sum((jnp.cumsum(expert_marks, axis=0) - expert_marks) * expert_marks, axis=1)
    pair_target = jnp.where(pair_ranks < capacity, pair_routes * capacity + pair_ranks, -1)
    pair_map = pair_target[:, None] == jnp.arange(slot_count, dtype=jnp.int32)[None, :]
    pair_low = pair_map.astype(jnp.bfloat16)
    token_map = jnp.sum(
        pair_map.reshape(token_count, top_count, slot_count).astype(jnp.int32), axis=1
    ).astype(jnp.bfloat16)
    outgoing = jnp.einsum(
        "tc,td->cd", token_map, low_two, preferred_element_type=jnp.float32
    ).astype(jnp.bfloat16)
    incoming = lax.all_to_all(
        outgoing.reshape(expert_count, capacity, model_width),
        "ctx",
        split_axis=0,
        concat_axis=1,
        tiled=True,
    )
    expert_in, expert_out = (
        lax.all_gather(w_expert_in, "fsdp", axis=1, tiled=True),
        lax.all_gather(w_expert_out, "fsdp", axis=1, tiled=True),
    )
    expert_pre = jnp.einsum("erd,edf->erf", incoming, expert_in, preferred_element_type=jnp.float32)
    expert_hid = swiglu(expert_pre, FE).astype(jnp.bfloat16)
    expert_res = jnp.einsum(
        "erf,efd->erd", expert_hid, expert_out, preferred_element_type=jnp.float32
    ).astype(jnp.bfloat16)
    returned = lax.all_to_all(expert_res, "ctx", split_axis=1, concat_axis=0, tiled=True).reshape(
        slot_count, model_width
    )
    pair_vals = jnp.dot(pair_low, returned, preferred_element_type=jnp.float32).reshape(
        token_count, top_count, model_width
    )
    routed = jnp.sum(gate_vals[..., None] * pair_vals, axis=1)
    output = (
        (residual + shared_scale[:, None] * shared_res + routed)
        .astype(jnp.bfloat16)
        .reshape(tokens.shape)
    )
    grad_out = cotangent.reshape(token_count, model_width).astype(jnp.float32)
    pair_grads = gate_vals[..., None] * grad_out[:, None, :]
    grad_gates = jnp.sum(grad_out[:, None, :] * pair_vals, axis=-1)
    grad_returned = jnp.einsum(
        "pc,pd->cd",
        pair_map.astype(jnp.float32),
        pair_grads.reshape(token_count * top_count, model_width),
        precision=HIGHEST,
    ).astype(jnp.bfloat16)
    grad_res = lax.all_to_all(
        grad_returned.reshape(expert_count, capacity, model_width),
        "ctx",
        split_axis=0,
        concat_axis=1,
        tiled=True,
    )
    grad_expert_out = jnp.einsum(
        "erf,erd->efd", expert_hid, grad_res, preferred_element_type=jnp.float32
    )
    grad_hid = jnp.einsum("erd,efd->erf", grad_res, expert_out, preferred_element_type=jnp.float32)
    grad_pre = swiglu_back(expert_pre, FE, grad_hid).astype(jnp.bfloat16)
    grad_expert_in = jnp.einsum(
        "erd,erf->edf", incoming, grad_pre, preferred_element_type=jnp.float32
    )
    grad_incoming = jnp.einsum(
        "erf,edf->erd", grad_pre, expert_in, preferred_element_type=jnp.float32
    ).astype(jnp.bfloat16)
    grad_outgoing = lax.all_to_all(
        grad_incoming, "ctx", split_axis=1, concat_axis=0, tiled=True
    ).reshape(slot_count, model_width)
    expert_grads = (
        lax.psum_scatter(
            grad_expert_in.astype(jnp.bfloat16), "fsdp", scatter_dimension=1, tiled=True
        ).astype(jnp.float32),
        lax.psum_scatter(
            grad_expert_out.astype(jnp.bfloat16), "fsdp", scatter_dimension=1, tiled=True
        ).astype(jnp.float32),
    )
    grad_two = jnp.einsum("tc,cd->td", token_map, grad_outgoing, preferred_element_type=jnp.float32)
    grad_probs = jnp.sum(jnp.where(chosen_mask, grad_gates[..., None], 0.0), axis=1)
    grad_logits = (
        router_probs * (grad_probs - jnp.sum(router_probs * grad_probs, axis=-1, keepdims=True))
    ).astype(jnp.bfloat16)
    grad_router = jnp.einsum("td,te->de", low_two, grad_logits, preferred_element_type=jnp.float32)
    grad_shared_res = (shared_scale[:, None] * grad_out).astype(jnp.bfloat16)
    grad_gate_pre = (
        jnp.sum(grad_out * shared_res, axis=-1) * shared_scale * (1.0 - shared_scale)
    ).astype(jnp.bfloat16)
    grad_shared_out = jnp.einsum(
        "tf,td->fd", shared_hid, grad_shared_res, preferred_element_type=jnp.float32
    )
    grad_shared_hid = jnp.einsum(
        "td,fd->tf", grad_shared_res, shared_out, preferred_element_type=jnp.float32
    )
    grad_shared_pre = swiglu_back(shared_pre, FS, grad_shared_hid).astype(jnp.bfloat16)
    grad_shared_in = jnp.einsum(
        "td,tf->df", low_two, grad_shared_pre, preferred_element_type=jnp.float32
    )
    grad_gate_vector = jnp.einsum(
        "td,t->d", low_two, grad_gate_pre, preferred_element_type=jnp.float32
    )
    grad_two = grad_two + jnp.einsum(
        "te,de->td", grad_logits, router_weight, preferred_element_type=jnp.float32
    )
    grad_two = grad_two + jnp.einsum(
        "tf,df->td", grad_shared_pre, shared_in, preferred_element_type=jnp.float32
    )
    grad_two = (
        grad_two
        + grad_gate_pre.astype(jnp.float32)[:, None] * gate_vector.astype(jnp.float32)[None, :]
    )
    grad_resid_norm, grad_gain_two = rms_back(
        residual, inv_two, ffn_gain.astype(jnp.float32), grad_two
    )
    grad_resid = grad_out + grad_resid_norm
    ffn_grads = (
        lax.psum_scatter(grad_gain_two, ("ctx", "fsdp"), scatter_dimension=0, tiled=True),
        lax.psum_scatter(grad_router, ("ctx", "fsdp"), scatter_dimension=0, tiled=True),
        lax.psum_scatter(grad_gate_vector, ("ctx", "fsdp"), scatter_dimension=0, tiled=True),
        lax.psum_scatter(grad_shared_in, ("ctx", "fsdp"), scatter_dimension=0, tiled=True),
        lax.psum_scatter(grad_shared_out, ("ctx", "fsdp"), scatter_dimension=0, tiled=True),
    )
    grad_mixed = grad_resid.astype(jnp.bfloat16)
    grad_out_weight = jnp.einsum(
        "tc,td->cd", attn_low, grad_mixed, preferred_element_type=jnp.float32
    )
    grad_attn = (
        jnp.einsum("td,cd->tc", grad_mixed, out_weight, preferred_element_type=jnp.float32)
        .astype(jnp.bfloat16)
        .reshape(head_shape)
    )

    def delta_step(summed, key_part):
        key_blk, value_blk, pos_blk, seg_blk = key_part
        weights = jnp.exp(score_block(key_blk, pos_blk, seg_blk)[0] - log_total[..., None])
        grad_weights = jnp.einsum(
            "qhd,khd->hqk", grad_attn, value_blk, preferred_element_type=jnp.float32
        )
        return (summed + jnp.sum(weights * grad_weights, axis=-1), None)

    delta_sum, unused = lax.scan(
        delta_step, jnp.zeros((head_count, token_count), jnp.float32), key_stack
    )

    def grad_step(summed, key_part):
        key_blk, value_blk, pos_blk, seg_blk = key_part
        scores, allowed = score_block(key_blk, pos_blk, seg_blk)
        weights = jnp.exp(scores - log_total[..., None])
        grad_weights = jnp.einsum(
            "qhd,khd->hqk", grad_attn, value_blk, preferred_element_type=jnp.float32
        )
        grad_scores = jnp.where(
            allowed[None], weights * (grad_weights - delta_sum[..., None]), 0.0
        ).astype(jnp.bfloat16)
        summed = (
            summed
            + jnp.einsum("hqk,khd->qhd", grad_scores, key_blk, preferred_element_type=jnp.float32)
            * score_scale
        )
        grad_key = (
            jnp.einsum("hqk,qhd->khd", grad_scores, queries, preferred_element_type=jnp.float32)
            * score_scale
        )
        grad_value = jnp.einsum(
            "hqk,qhd->khd",
            weights.astype(jnp.bfloat16),
            grad_attn,
            preferred_element_type=jnp.float32,
        )
        return (summed, (grad_key, grad_value))

    grad_query, (grad_keys, grad_values) = lax.scan(
        grad_step, jnp.zeros(head_shape, jnp.float32), key_stack
    )
    grad_keys_own, grad_values_own = (
        lax.psum_scatter(
            grad_keys.reshape(2, half_len, model_width).astype(jnp.bfloat16),
            "ctx",
            scatter_dimension=1,
            tiled=True,
        ).astype(jnp.float32),
        lax.psum_scatter(
            grad_values.reshape(2, half_len, model_width).astype(jnp.bfloat16),
            "ctx",
            scatter_dimension=1,
            tiled=True,
        ).astype(jnp.float32),
    )
    grad_q_rows = rotate_back(grad_query, cos_tab, sine_tab).reshape(token_count, model_width)
    grad_k_rows = rotate_back(grad_keys_own.reshape(head_shape), cos_tab, sine_tab).reshape(
        token_count, model_width
    )
    grad_projected = jnp.concatenate(
        [grad_q_rows, grad_k_rows, grad_values_own.reshape(token_count, model_width)], axis=-1
    ).astype(jnp.bfloat16)
    grad_qkv_weight = jnp.einsum(
        "td,te->de", normed_low, grad_projected, preferred_element_type=jnp.float32
    )
    grad_qkv_bias = jnp.sum(grad_projected.astype(jnp.float32), axis=0)
    grad_normed = jnp.einsum(
        "te,de->td", grad_projected, qkv_weight, preferred_element_type=jnp.float32
    )
    grad_inputs_norm, grad_gain_one = rms_back(
        inputs, inv_one, attn_gain.astype(jnp.float32), grad_normed
    )
    grad_tokens = (grad_resid + grad_inputs_norm).reshape(tokens.shape)
    attn_grads = (
        lax.psum_scatter(grad_qkv_weight, ("ctx", "fsdp"), scatter_dimension=0, tiled=True),
        lax.psum_scatter(grad_qkv_bias, ("ctx", "fsdp"), scatter_dimension=0, tiled=True),
        lax.psum_scatter(grad_out_weight, ("ctx", "fsdp"), scatter_dimension=0, tiled=True),
        lax.psum_scatter(grad_gain_one, ("ctx", "fsdp"), scatter_dimension=0, tiled=True),
    )
    return (
        output,
        grad_tokens,
        attn_grads[0],
        attn_grads[1],
        attn_grads[2],
        attn_grads[3],
        ffn_grads[0],
        ffn_grads[1],
        ffn_grads[2],
        ffn_grads[3],
        ffn_grads[4],
        expert_grads[0],
        expert_grads[1],
    )


def solution(mesh):
    in_specs = (
        P("fsdp", None, "ctx", None),
        P("fsdp", None, None),
        P("fsdp", None, "ctx", None),
        P("fsdp", None, "ctx", None),
        P(("ctx", "fsdp"), None),
        P(("ctx", "fsdp")),
        P(("ctx", "fsdp"), None),
        P(("ctx", "fsdp")),
        P(("ctx", "fsdp")),
        P(("ctx", "fsdp"), None),
        P(("ctx", "fsdp")),
        P(("ctx", "fsdp"), None),
        P(("ctx", "fsdp"), None),
        P("ctx", "fsdp", None),
        P("ctx", "fsdp", None),
    )
    out_specs = (
        P("fsdp", None, "ctx", None),
        P("fsdp", None, "ctx", None),
        P(("ctx", "fsdp"), None),
        P(("ctx", "fsdp")),
        P(("ctx", "fsdp"), None),
        P(("ctx", "fsdp")),
        P(("ctx", "fsdp")),
        P(("ctx", "fsdp"), None),
        P(("ctx", "fsdp")),
        P(("ctx", "fsdp"), None),
        P(("ctx", "fsdp"), None),
        P("ctx", "fsdp", None),
        P("ctx", "fsdp", None),
    )
    ctx_size = mesh.shape["ctx"]
    fsdp_size = mesh.shape["fsdp"]

    def local(*arrays):
        if HEADS % ctx_size:
            return local_wide(*arrays)
        return local_split(ctx_size, fsdp_size, *arrays)

    return jax.shard_map(local, mesh=mesh, in_specs=in_specs, out_specs=out_specs, check_vma=False)
```
